32 devices in a mesh: seq: 2 (over x), fsdp: 16 (over z, y, core).
Axes of the slice: x: 2, y: 2, z: 4, core: 2. Of those that a mesh axis runs over, the one named last changes fastest.
Arguments:
- tokens: bfloat16 [16, 336, 2048], P('fsdp', 'seq'), may hold values from -6 to 6
- cotangent: bfloat16 [16, 336, 2048], P('fsdp', 'seq'), may hold values from -6 to 6
- lengths: int32 [16], P('fsdp'), may hold values from 169 to 336, as said below
- qkv_weight: float32 [2048, 6144], P(('seq', 'fsdp')), may hold values from -0.125 to 0.125
- qkv_moment: float32 [2048, 6144], P(('seq', 'fsdp')), may hold values from -896 to 896
- qkv_square: float32 [2048, 6144], P(('seq', 'fsdp')), may hold values from 20800 to 83200
- out_weight: float32 [2048, 2048], P(('seq', 'fsdp')), may hold values from -1.5 to 1.5
- out_moment: float32 [2048, 2048], P(('seq', 'fsdp')), may hold values from -80 to 80
- out_square: float32 [2048, 2048], P(('seq', 'fsdp')), may hold values from 160 to 640
- up_weight: float32 [2048, 8192], P(('seq', 'fsdp')), may hold values from -0.125 to 0.125
- up_moment: float32 [2048, 8192], P(('seq', 'fsdp')), may hold values from -160 to 160
- up_square: float32 [2048, 8192], P(('seq', 'fsdp')), may hold values from 725.76 to 2903.04
- down_weight: float32 [4096, 2048], P(('seq', 'fsdp')), may hold values from -0.09375 to 0.09375
- down_moment: float32 [4096, 2048], P(('seq', 'fsdp')), may hold values from -224 to 224
- down_square: float32 [4096, 2048], P(('seq', 'fsdp')), may hold values from 1451.52 to 5806.08
- norm_gains: float32 [2, 2048], P(None, ('seq', 'fsdp')), may hold values from 0.5 to 1.5
- gains_moment: float32 [2, 2048], P(None, ('seq', 'fsdp')), may hold values from -896 to 896
- gains_square: float32 [2, 2048], P(None, ('seq', 'fsdp')), may hold values from 2688 to 256000
Outputs:
- block_output: bfloat16 [16, 336, 2048], P('fsdp', 'seq')
- input_grad: float32 [16, 336, 2048], P('fsdp', 'seq')
- qkv_updated: float32 [2048, 6144], P(('seq', 'fsdp'))
- qkv_moment_new: float32 [2048, 6144], P(('seq', 'fsdp'))
- qkv_square_new: float32 [2048, 6144], P(('seq', 'fsdp'))
- qkv_copy: bfloat16 [2048, 6144], P(('seq', 'fsdp'))
- out_updated: float32 [2048, 2048], P(('seq', 'fsdp'))
- out_moment_new: float32 [2048, 2048], P(('seq', 'fsdp'))
- out_square_new: float32 [2048, 2048], P(('seq', 'fsdp'))
- out_copy: bfloat16 [2048, 2048], P(('seq', 'fsdp'))
- up_updated: float32 [2048, 8192], P(('seq', 'fsdp'))
- up_moment_new: float32 [2048, 8192], P(('seq', 'fsdp'))
- up_square_new: float32 [2048, 8192], P(('seq', 'fsdp'))
- up_copy: bfloat16 [2048, 8192], P(('seq', 'fsdp'))
- down_updated: float32 [4096, 2048], P(('seq', 'fsdp'))
- down_moment_new: float32 [4096, 2048], P(('seq', 'fsdp'))
- down_square_new: float32 [4096, 2048], P(('seq', 'fsdp'))
- down_copy: bfloat16 [4096, 2048], P(('seq', 'fsdp'))
- gains_updated: float32 [2, 2048], P(None, ('seq', 'fsdp'))
- gains_moment_new: float32 [2, 2048], P(None, ('seq', 'fsdp'))
- gains_square_new: float32 [2, 2048], P(None, ('seq', 'fsdp'))
The draws below stay inside these ranges and needn't reach their ends.
Inputs may be any that keep to these rules, and one draw needn't show every extreme that they name: `lengths`: positions at or beyond a sequence's length are padding. In every draw one sequence has exactly 336 valid tokens.
All inputs are finite; a program needn't handle non-finite values.
Results may differ from the reference program's by a relative error of at most 0.014.
The reference program's roundings to bfloat16 on the way count: a program that leaves them out, or rounds other values in their place, can miss the bound.
Values may be sent and summed in bfloat16 or wider, within the bound.
A program may use at most 384 MiB of HBM per device.

```python
import math
import jax
import jax.numpy as jnp
from jax import lax

D = 2048
HEADS = 32
HEAD_DIM = 64
FF = 4096
WINDOW = 128
STEP = 5
LENGTH = 336
SEQS = 16


def draw_lengths(key, part):
    key = jax.random.fold_in(key, 7)
    first_key, second_key = jax.random.split(key)
    length_draw = jax.random.randint(first_key, (SEQS,), LENGTH // 2 + 1, LENGTH + 1, dtype=jnp.int32)
    chosen = jax.random.randint(second_key, (), 0, SEQS, dtype=jnp.int32)
    return jnp.where(jnp.arange(SEQS, dtype=jnp.int32) == chosen, LENGTH, length_draw).astype(jnp.int32)


def block_scale(key, shape, cuts, low, high):
    def one(dim, parts):
        draws = jax.random.uniform(jax.random.fold_in(jax.random.fold_in(key, 6), dim), (parts,), jnp.float32, low / len(cuts), high / len(cuts))
        return jnp.repeat(jnp.exp(draws), shape[dim] // parts).reshape((-1,) + (1,) * (len(shape) - dim - 1))

    gain = one(*cuts[0])
    for cut in cuts[1:]:
        gain = gain * one(*cut)
    return gain


def centred(stream_key, shape, scale, most, pieces=(), held_as=jnp.bfloat16):
    values = jax.random.normal(stream_key, shape, jnp.float32) * scale
    if len(pieces) > 0:
        values = block_scale(stream_key, shape, pieces, -0.22, 0.18) * values
    return jnp.clip(values, min=-most, max=most).astype(held_as)


def setup_inputs(seed: int = 0) -> dict:
    splits = jax.random.split(jax.random.key(seed), 19)
    return {
        "tokens": centred(splits[0], (SEQS, LENGTH, D), 1.0, 6.0, ((0, 16), (1, 2))),
        "cotangent": centred(splits[1], (SEQS, LENGTH, D), 1.0, 6.0, ((0, 16), (1, 2))),
        "lengths": draw_lengths(jax.random.fold_in(splits[18], 71), 0),
        "qkv_weight": centred(splits[3], (D, 3 * D), D ** -0.5, 0.125, ((0, 32),), jnp.float32),
        "qkv_moment": centred(splits[4], (D, 3 * D), ((1300 * SEQS) ** 0.5), 896.0, ((0, 32),), jnp.float32),
        "qkv_square": jnp.clip(jnp.exp(math.log(83200.0) - 1.3862944 * jax.random.uniform(splits[5], (D, 3 * D), jnp.float32) ** block_scale(splits[5], (D, 3 * D), ((0, 32),), -0.2, 0.2)), 20800.0, 83200.0),
        "out_weight": centred(splits[6], (D, D), (D // 128) ** -0.5, 1.5, ((0, 32),), jnp.float32),
        "out_moment": centred(splits[7], (D, D), ((10 * SEQS) ** 0.5), 80.0, ((0, 32),), jnp.float32),
        "out_square": jnp.clip(jnp.exp(math.log(640.0) - 1.3862944 * jax.random.uniform(splits[8], (D, D), jnp.float32) ** block_scale(splits[8], (D, D), ((0, 32),), -0.2, 0.2)), 160.0, 640.0),
        "up_weight": centred(splits[9], (D, 2 * FF), D ** -0.5, 0.125, ((0, 32),), jnp.float32),
        "up_moment": centred(splits[10], (D, 2 * FF), ((SEQS * LENGTH * 0.135) ** 0.5), 160.0, ((0, 32),), jnp.float32),
        "up_square": jnp.clip(jnp.exp(math.log(2903.04) - 1.3862944 * jax.random.uniform(splits[11], (D, 2 * FF), jnp.float32) ** block_scale(splits[11], (D, 2 * FF), ((0, 32),), -0.2, 0.2)), 725.76, 2903.04),
        "down_weight": centred(splits[12], (FF, D), FF ** -0.5, 0.09375, ((0, 32),), jnp.float32),
        "down_moment": centred(splits[13], (FF, D), ((SEQS * LENGTH * 0.27) ** 0.5), 224.0, ((0, 32),), jnp.float32),
        "down_square": jnp.clip(jnp.exp(math.log(5806.08) - 1.3862944 * jax.random.uniform(splits[14], (FF, D), jnp.float32) ** block_scale(splits[14], (FF, D), ((0, 32),), -0.2, 0.2)), 1451.52, 5806.08),
        "norm_gains": jnp.clip(1.0 + 0.1 * jax.random.normal(splits[15], (2, D), jnp.float32), 0.5, 1.5),
        "gains_moment": centred(splits[16], (2, D), ((1400 * SEQS) ** 0.5), 896.0, ((1, 32),), jnp.float32),
        "gains_square": jnp.clip(jnp.exp(math.log(256000.0) - 4.55638 * jax.random.uniform(splits[17], (2, D), jnp.float32) ** block_scale(splits[17], (2, D), ((1, 32),), -0.2, 0.2)), 2688.0, 256000.0),
    }


NORM_EPSILON = 1e-05
MOMENT_DECAY = 0.5
WEIGHT_DECAY = 0.1
ADAM_EPSILON = 1e-08
highest = lax.Precision.HIGHEST

@jax.custom_vjp
def low(v):
    return lax.optimization_barrier(v.astype(jnp.bfloat16)).astype(jnp.float32)

@jax.custom_vjp
def low_back(v):
    return v

def low_keep(v):
    return (low(v), None)

def low_pass(kept, grad):
    return (grad,)

def back_keep(v):
    return (v, None)

def back_low(kept, grad):
    return (low(grad),)
low.defvjp(low_keep, low_pass)
low_back.defvjp(back_keep, back_low)

def rotate_table(positions, head_dim):
    halves = head_dim // 2
    freqs = jnp.exp(-math.log(10000.0) * 2.0 * jnp.arange(halves).astype(jnp.float32) / head_dim)
    angles = positions.astype(jnp.float32)[:, None] * freqs[None, :]
    return (jnp.cos(angles), jnp.sin(angles))

def rotate(values, cos_part, sin_part, direction):
    halves = values.shape[-1] // 2
    first_half = values[..., :halves]
    second = values[..., halves:]
    cosine = cos_part[:, None, :]
    sine = sin_part[:, None, :] * direction
    return jnp.concatenate([first_half * cosine - second * sine, second * cosine + first_half * sine], axis=-1)

def adam_update(weight, moment, square, gradient, step_rate):
    moment_new = MOMENT_DECAY * moment + (1.0 - MOMENT_DECAY) * gradient
    square_new = MOMENT_DECAY * square + (1.0 - MOMENT_DECAY) * gradient * gradient
    correction = 1.0 - MOMENT_DECAY ** STEP
    update = moment_new / correction / (jnp.sqrt(square_new / correction) + ADAM_EPSILON)
    return (weight - step_rate * (update + WEIGHT_DECAY * weight), moment_new, square_new)

def forward(inputs, qkv_matrix, out_matrix, up_matrix, down_matrix, gain_rows, lengths):
    qkv_low = low(qkv_matrix)
    out_low = low(out_matrix)
    up_low = low(up_matrix)
    down_low = low(down_matrix)
    gain_low = low(gain_rows)
    positions = jnp.arange(LENGTH, dtype=jnp.int32)
    cos_part, sin_part = rotate_table(positions, HEAD_DIM)
    score_scale = HEAD_DIM ** (-0.5)
    row_index = positions[:, None]
    col_index = positions[None, :]

    def one_sequence(carried):
        sequence, length = carried
        first_scale = lax.rsqrt(lax.optimization_barrier(jnp.mean(sequence * sequence, axis=-1, keepdims=True)) + NORM_EPSILON)
        first_norm = low(sequence * first_scale * gain_low[0])
        projected = low_back(jnp.dot(first_norm, qkv_low, precision=highest, preferred_element_type=jnp.float32))
        projected = projected.reshape(LENGTH, 3, HEADS, HEAD_DIM)
        queries = low(low_back(rotate(projected[:, 0], cos_part, sin_part, 1.0)))
        key_vectors = low(low_back(rotate(projected[:, 1], cos_part, sin_part, 1.0)))
        value_vectors = low(low_back(projected[:, 2]))
        raw_scores = low_back(jnp.einsum('qhd,khd->hqk', queries, key_vectors, precision=highest) * score_scale)
        allowed = (col_index <= row_index) & (row_index - col_index < WINDOW) & (col_index < length)
        masked = jnp.where(allowed[None], raw_scores, -1e+30)
        row_max = lax.optimization_barrier(jnp.max(masked, axis=-1, keepdims=True))
        exp_scores = jnp.exp(masked - row_max)
        probability = low(exp_scores / lax.optimization_barrier(jnp.sum(exp_scores, axis=-1, keepdims=True)))
        attended = jnp.einsum('hqk,khd->qhd', probability, value_vectors, precision=highest).reshape(LENGTH, D)
        attended = low(low_back(attended))
        attention = low_back(jnp.dot(attended, out_low, precision=highest, preferred_element_type=jnp.float32))
        residual = sequence + attention
        second_scale = lax.rsqrt(lax.optimization_barrier(jnp.mean(residual * residual, axis=-1, keepdims=True)) + NORM_EPSILON)
        second_norm = low(residual * second_scale * gain_low[1])
        both_parts = low_back(jnp.dot(second_norm, up_low, precision=highest, preferred_element_type=jnp.float32))
        gate_part = both_parts[:, :FF]
        up_part = both_parts[:, FF:]
        hidden = low(jax.nn.silu(gate_part) * up_part)
        return residual + jnp.dot(hidden, down_low, precision=highest, preferred_element_type=jnp.float32)
    return lax.map(jax.checkpoint(one_sequence), (inputs, lengths))

def reference(tokens, cotangent, lengths, qkv_weight, qkv_moment, qkv_square, out_weight, out_moment, out_square, up_weight, up_moment, up_square, down_weight, down_moment, down_square, norm_gains, gains_moment, gains_square):

    def apply_block(inputs, qkv_matrix, out_matrix, up_matrix, down_matrix, gain_rows):
        return forward(inputs, qkv_matrix, out_matrix, up_matrix, down_matrix, gain_rows, lengths)
    outputs, pullback = jax.vjp(apply_block, tokens.astype(jnp.float32), qkv_weight, out_weight, up_weight, down_weight, norm_gains)
    positions = jnp.arange(LENGTH, dtype=jnp.int32)
    valid_mask = (positions[None, :] < lengths[:, None]).astype(jnp.float32)[:, :, None]
    input_grad, qkv_grad, out_grad, up_grad, down_grad, gains_grad = pullback(cotangent.astype(jnp.float32) * valid_mask)
    qkv_updated, qkv_moment_new, qkv_square_new = adam_update(qkv_weight, qkv_moment, qkv_square, qkv_grad, D ** (-0.5))
    out_updated, out_moment_new, out_square_new = adam_update(out_weight, out_moment, out_square, out_grad, (D // 128) ** (-0.5))
    up_updated, up_moment_new, up_square_new = adam_update(up_weight, up_moment, up_square, up_grad, D ** (-0.5))
    down_updated, down_moment_new, down_square_new = adam_update(down_weight, down_moment, down_square, down_grad, FF ** (-0.5))
    gains_updated, gains_moment_new, gains_square_new = adam_update(norm_gains, gains_moment, gains_square, gains_grad, 0.3)
    return (outputs.astype(jnp.bfloat16), input_grad, qkv_updated, qkv_moment_new, qkv_square_new, qkv_updated.astype(jnp.bfloat16), out_updated, out_moment_new, out_square_new, out_updated.astype(jnp.bfloat16), up_updated, up_moment_new, up_square_new, up_updated.astype(jnp.bfloat16), down_updated, down_moment_new, down_square_new, down_updated.astype(jnp.bfloat16), gains_updated, gains_moment_new, gains_square_new)
```

```python
import math

import jax
import jax.numpy as jnp
from jax import lax
from jax.experimental import pallas as pl
from jax.experimental.pallas import tpu as pltpu
from jax.sharding import Mesh, PartitionSpec as P

D = 2048
HEADS = 32
HEAD_DIM = 64
FF = 4096
WINDOW = 128
STEP = 5


NORM_EPSILON = 1e-05
MOMENT_DECAY = 0.5
WEIGHT_DECAY = 0.1
ADAM_EPSILON = 1e-08

SEATS = ("row", "core", "seq")
RANKS = ("seq", "row", "core")
EVERY = ("seq", "grp", "row", "core")
QUAD = 4

bf16 = jnp.bfloat16
f32 = jnp.float32


def rotate_table(length, copies):
    halves = HEAD_DIM // 2
    freqs = jnp.exp(-math.log(10000.0) * 2.0 * jnp.arange(halves).astype(f32) / HEAD_DIM)
    angles = jnp.arange(length, dtype=jnp.int32).astype(f32)[:, None] * freqs[None, :]
    cosine, sine = jnp.cos(angles), jnp.sin(angles)
    return (
        jnp.tile(jnp.concatenate([cosine, cosine], axis=1), (1, copies)),
        jnp.tile(jnp.concatenate([-sine, sine], axis=1), (1, copies)),
    )


def adam_update(weight, moment, square, gradient, step_rate):
    moment_new = MOMENT_DECAY * moment + (1.0 - MOMENT_DECAY) * gradient
    square_new = MOMENT_DECAY * square + (1.0 - MOMENT_DECAY) * gradient * gradient
    correction = 1.0 - MOMENT_DECAY**STEP
    update = moment_new / correction / (jnp.sqrt(square_new / correction) + ADAM_EPSILON)
    return (weight - step_rate * (update + WEIGHT_DECAY * weight), moment_new, square_new)


def norm_back(row_values, row_scale, gain_row, gradient):
    scaled_grad = gradient * gain_row
    gain_grad = jnp.sum(gradient * row_values * row_scale, axis=0)
    inner_mean = jnp.mean(scaled_grad * row_values, axis=-1, keepdims=True)
    row_grad = row_scale * (scaled_grad - row_values * row_scale * row_scale * inner_mean)
    return (row_grad, gain_grad)


def dot(a, b, lhs=1, rhs=0):
    return lax.dot_general(a, b, (((lhs,), (rhs,)), ((), ())), preferred_element_type=f32)


def swap_halves(values, first):
    width = values.shape[1]
    half = HEAD_DIM // 2
    return jnp.where(
        first, pltpu.roll(values, width - half, 1), pltpu.roll(values, half, 1)
    )


def allowed_mask(rows, length):
    row = lax.broadcasted_iota(jnp.int32, (rows, rows), 0)
    col = lax.broadcasted_iota(jnp.int32, (rows, rows), 1)
    return (col <= row) & (row - col < WINDOW) & (col < length)


def head_lanes(rows, width, head):
    lane = lax.broadcasted_iota(jnp.int32, (rows, width), 1)
    return (lane // HEAD_DIM) == head


def softmax_rows(queries, key_vectors, allowed):
    scores = jnp.where(allowed, dot(queries, key_vectors, 1, 1) * (HEAD_DIM**-0.5), -1e30)
    shifted = jnp.exp(scores - jnp.max(scores, axis=-1, keepdims=True))
    return shifted / jnp.sum(shifted, axis=-1, keepdims=True)


def attend_kernel(lengths, proj, cosine, sine, q_out, k_out, v_out, o_out):
    rows, width = q_out.shape[1], q_out.shape[2]
    length = lengths[pl.program_id(0)]
    lane = lax.broadcasted_iota(jnp.int32, (rows, width), 1)
    first = (lane % HEAD_DIM) < HEAD_DIM // 2
    turned = []
    for part in range(2):
        values = proj[0, :, part * width : (part + 1) * width]
        turned.append((values * cosine[...] + swap_halves(values, first) * sine[...]).astype(bf16))
    queries, key_vectors = turned
    value_vectors = proj[0, :, 2 * width : 3 * width].astype(bf16)
    q_out[0], k_out[0], v_out[0] = queries, key_vectors, value_vectors
    allowed = allowed_mask(rows, length)
    total = jnp.zeros((rows, width), f32)
    for head in range(width // HEAD_DIM):
        mine = head_lanes(rows, width, head)
        weights = softmax_rows(jnp.where(mine, queries, 0), key_vectors, allowed)
        total += dot(weights.astype(bf16), jnp.where(mine, value_vectors, 0))
    o_out[0] = total.astype(bf16)


def attend(lengths, proj, tables):
    count, rows, triple = proj.shape
    width = triple // 3
    block = pl.BlockSpec((1, rows, width), lambda i: (i, 0, 0))
    table = pl.BlockSpec((rows, width), lambda i: (0, 0))
    return pl.pallas_call(
        attend_kernel,
        grid=(count,),
        in_specs=[
            pl.BlockSpec(memory_space=pltpu.SMEM),
            pl.BlockSpec((1, rows, triple), lambda i: (i, 0, 0)),
            table,
            table,
        ],
        out_specs=[block] * 4,
        out_shape=[jax.ShapeDtypeStruct((count, rows, width), bf16)] * 4,
        compiler_params=pltpu.CompilerParams(vmem_limit_bytes=48 * 2**20),
        cost_estimate=pl.CostEstimate(
            flops=count * rows * rows * width * 16, bytes_accessed=count * rows * width * 24,
            transcendentals=count * rows * rows * 4,
        ),
        name="attend",
    )(lengths, proj, *tables)


def attend_back_kernel(lengths, q_in, k_in, v_in, o_grad, cosine, sine, out):
    rows, width = q_in.shape[1], q_in.shape[2]
    length = lengths[pl.program_id(0)]
    queries, key_vectors, value_vectors, grads = q_in[0], k_in[0], v_in[0], o_grad[0]
    allowed = allowed_mask(rows, length)
    lane = lax.broadcasted_iota(jnp.int32, (rows, width), 1)
    first = (lane % HEAD_DIM) < HEAD_DIM // 2
    grad_q = jnp.zeros((rows, width), f32)
    grad_k = jnp.zeros((rows, width), f32)
    grad_v = jnp.zeros((rows, width), f32)
    for head in range(width // HEAD_DIM):
        mine = head_lanes(rows, width, head)
        q_head = jnp.where(mine, queries, 0)
        g_head = jnp.where(mine, grads, 0)
        weights = softmax_rows(q_head, key_vectors, allowed)
        grad_p = dot(g_head, value_vectors, 1, 1)
        delta = jnp.sum(weights * grad_p, axis=-1, keepdims=True)
        grad_s = jnp.where(allowed, weights * (grad_p - delta), 0.0).astype(bf16)
        grad_q += dot(grad_s, jnp.where(mine, key_vectors, 0))
        grad_k += dot(grad_s, q_head, 0, 0)
        grad_v += dot(weights.astype(bf16), g_head, 0, 0)
    scale = HEAD_DIM**-0.5
    for part, grad in enumerate((grad_q, grad_k)):
        values = (grad * scale).astype(bf16).astype(f32)
        turned = values * cosine[...] - swap_halves(values, first) * sine[...]
        out[0, :, part * width : (part + 1) * width] = turned.astype(bf16)
    out[0, :, 2 * width : 3 * width] = grad_v.astype(bf16)


def attend_back(lengths, queries, key_vectors, value_vectors, grads, tables):
    count, rows, width = queries.shape
    block = pl.BlockSpec((1, rows, width), lambda i: (i, 0, 0))
    table = pl.BlockSpec((rows, width), lambda i: (0, 0))
    return pl.pallas_call(
        attend_back_kernel,
        grid=(count,),
        in_specs=[pl.BlockSpec(memory_space=pltpu.SMEM)] + [block] * 4 + [table] * 2,
        out_specs=pl.BlockSpec((1, rows, 3 * width), lambda i: (i, 0, 0)),
        out_shape=jax.ShapeDtypeStruct((count, rows, 3 * width), bf16),
        compiler_params=pltpu.CompilerParams(vmem_limit_bytes=48 * 2**20),
        cost_estimate=pl.CostEstimate(
            flops=count * rows * rows * width * 40, bytes_accessed=count * rows * width * 14,
            transcendentals=count * rows * rows * 4,
        ),
        name="attend_back",
    )(lengths, queries, key_vectors, value_vectors, grads, *tables)


def to_ranks(columns):
    rows, parts, seqs, units, quad, lanes = columns.shape
    sent = columns.transpose(2, 4, 0, 1, 3, 5).reshape(seqs * quad, rows, parts * units * lanes)
    return lax.all_to_all(sent, RANKS, split_axis=0, concat_axis=0, tiled=True)


def over_planes(rank_rows, seqs):
    planes = lax.all_gather(rank_rows, "grp", axis=0, tiled=False)
    count, ranks, rows, columns = planes.shape
    return (
        planes.reshape(count, seqs, QUAD * rows, columns)
        .transpose(1, 0, 2, 3)
        .reshape(count * ranks * rows, columns)
    )


def back_to_owners(gradient, seqs, grps, parts, units):
    total_rows, columns = gradient.shape
    rows = total_rows // (seqs * grps * QUAD)
    sent = (
        gradient.astype(bf16)
        .reshape(seqs, grps, QUAD * rows, columns)
        .transpose(1, 0, 2, 3)
        .reshape(grps, seqs * QUAD, rows, columns)
    )
    summed = lax.psum_scatter(sent, "grp", scatter_dimension=0, tiled=False)
    held = lax.all_to_all(summed, RANKS, split_axis=0, concat_axis=0, tiled=True)
    lanes = columns // (parts * units)
    return (
        held.reshape(seqs, QUAD, rows, parts, units, lanes)
        .transpose(2, 3, 0, 4, 1, 5)
        .reshape(rows, columns * seqs * QUAD)
        .astype(f32)
    )


def seat_gather(values):
    return lax.all_gather(values, SEATS, axis=0, tiled=True)


def seat_sum(partial):
    return lax.psum_scatter(
        partial.astype(bf16), SEATS, scatter_dimension=0, tiled=True
    ).astype(f32)


def on_device(
    tokens,
    cotangent,
    lengths,
    qkv_weight,
    qkv_moment,
    qkv_square,
    out_weight,
    out_moment,
    out_square,
    up_weight,
    up_moment,
    up_square,
    down_weight,
    down_moment,
    down_square,
    norm_gains,
    gains_moment,
    gains_square,
):
    seqs = lax.axis_size("seq")
    grps = lax.axis_size("grp")
    ranks = seqs * QUAD
    own_rows = tokens.shape[1]
    full_rows = own_rows * seqs
    all_rows = full_rows * QUAD
    shard = qkv_weight.shape[0]
    heads_local = HEADS // ranks
    head_width = heads_local * HEAD_DIM
    units = down_weight.shape[0]
    aligned = out_weight.shape[0] == HEAD_DIM
    tables = rotate_table(full_rows, heads_local)

    inputs = tokens[0].astype(f32)
    positions = lax.axis_index("seq") * own_rows + jnp.arange(own_rows, dtype=jnp.int32)
    grad_output = cotangent[0].astype(f32) * (positions < lengths[0]).astype(f32)[:, None]

    gains_full = lax.all_gather(norm_gains.astype(bf16), EVERY, axis=1, tiled=True).astype(f32)
    gain_first, gain_second = gains_full[0], gains_full[1]
    plane_lengths = lax.all_gather(lengths, ("row", "core"), axis=0, tiled=True)

    qkv_local = over_planes(
        to_ranks(
            qkv_weight.astype(bf16).reshape(shard, 3, seqs, heads_local, QUAD, HEAD_DIM)
        ),
        seqs,
    )
    x_all = seat_gather(tokens[0]).astype(f32)
    scale_all = lax.rsqrt(jnp.mean(x_all * x_all, axis=-1, keepdims=True) + NORM_EPSILON)
    first_norm = (x_all * scale_all * gain_first).astype(bf16)
    projected = dot(first_norm, qkv_local).reshape(QUAD, full_rows, 3 * head_width)
    queries, key_vectors, value_vectors, attended = attend(plane_lengths, projected, tables)
    mixed = attended.reshape(all_rows, head_width)

    out_low = out_weight.astype(bf16)
    if aligned:
        out_local = lax.all_gather(out_low, "grp", axis=0, tiled=True)
    else:
        out_all = lax.all_gather(out_low, EVERY, axis=0, tiled=True)
        out_all = out_all.reshape(seqs, heads_local, QUAD, HEAD_DIM, D)
        seat = lax.axis_index("row") * 2 + lax.axis_index("core")
        out_local = lax.dynamic_index_in_dim(
            lax.dynamic_index_in_dim(out_all, lax.axis_index("seq"), 0, False), seat, 1, False
        ).reshape(head_width, D)
    up_local = over_planes(
        to_ranks(up_weight.astype(bf16).reshape(shard, 2, seqs, grps, QUAD, units)), seqs
    )
    down_local = lax.all_gather(down_weight.astype(bf16), "grp", axis=0, tiled=True)

    residual = inputs + seat_sum(dot(mixed, out_local))
    second_scale = lax.rsqrt(jnp.mean(residual * residual, axis=-1, keepdims=True) + NORM_EPSILON)
    second_norm = seat_gather((residual * second_scale * gain_second).astype(bf16))
    both_parts = dot(second_norm, up_local)
    hidden_width = both_parts.shape[1] // 2
    gate_part = both_parts[:, :hidden_width]
    up_part = both_parts[:, hidden_width:]
    gate_sigmoid = jax.nn.sigmoid(gate_part)
    activated = gate_part * gate_sigmoid
    hidden = (activated * up_part).astype(bf16)
    block_output = (residual + seat_sum(dot(hidden, down_local))).astype(bf16)

    grad_low = seat_gather(grad_output.astype(bf16))
    down_term = dot(hidden, grad_low, 0, 0).astype(bf16).reshape(grps, units, D)
    down_sum = lax.psum_scatter(down_term, "grp", scatter_dimension=0, tiled=False).astype(f32)
    grad_hidden = dot(grad_low, down_local, 1, 1)
    grad_gate = grad_hidden * up_part * gate_sigmoid * (1.0 + gate_part * (1.0 - gate_sigmoid))
    grad_up = grad_hidden * activated
    grad_both = jnp.concatenate([grad_gate, grad_up], axis=1).astype(bf16)
    grad_second = seat_sum(dot(grad_both, up_local, 1, 1))
    up_sum = back_to_owners(dot(second_norm, grad_both, 0, 0), seqs, grps, 2, grps)
    residual_back, gain_grad_second = norm_back(residual, second_scale, gain_second, grad_second)
    grad_residual = grad_output + residual_back
    grad_attention = seat_gather(grad_residual.astype(bf16))
    grad_mixed = dot(grad_attention, out_local, 1, 1).astype(bf16)
    out_term = dot(mixed, grad_attention, 0, 0).astype(bf16)
    if aligned:
        out_sum = lax.psum_scatter(
            out_term.reshape(grps, HEAD_DIM, D), "grp", scatter_dimension=0, tiled=False
        ).astype(f32)
    else:
        placed_term = jnp.zeros((seqs, QUAD, heads_local, HEAD_DIM, D), bf16)
        placed_term = lax.dynamic_update_slice(
            placed_term,
            out_term.reshape(1, 1, heads_local, HEAD_DIM, D),
            (lax.axis_index("seq"), seat, 0, 0, 0),
        )
        out_sum = lax.psum_scatter(
            placed_term.transpose(0, 2, 1, 3, 4).reshape(D, D),
            EVERY,
            scatter_dimension=0,
            tiled=True,
        ).astype(f32)
    grad_projected = attend_back(
        plane_lengths,
        queries,
        key_vectors,
        value_vectors,
        grad_mixed.reshape(QUAD, full_rows, head_width),
        tables,
    ).reshape(all_rows, 3 * head_width)
    qkv_sum = back_to_owners(
        dot(first_norm, grad_projected, 0, 0), seqs, grps, 3, heads_local
    )
    grad_first = seat_sum(dot(grad_projected, qkv_local, 1, 1))
    first_scale = lax.rsqrt(jnp.mean(inputs * inputs, axis=-1, keepdims=True) + NORM_EPSILON)
    input_back, gain_grad_first = norm_back(inputs, first_scale, gain_first, grad_first)
    input_grad = grad_residual + input_back
    gains_sum = lax.psum_scatter(
        jnp.stack([gain_grad_first, gain_grad_second], axis=1),
        EVERY,
        scatter_dimension=0,
        tiled=True,
    )
    qkv_updated, qkv_moment_new, qkv_square_new = adam_update(
        qkv_weight, qkv_moment, qkv_square, qkv_sum, D ** (-0.5)
    )
    out_updated, out_moment_new, out_square_new = adam_update(
        out_weight, out_moment, out_square, out_sum, (D // 128) ** (-0.5)
    )
    up_updated, up_moment_new, up_square_new = adam_update(
        up_weight, up_moment, up_square, up_sum, D ** (-0.5)
    )
    down_updated, down_moment_new, down_square_new = adam_update(
        down_weight, down_moment, down_square, down_sum, FF ** (-0.5)
    )
    gains_updated, gains_moment_new, gains_square_new = adam_update(
        norm_gains, gains_moment, gains_square, gains_sum.T, 0.3
    )
    return (
        block_output[None],
        input_grad[None],
        qkv_updated,
        qkv_moment_new,
        qkv_square_new,
        qkv_updated.astype(bf16),
        out_updated,
        out_moment_new,
        out_square_new,
        out_updated.astype(bf16),
        up_updated,
        up_moment_new,
        up_square_new,
        up_updated.astype(bf16),
        down_updated,
        down_moment_new,
        down_square_new,
        down_updated.astype(bf16),
        gains_updated,
        gains_moment_new,
        gains_square_new,
    )


def solution(mesh):
    seqs, rest = mesh.shape["seq"], mesh.shape["fsdp"]
    planes = Mesh(
        mesh.devices.reshape(seqs, rest // QUAD, 2, 2), ("seq", "grp", "row", "core")
    )
    rows = P(("grp", "row", "core"), "seq", None)
    shards = P(EVERY, None)
    gains = P(None, EVERY)
    return jax.shard_map(
        on_device,
        mesh=planes,
        in_specs=(rows, rows, P(("grp", "row", "core"))) + (shards,) * 12 + (gains,) * 3,
        out_specs=(rows, rows) + (shards,) * 16 + (gains,) * 3,
        check_vma=False,
    )
```

```python
import math

import jax
import jax.numpy as jnp
from jax import lax
from jax.experimental import pallas as pl
from jax.experimental.pallas import tpu as pltpu
from jax.sharding import Mesh, PartitionSpec as P

D = 2048
HEADS = 32
HEAD_DIM = 64
FF = 4096
WINDOW = 128
STEP = 5


NORM_EPSILON = 1e-05
MOMENT_DECAY = 0.5
WEIGHT_DECAY = 0.1
ADAM_EPSILON = 1e-08

SEATS = ("row", "core", "seq")
RANKS = ("seq", "row", "core")
EVERY = ("seq", "grp", "row", "core")
QUAD = 4
VMEM_LIMIT = 63 * 2**20

bf16 = jnp.bfloat16
f32 = jnp.float32


def rotate_table(length, copies):
    halves = HEAD_DIM // 2
    freqs = jnp.exp(-math.log(10000.0) * 2.0 * jnp.arange(halves).astype(f32) / HEAD_DIM)
    angles = jnp.arange(length, dtype=jnp.int32).astype(f32)[:, None] * freqs[None, :]
    cosine, sine = jnp.cos(angles), jnp.sin(angles)
    return (
        jnp.tile(jnp.concatenate([cosine, cosine], axis=1), (1, copies)),
        jnp.tile(jnp.concatenate([-sine, sine], axis=1), (1, copies)),
    )


def adam_update(weight, moment, square, gradient, step_rate):
    moment_new = MOMENT_DECAY * moment + (1.0 - MOMENT_DECAY) * gradient
    square_new = MOMENT_DECAY * square + (1.0 - MOMENT_DECAY) * gradient * gradient
    correction = 1.0 - MOMENT_DECAY**STEP
    update = moment_new / correction / (jnp.sqrt(square_new / correction) + ADAM_EPSILON)
    return (weight - step_rate * (update + WEIGHT_DECAY * weight), moment_new, square_new)


def dot(a, b, lhs=1, rhs=0):
    return lax.dot_general(a, b, (((lhs,), (rhs,)), ((), ())), preferred_element_type=f32)


def swap_halves(values, first):
    width = values.shape[1]
    half = HEAD_DIM // 2
    return jnp.where(
        first, pltpu.roll(values, width - half, 1), pltpu.roll(values, half, 1)
    )


def allowed_mask(rows, length):
    row = lax.broadcasted_iota(jnp.int32, (rows, rows), 0)
    col = lax.broadcasted_iota(jnp.int32, (rows, rows), 1)
    return (col <= row) & (row - col < WINDOW) & (col < length)


def head_lanes(rows, width, head):
    lane = lax.broadcasted_iota(jnp.int32, (rows, width), 1)
    return (lane // HEAD_DIM) == head


def softmax_rows(queries, key_vectors, allowed):
    scores = jnp.where(allowed, dot(queries, key_vectors, 1, 1) * (HEAD_DIM**-0.5), -1e30)
    shifted = jnp.exp(scores - jnp.max(scores, axis=-1, keepdims=True))
    return shifted / jnp.sum(shifted, axis=-1, keepdims=True)


def attend_kernel(lengths, proj, cosine, sine, q_out, k_out, v_out, o_out):
    rows, width = q_out.shape[1], q_out.shape[2]
    length = lengths[pl.program_id(0)]
    lane = lax.broadcasted_iota(jnp.int32, (rows, width), 1)
    first = (lane % HEAD_DIM) < HEAD_DIM // 2
    turned = []
    for part in range(2):
        values = proj[0, :, part * width : (part + 1) * width]
        turned.append((values * cosine[...] + swap_halves(values, first) * sine[...]).astype(bf16))
    queries, key_vectors = turned
    value_vectors = proj[0, :, 2 * width : 3 * width].astype(bf16)
    q_out[0], k_out[0], v_out[0] = queries, key_vectors, value_vectors
    allowed = allowed_mask(rows, length)
    total = jnp.zeros((rows, width), f32)
    for head in range(width // HEAD_DIM):
        mine = head_lanes(rows, width, head)
        weights = softmax_rows(jnp.where(mine, queries, 0), key_vectors, allowed)
        total += dot(weights.astype(bf16), jnp.where(mine, value_vectors, 0))
    o_out[0] = total.astype(bf16)


def attend(lengths, proj, tables):
    count, rows, triple = proj.shape
    width = triple // 3
    block = pl.BlockSpec((1, rows, width), lambda i: (i, 0, 0))
    table = pl.BlockSpec((rows, width), lambda i: (0, 0))
    return pl.pallas_call(
        attend_kernel,
        grid=(count,),
        in_specs=[
            pl.BlockSpec(memory_space=pltpu.SMEM),
            pl.BlockSpec((1, rows, triple), lambda i: (i, 0, 0)),
            table,
            table,
        ],
        out_specs=[block] * 4,
        out_shape=[jax.ShapeDtypeStruct((count, rows, width), bf16)] * 4,
        compiler_params=pltpu.CompilerParams(vmem_limit_bytes=48 * 2**20),
        cost_estimate=pl.CostEstimate(
            flops=count * rows * rows * width * 16, bytes_accessed=count * rows * width * 24,
            transcendentals=count * rows * rows * 4,
        ),
        name="attend",
    )(lengths, proj, *tables)


def attention_grads(length, queries, key_vectors, value_vectors, grads):
    rows, width = queries.shape
    allowed = allowed_mask(rows, length)
    grad_q = jnp.zeros((rows, width), f32)
    grad_k = jnp.zeros((rows, width), f32)
    grad_v = jnp.zeros((rows, width), f32)
    for head in range(width // HEAD_DIM):
        mine = head_lanes(rows, width, head)
        q_head = jnp.where(mine, queries, 0)
        g_head = jnp.where(mine, grads, 0)
        weights = softmax_rows(q_head, key_vectors, allowed)
        grad_p = dot(g_head, value_vectors, 1, 1)
        delta = jnp.sum(weights * grad_p, axis=-1, keepdims=True)
        grad_s = jnp.where(allowed, weights * (grad_p - delta), 0.0).astype(bf16)
        grad_q += dot(grad_s, jnp.where(mine, key_vectors, 0))
        grad_k += dot(grad_s, q_head, 0, 0)
        grad_v += dot(weights.astype(bf16), g_head, 0, 0)
    return grad_q, grad_k, grad_v


MESH = pl.DeviceIdType.MESH
RELATIONS = tuple((a, b, d) for a in range(2) for b in range(2) for d in range(2))[1:]


class Place:
    def __init__(self, grps):
        self.grps = grps
        self.s = lax.axis_index("seq")
        self.g = lax.axis_index("grp")
        self.r = lax.axis_index("row")
        self.c = lax.axis_index("core")

    def peer(self, relation):
        ds, dr, dc = relation
        return ((self.s + ds) % 2, self.g, (self.r + dr) % 2, (self.c + dc) % 2)

    def plane(self, dz):
        return (self.s, (self.g + dz) % self.grps, self.r, self.c)

    def rank(self, relation=(0, 0, 0)):
        s, _, r, c = self.peer(relation)
        return (s * 2 + r) * 2 + c

    def seat(self, relation=(0, 0, 0)):
        s, _, r, c = self.peer(relation)
        return (r * 2 + c) * 2 + s

    def corner(self, relation=(0, 0, 0)):
        s, _, r, _ = self.peer(relation)
        return r * 2 + s

    def greet(self):
        barrier = pltpu.get_barrier_semaphore()
        for relation in RELATIONS:
            pl.semaphore_signal(barrier, inc=1, device_id=self.peer(relation), device_id_type=MESH)
        for dz in range(1, self.grps):
            pl.semaphore_signal(barrier, inc=1, device_id=self.plane(dz), device_id_type=MESH)
        pl.semaphore_wait(barrier, len(RELATIONS) + self.grps - 1)


SIBLING = (0, 0, 1)
ACROSS = ((1, 0, 0), (0, 1, 0), (1, 1, 0))


def remote(src, dst, send_sem, recv_sem, device):
    return pltpu.make_async_remote_copy(
        src_ref=src,
        dst_ref=dst,
        send_sem=send_sem,
        recv_sem=recv_sem,
        device_id=device,
        device_id_type=MESH,
    )


class PlaneSum:
    def __init__(self, place, part, near, far, sems):
        self.place, self.part, self.near, self.far = place, part, near, far
        self.near_send, self.near_recv, self.far_send, self.far_recv = sems
        self.first, self.second = [], []

    def start_near(self):
        place = self.place
        for k in range(4):
            block = ((k // 2) * 2 + (1 - place.c)) * 2 + k % 2
            copy = remote(
                self.part.at[block],
                self.near.at[k],
                self.near_send.at[k],
                self.near_recv.at[k],
                place.peer(SIBLING),
            )
            copy.start()
            self.first.append(copy)

    def start_far(self):
        place = self.place
        for copy in self.first:
            copy.wait()
        for k in range(4):
            block = ((k // 2) * 2 + place.c) * 2 + k % 2
            self.near[k] = (self.part[block].astype(f32) + self.near[k].astype(f32)).astype(bf16)
        for d, relation in enumerate(ACROSS):
            copy = remote(
                self.near.at[place.corner(relation)],
                self.far.at[d],
                self.far_send.at[d],
                self.far_recv.at[d],
                place.peer(relation),
            )
            copy.start()
            self.second.append(copy)

    def finish(self):
        for copy in self.second:
            copy.wait()

    def chunk(self, lanes):
        total = self.near[self.place.corner(), :, lanes].astype(f32)
        for d in range(3):
            total += self.far[d, :, lanes].astype(f32)
        return total


class PlaneGather:
    def __init__(self, place, blocks, send, recv):
        self.place, self.blocks, self.send, self.recv = place, blocks, send, recv
        self.first, self.second = [], []

    def copy(self, block, sem, relation):
        copy = remote(
            self.blocks.at[block],
            self.blocks.at[block],
            self.send.at[sem],
            self.recv.at[sem],
            self.place.peer(relation),
        )
        copy.start()
        return copy

    def start(self):
        mine = self.place.seat()
        self.first = [self.copy(mine, d, relation) for d, relation in enumerate(ACROSS)]
        self.first.append(self.copy(mine, 3, SIBLING))

    def forward(self):
        for d, relation in enumerate(ACROSS):
            self.first[d].wait_recv()
            self.second.append(self.copy(self.place.seat(relation), 4 + d, SIBLING))

    def finish(self):
        for copy in self.first[:3]:
            copy.wait_send()
        self.first[3].wait()
        for copy in self.second:
            copy.wait()


class ToOwners:
    def __init__(self, place, shares, landed, send, recv, own):
        self.copies = []
        for dz in range(1, place.grps):
            copy = remote(
                shares.at[(place.g + dz) % place.grps],
                landed.at[dz],
                send.at[dz],
                recv.at[dz],
                place.plane(dz),
            )
            copy.start()
            self.copies.append(copy)
        copy = pltpu.make_async_copy(shares.at[place.g], landed.at[0], own)
        copy.start()
        self.copies.append(copy)

    def finish(self):
        for copy in self.copies:
            copy.wait()


class Exchange:
    def __init__(self, place, blocks, held, send, recv, own):
        mine = place.rank()
        self.copies = []
        for n, relation in enumerate(RELATIONS):
            copy = remote(
                blocks.at[place.rank(relation)],
                held.at[mine],
                send.at[n],
                recv.at[n],
                place.peer(relation),
            )
            copy.start()
            self.copies.append(copy)
        copy = pltpu.make_async_copy(blocks.at[mine], held.at[mine], own)
        copy.start()
        self.copies.append(copy)

    def finish(self):
        for copy in self.copies:
            copy.wait()


LANES = 512


def lanes_of(n, width=LANES):
    return pl.ds(pl.multiple_of(n * width, width), width)


def shares_of(seq, values, weight, part):
    rows = part.shape[1]

    @pl.loop(0, part.shape[2] // LANES)
    def _(n):
        product = dot(values[seq], weight[lanes_of(n)], 1, 1)
        part[2 * seq, :, lanes_of(n)] = product[:rows].astype(bf16)
        part[2 * seq + 1, :, lanes_of(n)] = product[rows:].astype(bf16)


def over_tokens(first, lanes, second, other):
    total = dot(first[0, :, lanes], second[0, :, other], 0, 0)
    for seq in range(1, first.shape[0]):
        total += dot(first[seq, :, lanes], second[seq, :, other], 0, 0)
    return total


def row_shares(first, second, shares):
    grps, seqs, rows, _ = shares.shape
    width = 256
    pieces = width // rows

    @pl.loop(0, first.shape[2] // width)
    def _(b):
        product = over_tokens(first, lanes_of(b, width), second, slice(None)).astype(bf16)
        for p in range(pieces):
            index = b * pieces + p
            shares[index % grps, index // grps] = product[p * rows : (p + 1) * rows]


def summed_rows(landed, blocks):
    seqs, rows = landed.shape[1], blocks.shape[1]
    for seq in range(seqs):
        for quad in range(QUAD):
            block = slice(quad * rows, (quad + 1) * rows)
            total = landed[0, seq, block].astype(f32)
            for dz in range(1, landed.shape[0]):
                total += landed[dz, seq, block].astype(f32)
            blocks[seq * QUAD + quad] = total.astype(bf16)


def back_kernel(
    grps,
    aligned,
    lengths,
    gains,
    cosine,
    sine,
    residual,
    own_tokens,
    own_grad,
    dgu_h,
    up_h,
    hidden_h,
    grad_h,
    second_h,
    first_h,
    out_h,
    qkv_h,
    q_h,
    k_h,
    v_h,
    o_h,
    input_grad,
    gains_sum,
    down_landed,
    out_landed,
    up_held,
    qkv_held,
    up_landed,
    qkv_landed,
    wide,
    up,
    hidden,
    acts,
    second,
    out_w,
    qkv,
    part,
    near,
    far,
    blocks,
    turned,
    down_share,
    up_share,
    out_share,
    qkv_share,
    up_sum,
    qkv_sum,
    gain_part,
    gain_plane,
    gain_far,
    load,
    near_send,
    near_recv,
    far_send,
    far_recv,
    all_send,
    all_recv,
    z_send,
    z_recv,
    swap_send,
    swap_recv,
    gain_send,
    gain_recv,
    own_sem,
):
    place = Place(grps)
    rows = residual.shape[0]
    gain_part[...] = jnp.zeros_like(gain_part)
    count, full_rows, head_width = q_h.shape

    def fetch(src, dst, n):
        copy = pltpu.make_async_copy(src, dst, load.at[n])
        copy.start()
        return copy

    loads = [fetch(dgu_h, wide, 0), fetch(up_h, up, 1)]
    later = [fetch(hidden_h, hidden, 2), fetch(grad_h, acts, 3), fetch(second_h, second, 4)]
    weights = [fetch(out_h, out_w, 5), fetch(qkv_h, qkv, 6)]
    place.greet()
    for copy in loads:
        copy.wait()

    sums = (near_send, near_recv, far_send, far_recv)
    second_sum = PlaneSum(place, part, near, far, sums)
    for r in range(2):
        shares_of(2 * r + 1 - place.c, wide, up, part)
    second_sum.start_near()
    for r in range(2):
        shares_of(2 * r + place.c, wide, up, part)

    for copy in later[:2]:
        copy.wait()
    units = down_share.shape[1]
    width = min(256, hidden.shape[2])

    @pl.loop(0, hidden.shape[2] // width)
    def _(b):
        for half in range(2):
            lanes = slice(half * D // 2, (half + 1) * D // 2)
            product = over_tokens(hidden, lanes_of(b, width), acts, lanes).astype(bf16)
            for p in range(width // units):
                down_share[b * (width // units) + p, :, lanes] = product[p * units : (p + 1) * units]

    down_out = ToOwners(place, down_share, down_landed, z_send.at[0], z_recv.at[0], own_sem.at[0])
    fetch_first = fetch(first_h, acts, 3)
    second_sum.start_far()
    later[2].wait()
    row_shares(second, wide, up_share)
    up_out = ToOwners(place, up_share, up_landed, z_send.at[1], z_recv.at[1], own_sem.at[1])
    heads = [
        fetch(ref, wide.at[:, :, n * head_width : (n + 1) * head_width], 7 + n)
        for n, ref in enumerate((q_h, k_h, v_h, o_h))
    ]

    second_sum.finish()
    mine = place.seat()
    inner = jnp.zeros((rows, 1), f32)
    squares = jnp.zeros((rows, 1), f32)
    for n in range(D // LANES):
        lanes = slice(n * LANES, (n + 1) * LANES)
        grad = second_sum.chunk(lanes)
        values = residual[:, lanes]
        inner += jnp.sum(grad * gains[1:2, lanes] * values, axis=-1, keepdims=True)
        squares += jnp.sum(values * values, axis=-1, keepdims=True)
    scale = lax.rsqrt(squares / D + NORM_EPSILON)
    inner = inner / D
    for n in range(D // LANES):
        lanes = slice(n * LANES, (n + 1) * LANES)
        grad, values = second_sum.chunk(lanes), residual[:, lanes]
        gain_part[1:2, lanes] = jnp.sum(grad * values * scale, axis=0, keepdims=True)
        total = own_grad[:, lanes].astype(f32) + scale * (
            grad * gains[1:2, lanes] - values * scale * scale * inner
        )
        input_grad[:, lanes] = total
        blocks[mine, :, lanes] = total.astype(bf16)

    gather = PlaneGather(place, blocks, all_send, all_recv)
    gather.start()
    gather.forward()
    for copy in weights + heads:
        copy.wait()
    gather.finish()

    lane = lax.broadcasted_iota(jnp.int32, (full_rows, head_width), 1)
    first_half = (lane % HEAD_DIM) < HEAD_DIM // 2

    @pl.loop(0, count)
    def _(seq):
        grads = jnp.concatenate(
            [dot(blocks[2 * seq], out_w[...], 1, 1), dot(blocks[2 * seq + 1], out_w[...], 1, 1)],
            axis=0,
        ).astype(bf16)
        queries = wide[seq, :, 0:head_width]
        key_vectors = wide[seq, :, head_width : 2 * head_width]
        value_vectors = wide[seq, :, 2 * head_width : 3 * head_width]
        grad_q, grad_k, grad_v = attention_grads(
            lengths[seq], queries, key_vectors, value_vectors, grads
        )
        for n, grad in enumerate((grad_q, grad_k)):
            values = (grad * HEAD_DIM**-0.5).astype(bf16).astype(f32)
            back = values * cosine[...] - swap_halves(values, first_half) * sine[...]
            turned[seq, :, n * head_width : (n + 1) * head_width] = back.astype(bf16)
        turned[seq, :, 2 * head_width : 3 * head_width] = grad_v.astype(bf16)

    fetch_first.wait()
    row_shares(acts, turned, qkv_share)
    qkv_out = ToOwners(place, qkv_share, qkv_landed, z_send.at[2], z_recv.at[2], own_sem.at[2])

    first_sum = PlaneSum(place, part, near, far, sums)
    for r in range(2):
        shares_of(2 * r + 1 - place.c, turned, qkv, part)
    first_sum.start_near()
    for r in range(2):
        shares_of(2 * r + place.c, turned, qkv, part)
    first_sum.start_far()

    out_rows = out_share.shape[1]

    @pl.loop(0, D // LANES)
    def _(n):
        lanes = lanes_of(n)
        total = jnp.zeros((head_width, LANES), f32)
        for seq in range(count):
            values = wide[seq, :, 3 * head_width : 4 * head_width].astype(f32)
            total += dot(values[:rows].astype(bf16), blocks[2 * seq, :, lanes], 0, 0)
            total += dot(values[rows:].astype(bf16), blocks[2 * seq + 1, :, lanes], 0, 0)
        total = total.astype(bf16)
        for j in range(out_share.shape[0]):
            out_share[j, :, lanes] = total[j * out_rows : (j + 1) * out_rows]

    if aligned:
        out_out = ToOwners(place, out_share, out_landed, z_send.at[3], z_recv.at[3], own_sem.at[3])
    else:
        out_out = pltpu.make_async_copy(out_share, out_landed, own_sem.at[3])
        out_out.start()

    first_sum.finish()
    inner = jnp.zeros((rows, 1), f32)
    squares = jnp.zeros((rows, 1), f32)
    for n in range(D // LANES):
        lanes = slice(n * LANES, (n + 1) * LANES)
        grad = first_sum.chunk(lanes)
        values = own_tokens[:, lanes].astype(f32)
        inner += jnp.sum(grad * gains[0:1, lanes] * values, axis=-1, keepdims=True)
        squares += jnp.sum(values * values, axis=-1, keepdims=True)
    scale = lax.rsqrt(squares / D + NORM_EPSILON)
    inner = inner / D
    for n in range(D // LANES):
        lanes = slice(n * LANES, (n + 1) * LANES)
        grad, values = first_sum.chunk(lanes), own_tokens[:, lanes].astype(f32)
        gain_part[0:1, lanes] = jnp.sum(grad * values * scale, axis=0, keepdims=True)
        input_grad[:, lanes] += scale * (
            grad * gains[0:1, lanes] - values * scale * scale * inner
        )

    gain_copies = []
    for n, relation in enumerate(RELATIONS):
        copy = remote(
            gain_part, gain_plane.at[n], gain_send.at[n], gain_recv.at[n], place.peer(relation)
        )
        copy.start()
        gain_copies.append(copy)

    up_out.finish()
    landed = pltpu.make_async_copy(up_landed, up_share, load.at[1])
    landed.start()
    for copy in gain_copies:
        copy.wait()
    total = gain_part[...]
    for n in range(len(RELATIONS)):
        total += gain_plane[n]
    gain_far[0] = total
    gain_copies = []
    for dz in range(1, grps):
        copy = remote(
            gain_far.at[0],
            gain_far.at[dz],
            gain_send.at[7 + dz],
            gain_recv.at[7 + dz],
            place.plane(dz),
        )
        copy.start()
        gain_copies.append(copy)
    landed.wait()
    summed_rows(up_share, up_sum)
    up_swap = Exchange(place, up_sum, up_held, swap_send.at[0], swap_recv.at[0], own_sem.at[4])
    for copy in gain_copies:
        copy.wait()
    total = gain_far[0]
    for dz in range(1, grps):
        total += gain_far[dz]
    gains_sum[...] = total

    qkv_out.finish()
    landed = pltpu.make_async_copy(qkv_landed, qkv_share, load.at[6])
    landed.start()
    landed.wait()
    summed_rows(qkv_share, qkv_sum)
    qkv_swap = Exchange(place, qkv_sum, qkv_held, swap_send.at[1], swap_recv.at[1], own_sem.at[5])
    if aligned:
        out_out.finish()
    else:
        out_out.wait()
    down_out.finish()
    up_swap.finish()
    qkv_swap.finish()


def backward(
    grps,
    aligned,
    lengths,
    gains,
    tables,
    residual,
    own_tokens,
    own_grad,
    grad_both,
    up_local,
    hidden,
    grad_low,
    second_norm,
    first_norm,
    out_local,
    qkv_local,
    heads,
):
    rows = residual.shape[0]
    count, full_rows, head_width = heads[0].shape
    seqs = full_rows // rows
    ranks = seqs * QUAD
    units = hidden.shape[2] // grps
    both = grad_both.shape[2]
    quad_rows = D // (seqs * grps)
    shard = quad_rows // QUAD
    out_rows = head_width // grps if aligned else HEAD_DIM
    triple = 3 * head_width
    out_count = head_width // out_rows
    hbm = pl.BlockSpec(memory_space=pl.ANY)
    vmem = pl.BlockSpec(memory_space=pltpu.VMEM)
    shape = jax.ShapeDtypeStruct
    dma = pltpu.SemaphoreType.DMA
    return pl.pallas_call(
        lambda *refs: back_kernel(grps, aligned, *refs),
        in_specs=[pl.BlockSpec(memory_space=pltpu.SMEM)] + [vmem] * 6 + [hbm] * 12,
        out_specs=[vmem] * 2 + [hbm] * 6,
        out_shape=[
            shape((rows, D), f32),
            shape((8, D), f32),
            shape((grps, units, D), bf16),
            shape((out_count, out_rows, D), bf16),
            shape((ranks, shard, both), bf16),
            shape((ranks, shard, triple), bf16),
            shape((grps, seqs, quad_rows, both), bf16),
            shape((grps, seqs, quad_rows, triple), bf16),
        ],
        scratch_shapes=[
            pltpu.VMEM((count, full_rows, both), bf16),
            pltpu.VMEM((D, both), bf16),
            pltpu.VMEM((count, full_rows, hidden.shape[2]), bf16),
            pltpu.VMEM((count, full_rows, D), bf16),
            pltpu.VMEM((count, full_rows, D), bf16),
            pltpu.VMEM((head_width, D), bf16),
            pltpu.VMEM((D, triple), bf16),
            pltpu.VMEM((ranks, rows, D), bf16),
            pltpu.VMEM((4, rows, D), bf16),
            pltpu.VMEM((3, rows, D), bf16),
            pltpu.VMEM((ranks, rows, D), bf16),
            pltpu.VMEM((count, full_rows, triple), bf16),
            pltpu.VMEM((grps, units, D), bf16),
            pltpu.VMEM((grps, seqs, quad_rows, both), bf16),
            pltpu.VMEM((out_count, out_rows, D), bf16),
            pltpu.VMEM((grps, seqs, quad_rows, triple), bf16),
            pltpu.VMEM((ranks, shard, both), bf16),
            pltpu.VMEM((ranks, shard, triple), bf16),
            pltpu.VMEM((8, D), f32),
            pltpu.VMEM((7, 8, D), f32),
            pltpu.VMEM((grps, 8, D), f32),
            dma((11,)),
            dma((4,)),
            dma((4,)),
            dma((3,)),
            dma((3,)),
            dma((7,)),
            dma((7,)),
            dma((4, grps)),
            dma((4, grps)),
            dma((2, 7)),
            dma((2, 7)),
            dma((7 + grps,)),
            dma((7 + grps,)),
            dma((6,)),
        ],
        compiler_params=pltpu.CompilerParams(
            collective_id=0, has_side_effects=True, vmem_limit_bytes=VMEM_LIMIT
        ),
        cost_estimate=pl.CostEstimate(
            flops=30 * 10**9, bytes_accessed=60 * 2**20, transcendentals=2 * 10**6
        ),
        name="backward",
    )(
        lengths,
        gains,
        *tables,
        residual,
        own_tokens,
        own_grad,
        grad_both,
        up_local,
        hidden,
        grad_low,
        second_norm,
        first_norm,
        out_local,
        qkv_local,
        *heads,
    )


def to_ranks(columns):
    rows, parts, seqs, units, quad, lanes = columns.shape
    sent = columns.transpose(2, 4, 0, 1, 3, 5).reshape(seqs * quad, rows, parts * units * lanes)
    return lax.all_to_all(sent, RANKS, split_axis=0, concat_axis=0, tiled=True)


def over_planes(rank_rows, seqs):
    planes = lax.all_gather(rank_rows, "grp", axis=0, tiled=False)
    count, ranks, rows, columns = planes.shape
    return (
        planes.reshape(count, seqs, QUAD * rows, columns)
        .transpose(1, 0, 2, 3)
        .reshape(count * ranks * rows, columns)
    )


def in_own_rows(held, seqs, parts, units):
    ranks, rows, columns = held.shape
    lanes = columns // (parts * units)
    return (
        held.reshape(seqs, QUAD, rows, parts, units, lanes)
        .transpose(2, 3, 0, 4, 1, 5)
        .reshape(rows, columns * ranks)
        .astype(f32)
    )


def seat_gather(values):
    return lax.all_gather(values, SEATS, axis=0, tiled=True)


def seat_sum(partial):
    return lax.psum_scatter(
        partial.astype(bf16), SEATS, scatter_dimension=0, tiled=True
    ).astype(f32)


def on_device(
    tokens,
    cotangent,
    lengths,
    qkv_weight,
    qkv_moment,
    qkv_square,
    out_weight,
    out_moment,
    out_square,
    up_weight,
    up_moment,
    up_square,
    down_weight,
    down_moment,
    down_square,
    norm_gains,
    gains_moment,
    gains_square,
):
    seqs = lax.axis_size("seq")
    grps = lax.axis_size("grp")
    ranks = seqs * QUAD
    own_rows = tokens.shape[1]
    full_rows = own_rows * seqs
    all_rows = full_rows * QUAD
    shard = qkv_weight.shape[0]
    heads_local = HEADS // ranks
    head_width = heads_local * HEAD_DIM
    units = down_weight.shape[0]
    aligned = out_weight.shape[0] == HEAD_DIM
    tables = rotate_table(full_rows, heads_local)

    inputs = tokens[0].astype(f32)
    positions = lax.axis_index("seq") * own_rows + jnp.arange(own_rows, dtype=jnp.int32)
    grad_output = cotangent[0].astype(f32) * (positions < lengths[0]).astype(f32)[:, None]

    gains_full = lax.all_gather(norm_gains.astype(bf16), EVERY, axis=1, tiled=True).astype(f32)
    gain_first, gain_second = gains_full[0], gains_full[1]
    plane_lengths = lax.all_gather(lengths, ("row", "core"), axis=0, tiled=True)

    qkv_local = over_planes(
        to_ranks(
            qkv_weight.astype(bf16).reshape(shard, 3, seqs, heads_local, QUAD, HEAD_DIM)
        ),
        seqs,
    )
    x_all = seat_gather(tokens[0]).astype(f32)
    scale_all = lax.rsqrt(jnp.mean(x_all * x_all, axis=-1, keepdims=True) + NORM_EPSILON)
    first_norm = (x_all * scale_all * gain_first).astype(bf16)
    projected = dot(first_norm, qkv_local).reshape(QUAD, full_rows, 3 * head_width)
    queries, key_vectors, value_vectors, attended = attend(plane_lengths, projected, tables)
    mixed = attended.reshape(all_rows, head_width)

    out_low = out_weight.astype(bf16)
    if aligned:
        out_local = lax.all_gather(out_low, "grp", axis=0, tiled=True)
    else:
        out_all = lax.all_gather(out_low, EVERY, axis=0, tiled=True)
        out_all = out_all.reshape(seqs, heads_local, QUAD, HEAD_DIM, D)
        seat = lax.axis_index("row") * 2 + lax.axis_index("core")
        out_local = lax.dynamic_index_in_dim(
            lax.dynamic_index_in_dim(out_all, lax.axis_index("seq"), 0, False), seat, 1, False
        ).reshape(head_width, D)
    up_local = over_planes(
        to_ranks(up_weight.astype(bf16).reshape(shard, 2, seqs, grps, QUAD, units)), seqs
    )
    down_local = lax.all_gather(down_weight.astype(bf16), "grp", axis=0, tiled=True)

    residual = inputs + seat_sum(dot(mixed, out_local))
    second_scale = lax.rsqrt(jnp.mean(residual * residual, axis=-1, keepdims=True) + NORM_EPSILON)
    second_norm = seat_gather((residual * second_scale * gain_second).astype(bf16))
    both_parts = dot(second_norm, up_local)
    hidden_width = both_parts.shape[1] // 2
    gate_part = both_parts[:, :hidden_width]
    up_part = both_parts[:, hidden_width:]
    gate_sigmoid = jax.nn.sigmoid(gate_part)
    activated = gate_part * gate_sigmoid
    hidden = (activated * up_part).astype(bf16)
    block_output = (residual + seat_sum(dot(hidden, down_local))).astype(bf16)

    own_grad = grad_output.astype(bf16)
    grad_low = seat_gather(own_grad)
    grad_hidden = dot(grad_low, down_local, 1, 1)
    grad_gate = grad_hidden * up_part * gate_sigmoid * (1.0 + gate_part * (1.0 - gate_sigmoid))
    grad_up = grad_hidden * activated
    grad_both = jnp.concatenate([grad_gate, grad_up], axis=1).astype(bf16)

    def by_sequence(values):
        return values.reshape(QUAD, full_rows, values.shape[1])

    input_grad, gains_total, down_planes, out_planes, up_ranks, qkv_ranks, _, _ = backward(
        grps,
        aligned,
        plane_lengths,
        gains_full,
        tables,
        residual,
        tokens[0],
        own_grad,
        by_sequence(grad_both),
        up_local,
        by_sequence(hidden),
        by_sequence(grad_low),
        by_sequence(second_norm),
        by_sequence(first_norm),
        out_local,
        qkv_local,
        (queries, key_vectors, value_vectors, attended),
    )
    down_sum = jnp.sum(down_planes.astype(f32), axis=0)
    up_sum = in_own_rows(up_ranks, seqs, 2, grps)
    qkv_sum = in_own_rows(qkv_ranks, seqs, 3, heads_local)
    if aligned:
        out_sum = jnp.sum(out_planes.astype(f32), axis=0)
    else:
        placed_term = jnp.zeros((seqs, QUAD, heads_local, HEAD_DIM, D), bf16)
        placed_term = lax.dynamic_update_slice(
            placed_term,
            out_planes.reshape(1, 1, heads_local, HEAD_DIM, D),
            (lax.axis_index("seq"), seat, 0, 0, 0),
        )
        out_sum = lax.psum_scatter(
            placed_term.transpose(0, 2, 1, 3, 4).reshape(D, D),
            EVERY,
            scatter_dimension=0,
            tiled=True,
        ).astype(f32)
    own_gains = norm_gains.shape[1]
    device = ((lax.axis_index("seq") * grps + lax.axis_index("grp")) * 2 + lax.axis_index("row")) * 2
    gains_sum = lax.dynamic_slice(
        gains_total, (0, (device + lax.axis_index("core")) * own_gains), (2, own_gains)
    )
    qkv_updated, qkv_moment_new, qkv_square_new = adam_update(
        qkv_weight, qkv_moment, qkv_square, qkv_sum, D ** (-0.5)
    )
    out_updated, out_moment_new, out_square_new = adam_update(
        out_weight, out_moment, out_square, out_sum, (D // 128) ** (-0.5)
    )
    up_updated, up_moment_new, up_square_new = adam_update(
        up_weight, up_moment, up_square, up_sum, D ** (-0.5)
    )
    down_updated, down_moment_new, down_square_new = adam_update(
        down_weight, down_moment, down_square, down_sum, FF ** (-0.5)
    )
    gains_updated, gains_moment_new, gains_square_new = adam_update(
        norm_gains, gains_moment, gains_square, gains_sum, 0.3
    )
    return (
        block_output[None],
        input_grad[None],
        qkv_updated,
        qkv_moment_new,
        qkv_square_new,
        qkv_updated.astype(bf16),
        out_updated,
        out_moment_new,
        out_square_new,
        out_updated.astype(bf16),
        up_updated,
        up_moment_new,
        up_square_new,
        up_updated.astype(bf16),
        down_updated,
        down_moment_new,
        down_square_new,
        down_updated.astype(bf16),
        gains_updated,
        gains_moment_new,
        gains_square_new,
    )


def solution(mesh):
    seqs, rest = mesh.shape["seq"], mesh.shape["fsdp"]
    planes = Mesh(
        mesh.devices.reshape(seqs, rest // QUAD, 2, 2), ("seq", "grp", "row", "core")
    )
    rows = P(("grp", "row", "core"), "seq", None)
    shards = P(EVERY, None)
    gains = P(None, EVERY)
    return jax.shard_map(
        on_device,
        mesh=planes,
        in_specs=(rows, rows, P(("grp", "row", "core"))) + (shards,) * 12 + (gains,) * 3,
        out_specs=(rows, rows) + (shards,) * 16 + (gains,) * 3,
        check_vma=False,
    )
```

```python
import math

import jax
import jax.numpy as jnp
from jax import lax
from jax.experimental import pallas as pl
from jax.experimental.pallas import tpu as pltpu
from jax.sharding import Mesh, PartitionSpec as P

D = 2048
HEADS = 32
HEAD_DIM = 64
FF = 4096
WINDOW = 128
STEP = 5


NORM_EPSILON = 1e-05
MOMENT_DECAY = 0.5
WEIGHT_DECAY = 0.1
ADAM_EPSILON = 1e-08

SEATS = ("row", "core", "seq")
RANKS = ("seq", "row", "core")
EVERY = ("seq", "grp", "row", "core")
QUAD = 4
VMEM_LIMIT = 63 * 2**20

bf16 = jnp.bfloat16
f32 = jnp.float32


def rotate_table(length, copies):
    halves = HEAD_DIM // 2
    freqs = jnp.exp(-math.log(10000.0) * 2.0 * jnp.arange(halves).astype(f32) / HEAD_DIM)
    angles = jnp.arange(length, dtype=jnp.int32).astype(f32)[:, None] * freqs[None, :]
    cosine, sine = jnp.cos(angles), jnp.sin(angles)
    return (
        jnp.tile(jnp.concatenate([cosine, cosine], axis=1), (1, copies)),
        jnp.tile(jnp.concatenate([-sine, sine], axis=1), (1, copies)),
    )


def adam_update(weight, moment, square, gradient, step_rate):
    moment_new = MOMENT_DECAY * moment + (1.0 - MOMENT_DECAY) * gradient
    square_new = MOMENT_DECAY * square + (1.0 - MOMENT_DECAY) * gradient * gradient
    correction = 1.0 - MOMENT_DECAY**STEP
    update = moment_new / correction / (jnp.sqrt(square_new / correction) + ADAM_EPSILON)
    return (weight - step_rate * (update + WEIGHT_DECAY * weight), moment_new, square_new)


def dot(a, b, lhs=1, rhs=0):
    return lax.dot_general(a, b, (((lhs,), (rhs,)), ((), ())), preferred_element_type=f32)


def swap_halves(values, first):
    width = values.shape[1]
    half = HEAD_DIM // 2
    return jnp.where(
        first, pltpu.roll(values, width - half, 1), pltpu.roll(values, half, 1)
    )


def allowed_mask(rows, length):
    row = lax.broadcasted_iota(jnp.int32, (rows, rows), 0)
    col = lax.broadcasted_iota(jnp.int32, (rows, rows), 1)
    return (col <= row) & (row - col < WINDOW) & (col.astype(f32) < length)


def head_lanes(rows, width, head):
    lane = lax.broadcasted_iota(jnp.int32, (rows, width), 1)
    return (lane // HEAD_DIM) == head


def softmax_rows(queries, key_vectors, allowed):
    scores = jnp.where(allowed, dot(queries, key_vectors, 1, 1) * (HEAD_DIM**-0.5), -1e30)
    shifted = jnp.exp(scores - jnp.max(scores, axis=-1, keepdims=True))
    return shifted / jnp.sum(shifted, axis=-1, keepdims=True)


def attention(length, queries, key_vectors, value_vectors):
    rows, width = queries.shape
    allowed = allowed_mask(rows, length)
    total = jnp.zeros((rows, width), f32)
    for head in range(width // HEAD_DIM):
        mine = head_lanes(rows, width, head)
        weights = softmax_rows(jnp.where(mine, queries, 0), key_vectors, allowed)
        total += dot(weights.astype(bf16), jnp.where(mine, value_vectors, 0))
    return total.astype(bf16)


def attention_grads(length, queries, key_vectors, value_vectors, grads):
    rows, width = queries.shape
    allowed = allowed_mask(rows, length)
    grad_q = jnp.zeros((rows, width), f32)
    grad_k = jnp.zeros((rows, width), f32)
    grad_v = jnp.zeros((rows, width), f32)
    for head in range(width // HEAD_DIM):
        mine = head_lanes(rows, width, head)
        q_head = jnp.where(mine, queries, 0)
        g_head = jnp.where(mine, grads, 0)
        weights = softmax_rows(q_head, key_vectors, allowed)
        grad_p = dot(g_head, value_vectors, 1, 1)
        delta = jnp.sum(weights * grad_p, axis=-1, keepdims=True)
        grad_s = jnp.where(allowed, weights * (grad_p - delta), 0.0).astype(bf16)
        grad_q += dot(grad_s, jnp.where(mine, key_vectors, 0))
        grad_k += dot(grad_s, q_head, 0, 0)
        grad_v += dot(weights.astype(bf16), g_head, 0, 0)
    return grad_q, grad_k, grad_v


MESH = pl.DeviceIdType.MESH
RELATIONS = tuple((a, b, d) for a in range(2) for b in range(2) for d in range(2))[1:]


class Place:
    def __init__(self, grps):
        self.grps = grps
        self.s = lax.axis_index("seq")
        self.g = lax.axis_index("grp")
        self.r = lax.axis_index("row")
        self.c = lax.axis_index("core")

    def peer(self, relation):
        ds, dr, dc = relation
        return ((self.s + ds) % 2, self.g, (self.r + dr) % 2, (self.c + dc) % 2)

    def plane(self, dz):
        return (self.s, (self.g + dz) % self.grps, self.r, self.c)

    def rank(self, relation=(0, 0, 0)):
        s, _, r, c = self.peer(relation)
        return (s * 2 + r) * 2 + c

    def seat(self, relation=(0, 0, 0)):
        s, _, r, c = self.peer(relation)
        return (r * 2 + c) * 2 + s

    def corner(self, relation=(0, 0, 0)):
        s, _, r, _ = self.peer(relation)
        return r * 2 + s

    def greet(self):
        barrier = pltpu.get_barrier_semaphore()
        for relation in RELATIONS:
            pl.semaphore_signal(barrier, inc=1, device_id=self.peer(relation), device_id_type=MESH)
        for dz in range(1, self.grps):
            pl.semaphore_signal(barrier, inc=1, device_id=self.plane(dz), device_id_type=MESH)
        pl.semaphore_wait(barrier, len(RELATIONS) + self.grps - 1)


SIBLING = (0, 0, 1)
ACROSS = ((1, 0, 0), (0, 1, 0), (1, 1, 0))


def remote(src, dst, send_sem, recv_sem, device):
    return pltpu.make_async_remote_copy(
        src_ref=src,
        dst_ref=dst,
        send_sem=send_sem,
        recv_sem=recv_sem,
        device_id=device,
        device_id_type=MESH,
    )


class PlaneSum:
    def __init__(self, place, part, near, far, sems):
        self.place, self.part, self.near, self.far = place, part, near, far
        self.near_send, self.near_recv, self.far_send, self.far_recv = sems
        self.first, self.second = [], []

    def start_near(self):
        place = self.place
        for k in range(4):
            block = ((k // 2) * 2 + (1 - place.c)) * 2 + k % 2
            copy = remote(
                self.part.at[block],
                self.near.at[k],
                self.near_send.at[k],
                self.near_recv.at[k],
                place.peer(SIBLING),
            )
            copy.start()
            self.first.append(copy)

    def start_far(self):
        place = self.place
        for copy in self.first:
            copy.wait()
        for k in range(4):
            block = ((k // 2) * 2 + place.c) * 2 + k % 2
            self.near[k] = (self.part[block].astype(f32) + self.near[k].astype(f32)).astype(bf16)
        for d, relation in enumerate(ACROSS):
            copy = remote(
                self.near.at[place.corner(relation)],
                self.far.at[d],
                self.far_send.at[d],
                self.far_recv.at[d],
                place.peer(relation),
            )
            copy.start()
            self.second.append(copy)

    def finish(self):
        for copy in self.second:
            copy.wait()

    def chunk(self, lanes):
        total = self.near[self.place.corner(), :, lanes].astype(f32)
        for d in range(3):
            total += self.far[d, :, lanes].astype(f32)
        return total


class PlaneGather:
    def __init__(self, place, blocks, send, recv):
        self.place, self.blocks, self.send, self.recv = place, blocks, send, recv
        self.first, self.second = [], []

    def copy(self, block, sem, relation):
        copy = remote(
            self.blocks.at[block],
            self.blocks.at[block],
            self.send.at[sem],
            self.recv.at[sem],
            self.place.peer(relation),
        )
        copy.start()
        return copy

    def start(self):
        mine = self.place.seat()
        self.first = [self.copy(mine, d, relation) for d, relation in enumerate(ACROSS)]
        self.first.append(self.copy(mine, 3, SIBLING))

    def forward(self):
        for d, relation in enumerate(ACROSS):
            self.first[d].wait_recv()
            self.second.append(self.copy(self.place.seat(relation), 4 + d, SIBLING))

    def finish(self):
        for copy in self.first[:3]:
            copy.wait_send()
        self.first[3].wait()
        for copy in self.second:
            copy.wait()


class ToOwners:
    def __init__(self, place, shares, landed, send, recv, own):
        self.copies = []
        for dz in range(1, place.grps):
            copy = remote(
                shares.at[(place.g + dz) % place.grps],
                landed.at[dz],
                send.at[dz],
                recv.at[dz],
                place.plane(dz),
            )
            copy.start()
            self.copies.append(copy)
        copy = pltpu.make_async_copy(shares.at[place.g], landed.at[0], own)
        copy.start()
        self.copies.append(copy)

    def finish(self):
        for copy in self.copies:
            copy.wait()


class Exchange:
    def __init__(self, place, blocks, held, send, recv, own):
        mine = place.rank()
        kept = held.at[mine // QUAD, mine % QUAD] if len(held.shape) == 4 else held.at[mine]
        self.copies = []
        for n, relation in enumerate(RELATIONS):
            copy = remote(
                blocks.at[place.rank(relation)],
                kept,
                send.at[n],
                recv.at[n],
                place.peer(relation),
            )
            copy.start()
            self.copies.append(copy)
        copy = pltpu.make_async_copy(blocks.at[mine], kept, own)
        copy.start()
        self.copies.append(copy)

    def finish(self):
        for copy in self.copies:
            copy.wait()


LANES = 512


def lanes_of(n, width=LANES):
    return pl.ds(pl.multiple_of(n * width, width), width)


def shares_of(seq, values, weight, part):
    rows = part.shape[1]

    @pl.loop(0, part.shape[2] // LANES)
    def _(n):
        product = dot(values[seq], weight[lanes_of(n)], 1, 1)
        part[2 * seq, :, lanes_of(n)] = product[:rows].astype(bf16)
        part[2 * seq + 1, :, lanes_of(n)] = product[rows:].astype(bf16)


def over_tokens(first, lanes, second, other):
    total = dot(first[0, :, lanes], second[0, :, other], 0, 0)
    for seq in range(1, first.shape[0]):
        total += dot(first[seq, :, lanes], second[seq, :, other], 0, 0)
    return total


def row_shares(first, second, shares):
    grps, seqs, rows, _ = shares.shape
    width = 256
    pieces = width // rows

    @pl.loop(0, first.shape[2] // width)
    def _(b):
        product = over_tokens(first, lanes_of(b, width), second, slice(None)).astype(bf16)
        for p in range(pieces):
            index = b * pieces + p
            shares[index % grps, index // grps] = product[p * rows : (p + 1) * rows]


def summed_rows(landed, blocks):
    seqs, rows = landed.shape[1], blocks.shape[1]
    for seq in range(seqs):
        for quad in range(QUAD):
            block = slice(quad * rows, (quad + 1) * rows)
            total = landed[0, seq, block].astype(f32)
            for dz in range(1, landed.shape[0]):
                total += landed[dz, seq, block].astype(f32)
            blocks[seq * QUAD + quad] = total.astype(bf16)


def back_kernel(
    grps,
    aligned,
    facts,
    gains,
    cosine,
    sine,
    residual,
    own_tokens,
    own_grad,
    dgu_h,
    up_h,
    hidden_h,
    grad_h,
    second_h,
    first_h,
    out_h,
    qkv_h,
    q_h,
    k_h,
    v_h,
    o_h,
    input_grad,
    gains_sum,
    down_landed,
    out_landed,
    up_held,
    qkv_held,
    up_landed,
    qkv_landed,
    wide,
    up,
    hidden,
    acts,
    second,
    out_w,
    qkv,
    part,
    near,
    far,
    blocks,
    turned,
    down_share,
    up_share,
    out_share,
    qkv_share,
    up_sum,
    qkv_sum,
    gain_part,
    gain_plane,
    gain_far,
    load,
    near_send,
    near_recv,
    far_send,
    far_recv,
    all_send,
    all_recv,
    z_send,
    z_recv,
    swap_send,
    swap_recv,
    gain_send,
    gain_recv,
    own_sem,
):
    place = Place(grps)
    rows = residual.shape[0]
    gain_part[...] = jnp.zeros_like(gain_part)
    count, full_rows, head_width = q_h.shape

    def fetch(src, dst, n):
        copy = pltpu.make_async_copy(src, dst, load.at[n])
        copy.start()
        return copy

    loads = [fetch(dgu_h, wide, 0), fetch(up_h, up, 1)]
    later = [fetch(hidden_h, hidden, 2), fetch(grad_h, acts, 3), fetch(second_h, second, 4)]
    weights = [fetch(out_h, out_w, 5), fetch(qkv_h, qkv, 6)]
    place.greet()
    for copy in loads:
        copy.wait()

    sums = (near_send, near_recv, far_send, far_recv)
    second_sum = PlaneSum(place, part, near, far, sums)
    for r in range(2):
        shares_of(2 * r + 1 - place.c, wide, up, part)
    second_sum.start_near()
    for r in range(2):
        shares_of(2 * r + place.c, wide, up, part)

    for copy in later[:2]:
        copy.wait()
    units = down_share.shape[1]
    width = min(256, hidden.shape[2])

    @pl.loop(0, hidden.shape[2] // width)
    def _(b):
        for half in range(2):
            lanes = slice(half * D // 2, (half + 1) * D // 2)
            product = over_tokens(hidden, lanes_of(b, width), acts, lanes).astype(bf16)
            for p in range(width // units):
                down_share[b * (width // units) + p, :, lanes] = product[p * units : (p + 1) * units]

    down_out = ToOwners(place, down_share, down_landed, z_send.at[0], z_recv.at[0], own_sem.at[0])
    fetch_first = fetch(first_h, acts, 3)
    second_sum.start_far()
    later[2].wait()
    row_shares(second, wide, up_share)
    up_out = ToOwners(place, up_share, up_landed, z_send.at[1], z_recv.at[1], own_sem.at[1])
    heads = [
        fetch(ref, wide.at[:, :, n * head_width : (n + 1) * head_width], 7 + n)
        for n, ref in enumerate((q_h, k_h, v_h, o_h))
    ]

    second_sum.finish()
    mine = place.seat()
    inner = jnp.zeros((rows, 1), f32)
    squares = jnp.zeros((rows, 1), f32)
    for n in range(D // LANES):
        lanes = slice(n * LANES, (n + 1) * LANES)
        grad = second_sum.chunk(lanes)
        values = residual[:, lanes]
        inner += jnp.sum(grad * gains[1:2, lanes] * values, axis=-1, keepdims=True)
        squares += jnp.sum(values * values, axis=-1, keepdims=True)
    scale = lax.rsqrt(squares / D + NORM_EPSILON)
    inner = inner / D
    for n in range(D // LANES):
        lanes = slice(n * LANES, (n + 1) * LANES)
        grad, values = second_sum.chunk(lanes), residual[:, lanes]
        gain_part[1:2, lanes] = jnp.sum(grad * values * scale, axis=0, keepdims=True)
        total = own_grad[:, lanes].astype(f32) + scale * (
            grad * gains[1:2, lanes] - values * scale * scale * inner
        )
        input_grad[:, lanes] = total
        blocks[mine, :, lanes] = total.astype(bf16)

    gather = PlaneGather(place, blocks, all_send, all_recv)
    gather.start()
    gather.forward()
    for copy in weights + heads:
        copy.wait()
    gather.finish()

    lane = lax.broadcasted_iota(jnp.int32, (full_rows, head_width), 1)
    first_half = (lane % HEAD_DIM) < HEAD_DIM // 2

    @pl.loop(0, count)
    def _(seq):
        grads = jnp.concatenate(
            [dot(blocks[2 * seq], out_w[...], 1, 1), dot(blocks[2 * seq + 1], out_w[...], 1, 1)],
            axis=0,
        ).astype(bf16)
        queries = wide[seq, :, 0:head_width]
        key_vectors = wide[seq, :, head_width : 2 * head_width]
        value_vectors = wide[seq, :, 2 * head_width : 3 * head_width]
        grad_q, grad_k, grad_v = attention_grads(
            facts[seq, 2:3, 0:1], queries, key_vectors, value_vectors, grads
        )
        for n, grad in enumerate((grad_q, grad_k)):
            values = (grad * HEAD_DIM**-0.5).astype(bf16).astype(f32)
            back = values * cosine[...] - swap_halves(values, first_half) * sine[...]
            turned[seq, :, n * head_width : (n + 1) * head_width] = back.astype(bf16)
        turned[seq, :, 2 * head_width : 3 * head_width] = grad_v.astype(bf16)

    fetch_first.wait()
    row_shares(acts, turned, qkv_share)
    qkv_out = ToOwners(place, qkv_share, qkv_landed, z_send.at[2], z_recv.at[2], own_sem.at[2])

    first_sum = PlaneSum(place, part, near, far, sums)
    for r in range(2):
        shares_of(2 * r + 1 - place.c, turned, qkv, part)
    first_sum.start_near()
    for r in range(2):
        shares_of(2 * r + place.c, turned, qkv, part)
    first_sum.start_far()

    out_rows = out_share.shape[1]

    @pl.loop(0, D // LANES)
    def _(n):
        lanes = lanes_of(n)
        total = jnp.zeros((head_width, LANES), f32)
        for seq in range(count):
            values = wide[seq, :, 3 * head_width : 4 * head_width].astype(f32)
            total += dot(values[:rows].astype(bf16), blocks[2 * seq, :, lanes], 0, 0)
            total += dot(values[rows:].astype(bf16), blocks[2 * seq + 1, :, lanes], 0, 0)
        total = total.astype(bf16)
        for j in range(out_share.shape[0]):
            out_share[j, :, lanes] = total[j * out_rows : (j + 1) * out_rows]

    if aligned:
        out_out = ToOwners(place, out_share, out_landed, z_send.at[3], z_recv.at[3], own_sem.at[3])
    else:
        out_out = pltpu.make_async_copy(out_share, out_landed, own_sem.at[3])
        out_out.start()

    first_sum.finish()
    inner = jnp.zeros((rows, 1), f32)
    squares = jnp.zeros((rows, 1), f32)
    for n in range(D // LANES):
        lanes = slice(n * LANES, (n + 1) * LANES)
        grad = first_sum.chunk(lanes)
        values = own_tokens[:, lanes].astype(f32)
        inner += jnp.sum(grad * gains[0:1, lanes] * values, axis=-1, keepdims=True)
        squares += jnp.sum(values * values, axis=-1, keepdims=True)
    scale = lax.rsqrt(squares / D + NORM_EPSILON)
    inner = inner / D
    for n in range(D // LANES):
        lanes = slice(n * LANES, (n + 1) * LANES)
        grad, values = first_sum.chunk(lanes), own_tokens[:, lanes].astype(f32)
        gain_part[0:1, lanes] = jnp.sum(grad * values * scale, axis=0, keepdims=True)
        input_grad[:, lanes] += scale * (
            grad * gains[0:1, lanes] - values * scale * scale * inner
        )

    gain_copies = []
    for n, relation in enumerate(RELATIONS):
        copy = remote(
            gain_part, gain_plane.at[n], gain_send.at[n], gain_recv.at[n], place.peer(relation)
        )
        copy.start()
        gain_copies.append(copy)

    up_out.finish()
    landed = pltpu.make_async_copy(up_landed, up_share, load.at[1])
    landed.start()
    for copy in gain_copies:
        copy.wait()
    total = gain_part[...]
    for n in range(len(RELATIONS)):
        total += gain_plane[n]
    gain_far[0] = total
    gain_copies = []
    for dz in range(1, grps):
        copy = remote(
            gain_far.at[0],
            gain_far.at[dz],
            gain_send.at[7 + dz],
            gain_recv.at[7 + dz],
            place.plane(dz),
        )
        copy.start()
        gain_copies.append(copy)
    landed.wait()
    summed_rows(up_share, up_sum)
    up_swap = Exchange(place, up_sum, up_held, swap_send.at[0], swap_recv.at[0], own_sem.at[4])
    for copy in gain_copies:
        copy.wait()
    total = gain_far[0]
    for dz in range(1, grps):
        total += gain_far[dz]
    gains_sum[...] = total

    qkv_out.finish()
    landed = pltpu.make_async_copy(qkv_landed, qkv_share, load.at[6])
    landed.start()
    landed.wait()
    summed_rows(qkv_share, qkv_sum)
    qkv_swap = Exchange(place, qkv_sum, qkv_held, swap_send.at[1], swap_recv.at[1], own_sem.at[5])
    if aligned:
        out_out.finish()
    else:
        out_out.wait()
    down_out.finish()
    up_swap.finish()
    qkv_swap.finish()


def backward(
    grps,
    aligned,
    facts,
    gains,
    tables,
    residual,
    own_tokens,
    own_grad,
    grad_both,
    up_local,
    hidden,
    grad_low,
    second_norm,
    first_norm,
    out_local,
    qkv_local,
    heads,
):
    rows = residual.shape[0]
    count, full_rows, head_width = heads[0].shape
    seqs = full_rows // rows
    ranks = seqs * QUAD
    units = hidden.shape[2] // grps
    both = grad_both.shape[2]
    quad_rows = D // (seqs * grps)
    shard = quad_rows // QUAD
    out_rows = head_width // grps if aligned else HEAD_DIM
    triple = 3 * head_width
    out_count = head_width // out_rows
    hbm = pl.BlockSpec(memory_space=pl.ANY)
    vmem = pl.BlockSpec(memory_space=pltpu.VMEM)
    shape = jax.ShapeDtypeStruct
    dma = pltpu.SemaphoreType.DMA
    return pl.pallas_call(
        lambda *refs: back_kernel(grps, aligned, *refs),
        in_specs=[vmem] * 7 + [hbm] * 12,
        out_specs=[vmem] * 2 + [hbm] * 6,
        out_shape=[
            shape((rows, D), f32),
            shape((8, D), f32),
            shape((grps, units, D), bf16),
            shape((out_count, out_rows, D), bf16),
            shape((ranks, shard, both), bf16),
            shape((ranks, shard, triple), bf16),
            shape((grps, seqs, quad_rows, both), bf16),
            shape((grps, seqs, quad_rows, triple), bf16),
        ],
        scratch_shapes=[
            pltpu.VMEM((count, full_rows, both), bf16),
            pltpu.VMEM((D, both), bf16),
            pltpu.VMEM((count, full_rows, hidden.shape[2]), bf16),
            pltpu.VMEM((count, full_rows, D), bf16),
            pltpu.VMEM((count, full_rows, D), bf16),
            pltpu.VMEM((head_width, D), bf16),
            pltpu.VMEM((D, triple), bf16),
            pltpu.VMEM((ranks, rows, D), bf16),
            pltpu.VMEM((4, rows, D), bf16),
            pltpu.VMEM((3, rows, D), bf16),
            pltpu.VMEM((ranks, rows, D), bf16),
            pltpu.VMEM((count, full_rows, triple), bf16),
            pltpu.VMEM((grps, units, D), bf16),
            pltpu.VMEM((grps, seqs, quad_rows, both), bf16),
            pltpu.VMEM((out_count, out_rows, D), bf16),
            pltpu.VMEM((grps, seqs, quad_rows, triple), bf16),
            pltpu.VMEM((ranks, shard, both), bf16),
            pltpu.VMEM((ranks, shard, triple), bf16),
            pltpu.VMEM((8, D), f32),
            pltpu.VMEM((7, 8, D), f32),
            pltpu.VMEM((grps, 8, D), f32),
            dma((11,)),
            dma((4,)),
            dma((4,)),
            dma((3,)),
            dma((3,)),
            dma((7,)),
            dma((7,)),
            dma((4, grps)),
            dma((4, grps)),
            dma((2, 7)),
            dma((2, 7)),
            dma((7 + grps,)),
            dma((7 + grps,)),
            dma((6,)),
        ],
        compiler_params=pltpu.CompilerParams(
            collective_id=0, has_side_effects=True, vmem_limit_bytes=VMEM_LIMIT
        ),
        cost_estimate=pl.CostEstimate(
            flops=30 * 10**9, bytes_accessed=60 * 2**20, transcendentals=2 * 10**6
        ),
        name="backward",
    )(
        facts,
        gains,
        *tables,
        residual,
        own_tokens,
        own_grad,
        grad_both,
        up_local,
        hidden,
        grad_low,
        second_norm,
        first_norm,
        out_local,
        qkv_local,
        *heads,
    )


class FromOwners:
    def __init__(self, place, source, landed, landing, send, recv, own):
        self.place, self.source, self.send, self.recv = place, source, send, recv
        self.slot = lambda j: landing(landed, j)
        self.own = pltpu.make_async_copy(source, self.slot(place.g), own)
        self.line = place.grps == 4

    def copy(self, source, slot, sem, recv, target):
        place = self.place
        return remote(
            source, self.slot(slot), self.send.at[sem], self.recv.at[recv], (place.s, target, place.r, place.c)
        )

    def direct(self, g):
        targets = ((1, 2, 3), (0, 2), (3, 1), (2, 1, 0))[g]
        return [self.copy(self.source, g, t, g, t) for t in targets]

    def passed_on(self, g):
        inner, end = 3 - g, 0 if g == 1 else 3
        return self.copy(self.slot(inner), inner, 3 - end, inner, end)

    def arrival(self, j):
        return self.copy(self.source, j, j, j, j)

    def start(self):
        place = self.place
        self.own.start()
        if self.line:
            for g in range(4):

                @pl.when(place.g == g)
                def _():
                    for copy in self.direct(g):
                        copy.start()

        else:
            self.copies = [
                self.copy(self.source, place.g, dz, dz, (place.g + dz) % place.grps)
                for dz in range(1, place.grps)
            ]
            for copy in self.copies:
                copy.start()

    def relay(self):
        if self.line:
            for g in (1, 2):

                @pl.when(self.place.g == g)
                def _():
                    self.arrival(3 - g).wait_recv()
                    self.passed_on(g).start()

    def finish(self):
        self.own.wait()
        if self.line:
            for g in range(4):

                @pl.when(self.place.g == g)
                def _():
                    for j in range(4):
                        if j != g and not (g in (1, 2) and j == 3 - g):
                            self.arrival(j).wait_recv()
                    for copy in self.direct(g):
                        copy.wait_send()
                    if g in (1, 2):
                        self.passed_on(g).wait_send()

        else:
            for copy in self.copies:
                copy.wait()


def shares_from(seq, values, weight, part):
    rows = part.shape[1]

    @pl.loop(0, part.shape[2] // LANES)
    def _(n):
        product = dot(values[seq], weight[:, lanes_of(n)])
        part[2 * seq, :, lanes_of(n)] = product[:rows].astype(bf16)
        part[2 * seq + 1, :, lanes_of(n)] = product[rows:].astype(bf16)


def times_slices(values, weight, lanes):
    seqs, grps, quad, shard, _ = weight.shape
    depth = quad * shard
    total = None
    for n in range(seqs * grps):
        piece = weight[n // grps, n % grps, :, :, lanes]
        term = dot(values[:, n * depth : (n + 1) * depth], piece.reshape(depth, piece.shape[2]))
        total = term if total is None else total + term
    return total


def both_blocks(blocks, seq):
    return jnp.concatenate([blocks[2 * seq].astype(f32), blocks[2 * seq + 1].astype(f32)], axis=0)


def forward_kernel(
    grps,
    aligned,
    cosine,
    sine,
    own_facts,
    tokens_h,
    own_grad_h,
    qkv_sent,
    up_sent,
    out_own,
    down_own,
    residual,
    gains,
    facts,
    first_h,
    q_h,
    k_h,
    v_h,
    o_h,
    second_h,
    grad_h,
    hidden_h,
    dgu_h,
    qkv_landed,
    up_landed,
    out_landed,
    down_landed,
    blocks,
    grad_blocks,
    norm,
    grad_seq,
    qkv_rank,
    up_rank,
    qkv,
    up,
    out_w,
    down,
    heads,
    part,
    near,
    far,
    both,
    hidden,
    dgu,
    all_facts,
    load,
    store,
    swap_send,
    swap_recv,
    near_send,
    near_recv,
    far_send,
    far_recv,
    all_send,
    all_recv,
    z_send,
    z_recv,
    fact_send,
    fact_recv,
    own_sem,
):
    place = Place(grps)
    count, full_rows, _ = norm.shape
    rows = residual.shape[0]
    head_width = heads.shape[3]
    mine, rank = place.seat(), place.rank()

    def fetch(src, dst, n):
        copy = pltpu.make_async_copy(src, dst, load.at[n])
        copy.start()
        return copy

    def keep(src, dst, n):
        copy = pltpu.make_async_copy(src, dst, store.at[n])
        copy.start()
        return copy

    facts[rank] = own_facts[...]
    own_blocks = [fetch(tokens_h, blocks.at[mine], 0), fetch(own_grad_h, grad_blocks.at[mine], 1)]
    place.greet()

    def plane_rows(ref, j):
        return ref.at[:, j]

    def own_rows(ref, j):
        size = ref.shape[0] // grps
        return ref.at[pl.ds(pl.multiple_of(j * size, size), size)]

    def from_owners(n, source, landed, landing):
        return FromOwners(place, source, landed, landing, z_send.at[n], z_recv.at[n], own_sem.at[n])

    down_z = from_owners(3, down_own, down_landed, own_rows)
    if aligned:
        out_z = from_owners(2, out_own, out_landed, own_rows)
        out_z.start()
    qkv_swap = Exchange(place, qkv_sent, qkv_rank, swap_send.at[0], swap_recv.at[0], own_sem.at[4])
    fact_copies = []
    for n, relation in enumerate(RELATIONS):
        copy = remote(own_facts, facts.at[rank], fact_send.at[n], fact_recv.at[n], place.peer(relation))
        copy.start()
        fact_copies.append(copy)
    for copy in own_blocks:
        copy.wait()
    token_gather = PlaneGather(place, blocks, all_send.at[0], all_recv.at[0])
    token_gather.start()
    up_swap = Exchange(place, up_sent, up_rank, swap_send.at[1], swap_recv.at[1], own_sem.at[5])
    qkv_swap.finish()
    seqs = qkv_landed.shape[0]
    qkv_z = from_owners(0, qkv_rank, qkv_landed, plane_rows)
    up_z = from_owners(1, up_rank, up_landed, plane_rows)
    qkv_z.start()
    for copy in fact_copies:
        copy.wait()
    all_facts[place.g] = facts[...]
    fact_copies = []
    for dz in range(1, grps):
        copy = remote(
            facts,
            all_facts.at[place.g],
            fact_send.at[7 + dz],
            fact_recv.at[7 + dz],
            place.plane(dz),
        )
        copy.start()
        fact_copies.append(copy)
    token_gather.forward()
    up_swap.finish()
    if aligned:
        out_z.relay()
    for copy in fact_copies:
        copy.wait()
    width = D // (seqs * grps * QUAD)
    for n in range(seqs * grps):
        pieces = [all_facts[n % grps, (n // grps) * QUAD + q, :, :width] for q in range(QUAD)]
        gains[:, n * QUAD * width : (n + 1) * QUAD * width] = jnp.concatenate(pieces, axis=1)
    token_gather.finish()
    grad_gather = PlaneGather(place, grad_blocks, all_send.at[1], all_recv.at[1])
    grad_gather.start()

    @pl.loop(0, count)
    def _(seq):
        values = both_blocks(blocks, seq)
        scale = lax.rsqrt(jnp.mean(values * values, axis=-1, keepdims=True) + NORM_EPSILON)
        norm[seq] = (values * scale * gains[0:1, :]).astype(bf16)

    stores = [keep(norm, first_h, 0)]
    qkv_z.relay()
    grad_gather.forward()
    qkv_z.finish()
    up_z.start()
    fetch(qkv_landed, qkv, 2).wait()

    lane = lax.broadcasted_iota(jnp.int32, (full_rows, head_width), 1)
    first_half = (lane % HEAD_DIM) < HEAD_DIM // 2

    @pl.loop(0, count)
    def _(seq):
        for n in range(3):
            lanes = slice(n * head_width, (n + 1) * head_width)
            values = times_slices(norm[seq], qkv, lanes)
            if n < 2:
                values = values * cosine[...] + swap_halves(values, first_half) * sine[...]
            heads[n, seq] = values.astype(bf16)
        heads[3, seq] = attention(facts[seq, 2:3, 0:1], heads[0, seq], heads[1, seq], heads[2, seq])

    stores += [keep(heads.at[n], ref, 1 + n) for n, ref in enumerate((q_h, k_h, v_h, o_h))]
    if aligned:
        out_z.finish()
        fetch(out_landed, out_w, 3).wait()
    else:
        fetch(out_own, out_w, 3).wait()

    plane_sum = PlaneSum(place, part, near, far, (near_send, near_recv, far_send, far_recv))
    mixed = heads.at[3]
    for r in range(2):
        shares_from(2 * r + 1 - place.c, mixed, out_w, part)
    plane_sum.start_near()
    for r in range(2):
        shares_from(2 * r + place.c, mixed, out_w, part)
    grad_gather.finish()
    plane_sum.start_far()

    @pl.loop(0, count)
    def _(seq):
        grad_seq[seq] = both_blocks(grad_blocks, seq).astype(bf16)

    stores.append(keep(grad_seq, grad_h, 6))
    up_z.relay()
    fetch(tokens_h, grad_blocks.at[mine], 4).wait()
    plane_sum.finish()
    squares = jnp.zeros((rows, 1), f32)
    for n in range(D // LANES):
        lanes = slice(n * LANES, (n + 1) * LANES)
        values = grad_blocks[mine, :, lanes].astype(f32) + plane_sum.chunk(lanes)
        residual[:, lanes] = values
        squares += jnp.sum(values * values, axis=-1, keepdims=True)
    scale = lax.rsqrt(squares / D + NORM_EPSILON)
    for n in range(D // LANES):
        lanes = slice(n * LANES, (n + 1) * LANES)
        blocks[mine, :, lanes] = (residual[:, lanes] * scale * gains[1:2, lanes]).astype(bf16)
    norm_gather = PlaneGather(place, blocks, all_send.at[2], all_recv.at[2])
    norm_gather.start()
    down_z.start()
    norm_gather.forward()
    stores[0].wait()
    norm_gather.finish()

    @pl.loop(0, count)
    def _(seq):
        norm[seq] = both_blocks(blocks, seq).astype(bf16)

    stores[0] = keep(norm, second_h, 5)
    up_z.finish()
    down_z.relay()
    fetch(up_landed, up, 5).wait()
    half = hidden.shape[2]

    @pl.loop(0, count)
    def _(seq):
        gate = times_slices(norm[seq], up, slice(0, half))
        above = times_slices(norm[seq], up, slice(half, 2 * half))
        both[seq, :, :half] = gate
        both[seq, :, half:] = above
        hidden[seq] = (gate * jax.nn.sigmoid(gate) * above).astype(bf16)

    stores.append(keep(hidden, hidden_h, 7))
    down_z.finish()
    fetch(down_landed, down, 6).wait()

    @pl.loop(0, count)
    def _(seq):
        grads = dot(grad_seq[seq], down[...], 1, 1)
        gate, above = both[seq, :, :half], both[seq, :, half:]
        sigmoid = jax.nn.sigmoid(gate)
        dgu[seq, :, :half] = (grads * above * sigmoid * (1.0 + gate * (1.0 - sigmoid))).astype(bf16)
        dgu[seq, :, half:] = (grads * (gate * sigmoid)).astype(bf16)

    stores.append(keep(dgu, dgu_h, 8))
    for copy in stores:
        copy.wait()


def forward(grps, aligned, tables, own_facts, tokens, own_grad, qkv_sent, up_sent, out_own, down_own):
    rows = tokens.shape[0]
    ranks, shard, triple = qkv_sent.shape
    both = up_sent.shape[2]
    seqs = ranks // QUAD
    count, full_rows, head_width = QUAD, rows * seqs, triple // 3
    half = both // 2
    hbm = pl.BlockSpec(memory_space=pl.ANY)
    vmem = pl.BlockSpec(memory_space=pltpu.VMEM)
    shape = jax.ShapeDtypeStruct
    dma = pltpu.SemaphoreType.DMA
    by_heads = shape((count, full_rows, head_width), bf16)
    return pl.pallas_call(
        lambda *refs: forward_kernel(grps, aligned, *refs),
        in_specs=[vmem] * 3 + [hbm] * 6,
        out_specs=[vmem] * 3 + [hbm] * 13,
        out_shape=[
            shape((rows, D), f32),
            shape((8, D), f32),
            shape((ranks, 8, 128), f32),
            shape((count, full_rows, D), bf16),
            by_heads,
            by_heads,
            by_heads,
            by_heads,
            shape((count, full_rows, D), bf16),
            shape((count, full_rows, D), bf16),
            shape((count, full_rows, half), bf16),
            shape((count, full_rows, both), bf16),
            shape((seqs, grps, QUAD, shard, triple), bf16),
            shape((seqs, grps, QUAD, shard, both), bf16),
            shape((head_width, D), bf16),
            shape((half, D), bf16),
        ],
        scratch_shapes=[
            pltpu.VMEM((ranks, rows, D), bf16),
            pltpu.VMEM((ranks, rows, D), bf16),
            pltpu.VMEM((count, full_rows, D), bf16),
            pltpu.VMEM((count, full_rows, D), bf16),
            pltpu.VMEM((seqs, QUAD, shard, triple), bf16),
            pltpu.VMEM((seqs, QUAD, shard, both), bf16),
            pltpu.VMEM((seqs, grps, QUAD, shard, triple), bf16),
            pltpu.VMEM((seqs, grps, QUAD, shard, both), bf16),
            pltpu.VMEM((head_width, D), bf16),
            pltpu.VMEM((half, D), bf16),
            pltpu.VMEM((4, count, full_rows, head_width), bf16),
            pltpu.VMEM((ranks, rows, D), bf16),
            pltpu.VMEM((4, rows, D), bf16),
            pltpu.VMEM((3, rows, D), bf16),
            pltpu.VMEM((count, full_rows, both), f32),
            pltpu.VMEM((count, full_rows, half), bf16),
            pltpu.VMEM((count, full_rows, both), bf16),
            pltpu.VMEM((grps, ranks, 8, 128), f32),
            dma((7,)),
            dma((9,)),
            dma((2, 7)),
            dma((2, 7)),
            dma((4,)),
            dma((4,)),
            dma((3,)),
            dma((3,)),
            dma((3, 7)),
            dma((3, 7)),
            dma((4, grps)),
            dma((4, grps)),
            dma((7 + grps,)),
            dma((7 + grps,)),
            dma((6,)),
        ],
        compiler_params=pltpu.CompilerParams(
            collective_id=1, has_side_effects=True, vmem_limit_bytes=VMEM_LIMIT
        ),
        cost_estimate=pl.CostEstimate(
            flops=20 * 10**9, bytes_accessed=60 * 2**20, transcendentals=4 * 10**6
        ),
        name="forward",
    )(*tables, own_facts, tokens, own_grad, qkv_sent, up_sent, out_own, down_own)


def to_ranks(columns):
    rows, parts, seqs, units, quad, lanes = columns.shape
    return columns.transpose(2, 4, 0, 1, 3, 5).reshape(seqs * quad, rows, parts * units * lanes)


def in_own_rows(held, seqs, parts, units):
    ranks, rows, columns = held.shape
    lanes = columns // (parts * units)
    return (
        held.reshape(seqs, QUAD, rows, parts, units, lanes)
        .transpose(2, 3, 0, 4, 1, 5)
        .reshape(rows, columns * ranks)
        .astype(f32)
    )


def seat_sum(partial):
    return lax.psum_scatter(
        partial.astype(bf16), SEATS, scatter_dimension=0, tiled=True
    ).astype(f32)


def on_device(
    tokens,
    cotangent,
    lengths,
    qkv_weight,
    qkv_moment,
    qkv_square,
    out_weight,
    out_moment,
    out_square,
    up_weight,
    up_moment,
    up_square,
    down_weight,
    down_moment,
    down_square,
    norm_gains,
    gains_moment,
    gains_square,
):
    seqs = lax.axis_size("seq")
    grps = lax.axis_size("grp")
    ranks = seqs * QUAD
    own_rows = tokens.shape[1]
    full_rows = own_rows * seqs
    all_rows = full_rows * QUAD
    shard = qkv_weight.shape[0]
    heads_local = HEADS // ranks
    head_width = heads_local * HEAD_DIM
    units = down_weight.shape[0]
    aligned = out_weight.shape[0] == HEAD_DIM
    tables = rotate_table(full_rows, heads_local)

    positions = lax.axis_index("seq") * own_rows + jnp.arange(own_rows, dtype=jnp.int32)
    own_grad = jnp.where((positions < lengths[0])[:, None], cotangent[0], 0)
    own_gains = norm_gains.shape[1]
    own_facts = jnp.zeros((8, 128), f32)
    own_facts = own_facts.at[:2, :own_gains].set(norm_gains.astype(bf16).astype(f32))
    own_facts = own_facts.at[2].set(lengths[0].astype(f32))

    qkv_sent = to_ranks(
        qkv_weight.astype(bf16).reshape(shard, 3, seqs, heads_local, QUAD, HEAD_DIM)
    )
    up_sent = to_ranks(up_weight.astype(bf16).reshape(shard, 2, seqs, grps, QUAD, units))
    out_low = out_weight.astype(bf16)
    if not aligned:
        out_all = lax.all_gather(out_low, EVERY, axis=0, tiled=True)
        out_all = out_all.reshape(seqs, heads_local, QUAD, HEAD_DIM, D)
        seat = lax.axis_index("row") * 2 + lax.axis_index("core")
        out_low = lax.dynamic_index_in_dim(
            lax.dynamic_index_in_dim(out_all, lax.axis_index("seq"), 0, False), seat, 1, False
        ).reshape(head_width, D)
    (
        residual,
        gains,
        facts,
        first_norm,
        queries,
        key_vectors,
        value_vectors,
        attended,
        second_norm,
        grad_low,
        hidden,
        grad_both,
        qkv_local,
        up_local,
        out_local,
        down_local,
    ) = forward(
        grps,
        aligned,
        tables,
        own_facts,
        tokens[0],
        own_grad,
        qkv_sent,
        up_sent,
        out_low,
        down_weight.astype(bf16),
    )
    if not aligned:
        out_local = out_low
    (
        input_grad,
        gains_total,
        down_planes,
        out_planes,
        up_ranks,
        qkv_ranks,
        _,
        _,
    ) = backward(
        grps,
        aligned,
        facts,
        gains,
        tables,
        residual,
        tokens[0],
        own_grad,
        grad_both,
        up_local.reshape(D, -1),
        hidden,
        grad_low,
        second_norm,
        first_norm,
        out_local,
        qkv_local.reshape(D, -1),
        (queries, key_vectors, value_vectors, attended),
    )
    block_output = (
        residual + seat_sum(dot(hidden.reshape(all_rows, -1), down_local))
    ).astype(bf16)
    down_sum = jnp.sum(down_planes.astype(f32), axis=0)
    up_sum = in_own_rows(up_ranks, seqs, 2, grps)
    qkv_sum = in_own_rows(qkv_ranks, seqs, 3, heads_local)
    if aligned:
        out_sum = jnp.sum(out_planes.astype(f32), axis=0)
    else:
        placed_term = jnp.zeros((seqs, QUAD, heads_local, HEAD_DIM, D), bf16)
        placed_term = lax.dynamic_update_slice(
            placed_term,
            out_planes.reshape(1, 1, heads_local, HEAD_DIM, D),
            (lax.axis_index("seq"), seat, 0, 0, 0),
        )
        out_sum = lax.psum_scatter(
            placed_term.transpose(0, 2, 1, 3, 4).reshape(D, D),
            EVERY,
            scatter_dimension=0,
            tiled=True,
        ).astype(f32)
    device = ((lax.axis_index("seq") * grps + lax.axis_index("grp")) * 2 + lax.axis_index("row")) * 2
    gains_sum = lax.dynamic_slice(
        gains_total, (0, (device + lax.axis_index("core")) * own_gains), (2, own_gains)
    )
    qkv_updated, qkv_moment_new, qkv_square_new = adam_update(
        qkv_weight, qkv_moment, qkv_square, qkv_sum, D ** (-0.5)
    )
    out_updated, out_moment_new, out_square_new = adam_update(
        out_weight, out_moment, out_square, out_sum, (D // 128) ** (-0.5)
    )
    up_updated, up_moment_new, up_square_new = adam_update(
        up_weight, up_moment, up_square, up_sum, D ** (-0.5)
    )
    down_updated, down_moment_new, down_square_new = adam_update(
        down_weight, down_moment, down_square, down_sum, FF ** (-0.5)
    )
    gains_updated, gains_moment_new, gains_square_new = adam_update(
        norm_gains, gains_moment, gains_square, gains_sum, 0.3
    )
    return (
        block_output[None],
        input_grad[None],
        qkv_updated,
        qkv_moment_new,
        qkv_square_new,
        qkv_updated.astype(bf16),
        out_updated,
        out_moment_new,
        out_square_new,
        out_updated.astype(bf16),
        up_updated,
        up_moment_new,
        up_square_new,
        up_updated.astype(bf16),
        down_updated,
        down_moment_new,
        down_square_new,
        down_updated.astype(bf16),
        gains_updated,
        gains_moment_new,
        gains_square_new,
    )


def solution(mesh):
    seqs, rest = mesh.shape["seq"], mesh.shape["fsdp"]
    planes = Mesh(
        mesh.devices.reshape(seqs, rest // QUAD, 2, 2), ("seq", "grp", "row", "core")
    )
    rows = P(("grp", "row", "core"), "seq", None)
    shards = P(EVERY, None)
    gains = P(None, EVERY)
    return jax.shard_map(
        on_device,
        mesh=planes,
        in_specs=(rows, rows, P(("grp", "row", "core"))) + (shards,) * 12 + (gains,) * 3,
        out_specs=(rows, rows) + (shards,) * 16 + (gains,) * 3,
        check_vma=False,
    )
```

```python
import math

import jax
import jax.numpy as jnp
from jax import lax
from jax.experimental import pallas as pl
from jax.experimental.pallas import tpu as pltpu
from jax.sharding import Mesh, PartitionSpec as P

D = 2048
HEADS = 32
HEAD_DIM = 64
FF = 4096
WINDOW = 128
STEP = 5


NORM_EPSILON = 1e-05
MOMENT_DECAY = 0.5
WEIGHT_DECAY = 0.1
ADAM_EPSILON = 1e-08

SEATS = ("row", "core", "seq")
RANKS = ("seq", "row", "core")
EVERY = ("seq", "grp", "row", "core")
QUAD = 4
VMEM_LIMIT = 63 * 2**20

bf16 = jnp.bfloat16
f32 = jnp.float32


def rotate_table(length, copies):
    halves = HEAD_DIM // 2
    freqs = jnp.exp(-math.log(10000.0) * 2.0 * jnp.arange(halves).astype(f32) / HEAD_DIM)
    angles = jnp.arange(length, dtype=jnp.int32).astype(f32)[:, None] * freqs[None, :]
    cosine, sine = jnp.cos(angles), jnp.sin(angles)
    return (
        jnp.tile(jnp.concatenate([cosine, cosine], axis=1), (1, copies)),
        jnp.tile(jnp.concatenate([-sine, sine], axis=1), (1, copies)),
    )


def adam_update(weight, moment, square, gradient, step_rate):
    moment_new = MOMENT_DECAY * moment + (1.0 - MOMENT_DECAY) * gradient
    square_new = MOMENT_DECAY * square + (1.0 - MOMENT_DECAY) * gradient * gradient
    correction = 1.0 - MOMENT_DECAY**STEP
    update = moment_new / correction / (jnp.sqrt(square_new / correction) + ADAM_EPSILON)
    return (weight - step_rate * (update + WEIGHT_DECAY * weight), moment_new, square_new)


def dot(a, b, lhs=1, rhs=0):
    return lax.dot_general(a, b, (((lhs,), (rhs,)), ((), ())), preferred_element_type=f32)


def swap_halves(values, first):
    width = values.shape[1]
    half = HEAD_DIM // 2
    return jnp.where(
        first, pltpu.roll(values, width - half, 1), pltpu.roll(values, half, 1)
    )


def allowed_mask(rows, length):
    row = lax.broadcasted_iota(jnp.int32, (rows, rows), 0)
    col = lax.broadcasted_iota(jnp.int32, (rows, rows), 1)
    return (col <= row) & (row - col < WINDOW) & (col.astype(f32) < length)


def head_lanes(rows, width, head):
    lane = lax.broadcasted_iota(jnp.int32, (rows, width), 1)
    return (lane // HEAD_DIM) == head


def softmax_rows(queries, key_vectors, allowed):
    scores = jnp.where(allowed, dot(queries, key_vectors, 1, 1) * (HEAD_DIM**-0.5), -1e30)
    shifted = jnp.exp(scores - jnp.max(scores, axis=-1, keepdims=True))
    return shifted / jnp.sum(shifted, axis=-1, keepdims=True)


def attention(length, queries, key_vectors, value_vectors):
    rows, width = queries.shape
    allowed = allowed_mask(rows, length)
    total = jnp.zeros((rows, width), f32)
    for head in range(width // HEAD_DIM):
        mine = head_lanes(rows, width, head)
        weights = softmax_rows(jnp.where(mine, queries, 0), key_vectors, allowed)
        total += dot(weights.astype(bf16), jnp.where(mine, value_vectors, 0))
    return total.astype(bf16)


def attention_grads(length, queries, key_vectors, value_vectors, grads):
    rows, width = queries.shape
    allowed = allowed_mask(rows, length)
    grad_q = jnp.zeros((rows, width), f32)
    grad_k = jnp.zeros((rows, width), f32)
    grad_v = jnp.zeros((rows, width), f32)
    for head in range(width // HEAD_DIM):
        mine = head_lanes(rows, width, head)
        q_head = jnp.where(mine, queries, 0)
        g_head = jnp.where(mine, grads, 0)
        weights = softmax_rows(q_head, key_vectors, allowed)
        grad_p = dot(g_head, value_vectors, 1, 1)
        delta = jnp.sum(weights * grad_p, axis=-1, keepdims=True)
        grad_s = jnp.where(allowed, weights * (grad_p - delta), 0.0).astype(bf16)
        grad_q += dot(grad_s, jnp.where(mine, key_vectors, 0))
        grad_k += dot(grad_s, q_head, 0, 0)
        grad_v += dot(weights.astype(bf16), g_head, 0, 0)
    return grad_q, grad_k, grad_v


MESH = pl.DeviceIdType.MESH
RELATIONS = tuple((a, b, d) for a in range(2) for b in range(2) for d in range(2))[1:]


class Place:
    def __init__(self, grps):
        self.grps = grps
        self.s = lax.axis_index("seq")
        self.g = lax.axis_index("grp")
        self.r = lax.axis_index("row")
        self.c = lax.axis_index("core")

    def peer(self, relation):
        ds, dr, dc = relation
        return ((self.s + ds) % 2, self.g, (self.r + dr) % 2, (self.c + dc) % 2)

    def plane(self, dz):
        return (self.s, (self.g + dz) % self.grps, self.r, self.c)

    def rank(self, relation=(0, 0, 0)):
        s, _, r, c = self.peer(relation)
        return (s * 2 + r) * 2 + c

    def seat(self, relation=(0, 0, 0)):
        s, _, r, c = self.peer(relation)
        return (r * 2 + c) * 2 + s

    def corner(self, relation=(0, 0, 0)):
        s, _, r, _ = self.peer(relation)
        return r * 2 + s

    def greet(self):
        barrier = pltpu.get_barrier_semaphore()
        for relation in RELATIONS:
            pl.semaphore_signal(barrier, inc=1, device_id=self.peer(relation), device_id_type=MESH)
        for dz in range(1, self.grps):
            pl.semaphore_signal(barrier, inc=1, device_id=self.plane(dz), device_id_type=MESH)
        pl.semaphore_wait(barrier, len(RELATIONS) + self.grps - 1)


SIBLING = (0, 0, 1)
ACROSS = ((1, 0, 0), (0, 1, 0), (1, 1, 0))


def remote(src, dst, send_sem, recv_sem, device):
    return pltpu.make_async_remote_copy(
        src_ref=src,
        dst_ref=dst,
        send_sem=send_sem,
        recv_sem=recv_sem,
        device_id=device,
        device_id_type=MESH,
    )


class PlaneSum:
    def __init__(self, place, part, near, far, sems):
        self.place, self.part, self.near, self.far = place, part, near, far
        self.near_send, self.near_recv, self.far_send, self.far_recv = sems
        self.first, self.second = [], []

    def start_near(self):
        place = self.place
        for k in range(4):
            block = ((k // 2) * 2 + (1 - place.c)) * 2 + k % 2
            copy = remote(
                self.part.at[block],
                self.near.at[k],
                self.near_send.at[k],
                self.near_recv.at[k],
                place.peer(SIBLING),
            )
            copy.start()
            self.first.append(copy)

    def start_far(self):
        place = self.place
        for copy in self.first:
            copy.wait()
        for k in range(4):
            block = ((k // 2) * 2 + place.c) * 2 + k % 2
            self.near[k] = (self.part[block].astype(f32) + self.near[k].astype(f32)).astype(bf16)
        for d, relation in enumerate(ACROSS):
            copy = remote(
                self.near.at[place.corner(relation)],
                self.far.at[d],
                self.far_send.at[d],
                self.far_recv.at[d],
                place.peer(relation),
            )
            copy.start()
            self.second.append(copy)

    def finish(self):
        for copy in self.second:
            copy.wait()

    def chunk(self, lanes):
        total = self.near[self.place.corner(), :, lanes].astype(f32)
        for d in range(3):
            total += self.far[d, :, lanes].astype(f32)
        return total


class PlaneGather:
    def __init__(self, place, blocks, send, recv):
        self.place, self.blocks, self.send, self.recv = place, blocks, send, recv
        self.first, self.second = [], []

    def copy(self, block, sem, relation):
        copy = remote(
            self.blocks.at[block],
            self.blocks.at[block],
            self.send.at[sem],
            self.recv.at[sem],
            self.place.peer(relation),
        )
        copy.start()
        return copy

    def start(self):
        mine = self.place.seat()
        self.first = [self.copy(mine, d, relation) for d, relation in enumerate(ACROSS)]
        self.first.append(self.copy(mine, 3, SIBLING))

    def forward(self):
        for d, relation in enumerate(ACROSS):
            self.first[d].wait_recv()
            self.second.append(self.copy(self.place.seat(relation), 4 + d, SIBLING))

    def finish(self):
        for copy in self.first[:3]:
            copy.wait_send()
        self.first[3].wait()
        for copy in self.second:
            copy.wait()


class ToOwners:
    def __init__(self, place, shares, landed, met, stage, send, recv, own):
        self.place, self.shares, self.landed, self.met, self.stage = place, shares, landed, met, stage
        self.send, self.recv, self.own_sem = send, recv, own
        self.line = place.grps == 4
        self.own = pltpu.make_async_copy(shares.at[place.g], landed.at[place.g], own)

    def copy(self, block, landing, sem, recv, target):
        place = self.place
        return remote(
            self.shares.at[block],
            landing,
            self.send.at[sem],
            self.recv.at[recv],
            (place.s, target, place.r, place.c),
        )

    def direct(self, g):
        targets = ((2, 1), (2, 0), (1, 3), (1, 2))[g]
        return [self.copy(t, self.landed.at[g], t, g, t) for t in targets]

    def meeting(self, g):
        far, inner = (3, 1) if g == 0 else (0, 2)
        return self.copy(far, self.met, far, inner, inner)

    def joined(self, g):
        far = 3 if g == 1 else 0
        return self.copy(far, self.landed.at[g], far, g, far)

    def start(self):
        place = self.place
        self.own.start()
        if self.line:
            for g in range(4):

                @pl.when(place.g == g)
                def _():
                    if g in (0, 3):
                        self.meeting(g).start()
                    for copy in self.direct(g):
                        copy.start()

        else:
            self.copies = [
                self.copy((place.g + dz) % place.grps, self.landed.at[place.g], dz, dz, (place.g + dz) % place.grps)
                for dz in range(1, place.grps)
            ]
            for copy in self.copies:
                copy.start()
        return self

    def join(self):
        if not self.line:
            return
        for g in (1, 2):

            @pl.when(self.place.g == g)
            def _():
                outer, far = (0, 3) if g == 1 else (3, 0)
                self.copy(far, self.met, far, g, outer).wait_recv()
                copy = pltpu.make_async_copy(self.met, self.stage, self.own_sem)
                self.own.wait()
                copy.start()
                copy.wait()
                if len(self.stage.shape) == 2:
                    self.shares[far] = (
                        self.shares[far].astype(f32) + self.stage[...].astype(f32)
                    ).astype(bf16)
                else:
                    for n in range(self.stage.shape[0]):
                        self.shares[far, n] = (
                            self.shares[far, n].astype(f32) + self.stage[n].astype(f32)
                        ).astype(bf16)
                self.joined(g).start()

        for g in (0, 3):

            @pl.when(self.place.g == g)
            def _():
                self.own.wait()

    def finish(self):
        if not self.line:
            self.own.wait()
            for copy in self.copies:
                copy.wait()
            return
        for g in range(4):

            @pl.when(self.place.g == g)
            def _():
                for j in ((1, 2), (0, 2, 3), (0, 1, 3), (1, 2))[g]:
                    self.copy(g, self.landed.at[j], j, j, j).wait_recv()
                for copy in self.direct(g):
                    copy.wait_send()
                if g in (0, 3):
                    self.meeting(g).wait_send()
                else:
                    self.joined(g).wait_send()

    def holds(self, j):
        g = self.place.g
        return (g % 3 != 0) | (j + g != 3) if self.line else True


class Exchange:
    def __init__(self, place, blocks, held, send, recv, own):
        mine = place.rank()
        kept = held.at[mine // QUAD, mine % QUAD] if len(held.shape) == 4 else held.at[mine]
        self.copies = []
        for n, relation in enumerate(RELATIONS):
            copy = remote(
                blocks.at[place.rank(relation)],
                kept,
                send.at[n],
                recv.at[n],
                place.peer(relation),
            )
            copy.start()
            self.copies.append(copy)
        copy = pltpu.make_async_copy(blocks.at[mine], kept, own)
        copy.start()
        self.copies.append(copy)

    def finish(self):
        for copy in self.copies:
            copy.wait()


LANES = 512


def lanes_of(n, width=LANES):
    return pl.ds(pl.multiple_of(n * width, width), width)


def shares_of(seq, values, weight, part):
    rows = part.shape[1]

    @pl.loop(0, part.shape[2] // LANES)
    def _(n):
        product = dot(values[seq], weight[lanes_of(n)], 1, 1)
        part[2 * seq, :, lanes_of(n)] = product[:rows].astype(bf16)
        part[2 * seq + 1, :, lanes_of(n)] = product[rows:].astype(bf16)


def over_tokens(first, lanes, second, other):
    total = dot(first[0, :, lanes], second[0, :, other], 0, 0)
    for seq in range(1, first.shape[0]):
        total += dot(first[seq, :, lanes], second[seq, :, other], 0, 0)
    return total


def row_shares(first, second, shares):
    grps, seqs, rows, _ = shares.shape
    width = 256
    pieces = width // rows

    @pl.loop(0, first.shape[2] // width)
    def _(b):
        product = over_tokens(first, lanes_of(b, width), second, slice(None)).astype(bf16)
        for p in range(pieces):
            index = b * pieces + p
            shares[index % grps, index // grps] = product[p * rows : (p + 1) * rows]


def summed_rows(landed, holds, blocks):
    seqs, rows = landed.shape[1], blocks.shape[1]
    for seq in range(seqs):
        for quad in range(QUAD):
            block = slice(quad * rows, (quad + 1) * rows)
            total = jnp.zeros((rows, landed.shape[3]), f32)
            for j in range(landed.shape[0]):
                total += jnp.where(holds(j), landed[j, seq, block].astype(f32), 0.0)
            blocks[seq * QUAD + quad] = total.astype(bf16)


def back_kernel(
    grps,
    aligned,
    facts,
    gains,
    cosine,
    sine,
    residual,
    own_tokens,
    own_grad,
    dgu_h,
    up_h,
    hidden_h,
    grad_h,
    second_h,
    first_h,
    out_h,
    qkv_h,
    q_h,
    k_h,
    v_h,
    o_h,
    input_grad,
    gains_sum,
    down_landed,
    out_landed,
    up_held,
    qkv_held,
    up_landed,
    qkv_landed,
    down_met,
    up_met,
    out_met,
    qkv_met,
    wide,
    up,
    acts,
    second,
    out_w,
    qkv,
    part,
    near,
    far,
    blocks,
    turned,
    down_share,
    up_share,
    out_share,
    qkv_share,
    up_sum,
    qkv_sum,
    stage_low,
    stage_wide,
    gain_part,
    gain_plane,
    gain_far,
    load,
    near_send,
    near_recv,
    far_send,
    far_recv,
    all_send,
    all_recv,
    z_send,
    z_recv,
    swap_send,
    swap_recv,
    gain_send,
    gain_recv,
    own_sem,
):
    place = Place(grps)
    rows = residual.shape[0]
    gain_part[...] = jnp.zeros_like(gain_part)
    count, full_rows, head_width = q_h.shape

    hidden = turned.at[:, :, : hidden_h.shape[2]]

    def fetch(src, dst, n):
        copy = pltpu.make_async_copy(src, dst, load.at[n])
        copy.start()
        return copy

    loads = [fetch(dgu_h, wide, 0), fetch(up_h, up, 1)]
    later = [fetch(hidden_h, hidden, 2), fetch(grad_h, acts, 3), fetch(second_h, second, 4)]
    weights = [fetch(out_h, out_w, 5), fetch(qkv_h, qkv, 6)]
    place.greet()
    for copy in loads:
        copy.wait()

    sums = (near_send, near_recv, far_send, far_recv)
    second_sum = PlaneSum(place, part, near, far, sums)
    for r in range(2):
        shares_of(2 * r + 1 - place.c, wide, up, part)
    second_sum.start_near()
    for r in range(2):
        shares_of(2 * r + place.c, wide, up, part)

    for copy in later[:2]:
        copy.wait()
    units = down_share.shape[1]
    width = min(256, hidden.shape[2])

    @pl.loop(0, hidden.shape[2] // width)
    def _(b):
        for half in range(2):
            lanes = slice(half * D // 2, (half + 1) * D // 2)
            product = over_tokens(hidden, lanes_of(b, width), acts, lanes).astype(bf16)
            for p in range(width // units):
                down_share[b * (width // units) + p, :, lanes] = product[p * units : (p + 1) * units]

    def to_owners(n, shares, landed, met, stage):
        return ToOwners(place, shares, landed, met, stage, z_send.at[n], z_recv.at[n], own_sem.at[n]).start()

    down_out = to_owners(0, down_share, down_landed, down_met, stage_low)
    fetch_first = fetch(first_h, acts, 3)
    second_sum.start_far()
    later[2].wait()
    row_shares(second, wide, up_share)
    up_out = to_owners(1, up_share, up_landed, up_met, stage_wide)
    down_out.join()
    heads = [
        fetch(ref, wide.at[:, :, n * head_width : (n + 1) * head_width], 7 + n)
        for n, ref in enumerate((q_h, k_h, v_h, o_h))
    ]

    second_sum.finish()
    mine = place.seat()
    inner = jnp.zeros((rows, 1), f32)
    squares = jnp.zeros((rows, 1), f32)
    for n in range(D // LANES):
        lanes = slice(n * LANES, (n + 1) * LANES)
        grad = second_sum.chunk(lanes)
        values = residual[:, lanes]
        inner += jnp.sum(grad * gains[1:2, lanes] * values, axis=-1, keepdims=True)
        squares += jnp.sum(values * values, axis=-1, keepdims=True)
    scale = lax.rsqrt(squares / D + NORM_EPSILON)
    inner = inner / D
    for n in range(D // LANES):
        lanes = slice(n * LANES, (n + 1) * LANES)
        grad, values = second_sum.chunk(lanes), residual[:, lanes]
        gain_part[1:2, lanes] = jnp.sum(grad * values * scale, axis=0, keepdims=True)
        total = own_grad[:, lanes].astype(f32) + scale * (
            grad * gains[1:2, lanes] - values * scale * scale * inner
        )
        input_grad[:, lanes] = total
        blocks[mine, :, lanes] = total.astype(bf16)

    gather = PlaneGather(place, blocks, all_send, all_recv)
    gather.start()
    gather.forward()
    up_out.join()
    for copy in weights + heads:
        copy.wait()
    gather.finish()

    lane = lax.broadcasted_iota(jnp.int32, (full_rows, head_width), 1)
    first_half = (lane % HEAD_DIM) < HEAD_DIM // 2

    @pl.loop(0, count)
    def _(seq):
        grads = jnp.concatenate(
            [dot(blocks[2 * seq], out_w[...], 1, 1), dot(blocks[2 * seq + 1], out_w[...], 1, 1)],
            axis=0,
        ).astype(bf16)
        queries = wide[seq, :, 0:head_width]
        key_vectors = wide[seq, :, head_width : 2 * head_width]
        value_vectors = wide[seq, :, 2 * head_width : 3 * head_width]
        grad_q, grad_k, grad_v = attention_grads(
            facts[seq, 2:3, 0:1], queries, key_vectors, value_vectors, grads
        )
        for n, grad in enumerate((grad_q, grad_k)):
            values = (grad * HEAD_DIM**-0.5).astype(bf16).astype(f32)
            back = values * cosine[...] - swap_halves(values, first_half) * sine[...]
            turned[seq, :, n * head_width : (n + 1) * head_width] = back.astype(bf16)
        turned[seq, :, 2 * head_width : 3 * head_width] = grad_v.astype(bf16)

    fetch_first.wait()
    row_shares(acts, turned, qkv_share)
    triple = turned.shape[2]
    qkv_out = to_owners(2, qkv_share, qkv_landed, qkv_met, stage_wide.at[:, :, :triple])

    first_sum = PlaneSum(place, part, near, far, sums)
    for r in range(2):
        shares_of(2 * r + 1 - place.c, turned, qkv, part)
    first_sum.start_near()
    for r in range(2):
        shares_of(2 * r + place.c, turned, qkv, part)
    first_sum.start_far()

    out_rows = out_share.shape[1]

    @pl.loop(0, D // LANES)
    def _(n):
        lanes = lanes_of(n)
        total = jnp.zeros((head_width, LANES), f32)
        for seq in range(count):
            values = wide[seq, :, 3 * head_width : 4 * head_width].astype(f32)
            total += dot(values[:rows].astype(bf16), blocks[2 * seq, :, lanes], 0, 0)
            total += dot(values[rows:].astype(bf16), blocks[2 * seq + 1, :, lanes], 0, 0)
        total = total.astype(bf16)
        for j in range(out_share.shape[0]):
            out_share[j, :, lanes] = total[j * out_rows : (j + 1) * out_rows]

    if aligned:
        out_out = to_owners(3, out_share, out_landed, out_met, stage_low.at[:out_rows])
    else:
        out_out = pltpu.make_async_copy(out_share, out_landed, own_sem.at[3])
        out_out.start()

    qkv_out.join()
    first_sum.finish()
    if aligned:
        out_out.join()
    inner = jnp.zeros((rows, 1), f32)
    squares = jnp.zeros((rows, 1), f32)
    for n in range(D // LANES):
        lanes = slice(n * LANES, (n + 1) * LANES)
        grad = first_sum.chunk(lanes)
        values = own_tokens[:, lanes].astype(f32)
        inner += jnp.sum(grad * gains[0:1, lanes] * values, axis=-1, keepdims=True)
        squares += jnp.sum(values * values, axis=-1, keepdims=True)
    scale = lax.rsqrt(squares / D + NORM_EPSILON)
    inner = inner / D
    for n in range(D // LANES):
        lanes = slice(n * LANES, (n + 1) * LANES)
        grad, values = first_sum.chunk(lanes), own_tokens[:, lanes].astype(f32)
        gain_part[0:1, lanes] = jnp.sum(grad * values * scale, axis=0, keepdims=True)
        input_grad[:, lanes] += scale * (
            grad * gains[0:1, lanes] - values * scale * scale * inner
        )

    gain_copies = []
    for n, relation in enumerate(RELATIONS):
        copy = remote(
            gain_part, gain_plane.at[n], gain_send.at[n], gain_recv.at[n], place.peer(relation)
        )
        copy.start()
        gain_copies.append(copy)

    up_out.finish()
    landed = pltpu.make_async_copy(up_landed, up_share, load.at[1])
    landed.start()
    for copy in gain_copies:
        copy.wait()
    total = gain_part[...]
    for n in range(len(RELATIONS)):
        total += gain_plane[n]
    gain_far[0] = total
    gain_copies = []
    for dz in range(1, grps):
        copy = remote(
            gain_far.at[0],
            gain_far.at[dz],
            gain_send.at[7 + dz],
            gain_recv.at[7 + dz],
            place.plane(dz),
        )
        copy.start()
        gain_copies.append(copy)
    landed.wait()
    summed_rows(up_share, up_out.holds, up_sum)
    up_swap = Exchange(place, up_sum, up_held, swap_send.at[0], swap_recv.at[0], own_sem.at[4])
    for copy in gain_copies:
        copy.wait()
    total = gain_far[0]
    for dz in range(1, grps):
        total += gain_far[dz]
    gains_sum[...] = total

    qkv_out.finish()
    landed = pltpu.make_async_copy(qkv_landed, qkv_share, load.at[6])
    landed.start()
    landed.wait()
    summed_rows(qkv_share, qkv_out.holds, qkv_sum)
    qkv_swap = Exchange(place, qkv_sum, qkv_held, swap_send.at[1], swap_recv.at[1], own_sem.at[5])
    if aligned:
        out_out.finish()
    else:
        out_out.wait()
    down_out.finish()
    up_swap.finish()
    qkv_swap.finish()


def backward(
    grps,
    aligned,
    facts,
    gains,
    tables,
    residual,
    own_tokens,
    own_grad,
    grad_both,
    up_local,
    hidden,
    grad_low,
    second_norm,
    first_norm,
    out_local,
    qkv_local,
    heads,
):
    rows = residual.shape[0]
    count, full_rows, head_width = heads[0].shape
    seqs = full_rows // rows
    ranks = seqs * QUAD
    units = hidden.shape[2] // grps
    both = grad_both.shape[2]
    quad_rows = D // (seqs * grps)
    shard = quad_rows // QUAD
    out_rows = head_width // grps if aligned else HEAD_DIM
    triple = 3 * head_width
    out_count = head_width // out_rows
    hbm = pl.BlockSpec(memory_space=pl.ANY)
    vmem = pl.BlockSpec(memory_space=pltpu.VMEM)
    shape = jax.ShapeDtypeStruct
    dma = pltpu.SemaphoreType.DMA
    return pl.pallas_call(
        lambda *refs: back_kernel(grps, aligned, *refs),
        in_specs=[vmem] * 7 + [hbm] * 12,
        out_specs=[vmem] * 2 + [hbm] * 10,
        out_shape=[
            shape((rows, D), f32),
            shape((8, D), f32),
            shape((grps, units, D), bf16),
            shape((out_count, out_rows, D), bf16),
            shape((ranks, shard, both), bf16),
            shape((ranks, shard, triple), bf16),
            shape((grps, seqs, quad_rows, both), bf16),
            shape((grps, seqs, quad_rows, triple), bf16),
            shape((units, D), bf16),
            shape((seqs, quad_rows, both), bf16),
            shape((out_rows, D), bf16),
            shape((seqs, quad_rows, triple), bf16),
        ],
        scratch_shapes=[
            pltpu.VMEM((count, full_rows, both), bf16),
            pltpu.VMEM((D, both), bf16),
            pltpu.VMEM((count, full_rows, D), bf16),
            pltpu.VMEM((count, full_rows, D), bf16),
            pltpu.VMEM((head_width, D), bf16),
            pltpu.VMEM((D, triple), bf16),
            pltpu.VMEM((ranks, rows, D), bf16),
            pltpu.VMEM((4, rows, D), bf16),
            pltpu.VMEM((3, rows, D), bf16),
            pltpu.VMEM((ranks, rows, D), bf16),
            pltpu.VMEM((count, full_rows, triple), bf16),
            pltpu.VMEM((grps, units, D), bf16),
            pltpu.VMEM((grps, seqs, quad_rows, both), bf16),
            pltpu.VMEM((out_count, out_rows, D), bf16),
            pltpu.VMEM((grps, seqs, quad_rows, triple), bf16),
            pltpu.VMEM((ranks, shard, both), bf16),
            pltpu.VMEM((ranks, shard, triple), bf16),
            pltpu.VMEM((units, D), bf16),
            pltpu.VMEM((seqs, quad_rows, both), bf16),
            pltpu.VMEM((8, D), f32),
            pltpu.VMEM((7, 8, D), f32),
            pltpu.VMEM((grps, 8, D), f32),
            dma((11,)),
            dma((4,)),
            dma((4,)),
            dma((3,)),
            dma((3,)),
            dma((7,)),
            dma((7,)),
            dma((4, grps)),
            dma((4, grps)),
            dma((2, 7)),
            dma((2, 7)),
            dma((7 + grps,)),
            dma((7 + grps,)),
            dma((6,)),
        ],
        compiler_params=pltpu.CompilerParams(
            collective_id=0, has_side_effects=True, vmem_limit_bytes=VMEM_LIMIT
        ),
        cost_estimate=pl.CostEstimate(
            flops=30 * 10**9, bytes_accessed=60 * 2**20, transcendentals=2 * 10**6
        ),
        name="backward",
    )(
        facts,
        gains,
        *tables,
        residual,
        own_tokens,
        own_grad,
        grad_both,
        up_local,
        hidden,
        grad_low,
        second_norm,
        first_norm,
        out_local,
        qkv_local,
        *heads,
    )


class FromOwners:
    def __init__(self, place, source, landed, landing, send, recv, own):
        self.place, self.source, self.send, self.recv = place, source, send, recv
        self.slot = lambda j: landing(landed, j)
        self.own = pltpu.make_async_copy(source, self.slot(place.g), own)
        self.line = place.grps == 4

    def copy(self, source, slot, sem, recv, target):
        place = self.place
        return remote(
            source, self.slot(slot), self.send.at[sem], self.recv.at[recv], (place.s, target, place.r, place.c)
        )

    def direct(self, g):
        targets = ((1, 2, 3), (0, 2), (3, 1), (2, 1, 0))[g]
        return [self.copy(self.source, g, t, g, t) for t in targets]

    def passed_on(self, g):
        inner, end = 3 - g, 0 if g == 1 else 3
        return self.copy(self.slot(inner), inner, 3 - end, inner, end)

    def arrival(self, j):
        return self.copy(self.source, j, j, j, j)

    def start(self):
        place = self.place
        self.own.start()
        if self.line:
            for g in range(4):

                @pl.when(place.g == g)
                def _():
                    for copy in self.direct(g):
                        copy.start()

        else:
            self.copies = [
                self.copy(self.source, place.g, dz, dz, (place.g + dz) % place.grps)
                for dz in range(1, place.grps)
            ]
            for copy in self.copies:
                copy.start()

    def relay(self):
        if self.line:
            for g in (1, 2):

                @pl.when(self.place.g == g)
                def _():
                    self.arrival(3 - g).wait_recv()
                    self.passed_on(g).start()

    def finish(self):
        self.own.wait()
        if self.line:
            for g in range(4):

                @pl.when(self.place.g == g)
                def _():
                    for j in range(4):
                        if j != g and not (g in (1, 2) and j == 3 - g):
                            self.arrival(j).wait_recv()
                    for copy in self.direct(g):
                        copy.wait_send()
                    if g in (1, 2):
                        self.passed_on(g).wait_send()

        else:
            for copy in self.copies:
                copy.wait()


def shares_from(seq, values, weight, part):
    rows = part.shape[1]

    @pl.loop(0, part.shape[2] // LANES)
    def _(n):
        product = dot(values[seq], weight[:, lanes_of(n)])
        part[2 * seq, :, lanes_of(n)] = product[:rows].astype(bf16)
        part[2 * seq + 1, :, lanes_of(n)] = product[rows:].astype(bf16)


def times_slices(values, weight, lanes):
    seqs, grps, quad, shard, _ = weight.shape
    depth = quad * shard
    total = None
    for n in range(seqs * grps):
        piece = weight[n // grps, n % grps, :, :, lanes]
        term = dot(values[:, n * depth : (n + 1) * depth], piece.reshape(depth, piece.shape[2]))
        total = term if total is None else total + term
    return total


def both_blocks(blocks, seq):
    return jnp.concatenate([blocks[2 * seq].astype(f32), blocks[2 * seq + 1].astype(f32)], axis=0)


def forward_kernel(
    grps,
    aligned,
    cosine,
    sine,
    own_facts,
    tokens_h,
    own_grad_h,
    qkv_sent,
    up_sent,
    out_own,
    down_own,
    residual,
    gains,
    facts,
    first_h,
    q_h,
    k_h,
    v_h,
    o_h,
    second_h,
    grad_h,
    hidden_h,
    dgu_h,
    qkv_landed,
    up_landed,
    out_landed,
    down_landed,
    blocks,
    grad_blocks,
    norm,
    grad_seq,
    qkv_rank,
    up_rank,
    qkv,
    up,
    out_w,
    down,
    heads,
    part,
    near,
    far,
    both,
    hidden,
    dgu,
    all_facts,
    load,
    store,
    swap_send,
    swap_recv,
    near_send,
    near_recv,
    far_send,
    far_recv,
    all_send,
    all_recv,
    z_send,
    z_recv,
    fact_send,
    fact_recv,
    own_sem,
):
    place = Place(grps)
    count, full_rows, _ = norm.shape
    rows = residual.shape[0]
    head_width = heads.shape[3]
    mine, rank = place.seat(), place.rank()

    def fetch(src, dst, n):
        copy = pltpu.make_async_copy(src, dst, load.at[n])
        copy.start()
        return copy

    def keep(src, dst, n):
        copy = pltpu.make_async_copy(src, dst, store.at[n])
        copy.start()
        return copy

    facts[rank] = own_facts[...]
    own_blocks = [fetch(tokens_h, blocks.at[mine], 0), fetch(own_grad_h, grad_blocks.at[mine], 1)]
    place.greet()

    def plane_rows(ref, j):
        return ref.at[:, j]

    def own_rows(ref, j):
        size = ref.shape[0] // grps
        return ref.at[pl.ds(pl.multiple_of(j * size, size), size)]

    def from_owners(n, source, landed, landing):
        return FromOwners(place, source, landed, landing, z_send.at[n], z_recv.at[n], own_sem.at[n])

    down_z = from_owners(3, down_own, down_landed, own_rows)
    if aligned:
        out_z = from_owners(2, out_own, out_landed, own_rows)
    qkv_swap = Exchange(place, qkv_sent, qkv_rank, swap_send.at[0], swap_recv.at[0], own_sem.at[4])
    fact_copies = []
    for n, relation in enumerate(RELATIONS):
        copy = remote(own_facts, facts.at[rank], fact_send.at[n], fact_recv.at[n], place.peer(relation))
        copy.start()
        fact_copies.append(copy)
    for copy in own_blocks:
        copy.wait()
    token_gather = PlaneGather(place, blocks, all_send.at[0], all_recv.at[0])
    token_gather.start()
    up_swap = Exchange(place, up_sent, up_rank, swap_send.at[1], swap_recv.at[1], own_sem.at[5])
    qkv_swap.finish()
    seqs = qkv_landed.shape[0]
    qkv_z = from_owners(0, qkv_rank, qkv_landed, plane_rows)
    up_z = from_owners(1, up_rank, up_landed, plane_rows)
    qkv_z.start()
    if aligned:
        out_z.start()
    for copy in fact_copies:
        copy.wait()
    all_facts[place.g] = facts[...]
    fact_copies = []
    for dz in range(1, grps):
        copy = remote(
            facts,
            all_facts.at[place.g],
            fact_send.at[7 + dz],
            fact_recv.at[7 + dz],
            place.plane(dz),
        )
        copy.start()
        fact_copies.append(copy)
    token_gather.forward()
    up_swap.finish()
    for copy in fact_copies:
        copy.wait()
    width = D // (seqs * grps * QUAD)
    for n in range(seqs * grps):
        pieces = [all_facts[n % grps, (n // grps) * QUAD + q, :, :width] for q in range(QUAD)]
        gains[:, n * QUAD * width : (n + 1) * QUAD * width] = jnp.concatenate(pieces, axis=1)
    qkv_z.relay()
    token_gather.finish()
    grad_gather = PlaneGather(place, grad_blocks, all_send.at[1], all_recv.at[1])
    grad_gather.start()

    @pl.loop(0, count)
    def _(seq):
        values = both_blocks(blocks, seq)
        scale = lax.rsqrt(jnp.mean(values * values, axis=-1, keepdims=True) + NORM_EPSILON)
        norm[seq] = (values * scale * gains[0:1, :]).astype(bf16)

    stores = [keep(norm, first_h, 0)]
    if aligned:
        out_z.relay()
    grad_gather.forward()
    qkv_z.finish()
    up_z.start()
    fetch(qkv_landed, qkv, 2).wait()

    lane = lax.broadcasted_iota(jnp.int32, (full_rows, head_width), 1)
    first_half = (lane % HEAD_DIM) < HEAD_DIM // 2

    @pl.loop(0, count)
    def _(seq):
        for n in range(3):
            lanes = slice(n * head_width, (n + 1) * head_width)
            values = times_slices(norm[seq], qkv, lanes)
            if n < 2:
                values = values * cosine[...] + swap_halves(values, first_half) * sine[...]
            heads[n, seq] = values.astype(bf16)
        heads[3, seq] = attention(facts[seq, 2:3, 0:1], heads[0, seq], heads[1, seq], heads[2, seq])

    stores += [keep(heads.at[n], ref, 1 + n) for n, ref in enumerate((q_h, k_h, v_h, o_h))]
    if aligned:
        out_z.finish()
        fetch(out_landed, out_w, 3).wait()
    else:
        fetch(out_own, out_w, 3).wait()

    plane_sum = PlaneSum(place, part, near, far, (near_send, near_recv, far_send, far_recv))
    mixed = heads.at[3]
    for r in range(2):
        shares_from(2 * r + 1 - place.c, mixed, out_w, part)
    plane_sum.start_near()
    for r in range(2):
        shares_from(2 * r + place.c, mixed, out_w, part)
    up_z.relay()
    plane_sum.start_far()
    grad_gather.finish()

    @pl.loop(0, count)
    def _(seq):
        grad_seq[seq] = both_blocks(grad_blocks, seq).astype(bf16)

    stores.append(keep(grad_seq, grad_h, 6))
    fetch(tokens_h, grad_blocks.at[mine], 4).wait()
    plane_sum.finish()
    squares = jnp.zeros((rows, 1), f32)
    for n in range(D // LANES):
        lanes = slice(n * LANES, (n + 1) * LANES)
        values = grad_blocks[mine, :, lanes].astype(f32) + plane_sum.chunk(lanes)
        residual[:, lanes] = values
        squares += jnp.sum(values * values, axis=-1, keepdims=True)
    scale = lax.rsqrt(squares / D + NORM_EPSILON)
    for n in range(D // LANES):
        lanes = slice(n * LANES, (n + 1) * LANES)
        blocks[mine, :, lanes] = (residual[:, lanes] * scale * gains[1:2, lanes]).astype(bf16)
    norm_gather = PlaneGather(place, blocks, all_send.at[2], all_recv.at[2])
    norm_gather.start()
    down_z.start()
    norm_gather.forward()
    stores[0].wait()
    norm_gather.finish()

    @pl.loop(0, count)
    def _(seq):
        norm[seq] = both_blocks(blocks, seq).astype(bf16)

    stores[0] = keep(norm, second_h, 5)
    up_z.finish()
    down_z.relay()
    fetch(up_landed, up, 5).wait()
    half = hidden.shape[2]

    @pl.loop(0, count)
    def _(seq):
        gate = times_slices(norm[seq], up, slice(0, half))
        above = times_slices(norm[seq], up, slice(half, 2 * half))
        both[seq, :, :half] = gate
        both[seq, :, half:] = above
        hidden[seq] = (gate * jax.nn.sigmoid(gate) * above).astype(bf16)

    stores.append(keep(hidden, hidden_h, 7))
    down_z.finish()
    fetch(down_landed, down, 6).wait()

    @pl.loop(0, count)
    def _(seq):
        grads = dot(grad_seq[seq], down[...], 1, 1)
        gate, above = both[seq, :, :half], both[seq, :, half:]
        sigmoid = jax.nn.sigmoid(gate)
        dgu[seq, :, :half] = (grads * above * sigmoid * (1.0 + gate * (1.0 - sigmoid))).astype(bf16)
        dgu[seq, :, half:] = (grads * (gate * sigmoid)).astype(bf16)

    stores.append(keep(dgu, dgu_h, 8))
    for copy in stores:
        copy.wait()


def forward(grps, aligned, tables, own_facts, tokens, own_grad, qkv_sent, up_sent, out_own, down_own):
    rows = tokens.shape[0]
    ranks, shard, triple = qkv_sent.shape
    both = up_sent.shape[2]
    seqs = ranks // QUAD
    count, full_rows, head_width = QUAD, rows * seqs, triple // 3
    half = both // 2
    hbm = pl.BlockSpec(memory_space=pl.ANY)
    vmem = pl.BlockSpec(memory_space=pltpu.VMEM)
    shape = jax.ShapeDtypeStruct
    dma = pltpu.SemaphoreType.DMA
    by_heads = shape((count, full_rows, head_width), bf16)
    return pl.pallas_call(
        lambda *refs: forward_kernel(grps, aligned, *refs),
        in_specs=[vmem] * 3 + [hbm] * 6,
        out_specs=[vmem] * 3 + [hbm] * 13,
        out_shape=[
            shape((rows, D), f32),
            shape((8, D), f32),
            shape((ranks, 8, 128), f32),
            shape((count, full_rows, D), bf16),
            by_heads,
            by_heads,
            by_heads,
            by_heads,
            shape((count, full_rows, D), bf16),
            shape((count, full_rows, D), bf16),
            shape((count, full_rows, half), bf16),
            shape((count, full_rows, both), bf16),
            shape((seqs, grps, QUAD, shard, triple), bf16),
            shape((seqs, grps, QUAD, shard, both), bf16),
            shape((head_width, D), bf16),
            shape((half, D), bf16),
        ],
        scratch_shapes=[
            pltpu.VMEM((ranks, rows, D), bf16),
            pltpu.VMEM((ranks, rows, D), bf16),
            pltpu.VMEM((count, full_rows, D), bf16),
            pltpu.VMEM((count, full_rows, D), bf16),
            pltpu.VMEM((seqs, QUAD, shard, triple), bf16),
            pltpu.VMEM((seqs, QUAD, shard, both), bf16),
            pltpu.VMEM((seqs, grps, QUAD, shard, triple), bf16),
            pltpu.VMEM((seqs, grps, QUAD, shard, both), bf16),
            pltpu.VMEM((head_width, D), bf16),
            pltpu.VMEM((half, D), bf16),
            pltpu.VMEM((4, count, full_rows, head_width), bf16),
            pltpu.VMEM((ranks, rows, D), bf16),
            pltpu.VMEM((4, rows, D), bf16),
            pltpu.VMEM((3, rows, D), bf16),
            pltpu.VMEM((count, full_rows, both), f32),
            pltpu.VMEM((count, full_rows, half), bf16),
            pltpu.VMEM((count, full_rows, both), bf16),
            pltpu.VMEM((grps, ranks, 8, 128), f32),
            dma((7,)),
            dma((9,)),
            dma((2, 7)),
            dma((2, 7)),
            dma((4,)),
            dma((4,)),
            dma((3,)),
            dma((3,)),
            dma((3, 7)),
            dma((3, 7)),
            dma((4, grps)),
            dma((4, grps)),
            dma((7 + grps,)),
            dma((7 + grps,)),
            dma((6,)),
        ],
        compiler_params=pltpu.CompilerParams(
            collective_id=1, has_side_effects=True, vmem_limit_bytes=VMEM_LIMIT
        ),
        cost_estimate=pl.CostEstimate(
            flops=20 * 10**9, bytes_accessed=60 * 2**20, transcendentals=4 * 10**6
        ),
        name="forward",
    )(*tables, own_facts, tokens, own_grad, qkv_sent, up_sent, out_own, down_own)


ADAM_WIDTH = 512


def adam_step(gradient, weight, moment, square, step_rate, outs):
    results = adam_update(weight[...], moment[...], square[...], gradient, step_rate)
    for out, result in zip(outs, results):
        out[...] = result
    outs[3][...] = results[0].astype(bf16)


def adam_ranks_kernel(lanes, step_rate, held, weight, moment, square, *outs):
    pieces = [
        held[0, q, :, n * lanes : (n + 1) * lanes] for n in range(128 // lanes) for q in range(QUAD)
    ]
    gradient = jnp.concatenate([piece.astype(f32) for piece in pieces], axis=1)
    adam_step(gradient, weight, moment, square, step_rate, outs)


def adam_planes_kernel(step_rate, holds, landed, weight, moment, square, *outs):
    total = jnp.zeros(weight.shape, f32)
    for j in range(landed.shape[0]):
        total += jnp.where(holds[j] > 0, landed[j].astype(f32), 0.0)
    adam_step(total, weight, moment, square, step_rate, outs)


def adam_call(kernel, grads, grad_specs, state):
    rows, columns = state[0].shape
    block = pl.BlockSpec((rows, ADAM_WIDTH), lambda n: (0, n))
    like = jax.ShapeDtypeStruct((rows, columns), f32)
    return pl.pallas_call(
        kernel,
        grid=(columns // ADAM_WIDTH,),
        in_specs=grad_specs + [block] * 3,
        out_specs=[block] * 4,
        out_shape=[like] * 3 + [jax.ShapeDtypeStruct((rows, columns), bf16)],
        cost_estimate=pl.CostEstimate(
            flops=rows * columns * 16, bytes_accessed=rows * columns * 28, transcendentals=rows * columns
        ),
        name="adam",
    )(*grads, *state)


def adam_from_ranks(held, seqs, parts, lanes, step_rate, *state):
    ranks, rows, columns = held.shape
    blocks = columns // (parts * 128)
    grouped = held.reshape(seqs, QUAD, rows, columns)
    spec = pl.BlockSpec(
        (1, QUAD, rows, 128),
        lambda n: ((n // blocks) % seqs, 0, 0, n // (blocks * seqs) * blocks + n % blocks),
    )
    return adam_call(
        lambda *refs: adam_ranks_kernel(lanes, step_rate, *refs), (grouped,), [spec], state
    )


def adam_from_planes(landed, holds, step_rate, *state):
    planes, rows, _ = landed.shape
    specs = [
        pl.BlockSpec(memory_space=pltpu.SMEM),
        pl.BlockSpec((planes, rows, ADAM_WIDTH), lambda n: (0, 0, n)),
    ]
    return adam_call(
        lambda *refs: adam_planes_kernel(step_rate, *refs), (holds, landed), specs, state
    )


def to_ranks(columns):
    rows, parts, seqs, units, quad, lanes = columns.shape
    return columns.transpose(2, 4, 0, 1, 3, 5).reshape(seqs * quad, rows, parts * units * lanes)


def seat_sum(partial):
    return lax.psum_scatter(
        partial.astype(bf16), SEATS, scatter_dimension=0, tiled=True
    ).astype(f32)


def on_device(
    tokens,
    cotangent,
    lengths,
    qkv_weight,
    qkv_moment,
    qkv_square,
    out_weight,
    out_moment,
    out_square,
    up_weight,
    up_moment,
    up_square,
    down_weight,
    down_moment,
    down_square,
    norm_gains,
    gains_moment,
    gains_square,
):
    seqs = lax.axis_size("seq")
    grps = lax.axis_size("grp")
    ranks = seqs * QUAD
    own_rows = tokens.shape[1]
    full_rows = own_rows * seqs
    all_rows = full_rows * QUAD
    shard = qkv_weight.shape[0]
    heads_local = HEADS // ranks
    head_width = heads_local * HEAD_DIM
    units = down_weight.shape[0]
    aligned = out_weight.shape[0] == HEAD_DIM
    tables = rotate_table(full_rows, heads_local)

    positions = lax.axis_index("seq") * own_rows + jnp.arange(own_rows, dtype=jnp.int32)
    own_grad = jnp.where((positions < lengths[0])[:, None], cotangent[0], 0)
    own_gains = norm_gains.shape[1]
    own_facts = jnp.zeros((8, 128), f32)
    own_facts = own_facts.at[:2, :own_gains].set(norm_gains.astype(bf16).astype(f32))
    own_facts = own_facts.at[2].set(lengths[0].astype(f32))

    qkv_sent = to_ranks(
        qkv_weight.astype(bf16).reshape(shard, 3, seqs, heads_local, QUAD, HEAD_DIM)
    )
    up_sent = to_ranks(up_weight.astype(bf16).reshape(shard, 2, seqs, grps, QUAD, units))
    out_low = out_weight.astype(bf16)
    if not aligned:
        out_all = lax.all_gather(out_low, EVERY, axis=0, tiled=True)
        out_all = out_all.reshape(seqs, heads_local, QUAD, HEAD_DIM, D)
        seat = lax.axis_index("row") * 2 + lax.axis_index("core")
        out_low = lax.dynamic_index_in_dim(
            lax.dynamic_index_in_dim(out_all, lax.axis_index("seq"), 0, False), seat, 1, False
        ).reshape(head_width, D)
    (
        residual,
        gains,
        facts,
        first_norm,
        queries,
        key_vectors,
        value_vectors,
        attended,
        second_norm,
        grad_low,
        hidden,
        grad_both,
        qkv_local,
        up_local,
        out_local,
        down_local,
    ) = forward(
        grps,
        aligned,
        tables,
        own_facts,
        tokens[0],
        own_grad,
        qkv_sent,
        up_sent,
        out_low,
        down_weight.astype(bf16),
    )
    if not aligned:
        out_local = out_low
    (
        input_grad,
        gains_total,
        down_planes,
        out_planes,
        up_ranks,
        qkv_ranks,
        *_,
    ) = backward(
        grps,
        aligned,
        facts,
        gains,
        tables,
        residual,
        tokens[0],
        own_grad,
        grad_both,
        up_local.reshape(D, -1),
        hidden,
        grad_low,
        second_norm,
        first_norm,
        out_local,
        qkv_local.reshape(D, -1),
        (queries, key_vectors, value_vectors, attended),
    )
    block_output = (
        residual + seat_sum(dot(hidden.reshape(all_rows, -1), down_local))
    ).astype(bf16)
    if aligned:
        out_sum = out_planes
    else:
        placed_term = jnp.zeros((seqs, QUAD, heads_local, HEAD_DIM, D), bf16)
        placed_term = lax.dynamic_update_slice(
            placed_term,
            out_planes.reshape(1, 1, heads_local, HEAD_DIM, D),
            (lax.axis_index("seq"), seat, 0, 0, 0),
        )
        out_sum = lax.psum_scatter(
            placed_term.transpose(0, 2, 1, 3, 4).reshape(D, D),
            EVERY,
            scatter_dimension=0,
            tiled=True,
        )[None]
    device = ((lax.axis_index("seq") * grps + lax.axis_index("grp")) * 2 + lax.axis_index("row")) * 2
    gains_sum = lax.dynamic_slice(
        gains_total, (0, (device + lax.axis_index("core")) * own_gains), (2, own_gains)
    )
    planes = jnp.arange(grps)
    plane = lax.axis_index("grp")
    holds = ((planes + plane != 3) | (plane % 3 != 0) | (grps != 4)).astype(jnp.int32)
    qkv_new = adam_from_ranks(
        qkv_ranks, seqs, 3, HEAD_DIM, D ** (-0.5), qkv_weight, qkv_moment, qkv_square
    )
    up_new = adam_from_ranks(
        up_ranks, seqs, 2, units, D ** (-0.5), up_weight, up_moment, up_square
    )
    out_new = adam_from_planes(
        out_sum, holds, (D // 128) ** (-0.5), out_weight, out_moment, out_square
    )
    down_new = adam_from_planes(
        down_planes, holds, FF ** (-0.5), down_weight, down_moment, down_square
    )
    gains_new = adam_update(norm_gains, gains_moment, gains_square, gains_sum, 0.3)
    return (
        block_output[None],
        input_grad[None],
        *qkv_new,
        *out_new,
        *up_new,
        *down_new,
        *gains_new,
    )


def solution(mesh):
    seqs, rest = mesh.shape["seq"], mesh.shape["fsdp"]
    planes = Mesh(
        mesh.devices.reshape(seqs, rest // QUAD, 2, 2), ("seq", "grp", "row", "core")
    )
    rows = P(("grp", "row", "core"), "seq", None)
    shards = P(EVERY, None)
    gains = P(None, EVERY)
    return jax.shard_map(
        on_device,
        mesh=planes,
        in_specs=(rows, rows, P(("grp", "row", "core"))) + (shards,) * 12 + (gains,) * 3,
        out_specs=(rows, rows) + (shards,) * 16 + (gains,) * 3,
        check_vma=False,
    )
```

```python
import math

import jax
import jax.numpy as jnp
from jax import lax
from jax.experimental import pallas as pl
from jax.experimental.pallas import tpu as pltpu
from jax.sharding import Mesh, PartitionSpec as P

D = 2048
HEADS = 32
HEAD_DIM = 64
FF = 4096
WINDOW = 128
STEP = 5


NORM_EPSILON = 1e-05
MOMENT_DECAY = 0.5
WEIGHT_DECAY = 0.1
ADAM_EPSILON = 1e-08

SEATS = ("row", "core", "seq")
RANKS = ("seq", "row", "core")
EVERY = ("seq", "grp", "row", "core")
QUAD = 4
VMEM_LIMIT = 63 * 2**20

bf16 = jnp.bfloat16
f32 = jnp.float32


def rotate_table(length, copies):
    halves = HEAD_DIM // 2
    freqs = jnp.exp(-math.log(10000.0) * 2.0 * jnp.arange(halves).astype(f32) / HEAD_DIM)
    angles = jnp.arange(length, dtype=jnp.int32).astype(f32)[:, None] * freqs[None, :]
    cosine, sine = jnp.cos(angles), jnp.sin(angles)
    return (
        jnp.tile(jnp.concatenate([cosine, cosine], axis=1), (1, copies)),
        jnp.tile(jnp.concatenate([-sine, sine], axis=1), (1, copies)),
    )


def adam_update(weight, moment, square, gradient, step_rate):
    moment_new = MOMENT_DECAY * moment + (1.0 - MOMENT_DECAY) * gradient
    square_new = MOMENT_DECAY * square + (1.0 - MOMENT_DECAY) * gradient * gradient
    correction = 1.0 - MOMENT_DECAY**STEP
    update = moment_new / correction / (jnp.sqrt(square_new / correction) + ADAM_EPSILON)
    return (weight - step_rate * (update + WEIGHT_DECAY * weight), moment_new, square_new)


def dot(a, b, lhs=1, rhs=0):
    return lax.dot_general(a, b, (((lhs,), (rhs,)), ((), ())), preferred_element_type=f32)


def swap_halves(values, first):
    width = values.shape[1]
    half = HEAD_DIM // 2
    return jnp.where(
        first, pltpu.roll(values, width - half, 1), pltpu.roll(values, half, 1)
    )


def allowed_mask(rows, length):
    row = lax.broadcasted_iota(jnp.int32, (rows, rows), 0)
    col = lax.broadcasted_iota(jnp.int32, (rows, rows), 1)
    return (col <= row) & (row - col < WINDOW) & (col.astype(f32) < length)


def head_lanes(rows, width, head):
    lane = lax.broadcasted_iota(jnp.int32, (rows, width), 1)
    return (lane // HEAD_DIM) == head


def softmax_rows(queries, key_vectors, allowed):
    scores = jnp.where(allowed, dot(queries, key_vectors, 1, 1) * (HEAD_DIM**-0.5), -1e30)
    shifted = jnp.exp(scores - jnp.max(scores, axis=-1, keepdims=True))
    return shifted / jnp.sum(shifted, axis=-1, keepdims=True)


def attention(length, queries, key_vectors, value_vectors):
    rows, width = queries.shape
    allowed = allowed_mask(rows, length)
    total = jnp.zeros((rows, width), f32)
    for head in range(width // HEAD_DIM):
        mine = head_lanes(rows, width, head)
        weights = softmax_rows(jnp.where(mine, queries, 0), key_vectors, allowed)
        total += dot(weights.astype(bf16), jnp.where(mine, value_vectors, 0))
    return total.astype(bf16)


def attention_grads(length, queries, key_vectors, value_vectors, grads):
    rows, width = queries.shape
    allowed = allowed_mask(rows, length)
    grad_q = jnp.zeros((rows, width), f32)
    grad_k = jnp.zeros((rows, width), f32)
    grad_v = jnp.zeros((rows, width), f32)
    for head in range(width // HEAD_DIM):
        mine = head_lanes(rows, width, head)
        q_head = jnp.where(mine, queries, 0)
        g_head = jnp.where(mine, grads, 0)
        weights = softmax_rows(q_head, key_vectors, allowed)
        grad_p = dot(g_head, value_vectors, 1, 1)
        delta = jnp.sum(weights * grad_p, axis=-1, keepdims=True)
        grad_s = jnp.where(allowed, weights * (grad_p - delta), 0.0).astype(bf16)
        grad_q += dot(grad_s, jnp.where(mine, key_vectors, 0))
        grad_k += dot(grad_s, q_head, 0, 0)
        grad_v += dot(weights.astype(bf16), g_head, 0, 0)
    return grad_q, grad_k, grad_v


MESH = pl.DeviceIdType.MESH
RELATIONS = tuple((a, b, d) for a in range(2) for b in range(2) for d in range(2))[1:]


class Place:
    def __init__(self, grps):
        self.grps = grps
        self.s = lax.axis_index("seq")
        self.g = lax.axis_index("grp")
        self.r = lax.axis_index("row")
        self.c = lax.axis_index("core")

    def peer(self, relation):
        ds, dr, dc = relation
        return ((self.s + ds) % 2, self.g, (self.r + dr) % 2, (self.c + dc) % 2)

    def plane(self, dz):
        return (self.s, (self.g + dz) % self.grps, self.r, self.c)

    def rank(self, relation=(0, 0, 0)):
        s, _, r, c = self.peer(relation)
        return (s * 2 + r) * 2 + c

    def seat(self, relation=(0, 0, 0)):
        s, _, r, c = self.peer(relation)
        return (r * 2 + c) * 2 + s

    def corner(self, relation=(0, 0, 0)):
        s, _, r, _ = self.peer(relation)
        return r * 2 + s

    def greet(self):
        barrier = pltpu.get_barrier_semaphore()
        for relation in RELATIONS:
            pl.semaphore_signal(barrier, inc=1, device_id=self.peer(relation), device_id_type=MESH)
        for dz in range(1, self.grps):
            pl.semaphore_signal(barrier, inc=1, device_id=self.plane(dz), device_id_type=MESH)
        pl.semaphore_wait(barrier, len(RELATIONS) + self.grps - 1)


SIBLING = (0, 0, 1)
ACROSS = ((1, 0, 0), (0, 1, 0), (1, 1, 0))


def remote(src, dst, send_sem, recv_sem, device):
    return pltpu.make_async_remote_copy(
        src_ref=src,
        dst_ref=dst,
        send_sem=send_sem,
        recv_sem=recv_sem,
        device_id=device,
        device_id_type=MESH,
    )


class PlaneSum:
    def __init__(self, place, part, near, far, sems):
        self.place, self.part, self.near, self.far = place, part, near, far
        self.near_send, self.near_recv, self.far_send, self.far_recv = sems
        self.first, self.second = [], []

    def start_near(self):
        place = self.place
        for k in range(4):
            block = ((k // 2) * 2 + (1 - place.c)) * 2 + k % 2
            copy = remote(
                self.part.at[block],
                self.near.at[k],
                self.near_send.at[k],
                self.near_recv.at[k],
                place.peer(SIBLING),
            )
            copy.start()
            self.first.append(copy)

    def start_far(self):
        place = self.place
        for copy in self.first:
            copy.wait()
        for k in range(4):
            block = ((k // 2) * 2 + place.c) * 2 + k % 2
            self.near[k] = (self.part[block].astype(f32) + self.near[k].astype(f32)).astype(bf16)
        for d, relation in enumerate(ACROSS):
            copy = remote(
                self.near.at[place.corner(relation)],
                self.far.at[d],
                self.far_send.at[d],
                self.far_recv.at[d],
                place.peer(relation),
            )
            copy.start()
            self.second.append(copy)

    def finish(self):
        for copy in self.second:
            copy.wait()

    def chunk(self, lanes):
        total = self.near[self.place.corner(), :, lanes].astype(f32)
        for d in range(3):
            total += self.far[d, :, lanes].astype(f32)
        return total


class PlaneGather:
    def __init__(self, place, blocks, send, recv):
        self.place, self.blocks, self.send, self.recv = place, blocks, send, recv
        self.first, self.second = [], []

    def copy(self, block, sem, relation):
        copy = remote(
            self.blocks.at[block],
            self.blocks.at[block],
            self.send.at[sem],
            self.recv.at[sem],
            self.place.peer(relation),
        )
        copy.start()
        return copy

    def start(self):
        mine = self.place.seat()
        self.first = [self.copy(mine, d, relation) for d, relation in enumerate(ACROSS)]
        self.first.append(self.copy(mine, 3, SIBLING))

    def forward(self):
        for d, relation in enumerate(ACROSS):
            self.first[d].wait_recv()
            self.second.append(self.copy(self.place.seat(relation), 4 + d, SIBLING))

    def finish(self):
        for copy in self.first[:3]:
            copy.wait_send()
        self.first[3].wait()
        for copy in self.second:
            copy.wait()


class ToOwners:
    def __init__(self, place, shares, landed, met, stage, send, recv, own):
        self.place, self.shares, self.landed, self.met, self.stage = place, shares, landed, met, stage
        self.send, self.recv, self.own_sem = send, recv, own
        self.line = place.grps == 4
        self.own = pltpu.make_async_copy(shares.at[place.g], landed.at[place.g], own)

    def copy(self, block, landing, sem, recv, target):
        place = self.place
        return remote(
            self.shares.at[block],
            landing,
            self.send.at[sem],
            self.recv.at[recv],
            (place.s, target, place.r, place.c),
        )

    def direct(self, g):
        targets = ((2, 1), (2, 0), (1, 3), (1, 2))[g]
        return [self.copy(t, self.landed.at[g], t, g, t) for t in targets]

    def meeting(self, g):
        far, inner = (3, 1) if g == 0 else (0, 2)
        return self.copy(far, self.met, far, inner, inner)

    def joined(self, g):
        far = 3 if g == 1 else 0
        return self.copy(far, self.landed.at[g], far, g, far)

    def start(self):
        place = self.place
        self.own.start()
        if self.line:
            for g in range(4):

                @pl.when(place.g == g)
                def _():
                    if g in (0, 3):
                        self.meeting(g).start()
                    for copy in self.direct(g):
                        copy.start()

        else:
            self.copies = [
                self.copy((place.g + dz) % place.grps, self.landed.at[place.g], dz, dz, (place.g + dz) % place.grps)
                for dz in range(1, place.grps)
            ]
            for copy in self.copies:
                copy.start()
        return self

    def join(self):
        if not self.line:
            return
        for g in (1, 2):

            @pl.when(self.place.g == g)
            def _():
                outer, far = (0, 3) if g == 1 else (3, 0)
                self.copy(far, self.met, far, g, outer).wait_recv()
                copy = pltpu.make_async_copy(self.met, self.stage, self.own_sem)
                self.own.wait()
                copy.start()
                copy.wait()
                if len(self.stage.shape) == 2:
                    self.shares[far] = (
                        self.shares[far].astype(f32) + self.stage[...].astype(f32)
                    ).astype(bf16)
                else:
                    for n in range(self.stage.shape[0]):
                        self.shares[far, n] = (
                            self.shares[far, n].astype(f32) + self.stage[n].astype(f32)
                        ).astype(bf16)
                self.joined(g).start()

        for g in (0, 3):

            @pl.when(self.place.g == g)
            def _():
                self.own.wait()

    def finish(self):
        if not self.line:
            self.own.wait()
            for copy in self.copies:
                copy.wait()
            return
        for g in range(4):

            @pl.when(self.place.g == g)
            def _():
                for j in ((1, 2), (0, 2, 3), (0, 1, 3), (1, 2))[g]:
                    self.copy(g, self.landed.at[j], j, j, j).wait_recv()
                for copy in self.direct(g):
                    copy.wait_send()
                if g in (0, 3):
                    self.meeting(g).wait_send()
                else:
                    self.joined(g).wait_send()

    def holds(self, j):
        g = self.place.g
        return (g % 3 != 0) | (j + g != 3) if self.line else True


class Exchange:
    def __init__(self, place, blocks, held, send, recv, own):
        mine = place.rank()
        kept = held.at[mine // QUAD, mine % QUAD] if len(held.shape) == 4 else held.at[mine]

        def block(t):
            return blocks.at[0, t // QUAD, t % QUAD] if len(blocks.shape) == 5 else blocks.at[t]

        self.copies = []
        for n, relation in enumerate(RELATIONS):
            copy = remote(
                block(place.rank(relation)),
                kept,
                send.at[n],
                recv.at[n],
                place.peer(relation),
            )
            copy.start()
            self.copies.append(copy)
        copy = pltpu.make_async_copy(block(mine), kept, own)
        copy.start()
        self.copies.append(copy)

    def finish(self):
        for copy in self.copies:
            copy.wait()


LANES = 512


def lanes_of(n, width=LANES):
    return pl.ds(pl.multiple_of(n * width, width), width)


def shares_of(seq, values, weight, part):
    rows = part.shape[1]

    @pl.loop(0, part.shape[2] // LANES)
    def _(n):
        product = dot(values[seq], weight[lanes_of(n)], 1, 1)
        part[2 * seq, :, lanes_of(n)] = product[:rows].astype(bf16)
        part[2 * seq + 1, :, lanes_of(n)] = product[rows:].astype(bf16)


def over_tokens(first, lanes, second, other):
    total = dot(first[0, :, lanes], second[0, :, other], 0, 0)
    for seq in range(1, first.shape[0]):
        total += dot(first[seq, :, lanes], second[seq, :, other], 0, 0)
    return total


def row_shares(first, second, shares):
    grps, seqs, rows, _ = shares.shape
    width = 256
    pieces = width // rows

    @pl.loop(0, first.shape[2] // width)
    def _(b):
        product = over_tokens(first, lanes_of(b, width), second, slice(None)).astype(bf16)
        for p in range(pieces):
            index = b * pieces + p
            shares[index % grps, index // grps] = product[p * rows : (p + 1) * rows]


def summed_rows(landed, holds, blocks):
    seqs, rows = landed.shape[1], blocks.shape[1]
    for seq in range(seqs):
        for quad in range(QUAD):
            block = slice(quad * rows, (quad + 1) * rows)
            total = jnp.zeros((rows, landed.shape[3]), f32)
            for j in range(landed.shape[0]):
                total += jnp.where(holds(j), landed[j, seq, block].astype(f32), 0.0)
            blocks[seq * QUAD + quad] = total.astype(bf16)


def back_kernel(
    grps,
    aligned,
    facts,
    gains,
    cosine,
    sine,
    residual,
    own_tokens,
    own_grad,
    dgu_h,
    up_h,
    hidden_h,
    grad_h,
    second_h,
    first_h,
    out_h,
    qkv_h,
    q_h,
    k_h,
    v_h,
    o_h,
    input_grad,
    gains_sum,
    down_landed,
    out_landed,
    up_held,
    qkv_held,
    up_landed,
    qkv_landed,
    down_met,
    up_met,
    out_met,
    qkv_met,
    wide,
    up,
    acts,
    second,
    out_w,
    qkv,
    part,
    near,
    far,
    blocks,
    turned,
    down_share,
    up_share,
    out_share,
    qkv_share,
    up_sum,
    qkv_sum,
    stage_low,
    stage_wide,
    gain_part,
    gain_plane,
    gain_far,
    load,
    near_send,
    near_recv,
    far_send,
    far_recv,
    all_send,
    all_recv,
    z_send,
    z_recv,
    swap_send,
    swap_recv,
    gain_send,
    gain_recv,
    own_sem,
):
    place = Place(grps)
    rows = residual.shape[0]
    gain_part[...] = jnp.zeros_like(gain_part)
    count, full_rows, head_width = q_h.shape

    hidden = turned.at[:, :, : hidden_h.shape[2]]

    def fetch(src, dst, n):
        copy = pltpu.make_async_copy(src, dst, load.at[n])
        copy.start()
        return copy

    loads = [fetch(dgu_h, wide, 0), fetch(up_h, up, 1)]
    later = [fetch(hidden_h, hidden, 2), fetch(grad_h, acts, 3), fetch(second_h, second, 4)]
    weights = [fetch(out_h, out_w, 5), fetch(qkv_h, qkv, 6)]
    place.greet()
    for copy in loads:
        copy.wait()

    sums = (near_send, near_recv, far_send, far_recv)
    second_sum = PlaneSum(place, part, near, far, sums)
    for r in range(2):
        shares_of(2 * r + 1 - place.c, wide, up, part)
    second_sum.start_near()
    for r in range(2):
        shares_of(2 * r + place.c, wide, up, part)

    for copy in later[:2]:
        copy.wait()
    units = down_share.shape[1]
    width = min(256, hidden.shape[2])

    @pl.loop(0, hidden.shape[2] // width)
    def _(b):
        for half in range(2):
            lanes = slice(half * D // 2, (half + 1) * D // 2)
            product = over_tokens(hidden, lanes_of(b, width), acts, lanes).astype(bf16)
            for p in range(width // units):
                down_share[b * (width // units) + p, :, lanes] = product[p * units : (p + 1) * units]

    def to_owners(n, shares, landed, met, stage):
        return ToOwners(place, shares, landed, met, stage, z_send.at[n], z_recv.at[n], own_sem.at[n]).start()

    down_out = to_owners(0, down_share, down_landed, down_met, stage_low)
    fetch_first = fetch(first_h, acts, 3)
    second_sum.start_far()
    later[2].wait()
    row_shares(second, wide, up_share)
    up_out = to_owners(1, up_share, up_landed, up_met, stage_wide)
    down_out.join()
    heads = [
        fetch(ref, wide.at[:, :, n * head_width : (n + 1) * head_width], 7 + n)
        for n, ref in enumerate((q_h, k_h, v_h, o_h))
    ]

    second_sum.finish()
    mine = place.seat()
    inner = jnp.zeros((rows, 1), f32)
    squares = jnp.zeros((rows, 1), f32)
    for n in range(D // LANES):
        lanes = slice(n * LANES, (n + 1) * LANES)
        grad = second_sum.chunk(lanes)
        values = residual[:, lanes]
        inner += jnp.sum(grad * gains[1:2, lanes] * values, axis=-1, keepdims=True)
        squares += jnp.sum(values * values, axis=-1, keepdims=True)
    scale = lax.rsqrt(squares / D + NORM_EPSILON)
    inner = inner / D
    for n in range(D // LANES):
        lanes = slice(n * LANES, (n + 1) * LANES)
        grad, values = second_sum.chunk(lanes), residual[:, lanes]
        gain_part[1:2, lanes] = jnp.sum(grad * values * scale, axis=0, keepdims=True)
        total = own_grad[:, lanes].astype(f32) + scale * (
            grad * gains[1:2, lanes] - values * scale * scale * inner
        )
        input_grad[:, lanes] = total
        blocks[mine, :, lanes] = total.astype(bf16)

    gather = PlaneGather(place, blocks, all_send, all_recv)
    gather.start()
    gather.forward()
    up_out.join()
    for copy in weights + heads:
        copy.wait()
    gather.finish()

    lane = lax.broadcasted_iota(jnp.int32, (full_rows, head_width), 1)
    first_half = (lane % HEAD_DIM) < HEAD_DIM // 2

    @pl.loop(0, count)
    def _(seq):
        grads = jnp.concatenate(
            [dot(blocks[2 * seq], out_w[...], 1, 1), dot(blocks[2 * seq + 1], out_w[...], 1, 1)],
            axis=0,
        ).astype(bf16)
        queries = wide[seq, :, 0:head_width]
        key_vectors = wide[seq, :, head_width : 2 * head_width]
        value_vectors = wide[seq, :, 2 * head_width : 3 * head_width]
        grad_q, grad_k, grad_v = attention_grads(
            facts[seq, 2:3, 0:1], queries, key_vectors, value_vectors, grads
        )
        for n, grad in enumerate((grad_q, grad_k)):
            values = (grad * HEAD_DIM**-0.5).astype(bf16).astype(f32)
            back = values * cosine[...] - swap_halves(values, first_half) * sine[...]
            turned[seq, :, n * head_width : (n + 1) * head_width] = back.astype(bf16)
        turned[seq, :, 2 * head_width : 3 * head_width] = grad_v.astype(bf16)

    fetch_first.wait()
    row_shares(acts, turned, qkv_share)
    triple = turned.shape[2]
    qkv_out = to_owners(2, qkv_share, qkv_landed, qkv_met, stage_wide.at[:, :, :triple])

    first_sum = PlaneSum(place, part, near, far, sums)
    for r in range(2):
        shares_of(2 * r + 1 - place.c, turned, qkv, part)
    first_sum.start_near()
    for r in range(2):
        shares_of(2 * r + place.c, turned, qkv, part)
    first_sum.start_far()

    out_rows = out_share.shape[1]

    @pl.loop(0, D // LANES)
    def _(n):
        lanes = lanes_of(n)
        total = jnp.zeros((head_width, LANES), f32)
        for seq in range(count):
            values = wide[seq, :, 3 * head_width : 4 * head_width].astype(f32)
            total += dot(values[:rows].astype(bf16), blocks[2 * seq, :, lanes], 0, 0)
            total += dot(values[rows:].astype(bf16), blocks[2 * seq + 1, :, lanes], 0, 0)
        total = total.astype(bf16)
        for j in range(out_share.shape[0]):
            out_share[j, :, lanes] = total[j * out_rows : (j + 1) * out_rows]

    if aligned:
        out_out = to_owners(3, out_share, out_landed, out_met, stage_low.at[:out_rows])
    else:
        out_out = pltpu.make_async_copy(out_share, out_landed, own_sem.at[3])
        out_out.start()

    qkv_out.join()
    first_sum.finish()
    if aligned:
        out_out.join()
    inner = jnp.zeros((rows, 1), f32)
    squares = jnp.zeros((rows, 1), f32)
    for n in range(D // LANES):
        lanes = slice(n * LANES, (n + 1) * LANES)
        grad = first_sum.chunk(lanes)
        values = own_tokens[:, lanes].astype(f32)
        inner += jnp.sum(grad * gains[0:1, lanes] * values, axis=-1, keepdims=True)
        squares += jnp.sum(values * values, axis=-1, keepdims=True)
    scale = lax.rsqrt(squares / D + NORM_EPSILON)
    inner = inner / D
    for n in range(D // LANES):
        lanes = slice(n * LANES, (n + 1) * LANES)
        grad, values = first_sum.chunk(lanes), own_tokens[:, lanes].astype(f32)
        gain_part[0:1, lanes] = jnp.sum(grad * values * scale, axis=0, keepdims=True)
        input_grad[:, lanes] += scale * (
            grad * gains[0:1, lanes] - values * scale * scale * inner
        )

    gain_copies = []
    for n, relation in enumerate(RELATIONS):
        copy = remote(
            gain_part, gain_plane.at[n], gain_send.at[n], gain_recv.at[n], place.peer(relation)
        )
        copy.start()
        gain_copies.append(copy)

    up_out.finish()
    landed = pltpu.make_async_copy(up_landed, up_share, load.at[1])
    landed.start()
    for copy in gain_copies:
        copy.wait()
    total = gain_part[...]
    for n in range(len(RELATIONS)):
        total += gain_plane[n]
    gain_far[0] = total
    gain_copies = []
    for dz in range(1, grps):
        copy = remote(
            gain_far.at[0],
            gain_far.at[dz],
            gain_send.at[7 + dz],
            gain_recv.at[7 + dz],
            place.plane(dz),
        )
        copy.start()
        gain_copies.append(copy)
    landed.wait()
    summed_rows(up_share, up_out.holds, up_sum)
    up_swap = Exchange(place, up_sum, up_held, swap_send.at[0], swap_recv.at[0], own_sem.at[4])
    for copy in gain_copies:
        copy.wait()
    total = gain_far[0]
    for dz in range(1, grps):
        total += gain_far[dz]
    gains_sum[...] = total

    qkv_out.finish()
    landed = pltpu.make_async_copy(qkv_landed, qkv_share, load.at[6])
    landed.start()
    landed.wait()
    summed_rows(qkv_share, qkv_out.holds, qkv_sum)
    qkv_swap = Exchange(place, qkv_sum, qkv_held, swap_send.at[1], swap_recv.at[1], own_sem.at[5])
    if aligned:
        out_out.finish()
    else:
        out_out.wait()
    down_out.finish()
    up_swap.finish()
    qkv_swap.finish()


def backward(
    grps,
    aligned,
    facts,
    gains,
    tables,
    residual,
    own_tokens,
    own_grad,
    grad_both,
    up_local,
    hidden,
    grad_low,
    second_norm,
    first_norm,
    out_local,
    qkv_local,
    heads,
):
    rows = residual.shape[0]
    count, full_rows, head_width = heads[0].shape
    seqs = full_rows // rows
    ranks = seqs * QUAD
    units = hidden.shape[2] // grps
    both = grad_both.shape[2]
    quad_rows = D // (seqs * grps)
    shard = quad_rows // QUAD
    out_rows = head_width // grps if aligned else HEAD_DIM
    triple = 3 * head_width
    out_count = head_width // out_rows
    hbm = pl.BlockSpec(memory_space=pl.ANY)
    vmem = pl.BlockSpec(memory_space=pltpu.VMEM)
    shape = jax.ShapeDtypeStruct
    dma = pltpu.SemaphoreType.DMA
    return pl.pallas_call(
        lambda *refs: back_kernel(grps, aligned, *refs),
        in_specs=[vmem] * 7 + [hbm] * 12,
        out_specs=[vmem] * 2 + [hbm] * 10,
        out_shape=[
            shape((rows, D), f32),
            shape((8, D), f32),
            shape((grps, units, D), bf16),
            shape((out_count, out_rows, D), bf16),
            shape((ranks, shard, both), bf16),
            shape((ranks, shard, triple), bf16),
            shape((grps, seqs, quad_rows, both), bf16),
            shape((grps, seqs, quad_rows, triple), bf16),
            shape((units, D), bf16),
            shape((seqs, quad_rows, both), bf16),
            shape((out_rows, D), bf16),
            shape((seqs, quad_rows, triple), bf16),
        ],
        scratch_shapes=[
            pltpu.VMEM((count, full_rows, both), bf16),
            pltpu.VMEM((D, both), bf16),
            pltpu.VMEM((count, full_rows, D), bf16),
            pltpu.VMEM((count, full_rows, D), bf16),
            pltpu.VMEM((head_width, D), bf16),
            pltpu.VMEM((D, triple), bf16),
            pltpu.VMEM((ranks, rows, D), bf16),
            pltpu.VMEM((4, rows, D), bf16),
            pltpu.VMEM((3, rows, D), bf16),
            pltpu.VMEM((ranks, rows, D), bf16),
            pltpu.VMEM((count, full_rows, triple), bf16),
            pltpu.VMEM((grps, units, D), bf16),
            pltpu.VMEM((grps, seqs, quad_rows, both), bf16),
            pltpu.VMEM((out_count, out_rows, D), bf16),
            pltpu.VMEM((grps, seqs, quad_rows, triple), bf16),
            pltpu.VMEM((ranks, shard, both), bf16),
            pltpu.VMEM((ranks, shard, triple), bf16),
            pltpu.VMEM((units, D), bf16),
            pltpu.VMEM((seqs, quad_rows, both), bf16),
            pltpu.VMEM((8, D), f32),
            pltpu.VMEM((7, 8, D), f32),
            pltpu.VMEM((grps, 8, D), f32),
            dma((11,)),
            dma((4,)),
            dma((4,)),
            dma((3,)),
            dma((3,)),
            dma((7,)),
            dma((7,)),
            dma((4, grps)),
            dma((4, grps)),
            dma((2, 7)),
            dma((2, 7)),
            dma((7 + grps,)),
            dma((7 + grps,)),
            dma((6,)),
        ],
        compiler_params=pltpu.CompilerParams(
            collective_id=0, has_side_effects=True, vmem_limit_bytes=VMEM_LIMIT
        ),
        cost_estimate=pl.CostEstimate(
            flops=30 * 10**9, bytes_accessed=60 * 2**20, transcendentals=2 * 10**6
        ),
        name="backward",
    )(
        facts,
        gains,
        *tables,
        residual,
        own_tokens,
        own_grad,
        grad_both,
        up_local,
        hidden,
        grad_low,
        second_norm,
        first_norm,
        out_local,
        qkv_local,
        *heads,
    )


CHUNK = 1024


class FromOwners:
    def __init__(self, place, source, landed, landing, send, recv, own):
        self.place, self.source, self.send, self.recv = place, source, send, recv
        self.slot = lambda j: landing(landed, j)
        self.own = pltpu.make_async_copy(source, self.slot(place.g), own)
        self.line = place.grps == 4

    def copy(self, source, slot, sem, recv, target):
        place = self.place
        return remote(
            source, self.slot(slot), self.send.at[sem], self.recv.at[recv], (place.s, target, place.r, place.c)
        )

    def direct(self, g):
        targets = ((1, 2, 3), (0, 2), (3, 1), (2, 1, 0))[g]
        return [self.copy(self.source, g, t, g, t) for t in targets]

    def passed_on(self, g):
        inner, end = 3 - g, 0 if g == 1 else 3
        return self.copy(self.slot(inner), inner, 3 - end, inner, end)

    def arrival(self, j):
        return self.copy(self.source, j, j, j, j)

    def start(self):
        place = self.place
        self.own.start()
        if self.line:
            for g in range(4):

                @pl.when(place.g == g)
                def _():
                    for copy in self.direct(g):
                        copy.start()

        else:
            self.copies = [
                self.copy(self.source, place.g, dz, dz, (place.g + dz) % place.grps)
                for dz in range(1, place.grps)
            ]
            for copy in self.copies:
                copy.start()

    def relay(self):
        if self.line:
            for g in (1, 2):

                @pl.when(self.place.g == g)
                def _():
                    self.arrival(3 - g).wait_recv()
                    self.passed_on(g).start()

    def finish(self):
        self.own.wait()
        if self.line:
            for g in range(4):

                @pl.when(self.place.g == g)
                def _():
                    for j in range(4):
                        if j != g and not (g in (1, 2) and j == 3 - g):
                            self.arrival(j).wait_recv()
                    for copy in self.direct(g):
                        copy.wait_send()
                    if g in (1, 2):
                        self.passed_on(g).wait_send()

        else:
            for copy in self.copies:
                copy.wait()


def shares_from(seq, values, weight, part):
    rows = part.shape[1]

    @pl.loop(0, part.shape[2] // LANES)
    def _(n):
        product = dot(values[seq], weight[:, lanes_of(n)])
        part[2 * seq, :, lanes_of(n)] = product[:rows].astype(bf16)
        part[2 * seq + 1, :, lanes_of(n)] = product[rows:].astype(bf16)


def times_slices(values, weight, lanes):
    seqs, grps, quad, shard, _ = weight.shape
    depth = quad * shard
    total = None
    for n in range(seqs * grps):
        piece = weight[n // grps, n % grps, :, :, lanes]
        term = dot(values[:, n * depth : (n + 1) * depth], piece.reshape(depth, piece.shape[2]))
        total = term if total is None else total + term
    return total


def both_blocks(blocks, seq):
    return jnp.concatenate([blocks[2 * seq].astype(f32), blocks[2 * seq + 1].astype(f32)], axis=0)


def forward_kernel(
    grps,
    aligned,
    cosine,
    sine,
    own_facts,
    tokens_h,
    own_grad_h,
    qkv_own,
    up_own,
    out_own,
    down_own,
    residual,
    gains,
    facts,
    first_h,
    q_h,
    k_h,
    v_h,
    o_h,
    second_h,
    grad_h,
    hidden_h,
    dgu_h,
    qkv_landed,
    up_landed,
    out_landed,
    down_landed,
    blocks,
    grad_blocks,
    norm,
    grad_seq,
    qkv_rank,
    up_rank,
    qkv,
    up,
    out_w,
    down,
    heads,
    part,
    near,
    far,
    both,
    hidden,
    dgu,
    all_facts,
    early,
    load,
    store,
    swap_send,
    swap_recv,
    near_send,
    near_recv,
    far_send,
    far_recv,
    all_send,
    all_recv,
    z_send,
    z_recv,
    fact_send,
    fact_recv,
    own_sem,
):
    place = Place(grps)
    count, full_rows, _ = norm.shape
    rows = residual.shape[0]
    head_width = heads.shape[3]
    mine, rank = place.seat(), place.rank()

    def fetch(src, dst, n):
        copy = pltpu.make_async_copy(src, dst, load.at[n])
        copy.start()
        return copy

    def keep(src, dst, n):
        copy = pltpu.make_async_copy(src, dst, store.at[n])
        copy.start()
        return copy

    shard = qkv_own.shape[0]
    units = down.shape[0] // grps
    seqs = qkv_landed.shape[0]
    slots = iter(range(20))

    def fetch_chunks(src):
        pieces = []
        for top in range(0, src.shape[0], shard):
            for left in range(0, src.shape[1], CHUNK):
                slot = next(slots)
                space = both.at[slot // 5, (slot % 5) * shard : (slot % 5 + 1) * shard]
                copy = pltpu.make_async_copy(
                    src.at[top : top + shard, left : left + CHUNK], space, early.at[slot]
                )
                copy.start()
                pieces.append((copy, space))
        return pieces

    def dealt(pieces, weight, lanes, parts):
        count = CHUNK // (QUAD * lanes)
        width = count * lanes
        each = len(pieces) // (parts * seqs)
        for n, (copy, space) in enumerate(pieces):
            copy.wait()
            values = space[...]
            seq = n // each % seqs
            first = (n // (each * seqs) * each + n % each) * width
            for q in range(QUAD):
                taken = [
                    values[:, (k * QUAD + q) * lanes : (k * QUAD + q + 1) * lanes] for k in range(count)
                ]
                weight[0, seq, q, :, first : first + width] = jnp.concatenate(taken, axis=1).astype(bf16)

    facts[rank] = own_facts[...]
    qkv_pieces = fetch_chunks(qkv_own)
    if aligned:
        out_pieces = fetch_chunks(out_own)
    up_pieces = fetch_chunks(up_own)
    down_pieces = fetch_chunks(down_own)
    own_blocks = [fetch(tokens_h, blocks.at[mine], 0), fetch(own_grad_h, grad_blocks.at[mine], 1)]

    def plane_rows(ref, j):
        return ref.at[:, j]

    def own_rows(ref, j):
        size = ref.shape[0] // grps
        return ref.at[pl.ds(pl.multiple_of(j * size, size), size)]

    def from_owners(n, source, landed, landing):
        return FromOwners(place, source, landed, landing, z_send.at[n], z_recv.at[n], own_sem.at[n])

    def stacked(pieces, weight):
        across = weight.shape[1] // CHUNK
        for n, (copy, space) in enumerate(pieces):
            copy.wait()
            top, left = n // across * shard, n % across * CHUNK
            weight[top : top + shard, left : left + CHUNK] = space[...].astype(bf16)

    down_z = from_owners(3, down.at[:units], down_landed, own_rows)
    dealt(qkv_pieces, qkv, HEAD_DIM, 3)
    place.greet()
    if aligned:
        stacked(out_pieces, out_w)
        out_z = from_owners(2, out_w.at[:shard], out_landed, own_rows)
        out_z.start()
    qkv_swap = Exchange(place, qkv, qkv_rank, swap_send.at[0], swap_recv.at[0], own_sem.at[4])
    fact_copies = []
    for n, relation in enumerate(RELATIONS):
        copy = remote(own_facts, facts.at[rank], fact_send.at[n], fact_recv.at[n], place.peer(relation))
        copy.start()
        fact_copies.append(copy)
    dealt(up_pieces, up, units, 2)
    stacked(down_pieces, down)
    for copy in own_blocks:
        copy.wait()
    qkv_swap.finish()
    qkv_z = from_owners(0, qkv_rank, qkv_landed, plane_rows)
    up_z = from_owners(1, up_rank, up_landed, plane_rows)
    qkv_z.start()
    token_gather = PlaneGather(place, blocks, all_send.at[0], all_recv.at[0])
    token_gather.start()
    for copy in fact_copies:
        copy.wait()
    all_facts[place.g] = facts[...]
    fact_copies = []
    for dz in range(1, grps):
        copy = remote(
            facts,
            all_facts.at[place.g],
            fact_send.at[7 + dz],
            fact_recv.at[7 + dz],
            place.plane(dz),
        )
        copy.start()
        fact_copies.append(copy)
    if aligned:
        out_z.relay()
    for copy in fact_copies:
        copy.wait()
    width = D // (seqs * grps * QUAD)
    for n in range(seqs * grps):
        pieces = [all_facts[n % grps, (n // grps) * QUAD + q, :, :width] for q in range(QUAD)]
        gains[:, n * QUAD * width : (n + 1) * QUAD * width] = jnp.concatenate(pieces, axis=1)
    token_gather.forward()
    up_swap = Exchange(place, up, up_rank, swap_send.at[1], swap_recv.at[1], own_sem.at[5])
    qkv_z.relay()
    token_gather.finish()

    @pl.loop(0, count)
    def _(seq):
        values = both_blocks(blocks, seq)
        scale = lax.rsqrt(jnp.mean(values * values, axis=-1, keepdims=True) + NORM_EPSILON)
        norm[seq] = (values * scale * gains[0:1, :]).astype(bf16)

    stores = [keep(norm, first_h, 0)]
    grad_gather = PlaneGather(place, grad_blocks, all_send.at[1], all_recv.at[1])
    grad_gather.start()
    up_swap.finish()
    qkv_z.finish()
    up_z.start()
    fetch(qkv_landed, qkv, 2).wait()

    lane = lax.broadcasted_iota(jnp.int32, (full_rows, head_width), 1)
    first_half = (lane % HEAD_DIM) < HEAD_DIM // 2

    @pl.loop(0, count)
    def _(seq):
        for n in range(3):
            lanes = slice(n * head_width, (n + 1) * head_width)
            values = times_slices(norm[seq], qkv, lanes)
            if n < 2:
                values = values * cosine[...] + swap_halves(values, first_half) * sine[...]
            heads[n, seq] = values.astype(bf16)
        heads[3, seq] = attention(facts[seq, 2:3, 0:1], heads[0, seq], heads[1, seq], heads[2, seq])

    grad_gather.forward()
    stores += [keep(heads.at[n], ref, 1 + n) for n, ref in enumerate((q_h, k_h, v_h, o_h))]
    if aligned:
        out_z.finish()
        fetch(out_landed, out_w, 3).wait()
    else:
        fetch(out_own, out_w, 3).wait()

    plane_sum = PlaneSum(place, part, near, far, (near_send, near_recv, far_send, far_recv))
    mixed = heads.at[3]
    for r in range(2):
        shares_from(2 * r + 1 - place.c, mixed, out_w, part)
    plane_sum.start_near()
    for r in range(2):
        shares_from(2 * r + place.c, mixed, out_w, part)
    up_z.relay()
    plane_sum.start_far()
    grad_gather.finish()

    @pl.loop(0, count)
    def _(seq):
        grad_seq[seq] = both_blocks(grad_blocks, seq).astype(bf16)

    stores.append(keep(grad_seq, grad_h, 6))
    fetch(tokens_h, grad_blocks.at[mine], 4).wait()
    plane_sum.finish()
    squares = jnp.zeros((rows, 1), f32)
    for n in range(D // LANES):
        lanes = slice(n * LANES, (n + 1) * LANES)
        values = grad_blocks[mine, :, lanes].astype(f32) + plane_sum.chunk(lanes)
        residual[:, lanes] = values
        squares += jnp.sum(values * values, axis=-1, keepdims=True)
    scale = lax.rsqrt(squares / D + NORM_EPSILON)
    for n in range(D // LANES):
        lanes = slice(n * LANES, (n + 1) * LANES)
        blocks[mine, :, lanes] = (residual[:, lanes] * scale * gains[1:2, lanes]).astype(bf16)
    norm_gather = PlaneGather(place, blocks, all_send.at[2], all_recv.at[2])
    norm_gather.start()
    down_z.start()
    norm_gather.forward()
    stores[0].wait()
    norm_gather.finish()

    @pl.loop(0, count)
    def _(seq):
        norm[seq] = both_blocks(blocks, seq).astype(bf16)

    stores[0] = keep(norm, second_h, 5)
    up_z.finish()
    down_z.relay()
    fetch(up_landed, up, 5).wait()
    half = hidden.shape[2]

    @pl.loop(0, count)
    def _(seq):
        gate = times_slices(norm[seq], up, slice(0, half))
        above = times_slices(norm[seq], up, slice(half, 2 * half))
        both[seq, :, :half] = gate
        both[seq, :, half:] = above
        hidden[seq] = (gate * jax.nn.sigmoid(gate) * above).astype(bf16)

    stores.append(keep(hidden, hidden_h, 7))
    down_z.finish()
    fetch(down_landed, down, 6).wait()

    @pl.loop(0, count)
    def _(seq):
        grads = dot(grad_seq[seq], down[...], 1, 1)
        gate, above = both[seq, :, :half], both[seq, :, half:]
        sigmoid = jax.nn.sigmoid(gate)
        dgu[seq, :, :half] = (grads * above * sigmoid * (1.0 + gate * (1.0 - sigmoid))).astype(bf16)
        dgu[seq, :, half:] = (grads * (gate * sigmoid)).astype(bf16)

    stores.append(keep(dgu, dgu_h, 8))
    for copy in stores:
        copy.wait()


def forward(grps, aligned, tables, own_facts, tokens, own_grad, qkv_own, up_own, out_own, down_own):
    rows = tokens.shape[0]
    shard = qkv_own.shape[0]
    seqs = D // (shard * grps * QUAD)
    ranks = seqs * QUAD
    triple, both = qkv_own.shape[1] // ranks, up_own.shape[1] // ranks
    count, full_rows, head_width = QUAD, rows * seqs, triple // 3
    half = both // 2
    hbm = pl.BlockSpec(memory_space=pl.ANY)
    vmem = pl.BlockSpec(memory_space=pltpu.VMEM)
    shape = jax.ShapeDtypeStruct
    dma = pltpu.SemaphoreType.DMA
    by_heads = shape((count, full_rows, head_width), bf16)
    return pl.pallas_call(
        lambda *refs: forward_kernel(grps, aligned, *refs),
        in_specs=[vmem] * 3 + [hbm] * 6,
        out_specs=[vmem] * 3 + [hbm] * 13,
        out_shape=[
            shape((rows, D), f32),
            shape((8, D), f32),
            shape((ranks, 8, 128), f32),
            shape((count, full_rows, D), bf16),
            by_heads,
            by_heads,
            by_heads,
            by_heads,
            shape((count, full_rows, D), bf16),
            shape((count, full_rows, D), bf16),
            shape((count, full_rows, half), bf16),
            shape((count, full_rows, both), bf16),
            shape((seqs, grps, QUAD, shard, triple), bf16),
            shape((seqs, grps, QUAD, shard, both), bf16),
            shape((head_width, D), bf16),
            shape((half, D), bf16),
        ],
        scratch_shapes=[
            pltpu.VMEM((ranks, rows, D), bf16),
            pltpu.VMEM((ranks, rows, D), bf16),
            pltpu.VMEM((count, full_rows, D), bf16),
            pltpu.VMEM((count, full_rows, D), bf16),
            pltpu.VMEM((seqs, QUAD, shard, triple), bf16),
            pltpu.VMEM((seqs, QUAD, shard, both), bf16),
            pltpu.VMEM((seqs, grps, QUAD, shard, triple), bf16),
            pltpu.VMEM((seqs, grps, QUAD, shard, both), bf16),
            pltpu.VMEM((head_width, D), bf16),
            pltpu.VMEM((half, D), bf16),
            pltpu.VMEM((4, count, full_rows, head_width), bf16),
            pltpu.VMEM((ranks, rows, D), bf16),
            pltpu.VMEM((4, rows, D), bf16),
            pltpu.VMEM((3, rows, D), bf16),
            pltpu.VMEM((count, full_rows, both), f32),
            pltpu.VMEM((count, full_rows, half), bf16),
            pltpu.VMEM((count, full_rows, both), bf16),
            pltpu.VMEM((grps, ranks, 8, 128), f32),
            dma((20,)),
            dma((7,)),
            dma((9,)),
            dma((2, 7)),
            dma((2, 7)),
            dma((4,)),
            dma((4,)),
            dma((3,)),
            dma((3,)),
            dma((3, 7)),
            dma((3, 7)),
            dma((4, grps)),
            dma((4, grps)),
            dma((7 + grps,)),
            dma((7 + grps,)),
            dma((6,)),
        ],
        compiler_params=pltpu.CompilerParams(
            collective_id=1, has_side_effects=True, vmem_limit_bytes=VMEM_LIMIT
        ),
        cost_estimate=pl.CostEstimate(
            flops=20 * 10**9, bytes_accessed=60 * 2**20, transcendentals=4 * 10**6
        ),
        name="forward",
    )(*tables, own_facts, tokens, own_grad, qkv_own, up_own, out_own, down_own)


ADAM_WIDTH = 1024


def adam_step(gradient, weight, moment, square, step_rate, outs):
    results = adam_update(weight[...], moment[...], square[...], gradient, step_rate)
    for out, result in zip(outs, results):
        out[...] = result
    outs[3][...] = results[0].astype(bf16)


def adam_ranks_kernel(lanes, step_rate, held, weight, moment, square, *outs):
    values = [held[0, q].astype(f32) for q in range(QUAD)]
    gradient = jnp.concatenate(
        [
            values[q][:, n * lanes : (n + 1) * lanes]
            for n in range(held.shape[3] // lanes)
            for q in range(QUAD)
        ],
        axis=1,
    )
    adam_step(gradient, weight, moment, square, step_rate, outs)


def adam_planes_kernel(step_rate, holds, landed, weight, moment, square, *outs):
    total = jnp.zeros(weight.shape, f32)
    for j in range(landed.shape[0]):
        total += jnp.where(holds[j] > 0, landed[j].astype(f32), 0.0)
    adam_step(total, weight, moment, square, step_rate, outs)


def adam_call(kernel, grads, grad_specs, state):
    rows, columns = state[0].shape
    block = pl.BlockSpec((rows, ADAM_WIDTH), lambda n: (0, n))
    like = jax.ShapeDtypeStruct((rows, columns), f32)
    return pl.pallas_call(
        kernel,
        grid=(columns // ADAM_WIDTH,),
        in_specs=grad_specs + [block] * 3,
        out_specs=[block] * 4,
        out_shape=[like] * 3 + [jax.ShapeDtypeStruct((rows, columns), bf16)],
        compiler_params=pltpu.CompilerParams(vmem_limit_bytes=32 * 2**20),
        cost_estimate=pl.CostEstimate(
            flops=rows * columns * 16, bytes_accessed=rows * columns * 28, transcendentals=rows * columns
        ),
        name="adam",
    )(*grads, *state)


def adam_from_ranks(held, seqs, parts, lanes, step_rate, *state):
    ranks, rows, columns = held.shape
    width = ADAM_WIDTH // QUAD
    blocks = columns // (parts * width)
    grouped = held.reshape(seqs, QUAD, rows, columns)
    spec = pl.BlockSpec(
        (1, QUAD, rows, width),
        lambda n: ((n // blocks) % seqs, 0, 0, n // (blocks * seqs) * blocks + n % blocks),
    )
    return adam_call(
        lambda *refs: adam_ranks_kernel(lanes, step_rate, *refs), (grouped,), [spec], state
    )


def adam_from_planes(landed, holds, step_rate, *state):
    planes, rows, _ = landed.shape
    specs = [
        pl.BlockSpec(memory_space=pltpu.SMEM),
        pl.BlockSpec((planes, rows, ADAM_WIDTH), lambda n: (0, 0, n)),
    ]
    return adam_call(
        lambda *refs: adam_planes_kernel(step_rate, *refs), (holds, landed), specs, state
    )


def seat_sum(partial):
    return lax.psum_scatter(
        partial.astype(bf16), SEATS, scatter_dimension=0, tiled=True
    ).astype(f32)


def on_device(
    tokens,
    cotangent,
    lengths,
    qkv_weight,
    qkv_moment,
    qkv_square,
    out_weight,
    out_moment,
    out_square,
    up_weight,
    up_moment,
    up_square,
    down_weight,
    down_moment,
    down_square,
    norm_gains,
    gains_moment,
    gains_square,
):
    seqs = lax.axis_size("seq")
    grps = lax.axis_size("grp")
    ranks = seqs * QUAD
    own_rows = tokens.shape[1]
    full_rows = own_rows * seqs
    all_rows = full_rows * QUAD
    heads_local = HEADS // ranks
    head_width = heads_local * HEAD_DIM
    units = down_weight.shape[0]
    aligned = out_weight.shape[0] == HEAD_DIM
    tables = rotate_table(full_rows, heads_local)

    positions = lax.axis_index("seq") * own_rows + jnp.arange(own_rows, dtype=jnp.int32)
    own_grad = jnp.where((positions < lengths[0])[:, None], cotangent[0], 0)
    own_gains = norm_gains.shape[1]
    own_facts = jnp.zeros((8, 128), f32)
    own_facts = own_facts.at[:2, :own_gains].set(norm_gains.astype(bf16).astype(f32))
    own_facts = own_facts.at[2].set(lengths[0].astype(f32))

    out_own = out_weight
    if not aligned:
        out_all = lax.all_gather(out_weight.astype(bf16), EVERY, axis=0, tiled=True)
        out_all = out_all.reshape(seqs, heads_local, QUAD, HEAD_DIM, D)
        seat = lax.axis_index("row") * 2 + lax.axis_index("core")
        out_own = lax.dynamic_index_in_dim(
            lax.dynamic_index_in_dim(out_all, lax.axis_index("seq"), 0, False), seat, 1, False
        ).reshape(head_width, D)
    (
        residual,
        gains,
        facts,
        first_norm,
        queries,
        key_vectors,
        value_vectors,
        attended,
        second_norm,
        grad_low,
        hidden,
        grad_both,
        qkv_local,
        up_local,
        out_local,
        down_local,
    ) = forward(
        grps,
        aligned,
        tables,
        own_facts,
        tokens[0],
        own_grad,
        qkv_weight,
        up_weight,
        out_own,
        down_weight,
    )
    if not aligned:
        out_local = out_own
    (
        input_grad,
        gains_total,
        down_planes,
        out_planes,
        up_ranks,
        qkv_ranks,
        *_,
    ) = backward(
        grps,
        aligned,
        facts,
        gains,
        tables,
        residual,
        tokens[0],
        own_grad,
        grad_both,
        up_local.reshape(D, -1),
        hidden,
        grad_low,
        second_norm,
        first_norm,
        out_local,
        qkv_local.reshape(D, -1),
        (queries, key_vectors, value_vectors, attended),
    )
    block_output = (
        residual + seat_sum(dot(hidden.reshape(all_rows, -1), down_local))
    ).astype(bf16)
    if aligned:
        out_sum = out_planes
    else:
        placed_term = jnp.zeros((seqs, QUAD, heads_local, HEAD_DIM, D), bf16)
        placed_term = lax.dynamic_update_slice(
            placed_term,
            out_planes.reshape(1, 1, heads_local, HEAD_DIM, D),
            (lax.axis_index("seq"), seat, 0, 0, 0),
        )
        out_sum = lax.psum_scatter(
            placed_term.transpose(0, 2, 1, 3, 4).reshape(D, D),
            EVERY,
            scatter_dimension=0,
            tiled=True,
        )[None]
    device = ((lax.axis_index("seq") * grps + lax.axis_index("grp")) * 2 + lax.axis_index("row")) * 2
    gains_sum = lax.dynamic_slice(
        gains_total, (0, (device + lax.axis_index("core")) * own_gains), (2, own_gains)
    )
    planes = jnp.arange(grps)
    plane = lax.axis_index("grp")
    holds = ((planes + plane != 3) | (plane % 3 != 0) | (grps != 4)).astype(jnp.int32)
    qkv_new = adam_from_ranks(
        qkv_ranks, seqs, 3, HEAD_DIM, D ** (-0.5), qkv_weight, qkv_moment, qkv_square
    )
    up_new = adam_from_ranks(
        up_ranks, seqs, 2, units, D ** (-0.5), up_weight, up_moment, up_square
    )
    out_new = adam_from_planes(
        out_sum, holds, (D // 128) ** (-0.5), out_weight, out_moment, out_square
    )
    down_new = adam_from_planes(
        down_planes, holds, FF ** (-0.5), down_weight, down_moment, down_square
    )
    gains_new = adam_update(norm_gains, gains_moment, gains_square, gains_sum, 0.3)
    return (
        block_output[None],
        input_grad[None],
        *qkv_new,
        *out_new,
        *up_new,
        *down_new,
        *gains_new,
    )


def solution(mesh):
    seqs, rest = mesh.shape["seq"], mesh.shape["fsdp"]
    planes = Mesh(
        mesh.devices.reshape(seqs, rest // QUAD, 2, 2), ("seq", "grp", "row", "core")
    )
    rows = P(("grp", "row", "core"), "seq", None)
    shards = P(EVERY, None)
    gains = P(None, EVERY)
    return jax.shard_map(
        on_device,
        mesh=planes,
        in_specs=(rows, rows, P(("grp", "row", "core"))) + (shards,) * 12 + (gains,) * 3,
        out_specs=(rows, rows) + (shards,) * 16 + (gains,) * 3,
        check_vma=False,
    )
```

```python
import math

import jax
import jax.numpy as jnp
from jax import lax
from jax.experimental import pallas as pl
from jax.experimental.pallas import tpu as pltpu
from jax.sharding import Mesh, PartitionSpec as P

D = 2048
HEADS = 32
HEAD_DIM = 64
FF = 4096
WINDOW = 128
STEP = 5


NORM_EPSILON = 1e-05
MOMENT_DECAY = 0.5
WEIGHT_DECAY = 0.1
ADAM_EPSILON = 1e-08

SEATS = ("row", "core", "seq")
RANKS = ("seq", "row", "core")
EVERY = ("seq", "grp", "row", "core")
QUAD = 4
VMEM_LIMIT = 63 * 2**20

bf16 = jnp.bfloat16
f32 = jnp.float32


def rotate_table(length, copies):
    halves = HEAD_DIM // 2
    freqs = jnp.exp(-math.log(10000.0) * 2.0 * jnp.arange(halves).astype(f32) / HEAD_DIM)
    angles = jnp.arange(length, dtype=jnp.int32).astype(f32)[:, None] * freqs[None, :]
    cosine, sine = jnp.cos(angles), jnp.sin(angles)
    return (
        jnp.tile(jnp.concatenate([cosine, cosine], axis=1), (1, copies)),
        jnp.tile(jnp.concatenate([-sine, sine], axis=1), (1, copies)),
    )


def adam_update(weight, moment, square, gradient, step_rate):
    moment_new = MOMENT_DECAY * moment + (1.0 - MOMENT_DECAY) * gradient
    square_new = MOMENT_DECAY * square + (1.0 - MOMENT_DECAY) * gradient * gradient
    correction = 1.0 - MOMENT_DECAY**STEP
    update = moment_new / correction / (jnp.sqrt(square_new / correction) + ADAM_EPSILON)
    return (weight - step_rate * (update + WEIGHT_DECAY * weight), moment_new, square_new)


def dot(a, b, lhs=1, rhs=0):
    return lax.dot_general(a, b, (((lhs,), (rhs,)), ((), ())), preferred_element_type=f32)


def swap_halves(values, first):
    width = values.shape[1]
    half = HEAD_DIM // 2
    return jnp.where(
        first, pltpu.roll(values, width - half, 1), pltpu.roll(values, half, 1)
    )


def allowed_mask(rows, length):
    row = lax.broadcasted_iota(jnp.int32, (rows, rows), 0)
    col = lax.broadcasted_iota(jnp.int32, (rows, rows), 1)
    return (col <= row) & (row - col < WINDOW) & (col.astype(f32) < length)


def head_lanes(rows, width, head):
    lane = lax.broadcasted_iota(jnp.int32, (rows, width), 1)
    return (lane // HEAD_DIM) == head


def softmax_rows(queries, key_vectors, allowed):
    scores = jnp.where(allowed, dot(queries, key_vectors, 1, 1) * (HEAD_DIM**-0.5), -1e30)
    shifted = jnp.exp(scores - jnp.max(scores, axis=-1, keepdims=True))
    return shifted / jnp.sum(shifted, axis=-1, keepdims=True)


def attention(length, queries, key_vectors, value_vectors):
    rows, width = queries.shape
    allowed = allowed_mask(rows, length)
    total = jnp.zeros((rows, width), f32)
    for head in range(width // HEAD_DIM):
        mine = head_lanes(rows, width, head)
        weights = softmax_rows(jnp.where(mine, queries, 0), key_vectors, allowed)
        total += dot(weights.astype(bf16), jnp.where(mine, value_vectors, 0))
    return total.astype(bf16)


def attention_grads(length, queries, key_vectors, value_vectors, grads):
    rows, width = queries.shape
    allowed = allowed_mask(rows, length)
    grad_q = jnp.zeros((rows, width), f32)
    grad_k = jnp.zeros((rows, width), f32)
    grad_v = jnp.zeros((rows, width), f32)
    for head in range(width // HEAD_DIM):
        mine = head_lanes(rows, width, head)
        q_head = jnp.where(mine, queries, 0)
        g_head = jnp.where(mine, grads, 0)
        weights = softmax_rows(q_head, key_vectors, allowed)
        grad_p = dot(g_head, value_vectors, 1, 1)
        delta = jnp.sum(weights * grad_p, axis=-1, keepdims=True)
        grad_s = jnp.where(allowed, weights * (grad_p - delta), 0.0).astype(bf16)
        grad_q += dot(grad_s, jnp.where(mine, key_vectors, 0))
        grad_k += dot(grad_s, q_head, 0, 0)
        grad_v += dot(weights.astype(bf16), g_head, 0, 0)
    return grad_q, grad_k, grad_v


MESH = pl.DeviceIdType.MESH
RELATIONS = tuple((a, b, d) for a in range(2) for b in range(2) for d in range(2))[1:]


class Place:
    def __init__(self, grps):
        self.grps = grps
        self.s = lax.axis_index("seq")
        self.g = lax.axis_index("grp")
        self.r = lax.axis_index("row")
        self.c = lax.axis_index("core")

    def peer(self, relation):
        ds, dr, dc = relation
        return ((self.s + ds) % 2, self.g, (self.r + dr) % 2, (self.c + dc) % 2)

    def plane(self, dz):
        return (self.s, (self.g + dz) % self.grps, self.r, self.c)

    def rank(self, relation=(0, 0, 0)):
        s, _, r, c = self.peer(relation)
        return (s * 2 + r) * 2 + c

    def seat(self, relation=(0, 0, 0)):
        s, _, r, c = self.peer(relation)
        return (r * 2 + c) * 2 + s

    def corner(self, relation=(0, 0, 0)):
        s, _, r, _ = self.peer(relation)
        return r * 2 + s

    def greet(self):
        barrier = pltpu.get_barrier_semaphore()
        for relation in RELATIONS:
            pl.semaphore_signal(barrier, inc=1, device_id=self.peer(relation), device_id_type=MESH)
        for dz in range(1, self.grps):
            pl.semaphore_signal(barrier, inc=1, device_id=self.plane(dz), device_id_type=MESH)
        pl.semaphore_wait(barrier, len(RELATIONS) + self.grps - 1)


SIBLING = (0, 0, 1)
ACROSS = ((1, 0, 0), (0, 1, 0), (1, 1, 0))


def remote(src, dst, send_sem, recv_sem, device):
    return pltpu.make_async_remote_copy(
        src_ref=src,
        dst_ref=dst,
        send_sem=send_sem,
        recv_sem=recv_sem,
        device_id=device,
        device_id_type=MESH,
    )


class PlaneSum:
    def __init__(self, place, part, near, far, sems):
        self.place, self.part, self.nears, self.fars = place, part, near, far
        self.near_send, self.near_recv, self.far_send, self.far_recv = sems
        self.first, self.second = [None] * 4, []

    def sequence(self, k):
        place = self.place
        row = (place.r + 1) % 2 if k < 2 else place.r
        return row * 2 + ((place.c + 1) % 2 if k % 2 == 0 else place.c)

    def near(self, k):
        for s in range(2):
            copy = remote(
                self.part.at[2 * self.sequence(k) + s],
                self.nears.at[k + s],
                self.near_send.at[k + s],
                self.near_recv.at[k + s],
                self.place.peer(SIBLING),
            )
            copy.start()
            self.first[k + s] = copy

    def far(self, k):
        place = self.place
        for s in range(2):
            self.first[k - 1 + s].wait()
            self.nears[k - 1 + s] = (
                self.part[2 * self.sequence(k) + s].astype(f32)
                + self.nears[k - 1 + s].astype(f32)
            ).astype(bf16)
        for d in (1, 2) if k == 1 else (0,):
            relation = ACROSS[d]
            copy = remote(
                self.nears.at[k - 1 + (place.s + relation[0]) % 2],
                self.fars.at[d],
                self.far_send.at[d],
                self.far_recv.at[d],
                place.peer(relation),
            )
            copy.start()
            self.second.append(copy)

    def finish(self):
        for copy in self.second:
            copy.wait()

    def chunk(self, lanes):
        total = self.nears[2 + self.place.s, :, lanes].astype(f32)
        for d in range(3):
            total += self.fars[d, :, lanes].astype(f32)
        return total


class PlaneGather:
    def __init__(self, place, blocks, send, recv):
        self.place, self.blocks, self.sends, self.recvs = place, blocks, send, recv
        self.copies = [None] * 7

    def send(self, block, sem, relation):
        copy = remote(
            self.blocks.at[block],
            self.blocks.at[block],
            self.sends.at[sem],
            self.recvs.at[sem],
            self.place.peer(relation),
        )
        copy.start()
        self.copies[sem] = copy

    def start(self):
        mine = self.place.seat()
        for d in range(2):
            self.send(mine, d, ACROSS[d])
        self.send(mine, 3, SIBLING)

    def forward(self, d):
        self.copies[d].wait_recv()
        self.send(self.place.seat(ACROSS[d]), 4 + d, SIBLING)
        if d == 0:
            self.send(self.place.seat(), 2, ACROSS[2])

    def sequence(self, k):
        place = self.place
        row = place.r if k < 2 else (place.r + 1) % 2
        return row * 2 + (place.c if k % 2 == 0 else (place.c + 1) % 2)

    def arrive(self, k):
        if k == 0:
            self.forward(0)
        elif k == 1:
            self.forward(1)
            self.copies[3].wait_recv()
            self.copies[4].wait_recv()
        elif k == 2:
            self.forward(2)
        else:
            self.copies[5].wait_recv()
            self.copies[6].wait_recv()

    def finish(self):
        for copy in self.copies:
            copy.wait_send()


class ToOwners:
    def __init__(self, place, shares, landed, met, stage, send, recv, own):
        self.place, self.shares, self.landed, self.met, self.stage = place, shares, landed, met, stage
        self.send, self.recv, self.own_sem = send, recv, own
        self.line = place.grps == 4
        self.own = pltpu.make_async_copy(shares.at[place.g], landed.at[place.g], own)

    def copy(self, block, landing, sem, recv, target):
        place = self.place
        return remote(
            self.shares.at[block],
            landing,
            self.send.at[sem],
            self.recv.at[recv],
            (place.s, target, place.r, place.c),
        )

    def direct(self, g):
        targets = ((2, 1), (2, 0), (1, 3), (1, 2))[g]
        return [self.copy(t, self.landed.at[g], t, g, t) for t in targets]

    def meeting(self, g):
        far, inner = (3, 1) if g == 0 else (0, 2)
        return self.copy(far, self.met, far, inner, inner)

    def joined(self, g):
        far = 3 if g == 1 else 0
        return self.copy(far, self.landed.at[g], far, g, far)

    def start(self):
        place = self.place
        self.own.start()
        if self.line:
            for g in range(4):

                @pl.when(place.g == g)
                def _():
                    if g in (0, 3):
                        self.meeting(g).start()
                    for copy in self.direct(g):
                        copy.start()

        else:
            self.copies = [
                self.copy((place.g + dz) % place.grps, self.landed.at[place.g], dz, dz, (place.g + dz) % place.grps)
                for dz in range(1, place.grps)
            ]
            for copy in self.copies:
                copy.start()
        return self

    def join(self):
        if not self.line:
            return
        for g in (1, 2):

            @pl.when(self.place.g == g)
            def _():
                outer, far = (0, 3) if g == 1 else (3, 0)
                self.copy(far, self.met, far, g, outer).wait_recv()
                copy = pltpu.make_async_copy(self.met, self.stage, self.own_sem)
                self.own.wait()
                copy.start()
                copy.wait()
                if len(self.stage.shape) == 2:
                    self.shares[far] = (
                        self.shares[far].astype(f32) + self.stage[...].astype(f32)
                    ).astype(bf16)
                else:
                    for n in range(self.stage.shape[0]):
                        self.shares[far, n] = (
                            self.shares[far, n].astype(f32) + self.stage[n].astype(f32)
                        ).astype(bf16)
                self.joined(g).start()

        for g in (0, 3):

            @pl.when(self.place.g == g)
            def _():
                self.own.wait()

    def finish(self):
        if not self.line:
            self.own.wait()
            for copy in self.copies:
                copy.wait()
            return
        for g in range(4):

            @pl.when(self.place.g == g)
            def _():
                for j in ((1, 2), (0, 2, 3), (0, 1, 3), (1, 2))[g]:
                    self.copy(g, self.landed.at[j], j, j, j).wait_recv()
                for copy in self.direct(g):
                    copy.wait_send()
                if g in (0, 3):
                    self.meeting(g).wait_send()
                else:
                    self.joined(g).wait_send()

    def holds(self, j):
        g = self.place.g
        return (g % 3 != 0) | (j + g != 3) if self.line else True


class Exchange:
    def __init__(self, place, blocks, held, send, recv, own):
        mine = place.rank()
        kept = held.at[mine // QUAD, mine % QUAD] if len(held.shape) == 4 else held.at[mine]

        def block(t):
            return blocks.at[0, t // QUAD, t % QUAD] if len(blocks.shape) == 5 else blocks.at[t]

        self.copies = []
        for n, relation in enumerate(RELATIONS):
            copy = remote(
                block(place.rank(relation)),
                kept,
                send.at[n],
                recv.at[n],
                place.peer(relation),
            )
            copy.start()
            self.copies.append(copy)
        copy = pltpu.make_async_copy(block(mine), kept, own)
        copy.start()
        self.copies.append(copy)

    def finish(self):
        for copy in self.copies:
            copy.wait()


LANES = 512


def lanes_of(n, width=LANES):
    return pl.ds(pl.multiple_of(n * width, width), width)


def shares_of(seq, values, weight, part):
    rows = part.shape[1]

    @pl.loop(0, part.shape[2] // LANES)
    def _(n):
        product = dot(values[seq], weight[lanes_of(n)], 1, 1)
        part[2 * seq, :, lanes_of(n)] = product[:rows].astype(bf16)
        part[2 * seq + 1, :, lanes_of(n)] = product[rows:].astype(bf16)


def over_tokens(first, lanes, second, other):
    total = dot(first[0, :, lanes], second[0, :, other], 0, 0)
    for seq in range(1, first.shape[0]):
        total += dot(first[seq, :, lanes], second[seq, :, other], 0, 0)
    return total


def row_shares(first, second, shares):
    grps, seqs, rows, _ = shares.shape
    width = 256
    pieces = width // rows

    @pl.loop(0, first.shape[2] // width)
    def _(b):
        product = over_tokens(first, lanes_of(b, width), second, slice(None)).astype(bf16)
        for p in range(pieces):
            index = b * pieces + p
            shares[index % grps, index // grps] = product[p * rows : (p + 1) * rows]


def summed_rows(landed, holds, blocks):
    seqs, rows = landed.shape[1], blocks.shape[1]
    for seq in range(seqs):
        for quad in range(QUAD):
            block = slice(quad * rows, (quad + 1) * rows)
            total = jnp.zeros((rows, landed.shape[3]), f32)
            for j in range(landed.shape[0]):
                total += jnp.where(holds(j), landed[j, seq, block].astype(f32), 0.0)
            blocks[seq * QUAD + quad] = total.astype(bf16)


def back_kernel(
    grps,
    aligned,
    facts,
    gains,
    cosine,
    sine,
    residual,
    own_tokens,
    own_grad,
    dgu_h,
    up_h,
    down_share_h,
    second_h,
    first_h,
    out_h,
    qkv_h,
    q_h,
    k_h,
    v_h,
    o_h,
    input_grad,
    gains_sum,
    down_landed,
    out_landed,
    up_held,
    qkv_held,
    up_landed,
    qkv_landed,
    down_met,
    up_met,
    out_met,
    qkv_met,
    wide,
    up,
    acts,
    out_w,
    qkv,
    part,
    near,
    far,
    blocks,
    turned,
    down_share,
    up_share,
    out_share,
    qkv_share,
    up_sum,
    qkv_sum,
    stage_low,
    stage_wide,
    gain_part,
    gain_plane,
    gain_far,
    load,
    near_send,
    near_recv,
    far_send,
    far_recv,
    all_send,
    all_recv,
    z_send,
    z_recv,
    swap_send,
    swap_recv,
    gain_send,
    gain_recv,
    own_sem,
):
    place = Place(grps)
    rows = residual.shape[0]
    gain_part[...] = jnp.zeros_like(gain_part)
    count, full_rows, head_width = q_h.shape

    def fetch(src, dst, n):
        copy = pltpu.make_async_copy(src, dst, load.at[n])
        copy.start()
        return copy

    loads = [fetch(dgu_h, wide, 0), fetch(up_h, up, 1), fetch(down_share_h, down_share, 2)]
    later = fetch(second_h, acts, 3)
    weights = [fetch(out_h, out_w, 5), fetch(qkv_h, qkv, 6)]
    place.greet()
    for copy in loads:
        copy.wait()

    sums = (near_send, near_recv, far_send, far_recv)
    def to_owners(n, shares, landed, met, stage):
        return ToOwners(place, shares, landed, met, stage, z_send.at[n], z_recv.at[n], own_sem.at[n]).start()

    def summed_over_plane(values, weight):
        total = PlaneSum(place, part, near, far, sums)
        for k in range(4):
            shares_of(total.sequence(k), values, weight, part)
            if k % 2 == 0:
                total.near(k)
            else:
                total.far(k)
        return total

    down_out = to_owners(0, down_share, down_landed, down_met, stage_low)
    second_sum = summed_over_plane(wide, up)
    later.wait()
    row_shares(acts, wide, up_share)
    up_out = to_owners(1, up_share, up_landed, up_met, stage_wide)
    fetch_first = fetch(first_h, acts, 3)
    down_out.join()
    heads = [
        fetch(ref, wide.at[:, :, n * head_width : (n + 1) * head_width], 7 + n)
        for n, ref in enumerate((q_h, k_h, v_h, o_h))
    ]

    second_sum.finish()
    mine = place.seat()
    inner = jnp.zeros((rows, 1), f32)
    squares = jnp.zeros((rows, 1), f32)
    for n in range(D // LANES):
        lanes = slice(n * LANES, (n + 1) * LANES)
        grad = second_sum.chunk(lanes)
        values = residual[:, lanes]
        inner += jnp.sum(grad * gains[1:2, lanes] * values, axis=-1, keepdims=True)
        squares += jnp.sum(values * values, axis=-1, keepdims=True)
    scale = lax.rsqrt(squares / D + NORM_EPSILON)
    inner = inner / D
    for n in range(D // LANES):
        lanes = slice(n * LANES, (n + 1) * LANES)
        grad, values = second_sum.chunk(lanes), residual[:, lanes]
        gain_part[1:2, lanes] = jnp.sum(grad * values * scale, axis=0, keepdims=True)
        total = own_grad[:, lanes].astype(f32) + scale * (
            grad * gains[1:2, lanes] - values * scale * scale * inner
        )
        input_grad[:, lanes] = total
        blocks[mine, :, lanes] = total.astype(bf16)

    gather = PlaneGather(place, blocks, all_send, all_recv)
    gather.start()
    for copy in weights + heads:
        copy.wait()

    lane = lax.broadcasted_iota(jnp.int32, (full_rows, head_width), 1)
    first_half = (lane % HEAD_DIM) < HEAD_DIM // 2

    for k in range(4):
        gather.arrive(k)
        seq = gather.sequence(k)
        grads = jnp.concatenate(
            [dot(blocks[2 * seq], out_w[...], 1, 1), dot(blocks[2 * seq + 1], out_w[...], 1, 1)],
            axis=0,
        ).astype(bf16)
        queries = wide[seq, :, 0:head_width]
        key_vectors = wide[seq, :, head_width : 2 * head_width]
        value_vectors = wide[seq, :, 2 * head_width : 3 * head_width]
        grad_q, grad_k, grad_v = attention_grads(
            facts[seq, 2:3, 0:1], queries, key_vectors, value_vectors, grads
        )
        for n, grad in enumerate((grad_q, grad_k)):
            values = (grad * HEAD_DIM**-0.5).astype(bf16).astype(f32)
            back = values * cosine[...] - swap_halves(values, first_half) * sine[...]
            turned[seq, :, n * head_width : (n + 1) * head_width] = back.astype(bf16)
        turned[seq, :, 2 * head_width : 3 * head_width] = grad_v.astype(bf16)
        if k == 1:
            up_out.join()

    gather.finish()
    fetch_first.wait()
    row_shares(acts, turned, qkv_share)
    triple = turned.shape[2]
    qkv_out = to_owners(2, qkv_share, qkv_landed, qkv_met, stage_wide.at[:, :, :triple])

    first_sum = summed_over_plane(turned, qkv)
    out_rows = out_share.shape[1]

    @pl.loop(0, D // LANES)
    def _(n):
        lanes = lanes_of(n)
        total = jnp.zeros((head_width, LANES), f32)
        for seq in range(count):
            values = wide[seq, :, 3 * head_width : 4 * head_width].astype(f32)
            total += dot(values[:rows].astype(bf16), blocks[2 * seq, :, lanes], 0, 0)
            total += dot(values[rows:].astype(bf16), blocks[2 * seq + 1, :, lanes], 0, 0)
        total = total.astype(bf16)
        for j in range(out_share.shape[0]):
            out_share[j, :, lanes] = total[j * out_rows : (j + 1) * out_rows]

    if aligned:
        out_out = to_owners(3, out_share, out_landed, out_met, stage_low.at[:out_rows])
    else:
        out_out = pltpu.make_async_copy(out_share, out_landed, own_sem.at[3])
        out_out.start()

    qkv_out.join()
    first_sum.finish()
    if aligned:
        out_out.join()
    inner = jnp.zeros((rows, 1), f32)
    squares = jnp.zeros((rows, 1), f32)
    for n in range(D // LANES):
        lanes = slice(n * LANES, (n + 1) * LANES)
        grad = first_sum.chunk(lanes)
        values = own_tokens[:, lanes].astype(f32)
        inner += jnp.sum(grad * gains[0:1, lanes] * values, axis=-1, keepdims=True)
        squares += jnp.sum(values * values, axis=-1, keepdims=True)
    scale = lax.rsqrt(squares / D + NORM_EPSILON)
    inner = inner / D
    for n in range(D // LANES):
        lanes = slice(n * LANES, (n + 1) * LANES)
        grad, values = first_sum.chunk(lanes), own_tokens[:, lanes].astype(f32)
        gain_part[0:1, lanes] = jnp.sum(grad * values * scale, axis=0, keepdims=True)
        input_grad[:, lanes] += scale * (
            grad * gains[0:1, lanes] - values * scale * scale * inner
        )

    gain_copies = []
    for n, relation in enumerate(RELATIONS):
        copy = remote(
            gain_part, gain_plane.at[n], gain_send.at[n], gain_recv.at[n], place.peer(relation)
        )
        copy.start()
        gain_copies.append(copy)

    up_out.finish()
    landed = pltpu.make_async_copy(up_landed, up_share, load.at[1])
    landed.start()
    for copy in gain_copies:
        copy.wait()
    total = gain_part[...]
    for n in range(len(RELATIONS)):
        total += gain_plane[n]
    gain_far[0] = total
    gain_copies = []
    for dz in range(1, grps):
        copy = remote(
            gain_far.at[0],
            gain_far.at[dz],
            gain_send.at[7 + dz],
            gain_recv.at[7 + dz],
            place.plane(dz),
        )
        copy.start()
        gain_copies.append(copy)
    landed.wait()
    summed_rows(up_share, up_out.holds, up_sum)
    up_swap = Exchange(place, up_sum, up_held, swap_send.at[0], swap_recv.at[0], own_sem.at[4])
    for copy in gain_copies:
        copy.wait()
    total = gain_far[0]
    for dz in range(1, grps):
        total += gain_far[dz]
    gains_sum[...] = total

    qkv_out.finish()
    landed = pltpu.make_async_copy(qkv_landed, qkv_share, load.at[6])
    landed.start()
    landed.wait()
    summed_rows(qkv_share, qkv_out.holds, qkv_sum)
    qkv_swap = Exchange(place, qkv_sum, qkv_held, swap_send.at[1], swap_recv.at[1], own_sem.at[5])
    if aligned:
        out_out.finish()
    else:
        out_out.wait()
    down_out.finish()
    up_swap.finish()
    qkv_swap.finish()


def backward(
    grps,
    aligned,
    facts,
    gains,
    tables,
    residual,
    own_tokens,
    own_grad,
    grad_both,
    up_local,
    down_share,
    second_norm,
    first_norm,
    out_local,
    qkv_local,
    heads,
):
    rows = residual.shape[0]
    count, full_rows, head_width = heads[0].shape
    seqs = full_rows // rows
    ranks = seqs * QUAD
    units = down_share.shape[1]
    both = grad_both.shape[2]
    quad_rows = D // (seqs * grps)
    shard = quad_rows // QUAD
    out_rows = head_width // grps if aligned else HEAD_DIM
    triple = 3 * head_width
    out_count = head_width // out_rows
    hbm = pl.BlockSpec(memory_space=pl.ANY)
    vmem = pl.BlockSpec(memory_space=pltpu.VMEM)
    shape = jax.ShapeDtypeStruct
    dma = pltpu.SemaphoreType.DMA
    return pl.pallas_call(
        lambda *refs: back_kernel(grps, aligned, *refs),
        in_specs=[vmem] * 7 + [hbm] * 11,
        out_specs=[vmem] * 2 + [hbm] * 10,
        out_shape=[
            shape((rows, D), f32),
            shape((8, D), f32),
            shape((grps, units, D), bf16),
            shape((out_count, out_rows, D), bf16),
            shape((ranks, shard, both), bf16),
            shape((ranks, shard, triple), bf16),
            shape((grps, seqs, quad_rows, both), bf16),
            shape((grps, seqs, quad_rows, triple), bf16),
            shape((units, D), bf16),
            shape((seqs, quad_rows, both), bf16),
            shape((out_rows, D), bf16),
            shape((seqs, quad_rows, triple), bf16),
        ],
        scratch_shapes=[
            pltpu.VMEM((count, full_rows, both), bf16),
            pltpu.VMEM((D, both), bf16),
            pltpu.VMEM((count, full_rows, D), bf16),
            pltpu.VMEM((head_width, D), bf16),
            pltpu.VMEM((D, triple), bf16),
            pltpu.VMEM((ranks, rows, D), bf16),
            pltpu.VMEM((4, rows, D), bf16),
            pltpu.VMEM((3, rows, D), bf16),
            pltpu.VMEM((ranks, rows, D), bf16),
            pltpu.VMEM((count, full_rows, triple), bf16),
            pltpu.VMEM((grps, units, D), bf16),
            pltpu.VMEM((grps, seqs, quad_rows, both), bf16),
            pltpu.VMEM((out_count, out_rows, D), bf16),
            pltpu.VMEM((grps, seqs, quad_rows, triple), bf16),
            pltpu.VMEM((ranks, shard, both), bf16),
            pltpu.VMEM((ranks, shard, triple), bf16),
            pltpu.VMEM((units, D), bf16),
            pltpu.VMEM((seqs, quad_rows, both), bf16),
            pltpu.VMEM((8, D), f32),
            pltpu.VMEM((7, 8, D), f32),
            pltpu.VMEM((grps, 8, D), f32),
            dma((11,)),
            dma((4,)),
            dma((4,)),
            dma((3,)),
            dma((3,)),
            dma((7,)),
            dma((7,)),
            dma((4, grps)),
            dma((4, grps)),
            dma((2, 7)),
            dma((2, 7)),
            dma((7 + grps,)),
            dma((7 + grps,)),
            dma((6,)),
        ],
        compiler_params=pltpu.CompilerParams(
            collective_id=0, has_side_effects=True, vmem_limit_bytes=VMEM_LIMIT
        ),
        cost_estimate=pl.CostEstimate(
            flops=30 * 10**9, bytes_accessed=60 * 2**20, transcendentals=2 * 10**6
        ),
        name="backward",
    )(
        facts,
        gains,
        *tables,
        residual,
        own_tokens,
        own_grad,
        grad_both,
        up_local,
        down_share,
        second_norm,
        first_norm,
        out_local,
        qkv_local,
        *heads,
    )


CHUNK = 1024


class FromOwners:
    def __init__(self, place, source, landed, landing, send, recv, own):
        self.place, self.source, self.send, self.recv = place, source, send, recv
        self.slot = lambda j: landing(landed, j)
        self.own = pltpu.make_async_copy(source, self.slot(place.g), own)
        self.line = place.grps == 4

    def copy(self, source, slot, sem, recv, target):
        place = self.place
        return remote(
            source, self.slot(slot), self.send.at[sem], self.recv.at[recv], (place.s, target, place.r, place.c)
        )

    def direct(self, g):
        targets = ((1, 2, 3), (0, 2), (3, 1), (2, 1, 0))[g]
        return [self.copy(self.source, g, t, g, t) for t in targets]

    def passed_on(self, g):
        inner, end = 3 - g, 0 if g == 1 else 3
        return self.copy(self.slot(inner), inner, 3 - end, inner, end)

    def arrival(self, j):
        return self.copy(self.source, j, j, j, j)

    def start(self):
        place = self.place
        self.own.start()
        if self.line:
            for g in range(4):

                @pl.when(place.g == g)
                def _():
                    for copy in self.direct(g):
                        copy.start()

        else:
            self.copies = [
                self.copy(self.source, place.g, dz, dz, (place.g + dz) % place.grps)
                for dz in range(1, place.grps)
            ]
            for copy in self.copies:
                copy.start()

    def relay(self):
        if self.line:
            for g in (1, 2):

                @pl.when(self.place.g == g)
                def _():
                    self.arrival(3 - g).wait_recv()
                    self.passed_on(g).start()

    def finish(self):
        self.own.wait()
        if self.line:
            for g in range(4):

                @pl.when(self.place.g == g)
                def _():
                    for j in range(4):
                        if j != g and not (g in (1, 2) and j == 3 - g):
                            self.arrival(j).wait_recv()
                    for copy in self.direct(g):
                        copy.wait_send()
                    if g in (1, 2):
                        self.passed_on(g).wait_send()

        else:
            for copy in self.copies:
                copy.wait()


def shares_from(seq, values, weight, part):
    rows = part.shape[1]

    @pl.loop(0, part.shape[2] // LANES)
    def _(n):
        product = dot(values[seq], weight[:, lanes_of(n)])
        part[2 * seq, :, lanes_of(n)] = product[:rows].astype(bf16)
        part[2 * seq + 1, :, lanes_of(n)] = product[rows:].astype(bf16)


def times_slices(values, weight, lanes):
    seqs, grps, quad, shard, _ = weight.shape
    depth = quad * shard
    total = None
    for n in range(seqs * grps):
        piece = weight[n // grps, n % grps, :, :, lanes]
        term = dot(values[:, n * depth : (n + 1) * depth], piece.reshape(depth, piece.shape[2]))
        total = term if total is None else total + term
    return total


def both_blocks(blocks, seq):
    return jnp.concatenate([blocks[2 * seq].astype(f32), blocks[2 * seq + 1].astype(f32)], axis=0)


def forward_kernel(
    grps,
    aligned,
    cosine,
    sine,
    own_facts,
    tokens_h,
    own_grad_h,
    qkv_own,
    up_own,
    out_own,
    down_own,
    residual,
    gains,
    facts,
    first_h,
    q_h,
    k_h,
    v_h,
    o_h,
    second_h,
    down_share_h,
    hidden_h,
    dgu_h,
    qkv_landed,
    up_landed,
    out_landed,
    down_landed,
    blocks,
    grad_blocks,
    norm,
    grad_seq,
    qkv_rank,
    up_rank,
    qkv,
    up,
    out_w,
    down,
    heads,
    part,
    near,
    far,
    both,
    hidden,
    dgu,
    all_facts,
    early,
    load,
    store,
    swap_send,
    swap_recv,
    near_send,
    near_recv,
    far_send,
    far_recv,
    all_send,
    all_recv,
    z_send,
    z_recv,
    fact_send,
    fact_recv,
    own_sem,
):
    place = Place(grps)
    count, full_rows, _ = norm.shape
    rows = residual.shape[0]
    head_width = heads.shape[3]
    mine, rank = place.seat(), place.rank()

    def fetch(src, dst, n):
        copy = pltpu.make_async_copy(src, dst, load.at[n])
        copy.start()
        return copy

    def keep(src, dst, n):
        copy = pltpu.make_async_copy(src, dst, store.at[n])
        copy.start()
        return copy

    shard = qkv_own.shape[0]
    units = down.shape[0] // grps
    seqs = qkv_landed.shape[0]
    slots = iter(range(20))

    def fetch_chunks(src):
        pieces = []
        for top in range(0, src.shape[0], shard):
            for left in range(0, src.shape[1], CHUNK):
                slot = next(slots)
                space = both.at[slot // 5, (slot % 5) * shard : (slot % 5 + 1) * shard]
                copy = pltpu.make_async_copy(
                    src.at[top : top + shard, left : left + CHUNK], space, early.at[slot]
                )
                copy.start()
                pieces.append((copy, space))
        return pieces

    def dealt(pieces, weight, lanes, parts):
        count = CHUNK // (QUAD * lanes)
        width = count * lanes
        each = len(pieces) // (parts * seqs)
        for n, (copy, space) in enumerate(pieces):
            copy.wait()
            values = space[...]
            seq = n // each % seqs
            first = (n // (each * seqs) * each + n % each) * width
            for q in range(QUAD):
                taken = [
                    values[:, (k * QUAD + q) * lanes : (k * QUAD + q + 1) * lanes] for k in range(count)
                ]
                weight[0, seq, q, :, first : first + width] = jnp.concatenate(taken, axis=1).astype(bf16)

    facts[rank] = own_facts[...]
    qkv_pieces = fetch_chunks(qkv_own)
    if aligned:
        out_pieces = fetch_chunks(out_own)
    up_pieces = fetch_chunks(up_own)
    down_pieces = fetch_chunks(down_own)
    own_blocks = [fetch(tokens_h, blocks.at[mine], 0), fetch(own_grad_h, grad_blocks.at[mine], 1)]

    def plane_rows(ref, j):
        return ref.at[:, j]

    def own_rows(ref, j):
        size = ref.shape[0] // grps
        return ref.at[pl.ds(pl.multiple_of(j * size, size), size)]

    def from_owners(n, source, landed, landing):
        return FromOwners(place, source, landed, landing, z_send.at[n], z_recv.at[n], own_sem.at[n])

    def stacked(pieces, weight):
        across = weight.shape[1] // CHUNK
        for n, (copy, space) in enumerate(pieces):
            copy.wait()
            top, left = n // across * shard, n % across * CHUNK
            weight[top : top + shard, left : left + CHUNK] = space[...].astype(bf16)

    down_z = from_owners(3, down.at[:units], down_landed, own_rows)
    dealt(qkv_pieces, qkv, HEAD_DIM, 3)
    place.greet()
    if aligned:
        stacked(out_pieces, out_w)
        out_z = from_owners(2, out_w.at[:shard], out_landed, own_rows)
        out_z.start()
    qkv_swap = Exchange(place, qkv, qkv_rank, swap_send.at[0], swap_recv.at[0], own_sem.at[4])
    fact_copies = []
    for n, relation in enumerate(RELATIONS):
        copy = remote(own_facts, facts.at[rank], fact_send.at[n], fact_recv.at[n], place.peer(relation))
        copy.start()
        fact_copies.append(copy)
    dealt(up_pieces, up, units, 2)
    stacked(down_pieces, down)
    for copy in own_blocks:
        copy.wait()
    qkv_swap.finish()
    qkv_z = from_owners(0, qkv_rank, qkv_landed, plane_rows)
    up_z = from_owners(1, up_rank, up_landed, plane_rows)
    qkv_z.start()
    token_gather = PlaneGather(place, blocks, all_send.at[0], all_recv.at[0])
    token_gather.start()
    for copy in fact_copies:
        copy.wait()
    all_facts[place.g] = facts[...]
    fact_copies = []
    for dz in range(1, grps):
        copy = remote(
            facts,
            all_facts.at[place.g],
            fact_send.at[7 + dz],
            fact_recv.at[7 + dz],
            place.plane(dz),
        )
        copy.start()
        fact_copies.append(copy)
    if aligned:
        out_z.relay()
    for copy in fact_copies:
        copy.wait()
    width = D // (seqs * grps * QUAD)
    for n in range(seqs * grps):
        pieces = [all_facts[n % grps, (n // grps) * QUAD + q, :, :width] for q in range(QUAD)]
        gains[:, n * QUAD * width : (n + 1) * QUAD * width] = jnp.concatenate(pieces, axis=1)
    token_gather.forward(0)
    token_gather.forward(1)
    up_swap = Exchange(place, up, up_rank, swap_send.at[1], swap_recv.at[1], own_sem.at[5])
    qkv_z.relay()
    token_gather.forward(2)
    token_gather.arrive(3)
    token_gather.copies[3].wait_recv()
    token_gather.copies[4].wait_recv()
    token_gather.finish()

    @pl.loop(0, count)
    def _(seq):
        values = both_blocks(blocks, seq)
        scale = lax.rsqrt(jnp.mean(values * values, axis=-1, keepdims=True) + NORM_EPSILON)
        norm[seq] = (values * scale * gains[0:1, :]).astype(bf16)

    stores = [keep(norm, first_h, 0)]
    grad_gather = PlaneGather(place, grad_blocks, all_send.at[1], all_recv.at[1])
    grad_gather.start()
    up_swap.finish()
    qkv_z.finish()
    up_z.start()
    fetch(qkv_landed, qkv, 2).wait()

    lane = lax.broadcasted_iota(jnp.int32, (full_rows, head_width), 1)
    first_half = (lane % HEAD_DIM) < HEAD_DIM // 2

    if aligned:
        out_z.finish()
        fetch(out_landed, out_w, 3).wait()
    else:
        fetch(out_own, out_w, 3).wait()

    plane_sum = PlaneSum(place, part, near, far, (near_send, near_recv, far_send, far_recv))
    mixed = heads.at[3]
    for k in range(4):
        seq = plane_sum.sequence(k)
        for n in range(3):
            lanes = slice(n * head_width, (n + 1) * head_width)
            values = times_slices(norm[seq], qkv, lanes)
            if n < 2:
                values = values * cosine[...] + swap_halves(values, first_half) * sine[...]
            heads[n, seq] = values.astype(bf16)
        heads[3, seq] = attention(facts[seq, 2:3, 0:1], heads[0, seq], heads[1, seq], heads[2, seq])
        shares_from(seq, mixed, out_w, part)
        if k % 2 == 0:
            plane_sum.near(k)
        else:
            plane_sum.far(k)
        if k == 0:
            grad_gather.forward(0)
            grad_gather.forward(1)
    grad_gather.forward(2)
    grad_gather.arrive(3)
    grad_gather.copies[3].wait_recv()
    grad_gather.copies[4].wait_recv()
    grad_gather.finish()
    stores += [keep(heads.at[n], ref, 1 + n) for n, ref in enumerate((q_h, k_h, v_h, o_h))]
    up_z.relay()

    @pl.loop(0, count)
    def _(seq):
        grad_seq[seq] = both_blocks(grad_blocks, seq).astype(bf16)

    fetch(tokens_h, grad_blocks.at[mine], 4).wait()
    plane_sum.finish()
    squares = jnp.zeros((rows, 1), f32)
    for n in range(D // LANES):
        lanes = slice(n * LANES, (n + 1) * LANES)
        values = grad_blocks[mine, :, lanes].astype(f32) + plane_sum.chunk(lanes)
        residual[:, lanes] = values
        squares += jnp.sum(values * values, axis=-1, keepdims=True)
    scale = lax.rsqrt(squares / D + NORM_EPSILON)
    for n in range(D // LANES):
        lanes = slice(n * LANES, (n + 1) * LANES)
        blocks[mine, :, lanes] = (residual[:, lanes] * scale * gains[1:2, lanes]).astype(bf16)
    norm_gather = PlaneGather(place, blocks, all_send.at[2], all_recv.at[2])
    norm_gather.start()
    down_z.start()
    stores[0].wait()
    half = hidden.shape[2]
    for k in range(4):
        norm_gather.arrive(k)
        seq = norm_gather.sequence(k)
        norm[seq] = both_blocks(blocks, seq).astype(bf16)
        if k == 0:
            up_z.finish()
            fetch(up_landed, up, 5).wait()
        gate = times_slices(norm[seq], up, slice(0, half))
        above = times_slices(norm[seq], up, slice(half, 2 * half))
        both[seq, :, :half] = gate
        both[seq, :, half:] = above
        hidden[seq] = (gate * jax.nn.sigmoid(gate) * above).astype(bf16)
    norm_gather.finish()
    stores[0] = keep(norm, second_h, 5)
    down_z.relay()
    stores.append(keep(hidden, hidden_h, 7))
    tall = min(256, half)
    slab = part.shape[1] // 128 * 128

    @pl.loop(0, half // tall)
    def _(b):
        for side in range(2):
            lanes = slice(side * D // 2, (side + 1) * D // 2)
            product = over_tokens(hidden, lanes_of(b, tall), grad_seq, lanes).astype(bf16)
            for p in range(tall // slab):
                part[b * (tall // slab) + p, :slab, lanes] = product[p * slab : (p + 1) * slab]

    stores.append(keep(part.at[: half // slab, :slab], down_share_h, 6))
    down_z.finish()
    fetch(down_landed, down, 6).wait()

    @pl.loop(0, count)
    def _(seq):
        grads = dot(grad_seq[seq], down[...], 1, 1)
        gate, above = both[seq, :, :half], both[seq, :, half:]
        sigmoid = jax.nn.sigmoid(gate)
        dgu[seq, :, :half] = (grads * above * sigmoid * (1.0 + gate * (1.0 - sigmoid))).astype(bf16)
        dgu[seq, :, half:] = (grads * (gate * sigmoid)).astype(bf16)

    stores.append(keep(dgu, dgu_h, 8))
    for copy in stores:
        copy.wait()


def forward(grps, aligned, tables, own_facts, tokens, own_grad, qkv_own, up_own, out_own, down_own):
    rows = tokens.shape[0]
    shard = qkv_own.shape[0]
    seqs = D // (shard * grps * QUAD)
    ranks = seqs * QUAD
    triple, both = qkv_own.shape[1] // ranks, up_own.shape[1] // ranks
    count, full_rows, head_width = QUAD, rows * seqs, triple // 3
    half = both // 2
    hbm = pl.BlockSpec(memory_space=pl.ANY)
    vmem = pl.BlockSpec(memory_space=pltpu.VMEM)
    shape = jax.ShapeDtypeStruct
    dma = pltpu.SemaphoreType.DMA
    by_heads = shape((count, full_rows, head_width), bf16)
    return pl.pallas_call(
        lambda *refs: forward_kernel(grps, aligned, *refs),
        in_specs=[vmem] * 3 + [hbm] * 6,
        out_specs=[vmem] * 3 + [hbm] * 13,
        out_shape=[
            shape((rows, D), f32),
            shape((8, D), f32),
            shape((ranks, 8, 128), f32),
            shape((count, full_rows, D), bf16),
            by_heads,
            by_heads,
            by_heads,
            by_heads,
            shape((count, full_rows, D), bf16),
            shape((half // 128, 128, D), bf16),
            shape((count, full_rows, half), bf16),
            shape((count, full_rows, both), bf16),
            shape((seqs, grps, QUAD, shard, triple), bf16),
            shape((seqs, grps, QUAD, shard, both), bf16),
            shape((head_width, D), bf16),
            shape((half, D), bf16),
        ],
        scratch_shapes=[
            pltpu.VMEM((ranks, rows, D), bf16),
            pltpu.VMEM((ranks, rows, D), bf16),
            pltpu.VMEM((count, full_rows, D), bf16),
            pltpu.VMEM((count, full_rows, D), bf16),
            pltpu.VMEM((seqs, QUAD, shard, triple), bf16),
            pltpu.VMEM((seqs, QUAD, shard, both), bf16),
            pltpu.VMEM((seqs, grps, QUAD, shard, triple), bf16),
            pltpu.VMEM((seqs, grps, QUAD, shard, both), bf16),
            pltpu.VMEM((head_width, D), bf16),
            pltpu.VMEM((half, D), bf16),
            pltpu.VMEM((4, count, full_rows, head_width), bf16),
            pltpu.VMEM((ranks, rows, D), bf16),
            pltpu.VMEM((4, rows, D), bf16),
            pltpu.VMEM((3, rows, D), bf16),
            pltpu.VMEM((count, full_rows, both), f32),
            pltpu.VMEM((count, full_rows, half), bf16),
            pltpu.VMEM((count, full_rows, both), bf16),
            pltpu.VMEM((grps, ranks, 8, 128), f32),
            dma((20,)),
            dma((7,)),
            dma((9,)),
            dma((2, 7)),
            dma((2, 7)),
            dma((4,)),
            dma((4,)),
            dma((3,)),
            dma((3,)),
            dma((3, 7)),
            dma((3, 7)),
            dma((4, grps)),
            dma((4, grps)),
            dma((7 + grps,)),
            dma((7 + grps,)),
            dma((6,)),
        ],
        compiler_params=pltpu.CompilerParams(
            collective_id=1, has_side_effects=True, vmem_limit_bytes=VMEM_LIMIT
        ),
        cost_estimate=pl.CostEstimate(
            flops=20 * 10**9, bytes_accessed=60 * 2**20, transcendentals=4 * 10**6
        ),
        name="forward",
    )(*tables, own_facts, tokens, own_grad, qkv_own, up_own, out_own, down_own)


ADAM_WIDTH = 1024


def adam_step(gradient, weight, moment, square, step_rate, outs):
    results = adam_update(weight[...], moment[...], square[...], gradient, step_rate)
    for out, result in zip(outs, results):
        out[...] = result
    outs[3][...] = results[0].astype(bf16)


def adam_ranks_kernel(lanes, step_rate, held, weight, moment, square, *outs):
    values = [held[0, q].astype(f32) for q in range(QUAD)]
    gradient = jnp.concatenate(
        [
            values[q][:, n * lanes : (n + 1) * lanes]
            for n in range(held.shape[3] // lanes)
            for q in range(QUAD)
        ],
        axis=1,
    )
    adam_step(gradient, weight, moment, square, step_rate, outs)


def adam_planes_kernel(step_rate, holds, landed, weight, moment, square, *outs):
    total = jnp.zeros(weight.shape, f32)
    for j in range(landed.shape[0]):
        total += jnp.where(holds[j] > 0, landed[j].astype(f32), 0.0)
    adam_step(total, weight, moment, square, step_rate, outs)


def adam_call(kernel, grads, grad_specs, state):
    rows, columns = state[0].shape
    block = pl.BlockSpec((rows, ADAM_WIDTH), lambda n: (0, n))
    like = jax.ShapeDtypeStruct((rows, columns), f32)
    return pl.pallas_call(
        kernel,
        grid=(columns // ADAM_WIDTH,),
        in_specs=grad_specs + [block] * 3,
        out_specs=[block] * 4,
        out_shape=[like] * 3 + [jax.ShapeDtypeStruct((rows, columns), bf16)],
        compiler_params=pltpu.CompilerParams(vmem_limit_bytes=32 * 2**20),
        cost_estimate=pl.CostEstimate(
            flops=rows * columns * 16, bytes_accessed=rows * columns * 28, transcendentals=rows * columns
        ),
        name="adam",
    )(*grads, *state)


def adam_from_ranks(held, seqs, parts, lanes, step_rate, *state):
    ranks, rows, columns = held.shape
    width = ADAM_WIDTH // QUAD
    blocks = columns // (parts * width)
    grouped = held.reshape(seqs, QUAD, rows, columns)
    spec = pl.BlockSpec(
        (1, QUAD, rows, width),
        lambda n: ((n // blocks) % seqs, 0, 0, n // (blocks * seqs) * blocks + n % blocks),
    )
    return adam_call(
        lambda *refs: adam_ranks_kernel(lanes, step_rate, *refs), (grouped,), [spec], state
    )


def adam_from_planes(landed, holds, step_rate, *state):
    planes, rows, _ = landed.shape
    specs = [
        pl.BlockSpec(memory_space=pltpu.SMEM),
        pl.BlockSpec((planes, rows, ADAM_WIDTH), lambda n: (0, 0, n)),
    ]
    return adam_call(
        lambda *refs: adam_planes_kernel(step_rate, *refs), (holds, landed), specs, state
    )


def seat_sum(partial):
    return lax.psum_scatter(
        partial.astype(bf16), SEATS, scatter_dimension=0, tiled=True
    ).astype(f32)


def on_device(
    tokens,
    cotangent,
    lengths,
    qkv_weight,
    qkv_moment,
    qkv_square,
    out_weight,
    out_moment,
    out_square,
    up_weight,
    up_moment,
    up_square,
    down_weight,
    down_moment,
    down_square,
    norm_gains,
    gains_moment,
    gains_square,
):
    seqs = lax.axis_size("seq")
    grps = lax.axis_size("grp")
    ranks = seqs * QUAD
    own_rows = tokens.shape[1]
    full_rows = own_rows * seqs
    all_rows = full_rows * QUAD
    heads_local = HEADS // ranks
    head_width = heads_local * HEAD_DIM
    units = down_weight.shape[0]
    aligned = out_weight.shape[0] == HEAD_DIM
    tables = rotate_table(full_rows, heads_local)

    positions = lax.axis_index("seq") * own_rows + jnp.arange(own_rows, dtype=jnp.int32)
    own_grad = jnp.where((positions < lengths[0])[:, None], cotangent[0], 0)
    own_gains = norm_gains.shape[1]
    own_facts = jnp.zeros((8, 128), f32)
    own_facts = own_facts.at[:2, :own_gains].set(norm_gains.astype(bf16).astype(f32))
    own_facts = own_facts.at[2].set(lengths[0].astype(f32))

    out_own = out_weight
    if not aligned:
        out_all = lax.all_gather(out_weight.astype(bf16), EVERY, axis=0, tiled=True)
        out_all = out_all.reshape(seqs, heads_local, QUAD, HEAD_DIM, D)
        seat = lax.axis_index("row") * 2 + lax.axis_index("core")
        out_own = lax.dynamic_index_in_dim(
            lax.dynamic_index_in_dim(out_all, lax.axis_index("seq"), 0, False), seat, 1, False
        ).reshape(head_width, D)
    (
        residual,
        gains,
        facts,
        first_norm,
        queries,
        key_vectors,
        value_vectors,
        attended,
        second_norm,
        down_share,
        hidden,
        grad_both,
        qkv_local,
        up_local,
        out_local,
        down_local,
    ) = forward(
        grps,
        aligned,
        tables,
        own_facts,
        tokens[0],
        own_grad,
        qkv_weight,
        up_weight,
        out_own,
        down_weight,
    )
    if not aligned:
        out_local = out_own
    (
        input_grad,
        gains_total,
        down_planes,
        out_planes,
        up_ranks,
        qkv_ranks,
        *_,
    ) = backward(
        grps,
        aligned,
        facts,
        gains,
        tables,
        residual,
        tokens[0],
        own_grad,
        grad_both,
        up_local.reshape(D, -1),
        down_share.reshape(grps, units, D),
        second_norm,
        first_norm,
        out_local,
        qkv_local.reshape(D, -1),
        (queries, key_vectors, value_vectors, attended),
    )
    block_output = (
        residual + seat_sum(dot(hidden.reshape(all_rows, -1), down_local))
    ).astype(bf16)
    if aligned:
        out_sum = out_planes
    else:
        placed_term = jnp.zeros((seqs, QUAD, heads_local, HEAD_DIM, D), bf16)
        placed_term = lax.dynamic_update_slice(
            placed_term,
            out_planes.reshape(1, 1, heads_local, HEAD_DIM, D),
            (lax.axis_index("seq"), seat, 0, 0, 0),
        )
        out_sum = lax.psum_scatter(
            placed_term.transpose(0, 2, 1, 3, 4).reshape(D, D),
            EVERY,
            scatter_dimension=0,
            tiled=True,
        )[None]
    device = ((lax.axis_index("seq") * grps + lax.axis_index("grp")) * 2 + lax.axis_index("row")) * 2
    gains_sum = lax.dynamic_slice(
        gains_total, (0, (device + lax.axis_index("core")) * own_gains), (2, own_gains)
    )
    planes = jnp.arange(grps)
    plane = lax.axis_index("grp")
    holds = ((planes + plane != 3) | (plane % 3 != 0) | (grps != 4)).astype(jnp.int32)
    qkv_new = adam_from_ranks(
        qkv_ranks, seqs, 3, HEAD_DIM, D ** (-0.5), qkv_weight, qkv_moment, qkv_square
    )
    up_new = adam_from_ranks(
        up_ranks, seqs, 2, units, D ** (-0.5), up_weight, up_moment, up_square
    )
    out_new = adam_from_planes(
        out_sum, holds, (D // 128) ** (-0.5), out_weight, out_moment, out_square
    )
    down_new = adam_from_planes(
        down_planes, holds, FF ** (-0.5), down_weight, down_moment, down_square
    )
    gains_new = adam_update(norm_gains, gains_moment, gains_square, gains_sum, 0.3)
    return (
        block_output[None],
        input_grad[None],
        *qkv_new,
        *out_new,
        *up_new,
        *down_new,
        *gains_new,
    )


def solution(mesh):
    seqs, rest = mesh.shape["seq"], mesh.shape["fsdp"]
    planes = Mesh(
        mesh.devices.reshape(seqs, rest // QUAD, 2, 2), ("seq", "grp", "row", "core")
    )
    rows = P(("grp", "row", "core"), "seq", None)
    shards = P(EVERY, None)
    gains = P(None, EVERY)
    return jax.shard_map(
        on_device,
        mesh=planes,
        in_specs=(rows, rows, P(("grp", "row", "core"))) + (shards,) * 12 + (gains,) * 3,
        out_specs=(rows, rows) + (shards,) * 16 + (gains,) * 3,
        check_vma=False,
    )
```

```python
import math

import jax
import jax.numpy as jnp
from jax import lax
from jax.experimental import pallas as pl
from jax.experimental.pallas import tpu as pltpu
from jax.sharding import Mesh, PartitionSpec as P

D = 2048
HEADS = 32
HEAD_DIM = 64
FF = 4096
WINDOW = 128
STEP = 5


NORM_EPSILON = 1e-05
MOMENT_DECAY = 0.5
WEIGHT_DECAY = 0.1
ADAM_EPSILON = 1e-08

SEATS = ("row", "core", "seq")
RANKS = ("seq", "row", "core")
EVERY = ("seq", "grp", "row", "core")
QUAD = 4
VMEM_LIMIT = 63 * 2**20

bf16 = jnp.bfloat16
f32 = jnp.float32


def rotate_table(length, copies):
    halves = HEAD_DIM // 2
    freqs = jnp.exp(-math.log(10000.0) * 2.0 * jnp.arange(halves).astype(f32) / HEAD_DIM)
    angles = jnp.arange(length, dtype=jnp.int32).astype(f32)[:, None] * freqs[None, :]
    cosine, sine = jnp.cos(angles), jnp.sin(angles)
    return (
        jnp.tile(jnp.concatenate([cosine, cosine], axis=1), (1, copies)),
        jnp.tile(jnp.concatenate([-sine, sine], axis=1), (1, copies)),
    )


def adam_update(weight, moment, square, gradient, step_rate):
    moment_new = MOMENT_DECAY * moment + (1.0 - MOMENT_DECAY) * gradient
    square_new = MOMENT_DECAY * square + (1.0 - MOMENT_DECAY) * gradient * gradient
    correction = 1.0 - MOMENT_DECAY**STEP
    update = moment_new / correction / (jnp.sqrt(square_new / correction) + ADAM_EPSILON)
    return (weight - step_rate * (update + WEIGHT_DECAY * weight), moment_new, square_new)


def dot(a, b, lhs=1, rhs=0):
    return lax.dot_general(a, b, (((lhs,), (rhs,)), ((), ())), preferred_element_type=f32)


def swap_halves(values, first):
    width = values.shape[1]
    half = HEAD_DIM // 2
    return jnp.where(
        first, pltpu.roll(values, width - half, 1), pltpu.roll(values, half, 1)
    )


def allowed_mask(rows, length):
    row = lax.broadcasted_iota(jnp.int32, (rows, rows), 0)
    col = lax.broadcasted_iota(jnp.int32, (rows, rows), 1)
    return (col <= row) & (row - col < WINDOW) & (col.astype(f32) < length)


def head_lanes(rows, width, head):
    lane = lax.broadcasted_iota(jnp.int32, (rows, width), 1)
    return (lane // HEAD_DIM) == head


def softmax_rows(queries, key_vectors, allowed):
    scores = jnp.where(allowed, dot(queries, key_vectors, 1, 1) * (HEAD_DIM**-0.5), -1e30)
    shifted = jnp.exp(scores - jnp.max(scores, axis=-1, keepdims=True))
    return shifted / jnp.sum(shifted, axis=-1, keepdims=True)


def attention(length, queries, key_vectors, value_vectors):
    rows, width = queries.shape
    allowed = allowed_mask(rows, length)
    total = jnp.zeros((rows, width), f32)
    for head in range(width // HEAD_DIM):
        mine = head_lanes(rows, width, head)
        weights = softmax_rows(jnp.where(mine, queries, 0), key_vectors, allowed)
        total += dot(weights.astype(bf16), jnp.where(mine, value_vectors, 0))
    return total.astype(bf16)


def attention_grads(length, queries, key_vectors, value_vectors, grads):
    rows, width = queries.shape
    allowed = allowed_mask(rows, length)
    grad_q = jnp.zeros((rows, width), f32)
    grad_k = jnp.zeros((rows, width), f32)
    grad_v = jnp.zeros((rows, width), f32)
    for head in range(width // HEAD_DIM):
        mine = head_lanes(rows, width, head)
        q_head = jnp.where(mine, queries, 0)
        g_head = jnp.where(mine, grads, 0)
        weights = softmax_rows(q_head, key_vectors, allowed)
        grad_p = dot(g_head, value_vectors, 1, 1)
        delta = jnp.sum(weights * grad_p, axis=-1, keepdims=True)
        grad_s = jnp.where(allowed, weights * (grad_p - delta), 0.0).astype(bf16)
        grad_q += dot(grad_s, jnp.where(mine, key_vectors, 0))
        grad_k += dot(grad_s, q_head, 0, 0)
        grad_v += dot(weights.astype(bf16), g_head, 0, 0)
    return grad_q, grad_k, grad_v


MESH = pl.DeviceIdType.MESH
RELATIONS = tuple((a, b, d) for a in range(2) for b in range(2) for d in range(2))[1:]


class Place:
    def __init__(self, grps):
        self.grps = grps
        self.s = lax.axis_index("seq")
        self.g = lax.axis_index("grp")
        self.r = lax.axis_index("row")
        self.c = lax.axis_index("core")

    def peer(self, relation):
        ds, dr, dc = relation
        return ((self.s + ds) % 2, self.g, (self.r + dr) % 2, (self.c + dc) % 2)

    def plane(self, dz):
        return (self.s, (self.g + dz) % self.grps, self.r, self.c)

    def rank(self, relation=(0, 0, 0)):
        s, _, r, c = self.peer(relation)
        return (s * 2 + r) * 2 + c

    def seat(self, relation=(0, 0, 0)):
        s, _, r, c = self.peer(relation)
        return (r * 2 + c) * 2 + s

    def corner(self, relation=(0, 0, 0)):
        s, _, r, _ = self.peer(relation)
        return r * 2 + s

    def greet(self):
        barrier = pltpu.get_barrier_semaphore()
        for relation in RELATIONS:
            pl.semaphore_signal(barrier, inc=1, device_id=self.peer(relation), device_id_type=MESH)
        for dz in range(1, self.grps):
            pl.semaphore_signal(barrier, inc=1, device_id=self.plane(dz), device_id_type=MESH)
        pl.semaphore_wait(barrier, len(RELATIONS) + self.grps - 1)


SIBLING = (0, 0, 1)
ACROSS = ((1, 0, 0), (0, 1, 0), (1, 1, 0))


def remote(src, dst, send_sem, recv_sem, device):
    return pltpu.make_async_remote_copy(
        src_ref=src,
        dst_ref=dst,
        send_sem=send_sem,
        recv_sem=recv_sem,
        device_id=device,
        device_id_type=MESH,
    )


class PlaneSum:
    def __init__(self, place, part, near, far, sems):
        self.place, self.part, self.nears, self.fars = place, part, near, far
        self.near_send, self.near_recv, self.far_send, self.far_recv = sems
        self.first, self.second = [None] * 4, []

    def sequence(self, k):
        place = self.place
        row = (place.r + 1) % 2 if k < 2 else place.r
        return row * 2 + ((place.c + 1) % 2 if k % 2 == 0 else place.c)

    def near(self, k):
        for s in range(2):
            copy = remote(
                self.part.at[2 * self.sequence(k) + s],
                self.nears.at[k + s],
                self.near_send.at[k + s],
                self.near_recv.at[k + s],
                self.place.peer(SIBLING),
            )
            copy.start()
            self.first[k + s] = copy

    def far(self, k):
        place = self.place
        for s in range(2):
            self.first[k - 1 + s].wait()
            self.nears[k - 1 + s] = (
                self.part[2 * self.sequence(k) + s].astype(f32)
                + self.nears[k - 1 + s].astype(f32)
            ).astype(bf16)
        for d in (1, 2) if k == 1 else (0,):
            relation = ACROSS[d]
            copy = remote(
                self.nears.at[k - 1 + (place.s + relation[0]) % 2],
                self.fars.at[d],
                self.far_send.at[d],
                self.far_recv.at[d],
                place.peer(relation),
            )
            copy.start()
            self.second.append(copy)

    def finish(self):
        for copy in self.second:
            copy.wait()

    def chunk(self, lanes):
        total = self.nears[2 + self.place.s, :, lanes].astype(f32)
        for d in range(3):
            total += self.fars[d, :, lanes].astype(f32)
        return total


class PlaneGather:
    def __init__(self, place, blocks, send, recv):
        self.place, self.blocks, self.sends, self.recvs = place, blocks, send, recv
        self.copies = [None] * 7

    def send(self, block, sem, relation):
        copy = remote(
            self.blocks.at[block],
            self.blocks.at[block],
            self.sends.at[sem],
            self.recvs.at[sem],
            self.place.peer(relation),
        )
        copy.start()
        self.copies[sem] = copy

    def start(self):
        mine = self.place.seat()
        for d in range(2):
            self.send(mine, d, ACROSS[d])
        self.send(mine, 3, SIBLING)

    def forward(self, d):
        self.copies[d].wait_recv()
        self.send(self.place.seat(ACROSS[d]), 4 + d, SIBLING)
        if d == 0:
            self.send(self.place.seat(), 2, ACROSS[2])

    def sequence(self, k):
        place = self.place
        row = place.r if k < 2 else (place.r + 1) % 2
        return row * 2 + (place.c if k % 2 == 0 else (place.c + 1) % 2)

    def arrive(self, k, forwarded=False):
        if k == 0:
            self.forward(0)
        elif k == 1:
            if not forwarded:
                self.forward(1)
            self.copies[3].wait_recv()
            self.copies[4].wait_recv()
        elif k == 2:
            self.forward(2)
        else:
            self.copies[5].wait_recv()
            self.copies[6].wait_recv()

    def finish(self):
        for copy in self.copies:
            copy.wait_send()


class ToOwners:
    def __init__(self, place, shares, landed, met, stage, send, recv, own):
        self.place, self.shares, self.landed, self.met, self.stage = place, shares, landed, met, stage
        self.send, self.recv, self.own_sem = send, recv, own
        self.line = place.grps == 4
        self.own = pltpu.make_async_copy(shares.at[place.g], landed.at[place.g], own)

    def copy(self, block, landing, sem, recv, target):
        place = self.place
        return remote(
            self.shares.at[block],
            landing,
            self.send.at[sem],
            self.recv.at[recv],
            (place.s, target, place.r, place.c),
        )

    def direct(self, g):
        targets = ((2, 1), (2, 0), (1, 3), (1, 2))[g]
        return [self.copy(t, self.landed.at[g], t, g, t) for t in targets]

    def meeting(self, g):
        far, inner = (3, 1) if g == 0 else (0, 2)
        return self.copy(far, self.met, far, inner, inner)

    def joined(self, g):
        far = 3 if g == 1 else 0
        return self.copy(far, self.landed.at[g], far, g, far)

    def start(self, waits=False):
        place, self.waits = self.place, waits
        self.own.start()
        if self.line:
            for g in range(4):

                @pl.when(place.g == g)
                def _():
                    if g in (0, 3):
                        self.meeting(g).start()
                    if g in (1, 2) or not waits:
                        for copy in self.direct(g):
                            copy.start()

        else:
            self.copies = [
                self.copy((place.g + dz) % place.grps, self.landed.at[place.g], dz, dz, (place.g + dz) % place.grps)
                for dz in range(1, place.grps)
            ]
            for copy in self.copies:
                copy.start()
        return self

    def proceed(self):
        if self.line:
            for g in (0, 3):

                @pl.when(self.place.g == g)
                def _():
                    self.meeting(g).wait_send()
                    for copy in self.direct(g):
                        copy.start()

    def join(self):
        if not self.line:
            return
        for g in (1, 2):

            @pl.when(self.place.g == g)
            def _():
                outer, far = (0, 3) if g == 1 else (3, 0)
                self.copy(far, self.met, far, g, outer).wait_recv()
                copy = pltpu.make_async_copy(self.met, self.stage, self.own_sem)
                self.own.wait()
                copy.start()
                copy.wait()
                if len(self.stage.shape) == 2:
                    self.shares[far] = (
                        self.shares[far].astype(f32) + self.stage[...].astype(f32)
                    ).astype(bf16)
                else:
                    for n in range(self.stage.shape[0]):
                        self.shares[far, n] = (
                            self.shares[far, n].astype(f32) + self.stage[n].astype(f32)
                        ).astype(bf16)
                self.joined(g).start()

        for g in (0, 3):

            @pl.when(self.place.g == g)
            def _():
                self.own.wait()

    def finish(self):
        if not self.line:
            self.own.wait()
            for copy in self.copies:
                copy.wait()
            return
        for g in range(4):

            @pl.when(self.place.g == g)
            def _():
                for j in ((1, 2), (0, 2, 3), (0, 1, 3), (1, 2))[g]:
                    self.copy(g, self.landed.at[j], j, j, j).wait_recv()
                for copy in self.direct(g):
                    copy.wait_send()
                if g in (1, 2):
                    self.joined(g).wait_send()
                elif not self.waits:
                    self.meeting(g).wait_send()

    def holds(self, j):
        g = self.place.g
        return (g % 3 != 0) | (j + g != 3) if self.line else True


class Exchange:
    def __init__(self, place, blocks, held, send, recv, own):
        mine = place.rank()
        kept = held.at[mine // QUAD, mine % QUAD] if len(held.shape) == 4 else held.at[mine]

        def block(t):
            return blocks.at[0, t // QUAD, t % QUAD] if len(blocks.shape) == 5 else blocks.at[t]

        self.copies = []
        for n, relation in enumerate(RELATIONS):
            copy = remote(
                block(place.rank(relation)),
                kept,
                send.at[n],
                recv.at[n],
                place.peer(relation),
            )
            copy.start()
            self.copies.append(copy)
        copy = pltpu.make_async_copy(block(mine), kept, own)
        copy.start()
        self.copies.append(copy)

    def finish(self):
        for copy in self.copies:
            copy.wait()


LANES = 512


def lanes_of(n, width=LANES):
    return pl.ds(pl.multiple_of(n * width, width), width)


def shares_of(seq, values, weight, part):
    rows = part.shape[1]

    @pl.loop(0, part.shape[2] // LANES)
    def _(n):
        product = dot(values[seq], weight[lanes_of(n)], 1, 1)
        part[2 * seq, :, lanes_of(n)] = product[:rows].astype(bf16)
        part[2 * seq + 1, :, lanes_of(n)] = product[rows:].astype(bf16)


def over_tokens(first, lanes, second, other):
    total = dot(first[0, :, lanes], second[0, :, other], 0, 0)
    for seq in range(1, first.shape[0]):
        total += dot(first[seq, :, lanes], second[seq, :, other], 0, 0)
    return total


def row_shares(first, second, shares):
    grps, seqs, rows, _ = shares.shape
    width = 256
    pieces = width // rows

    @pl.loop(0, first.shape[2] // width)
    def _(b):
        product = over_tokens(first, lanes_of(b, width), second, slice(None)).astype(bf16)
        for p in range(pieces):
            index = b * pieces + p
            shares[index % grps, index // grps] = product[p * rows : (p + 1) * rows]


def summed_rows(landed, holds, blocks):
    seqs, rows = landed.shape[1], blocks.shape[1]
    for seq in range(seqs):
        for quad in range(QUAD):
            block = slice(quad * rows, (quad + 1) * rows)
            total = jnp.zeros((rows, landed.shape[3]), f32)
            for j in range(landed.shape[0]):
                total += jnp.where(holds(j), landed[j, seq, block].astype(f32), 0.0)
            blocks[seq * QUAD + quad] = total.astype(bf16)


def back_kernel(
    grps,
    aligned,
    facts,
    gains,
    cosine,
    sine,
    residual,
    own_tokens,
    own_grad,
    dgu_h,
    up_h,
    down_share_h,
    second_h,
    first_h,
    out_h,
    qkv_h,
    q_h,
    k_h,
    v_h,
    o_h,
    input_grad,
    gains_sum,
    down_landed,
    out_landed,
    up_held,
    qkv_held,
    up_landed,
    qkv_landed,
    down_met,
    up_met,
    out_met,
    qkv_met,
    wide,
    up,
    acts,
    out_w,
    qkv,
    part,
    near,
    far,
    blocks,
    turned,
    down_share,
    up_share,
    out_share,
    qkv_share,
    up_sum,
    qkv_sum,
    stage_low,
    stage_wide,
    gain_part,
    gain_plane,
    gain_far,
    load,
    near_send,
    near_recv,
    far_send,
    far_recv,
    all_send,
    all_recv,
    z_send,
    z_recv,
    swap_send,
    swap_recv,
    gain_send,
    gain_recv,
    own_sem,
):
    place = Place(grps)
    rows = residual.shape[0]
    gain_part[...] = jnp.zeros_like(gain_part)
    count, full_rows, head_width = q_h.shape

    def fetch(src, dst, n):
        copy = pltpu.make_async_copy(src, dst, load.at[n])
        copy.start()
        return copy

    loads = [fetch(dgu_h, wide, 0), fetch(up_h, up, 1), fetch(down_share_h, down_share, 2)]
    later = fetch(second_h, acts, 3)
    weights = [fetch(out_h, out_w, 5), fetch(qkv_h, qkv, 6)]
    place.greet()
    for copy in loads:
        copy.wait()

    sums = (near_send, near_recv, far_send, far_recv)
    def to_owners(n, shares, landed, met, stage, waits=False):
        return ToOwners(
            place, shares, landed, met, stage, z_send.at[n], z_recv.at[n], own_sem.at[n]
        ).start(waits)

    def summed_over_plane(values, weight):
        total = PlaneSum(place, part, near, far, sums)
        for k in range(4):
            shares_of(total.sequence(k), values, weight, part)
            if k % 2 == 0:
                total.near(k)
            else:
                total.far(k)
        return total

    down_out = to_owners(0, down_share, down_landed, down_met, stage_low)
    second_sum = summed_over_plane(wide, up)
    later.wait()
    row_shares(acts, wide, up_share)
    up_out = to_owners(1, up_share, up_landed, up_met, stage_wide)
    fetch_first = fetch(first_h, acts, 3)
    down_out.join()
    heads = [
        fetch(ref, wide.at[:, :, n * head_width : (n + 1) * head_width], 7 + n)
        for n, ref in enumerate((q_h, k_h, v_h, o_h))
    ]

    second_sum.finish()
    mine = place.seat()
    inner = jnp.zeros((rows, 1), f32)
    squares = jnp.zeros((rows, 1), f32)
    for n in range(D // LANES):
        lanes = slice(n * LANES, (n + 1) * LANES)
        grad = second_sum.chunk(lanes)
        values = residual[:, lanes]
        inner += jnp.sum(grad * gains[1:2, lanes] * values, axis=-1, keepdims=True)
        squares += jnp.sum(values * values, axis=-1, keepdims=True)
    scale = lax.rsqrt(squares / D + NORM_EPSILON)
    inner = inner / D
    for n in range(D // LANES):
        lanes = slice(n * LANES, (n + 1) * LANES)
        grad, values = second_sum.chunk(lanes), residual[:, lanes]
        gain_part[1:2, lanes] = jnp.sum(grad * values * scale, axis=0, keepdims=True)
        total = own_grad[:, lanes].astype(f32) + scale * (
            grad * gains[1:2, lanes] - values * scale * scale * inner
        )
        input_grad[:, lanes] = total
        blocks[mine, :, lanes] = total.astype(bf16)

    gather = PlaneGather(place, blocks, all_send, all_recv)
    gather.start()
    for copy in weights + heads:
        copy.wait()

    lane = lax.broadcasted_iota(jnp.int32, (full_rows, head_width), 1)
    first_half = (lane % HEAD_DIM) < HEAD_DIM // 2

    for k in range(4):
        gather.arrive(k)
        seq = gather.sequence(k)
        grads = jnp.concatenate(
            [dot(blocks[2 * seq], out_w[...], 1, 1), dot(blocks[2 * seq + 1], out_w[...], 1, 1)],
            axis=0,
        ).astype(bf16)
        queries = wide[seq, :, 0:head_width]
        key_vectors = wide[seq, :, head_width : 2 * head_width]
        value_vectors = wide[seq, :, 2 * head_width : 3 * head_width]
        grad_q, grad_k, grad_v = attention_grads(
            facts[seq, 2:3, 0:1], queries, key_vectors, value_vectors, grads
        )
        for n, grad in enumerate((grad_q, grad_k)):
            values = (grad * HEAD_DIM**-0.5).astype(bf16).astype(f32)
            back = values * cosine[...] - swap_halves(values, first_half) * sine[...]
            turned[seq, :, n * head_width : (n + 1) * head_width] = back.astype(bf16)
        turned[seq, :, 2 * head_width : 3 * head_width] = grad_v.astype(bf16)
        if k == 1:
            up_out.join()

    gather.finish()
    out_rows = out_share.shape[1]

    @pl.loop(0, D // LANES)
    def _(n):
        lanes = lanes_of(n)
        total = jnp.zeros((head_width, LANES), f32)
        for seq in range(count):
            values = wide[seq, :, 3 * head_width : 4 * head_width].astype(f32)
            total += dot(values[:rows].astype(bf16), blocks[2 * seq, :, lanes], 0, 0)
            total += dot(values[rows:].astype(bf16), blocks[2 * seq + 1, :, lanes], 0, 0)
        total = total.astype(bf16)
        for j in range(out_share.shape[0]):
            out_share[j, :, lanes] = total[j * out_rows : (j + 1) * out_rows]

    if aligned:
        out_out = to_owners(3, out_share, out_landed, out_met, stage_low.at[:out_rows])
    else:
        out_out = pltpu.make_async_copy(out_share, out_landed, own_sem.at[3])
        out_out.start()

    fetch_first.wait()
    row_shares(acts, turned, qkv_share)
    triple = turned.shape[2]
    qkv_out = to_owners(2, qkv_share, qkv_landed, qkv_met, stage_wide.at[:, :, :triple], True)

    first_sum = summed_over_plane(turned, qkv)
    if aligned:
        out_out.join()
    qkv_out.proceed()
    qkv_out.join()
    first_sum.finish()
    inner = jnp.zeros((rows, 1), f32)
    squares = jnp.zeros((rows, 1), f32)
    for n in range(D // LANES):
        lanes = slice(n * LANES, (n + 1) * LANES)
        grad = first_sum.chunk(lanes)
        values = own_tokens[:, lanes].astype(f32)
        inner += jnp.sum(grad * gains[0:1, lanes] * values, axis=-1, keepdims=True)
        squares += jnp.sum(values * values, axis=-1, keepdims=True)
    scale = lax.rsqrt(squares / D + NORM_EPSILON)
    inner = inner / D
    for n in range(D // LANES):
        lanes = slice(n * LANES, (n + 1) * LANES)
        grad, values = first_sum.chunk(lanes), own_tokens[:, lanes].astype(f32)
        gain_part[0:1, lanes] = jnp.sum(grad * values * scale, axis=0, keepdims=True)
        input_grad[:, lanes] += scale * (
            grad * gains[0:1, lanes] - values * scale * scale * inner
        )

    gain_copies = []
    for n, relation in enumerate(RELATIONS):
        copy = remote(
            gain_part, gain_plane.at[n], gain_send.at[n], gain_recv.at[n], place.peer(relation)
        )
        copy.start()
        gain_copies.append(copy)

    up_out.finish()
    landed = pltpu.make_async_copy(up_landed, up_share, load.at[1])
    landed.start()
    for copy in gain_copies:
        copy.wait()
    total = gain_part[...]
    for n in range(len(RELATIONS)):
        total += gain_plane[n]
    gain_far[0] = total
    gain_copies = []
    for dz in range(1, grps):
        copy = remote(
            gain_far.at[0],
            gain_far.at[dz],
            gain_send.at[7 + dz],
            gain_recv.at[7 + dz],
            place.plane(dz),
        )
        copy.start()
        gain_copies.append(copy)
    landed.wait()
    summed_rows(up_share, up_out.holds, up_sum)
    up_swap = Exchange(place, up_sum, up_held, swap_send.at[0], swap_recv.at[0], own_sem.at[4])
    for copy in gain_copies:
        copy.wait()
    total = gain_far[0]
    for dz in range(1, grps):
        total += gain_far[dz]
    gains_sum[...] = total

    qkv_out.finish()
    landed = pltpu.make_async_copy(qkv_landed, qkv_share, load.at[6])
    landed.start()
    landed.wait()
    summed_rows(qkv_share, qkv_out.holds, qkv_sum)
    qkv_swap = Exchange(place, qkv_sum, qkv_held, swap_send.at[1], swap_recv.at[1], own_sem.at[5])
    if aligned:
        out_out.finish()
    else:
        out_out.wait()
    down_out.finish()
    up_swap.finish()
    qkv_swap.finish()


def backward(
    grps,
    aligned,
    facts,
    gains,
    tables,
    residual,
    own_tokens,
    own_grad,
    grad_both,
    up_local,
    down_share,
    second_norm,
    first_norm,
    out_local,
    qkv_local,
    heads,
):
    rows = residual.shape[0]
    count, full_rows, head_width = heads[0].shape
    seqs = full_rows // rows
    ranks = seqs * QUAD
    units = down_share.shape[1]
    both = grad_both.shape[2]
    quad_rows = D // (seqs * grps)
    shard = quad_rows // QUAD
    out_rows = head_width // grps if aligned else HEAD_DIM
    triple = 3 * head_width
    out_count = head_width // out_rows
    hbm = pl.BlockSpec(memory_space=pl.ANY)
    vmem = pl.BlockSpec(memory_space=pltpu.VMEM)
    shape = jax.ShapeDtypeStruct
    dma = pltpu.SemaphoreType.DMA
    return pl.pallas_call(
        lambda *refs: back_kernel(grps, aligned, *refs),
        in_specs=[vmem] * 7 + [hbm] * 11,
        out_specs=[vmem] * 2 + [hbm] * 10,
        out_shape=[
            shape((rows, D), f32),
            shape((8, D), f32),
            shape((grps, units, D), bf16),
            shape((out_count, out_rows, D), bf16),
            shape((ranks, shard, both), bf16),
            shape((ranks, shard, triple), bf16),
            shape((grps, seqs, quad_rows, both), bf16),
            shape((grps, seqs, quad_rows, triple), bf16),
            shape((units, D), bf16),
            shape((seqs, quad_rows, both), bf16),
            shape((out_rows, D), bf16),
            shape((seqs, quad_rows, triple), bf16),
        ],
        scratch_shapes=[
            pltpu.VMEM((count, full_rows, both), bf16),
            pltpu.VMEM((D, both), bf16),
            pltpu.VMEM((count, full_rows, D), bf16),
            pltpu.VMEM((head_width, D), bf16),
            pltpu.VMEM((D, triple), bf16),
            pltpu.VMEM((ranks, rows, D), bf16),
            pltpu.VMEM((4, rows, D), bf16),
            pltpu.VMEM((3, rows, D), bf16),
            pltpu.VMEM((ranks, rows, D), bf16),
            pltpu.VMEM((count, full_rows, triple), bf16),
            pltpu.VMEM((grps, units, D), bf16),
            pltpu.VMEM((grps, seqs, quad_rows, both), bf16),
            pltpu.VMEM((out_count, out_rows, D), bf16),
            pltpu.VMEM((grps, seqs, quad_rows, triple), bf16),
            pltpu.VMEM((ranks, shard, both), bf16),
            pltpu.VMEM((ranks, shard, triple), bf16),
            pltpu.VMEM((units, D), bf16),
            pltpu.VMEM((seqs, quad_rows, both), bf16),
            pltpu.VMEM((8, D), f32),
            pltpu.VMEM((7, 8, D), f32),
            pltpu.VMEM((grps, 8, D), f32),
            dma((11,)),
            dma((4,)),
            dma((4,)),
            dma((3,)),
            dma((3,)),
            dma((7,)),
            dma((7,)),
            dma((4, grps)),
            dma((4, grps)),
            dma((2, 7)),
            dma((2, 7)),
            dma((7 + grps,)),
            dma((7 + grps,)),
            dma((6,)),
        ],
        compiler_params=pltpu.CompilerParams(
            collective_id=0, has_side_effects=True, vmem_limit_bytes=VMEM_LIMIT
        ),
        cost_estimate=pl.CostEstimate(
            flops=30 * 10**9, bytes_accessed=60 * 2**20, transcendentals=2 * 10**6
        ),
        name="backward",
    )(
        facts,
        gains,
        *tables,
        residual,
        own_tokens,
        own_grad,
        grad_both,
        up_local,
        down_share,
        second_norm,
        first_norm,
        out_local,
        qkv_local,
        *heads,
    )


CHUNK = 1024


class FromOwners:
    def __init__(self, place, source, landed, landing, send, recv, own):
        self.place, self.source, self.send, self.recv = place, source, send, recv
        self.slot = lambda j: landing(landed, j)
        self.own = pltpu.make_async_copy(source, self.slot(place.g), own)
        self.line = place.grps == 4

    def copy(self, source, slot, sem, recv, target):
        place = self.place
        return remote(
            source, self.slot(slot), self.send.at[sem], self.recv.at[recv], (place.s, target, place.r, place.c)
        )

    def passed(self, g, j, target):
        source = self.source if j == g else self.slot(j)
        return self.copy(source, j, j + (4 if target > g else 0), j, target)

    def arrived(self, j):
        self.copy(self.source, j, j, j, j).wait_recv()

    def on_line(self, steps):
        for g in range(4):
            if steps[g]:

                @pl.when(self.place.g == g)
                def _():
                    for awaited, j, target in steps[g]:
                        if awaited is not None:
                            self.arrived(awaited)
                        self.passed(g, j, target).start()

    FIRST = (
        ((None, 0, 1),),
        ((None, 1, 0), (None, 1, 2)),
        ((None, 2, 3), (None, 2, 1)),
        ((None, 3, 2),),
    )
    SECOND = ((), ((2, 2, 0), (0, 0, 2)), ((1, 1, 3), (3, 3, 1)), ())
    THIRD = ((), ((3, 3, 0),), ((0, 0, 3),), ())

    def start(self):
        place = self.place
        self.own.start()
        if self.line:
            self.on_line(self.FIRST)
        else:
            self.copies = [
                self.copy(self.source, place.g, dz, dz, (place.g + dz) % place.grps)
                for dz in range(1, place.grps)
            ]
            for copy in self.copies:
                copy.start()

    def second(self):
        if self.line:
            self.on_line(self.SECOND)

    def third(self):
        if self.line:
            self.on_line(self.THIRD)

    def finish(self):
        self.own.wait()
        if self.line:
            for g in range(4):

                @pl.when(self.place.g == g)
                def _():
                    for j in range(4):
                        if g in (0, 3) and j != g:
                            self.arrived(j)
                    for steps in (self.FIRST, self.SECOND, self.THIRD):
                        for _, j, target in steps[g]:
                            self.passed(g, j, target).wait_send()

        else:
            for copy in self.copies:
                copy.wait()


def shares_from(seq, values, weight, part):
    rows = part.shape[1]

    @pl.loop(0, part.shape[2] // LANES)
    def _(n):
        product = dot(values[seq], weight[:, lanes_of(n)])
        part[2 * seq, :, lanes_of(n)] = product[:rows].astype(bf16)
        part[2 * seq + 1, :, lanes_of(n)] = product[rows:].astype(bf16)


def times_slices(values, weight, lanes):
    seqs, grps, quad, shard, _ = weight.shape
    depth = quad * shard
    total = None
    for n in range(seqs * grps):
        piece = weight[n // grps, n % grps, :, :, lanes]
        term = dot(values[:, n * depth : (n + 1) * depth], piece.reshape(depth, piece.shape[2]))
        total = term if total is None else total + term
    return total


def both_blocks(blocks, seq):
    return jnp.concatenate([blocks[2 * seq].astype(f32), blocks[2 * seq + 1].astype(f32)], axis=0)


def forward_kernel(
    grps,
    aligned,
    cosine,
    sine,
    own_facts,
    tokens_h,
    own_grad_h,
    qkv_own,
    up_own,
    out_own,
    down_own,
    residual,
    gains,
    facts,
    first_h,
    q_h,
    k_h,
    v_h,
    o_h,
    second_h,
    down_share_h,
    hidden_h,
    dgu_h,
    qkv_landed,
    up_landed,
    out_landed,
    down_landed,
    blocks,
    grad_blocks,
    norm,
    grad_seq,
    qkv_rank,
    up_rank,
    qkv,
    up,
    out_w,
    down,
    heads,
    part,
    near,
    far,
    both,
    hidden,
    dgu,
    all_facts,
    early,
    load,
    store,
    swap_send,
    swap_recv,
    near_send,
    near_recv,
    far_send,
    far_recv,
    all_send,
    all_recv,
    z_send,
    z_recv,
    fact_send,
    fact_recv,
    own_sem,
):
    place = Place(grps)
    count, full_rows, _ = norm.shape
    rows = residual.shape[0]
    head_width = heads.shape[3]
    mine, rank = place.seat(), place.rank()

    def fetch(src, dst, n):
        copy = pltpu.make_async_copy(src, dst, load.at[n])
        copy.start()
        return copy

    def keep(src, dst, n):
        copy = pltpu.make_async_copy(src, dst, store.at[n])
        copy.start()
        return copy

    shard = qkv_own.shape[0]
    units = down.shape[0] // grps
    seqs = qkv_landed.shape[0]
    slots = iter(range(20))

    def fetch_chunks(src):
        pieces = []
        for top in range(0, src.shape[0], shard):
            for left in range(0, src.shape[1], CHUNK):
                slot = next(slots)
                space = both.at[slot // 5, (slot % 5) * shard : (slot % 5 + 1) * shard]
                copy = pltpu.make_async_copy(
                    src.at[top : top + shard, left : left + CHUNK], space, early.at[slot]
                )
                copy.start()
                pieces.append((copy, space))
        return pieces

    def dealt(pieces, weight, lanes, parts):
        count = CHUNK // (QUAD * lanes)
        width = count * lanes
        each = len(pieces) // (parts * seqs)
        for n, (copy, space) in enumerate(pieces):
            copy.wait()
            values = space[...]
            seq = n // each % seqs
            first = (n // (each * seqs) * each + n % each) * width
            for q in range(QUAD):
                taken = [
                    values[:, (k * QUAD + q) * lanes : (k * QUAD + q + 1) * lanes] for k in range(count)
                ]
                weight[0, seq, q, :, first : first + width] = jnp.concatenate(taken, axis=1).astype(bf16)

    facts[rank] = own_facts[...]
    if aligned:
        out_pieces = fetch_chunks(out_own)
    qkv_pieces = fetch_chunks(qkv_own)
    up_pieces = fetch_chunks(up_own)
    down_pieces = fetch_chunks(down_own)
    own_blocks = [fetch(tokens_h, blocks.at[mine], 0), fetch(own_grad_h, grad_blocks.at[mine], 1)]

    def plane_rows(ref, j):
        return ref.at[:, j]

    def own_rows(ref, j):
        size = ref.shape[0] // grps
        return ref.at[pl.ds(pl.multiple_of(j * size, size), size)]

    def from_owners(n, source, landed, landing):
        return FromOwners(place, source, landed, landing, z_send.at[n], z_recv.at[n], own_sem.at[n])

    def stacked(pieces, weight):
        across = weight.shape[1] // CHUNK
        for n, (copy, space) in enumerate(pieces):
            copy.wait()
            top, left = n // across * shard, n % across * CHUNK
            weight[top : top + shard, left : left + CHUNK] = space[...].astype(bf16)

    down_z = from_owners(3, down.at[:units], down_landed, own_rows)
    if aligned:
        stacked(out_pieces, out_w)
        out_z = from_owners(2, out_w.at[:shard], out_landed, own_rows)
    place.greet()
    if aligned:
        out_z.start()
    dealt(qkv_pieces, qkv, HEAD_DIM, 3)
    qkv_swap = Exchange(place, qkv, qkv_rank, swap_send.at[0], swap_recv.at[0], own_sem.at[4])
    fact_copies = []
    for n, relation in enumerate(RELATIONS):
        copy = remote(own_facts, facts.at[rank], fact_send.at[n], fact_recv.at[n], place.peer(relation))
        copy.start()
        fact_copies.append(copy)
    if aligned:
        out_z.second()
    dealt(up_pieces, up, units, 2)
    stacked(down_pieces, down)
    for copy in own_blocks:
        copy.wait()
    if aligned:
        out_z.third()
    qkv_swap.finish()
    qkv_z = from_owners(0, qkv_rank, qkv_landed, plane_rows)
    up_z = from_owners(1, up_rank, up_landed, plane_rows)
    qkv_z.start()
    token_gather = PlaneGather(place, blocks, all_send.at[0], all_recv.at[0])
    token_gather.start()
    for copy in fact_copies:
        copy.wait()
    all_facts[place.g] = facts[...]
    fact_copies = []
    for dz in range(1, grps):
        copy = remote(
            facts,
            all_facts.at[place.g],
            fact_send.at[7 + dz],
            fact_recv.at[7 + dz],
            place.plane(dz),
        )
        copy.start()
        fact_copies.append(copy)
    for copy in fact_copies:
        copy.wait()
    width = D // (seqs * grps * QUAD)
    for n in range(seqs * grps):
        pieces = [all_facts[n % grps, (n // grps) * QUAD + q, :, :width] for q in range(QUAD)]
        gains[:, n * QUAD * width : (n + 1) * QUAD * width] = jnp.concatenate(pieces, axis=1)
    token_gather.forward(0)
    token_gather.forward(1)
    up_swap = Exchange(place, up, up_rank, swap_send.at[1], swap_recv.at[1], own_sem.at[5])
    qkv_z.second()
    token_gather.forward(2)
    token_gather.arrive(3)
    token_gather.copies[3].wait_recv()
    token_gather.copies[4].wait_recv()
    token_gather.finish()

    @pl.loop(0, count)
    def _(seq):
        values = both_blocks(blocks, seq)
        scale = lax.rsqrt(jnp.mean(values * values, axis=-1, keepdims=True) + NORM_EPSILON)
        norm[seq] = (values * scale * gains[0:1, :]).astype(bf16)

    stores = [keep(norm, first_h, 0)]
    grad_gather = PlaneGather(place, grad_blocks, all_send.at[1], all_recv.at[1])
    grad_gather.start()
    qkv_z.third()
    up_swap.finish()
    qkv_z.finish()
    up_z.start()
    fetch(qkv_landed, qkv, 2).wait()

    lane = lax.broadcasted_iota(jnp.int32, (full_rows, head_width), 1)
    first_half = (lane % HEAD_DIM) < HEAD_DIM // 2

    if aligned:
        out_z.finish()
        fetch(out_landed, out_w, 3).wait()
    else:
        fetch(out_own, out_w, 3).wait()

    plane_sum = PlaneSum(place, part, near, far, (near_send, near_recv, far_send, far_recv))
    mixed = heads.at[3]
    for k in range(4):
        seq = plane_sum.sequence(k)
        for n in range(3):
            lanes = slice(n * head_width, (n + 1) * head_width)
            values = times_slices(norm[seq], qkv, lanes)
            if n < 2:
                values = values * cosine[...] + swap_halves(values, first_half) * sine[...]
            heads[n, seq] = values.astype(bf16)
        heads[3, seq] = attention(facts[seq, 2:3, 0:1], heads[0, seq], heads[1, seq], heads[2, seq])
        shares_from(seq, mixed, out_w, part)
        if k % 2 == 0:
            plane_sum.near(k)
        else:
            plane_sum.far(k)
        if k == 0:
            grad_gather.forward(0)
            grad_gather.forward(1)
    grad_gather.forward(2)
    grad_gather.arrive(3)
    grad_gather.copies[3].wait_recv()
    grad_gather.copies[4].wait_recv()
    grad_gather.finish()
    stores += [keep(heads.at[n], ref, 1 + n) for n, ref in enumerate((q_h, k_h, v_h, o_h))]
    up_z.second()

    @pl.loop(0, count)
    def _(seq):
        grad_seq[seq] = both_blocks(grad_blocks, seq).astype(bf16)

    fetch(tokens_h, grad_blocks.at[mine], 4).wait()
    plane_sum.finish()
    squares = jnp.zeros((rows, 1), f32)
    for n in range(D // LANES):
        lanes = slice(n * LANES, (n + 1) * LANES)
        values = grad_blocks[mine, :, lanes].astype(f32) + plane_sum.chunk(lanes)
        residual[:, lanes] = values
        squares += jnp.sum(values * values, axis=-1, keepdims=True)
    scale = lax.rsqrt(squares / D + NORM_EPSILON)
    for n in range(D // LANES):
        lanes = slice(n * LANES, (n + 1) * LANES)
        blocks[mine, :, lanes] = (residual[:, lanes] * scale * gains[1:2, lanes]).astype(bf16)
    norm_gather = PlaneGather(place, blocks, all_send.at[2], all_recv.at[2])
    norm_gather.start()
    up_z.third()
    stores[0].wait()
    half = hidden.shape[2]
    for k in range(4):
        norm_gather.arrive(k, forwarded=k == 1)
        seq = norm_gather.sequence(k)
        norm[seq] = both_blocks(blocks, seq).astype(bf16)
        if k == 0:
            norm_gather.forward(1)
            up_z.finish()
            down_z.start()
            fetch(up_landed, up, 5).wait()
        elif k == 2:
            down_z.second()
        gate = times_slices(norm[seq], up, slice(0, half))
        above = times_slices(norm[seq], up, slice(half, 2 * half))
        both[seq, :, :half] = gate
        both[seq, :, half:] = above
        hidden[seq] = (gate * jax.nn.sigmoid(gate) * above).astype(bf16)
    norm_gather.finish()
    stores[0] = keep(norm, second_h, 5)
    down_z.third()
    stores.append(keep(hidden, hidden_h, 7))
    tall = min(256, half)
    slab = part.shape[1] // 128 * 128

    @pl.loop(0, half // tall)
    def _(b):
        for side in range(2):
            lanes = slice(side * D // 2, (side + 1) * D // 2)
            product = over_tokens(hidden, lanes_of(b, tall), grad_seq, lanes).astype(bf16)
            for p in range(tall // slab):
                part[b * (tall // slab) + p, :slab, lanes] = product[p * slab : (p + 1) * slab]

    stores.append(keep(part.at[: half // slab, :slab], down_share_h, 6))
    down_z.finish()
    fetch(down_landed, down, 6).wait()

    @pl.loop(0, count)
    def _(seq):
        grads = dot(grad_seq[seq], down[...], 1, 1)
        gate, above = both[seq, :, :half], both[seq, :, half:]
        sigmoid = jax.nn.sigmoid(gate)
        dgu[seq, :, :half] = (grads * above * sigmoid * (1.0 + gate * (1.0 - sigmoid))).astype(bf16)
        dgu[seq, :, half:] = (grads * (gate * sigmoid)).astype(bf16)

    stores.append(keep(dgu, dgu_h, 8))
    for copy in stores:
        copy.wait()


def forward(grps, aligned, tables, own_facts, tokens, own_grad, qkv_own, up_own, out_own, down_own):
    rows = tokens.shape[0]
    shard = qkv_own.shape[0]
    seqs = D // (shard * grps * QUAD)
    ranks = seqs * QUAD
    triple, both = qkv_own.shape[1] // ranks, up_own.shape[1] // ranks
    count, full_rows, head_width = QUAD, rows * seqs, triple // 3
    half = both // 2
    hbm = pl.BlockSpec(memory_space=pl.ANY)
    vmem = pl.BlockSpec(memory_space=pltpu.VMEM)
    shape = jax.ShapeDtypeStruct
    dma = pltpu.SemaphoreType.DMA
    by_heads = shape((count, full_rows, head_width), bf16)
    return pl.pallas_call(
        lambda *refs: forward_kernel(grps, aligned, *refs),
        in_specs=[vmem] * 3 + [hbm] * 6,
        out_specs=[vmem] * 3 + [hbm] * 13,
        out_shape=[
            shape((rows, D), f32),
            shape((8, D), f32),
            shape((ranks, 8, 128), f32),
            shape((count, full_rows, D), bf16),
            by_heads,
            by_heads,
            by_heads,
            by_heads,
            shape((count, full_rows, D), bf16),
            shape((half // 128, 128, D), bf16),
            shape((count, full_rows, half), bf16),
            shape((count, full_rows, both), bf16),
            shape((seqs, grps, QUAD, shard, triple), bf16),
            shape((seqs, grps, QUAD, shard, both), bf16),
            shape((head_width, D), bf16),
            shape((half, D), bf16),
        ],
        scratch_shapes=[
            pltpu.VMEM((ranks, rows, D), bf16),
            pltpu.VMEM((ranks, rows, D), bf16),
            pltpu.VMEM((count, full_rows, D), bf16),
            pltpu.VMEM((count, full_rows, D), bf16),
            pltpu.VMEM((seqs, QUAD, shard, triple), bf16),
            pltpu.VMEM((seqs, QUAD, shard, both), bf16),
            pltpu.VMEM((seqs, grps, QUAD, shard, triple), bf16),
            pltpu.VMEM((seqs, grps, QUAD, shard, both), bf16),
            pltpu.VMEM((head_width, D), bf16),
            pltpu.VMEM((half, D), bf16),
            pltpu.VMEM((4, count, full_rows, head_width), bf16),
            pltpu.VMEM((ranks, rows, D), bf16),
            pltpu.VMEM((4, rows, D), bf16),
            pltpu.VMEM((3, rows, D), bf16),
            pltpu.VMEM((count, full_rows, both), f32),
            pltpu.VMEM((count, full_rows, half), bf16),
            pltpu.VMEM((count, full_rows, both), bf16),
            pltpu.VMEM((grps, ranks, 8, 128), f32),
            dma((20,)),
            dma((7,)),
            dma((9,)),
            dma((2, 7)),
            dma((2, 7)),
            dma((4,)),
            dma((4,)),
            dma((3,)),
            dma((3,)),
            dma((3, 7)),
            dma((3, 7)),
            dma((4, 2 * grps)),
            dma((4, grps)),
            dma((7 + grps,)),
            dma((7 + grps,)),
            dma((6,)),
        ],
        compiler_params=pltpu.CompilerParams(
            collective_id=1, has_side_effects=True, vmem_limit_bytes=VMEM_LIMIT
        ),
        cost_estimate=pl.CostEstimate(
            flops=20 * 10**9, bytes_accessed=60 * 2**20, transcendentals=4 * 10**6
        ),
        name="forward",
    )(*tables, own_facts, tokens, own_grad, qkv_own, up_own, out_own, down_own)


ADAM_WIDTH = 1024


def adam_step(gradient, weight, moment, square, step_rate, outs):
    results = adam_update(weight[...], moment[...], square[...], gradient, step_rate)
    for out, result in zip(outs, results):
        out[...] = result
    outs[3][...] = results[0].astype(bf16)


def adam_ranks_kernel(lanes, step_rate, held, weight, moment, square, *outs):
    values = [held[0, q].astype(f32) for q in range(QUAD)]
    gradient = jnp.concatenate(
        [
            values[q][:, n * lanes : (n + 1) * lanes]
            for n in range(held.shape[3] // lanes)
            for q in range(QUAD)
        ],
        axis=1,
    )
    adam_step(gradient, weight, moment, square, step_rate, outs)


def adam_planes_kernel(step_rate, holds, landed, weight, moment, square, *outs):
    total = jnp.zeros(weight.shape, f32)
    for j in range(landed.shape[0]):
        total += jnp.where(holds[j] > 0, landed[j].astype(f32), 0.0)
    adam_step(total, weight, moment, square, step_rate, outs)


def adam_call(kernel, grads, grad_specs, state):
    rows, columns = state[0].shape
    block = pl.BlockSpec((rows, ADAM_WIDTH), lambda n: (0, n))
    like = jax.ShapeDtypeStruct((rows, columns), f32)
    return pl.pallas_call(
        kernel,
        grid=(columns // ADAM_WIDTH,),
        in_specs=grad_specs + [block] * 3,
        out_specs=[block] * 4,
        out_shape=[like] * 3 + [jax.ShapeDtypeStruct((rows, columns), bf16)],
        compiler_params=pltpu.CompilerParams(vmem_limit_bytes=32 * 2**20),
        cost_estimate=pl.CostEstimate(
            flops=rows * columns * 16, bytes_accessed=rows * columns * 28, transcendentals=rows * columns
        ),
        name="adam",
    )(*grads, *state)


def adam_from_ranks(held, seqs, parts, lanes, step_rate, *state):
    ranks, rows, columns = held.shape
    width = ADAM_WIDTH // QUAD
    blocks = columns // (parts * width)
    grouped = held.reshape(seqs, QUAD, rows, columns)
    spec = pl.BlockSpec(
        (1, QUAD, rows, width),
        lambda n: ((n // blocks) % seqs, 0, 0, n // (blocks * seqs) * blocks + n % blocks),
    )
    return adam_call(
        lambda *refs: adam_ranks_kernel(lanes, step_rate, *refs), (grouped,), [spec], state
    )


def adam_from_planes(landed, holds, step_rate, *state):
    planes, rows, _ = landed.shape
    specs = [
        pl.BlockSpec(memory_space=pltpu.SMEM),
        pl.BlockSpec((planes, rows, ADAM_WIDTH), lambda n: (0, 0, n)),
    ]
    return adam_call(
        lambda *refs: adam_planes_kernel(step_rate, *refs), (holds, landed), specs, state
    )


def seat_sum(partial):
    return lax.psum_scatter(
        partial.astype(bf16), SEATS, scatter_dimension=0, tiled=True
    ).astype(f32)


def on_device(
    tokens,
    cotangent,
    lengths,
    qkv_weight,
    qkv_moment,
    qkv_square,
    out_weight,
    out_moment,
    out_square,
    up_weight,
    up_moment,
    up_square,
    down_weight,
    down_moment,
    down_square,
    norm_gains,
    gains_moment,
    gains_square,
):
    seqs = lax.axis_size("seq")
    grps = lax.axis_size("grp")
    ranks = seqs * QUAD
    own_rows = tokens.shape[1]
    full_rows = own_rows * seqs
    all_rows = full_rows * QUAD
    heads_local = HEADS // ranks
    head_width = heads_local * HEAD_DIM
    units = down_weight.shape[0]
    aligned = out_weight.shape[0] == HEAD_DIM
    tables = rotate_table(full_rows, heads_local)

    positions = lax.axis_index("seq") * own_rows + jnp.arange(own_rows, dtype=jnp.int32)
    own_grad = jnp.where((positions < lengths[0])[:, None], cotangent[0], 0)
    own_gains = norm_gains.shape[1]
    own_facts = jnp.zeros((8, 128), f32)
    own_facts = own_facts.at[:2, :own_gains].set(norm_gains.astype(bf16).astype(f32))
    own_facts = own_facts.at[2].set(lengths[0].astype(f32))

    out_own = out_weight
    if not aligned:
        out_all = lax.all_gather(out_weight.astype(bf16), EVERY, axis=0, tiled=True)
        out_all = out_all.reshape(seqs, heads_local, QUAD, HEAD_DIM, D)
        seat = lax.axis_index("row") * 2 + lax.axis_index("core")
        out_own = lax.dynamic_index_in_dim(
            lax.dynamic_index_in_dim(out_all, lax.axis_index("seq"), 0, False), seat, 1, False
        ).reshape(head_width, D)
    (
        residual,
        gains,
        facts,
        first_norm,
        queries,
        key_vectors,
        value_vectors,
        attended,
        second_norm,
        down_share,
        hidden,
        grad_both,
        qkv_local,
        up_local,
        out_local,
        down_local,
    ) = forward(
        grps,
        aligned,
        tables,
        own_facts,
        tokens[0],
        own_grad,
        qkv_weight,
        up_weight,
        out_own,
        down_weight,
    )
    if not aligned:
        out_local = out_own
    (
        input_grad,
        gains_total,
        down_planes,
        out_planes,
        up_ranks,
        qkv_ranks,
        *_,
    ) = backward(
        grps,
        aligned,
        facts,
        gains,
        tables,
        residual,
        tokens[0],
        own_grad,
        grad_both,
        up_local.reshape(D, -1),
        down_share.reshape(grps, units, D),
        second_norm,
        first_norm,
        out_local,
        qkv_local.reshape(D, -1),
        (queries, key_vectors, value_vectors, attended),
    )
    block_output = (
        residual + seat_sum(dot(hidden.reshape(all_rows, -1), down_local))
    ).astype(bf16)
    if aligned:
        out_sum = out_planes
    else:
        placed_term = jnp.zeros((seqs, QUAD, heads_local, HEAD_DIM, D), bf16)
        placed_term = lax.dynamic_update_slice(
            placed_term,
            out_planes.reshape(1, 1, heads_local, HEAD_DIM, D),
            (lax.axis_index("seq"), seat, 0, 0, 0),
        )
        out_sum = lax.psum_scatter(
            placed_term.transpose(0, 2, 1, 3, 4).reshape(D, D),
            EVERY,
            scatter_dimension=0,
            tiled=True,
        )[None]
    device = ((lax.axis_index("seq") * grps + lax.axis_index("grp")) * 2 + lax.axis_index("row")) * 2
    gains_sum = lax.dynamic_slice(
        gains_total, (0, (device + lax.axis_index("core")) * own_gains), (2, own_gains)
    )
    planes = jnp.arange(grps)
    plane = lax.axis_index("grp")
    holds = ((planes + plane != 3) | (plane % 3 != 0) | (grps != 4)).astype(jnp.int32)
    qkv_new = adam_from_ranks(
        qkv_ranks, seqs, 3, HEAD_DIM, D ** (-0.5), qkv_weight, qkv_moment, qkv_square
    )
    up_new = adam_from_ranks(
        up_ranks, seqs, 2, units, D ** (-0.5), up_weight, up_moment, up_square
    )
    out_new = adam_from_planes(
        out_sum, holds, (D // 128) ** (-0.5), out_weight, out_moment, out_square
    )
    down_new = adam_from_planes(
        down_planes, holds, FF ** (-0.5), down_weight, down_moment, down_square
    )
    gains_new = adam_update(norm_gains, gains_moment, gains_square, gains_sum, 0.3)
    return (
        block_output[None],
        input_grad[None],
        *qkv_new,
        *out_new,
        *up_new,
        *down_new,
        *gains_new,
    )


def solution(mesh):
    seqs, rest = mesh.shape["seq"], mesh.shape["fsdp"]
    planes = Mesh(
        mesh.devices.reshape(seqs, rest // QUAD, 2, 2), ("seq", "grp", "row", "core")
    )
    rows = P(("grp", "row", "core"), "seq", None)
    shards = P(EVERY, None)
    gains = P(None, EVERY)
    return jax.shard_map(
        on_device,
        mesh=planes,
        in_specs=(rows, rows, P(("grp", "row", "core"))) + (shards,) * 12 + (gains,) * 3,
        out_specs=(rows, rows) + (shards,) * 16 + (gains,) * 3,
        check_vma=False,
    )
```

```python
import math

import jax
import jax.numpy as jnp
from jax import lax
from jax.experimental import pallas as pl
from jax.experimental.pallas import tpu as pltpu
from jax.sharding import Mesh, PartitionSpec as P

D = 2048
HEADS = 32
HEAD_DIM = 64
FF = 4096
WINDOW = 128
STEP = 5


NORM_EPSILON = 1e-05
MOMENT_DECAY = 0.5
WEIGHT_DECAY = 0.1
ADAM_EPSILON = 1e-08

SEATS = ("row", "core", "seq")
RANKS = ("seq", "row", "core")
EVERY = ("seq", "grp", "row", "core")
QUAD = 4
VMEM_LIMIT = 63 * 2**20

bf16 = jnp.bfloat16
f32 = jnp.float32


def rotate_table(length, copies):
    halves = HEAD_DIM // 2
    freqs = jnp.exp(-math.log(10000.0) * 2.0 * jnp.arange(halves).astype(f32) / HEAD_DIM)
    angles = jnp.arange(length, dtype=jnp.int32).astype(f32)[:, None] * freqs[None, :]
    cosine, sine = jnp.cos(angles), jnp.sin(angles)
    return (
        jnp.tile(jnp.concatenate([cosine, cosine], axis=1), (1, copies)),
        jnp.tile(jnp.concatenate([-sine, sine], axis=1), (1, copies)),
    )


def adam_update(weight, moment, square, gradient, step_rate):
    moment_new = MOMENT_DECAY * moment + (1.0 - MOMENT_DECAY) * gradient
    square_new = MOMENT_DECAY * square + (1.0 - MOMENT_DECAY) * gradient * gradient
    correction = 1.0 - MOMENT_DECAY**STEP
    update = moment_new / correction / (jnp.sqrt(square_new / correction) + ADAM_EPSILON)
    return (weight - step_rate * (update + WEIGHT_DECAY * weight), moment_new, square_new)


def dot(a, b, lhs=1, rhs=0):
    return lax.dot_general(a, b, (((lhs,), (rhs,)), ((), ())), preferred_element_type=f32)


def swap_halves(values, first):
    width = values.shape[1]
    half = HEAD_DIM // 2
    return jnp.where(
        first, pltpu.roll(values, width - half, 1), pltpu.roll(values, half, 1)
    )


def allowed_mask(rows, length):
    row = lax.broadcasted_iota(jnp.int32, (rows, rows), 0)
    col = lax.broadcasted_iota(jnp.int32, (rows, rows), 1)
    return (col <= row) & (row - col < WINDOW) & (col.astype(f32) < length)


def head_lanes(rows, width, head):
    lane = lax.broadcasted_iota(jnp.int32, (rows, width), 1)
    return (lane // HEAD_DIM) == head


def softmax_rows(queries, key_vectors, allowed):
    scores = jnp.where(allowed, dot(queries, key_vectors, 1, 1) * (HEAD_DIM**-0.5), -1e30)
    shifted = jnp.exp(scores - jnp.max(scores, axis=-1, keepdims=True))
    return shifted / jnp.sum(shifted, axis=-1, keepdims=True)


def attention(length, queries, key_vectors, value_vectors):
    rows, width = queries.shape
    allowed = allowed_mask(rows, length)
    total = jnp.zeros((rows, width), f32)
    for head in range(width // HEAD_DIM):
        mine = head_lanes(rows, width, head)
        weights = softmax_rows(jnp.where(mine, queries, 0), key_vectors, allowed)
        total += dot(weights.astype(bf16), jnp.where(mine, value_vectors, 0))
    return total.astype(bf16)


def attention_grads(length, queries, key_vectors, value_vectors, grads):
    rows, width = queries.shape
    allowed = allowed_mask(rows, length)
    grad_q = jnp.zeros((rows, width), f32)
    grad_k = jnp.zeros((rows, width), f32)
    grad_v = jnp.zeros((rows, width), f32)
    for head in range(width // HEAD_DIM):
        mine = head_lanes(rows, width, head)
        q_head = jnp.where(mine, queries, 0)
        g_head = jnp.where(mine, grads, 0)
        weights = softmax_rows(q_head, key_vectors, allowed)
        grad_p = dot(g_head, value_vectors, 1, 1)
        delta = jnp.sum(weights * grad_p, axis=-1, keepdims=True)
        grad_s = jnp.where(allowed, weights * (grad_p - delta), 0.0).astype(bf16)
        grad_q += dot(grad_s, jnp.where(mine, key_vectors, 0))
        grad_k += dot(grad_s, q_head, 0, 0)
        grad_v += dot(weights.astype(bf16), g_head, 0, 0)
    return grad_q, grad_k, grad_v


MESH = pl.DeviceIdType.MESH
RELATIONS = tuple((a, b, d) for a in range(2) for b in range(2) for d in range(2))[1:]


class Place:
    def __init__(self, grps):
        self.grps = grps
        self.s = lax.axis_index("seq")
        self.g = lax.axis_index("grp")
        self.r = lax.axis_index("row")
        self.c = lax.axis_index("core")

    def peer(self, relation):
        ds, dr, dc = relation
        return ((self.s + ds) % 2, self.g, (self.r + dr) % 2, (self.c + dc) % 2)

    def plane(self, dz):
        return (self.s, (self.g + dz) % self.grps, self.r, self.c)

    def rank(self, relation=(0, 0, 0)):
        s, _, r, c = self.peer(relation)
        return (s * 2 + r) * 2 + c

    def seat(self, relation=(0, 0, 0)):
        s, _, r, c = self.peer(relation)
        return (r * 2 + c) * 2 + s

    def corner(self, relation=(0, 0, 0)):
        s, _, r, _ = self.peer(relation)
        return r * 2 + s

    def greet(self):
        barrier = pltpu.get_barrier_semaphore()
        for relation in RELATIONS:
            pl.semaphore_signal(barrier, inc=1, device_id=self.peer(relation), device_id_type=MESH)
        for dz in range(1, self.grps):
            pl.semaphore_signal(barrier, inc=1, device_id=self.plane(dz), device_id_type=MESH)
        pl.semaphore_wait(barrier, len(RELATIONS) + self.grps - 1)


SIBLING = (0, 0, 1)
ACROSS = ((1, 0, 0), (0, 1, 0), (1, 1, 0))


def remote(src, dst, send_sem, recv_sem, device):
    return pltpu.make_async_remote_copy(
        src_ref=src,
        dst_ref=dst,
        send_sem=send_sem,
        recv_sem=recv_sem,
        device_id=device,
        device_id_type=MESH,
    )


class PlaneSum:
    def __init__(self, place, part, near, far, sems):
        self.place, self.part, self.nears, self.fars = place, part, near, far
        self.near_send, self.near_recv, self.far_send, self.far_recv = sems
        self.first, self.second = [None] * 4, []

    def sequence(self, k):
        place = self.place
        row = (place.r + 1) % 2 if k < 2 else place.r
        return row * 2 + ((place.c + 1) % 2 if k % 2 == 0 else place.c)

    def near(self, k):
        for s in range(2):
            copy = remote(
                self.part.at[2 * self.sequence(k) + s],
                self.nears.at[k + s],
                self.near_send.at[k + s],
                self.near_recv.at[k + s],
                self.place.peer(SIBLING),
            )
            copy.start()
            self.first[k + s] = copy

    def far(self, k):
        place = self.place
        for s in range(2):
            self.first[k - 1 + s].wait()
            self.nears[k - 1 + s] = (
                self.part[2 * self.sequence(k) + s].astype(f32)
                + self.nears[k - 1 + s].astype(f32)
            ).astype(bf16)
        for d in (1, 2) if k == 1 else (0,):
            relation = ACROSS[d]
            copy = remote(
                self.nears.at[k - 1 + (place.s + relation[0]) % 2],
                self.fars.at[d],
                self.far_send.at[d],
                self.far_recv.at[d],
                place.peer(relation),
            )
            copy.start()
            self.second.append(copy)

    def finish(self):
        for copy in self.second:
            copy.wait()

    def chunk(self, lanes):
        total = self.nears[2 + self.place.s, :, lanes].astype(f32)
        for d in range(3):
            total += self.fars[d, :, lanes].astype(f32)
        return total


class PlaneGather:
    def __init__(self, place, blocks, send, recv):
        self.place, self.blocks, self.sends, self.recvs = place, blocks, send, recv
        self.copies = [None] * 7

    def send(self, block, sem, relation):
        copy = remote(
            self.blocks.at[block],
            self.blocks.at[block],
            self.sends.at[sem],
            self.recvs.at[sem],
            self.place.peer(relation),
        )
        copy.start()
        self.copies[sem] = copy

    def start(self):
        mine = self.place.seat()
        for d in range(2):
            self.send(mine, d, ACROSS[d])
        self.send(mine, 3, SIBLING)

    def forward(self, d):
        self.copies[d].wait_recv()
        self.send(self.place.seat(ACROSS[d]), 4 + d, SIBLING)
        if d == 0:
            self.send(self.place.seat(), 2, ACROSS[2])

    def sequence(self, k):
        place = self.place
        row = place.r if k < 2 else (place.r + 1) % 2
        return row * 2 + (place.c if k % 2 == 0 else (place.c + 1) % 2)

    def arrive(self, k, forwarded=False):
        if k == 0:
            self.forward(0)
        elif k == 1:
            if not forwarded:
                self.forward(1)
            self.copies[3].wait_recv()
            self.copies[4].wait_recv()
        elif k == 2:
            self.forward(2)
        else:
            self.copies[5].wait_recv()
            self.copies[6].wait_recv()

    def finish(self):
        for copy in self.copies:
            copy.wait_send()


class ToOwners:
    def __init__(self, place, shares, landed, met, stage, send, recv, own):
        self.place, self.shares, self.landed, self.met, self.stage = place, shares, landed, met, stage
        self.send, self.recv, self.own_sem = send, recv, own
        self.line = place.grps == 4
        self.own = pltpu.make_async_copy(shares.at[place.g], landed.at[place.g], own)

    def copy(self, block, landing, sem, recv, target):
        place = self.place
        return remote(
            self.shares.at[block],
            landing,
            self.send.at[sem],
            self.recv.at[recv],
            (place.s, target, place.r, place.c),
        )

    def direct(self, g):
        targets = ((2, 1), (2, 0), (1, 3), (1, 2))[g]
        return [self.copy(t, self.landed.at[g], t, g, t) for t in targets]

    def meeting(self, g):
        far, inner = (3, 1) if g == 0 else (0, 2)
        return self.copy(far, self.met, far, inner, inner)

    def joined(self, g):
        far = 3 if g == 1 else 0
        return self.copy(far, self.landed.at[g], far, g, far)

    def start(self, waits=False):
        place, self.waits = self.place, waits
        self.own.start()
        if self.line:
            for g in range(4):

                @pl.when(place.g == g)
                def _():
                    if g in (0, 3):
                        self.meeting(g).start()
                    if g in (1, 2) or not waits:
                        for copy in self.direct(g):
                            copy.start()

        else:
            self.copies = [
                self.copy((place.g + dz) % place.grps, self.landed.at[place.g], dz, dz, (place.g + dz) % place.grps)
                for dz in range(1, place.grps)
            ]
            for copy in self.copies:
                copy.start()
        return self

    def proceed(self):
        if self.line:
            for g in (0, 3):

                @pl.when(self.place.g == g)
                def _():
                    self.meeting(g).wait_send()
                    for copy in self.direct(g):
                        copy.start()

    def join(self):
        if not self.line:
            return
        for g in (1, 2):

            @pl.when(self.place.g == g)
            def _():
                outer, far = (0, 3) if g == 1 else (3, 0)
                self.copy(far, self.met, far, g, outer).wait_recv()
                copy = pltpu.make_async_copy(self.met, self.stage, self.own_sem)
                self.own.wait()
                copy.start()
                copy.wait()
                if len(self.stage.shape) == 2:
                    self.shares[far] = (
                        self.shares[far].astype(f32) + self.stage[...].astype(f32)
                    ).astype(bf16)
                else:
                    for n in range(self.stage.shape[0]):
                        self.shares[far, n] = (
                            self.shares[far, n].astype(f32) + self.stage[n].astype(f32)
                        ).astype(bf16)
                self.joined(g).start()

        for g in (0, 3):

            @pl.when(self.place.g == g)
            def _():
                self.own.wait()

    def finish(self):
        if not self.line:
            self.own.wait()
            for copy in self.copies:
                copy.wait()
            return
        for g in range(4):

            @pl.when(self.place.g == g)
            def _():
                for j in ((1, 2), (0, 2, 3), (0, 1, 3), (1, 2))[g]:
                    self.copy(g, self.landed.at[j], j, j, j).wait_recv()
                for copy in self.direct(g):
                    copy.wait_send()
                if g in (1, 2):
                    self.joined(g).wait_send()
                elif not self.waits:
                    self.meeting(g).wait_send()

    def holds(self, j):
        g = self.place.g
        return (g % 3 != 0) | (j + g != 3) if self.line else True


class Exchange:
    def __init__(self, place, blocks, held, send, recv, own):
        mine = place.rank()
        kept = held.at[mine // QUAD, mine % QUAD] if len(held.shape) == 4 else held.at[mine]

        def block(t):
            return blocks.at[0, t // QUAD, t % QUAD] if len(blocks.shape) == 5 else blocks.at[t]

        self.copies = []
        for n, relation in enumerate(RELATIONS):
            copy = remote(
                block(place.rank(relation)),
                kept,
                send.at[n],
                recv.at[n],
                place.peer(relation),
            )
            copy.start()
            self.copies.append(copy)
        copy = pltpu.make_async_copy(block(mine), kept, own)
        copy.start()
        self.copies.append(copy)

    def finish(self):
        for copy in self.copies:
            copy.wait()


LANES = 512


def lanes_of(n, width=LANES):
    return pl.ds(pl.multiple_of(n * width, width), width)


def shares_of(seq, values, weight, part):
    rows = part.shape[1]

    @pl.loop(0, part.shape[2] // LANES)
    def _(n):
        product = dot(values[seq], weight[lanes_of(n)], 1, 1)
        part[2 * seq, :, lanes_of(n)] = product[:rows].astype(bf16)
        part[2 * seq + 1, :, lanes_of(n)] = product[rows:].astype(bf16)


def over_tokens(first, lanes, second, other):
    total = dot(first[0, :, lanes], second[0, :, other], 0, 0)
    for seq in range(1, first.shape[0]):
        total += dot(first[seq, :, lanes], second[seq, :, other], 0, 0)
    return total


def row_shares(first, second, shares):
    grps, seqs, rows, _ = shares.shape
    width = 256
    pieces = width // rows

    @pl.loop(0, first.shape[2] // width)
    def _(b):
        product = over_tokens(first, lanes_of(b, width), second, slice(None)).astype(bf16)
        for p in range(pieces):
            index = b * pieces + p
            shares[index % grps, index // grps] = product[p * rows : (p + 1) * rows]


def summed_rows(landed, holds, blocks):
    seqs, rows = landed.shape[1], blocks.shape[1]
    for seq in range(seqs):
        for quad in range(QUAD):
            block = slice(quad * rows, (quad + 1) * rows)
            total = jnp.zeros((rows, landed.shape[3]), f32)
            for j in range(landed.shape[0]):
                total += jnp.where(holds(j), landed[j, seq, block].astype(f32), 0.0)
            blocks[seq * QUAD + quad] = total.astype(bf16)


def back_kernel(
    grps,
    aligned,
    facts,
    gains,
    cosine,
    sine,
    residual,
    own_tokens,
    own_grad,
    dgu_h,
    up_h,
    down_share_h,
    second_h,
    first_h,
    out_h,
    qkv_h,
    q_h,
    k_h,
    v_h,
    o_h,
    hidden_h,
    down_h,
    input_grad,
    block_output,
    gains_sum,
    down_landed,
    out_landed,
    up_held,
    qkv_held,
    up_landed,
    qkv_landed,
    down_met,
    up_met,
    out_met,
    qkv_met,
    wide,
    up,
    acts,
    out_w,
    qkv,
    part,
    near,
    far,
    blocks,
    turned,
    down_share,
    up_share,
    out_share,
    qkv_share,
    up_sum,
    qkv_sum,
    stage_low,
    stage_wide,
    gain_part,
    gain_plane,
    gain_far,
    load,
    near_send,
    near_recv,
    far_send,
    far_recv,
    all_send,
    all_recv,
    z_send,
    z_recv,
    swap_send,
    swap_recv,
    gain_send,
    gain_recv,
    own_sem,
    near_free,
    far_free,
):
    place = Place(grps)
    rows = residual.shape[0]
    gain_part[...] = jnp.zeros_like(gain_part)
    count, full_rows, head_width = q_h.shape

    def fetch(src, dst, n):
        copy = pltpu.make_async_copy(src, dst, load.at[n])
        copy.start()
        return copy

    loads = [fetch(dgu_h, wide, 0), fetch(up_h, up, 1), fetch(down_share_h, down_share, 2)]
    later = fetch(second_h, acts, 3)
    weights = [fetch(out_h, out_w, 5), fetch(qkv_h, qkv, 6)]
    place.greet()
    for copy in loads:
        copy.wait()

    sums = (near_send, near_recv, far_send, far_recv)
    def to_owners(n, shares, landed, met, stage, waits=False):
        return ToOwners(
            place, shares, landed, met, stage, z_send.at[n], z_recv.at[n], own_sem.at[n]
        ).start(waits)

    def summed_over_plane(values, weight):
        total = PlaneSum(place, part, near, far, sums)
        for k in range(4):
            shares_of(total.sequence(k), values, weight, part)
            if k % 2 == 0:
                total.near(k)
            else:
                total.far(k)
        return total

    down_out = to_owners(0, down_share, down_landed, down_met, stage_low)
    second_sum = summed_over_plane(wide, up)
    later.wait()
    row_shares(acts, wide, up_share)
    up_out = to_owners(1, up_share, up_landed, up_met, stage_wide)
    fetch_first = fetch(first_h, acts, 3)
    down_out.join()
    heads = [
        fetch(ref, wide.at[:, :, n * head_width : (n + 1) * head_width], 7 + n)
        for n, ref in enumerate((q_h, k_h, v_h, o_h))
    ]

    half = hidden_h.shape[2]
    hidden = turned.at[:, :, :half]
    last = [fetch(hidden_h, hidden, 11)]
    for n in range(2):
        columns = slice(n * D // 2, (n + 1) * D // 2)
        last.append(fetch(down_h.at[:, columns], up.at[n * half : (n + 1) * half, : D // 2], 12 + n))
    second_sum.finish()
    mine = place.seat()
    inner = jnp.zeros((rows, 1), f32)
    squares = jnp.zeros((rows, 1), f32)
    for n in range(D // LANES):
        lanes = slice(n * LANES, (n + 1) * LANES)
        grad = second_sum.chunk(lanes)
        values = residual[:, lanes]
        inner += jnp.sum(grad * gains[1:2, lanes] * values, axis=-1, keepdims=True)
        squares += jnp.sum(values * values, axis=-1, keepdims=True)
    scale = lax.rsqrt(squares / D + NORM_EPSILON)
    inner = inner / D
    for n in range(D // LANES):
        lanes = slice(n * LANES, (n + 1) * LANES)
        grad, values = second_sum.chunk(lanes), residual[:, lanes]
        gain_part[1:2, lanes] = jnp.sum(grad * values * scale, axis=0, keepdims=True)
        total = own_grad[:, lanes].astype(f32) + scale * (
            grad * gains[1:2, lanes] - values * scale * scale * inner
        )
        input_grad[:, lanes] = total
        blocks[mine, :, lanes] = total.astype(bf16)

    gather = PlaneGather(place, blocks, all_send, all_recv)
    gather.start()
    for copy in weights + heads:
        copy.wait()

    lane = lax.broadcasted_iota(jnp.int32, (full_rows, head_width), 1)
    first_half = (lane % HEAD_DIM) < HEAD_DIM // 2

    for copy in last:
        copy.wait()

    @pl.loop(0, count)
    def _(seq):
        for n in range(D // LANES):
            top, left = n * LANES // (D // 2) * half, n * LANES % (D // 2)
            product = dot(hidden[seq], up[top : top + half, left : left + LANES])
            part[2 * seq, :, n * LANES : (n + 1) * LANES] = product[:rows].astype(bf16)
            part[2 * seq + 1, :, n * LANES : (n + 1) * LANES] = product[rows:].astype(bf16)

    last_sum = PlaneSum(place, part, near, far, sums)
    for k in range(4):
        gather.arrive(k)
        seq = gather.sequence(k)
        grads = jnp.concatenate(
            [dot(blocks[2 * seq], out_w[...], 1, 1), dot(blocks[2 * seq + 1], out_w[...], 1, 1)],
            axis=0,
        ).astype(bf16)
        queries = wide[seq, :, 0:head_width]
        key_vectors = wide[seq, :, head_width : 2 * head_width]
        value_vectors = wide[seq, :, 2 * head_width : 3 * head_width]
        grad_q, grad_k, grad_v = attention_grads(
            facts[seq, 2:3, 0:1], queries, key_vectors, value_vectors, grads
        )
        for n, grad in enumerate((grad_q, grad_k)):
            values = (grad * HEAD_DIM**-0.5).astype(bf16).astype(f32)
            back = values * cosine[...] - swap_halves(values, first_half) * sine[...]
            turned[seq, :, n * head_width : (n + 1) * head_width] = back.astype(bf16)
        turned[seq, :, 2 * head_width : 3 * head_width] = grad_v.astype(bf16)
        if k == 1:
            last_sum.near(0)
            last_sum.near(2)
            up_out.join()
        elif k == 2:
            last_sum.far(1)
            last_sum.far(3)

    gather.finish()
    out_rows = out_share.shape[1]

    @pl.loop(0, D // LANES)
    def _(n):
        lanes = lanes_of(n)
        total = jnp.zeros((head_width, LANES), f32)
        for seq in range(count):
            values = wide[seq, :, 3 * head_width : 4 * head_width].astype(f32)
            total += dot(values[:rows].astype(bf16), blocks[2 * seq, :, lanes], 0, 0)
            total += dot(values[rows:].astype(bf16), blocks[2 * seq + 1, :, lanes], 0, 0)
        total = total.astype(bf16)
        for j in range(out_share.shape[0]):
            out_share[j, :, lanes] = total[j * out_rows : (j + 1) * out_rows]

    if aligned:
        out_out = to_owners(3, out_share, out_landed, out_met, stage_low.at[:out_rows])
    else:
        out_out = pltpu.make_async_copy(out_share, out_landed, own_sem.at[3])
        out_out.start()

    fetch_first.wait()
    row_shares(acts, turned, qkv_share)
    triple = turned.shape[2]
    qkv_out = to_owners(2, qkv_share, qkv_landed, qkv_met, stage_wide.at[:, :, :triple], True)

    last_sum.finish()
    for n in range(D // LANES):
        lanes = slice(n * LANES, (n + 1) * LANES)
        block_output[:, lanes] = (residual[:, lanes] + last_sum.chunk(lanes)).astype(bf16)
    pl.semaphore_signal(near_free, inc=1, device_id=place.peer(SIBLING), device_id_type=MESH)
    for relation in ACROSS:
        pl.semaphore_signal(far_free, inc=1, device_id=place.peer(relation), device_id_type=MESH)
    pl.semaphore_wait(near_free, 1)
    pl.semaphore_wait(far_free, 3)
    first_sum = summed_over_plane(turned, qkv)
    if aligned:
        out_out.join()
    qkv_out.proceed()
    qkv_out.join()
    first_sum.finish()
    inner = jnp.zeros((rows, 1), f32)
    squares = jnp.zeros((rows, 1), f32)
    for n in range(D // LANES):
        lanes = slice(n * LANES, (n + 1) * LANES)
        grad = first_sum.chunk(lanes)
        values = own_tokens[:, lanes].astype(f32)
        inner += jnp.sum(grad * gains[0:1, lanes] * values, axis=-1, keepdims=True)
        squares += jnp.sum(values * values, axis=-1, keepdims=True)
    scale = lax.rsqrt(squares / D + NORM_EPSILON)
    inner = inner / D
    for n in range(D // LANES):
        lanes = slice(n * LANES, (n + 1) * LANES)
        grad, values = first_sum.chunk(lanes), own_tokens[:, lanes].astype(f32)
        gain_part[0:1, lanes] = jnp.sum(grad * values * scale, axis=0, keepdims=True)
        input_grad[:, lanes] += scale * (
            grad * gains[0:1, lanes] - values * scale * scale * inner
        )

    gain_copies = []
    for n, relation in enumerate(RELATIONS):
        copy = remote(
            gain_part, gain_plane.at[n], gain_send.at[n], gain_recv.at[n], place.peer(relation)
        )
        copy.start()
        gain_copies.append(copy)

    up_out.finish()
    landed = pltpu.make_async_copy(up_landed, up_share, load.at[1])
    landed.start()
    for copy in gain_copies:
        copy.wait()
    total = gain_part[...]
    for n in range(len(RELATIONS)):
        total += gain_plane[n]
    gain_far[0] = total
    gain_copies = []
    for dz in range(1, grps):
        copy = remote(
            gain_far.at[0],
            gain_far.at[dz],
            gain_send.at[7 + dz],
            gain_recv.at[7 + dz],
            place.plane(dz),
        )
        copy.start()
        gain_copies.append(copy)
    landed.wait()
    summed_rows(up_share, up_out.holds, up_sum)
    up_swap = Exchange(place, up_sum, up_held, swap_send.at[0], swap_recv.at[0], own_sem.at[4])
    for copy in gain_copies:
        copy.wait()
    total = gain_far[0]
    for dz in range(1, grps):
        total += gain_far[dz]
    gains_sum[...] = total

    qkv_out.finish()
    landed = pltpu.make_async_copy(qkv_landed, qkv_share, load.at[6])
    landed.start()
    landed.wait()
    summed_rows(qkv_share, qkv_out.holds, qkv_sum)
    qkv_swap = Exchange(place, qkv_sum, qkv_held, swap_send.at[1], swap_recv.at[1], own_sem.at[5])
    if aligned:
        out_out.finish()
    else:
        out_out.wait()
    down_out.finish()
    up_swap.finish()
    qkv_swap.finish()


def backward(
    grps,
    aligned,
    facts,
    gains,
    tables,
    residual,
    own_tokens,
    own_grad,
    grad_both,
    up_local,
    down_share,
    second_norm,
    first_norm,
    out_local,
    qkv_local,
    heads,
    hidden,
    down_local,
):
    rows = residual.shape[0]
    count, full_rows, head_width = heads[0].shape
    seqs = full_rows // rows
    ranks = seqs * QUAD
    units = down_share.shape[1]
    both = grad_both.shape[2]
    quad_rows = D // (seqs * grps)
    shard = quad_rows // QUAD
    out_rows = head_width // grps if aligned else HEAD_DIM
    triple = 3 * head_width
    out_count = head_width // out_rows
    hbm = pl.BlockSpec(memory_space=pl.ANY)
    vmem = pl.BlockSpec(memory_space=pltpu.VMEM)
    shape = jax.ShapeDtypeStruct
    dma = pltpu.SemaphoreType.DMA
    return pl.pallas_call(
        lambda *refs: back_kernel(grps, aligned, *refs),
        in_specs=[vmem] * 7 + [hbm] * 13,
        out_specs=[vmem] * 3 + [hbm] * 10,
        out_shape=[
            shape((rows, D), f32),
            shape((rows, D), bf16),
            shape((8, D), f32),
            shape((grps, units, D), bf16),
            shape((out_count, out_rows, D), bf16),
            shape((ranks, shard, both), bf16),
            shape((ranks, shard, triple), bf16),
            shape((grps, seqs, quad_rows, both), bf16),
            shape((grps, seqs, quad_rows, triple), bf16),
            shape((units, D), bf16),
            shape((seqs, quad_rows, both), bf16),
            shape((out_rows, D), bf16),
            shape((seqs, quad_rows, triple), bf16),
        ],
        scratch_shapes=[
            pltpu.VMEM((count, full_rows, both), bf16),
            pltpu.VMEM((D, both), bf16),
            pltpu.VMEM((count, full_rows, D), bf16),
            pltpu.VMEM((head_width, D), bf16),
            pltpu.VMEM((D, triple), bf16),
            pltpu.VMEM((ranks, rows, D), bf16),
            pltpu.VMEM((4, rows, D), bf16),
            pltpu.VMEM((3, rows, D), bf16),
            pltpu.VMEM((ranks, rows, D), bf16),
            pltpu.VMEM((count, full_rows, triple), bf16),
            pltpu.VMEM((grps, units, D), bf16),
            pltpu.VMEM((grps, seqs, quad_rows, both), bf16),
            pltpu.VMEM((out_count, out_rows, D), bf16),
            pltpu.VMEM((grps, seqs, quad_rows, triple), bf16),
            pltpu.VMEM((ranks, shard, both), bf16),
            pltpu.VMEM((ranks, shard, triple), bf16),
            pltpu.VMEM((units, D), bf16),
            pltpu.VMEM((seqs, quad_rows, both), bf16),
            pltpu.VMEM((8, D), f32),
            pltpu.VMEM((7, 8, D), f32),
            pltpu.VMEM((grps, 8, D), f32),
            dma((14,)),
            dma((4,)),
            dma((4,)),
            dma((3,)),
            dma((3,)),
            dma((7,)),
            dma((7,)),
            dma((4, grps)),
            dma((4, grps)),
            dma((2, 7)),
            dma((2, 7)),
            dma((7 + grps,)),
            dma((7 + grps,)),
            dma((6,)),
            pltpu.SemaphoreType.REGULAR,
            pltpu.SemaphoreType.REGULAR,
        ],
        compiler_params=pltpu.CompilerParams(
            collective_id=0, has_side_effects=True, vmem_limit_bytes=VMEM_LIMIT
        ),
        cost_estimate=pl.CostEstimate(
            flops=30 * 10**9, bytes_accessed=60 * 2**20, transcendentals=2 * 10**6
        ),
        name="backward",
    )(
        facts,
        gains,
        *tables,
        residual,
        own_tokens,
        own_grad,
        grad_both,
        up_local,
        down_share,
        second_norm,
        first_norm,
        out_local,
        qkv_local,
        *heads,
        hidden,
        down_local,
    )


CHUNK = 1024


class FromOwners:
    def __init__(self, place, source, landed, landing, send, recv, own):
        self.place, self.source, self.send, self.recv = place, source, send, recv
        self.slot = lambda j: landing(landed, j)
        self.own = pltpu.make_async_copy(source, self.slot(place.g), own)
        self.line = place.grps == 4

    def copy(self, source, slot, sem, recv, target):
        place = self.place
        return remote(
            source, self.slot(slot), self.send.at[sem], self.recv.at[recv], (place.s, target, place.r, place.c)
        )

    def passed(self, g, j, target):
        source = self.source if j == g else self.slot(j)
        return self.copy(source, j, j + (4 if target > g else 0), j, target)

    def arrived(self, j):
        self.copy(self.source, j, j, j, j).wait_recv()

    def on_line(self, steps):
        for g in range(4):
            if steps[g]:

                @pl.when(self.place.g == g)
                def _():
                    for awaited, j, target in steps[g]:
                        if awaited is not None:
                            self.arrived(awaited)
                        self.passed(g, j, target).start()

    FIRST = (
        ((None, 0, 1),),
        ((None, 1, 0), (None, 1, 2)),
        ((None, 2, 3), (None, 2, 1)),
        ((None, 3, 2),),
    )
    SECOND = ((), ((2, 2, 0), (0, 0, 2)), ((1, 1, 3), (3, 3, 1)), ())
    THIRD = ((), ((3, 3, 0),), ((0, 0, 3),), ())

    def start(self):
        place = self.place
        self.own.start()
        if self.line:
            self.on_line(self.FIRST)
        else:
            self.copies = [
                self.copy(self.source, place.g, dz, dz, (place.g + dz) % place.grps)
                for dz in range(1, place.grps)
            ]
            for copy in self.copies:
                copy.start()

    def second(self):
        if self.line:
            self.on_line(self.SECOND)

    def third(self):
        if self.line:
            self.on_line(self.THIRD)

    def finish(self):
        self.own.wait()
        if self.line:
            for g in range(4):

                @pl.when(self.place.g == g)
                def _():
                    for j in range(4):
                        if g in (0, 3) and j != g:
                            self.arrived(j)
                    for steps in (self.FIRST, self.SECOND, self.THIRD):
                        for _, j, target in steps[g]:
                            self.passed(g, j, target).wait_send()

        else:
            for copy in self.copies:
                copy.wait()


def shares_from(seq, values, weight, part):
    rows = part.shape[1]

    @pl.loop(0, part.shape[2] // LANES)
    def _(n):
        product = dot(values[seq], weight[:, lanes_of(n)])
        part[2 * seq, :, lanes_of(n)] = product[:rows].astype(bf16)
        part[2 * seq + 1, :, lanes_of(n)] = product[rows:].astype(bf16)


def times_slices(values, weight, lanes):
    seqs, grps, quad, shard, _ = weight.shape
    depth = quad * shard
    total = None
    for n in range(seqs * grps):
        piece = weight[n // grps, n % grps, :, :, lanes]
        term = dot(values[:, n * depth : (n + 1) * depth], piece.reshape(depth, piece.shape[2]))
        total = term if total is None else total + term
    return total


def both_blocks(blocks, seq):
    return jnp.concatenate([blocks[2 * seq].astype(f32), blocks[2 * seq + 1].astype(f32)], axis=0)


def forward_kernel(
    grps,
    aligned,
    cosine,
    sine,
    own_facts,
    tokens_h,
    own_grad_h,
    qkv_own,
    up_own,
    out_own,
    down_own,
    residual,
    gains,
    facts,
    first_h,
    q_h,
    k_h,
    v_h,
    o_h,
    second_h,
    down_share_h,
    hidden_h,
    dgu_h,
    qkv_landed,
    up_landed,
    out_landed,
    down_landed,
    blocks,
    grad_blocks,
    norm,
    grad_seq,
    qkv_rank,
    up_rank,
    qkv,
    up,
    out_w,
    down,
    heads,
    part,
    near,
    far,
    both,
    hidden,
    dgu,
    all_facts,
    early,
    load,
    store,
    swap_send,
    swap_recv,
    near_send,
    near_recv,
    far_send,
    far_recv,
    all_send,
    all_recv,
    z_send,
    z_recv,
    fact_send,
    fact_recv,
    own_sem,
):
    place = Place(grps)
    count, full_rows, _ = norm.shape
    rows = residual.shape[0]
    head_width = heads.shape[3]
    mine, rank = place.seat(), place.rank()

    def fetch(src, dst, n):
        copy = pltpu.make_async_copy(src, dst, load.at[n])
        copy.start()
        return copy

    def keep(src, dst, n):
        copy = pltpu.make_async_copy(src, dst, store.at[n])
        copy.start()
        return copy

    shard = qkv_own.shape[0]
    units = down.shape[0] // grps
    seqs = qkv_landed.shape[0]
    slots = iter(range(20))

    def fetch_chunks(src):
        pieces = []
        for top in range(0, src.shape[0], shard):
            for left in range(0, src.shape[1], CHUNK):
                slot = next(slots)
                space = both.at[slot // 5, (slot % 5) * shard : (slot % 5 + 1) * shard]
                copy = pltpu.make_async_copy(
                    src.at[top : top + shard, left : left + CHUNK], space, early.at[slot]
                )
                copy.start()
                pieces.append((copy, space))
        return pieces

    def dealt(pieces, weight, lanes, parts):
        count = CHUNK // (QUAD * lanes)
        width = count * lanes
        each = len(pieces) // (parts * seqs)
        for n, (copy, space) in enumerate(pieces):
            copy.wait()
            values = space[...]
            seq = n // each % seqs
            first = (n // (each * seqs) * each + n % each) * width
            for q in range(QUAD):
                taken = [
                    values[:, (k * QUAD + q) * lanes : (k * QUAD + q + 1) * lanes] for k in range(count)
                ]
                weight[0, seq, q, :, first : first + width] = jnp.concatenate(taken, axis=1).astype(bf16)

    facts[rank] = own_facts[...]
    if aligned:
        out_pieces = fetch_chunks(out_own)
    qkv_pieces = fetch_chunks(qkv_own)
    up_pieces = fetch_chunks(up_own)
    down_pieces = fetch_chunks(down_own)
    own_blocks = [fetch(tokens_h, blocks.at[mine], 0), fetch(own_grad_h, grad_blocks.at[mine], 1)]

    def plane_rows(ref, j):
        return ref.at[:, j]

    def own_rows(ref, j):
        size = ref.shape[0] // grps
        return ref.at[pl.ds(pl.multiple_of(j * size, size), size)]

    def from_owners(n, source, landed, landing):
        return FromOwners(place, source, landed, landing, z_send.at[n], z_recv.at[n], own_sem.at[n])

    def stacked(pieces, weight):
        across = weight.shape[1] // CHUNK
        for n, (copy, space) in enumerate(pieces):
            copy.wait()
            top, left = n // across * shard, n % across * CHUNK
            weight[top : top + shard, left : left + CHUNK] = space[...].astype(bf16)

    down_z = from_owners(3, down.at[:units], down_landed, own_rows)
    if aligned:
        stacked(out_pieces, out_w)
        out_z = from_owners(2, out_w.at[:shard], out_landed, own_rows)
    place.greet()
    if aligned:
        out_z.start()
    dealt(qkv_pieces, qkv, HEAD_DIM, 3)
    qkv_swap = Exchange(place, qkv, qkv_rank, swap_send.at[0], swap_recv.at[0], own_sem.at[4])
    fact_copies = []
    for n, relation in enumerate(RELATIONS):
        copy = remote(own_facts, facts.at[rank], fact_send.at[n], fact_recv.at[n], place.peer(relation))
        copy.start()
        fact_copies.append(copy)
    if aligned:
        out_z.second()
    dealt(up_pieces, up, units, 2)
    stacked(down_pieces, down)
    for copy in own_blocks:
        copy.wait()
    if aligned:
        out_z.third()
    qkv_swap.finish()
    qkv_z = from_owners(0, qkv_rank, qkv_landed, plane_rows)
    up_z = from_owners(1, up_rank, up_landed, plane_rows)
    qkv_z.start()
    token_gather = PlaneGather(place, blocks, all_send.at[0], all_recv.at[0])
    token_gather.start()
    for copy in fact_copies:
        copy.wait()
    all_facts[place.g] = facts[...]
    fact_copies = []
    for dz in range(1, grps):
        copy = remote(
            facts,
            all_facts.at[place.g],
            fact_send.at[7 + dz],
            fact_recv.at[7 + dz],
            place.plane(dz),
        )
        copy.start()
        fact_copies.append(copy)
    for copy in fact_copies:
        copy.wait()
    width = D // (seqs * grps * QUAD)
    for n in range(seqs * grps):
        pieces = [all_facts[n % grps, (n // grps) * QUAD + q, :, :width] for q in range(QUAD)]
        gains[:, n * QUAD * width : (n + 1) * QUAD * width] = jnp.concatenate(pieces, axis=1)
    token_gather.forward(0)
    token_gather.forward(1)
    up_swap = Exchange(place, up, up_rank, swap_send.at[1], swap_recv.at[1], own_sem.at[5])
    qkv_z.second()
    token_gather.forward(2)
    token_gather.arrive(3)
    token_gather.copies[3].wait_recv()
    token_gather.copies[4].wait_recv()
    token_gather.finish()

    @pl.loop(0, count)
    def _(seq):
        values = both_blocks(blocks, seq)
        scale = lax.rsqrt(jnp.mean(values * values, axis=-1, keepdims=True) + NORM_EPSILON)
        norm[seq] = (values * scale * gains[0:1, :]).astype(bf16)

    stores = [keep(norm, first_h, 0)]
    grad_gather = PlaneGather(place, grad_blocks, all_send.at[1], all_recv.at[1])
    grad_gather.start()
    qkv_z.third()
    up_swap.finish()
    qkv_z.finish()
    up_z.start()
    fetch(qkv_landed, qkv, 2).wait()

    lane = lax.broadcasted_iota(jnp.int32, (full_rows, head_width), 1)
    first_half = (lane % HEAD_DIM) < HEAD_DIM // 2

    if aligned:
        out_z.finish()
        fetch(out_landed, out_w, 3).wait()
    else:
        fetch(out_own, out_w, 3).wait()

    plane_sum = PlaneSum(place, part, near, far, (near_send, near_recv, far_send, far_recv))
    mixed = heads.at[3]
    for k in range(4):
        seq = plane_sum.sequence(k)
        for n in range(3):
            lanes = slice(n * head_width, (n + 1) * head_width)
            values = times_slices(norm[seq], qkv, lanes)
            if n < 2:
                values = values * cosine[...] + swap_halves(values, first_half) * sine[...]
            heads[n, seq] = values.astype(bf16)
        heads[3, seq] = attention(facts[seq, 2:3, 0:1], heads[0, seq], heads[1, seq], heads[2, seq])
        shares_from(seq, mixed, out_w, part)
        if k % 2 == 0:
            plane_sum.near(k)
        else:
            plane_sum.far(k)
        if k == 0:
            grad_gather.forward(0)
            grad_gather.forward(1)
    grad_gather.forward(2)
    grad_gather.arrive(3)
    grad_gather.copies[3].wait_recv()
    grad_gather.copies[4].wait_recv()
    grad_gather.finish()
    stores += [keep(heads.at[n], ref, 1 + n) for n, ref in enumerate((q_h, k_h, v_h, o_h))]
    up_z.second()

    @pl.loop(0, count)
    def _(seq):
        grad_seq[seq] = both_blocks(grad_blocks, seq).astype(bf16)

    fetch(tokens_h, grad_blocks.at[mine], 4).wait()
    plane_sum.finish()
    squares = jnp.zeros((rows, 1), f32)
    for n in range(D // LANES):
        lanes = slice(n * LANES, (n + 1) * LANES)
        values = grad_blocks[mine, :, lanes].astype(f32) + plane_sum.chunk(lanes)
        residual[:, lanes] = values
        squares += jnp.sum(values * values, axis=-1, keepdims=True)
    scale = lax.rsqrt(squares / D + NORM_EPSILON)
    for n in range(D // LANES):
        lanes = slice(n * LANES, (n + 1) * LANES)
        blocks[mine, :, lanes] = (residual[:, lanes] * scale * gains[1:2, lanes]).astype(bf16)
    norm_gather = PlaneGather(place, blocks, all_send.at[2], all_recv.at[2])
    norm_gather.start()
    up_z.third()
    stores[0].wait()
    half = hidden.shape[2]
    for k in range(4):
        norm_gather.arrive(k, forwarded=k == 1)
        seq = norm_gather.sequence(k)
        norm[seq] = both_blocks(blocks, seq).astype(bf16)
        if k == 0:
            norm_gather.forward(1)
            up_z.finish()
            down_z.start()
            fetch(up_landed, up, 5).wait()
        elif k == 2:
            down_z.second()
        gate = times_slices(norm[seq], up, slice(0, half))
        above = times_slices(norm[seq], up, slice(half, 2 * half))
        both[seq, :, :half] = gate
        both[seq, :, half:] = above
        hidden[seq] = (gate * jax.nn.sigmoid(gate) * above).astype(bf16)
    norm_gather.finish()
    stores[0] = keep(norm, second_h, 5)
    down_z.third()
    stores.append(keep(hidden, hidden_h, 7))
    tall = min(256, half)
    slab = part.shape[1] // 128 * 128

    @pl.loop(0, half // tall)
    def _(b):
        for side in range(2):
            lanes = slice(side * D // 2, (side + 1) * D // 2)
            product = over_tokens(hidden, lanes_of(b, tall), grad_seq, lanes).astype(bf16)
            for p in range(tall // slab):
                part[b * (tall // slab) + p, :slab, lanes] = product[p * slab : (p + 1) * slab]

    stores.append(keep(part.at[: half // slab, :slab], down_share_h, 6))
    down_z.finish()
    fetch(down_landed, down, 6).wait()

    @pl.loop(0, count)
    def _(seq):
        grads = dot(grad_seq[seq], down[...], 1, 1)
        gate, above = both[seq, :, :half], both[seq, :, half:]
        sigmoid = jax.nn.sigmoid(gate)
        dgu[seq, :, :half] = (grads * above * sigmoid * (1.0 + gate * (1.0 - sigmoid))).astype(bf16)
        dgu[seq, :, half:] = (grads * (gate * sigmoid)).astype(bf16)

    stores.append(keep(dgu, dgu_h, 8))
    for copy in stores:
        copy.wait()


def forward(grps, aligned, tables, own_facts, tokens, own_grad, qkv_own, up_own, out_own, down_own):
    rows = tokens.shape[0]
    shard = qkv_own.shape[0]
    seqs = D // (shard * grps * QUAD)
    ranks = seqs * QUAD
    triple, both = qkv_own.shape[1] // ranks, up_own.shape[1] // ranks
    count, full_rows, head_width = QUAD, rows * seqs, triple // 3
    half = both // 2
    hbm = pl.BlockSpec(memory_space=pl.ANY)
    vmem = pl.BlockSpec(memory_space=pltpu.VMEM)
    shape = jax.ShapeDtypeStruct
    dma = pltpu.SemaphoreType.DMA
    by_heads = shape((count, full_rows, head_width), bf16)
    return pl.pallas_call(
        lambda *refs: forward_kernel(grps, aligned, *refs),
        in_specs=[vmem] * 3 + [hbm] * 6,
        out_specs=[vmem] * 3 + [hbm] * 13,
        out_shape=[
            shape((rows, D), f32),
            shape((8, D), f32),
            shape((ranks, 8, 128), f32),
            shape((count, full_rows, D), bf16),
            by_heads,
            by_heads,
            by_heads,
            by_heads,
            shape((count, full_rows, D), bf16),
            shape((half // 128, 128, D), bf16),
            shape((count, full_rows, half), bf16),
            shape((count, full_rows, both), bf16),
            shape((seqs, grps, QUAD, shard, triple), bf16),
            shape((seqs, grps, QUAD, shard, both), bf16),
            shape((head_width, D), bf16),
            shape((half, D), bf16),
        ],
        scratch_shapes=[
            pltpu.VMEM((ranks, rows, D), bf16),
            pltpu.VMEM((ranks, rows, D), bf16),
            pltpu.VMEM((count, full_rows, D), bf16),
            pltpu.VMEM((count, full_rows, D), bf16),
            pltpu.VMEM((seqs, QUAD, shard, triple), bf16),
            pltpu.VMEM((seqs, QUAD, shard, both), bf16),
            pltpu.VMEM((seqs, grps, QUAD, shard, triple), bf16),
            pltpu.VMEM((seqs, grps, QUAD, shard, both), bf16),
            pltpu.VMEM((head_width, D), bf16),
            pltpu.VMEM((half, D), bf16),
            pltpu.VMEM((4, count, full_rows, head_width), bf16),
            pltpu.VMEM((ranks, rows, D), bf16),
            pltpu.VMEM((4, rows, D), bf16),
            pltpu.VMEM((3, rows, D), bf16),
            pltpu.VMEM((count, full_rows, both), f32),
            pltpu.VMEM((count, full_rows, half), bf16),
            pltpu.VMEM((count, full_rows, both), bf16),
            pltpu.VMEM((grps, ranks, 8, 128), f32),
            dma((20,)),
            dma((7,)),
            dma((9,)),
            dma((2, 7)),
            dma((2, 7)),
            dma((4,)),
            dma((4,)),
            dma((3,)),
            dma((3,)),
            dma((3, 7)),
            dma((3, 7)),
            dma((4, 2 * grps)),
            dma((4, grps)),
            dma((7 + grps,)),
            dma((7 + grps,)),
            dma((6,)),
        ],
        compiler_params=pltpu.CompilerParams(
            collective_id=1, has_side_effects=True, vmem_limit_bytes=VMEM_LIMIT
        ),
        cost_estimate=pl.CostEstimate(
            flops=20 * 10**9, bytes_accessed=60 * 2**20, transcendentals=4 * 10**6
        ),
        name="forward",
    )(*tables, own_facts, tokens, own_grad, qkv_own, up_own, out_own, down_own)


DEPTH = 3


def adam_kernel(grps, holds, down_planes, out_planes, up_ranks, qkv_ranks, gains_sum, gains, gains_m, gains_v, *refs):
    states, outs = refs[:12], refs[12:28]
    gains_outs = refs[28:31]
    state, planes, ranks, fresh, copied, in_sem, out_sem = refs[31:]
    rows = state.shape[2]
    units = CHUNK // QUAD
    pieces = []
    for n, (name, rate) in enumerate(
        (("down", FF ** (-0.5)), ("out", (D // 128) ** (-0.5)), ("up", D ** (-0.5)), ("qkv", D ** (-0.5)))
    ):
        arrays = states[3 * n : 3 * n + 3]
        for top in range(0, arrays[0].shape[0], rows):
            for left in range(0, arrays[0].shape[1], CHUNK):
                pieces.append((name, rate, n, top, left))

    def grad_source(name, top, left, slot):
        if name in ("down", "out"):
            source = down_planes if name == "down" else out_planes
            return (
                source.at[:, top : top + rows, left : left + CHUNK],
                planes.at[slot, : source.shape[0]],
            )
        source, parts = (up_ranks, 2) if name == "up" else (qkv_ranks, 3)
        width = source.shape[2] // parts
        per_seq = width // units
        n = left // CHUNK
        seqs = source.shape[0] // QUAD
        seq = n // per_seq % seqs
        first = n // (per_seq * seqs) * width + n % per_seq * units
        return source.at[seq * QUAD : (seq + 1) * QUAD, :, first : first + units], ranks.at[slot]

    def reads(k):
        name, _, n, top, left = pieces[k]
        slot = k % DEPTH
        window = (slice(top, top + rows), slice(left, left + CHUNK))
        copies = [
            pltpu.make_async_copy(states[3 * n + i].at[window], state.at[slot, i], in_sem.at[slot, i])
            for i in range(3)
        ]
        source, space = grad_source(name, top, left, slot)
        return copies + [pltpu.make_async_copy(source, space, in_sem.at[slot, 3])]

    def writes(k):
        _, _, n, top, left = pieces[k]
        slot = k % DEPTH
        window = (slice(top, top + rows), slice(left, left + CHUNK))
        copies = [
            pltpu.make_async_copy(fresh.at[slot, i], outs[4 * n + i].at[window], out_sem.at[slot, i])
            for i in range(3)
        ]
        return copies + [
            pltpu.make_async_copy(copied.at[slot], outs[4 * n + 3].at[window], out_sem.at[slot, 3])
        ]

    def gradient(name, slot):
        if name in ("down", "out"):
            total = jnp.zeros((rows, CHUNK), f32)
            for j in range((down_planes if name == "down" else out_planes).shape[0]):
                total += jnp.where(holds[j] > 0, planes[slot, j].astype(f32), 0.0)
            return total
        lanes = down_planes.shape[1] if name == "up" else HEAD_DIM
        values = [ranks[slot, q].astype(f32) for q in range(QUAD)]
        return jnp.concatenate(
            [
                values[q][:, n * lanes : (n + 1) * lanes]
                for n in range(units // lanes)
                for q in range(QUAD)
            ],
            axis=1,
        )

    for k in range(DEPTH - 1):
        for copy in reads(k):
            copy.start()
    results = adam_update(gains[...], gains_m[...], gains_v[...], gains_sum[...], 0.3)
    for out, result in zip(gains_outs, results):
        out[...] = result
    for k, (name, rate, _, _, _) in enumerate(pieces):
        slot = k % DEPTH
        if k + DEPTH - 1 < len(pieces):
            for copy in reads(k + DEPTH - 1):
                copy.start()
        for copy in reads(k):
            copy.wait()
        if k >= DEPTH:
            for copy in writes(k - DEPTH):
                copy.wait()
        results = adam_update(state[slot, 0], state[slot, 1], state[slot, 2], gradient(name, slot), rate)
        for i in range(3):
            fresh[slot, i] = results[i]
        copied[slot] = results[0].astype(bf16)
        for copy in writes(k):
            copy.start()
    for k in range(len(pieces) - DEPTH, len(pieces)):
        for copy in writes(k):
            copy.wait()


def adam(grps, holds, down_planes, out_planes, up_ranks, qkv_ranks, gains_sum, gains, states):
    rows = up_ranks.shape[1]
    hbm = pl.BlockSpec(memory_space=pl.ANY)
    vmem = pl.BlockSpec(memory_space=pltpu.VMEM)
    shapes = []
    for array in states[::3]:
        shapes += [jax.ShapeDtypeStruct(array.shape, f32)] * 3
        shapes.append(jax.ShapeDtypeStruct(array.shape, bf16))
    shapes += [jax.ShapeDtypeStruct(gains[0].shape, f32)] * 3
    size = sum(array.size for array in states) // 3
    outs = pl.pallas_call(
        lambda *refs: adam_kernel(grps, *refs),
        in_specs=[pl.BlockSpec(memory_space=pltpu.SMEM)] + [hbm] * 4 + [vmem] * 4 + [hbm] * 12,
        out_specs=[hbm] * 16 + [vmem] * 3,
        out_shape=shapes,
        scratch_shapes=[
            pltpu.VMEM((DEPTH, 3, rows, CHUNK), f32),
            pltpu.VMEM((DEPTH, grps, rows, CHUNK), bf16),
            pltpu.VMEM((DEPTH, QUAD, rows, CHUNK // QUAD), bf16),
            pltpu.VMEM((DEPTH, 3, rows, CHUNK), f32),
            pltpu.VMEM((DEPTH, rows, CHUNK), bf16),
            pltpu.SemaphoreType.DMA((DEPTH, 4)),
            pltpu.SemaphoreType.DMA((DEPTH, 4)),
        ],
        compiler_params=pltpu.CompilerParams(vmem_limit_bytes=VMEM_LIMIT),
        cost_estimate=pl.CostEstimate(flops=size * 16, bytes_accessed=size * 28, transcendentals=size),
        name="adam",
    )(holds, down_planes, out_planes, up_ranks, qkv_ranks, gains_sum, *gains, *states)
    return outs[:4], outs[4:8], outs[8:12], outs[12:16], outs[16:]


def on_device(
    tokens,
    cotangent,
    lengths,
    qkv_weight,
    qkv_moment,
    qkv_square,
    out_weight,
    out_moment,
    out_square,
    up_weight,
    up_moment,
    up_square,
    down_weight,
    down_moment,
    down_square,
    norm_gains,
    gains_moment,
    gains_square,
):
    seqs = lax.axis_size("seq")
    grps = lax.axis_size("grp")
    ranks = seqs * QUAD
    own_rows = tokens.shape[1]
    full_rows = own_rows * seqs
    all_rows = full_rows * QUAD
    heads_local = HEADS // ranks
    head_width = heads_local * HEAD_DIM
    units = down_weight.shape[0]
    aligned = out_weight.shape[0] == HEAD_DIM
    tables = rotate_table(full_rows, heads_local)

    positions = lax.axis_index("seq") * own_rows + jnp.arange(own_rows, dtype=jnp.int32)
    own_grad = jnp.where((positions < lengths[0])[:, None], cotangent[0], 0)
    own_gains = norm_gains.shape[1]
    own_facts = jnp.zeros((8, 128), f32)
    own_facts = own_facts.at[:2, :own_gains].set(norm_gains.astype(bf16).astype(f32))
    own_facts = own_facts.at[2].set(lengths[0].astype(f32))

    out_own = out_weight
    if not aligned:
        out_all = lax.all_gather(out_weight.astype(bf16), EVERY, axis=0, tiled=True)
        out_all = out_all.reshape(seqs, heads_local, QUAD, HEAD_DIM, D)
        seat = lax.axis_index("row") * 2 + lax.axis_index("core")
        out_own = lax.dynamic_index_in_dim(
            lax.dynamic_index_in_dim(out_all, lax.axis_index("seq"), 0, False), seat, 1, False
        ).reshape(head_width, D)
    (
        residual,
        gains,
        facts,
        first_norm,
        queries,
        key_vectors,
        value_vectors,
        attended,
        second_norm,
        down_share,
        hidden,
        grad_both,
        qkv_local,
        up_local,
        out_local,
        down_local,
    ) = forward(
        grps,
        aligned,
        tables,
        own_facts,
        tokens[0],
        own_grad,
        qkv_weight,
        up_weight,
        out_own,
        down_weight,
    )
    if not aligned:
        out_local = out_own
    (
        input_grad,
        block_output,
        gains_total,
        down_planes,
        out_planes,
        up_ranks,
        qkv_ranks,
        *_,
    ) = backward(
        grps,
        aligned,
        facts,
        gains,
        tables,
        residual,
        tokens[0],
        own_grad,
        grad_both,
        up_local.reshape(D, -1),
        down_share.reshape(grps, units, D),
        second_norm,
        first_norm,
        out_local,
        qkv_local.reshape(D, -1),
        (queries, key_vectors, value_vectors, attended),
        hidden,
        down_local,
    )
    if aligned:
        out_sum = out_planes
    else:
        placed_term = jnp.zeros((seqs, QUAD, heads_local, HEAD_DIM, D), bf16)
        placed_term = lax.dynamic_update_slice(
            placed_term,
            out_planes.reshape(1, 1, heads_local, HEAD_DIM, D),
            (lax.axis_index("seq"), seat, 0, 0, 0),
        )
        out_sum = lax.psum_scatter(
            placed_term.transpose(0, 2, 1, 3, 4).reshape(D, D),
            EVERY,
            scatter_dimension=0,
            tiled=True,
        )[None]
    device = ((lax.axis_index("seq") * grps + lax.axis_index("grp")) * 2 + lax.axis_index("row")) * 2
    gains_sum = lax.dynamic_slice(
        gains_total, (0, (device + lax.axis_index("core")) * own_gains), (2, own_gains)
    )
    planes = jnp.arange(grps)
    plane = lax.axis_index("grp")
    holds = ((planes + plane != 3) | (plane % 3 != 0) | (grps != 4)).astype(jnp.int32)
    down_new, out_new, up_new, qkv_new, gains_new = adam(
        grps,
        holds,
        down_planes,
        out_sum,
        up_ranks,
        qkv_ranks,
        gains_sum,
        (norm_gains, gains_moment, gains_square),
        (
            down_weight,
            down_moment,
            down_square,
            out_weight,
            out_moment,
            out_square,
            up_weight,
            up_moment,
            up_square,
            qkv_weight,
            qkv_moment,
            qkv_square,
        ),
    )
    return (
        block_output[None],
        input_grad[None],
        *qkv_new,
        *out_new,
        *up_new,
        *down_new,
        *gains_new,
    )


def solution(mesh):
    seqs, rest = mesh.shape["seq"], mesh.shape["fsdp"]
    planes = Mesh(
        mesh.devices.reshape(seqs, rest // QUAD, 2, 2), ("seq", "grp", "row", "core")
    )
    rows = P(("grp", "row", "core"), "seq", None)
    shards = P(EVERY, None)
    gains = P(None, EVERY)
    return jax.shard_map(
        on_device,
        mesh=planes,
        in_specs=(rows, rows, P(("grp", "row", "core"))) + (shards,) * 12 + (gains,) * 3,
        out_specs=(rows, rows) + (shards,) * 16 + (gains,) * 3,
        check_vma=False,
    )
```

```python
import math

import jax
import jax.numpy as jnp
from jax import lax
from jax.experimental import pallas as pl
from jax.experimental.pallas import tpu as pltpu
from jax.sharding import Mesh, PartitionSpec as P

D = 2048
HEADS = 32
HEAD_DIM = 64
FF = 4096
WINDOW = 128
STEP = 5


NORM_EPSILON = 1e-05
MOMENT_DECAY = 0.5
WEIGHT_DECAY = 0.1
ADAM_EPSILON = 1e-08

SEATS = ("row", "core", "seq")
RANKS = ("seq", "row", "core")
EVERY = ("seq", "grp", "row", "core")
QUAD = 4
VMEM_LIMIT = 63 * 2**20

bf16 = jnp.bfloat16
f32 = jnp.float32


def rotate_table(length, copies):
    halves = HEAD_DIM // 2
    freqs = jnp.exp(-math.log(10000.0) * 2.0 * jnp.arange(halves).astype(f32) / HEAD_DIM)
    angles = jnp.arange(length, dtype=jnp.int32).astype(f32)[:, None] * freqs[None, :]
    cosine, sine = jnp.cos(angles), jnp.sin(angles)
    return (
        jnp.tile(jnp.concatenate([cosine, cosine], axis=1), (1, copies)),
        jnp.tile(jnp.concatenate([-sine, sine], axis=1), (1, copies)),
    )


def adam_update(weight, moment, square, gradient, step_rate):
    moment_new = MOMENT_DECAY * moment + (1.0 - MOMENT_DECAY) * gradient
    square_new = MOMENT_DECAY * square + (1.0 - MOMENT_DECAY) * gradient * gradient
    correction = 1.0 - MOMENT_DECAY**STEP
    unbias = 1.0 / correction
    update = (moment_new * unbias) / (jnp.sqrt(square_new * unbias) + ADAM_EPSILON)
    return (weight - step_rate * (update + WEIGHT_DECAY * weight), moment_new, square_new)


def dot(a, b, lhs=1, rhs=0):
    return lax.dot_general(a, b, (((lhs,), (rhs,)), ((), ())), preferred_element_type=f32)


def swap_halves(values, first):
    width = values.shape[1]
    half = HEAD_DIM // 2
    return jnp.where(
        first, pltpu.roll(values, width - half, 1), pltpu.roll(values, half, 1)
    )


def allowed_mask(rows, length):
    row = lax.broadcasted_iota(jnp.int32, (rows, rows), 0)
    col = lax.broadcasted_iota(jnp.int32, (rows, rows), 1)
    return (col <= row) & (row - col < WINDOW) & (col.astype(f32) < length)


def head_lanes(rows, width, head):
    lane = lax.broadcasted_iota(jnp.int32, (rows, width), 1)
    return (lane // HEAD_DIM) == head


def softmax_rows(queries, key_vectors, allowed):
    scores = jnp.where(allowed, dot(queries, key_vectors, 1, 1) * (HEAD_DIM**-0.5), -1e30)
    shifted = jnp.exp(scores - jnp.max(scores, axis=-1, keepdims=True))
    return shifted / jnp.sum(shifted, axis=-1, keepdims=True)


def attention(length, queries, key_vectors, value_vectors):
    rows, width = queries.shape
    allowed = allowed_mask(rows, length)
    total = jnp.zeros((rows, width), f32)
    for head in range(width // HEAD_DIM):
        mine = head_lanes(rows, width, head)
        weights = softmax_rows(jnp.where(mine, queries, 0), key_vectors, allowed)
        total += dot(weights.astype(bf16), jnp.where(mine, value_vectors, 0))
    return total.astype(bf16)


def attention_grads(length, queries, key_vectors, value_vectors, grads):
    rows, width = queries.shape
    allowed = allowed_mask(rows, length)
    grad_q = jnp.zeros((rows, width), f32)
    grad_k = jnp.zeros((rows, width), f32)
    grad_v = jnp.zeros((rows, width), f32)
    for head in range(width // HEAD_DIM):
        mine = head_lanes(rows, width, head)
        q_head = jnp.where(mine, queries, 0)
        g_head = jnp.where(mine, grads, 0)
        weights = softmax_rows(q_head, key_vectors, allowed)
        grad_p = dot(g_head, value_vectors, 1, 1)
        delta = jnp.sum(weights * grad_p, axis=-1, keepdims=True)
        grad_s = jnp.where(allowed, weights * (grad_p - delta), 0.0).astype(bf16)
        grad_q += dot(grad_s, jnp.where(mine, key_vectors, 0))
        grad_k += dot(grad_s, q_head, 0, 0)
        grad_v += dot(weights.astype(bf16), g_head, 0, 0)
    return grad_q, grad_k, grad_v


MESH = pl.DeviceIdType.MESH
RELATIONS = tuple((a, b, d) for a in range(2) for b in range(2) for d in range(2))[1:]


class Place:
    def __init__(self, grps):
        self.grps = grps
        self.s = lax.axis_index("seq")
        self.g = lax.axis_index("grp")
        self.r = lax.axis_index("row")
        self.c = lax.axis_index("core")

    def peer(self, relation):
        ds, dr, dc = relation
        return ((self.s + ds) % 2, self.g, (self.r + dr) % 2, (self.c + dc) % 2)

    def plane(self, dz):
        return (self.s, (self.g + dz) % self.grps, self.r, self.c)

    def rank(self, relation=(0, 0, 0)):
        s, _, r, c = self.peer(relation)
        return (s * 2 + r) * 2 + c

    def seat(self, relation=(0, 0, 0)):
        s, _, r, c = self.peer(relation)
        return (r * 2 + c) * 2 + s

    def corner(self, relation=(0, 0, 0)):
        s, _, r, _ = self.peer(relation)
        return r * 2 + s

    def greet(self):
        barrier = pltpu.get_barrier_semaphore()
        for relation in RELATIONS:
            pl.semaphore_signal(barrier, inc=1, device_id=self.peer(relation), device_id_type=MESH)
        for dz in range(1, self.grps):
            pl.semaphore_signal(barrier, inc=1, device_id=self.plane(dz), device_id_type=MESH)
        pl.semaphore_wait(barrier, len(RELATIONS) + self.grps - 1)


SIBLING = (0, 0, 1)
ACROSS = ((1, 0, 0), (0, 1, 0), (1, 1, 0))


def remote(src, dst, send_sem, recv_sem, device):
    return pltpu.make_async_remote_copy(
        src_ref=src,
        dst_ref=dst,
        send_sem=send_sem,
        recv_sem=recv_sem,
        device_id=device,
        device_id_type=MESH,
    )


class PlaneSum:
    def __init__(self, place, part, near, far, sems):
        self.place, self.part, self.nears, self.fars = place, part, near, far
        self.near_send, self.near_recv, self.far_send, self.far_recv = sems
        self.first, self.second = [None] * 4, []

    def sequence(self, k):
        place = self.place
        row = (place.r + 1) % 2 if k < 2 else place.r
        return row * 2 + ((place.c + 1) % 2 if k % 2 == 0 else place.c)

    def near(self, k):
        for s in range(2):
            copy = remote(
                self.part.at[2 * self.sequence(k) + s],
                self.nears.at[k + s],
                self.near_send.at[k + s],
                self.near_recv.at[k + s],
                self.place.peer(SIBLING),
            )
            copy.start()
            self.first[k + s] = copy

    def far(self, k):
        place = self.place
        for s in range(2):
            self.first[k - 1 + s].wait()
            self.nears[k - 1 + s] = (
                self.part[2 * self.sequence(k) + s].astype(f32)
                + self.nears[k - 1 + s].astype(f32)
            ).astype(bf16)
        for d in (1, 2) if k == 1 else (0,):
            relation = ACROSS[d]
            copy = remote(
                self.nears.at[k - 1 + (place.s + relation[0]) % 2],
                self.fars.at[d],
                self.far_send.at[d],
                self.far_recv.at[d],
                place.peer(relation),
            )
            copy.start()
            self.second.append(copy)

    def finish(self):
        for copy in self.second:
            copy.wait()

    def chunk(self, lanes):
        total = self.nears[2 + self.place.s, :, lanes].astype(f32)
        for d in range(3):
            total += self.fars[d, :, lanes].astype(f32)
        return total


class PlaneGather:
    def __init__(self, place, blocks, send, recv):
        self.place, self.blocks, self.sends, self.recvs = place, blocks, send, recv
        self.copies = [None] * 7

    def send(self, block, sem, relation):
        copy = remote(
            self.blocks.at[block],
            self.blocks.at[block],
            self.sends.at[sem],
            self.recvs.at[sem],
            self.place.peer(relation),
        )
        copy.start()
        self.copies[sem] = copy

    def start(self):
        mine = self.place.seat()
        for d in range(2):
            self.send(mine, d, ACROSS[d])
        self.send(mine, 3, SIBLING)

    def forward(self, d):
        self.copies[d].wait_recv()
        self.send(self.place.seat(ACROSS[d]), 4 + d, SIBLING)
        if d == 0:
            self.send(self.place.seat(), 2, ACROSS[2])

    def sequence(self, k):
        place = self.place
        row = place.r if k < 2 else (place.r + 1) % 2
        return row * 2 + (place.c if k % 2 == 0 else (place.c + 1) % 2)

    def arrive(self, k, forwarded=False):
        if k == 0:
            self.forward(0)
        elif k == 1:
            if not forwarded:
                self.forward(1)
            self.copies[3].wait_recv()
            self.copies[4].wait_recv()
        elif k == 2:
            self.forward(2)
        else:
            self.copies[5].wait_recv()
            self.copies[6].wait_recv()

    def finish(self):
        for copy in self.copies:
            copy.wait_send()


class ToOwners:
    def __init__(self, place, shares, landed, met, stage, send, recv, own):
        self.place, self.shares, self.landed, self.met, self.stage = place, shares, landed, met, stage
        self.send, self.recv, self.own_sem = send, recv, own
        self.line = place.grps == 4
        self.own = pltpu.make_async_copy(shares.at[place.g], landed.at[place.g], own)

    def copy(self, block, landing, sem, recv, target):
        place = self.place
        return remote(
            self.shares.at[block],
            landing,
            self.send.at[sem],
            self.recv.at[recv],
            (place.s, target, place.r, place.c),
        )

    def direct(self, g):
        targets = ((2, 1), (2, 0), (1, 3), (1, 2))[g]
        return [self.copy(t, self.landed.at[g], t, g, t) for t in targets]

    def meeting(self, g):
        far, inner = (3, 1) if g == 0 else (0, 2)
        return self.copy(far, self.met, far, inner, inner)

    def joined(self, g):
        far = 3 if g == 1 else 0
        return self.copy(far, self.landed.at[g], far, g, far)

    def start(self, waits=False):
        place, self.waits = self.place, waits
        self.own.start()
        if self.line:
            for g in range(4):

                @pl.when(place.g == g)
                def _():
                    if g in (0, 3):
                        self.meeting(g).start()
                    if g in (1, 2) or not waits:
                        for copy in self.direct(g):
                            copy.start()

        else:
            self.copies = [
                self.copy((place.g + dz) % place.grps, self.landed.at[place.g], dz, dz, (place.g + dz) % place.grps)
                for dz in range(1, place.grps)
            ]
            for copy in self.copies:
                copy.start()
        return self

    def proceed(self):
        if self.line:
            for g in (0, 3):

                @pl.when(self.place.g == g)
                def _():
                    self.meeting(g).wait_send()
                    for copy in self.direct(g):
                        copy.start()

    def join(self):
        if not self.line:
            return
        for g in (1, 2):

            @pl.when(self.place.g == g)
            def _():
                outer, far = (0, 3) if g == 1 else (3, 0)
                self.copy(far, self.met, far, g, outer).wait_recv()
                copy = pltpu.make_async_copy(self.met, self.stage, self.own_sem)
                self.own.wait()
                copy.start()
                copy.wait()
                if len(self.stage.shape) == 2:
                    self.shares[far] = (
                        self.shares[far].astype(f32) + self.stage[...].astype(f32)
                    ).astype(bf16)
                else:
                    for n in range(self.stage.shape[0]):
                        self.shares[far, n] = (
                            self.shares[far, n].astype(f32) + self.stage[n].astype(f32)
                        ).astype(bf16)
                self.joined(g).start()

        for g in (0, 3):

            @pl.when(self.place.g == g)
            def _():
                self.own.wait()

    def sent(self):
        if not self.line:
            for copy in self.copies:
                copy.wait_send()
            return
        for g in range(4):

            @pl.when(self.place.g == g)
            def _():
                for copy in self.direct(g):
                    copy.wait_send()
                if g in (1, 2):
                    self.joined(g).wait_send()
                elif not self.waits:
                    self.meeting(g).wait_send()

    def received(self):
        if not self.line:
            self.own.wait()
            for copy in self.copies:
                copy.wait_recv()
            return
        for g in range(4):

            @pl.when(self.place.g == g)
            def _():
                for j in ((1, 2), (0, 2, 3), (0, 1, 3), (1, 2))[g]:
                    self.copy(g, self.landed.at[j], j, j, j).wait_recv()

    def finish(self):
        self.sent()
        self.received()

    def holds(self, j):
        g = self.place.g
        return (g % 3 != 0) | (j + g != 3) if self.line else True


class Exchange:
    def __init__(self, place, blocks, held, send, recv, own):
        mine = place.rank()
        kept = held.at[mine // QUAD, mine % QUAD] if len(held.shape) == 4 else held.at[mine]

        def block(t):
            return blocks.at[0, t // QUAD, t % QUAD] if len(blocks.shape) == 5 else blocks.at[t]

        self.copies = []
        for n, relation in enumerate(RELATIONS):
            copy = remote(
                block(place.rank(relation)),
                kept,
                send.at[n],
                recv.at[n],
                place.peer(relation),
            )
            copy.start()
            self.copies.append(copy)
        copy = pltpu.make_async_copy(block(mine), kept, own)
        copy.start()
        self.copies.append(copy)

    def finish(self):
        for copy in self.copies:
            copy.wait()


LANES = 512


def lanes_of(n, width=LANES):
    return pl.ds(pl.multiple_of(n * width, width), width)


def shares_of(seq, values, weight, part):
    rows = part.shape[1]

    @pl.loop(0, part.shape[2] // LANES)
    def _(n):
        product = dot(values[seq], weight[lanes_of(n)], 1, 1)
        part[2 * seq, :, lanes_of(n)] = product[:rows].astype(bf16)
        part[2 * seq + 1, :, lanes_of(n)] = product[rows:].astype(bf16)


def over_tokens(first, lanes, second, other):
    total = dot(first[0, :, lanes], second[0, :, other], 0, 0)
    for seq in range(1, first.shape[0]):
        total += dot(first[seq, :, lanes], second[seq, :, other], 0, 0)
    return total


def row_shares(first, second, shares):
    grps, seqs, rows, _ = shares.shape
    width = 256
    pieces = width // rows

    @pl.loop(0, first.shape[2] // width)
    def _(b):
        product = over_tokens(first, lanes_of(b, width), second, slice(None)).astype(bf16)
        for p in range(pieces):
            index = b * pieces + p
            shares[index % grps, index // grps] = product[p * rows : (p + 1) * rows]


def summed_rows(landed, holds, blocks):
    seqs, rows = landed.shape[1], blocks.shape[1]
    for seq in range(seqs):
        for quad in range(QUAD):
            block = slice(quad * rows, (quad + 1) * rows)
            total = jnp.zeros((rows, landed.shape[3]), f32)
            for j in range(landed.shape[0]):
                total += jnp.where(holds(j), landed[j, seq, block].astype(f32), 0.0)
            blocks[seq * QUAD + quad] = total.astype(bf16)


def back_kernel(
    grps,
    aligned,
    facts,
    gains,
    cosine,
    sine,
    residual,
    own_tokens,
    own_grad,
    dgu_h,
    up_h,
    second_h,
    first_h,
    out_h,
    qkv_h,
    q_h,
    k_h,
    v_h,
    o_h,
    hidden_h,
    down_h,
    input_grad,
    block_output,
    gains_sum,
    out_landed,
    up_held,
    qkv_held,
    up_landed,
    qkv_landed,
    up_met,
    out_met,
    qkv_met,
    wide,
    up,
    acts,
    out_w,
    qkv,
    part,
    near,
    far,
    blocks,
    turned,
    up_share,
    out_share,
    qkv_share,
    up_sum,
    qkv_sum,
    stage_low,
    stage_wide,
    gain_part,
    gain_plane,
    gain_far,
    load,
    near_send,
    near_recv,
    far_send,
    far_recv,
    all_send,
    all_recv,
    z_send,
    z_recv,
    swap_send,
    swap_recv,
    gain_send,
    gain_recv,
    own_sem,
    near_free,
    far_free,
):
    place = Place(grps)
    rows = residual.shape[0]
    gain_part[...] = jnp.zeros_like(gain_part)
    count, full_rows, head_width = q_h.shape

    def fetch(src, dst, n):
        copy = pltpu.make_async_copy(src, dst, load.at[n])
        copy.start()
        return copy

    loads = [fetch(dgu_h, wide, 0), fetch(up_h, up, 1)]
    later = fetch(second_h, acts, 3)
    weights = [fetch(out_h, out_w, 5), fetch(qkv_h, qkv, 6)]
    place.greet()
    for copy in loads:
        copy.wait()

    sums = (near_send, near_recv, far_send, far_recv)
    def to_owners(n, shares, landed, met, stage, waits=False):
        return ToOwners(
            place, shares, landed, met, stage, z_send.at[n], z_recv.at[n], own_sem.at[n]
        ).start(waits)

    def summed_over_plane(values, weight):
        total = PlaneSum(place, part, near, far, sums)
        for k in range(4):
            shares_of(total.sequence(k), values, weight, part)
            if k % 2 == 0:
                total.near(k)
            else:
                total.far(k)
        return total

    second_sum = summed_over_plane(wide, up)
    later.wait()
    row_shares(acts, wide, up_share)
    up_out = to_owners(1, up_share, up_landed, up_met, stage_wide)
    fetch_first = fetch(first_h, acts, 3)
    heads = [
        fetch(ref, wide.at[:, :, n * head_width : (n + 1) * head_width], 7 + n)
        for n, ref in enumerate((q_h, k_h, v_h, o_h))
    ]

    half = hidden_h.shape[2]
    hidden = turned.at[:, :, :half]
    last = [fetch(hidden_h, hidden, 11)]
    for n in range(2):
        columns = slice(n * D // 2, (n + 1) * D // 2)
        last.append(fetch(down_h.at[:, columns], up.at[n * half : (n + 1) * half, : D // 2], 12 + n))
    second_sum.finish()
    mine = place.seat()
    inner = jnp.zeros((rows, 1), f32)
    squares = jnp.zeros((rows, 1), f32)
    for n in range(D // LANES):
        lanes = slice(n * LANES, (n + 1) * LANES)
        grad = second_sum.chunk(lanes)
        values = residual[:, lanes]
        inner += jnp.sum(grad * gains[1:2, lanes] * values, axis=-1, keepdims=True)
        squares += jnp.sum(values * values, axis=-1, keepdims=True)
    scale = lax.rsqrt(squares / D + NORM_EPSILON)
    inner = inner / D
    for n in range(D // LANES):
        lanes = slice(n * LANES, (n + 1) * LANES)
        grad, values = second_sum.chunk(lanes), residual[:, lanes]
        gain_part[1:2, lanes] = jnp.sum(grad * values * scale, axis=0, keepdims=True)
        total = own_grad[:, lanes].astype(f32) + scale * (
            grad * gains[1:2, lanes] - values * scale * scale * inner
        )
        input_grad[:, lanes] = total
        blocks[mine, :, lanes] = total.astype(bf16)

    gather = PlaneGather(place, blocks, all_send, all_recv)
    gather.start()
    for copy in weights + heads:
        copy.wait()

    lane = lax.broadcasted_iota(jnp.int32, (full_rows, head_width), 1)
    first_half = (lane % HEAD_DIM) < HEAD_DIM // 2

    for copy in last:
        copy.wait()

    @pl.loop(0, count)
    def _(seq):
        for n in range(D // LANES):
            top, left = n * LANES // (D // 2) * half, n * LANES % (D // 2)
            product = dot(hidden[seq], up[top : top + half, left : left + LANES])
            part[2 * seq, :, n * LANES : (n + 1) * LANES] = product[:rows].astype(bf16)
            part[2 * seq + 1, :, n * LANES : (n + 1) * LANES] = product[rows:].astype(bf16)

    last_sum = PlaneSum(place, part, near, far, sums)
    for k in range(4):
        gather.arrive(k)
        seq = gather.sequence(k)
        grads = jnp.concatenate(
            [dot(blocks[2 * seq], out_w[...], 1, 1), dot(blocks[2 * seq + 1], out_w[...], 1, 1)],
            axis=0,
        ).astype(bf16)
        queries = wide[seq, :, 0:head_width]
        key_vectors = wide[seq, :, head_width : 2 * head_width]
        value_vectors = wide[seq, :, 2 * head_width : 3 * head_width]
        grad_q, grad_k, grad_v = attention_grads(
            facts[seq, 2:3, 0:1], queries, key_vectors, value_vectors, grads
        )
        for n, grad in enumerate((grad_q, grad_k)):
            values = (grad * HEAD_DIM**-0.5).astype(bf16).astype(f32)
            back = values * cosine[...] - swap_halves(values, first_half) * sine[...]
            turned[seq, :, n * head_width : (n + 1) * head_width] = back.astype(bf16)
        turned[seq, :, 2 * head_width : 3 * head_width] = grad_v.astype(bf16)
        if k == 1:
            last_sum.near(0)
            last_sum.near(2)
            up_out.join()
        elif k == 2:
            last_sum.far(1)
            last_sum.far(3)

    gather.finish()
    out_rows = out_share.shape[1]

    @pl.loop(0, D // LANES)
    def _(n):
        lanes = lanes_of(n)
        total = jnp.zeros((head_width, LANES), f32)
        for seq in range(count):
            values = wide[seq, :, 3 * head_width : 4 * head_width].astype(f32)
            total += dot(values[:rows].astype(bf16), blocks[2 * seq, :, lanes], 0, 0)
            total += dot(values[rows:].astype(bf16), blocks[2 * seq + 1, :, lanes], 0, 0)
        total = total.astype(bf16)
        for j in range(out_share.shape[0]):
            out_share[j, :, lanes] = total[j * out_rows : (j + 1) * out_rows]

    fetch_first.wait()
    row_shares(acts, turned, qkv_share)
    triple = turned.shape[2]
    qkv_out = to_owners(2, qkv_share, qkv_landed, qkv_met, stage_wide.at[:, :, :triple], True)

    last_sum.finish()
    for n in range(D // LANES):
        lanes = slice(n * LANES, (n + 1) * LANES)
        block_output[:, lanes] = (residual[:, lanes] + last_sum.chunk(lanes)).astype(bf16)
    pl.semaphore_signal(near_free, inc=1, device_id=place.peer(SIBLING), device_id_type=MESH)
    for relation in ACROSS:
        pl.semaphore_signal(far_free, inc=1, device_id=place.peer(relation), device_id_type=MESH)
    pl.semaphore_wait(near_free, 1)
    pl.semaphore_wait(far_free, 3)
    first_sum = summed_over_plane(turned, qkv)
    qkv_out.proceed()
    qkv_out.join()
    first_sum.finish()
    inner = jnp.zeros((rows, 1), f32)
    squares = jnp.zeros((rows, 1), f32)
    for n in range(D // LANES):
        lanes = slice(n * LANES, (n + 1) * LANES)
        grad = first_sum.chunk(lanes)
        values = own_tokens[:, lanes].astype(f32)
        inner += jnp.sum(grad * gains[0:1, lanes] * values, axis=-1, keepdims=True)
        squares += jnp.sum(values * values, axis=-1, keepdims=True)
    scale = lax.rsqrt(squares / D + NORM_EPSILON)
    inner = inner / D
    for n in range(D // LANES):
        lanes = slice(n * LANES, (n + 1) * LANES)
        grad, values = first_sum.chunk(lanes), own_tokens[:, lanes].astype(f32)
        gain_part[0:1, lanes] = jnp.sum(grad * values * scale, axis=0, keepdims=True)
        input_grad[:, lanes] += scale * (
            grad * gains[0:1, lanes] - values * scale * scale * inner
        )

    gain_copies = []
    for n, relation in enumerate(RELATIONS):
        copy = remote(
            gain_part, gain_plane.at[n], gain_send.at[n], gain_recv.at[n], place.peer(relation)
        )
        copy.start()
        gain_copies.append(copy)

    up_out.finish()
    landed = pltpu.make_async_copy(up_landed, up_share, load.at[1])
    landed.start()
    for copy in gain_copies:
        copy.wait()
    total = gain_part[...]
    for n in range(len(RELATIONS)):
        total += gain_plane[n]
    gain_far[0] = total
    gain_copies = []
    for dz in range(1, grps):
        copy = remote(
            gain_far.at[0],
            gain_far.at[dz],
            gain_send.at[7 + dz],
            gain_recv.at[7 + dz],
            place.plane(dz),
        )
        copy.start()
        gain_copies.append(copy)
    landed.wait()
    summed_rows(up_share, up_out.holds, up_sum)
    up_swap = Exchange(place, up_sum, up_held, swap_send.at[0], swap_recv.at[0], own_sem.at[4])
    for copy in gain_copies:
        copy.wait()
    total = gain_far[0]
    for dz in range(1, grps):
        total += gain_far[dz]
    gains_sum[...] = total

    qkv_out.sent()
    if aligned:
        out_out = to_owners(3, out_share, out_landed, out_met, stage_low)
    else:
        out_out = pltpu.make_async_copy(out_share, out_landed, own_sem.at[3])
        out_out.start()
    qkv_out.received()
    landed = pltpu.make_async_copy(qkv_landed, qkv_share, load.at[6])
    landed.start()
    landed.wait()
    summed_rows(qkv_share, qkv_out.holds, qkv_sum)
    qkv_swap = Exchange(place, qkv_sum, qkv_held, swap_send.at[1], swap_recv.at[1], own_sem.at[5])
    if aligned:
        out_out.join()
    if aligned:
        out_out.finish()
    else:
        out_out.wait()
    up_swap.finish()
    qkv_swap.finish()


def backward(
    grps,
    aligned,
    facts,
    gains,
    tables,
    residual,
    own_tokens,
    own_grad,
    grad_both,
    up_local,
    second_norm,
    first_norm,
    out_local,
    qkv_local,
    heads,
    hidden,
    down_local,
):
    rows = residual.shape[0]
    count, full_rows, head_width = heads[0].shape
    seqs = full_rows // rows
    ranks = seqs * QUAD
    both = grad_both.shape[2]
    quad_rows = D // (seqs * grps)
    shard = quad_rows // QUAD
    out_rows = head_width // grps if aligned else HEAD_DIM
    triple = 3 * head_width
    out_count = head_width // out_rows
    hbm = pl.BlockSpec(memory_space=pl.ANY)
    vmem = pl.BlockSpec(memory_space=pltpu.VMEM)
    shape = jax.ShapeDtypeStruct
    dma = pltpu.SemaphoreType.DMA
    return pl.pallas_call(
        lambda *refs: back_kernel(grps, aligned, *refs),
        in_specs=[vmem] * 7 + [hbm] * 12,
        out_specs=[vmem] * 3 + [hbm] * 8,
        out_shape=[
            shape((rows, D), f32),
            shape((rows, D), bf16),
            shape((8, D), f32),
            shape((out_count, out_rows, D), bf16),
            shape((ranks, shard, both), bf16),
            shape((ranks, shard, triple), bf16),
            shape((grps, seqs, quad_rows, both), bf16),
            shape((grps, seqs, quad_rows, triple), bf16),
            shape((seqs, quad_rows, both), bf16),
            shape((out_rows, D), bf16),
            shape((seqs, quad_rows, triple), bf16),
        ],
        scratch_shapes=[
            pltpu.VMEM((count, full_rows, both), bf16),
            pltpu.VMEM((D, both), bf16),
            pltpu.VMEM((count, full_rows, D), bf16),
            pltpu.VMEM((head_width, D), bf16),
            pltpu.VMEM((D, triple), bf16),
            pltpu.VMEM((ranks, rows, D), bf16),
            pltpu.VMEM((4, rows, D), bf16),
            pltpu.VMEM((3, rows, D), bf16),
            pltpu.VMEM((ranks, rows, D), bf16),
            pltpu.VMEM((count, full_rows, triple), bf16),
            pltpu.VMEM((grps, seqs, quad_rows, both), bf16),
            pltpu.VMEM((out_count, out_rows, D), bf16),
            pltpu.VMEM((grps, seqs, quad_rows, triple), bf16),
            pltpu.VMEM((ranks, shard, both), bf16),
            pltpu.VMEM((ranks, shard, triple), bf16),
            pltpu.VMEM((out_rows, D), bf16),
            pltpu.VMEM((seqs, quad_rows, both), bf16),
            pltpu.VMEM((8, D), f32),
            pltpu.VMEM((7, 8, D), f32),
            pltpu.VMEM((grps, 8, D), f32),
            dma((14,)),
            dma((4,)),
            dma((4,)),
            dma((3,)),
            dma((3,)),
            dma((7,)),
            dma((7,)),
            dma((4, grps)),
            dma((4, grps)),
            dma((2, 7)),
            dma((2, 7)),
            dma((7 + grps,)),
            dma((7 + grps,)),
            dma((6,)),
            pltpu.SemaphoreType.REGULAR,
            pltpu.SemaphoreType.REGULAR,
        ],
        compiler_params=pltpu.CompilerParams(
            collective_id=0, has_side_effects=True, vmem_limit_bytes=VMEM_LIMIT
        ),
        cost_estimate=pl.CostEstimate(
            flops=30 * 10**9, bytes_accessed=60 * 2**20, transcendentals=2 * 10**6
        ),
        name="backward",
    )(
        facts,
        gains,
        *tables,
        residual,
        own_tokens,
        own_grad,
        grad_both,
        up_local,
        second_norm,
        first_norm,
        out_local,
        qkv_local,
        *heads,
        hidden,
        down_local,
    )


CHUNK = 1024


class FromOwners:
    def __init__(self, place, source, landed, landing, send, recv, own):
        self.place, self.source, self.send, self.recv = place, source, send, recv
        self.slot = lambda j: landing(landed, j)
        self.own = pltpu.make_async_copy(source, self.slot(place.g), own)
        self.line = place.grps == 4

    def copy(self, source, slot, sem, recv, target):
        place = self.place
        return remote(
            source, self.slot(slot), self.send.at[sem], self.recv.at[recv], (place.s, target, place.r, place.c)
        )

    def passed(self, g, j, target):
        source = self.source if j == g else self.slot(j)
        return self.copy(source, j, j + (4 if target > g else 0), j, target)

    def arrived(self, j):
        self.copy(self.source, j, j, j, j).wait_recv()

    def on_line(self, steps):
        for g in range(4):
            if steps[g]:

                @pl.when(self.place.g == g)
                def _():
                    for awaited, j, target in steps[g]:
                        if awaited is not None:
                            self.arrived(awaited)
                        if target is not None:
                            self.passed(g, j, target).start()

    FIRST = (
        ((None, 0, 1),),
        ((None, 1, 0), (None, 1, 2)),
        ((None, 2, 3), (None, 2, 1)),
        ((None, 3, 2),),
    )
    SECOND = (
        ((1, 1, None),),
        ((2, 2, 0), (0, 0, 2)),
        ((1, 1, 3), (3, 3, 1)),
        ((2, 2, None),),
    )
    THIRD = ((), ((3, 3, 0),), ((0, 0, 3),), ())

    def start(self):
        place = self.place
        self.own.start()
        if self.line:
            self.on_line(self.FIRST)
        else:
            self.copies = [
                self.copy(self.source, place.g, dz, dz, (place.g + dz) % place.grps)
                for dz in range(1, place.grps)
            ]
            for copy in self.copies:
                copy.start()

    def second(self):
        if self.line:
            self.on_line(self.SECOND)

    def third(self):
        if self.line:
            self.on_line(self.THIRD)

    def finish(self):
        self.own.wait()
        if self.line:
            for g in range(4):

                @pl.when(self.place.g == g)
                def _():
                    for j in {0: (2, 3), 3: (1, 0)}.get(g, ()):
                        self.arrived(j)
                    for steps in (self.FIRST, self.SECOND, self.THIRD):
                        for _, j, target in steps[g]:
                            if target is not None:
                                self.passed(g, j, target).wait_send()

        else:
            for copy in self.copies:
                copy.wait()


class Chain:
    def __init__(self, place, part, through, landed, send, recv, own):
        self.place, self.part, self.through, self.landed = place, part, through, landed
        self.send, self.recv = send, recv
        self.units = landed.shape[1]
        self.own = pltpu.make_async_copy(self.block(part, place.g), landed.at[2], own)

    def block(self, ref, j):
        return ref.at[j, : self.units]

    def copy(self, g, j):
        place, target = self.place, g + 1 if j > g else g - 1
        if target == j:
            landing = self.landed.at[0 if j > g else 1]
        else:
            landing = self.block(self.through, j)
        recv = j if target != j else (j if j > g else 4)
        return remote(
            self.block(self.part, j), landing, self.send.at[j], self.recv.at[recv], (place.s, target, place.r, place.c)
        )

    def each(self, planes, action):
        for g in planes:

            @pl.when(self.place.g == g)
            def _():
                action(g)

    def blocks(self, g):
        return (3, 2, 1) if g == 0 else (0, 1, 2)

    def start(self):
        self.own.start()
        self.each((0, 3), lambda g: self.copy(g, self.blocks(g)[0]).start())

    def add(self, g, source, j):
        self.copy(source, j).wait_recv()
        self.part[j, : self.units] = (
            self.part[j, : self.units].astype(f32) + self.through[j, : self.units].astype(f32)
        ).astype(bf16)
        self.copy(g, j).start()

    def step(self, n):
        def ends(g):
            self.copy(g, self.blocks(g)[n - 1]).wait_send()
            self.copy(g, self.blocks(g)[n]).start()

        def inner(g):
            end = 0 if g == 1 else 3
            self.add(g, end, self.blocks(end)[n - 1])

        self.each((0, 3), ends)
        self.each((1, 2), inner)

    def last(self):
        self.each((1, 2), lambda g: self.add(g, 3 - g, 0 if g == 1 else 3))

    def finish(self):
        self.own.wait()

        def done(g):
            if g > 0:
                self.copy(g - 1, g).wait_recv()
            if g < 3:
                self.copy(g + 1, g).wait_recv()
            if g in (0, 3):
                self.copy(g, self.blocks(g)[2]).wait_send()
            else:
                for j in range(4):
                    if j != g:
                        self.copy(g, j).wait_send()

        self.each(range(4), done)


def shares_from(seq, values, weight, part):
    rows = part.shape[1]

    @pl.loop(0, part.shape[2] // LANES)
    def _(n):
        product = dot(values[seq], weight[:, lanes_of(n)])
        part[2 * seq, :, lanes_of(n)] = product[:rows].astype(bf16)
        part[2 * seq + 1, :, lanes_of(n)] = product[rows:].astype(bf16)


def times_slices(values, weight, lanes):
    seqs, grps, quad, shard, _ = weight.shape
    depth = quad * shard
    total = None
    for n in range(seqs * grps):
        piece = weight[n // grps, n % grps, :, :, lanes]
        term = dot(values[:, n * depth : (n + 1) * depth], piece.reshape(depth, piece.shape[2]))
        total = term if total is None else total + term
    return total


def both_blocks(blocks, seq):
    return jnp.concatenate([blocks[2 * seq].astype(f32), blocks[2 * seq + 1].astype(f32)], axis=0)


def forward_kernel(
    grps,
    aligned,
    cosine,
    sine,
    own_facts,
    tokens_h,
    own_grad_h,
    qkv_own,
    up_own,
    out_own,
    down_own,
    residual,
    gains,
    facts,
    first_h,
    q_h,
    k_h,
    v_h,
    o_h,
    second_h,
    grads_landed,
    hidden_h,
    dgu_h,
    qkv_landed,
    up_landed,
    out_landed,
    down_landed,
    blocks,
    grad_blocks,
    norm,
    grad_seq,
    qkv_rank,
    up_rank,
    qkv,
    up,
    out_w,
    down,
    heads,
    part,
    near,
    far,
    both,
    hidden,
    dgu,
    all_facts,
    early,
    load,
    store,
    swap_send,
    swap_recv,
    near_send,
    near_recv,
    far_send,
    far_recv,
    all_send,
    all_recv,
    z_send,
    z_recv,
    fact_send,
    fact_recv,
    chain_send,
    chain_recv,
    own_sem,
):
    place = Place(grps)
    count, full_rows, _ = norm.shape
    rows = residual.shape[0]
    head_width = heads.shape[3]
    mine, rank = place.seat(), place.rank()

    def fetch(src, dst, n):
        copy = pltpu.make_async_copy(src, dst, load.at[n])
        copy.start()
        return copy

    def keep(src, dst, n):
        copy = pltpu.make_async_copy(src, dst, store.at[n])
        copy.start()
        return copy

    shard = qkv_own.shape[0]
    units = down.shape[0] // grps
    seqs = qkv_landed.shape[0]
    slots = iter(range(20))

    def fetch_chunks(src):
        pieces = []
        for top in range(0, src.shape[0], shard):
            for left in range(0, src.shape[1], CHUNK):
                slot = next(slots)
                space = both.at[slot // 5, (slot % 5) * shard : (slot % 5 + 1) * shard]
                copy = pltpu.make_async_copy(
                    src.at[top : top + shard, left : left + CHUNK], space, early.at[slot]
                )
                copy.start()
                pieces.append((copy, space))
        return pieces

    def dealt(pieces, weight, lanes, parts):
        count = CHUNK // (QUAD * lanes)
        width = count * lanes
        each = len(pieces) // (parts * seqs)
        for n, (copy, space) in enumerate(pieces):
            copy.wait()
            values = space[...]
            seq = n // each % seqs
            first = (n // (each * seqs) * each + n % each) * width
            for q in range(QUAD):
                taken = [
                    values[:, (k * QUAD + q) * lanes : (k * QUAD + q + 1) * lanes] for k in range(count)
                ]
                weight[0, seq, q, :, first : first + width] = jnp.concatenate(taken, axis=1).astype(bf16)

    facts[rank] = own_facts[...]
    if aligned:
        out_pieces = fetch_chunks(out_own)
    qkv_pieces = fetch_chunks(qkv_own)
    up_pieces = fetch_chunks(up_own)
    down_pieces = fetch_chunks(down_own)
    own_blocks = [fetch(tokens_h, blocks.at[mine], 0), fetch(own_grad_h, grad_blocks.at[mine], 1)]

    def plane_rows(ref, j):
        return ref.at[:, j]

    def own_rows(ref, j):
        size = ref.shape[0] // grps
        return ref.at[pl.ds(pl.multiple_of(j * size, size), size)]

    def rows_of(ref, j):
        top = j * units
        return ref.at[top // 128, pl.ds(pl.multiple_of(top % 128, units), units)]

    def from_owners(n, source, landed, landing):
        return FromOwners(place, source, landed, landing, z_send.at[n], z_recv.at[n], own_sem.at[n])

    def stacked(pieces, weight):
        across = weight.shape[1] // CHUNK
        for n, (copy, space) in enumerate(pieces):
            copy.wait()
            top, left = n // across * shard, n % across * CHUNK
            weight[top : top + shard, left : left + CHUNK] = space[...].astype(bf16)

    down_z = from_owners(3, down.at[:units], down_landed, own_rows)
    if aligned:
        stacked(out_pieces, out_w)
        out_z = from_owners(2, out_w.at[:shard], out_landed, own_rows)
    place.greet()
    if aligned:
        out_z.start()
    dealt(qkv_pieces, qkv, HEAD_DIM, 3)
    qkv_swap = Exchange(place, qkv, qkv_rank, swap_send.at[0], swap_recv.at[0], own_sem.at[4])
    fact_copies = []
    for n, relation in enumerate(RELATIONS):
        copy = remote(own_facts, facts.at[rank], fact_send.at[n], fact_recv.at[n], place.peer(relation))
        copy.start()
        fact_copies.append(copy)
    if aligned:
        out_z.second()
    dealt(up_pieces, up, units, 2)
    stacked(down_pieces, down)
    for copy in own_blocks:
        copy.wait()
    if aligned:
        out_z.third()
    qkv_swap.finish()
    qkv_z = from_owners(0, qkv_rank, qkv_landed, plane_rows)
    up_z = from_owners(1, up_rank, up_landed, plane_rows)
    qkv_z.start()
    token_gather = PlaneGather(place, blocks, all_send.at[0], all_recv.at[0])
    token_gather.start()
    for copy in fact_copies:
        copy.wait()
    all_facts[place.g] = facts[...]
    fact_copies = []
    for dz in range(1, grps):
        copy = remote(
            facts,
            all_facts.at[place.g],
            fact_send.at[7 + dz],
            fact_recv.at[7 + dz],
            place.plane(dz),
        )
        copy.start()
        fact_copies.append(copy)
    for copy in fact_copies:
        copy.wait()
    width = D // (seqs * grps * QUAD)
    for n in range(seqs * grps):
        pieces = [all_facts[n % grps, (n // grps) * QUAD + q, :, :width] for q in range(QUAD)]
        gains[:, n * QUAD * width : (n + 1) * QUAD * width] = jnp.concatenate(pieces, axis=1)
    token_gather.forward(0)
    token_gather.forward(1)
    up_swap = Exchange(place, up, up_rank, swap_send.at[1], swap_recv.at[1], own_sem.at[5])
    qkv_z.second()
    token_gather.forward(2)
    token_gather.arrive(3)
    token_gather.copies[3].wait_recv()
    token_gather.copies[4].wait_recv()
    token_gather.finish()

    @pl.loop(0, count)
    def _(seq):
        values = both_blocks(blocks, seq)
        scale = lax.rsqrt(jnp.mean(values * values, axis=-1, keepdims=True) + NORM_EPSILON)
        norm[seq] = (values * scale * gains[0:1, :]).astype(bf16)

    stores = [keep(norm, first_h, 0)]
    grad_gather = PlaneGather(place, grad_blocks, all_send.at[1], all_recv.at[1])
    grad_gather.start()
    up_swap.finish()
    qkv_z.third()
    up_z.start()
    qkv_z.finish()
    fetch(qkv_landed, qkv, 2).wait()

    lane = lax.broadcasted_iota(jnp.int32, (full_rows, head_width), 1)
    first_half = (lane % HEAD_DIM) < HEAD_DIM // 2

    if aligned:
        out_z.finish()
        fetch(out_landed, out_w, 3).wait()
    else:
        fetch(out_own, out_w, 3).wait()

    plane_sum = PlaneSum(place, part, near, far, (near_send, near_recv, far_send, far_recv))
    mixed = heads.at[3]
    for k in range(4):
        seq = plane_sum.sequence(k)
        for n in range(3):
            lanes = slice(n * head_width, (n + 1) * head_width)
            values = times_slices(norm[seq], qkv, lanes)
            if n < 2:
                values = values * cosine[...] + swap_halves(values, first_half) * sine[...]
            heads[n, seq] = values.astype(bf16)
        heads[3, seq] = attention(facts[seq, 2:3, 0:1], heads[0, seq], heads[1, seq], heads[2, seq])
        shares_from(seq, mixed, out_w, part)
        if k % 2 == 0:
            plane_sum.near(k)
        else:
            plane_sum.far(k)
        if k == 0:
            grad_gather.forward(0)
            grad_gather.forward(1)
    grad_gather.forward(2)
    grad_gather.arrive(3)
    grad_gather.copies[3].wait_recv()
    grad_gather.copies[4].wait_recv()
    grad_gather.finish()
    stores += [keep(heads.at[n], ref, 1 + n) for n, ref in enumerate((q_h, k_h, v_h, o_h))]
    up_z.second()

    @pl.loop(0, count)
    def _(seq):
        grad_seq[seq] = both_blocks(grad_blocks, seq).astype(bf16)

    fetch(tokens_h, grad_blocks.at[mine], 4).wait()
    plane_sum.finish()
    squares = jnp.zeros((rows, 1), f32)
    for n in range(D // LANES):
        lanes = slice(n * LANES, (n + 1) * LANES)
        values = grad_blocks[mine, :, lanes].astype(f32) + plane_sum.chunk(lanes)
        residual[:, lanes] = values
        squares += jnp.sum(values * values, axis=-1, keepdims=True)
    scale = lax.rsqrt(squares / D + NORM_EPSILON)
    for n in range(D // LANES):
        lanes = slice(n * LANES, (n + 1) * LANES)
        blocks[mine, :, lanes] = (residual[:, lanes] * scale * gains[1:2, lanes]).astype(bf16)
    norm_gather = PlaneGather(place, blocks, all_send.at[2], all_recv.at[2])
    norm_gather.start()
    up_z.third()
    down_z.start()
    stores[0].wait()
    half = hidden.shape[2]
    for k in range(4):
        norm_gather.arrive(k, forwarded=k == 1)
        seq = norm_gather.sequence(k)
        norm[seq] = both_blocks(blocks, seq).astype(bf16)
        if k == 0:
            norm_gather.forward(1)
            up_z.finish()
            fetch(up_landed, up, 5).wait()
        elif k == 2:
            down_z.second()
        gate = times_slices(norm[seq], up, slice(0, half))
        above = times_slices(norm[seq], up, slice(half, 2 * half))
        both[seq, :, :half] = gate
        both[seq, :, half:] = above
        hidden[seq] = (gate * jax.nn.sigmoid(gate) * above).astype(bf16)
    norm_gather.finish()
    stores[0] = keep(norm, second_h, 5)
    stores.append(keep(hidden, hidden_h, 7))
    tall = min(256, half)
    slab = part.shape[1] // 128 * 128

    @pl.loop(0, half // tall)
    def _(b):
        for side in range(2):
            lanes = slice(side * D // 2, (side + 1) * D // 2)
            product = over_tokens(hidden, lanes_of(b, tall), grad_seq, lanes).astype(bf16)
            for p in range(tall // slab):
                part[b * (tall // slab) + p, :slab, lanes] = product[p * slab : (p + 1) * slab]

    if grps == 4:
        chain = Chain(place, part, near, grads_landed, chain_send, chain_recv, own_sem.at[6])
        chain.start()
    else:
        spread = [pltpu.make_async_copy(rows_of(part, place.g), grads_landed.at[place.g], own_sem.at[6])]
        for dz in range(1, grps):
            spread.append(
                remote(
                    rows_of(part, (place.g + dz) % grps),
                    grads_landed.at[place.g],
                    chain_send.at[dz],
                    chain_recv.at[dz],
                    place.plane(dz),
                )
            )
        for copy in spread:
            copy.start()
    down_z.third()
    down_z.finish()
    fetch(down_landed, down, 6).wait()

    def feed_forward_grads(seq):
        grads = dot(grad_seq[seq], down[...], 1, 1)
        gate, above = both[seq, :, :half], both[seq, :, half:]
        sigmoid = jax.nn.sigmoid(gate)
        dgu[seq, :, :half] = (grads * above * sigmoid * (1.0 + gate * (1.0 - sigmoid))).astype(bf16)
        dgu[seq, :, half:] = (grads * (gate * sigmoid)).astype(bf16)

    pl.loop(0, count // 2)(feed_forward_grads)
    if grps == 4:
        chain.step(1)
    pl.loop(count // 2, count)(feed_forward_grads)
    stores.append(keep(dgu, dgu_h, 8))
    if grps == 4:
        chain.step(2)
        chain.last()
        chain.finish()
    else:
        for copy in spread:
            copy.wait()
    for copy in stores:
        copy.wait()


def forward(grps, aligned, tables, own_facts, tokens, own_grad, qkv_own, up_own, out_own, down_own):
    rows = tokens.shape[0]
    shard = qkv_own.shape[0]
    seqs = D // (shard * grps * QUAD)
    ranks = seqs * QUAD
    triple, both = qkv_own.shape[1] // ranks, up_own.shape[1] // ranks
    count, full_rows, head_width = QUAD, rows * seqs, triple // 3
    half = both // 2
    hbm = pl.BlockSpec(memory_space=pl.ANY)
    vmem = pl.BlockSpec(memory_space=pltpu.VMEM)
    shape = jax.ShapeDtypeStruct
    dma = pltpu.SemaphoreType.DMA
    by_heads = shape((count, full_rows, head_width), bf16)
    return pl.pallas_call(
        lambda *refs: forward_kernel(grps, aligned, *refs),
        in_specs=[vmem] * 3 + [hbm] * 6,
        out_specs=[vmem] * 3 + [hbm] * 13,
        out_shape=[
            shape((rows, D), f32),
            shape((8, D), f32),
            shape((ranks, 8, 128), f32),
            shape((count, full_rows, D), bf16),
            by_heads,
            by_heads,
            by_heads,
            by_heads,
            shape((count, full_rows, D), bf16),
            shape((3 if grps == 4 else grps, half // grps, D), bf16),
            shape((count, full_rows, half), bf16),
            shape((count, full_rows, both), bf16),
            shape((seqs, grps, QUAD, shard, triple), bf16),
            shape((seqs, grps, QUAD, shard, both), bf16),
            shape((head_width, D), bf16),
            shape((half, D), bf16),
        ],
        scratch_shapes=[
            pltpu.VMEM((ranks, rows, D), bf16),
            pltpu.VMEM((ranks, rows, D), bf16),
            pltpu.VMEM((count, full_rows, D), bf16),
            pltpu.VMEM((count, full_rows, D), bf16),
            pltpu.VMEM((seqs, QUAD, shard, triple), bf16),
            pltpu.VMEM((seqs, QUAD, shard, both), bf16),
            pltpu.VMEM((seqs, grps, QUAD, shard, triple), bf16),
            pltpu.VMEM((seqs, grps, QUAD, shard, both), bf16),
            pltpu.VMEM((head_width, D), bf16),
            pltpu.VMEM((half, D), bf16),
            pltpu.VMEM((4, count, full_rows, head_width), bf16),
            pltpu.VMEM((ranks, rows, D), bf16),
            pltpu.VMEM((4, rows, D), bf16),
            pltpu.VMEM((3, rows, D), bf16),
            pltpu.VMEM((count, full_rows, both), f32),
            pltpu.VMEM((count, full_rows, half), bf16),
            pltpu.VMEM((count, full_rows, both), bf16),
            pltpu.VMEM((grps, ranks, 8, 128), f32),
            dma((20,)),
            dma((7,)),
            dma((9,)),
            dma((2, 7)),
            dma((2, 7)),
            dma((4,)),
            dma((4,)),
            dma((3,)),
            dma((3,)),
            dma((3, 7)),
            dma((3, 7)),
            dma((4, 2 * grps)),
            dma((4, grps)),
            dma((7 + grps,)),
            dma((7 + grps,)),
            dma((max(5, grps),)),
            dma((max(5, grps),)),
            dma((7,)),
        ],
        compiler_params=pltpu.CompilerParams(
            collective_id=1, has_side_effects=True, vmem_limit_bytes=VMEM_LIMIT
        ),
        cost_estimate=pl.CostEstimate(
            flops=20 * 10**9, bytes_accessed=60 * 2**20, transcendentals=4 * 10**6
        ),
        name="forward",
    )(*tables, own_facts, tokens, own_grad, qkv_own, up_own, out_own, down_own)


DEPTH = 3


def adam_kernel(grps, down_holds, out_holds, down_planes, out_planes, up_ranks, qkv_ranks, gains_sum, gains, gains_m, gains_v, *refs):
    states, outs = refs[:12], refs[12:28]
    gains_outs = refs[28:31]
    state, planes, ranks, fresh, copied, in_sem, out_sem = refs[31:]
    rows = state.shape[2]
    units = CHUNK // QUAD
    pieces = []
    for n, (name, rate) in enumerate(
        (("down", FF ** (-0.5)), ("out", (D // 128) ** (-0.5)), ("up", D ** (-0.5)), ("qkv", D ** (-0.5)))
    ):
        arrays = states[3 * n : 3 * n + 3]
        for top in range(0, arrays[0].shape[0], rows):
            for left in range(0, arrays[0].shape[1], CHUNK):
                pieces.append((name, rate, n, top, left))

    def grad_source(name, top, left, slot):
        if name in ("down", "out"):
            source = down_planes if name == "down" else out_planes
            return (
                source.at[:, top : top + rows, left : left + CHUNK],
                planes.at[slot, : source.shape[0]],
            )
        source, parts = (up_ranks, 2) if name == "up" else (qkv_ranks, 3)
        width = source.shape[2] // parts
        per_seq = width // units
        n = left // CHUNK
        seqs = source.shape[0] // QUAD
        seq = n // per_seq % seqs
        first = n // (per_seq * seqs) * width + n % per_seq * units
        return source.at[seq * QUAD : (seq + 1) * QUAD, :, first : first + units], ranks.at[slot]

    def reads(k):
        name, _, n, top, left = pieces[k]
        slot = k % DEPTH
        window = (slice(top, top + rows), slice(left, left + CHUNK))
        copies = [
            pltpu.make_async_copy(states[3 * n + i].at[window], state.at[slot, i], in_sem.at[slot, i])
            for i in range(3)
        ]
        source, space = grad_source(name, top, left, slot)
        return copies + [pltpu.make_async_copy(source, space, in_sem.at[slot, 3])]

    def writes(k):
        _, _, n, top, left = pieces[k]
        slot = k % DEPTH
        window = (slice(top, top + rows), slice(left, left + CHUNK))
        copies = [
            pltpu.make_async_copy(fresh.at[slot, i], outs[4 * n + i].at[window], out_sem.at[slot, i])
            for i in range(3)
        ]
        return copies + [
            pltpu.make_async_copy(copied.at[slot], outs[4 * n + 3].at[window], out_sem.at[slot, 3])
        ]

    def gradient(name, slot):
        if name in ("down", "out"):
            total = jnp.zeros((rows, CHUNK), f32)
            holds = down_holds if name == "down" else out_holds
            for j in range((down_planes if name == "down" else out_planes).shape[0]):
                total += jnp.where(holds[j] > 0, planes[slot, j].astype(f32), 0.0)
            return total
        lanes = down_planes.shape[1] if name == "up" else HEAD_DIM
        values = [ranks[slot, q].astype(f32) for q in range(QUAD)]
        return jnp.concatenate(
            [
                values[q][:, n * lanes : (n + 1) * lanes]
                for n in range(units // lanes)
                for q in range(QUAD)
            ],
            axis=1,
        )

    for k in range(DEPTH - 1):
        for copy in reads(k):
            copy.start()
    results = adam_update(gains[...], gains_m[...], gains_v[...], gains_sum[...], 0.3)
    for out, result in zip(gains_outs, results):
        out[...] = result
    for k, (name, rate, _, _, _) in enumerate(pieces):
        slot = k % DEPTH
        if k + DEPTH - 1 < len(pieces):
            for copy in reads(k + DEPTH - 1):
                copy.start()
        for copy in reads(k):
            copy.wait()
        if k >= DEPTH:
            for copy in writes(k - DEPTH):
                copy.wait()
        results = adam_update(state[slot, 0], state[slot, 1], state[slot, 2], gradient(name, slot), rate)
        for i in range(3):
            fresh[slot, i] = results[i]
        copied[slot] = results[0].astype(bf16)
        for copy in writes(k):
            copy.start()
    for k in range(len(pieces) - DEPTH, len(pieces)):
        for copy in writes(k):
            copy.wait()


def adam(grps, down_holds, out_holds, down_planes, out_planes, up_ranks, qkv_ranks, gains_sum, gains, states):
    rows = up_ranks.shape[1]
    hbm = pl.BlockSpec(memory_space=pl.ANY)
    vmem = pl.BlockSpec(memory_space=pltpu.VMEM)
    shapes = []
    for array in states[::3]:
        shapes += [jax.ShapeDtypeStruct(array.shape, f32)] * 3
        shapes.append(jax.ShapeDtypeStruct(array.shape, bf16))
    shapes += [jax.ShapeDtypeStruct(gains[0].shape, f32)] * 3
    size = sum(array.size for array in states) // 3
    outs = pl.pallas_call(
        lambda *refs: adam_kernel(grps, *refs),
        in_specs=[pl.BlockSpec(memory_space=pltpu.SMEM)] * 2 + [hbm] * 4 + [vmem] * 4 + [hbm] * 12,
        out_specs=[hbm] * 16 + [vmem] * 3,
        out_shape=shapes,
        scratch_shapes=[
            pltpu.VMEM((DEPTH, 3, rows, CHUNK), f32),
            pltpu.VMEM((DEPTH, grps, rows, CHUNK), bf16),
            pltpu.VMEM((DEPTH, QUAD, rows, CHUNK // QUAD), bf16),
            pltpu.VMEM((DEPTH, 3, rows, CHUNK), f32),
            pltpu.VMEM((DEPTH, rows, CHUNK), bf16),
            pltpu.SemaphoreType.DMA((DEPTH, 4)),
            pltpu.SemaphoreType.DMA((DEPTH, 4)),
        ],
        compiler_params=pltpu.CompilerParams(vmem_limit_bytes=VMEM_LIMIT),
        cost_estimate=pl.CostEstimate(flops=size * 16, bytes_accessed=size * 28, transcendentals=size),
        name="adam",
    )(down_holds, out_holds, down_planes, out_planes, up_ranks, qkv_ranks, gains_sum, *gains, *states)
    return outs[:4], outs[4:8], outs[8:12], outs[12:16], outs[16:]


def on_device(
    tokens,
    cotangent,
    lengths,
    qkv_weight,
    qkv_moment,
    qkv_square,
    out_weight,
    out_moment,
    out_square,
    up_weight,
    up_moment,
    up_square,
    down_weight,
    down_moment,
    down_square,
    norm_gains,
    gains_moment,
    gains_square,
):
    seqs = lax.axis_size("seq")
    grps = lax.axis_size("grp")
    ranks = seqs * QUAD
    own_rows = tokens.shape[1]
    full_rows = own_rows * seqs
    all_rows = full_rows * QUAD
    heads_local = HEADS // ranks
    head_width = heads_local * HEAD_DIM
    units = down_weight.shape[0]
    aligned = out_weight.shape[0] == HEAD_DIM
    tables = rotate_table(full_rows, heads_local)

    positions = lax.axis_index("seq") * own_rows + jnp.arange(own_rows, dtype=jnp.int32)
    own_grad = jnp.where((positions < lengths[0])[:, None], cotangent[0], 0)
    own_gains = norm_gains.shape[1]
    own_facts = jnp.zeros((8, 128), f32)
    own_facts = own_facts.at[:2, :own_gains].set(norm_gains.astype(bf16).astype(f32))
    own_facts = own_facts.at[2].set(lengths[0].astype(f32))

    out_own = out_weight
    if not aligned:
        out_all = lax.all_gather(out_weight.astype(bf16), EVERY, axis=0, tiled=True)
        out_all = out_all.reshape(seqs, heads_local, QUAD, HEAD_DIM, D)
        seat = lax.axis_index("row") * 2 + lax.axis_index("core")
        out_own = lax.dynamic_index_in_dim(
            lax.dynamic_index_in_dim(out_all, lax.axis_index("seq"), 0, False), seat, 1, False
        ).reshape(head_width, D)
    (
        residual,
        gains,
        facts,
        first_norm,
        queries,
        key_vectors,
        value_vectors,
        attended,
        second_norm,
        down_planes,
        hidden,
        grad_both,
        qkv_local,
        up_local,
        out_local,
        down_local,
    ) = forward(
        grps,
        aligned,
        tables,
        own_facts,
        tokens[0],
        own_grad,
        qkv_weight,
        up_weight,
        out_own,
        down_weight,
    )
    if not aligned:
        out_local = out_own
    (
        input_grad,
        block_output,
        gains_total,
        out_planes,
        up_ranks,
        qkv_ranks,
        *_,
    ) = backward(
        grps,
        aligned,
        facts,
        gains,
        tables,
        residual,
        tokens[0],
        own_grad,
        grad_both,
        up_local.reshape(D, -1),
        second_norm,
        first_norm,
        out_local,
        qkv_local.reshape(D, -1),
        (queries, key_vectors, value_vectors, attended),
        hidden,
        down_local,
    )
    if aligned:
        out_sum = out_planes
    else:
        placed_term = jnp.zeros((seqs, QUAD, heads_local, HEAD_DIM, D), bf16)
        placed_term = lax.dynamic_update_slice(
            placed_term,
            out_planes.reshape(1, 1, heads_local, HEAD_DIM, D),
            (lax.axis_index("seq"), seat, 0, 0, 0),
        )
        out_sum = lax.psum_scatter(
            placed_term.transpose(0, 2, 1, 3, 4).reshape(D, D),
            EVERY,
            scatter_dimension=0,
            tiled=True,
        )[None]
    device = ((lax.axis_index("seq") * grps + lax.axis_index("grp")) * 2 + lax.axis_index("row")) * 2
    gains_sum = lax.dynamic_slice(
        gains_total, (0, (device + lax.axis_index("core")) * own_gains), (2, own_gains)
    )
    planes = jnp.arange(grps)
    plane = lax.axis_index("grp")
    holds = ((planes + plane != 3) | (plane % 3 != 0) | (grps != 4)).astype(jnp.int32)
    if grps == 4:
        down_holds = jnp.stack([plane > 0, plane < 3, plane >= 0]).astype(jnp.int32)
    else:
        down_holds = holds
    down_new, out_new, up_new, qkv_new, gains_new = adam(
        grps,
        down_holds,
        holds,
        down_planes,
        out_sum,
        up_ranks,
        qkv_ranks,
        gains_sum,
        (norm_gains, gains_moment, gains_square),
        (
            down_weight,
            down_moment,
            down_square,
            out_weight,
            out_moment,
            out_square,
            up_weight,
            up_moment,
            up_square,
            qkv_weight,
            qkv_moment,
            qkv_square,
        ),
    )
    return (
        block_output[None],
        input_grad[None],
        *qkv_new,
        *out_new,
        *up_new,
        *down_new,
        *gains_new,
    )


def solution(mesh):
    seqs, rest = mesh.shape["seq"], mesh.shape["fsdp"]
    planes = Mesh(
        mesh.devices.reshape(seqs, rest // QUAD, 2, 2), ("seq", "grp", "row", "core")
    )
    rows = P(("grp", "row", "core"), "seq", None)
    shards = P(EVERY, None)
    gains = P(None, EVERY)
    return jax.shard_map(
        on_device,
        mesh=planes,
        in_specs=(rows, rows, P(("grp", "row", "core"))) + (shards,) * 12 + (gains,) * 3,
        out_specs=(rows, rows) + (shards,) * 16 + (gains,) * 3,
        check_vma=False,
    )
```

```python
import math

import jax
import jax.numpy as jnp
from jax import lax
from jax.experimental import pallas as pl
from jax.experimental.pallas import tpu as pltpu
from jax.sharding import Mesh, PartitionSpec as P

D = 2048
HEADS = 32
HEAD_DIM = 64
FF = 4096
WINDOW = 128
STEP = 5


NORM_EPSILON = 1e-05
MOMENT_DECAY = 0.5
WEIGHT_DECAY = 0.1
ADAM_EPSILON = 1e-08

SEATS = ("row", "core", "seq")
RANKS = ("seq", "row", "core")
EVERY = ("seq", "grp", "row", "core")
QUAD = 4
VMEM_LIMIT = 63 * 2**20

bf16 = jnp.bfloat16
f32 = jnp.float32


def rotate_table(length, copies):
    halves = HEAD_DIM // 2
    freqs = jnp.exp(-math.log(10000.0) * 2.0 * jnp.arange(halves).astype(f32) / HEAD_DIM)
    angles = jnp.arange(length, dtype=jnp.int32).astype(f32)[:, None] * freqs[None, :]
    cosine, sine = jnp.cos(angles), jnp.sin(angles)
    return (
        jnp.tile(jnp.concatenate([cosine, cosine], axis=1), (1, copies)),
        jnp.tile(jnp.concatenate([-sine, sine], axis=1), (1, copies)),
    )


def adam_update(weight, moment, square, gradient, step_rate):
    moment_new = MOMENT_DECAY * moment + (1.0 - MOMENT_DECAY) * gradient
    square_new = MOMENT_DECAY * square + (1.0 - MOMENT_DECAY) * gradient * gradient
    correction = 1.0 - MOMENT_DECAY**STEP
    unbias = 1.0 / correction
    update = (moment_new * unbias) / (jnp.sqrt(square_new * unbias) + ADAM_EPSILON)
    return (weight - step_rate * (update + WEIGHT_DECAY * weight), moment_new, square_new)


def dot(a, b, lhs=1, rhs=0):
    return lax.dot_general(a, b, (((lhs,), (rhs,)), ((), ())), preferred_element_type=f32)


def swap_halves(values, first):
    width = values.shape[1]
    half = HEAD_DIM // 2
    return jnp.where(
        first, pltpu.roll(values, width - half, 1), pltpu.roll(values, half, 1)
    )


def allowed_mask(rows, length):
    row = lax.broadcasted_iota(jnp.int32, (rows, rows), 0)
    col = lax.broadcasted_iota(jnp.int32, (rows, rows), 1)
    return (col <= row) & (row - col < WINDOW) & (col.astype(f32) < length)


def head_lanes(rows, width, head):
    lane = lax.broadcasted_iota(jnp.int32, (rows, width), 1)
    return (lane // HEAD_DIM) == head


def softmax_rows(queries, key_vectors, allowed):
    scores = jnp.where(allowed, dot(queries, key_vectors, 1, 1) * (HEAD_DIM**-0.5), -1e30)
    shifted = jnp.exp(scores - jnp.max(scores, axis=-1, keepdims=True))
    return shifted / jnp.sum(shifted, axis=-1, keepdims=True)


def attention(length, queries, key_vectors, value_vectors):
    rows, width = queries.shape
    allowed = allowed_mask(rows, length)
    total = jnp.zeros((rows, width), f32)
    for head in range(width // HEAD_DIM):
        mine = head_lanes(rows, width, head)
        weights = softmax_rows(jnp.where(mine, queries, 0), key_vectors, allowed)
        total += dot(weights.astype(bf16), jnp.where(mine, value_vectors, 0))
    return total.astype(bf16)


def attention_grads(length, queries, key_vectors, value_vectors, grads):
    rows, width = queries.shape
    allowed = allowed_mask(rows, length)
    grad_q = jnp.zeros((rows, width), f32)
    grad_k = jnp.zeros((rows, width), f32)
    grad_v = jnp.zeros((rows, width), f32)
    for head in range(width // HEAD_DIM):
        mine = head_lanes(rows, width, head)
        q_head = jnp.where(mine, queries, 0)
        g_head = jnp.where(mine, grads, 0)
        weights = softmax_rows(q_head, key_vectors, allowed)
        grad_p = dot(g_head, value_vectors, 1, 1)
        delta = jnp.sum(weights * grad_p, axis=-1, keepdims=True)
        grad_s = jnp.where(allowed, weights * (grad_p - delta), 0.0).astype(bf16)
        grad_q += dot(grad_s, jnp.where(mine, key_vectors, 0))
        grad_k += dot(grad_s, q_head, 0, 0)
        grad_v += dot(weights.astype(bf16), g_head, 0, 0)
    return grad_q, grad_k, grad_v


MESH = pl.DeviceIdType.MESH
RELATIONS = tuple((a, b, d) for a in range(2) for b in range(2) for d in range(2))[1:]


class Place:
    def __init__(self, grps):
        self.grps = grps
        self.s = lax.axis_index("seq")
        self.g = lax.axis_index("grp")
        self.r = lax.axis_index("row")
        self.c = lax.axis_index("core")

    def peer(self, relation):
        ds, dr, dc = relation
        return ((self.s + ds) % 2, self.g, (self.r + dr) % 2, (self.c + dc) % 2)

    def plane(self, dz):
        return (self.s, (self.g + dz) % self.grps, self.r, self.c)

    def rank(self, relation=(0, 0, 0)):
        s, _, r, c = self.peer(relation)
        return (s * 2 + r) * 2 + c

    def seat(self, relation=(0, 0, 0)):
        s, _, r, c = self.peer(relation)
        return (r * 2 + c) * 2 + s

    def corner(self, relation=(0, 0, 0)):
        s, _, r, _ = self.peer(relation)
        return r * 2 + s

    def greet(self):
        barrier = pltpu.get_barrier_semaphore()
        for relation in RELATIONS:
            pl.semaphore_signal(barrier, inc=1, device_id=self.peer(relation), device_id_type=MESH)
        for dz in range(1, self.grps):
            pl.semaphore_signal(barrier, inc=1, device_id=self.plane(dz), device_id_type=MESH)
        pl.semaphore_wait(barrier, len(RELATIONS) + self.grps - 1)


SIBLING = (0, 0, 1)
ACROSS = ((1, 0, 0), (0, 1, 0), (1, 1, 0))


def remote(src, dst, send_sem, recv_sem, device):
    return pltpu.make_async_remote_copy(
        src_ref=src,
        dst_ref=dst,
        send_sem=send_sem,
        recv_sem=recv_sem,
        device_id=device,
        device_id_type=MESH,
    )


class PlaneSum:
    def __init__(self, place, part, near, far, sems):
        self.place, self.part, self.nears, self.fars = place, part, near, far
        self.near_send, self.near_recv, self.far_send, self.far_recv = sems
        self.first, self.second = [None] * 4, []

    def sequence(self, k):
        place = self.place
        row = (place.r + 1) % 2 if k < 2 else place.r
        return row * 2 + ((place.c + 1) % 2 if k % 2 == 0 else place.c)

    def near(self, k):
        for s in range(2):
            copy = remote(
                self.part.at[2 * self.sequence(k) + s],
                self.nears.at[k + s],
                self.near_send.at[k + s],
                self.near_recv.at[k + s],
                self.place.peer(SIBLING),
            )
            copy.start()
            self.first[k + s] = copy

    def far(self, k):
        place = self.place
        for s in range(2):
            self.first[k - 1 + s].wait()
            self.nears[k - 1 + s] = (
                self.part[2 * self.sequence(k) + s].astype(f32)
                + self.nears[k - 1 + s].astype(f32)
            ).astype(bf16)
        for d in (1, 2) if k == 1 else (0,):
            relation = ACROSS[d]
            copy = remote(
                self.nears.at[k - 1 + (place.s + relation[0]) % 2],
                self.fars.at[d],
                self.far_send.at[d],
                self.far_recv.at[d],
                place.peer(relation),
            )
            copy.start()
            self.second.append(copy)

    def finish(self):
        for copy in self.second:
            copy.wait()

    def chunk(self, lanes):
        total = self.nears[2 + self.place.s, :, lanes].astype(f32)
        for d in range(3):
            total += self.fars[d, :, lanes].astype(f32)
        return total


class PlaneGather:
    def __init__(self, place, blocks, send, recv):
        self.place, self.blocks, self.sends, self.recvs = place, blocks, send, recv
        self.copies = [None] * 7

    def send(self, block, sem, relation):
        copy = remote(
            self.blocks.at[block],
            self.blocks.at[block],
            self.sends.at[sem],
            self.recvs.at[sem],
            self.place.peer(relation),
        )
        copy.start()
        self.copies[sem] = copy

    def start(self):
        mine = self.place.seat()
        for d in range(2):
            self.send(mine, d, ACROSS[d])
        self.send(mine, 3, SIBLING)

    def forward(self, d):
        self.copies[d].wait_recv()
        self.send(self.place.seat(ACROSS[d]), 4 + d, SIBLING)
        if d == 0:
            self.send(self.place.seat(), 2, ACROSS[2])

    def sequence(self, k):
        place = self.place
        row = place.r if k < 2 else (place.r + 1) % 2
        return row * 2 + (place.c if k % 2 == 0 else (place.c + 1) % 2)

    def arrive(self, k, forwarded=False):
        if k == 0:
            self.forward(0)
        elif k == 1:
            if not forwarded:
                self.forward(1)
            self.copies[3].wait_recv()
            self.copies[4].wait_recv()
        elif k == 2:
            self.forward(2)
        else:
            self.copies[5].wait_recv()
            self.copies[6].wait_recv()

    def finish(self):
        for copy in self.copies:
            copy.wait_send()


class ToOwners:
    def __init__(self, place, shares, landed, met, stage, send, recv, own):
        self.place, self.shares, self.landed, self.met, self.stage = place, shares, landed, met, stage
        self.send, self.recv, self.own_sem = send, recv, own
        self.line = place.grps == 4
        self.own = pltpu.make_async_copy(shares.at[place.g], landed.at[place.g], own)

    def copy(self, block, landing, sem, recv, target):
        place = self.place
        return remote(
            self.shares.at[block],
            landing,
            self.send.at[sem],
            self.recv.at[recv],
            (place.s, target, place.r, place.c),
        )

    def direct(self, g):
        targets = ((2, 1), (2, 0), (1, 3), (1, 2))[g]
        return [self.copy(t, self.landed.at[g], t, g, t) for t in targets]

    def meeting(self, g):
        far, inner = (3, 1) if g == 0 else (0, 2)
        return self.copy(far, self.met, far, inner, inner)

    def joined(self, g):
        far = 3 if g == 1 else 0
        return self.copy(far, self.landed.at[g], far, g, far)

    def start(self, waits=False):
        place, self.waits = self.place, waits
        self.own.start()
        if self.line:
            for g in range(4):

                @pl.when(place.g == g)
                def _():
                    if g in (0, 3):
                        self.meeting(g).start()
                    if g in (1, 2) or not waits:
                        for copy in self.direct(g):
                            copy.start()

        else:
            self.copies = [
                self.copy((place.g + dz) % place.grps, self.landed.at[place.g], dz, dz, (place.g + dz) % place.grps)
                for dz in range(1, place.grps)
            ]
            for copy in self.copies:
                copy.start()
        return self

    def proceed(self):
        if self.line:
            for g in (0, 3):

                @pl.when(self.place.g == g)
                def _():
                    self.meeting(g).wait_send()
                    for copy in self.direct(g):
                        copy.start()

    def join(self):
        if not self.line:
            return
        for g in (1, 2):

            @pl.when(self.place.g == g)
            def _():
                outer, far = (0, 3) if g == 1 else (3, 0)
                self.copy(far, self.met, far, g, outer).wait_recv()
                copy = pltpu.make_async_copy(self.met, self.stage, self.own_sem)
                self.own.wait()
                copy.start()
                copy.wait()
                if len(self.stage.shape) == 2:
                    self.shares[far] = (
                        self.shares[far].astype(f32) + self.stage[...].astype(f32)
                    ).astype(bf16)
                else:
                    for n in range(self.stage.shape[0]):
                        self.shares[far, n] = (
                            self.shares[far, n].astype(f32) + self.stage[n].astype(f32)
                        ).astype(bf16)
                self.joined(g).start()

        for g in (0, 3):

            @pl.when(self.place.g == g)
            def _():
                self.own.wait()

    def sent(self):
        if not self.line:
            for copy in self.copies:
                copy.wait_send()
            return
        for g in range(4):

            @pl.when(self.place.g == g)
            def _():
                for copy in self.direct(g):
                    copy.wait_send()
                if g in (1, 2):
                    self.joined(g).wait_send()
                elif not self.waits:
                    self.meeting(g).wait_send()

    def received(self):
        if not self.line:
            self.own.wait()
            for copy in self.copies:
                copy.wait_recv()
            return
        for g in range(4):

            @pl.when(self.place.g == g)
            def _():
                for j in ((1, 2), (0, 2, 3), (0, 1, 3), (1, 2))[g]:
                    self.copy(g, self.landed.at[j], j, j, j).wait_recv()

    def finish(self):
        self.sent()
        self.received()

    def holds(self, j):
        g = self.place.g
        return (g % 3 != 0) | (j + g != 3) if self.line else True


class Exchange:
    def __init__(self, place, blocks, held, send, recv, own):
        mine = place.rank()
        kept = held.at[mine // QUAD, mine % QUAD] if len(held.shape) == 4 else held.at[mine]

        def block(t):
            return blocks.at[0, t // QUAD, t % QUAD] if len(blocks.shape) == 5 else blocks.at[t]

        self.copies = []
        for n, relation in enumerate(RELATIONS):
            copy = remote(
                block(place.rank(relation)),
                kept,
                send.at[n],
                recv.at[n],
                place.peer(relation),
            )
            copy.start()
            self.copies.append(copy)
        copy = pltpu.make_async_copy(block(mine), kept, own)
        copy.start()
        self.copies.append(copy)

    def finish(self):
        for copy in self.copies:
            copy.wait()


LANES = 512


def lanes_of(n, width=LANES):
    return pl.ds(pl.multiple_of(n * width, width), width)


def shares_of(seq, values, weight, part):
    rows = part.shape[1]

    @pl.loop(0, part.shape[2] // LANES)
    def _(n):
        product = dot(values[seq], weight[lanes_of(n)], 1, 1)
        part[2 * seq, :, lanes_of(n)] = product[:rows].astype(bf16)
        part[2 * seq + 1, :, lanes_of(n)] = product[rows:].astype(bf16)


def over_tokens(first, lanes, second, other):
    total = dot(first[0, :, lanes], second[0, :, other], 0, 0)
    for seq in range(1, first.shape[0]):
        total += dot(first[seq, :, lanes], second[seq, :, other], 0, 0)
    return total


def row_shares(first, second, shares):
    grps, seqs, rows, _ = shares.shape
    width = 256
    pieces = width // rows

    @pl.loop(0, first.shape[2] // width)
    def _(b):
        product = over_tokens(first, lanes_of(b, width), second, slice(None)).astype(bf16)
        for p in range(pieces):
            index = b * pieces + p
            shares[index % grps, index // grps] = product[p * rows : (p + 1) * rows]


def summed_rows(landed, holds, blocks):
    seqs, rows = landed.shape[1], blocks.shape[1]
    for seq in range(seqs):
        for quad in range(QUAD):
            block = slice(quad * rows, (quad + 1) * rows)
            total = jnp.zeros((rows, landed.shape[3]), f32)
            for j in range(landed.shape[0]):
                total += jnp.where(holds(j), landed[j, seq, block].astype(f32), 0.0)
            blocks[seq * QUAD + quad] = total.astype(bf16)


def back_kernel(
    grps,
    aligned,
    facts,
    gains,
    cosine,
    sine,
    residual,
    own_tokens,
    own_grad,
    dgu_h,
    up_h,
    down_share_h,
    second_h,
    first_h,
    out_h,
    qkv_h,
    q_h,
    k_h,
    v_h,
    o_h,
    hidden_h,
    down_h,
    input_grad,
    block_output,
    gains_sum,
    down_landed,
    out_landed,
    up_held,
    qkv_held,
    up_landed,
    qkv_landed,
    down_met,
    up_met,
    out_met,
    qkv_met,
    wide,
    up,
    acts,
    out_w,
    qkv,
    part,
    near,
    far,
    blocks,
    turned,
    down_share,
    up_share,
    out_share,
    qkv_share,
    up_sum,
    qkv_sum,
    stage_down,
    stage_low,
    stage_wide,
    gain_part,
    gain_plane,
    gain_far,
    load,
    near_send,
    near_recv,
    far_send,
    far_recv,
    all_send,
    all_recv,
    z_send,
    z_recv,
    swap_send,
    swap_recv,
    gain_send,
    gain_recv,
    own_sem,
    near_free,
    far_free,
):
    place = Place(grps)
    rows = residual.shape[0]
    gain_part[...] = jnp.zeros_like(gain_part)
    count, full_rows, head_width = q_h.shape

    def fetch(src, dst, n):
        copy = pltpu.make_async_copy(src, dst, load.at[n])
        copy.start()
        return copy

    loads = [fetch(dgu_h, wide, 0), fetch(up_h, up, 1), fetch(down_share_h, down_share, 2)]
    later = fetch(second_h, acts, 3)
    weights = [fetch(out_h, out_w, 5), fetch(qkv_h, qkv, 6)]
    place.greet()
    for copy in loads:
        copy.wait()

    sums = (near_send, near_recv, far_send, far_recv)
    def to_owners(n, shares, landed, met, stage, waits=False):
        return ToOwners(
            place, shares, landed, met, stage, z_send.at[n], z_recv.at[n], own_sem.at[n]
        ).start(waits)

    def summed_over_plane(values, weight):
        total = PlaneSum(place, part, near, far, sums)
        for k in range(4):
            shares_of(total.sequence(k), values, weight, part)
            if k % 2 == 0:
                total.near(k)
            else:
                total.far(k)
        return total

    down_out = to_owners(0, down_share, down_landed, down_met, stage_down)
    second_sum = summed_over_plane(wide, up)
    later.wait()
    row_shares(acts, wide, up_share)
    up_out = to_owners(1, up_share, up_landed, up_met, stage_wide, True)
    down_out.join()
    fetch_first = fetch(first_h, acts, 3)
    heads = [
        fetch(ref, wide.at[:, :, n * head_width : (n + 1) * head_width], 7 + n)
        for n, ref in enumerate((q_h, k_h, v_h, o_h))
    ]

    half = hidden_h.shape[2]
    hidden = turned.at[:, :, :half]
    last = [fetch(hidden_h, hidden, 11)]
    for n in range(2):
        columns = slice(n * D // 2, (n + 1) * D // 2)
        last.append(fetch(down_h.at[:, columns], up.at[n * half : (n + 1) * half, : D // 2], 12 + n))
    second_sum.finish()
    mine = place.seat()
    inner = jnp.zeros((rows, 1), f32)
    squares = jnp.zeros((rows, 1), f32)
    for n in range(D // LANES):
        lanes = slice(n * LANES, (n + 1) * LANES)
        grad = second_sum.chunk(lanes)
        values = residual[:, lanes]
        inner += jnp.sum(grad * gains[1:2, lanes] * values, axis=-1, keepdims=True)
        squares += jnp.sum(values * values, axis=-1, keepdims=True)
    scale = lax.rsqrt(squares / D + NORM_EPSILON)
    inner = inner / D
    for n in range(D // LANES):
        lanes = slice(n * LANES, (n + 1) * LANES)
        grad, values = second_sum.chunk(lanes), residual[:, lanes]
        gain_part[1:2, lanes] = jnp.sum(grad * values * scale, axis=0, keepdims=True)
        total = own_grad[:, lanes].astype(f32) + scale * (
            grad * gains[1:2, lanes] - values * scale * scale * inner
        )
        input_grad[:, lanes] = total
        blocks[mine, :, lanes] = total.astype(bf16)

    gather = PlaneGather(place, blocks, all_send, all_recv)
    gather.start()
    for copy in weights + heads:
        copy.wait()

    lane = lax.broadcasted_iota(jnp.int32, (full_rows, head_width), 1)
    first_half = (lane % HEAD_DIM) < HEAD_DIM // 2

    for copy in last:
        copy.wait()

    @pl.loop(0, count)
    def _(seq):
        for n in range(D // LANES):
            top, left = n * LANES // (D // 2) * half, n * LANES % (D // 2)
            product = dot(hidden[seq], up[top : top + half, left : left + LANES])
            part[2 * seq, :, n * LANES : (n + 1) * LANES] = product[:rows].astype(bf16)
            part[2 * seq + 1, :, n * LANES : (n + 1) * LANES] = product[rows:].astype(bf16)

    up_out.proceed()
    last_sum = PlaneSum(place, part, near, far, sums)
    for k in range(4):
        gather.arrive(k)
        seq = gather.sequence(k)
        grads = jnp.concatenate(
            [dot(blocks[2 * seq], out_w[...], 1, 1), dot(blocks[2 * seq + 1], out_w[...], 1, 1)],
            axis=0,
        ).astype(bf16)
        queries = wide[seq, :, 0:head_width]
        key_vectors = wide[seq, :, head_width : 2 * head_width]
        value_vectors = wide[seq, :, 2 * head_width : 3 * head_width]
        grad_q, grad_k, grad_v = attention_grads(
            facts[seq, 2:3, 0:1], queries, key_vectors, value_vectors, grads
        )
        for n, grad in enumerate((grad_q, grad_k)):
            values = (grad * HEAD_DIM**-0.5).astype(bf16).astype(f32)
            back = values * cosine[...] - swap_halves(values, first_half) * sine[...]
            turned[seq, :, n * head_width : (n + 1) * head_width] = back.astype(bf16)
        turned[seq, :, 2 * head_width : 3 * head_width] = grad_v.astype(bf16)
        if k == 1:
            last_sum.near(0)
            last_sum.near(2)
            up_out.join()
        elif k == 2:
            last_sum.far(1)
            last_sum.far(3)

    gather.finish()
    fetch_first.wait()
    row_shares(acts, turned, qkv_share)
    triple = turned.shape[2]
    qkv_out = to_owners(2, qkv_share, qkv_landed, qkv_met, stage_wide.at[:, :, :triple], True)

    out_rows = out_share.shape[1]

    @pl.loop(0, D // LANES)
    def _(n):
        lanes = lanes_of(n)
        total = jnp.zeros((head_width, LANES), f32)
        for seq in range(count):
            values = wide[seq, :, 3 * head_width : 4 * head_width].astype(f32)
            total += dot(values[:rows].astype(bf16), blocks[2 * seq, :, lanes], 0, 0)
            total += dot(values[rows:].astype(bf16), blocks[2 * seq + 1, :, lanes], 0, 0)
        total = total.astype(bf16)
        for j in range(out_share.shape[0]):
            out_share[j, :, lanes] = total[j * out_rows : (j + 1) * out_rows]

    last_sum.finish()
    for n in range(D // LANES):
        lanes = slice(n * LANES, (n + 1) * LANES)
        block_output[:, lanes] = (residual[:, lanes] + last_sum.chunk(lanes)).astype(bf16)
    pl.semaphore_signal(near_free, inc=1, device_id=place.peer(SIBLING), device_id_type=MESH)
    for relation in ACROSS:
        pl.semaphore_signal(far_free, inc=1, device_id=place.peer(relation), device_id_type=MESH)
    pl.semaphore_wait(near_free, 1)
    pl.semaphore_wait(far_free, 3)
    first_sum = summed_over_plane(turned, qkv)
    qkv_out.proceed()
    qkv_out.join()
    first_sum.finish()
    inner = jnp.zeros((rows, 1), f32)
    squares = jnp.zeros((rows, 1), f32)
    for n in range(D // LANES):
        lanes = slice(n * LANES, (n + 1) * LANES)
        grad = first_sum.chunk(lanes)
        values = own_tokens[:, lanes].astype(f32)
        inner += jnp.sum(grad * gains[0:1, lanes] * values, axis=-1, keepdims=True)
        squares += jnp.sum(values * values, axis=-1, keepdims=True)
    scale = lax.rsqrt(squares / D + NORM_EPSILON)
    inner = inner / D
    for n in range(D // LANES):
        lanes = slice(n * LANES, (n + 1) * LANES)
        grad, values = first_sum.chunk(lanes), own_tokens[:, lanes].astype(f32)
        gain_part[0:1, lanes] = jnp.sum(grad * values * scale, axis=0, keepdims=True)
        input_grad[:, lanes] += scale * (
            grad * gains[0:1, lanes] - values * scale * scale * inner
        )

    gain_copies = []
    for n, relation in enumerate(RELATIONS):
        copy = remote(
            gain_part, gain_plane.at[n], gain_send.at[n], gain_recv.at[n], place.peer(relation)
        )
        copy.start()
        gain_copies.append(copy)

    up_out.finish()
    landed = pltpu.make_async_copy(up_landed, up_share, load.at[1])
    landed.start()
    for copy in gain_copies:
        copy.wait()
    total = gain_part[...]
    for n in range(len(RELATIONS)):
        total += gain_plane[n]
    gain_far[0] = total
    gain_copies = []
    for dz in range(1, grps):
        copy = remote(
            gain_far.at[0],
            gain_far.at[dz],
            gain_send.at[7 + dz],
            gain_recv.at[7 + dz],
            place.plane(dz),
        )
        copy.start()
        gain_copies.append(copy)
    landed.wait()
    summed_rows(up_share, up_out.holds, up_sum)
    up_swap = Exchange(place, up_sum, up_held, swap_send.at[0], swap_recv.at[0], own_sem.at[4])
    for copy in gain_copies:
        copy.wait()
    total = gain_far[0]
    for dz in range(1, grps):
        total += gain_far[dz]
    gains_sum[...] = total

    qkv_out.sent()
    if aligned:
        out_out = to_owners(3, out_share, out_landed, out_met, stage_low)
    else:
        out_out = pltpu.make_async_copy(out_share, out_landed, own_sem.at[3])
        out_out.start()
    qkv_out.received()
    landed = pltpu.make_async_copy(qkv_landed, qkv_share, load.at[6])
    landed.start()
    landed.wait()
    summed_rows(qkv_share, qkv_out.holds, qkv_sum)
    qkv_swap = Exchange(place, qkv_sum, qkv_held, swap_send.at[1], swap_recv.at[1], own_sem.at[5])
    if aligned:
        out_out.join()
    if aligned:
        out_out.finish()
    else:
        out_out.wait()
    down_out.finish()
    up_swap.finish()
    qkv_swap.finish()


def backward(
    grps,
    aligned,
    facts,
    gains,
    tables,
    residual,
    own_tokens,
    own_grad,
    grad_both,
    up_local,
    down_share,
    second_norm,
    first_norm,
    out_local,
    qkv_local,
    heads,
    hidden,
    down_local,
):
    rows = residual.shape[0]
    count, full_rows, head_width = heads[0].shape
    seqs = full_rows // rows
    ranks = seqs * QUAD
    both = grad_both.shape[2]
    down_shape = down_share.shape[1:]
    quad_rows = D // (seqs * grps)
    shard = quad_rows // QUAD
    out_rows = head_width // grps if aligned else HEAD_DIM
    triple = 3 * head_width
    out_count = head_width // out_rows
    hbm = pl.BlockSpec(memory_space=pl.ANY)
    vmem = pl.BlockSpec(memory_space=pltpu.VMEM)
    shape = jax.ShapeDtypeStruct
    dma = pltpu.SemaphoreType.DMA
    return pl.pallas_call(
        lambda *refs: back_kernel(grps, aligned, *refs),
        in_specs=[vmem] * 7 + [hbm] * 13,
        out_specs=[vmem] * 3 + [hbm] * 10,
        out_shape=[
            shape((rows, D), f32),
            shape((rows, D), bf16),
            shape((8, D), f32),
            shape((grps, *down_shape), bf16),
            shape((out_count, out_rows, D), bf16),
            shape((ranks, shard, both), bf16),
            shape((ranks, shard, triple), bf16),
            shape((grps, seqs, quad_rows, both), bf16),
            shape((grps, seqs, quad_rows, triple), bf16),
            shape(down_shape, bf16),
            shape((seqs, quad_rows, both), bf16),
            shape((out_rows, D), bf16),
            shape((seqs, quad_rows, triple), bf16),
        ],
        scratch_shapes=[
            pltpu.VMEM((count, full_rows, both), bf16),
            pltpu.VMEM((D, both), bf16),
            pltpu.VMEM((count, full_rows, D), bf16),
            pltpu.VMEM((head_width, D), bf16),
            pltpu.VMEM((D, triple), bf16),
            pltpu.VMEM((ranks, rows, D), bf16),
            pltpu.VMEM((4, rows, D), bf16),
            pltpu.VMEM((3, rows, D), bf16),
            pltpu.VMEM((ranks, rows, D), bf16),
            pltpu.VMEM((count, full_rows, triple), bf16),
            pltpu.VMEM((grps, *down_shape), bf16),
            pltpu.VMEM((grps, seqs, quad_rows, both), bf16),
            pltpu.VMEM((out_count, out_rows, D), bf16),
            pltpu.VMEM((grps, seqs, quad_rows, triple), bf16),
            pltpu.VMEM((ranks, shard, both), bf16),
            pltpu.VMEM((ranks, shard, triple), bf16),
            pltpu.VMEM(down_shape, bf16),
            pltpu.VMEM((out_rows, D), bf16),
            pltpu.VMEM((seqs, quad_rows, both), bf16),
            pltpu.VMEM((8, D), f32),
            pltpu.VMEM((7, 8, D), f32),
            pltpu.VMEM((grps, 8, D), f32),
            dma((14,)),
            dma((4,)),
            dma((4,)),
            dma((3,)),
            dma((3,)),
            dma((7,)),
            dma((7,)),
            dma((4, grps)),
            dma((4, grps)),
            dma((2, 7)),
            dma((2, 7)),
            dma((7 + grps,)),
            dma((7 + grps,)),
            dma((6,)),
            pltpu.SemaphoreType.REGULAR,
            pltpu.SemaphoreType.REGULAR,
        ],
        compiler_params=pltpu.CompilerParams(
            collective_id=0, has_side_effects=True, vmem_limit_bytes=VMEM_LIMIT
        ),
        cost_estimate=pl.CostEstimate(
            flops=30 * 10**9, bytes_accessed=60 * 2**20, transcendentals=2 * 10**6
        ),
        name="backward",
    )(
        facts,
        gains,
        *tables,
        residual,
        own_tokens,
        own_grad,
        grad_both,
        up_local,
        down_share,
        second_norm,
        first_norm,
        out_local,
        qkv_local,
        *heads,
        hidden,
        down_local,
    )


CHUNK = 1024


class FromOwners:
    def __init__(self, place, source, landed, landing, send, recv, own):
        self.place, self.source, self.send, self.recv = place, source, send, recv
        self.slot = lambda j: landing(landed, j)
        self.own = pltpu.make_async_copy(source, self.slot(place.g), own)
        self.line = place.grps == 4

    def copy(self, source, slot, sem, recv, target):
        place = self.place
        return remote(
            source, self.slot(slot), self.send.at[sem], self.recv.at[recv], (place.s, target, place.r, place.c)
        )

    def passed(self, g, j, target):
        source = self.source if j == g else self.slot(j)
        return self.copy(source, j, j + (4 if target > g else 0), j, target)

    def arrived(self, j):
        self.copy(self.source, j, j, j, j).wait_recv()

    def on_line(self, steps):
        for g in range(4):
            if steps[g]:

                @pl.when(self.place.g == g)
                def _():
                    for awaited, j, target in steps[g]:
                        if awaited is not None:
                            self.arrived(awaited)
                        if target is not None:
                            self.passed(g, j, target).start()

    FIRST = (
        ((None, 0, 1),),
        ((None, 1, 0), (None, 1, 2)),
        ((None, 2, 3), (None, 2, 1)),
        ((None, 3, 2),),
    )
    SECOND = (
        ((1, 1, None),),
        ((2, 2, 0), (0, 0, 2)),
        ((1, 1, 3), (3, 3, 1)),
        ((2, 2, None),),
    )
    THIRD = ((), ((3, 3, 0),), ((0, 0, 3),), ())

    def start(self):
        place = self.place
        self.own.start()
        if self.line:
            self.on_line(self.FIRST)
        else:
            self.copies = [
                self.copy(self.source, place.g, dz, dz, (place.g + dz) % place.grps)
                for dz in range(1, place.grps)
            ]
            for copy in self.copies:
                copy.start()

    def second(self):
        if self.line:
            self.on_line(self.SECOND)

    def third(self):
        if self.line:
            self.on_line(self.THIRD)

    def finish(self):
        self.own.wait()
        if self.line:
            for g in range(4):

                @pl.when(self.place.g == g)
                def _():
                    for j in {0: (2, 3), 3: (1, 0)}.get(g, ()):
                        self.arrived(j)
                    for steps in (self.FIRST, self.SECOND, self.THIRD):
                        for _, j, target in steps[g]:
                            if target is not None:
                                self.passed(g, j, target).wait_send()

        else:
            for copy in self.copies:
                copy.wait()


class Chain:
    def __init__(self, place, part, through, landed, send, recv, own):
        self.place, self.part, self.through, self.landed = place, part, through, landed
        self.send, self.recv = send, recv
        self.units, self.columns = landed.shape[1:]
        self.own = pltpu.make_async_copy(self.block(part, place.g), landed.at[2], own)

    def block(self, ref, j):
        return ref.at[j, : self.units, : self.columns]

    def copy(self, g, j):
        place, target = self.place, g + 1 if j > g else g - 1
        if target == j:
            landing = self.landed.at[0 if j > g else 1]
        else:
            landing = self.block(self.through, j)
        recv = j if target != j else (j if j > g else 4)
        return remote(
            self.block(self.part, j), landing, self.send.at[j], self.recv.at[recv], (place.s, target, place.r, place.c)
        )

    def each(self, planes, action):
        for g in planes:

            @pl.when(self.place.g == g)
            def _():
                action(g)

    def blocks(self, g):
        return (3, 2, 1) if g == 0 else (0, 1, 2)

    def start(self):
        self.own.start()
        self.each((0, 3), lambda g: self.copy(g, self.blocks(g)[0]).start())

    def add(self, g, source, j):
        self.copy(source, j).wait_recv()
        area = (j, slice(0, self.units), slice(0, self.columns))
        self.part[area] = (self.part[area].astype(f32) + self.through[area].astype(f32)).astype(bf16)
        self.copy(g, j).start()

    def step(self, n):
        def ends(g):
            self.copy(g, self.blocks(g)[n - 1]).wait_send()
            self.copy(g, self.blocks(g)[n]).start()

        def inner(g):
            end = 0 if g == 1 else 3
            self.add(g, end, self.blocks(end)[n - 1])

        self.each((0, 3), ends)
        self.each((1, 2), inner)

    def last(self):
        self.each((1, 2), lambda g: self.add(g, 3 - g, 0 if g == 1 else 3))

    def finish(self):
        self.own.wait()

        def done(g):
            if g > 0:
                self.copy(g - 1, g).wait_recv()
            if g < 3:
                self.copy(g + 1, g).wait_recv()
            if g in (0, 3):
                self.copy(g, self.blocks(g)[2]).wait_send()
            else:
                for j in range(4):
                    if j != g:
                        self.copy(g, j).wait_send()

        self.each(range(4), done)


def shares_from(seq, values, weight, part):
    rows = part.shape[1]

    @pl.loop(0, part.shape[2] // LANES)
    def _(n):
        product = dot(values[seq], weight[:, lanes_of(n)])
        part[2 * seq, :, lanes_of(n)] = product[:rows].astype(bf16)
        part[2 * seq + 1, :, lanes_of(n)] = product[rows:].astype(bf16)


def times_slices(values, weight, lanes):
    seqs, grps, quad, shard, _ = weight.shape
    depth = quad * shard
    total = None
    for n in range(seqs * grps):
        piece = weight[n // grps, n % grps, :, :, lanes]
        term = dot(values[:, n * depth : (n + 1) * depth], piece.reshape(depth, piece.shape[2]))
        total = term if total is None else total + term
    return total


def both_blocks(blocks, seq):
    return jnp.concatenate([blocks[2 * seq].astype(f32), blocks[2 * seq + 1].astype(f32)], axis=0)


def forward_kernel(
    grps,
    aligned,
    cosine,
    sine,
    own_facts,
    tokens_h,
    own_grad_h,
    qkv_own,
    up_own,
    out_own,
    down_own,
    residual,
    gains,
    facts,
    first_h,
    q_h,
    k_h,
    v_h,
    o_h,
    second_h,
    grads_landed,
    down_share_h,
    hidden_h,
    dgu_h,
    qkv_landed,
    up_landed,
    out_landed,
    down_landed,
    blocks,
    grad_blocks,
    norm,
    grad_seq,
    qkv_rank,
    up_rank,
    qkv,
    up,
    out_w,
    down,
    heads,
    part,
    near,
    far,
    both,
    hidden,
    dgu,
    all_facts,
    early,
    load,
    store,
    swap_send,
    swap_recv,
    near_send,
    near_recv,
    far_send,
    far_recv,
    all_send,
    all_recv,
    z_send,
    z_recv,
    fact_send,
    fact_recv,
    chain_send,
    chain_recv,
    own_sem,
):
    place = Place(grps)
    count, full_rows, _ = norm.shape
    rows = residual.shape[0]
    head_width = heads.shape[3]
    mine, rank = place.seat(), place.rank()

    def fetch(src, dst, n):
        copy = pltpu.make_async_copy(src, dst, load.at[n])
        copy.start()
        return copy

    def keep(src, dst, n):
        copy = pltpu.make_async_copy(src, dst, store.at[n])
        copy.start()
        return copy

    shard = qkv_own.shape[0]
    units = down.shape[0] // grps
    seqs = qkv_landed.shape[0]
    slots = iter(range(20))

    def fetch_chunks(src):
        pieces = []
        for top in range(0, src.shape[0], shard):
            for left in range(0, src.shape[1], CHUNK):
                slot = next(slots)
                space = both.at[slot // 5, (slot % 5) * shard : (slot % 5 + 1) * shard]
                copy = pltpu.make_async_copy(
                    src.at[top : top + shard, left : left + CHUNK], space, early.at[slot]
                )
                copy.start()
                pieces.append((copy, space))
        return pieces

    def dealt(pieces, weight, lanes, parts):
        count = CHUNK // (QUAD * lanes)
        width = count * lanes
        each = len(pieces) // (parts * seqs)
        for n, (copy, space) in enumerate(pieces):
            copy.wait()
            values = space[...]
            seq = n // each % seqs
            first = (n // (each * seqs) * each + n % each) * width
            for q in range(QUAD):
                taken = [
                    values[:, (k * QUAD + q) * lanes : (k * QUAD + q + 1) * lanes] for k in range(count)
                ]
                weight[0, seq, q, :, first : first + width] = jnp.concatenate(taken, axis=1).astype(bf16)

    facts[rank] = own_facts[...]
    if aligned:
        out_pieces = fetch_chunks(out_own)
    qkv_pieces = fetch_chunks(qkv_own)
    up_pieces = fetch_chunks(up_own)
    down_pieces = fetch_chunks(down_own)
    own_blocks = [fetch(tokens_h, blocks.at[mine], 0), fetch(own_grad_h, grad_blocks.at[mine], 1)]

    def plane_rows(ref, j):
        return ref.at[:, j]

    def own_rows(ref, j):
        size = ref.shape[0] // grps
        return ref.at[pl.ds(pl.multiple_of(j * size, size), size)]

    def rows_of(ref, j):
        top = j * units
        return ref.at[top // 128, pl.ds(pl.multiple_of(top % 128, units), units), : D // 2]

    def from_owners(n, source, landed, landing):
        return FromOwners(place, source, landed, landing, z_send.at[n], z_recv.at[n], own_sem.at[n])

    def stacked(pieces, weight):
        across = weight.shape[1] // CHUNK
        for n, (copy, space) in enumerate(pieces):
            copy.wait()
            top, left = n // across * shard, n % across * CHUNK
            weight[top : top + shard, left : left + CHUNK] = space[...].astype(bf16)

    down_z = from_owners(3, down.at[:units], down_landed, own_rows)
    if aligned:
        stacked(out_pieces, out_w)
        out_z = from_owners(2, out_w.at[:shard], out_landed, own_rows)
    place.greet()
    if aligned:
        out_z.start()
    dealt(qkv_pieces, qkv, HEAD_DIM, 3)
    qkv_swap = Exchange(place, qkv, qkv_rank, swap_send.at[0], swap_recv.at[0], own_sem.at[4])
    fact_copies = []
    for n, relation in enumerate(RELATIONS):
        copy = remote(own_facts, facts.at[rank], fact_send.at[n], fact_recv.at[n], place.peer(relation))
        copy.start()
        fact_copies.append(copy)
    if aligned:
        out_z.second()
    dealt(up_pieces, up, units, 2)
    stacked(down_pieces, down)
    for copy in own_blocks:
        copy.wait()
    if aligned:
        out_z.third()
    qkv_swap.finish()
    qkv_z = from_owners(0, qkv_rank, qkv_landed, plane_rows)
    up_z = from_owners(1, up_rank, up_landed, plane_rows)
    qkv_z.start()
    token_gather = PlaneGather(place, blocks, all_send.at[0], all_recv.at[0])
    token_gather.start()
    for copy in fact_copies:
        copy.wait()
    all_facts[place.g] = facts[...]
    fact_copies = []
    for dz in range(1, grps):
        copy = remote(
            facts,
            all_facts.at[place.g],
            fact_send.at[7 + dz],
            fact_recv.at[7 + dz],
            place.plane(dz),
        )
        copy.start()
        fact_copies.append(copy)
    for copy in fact_copies:
        copy.wait()
    width = D // (seqs * grps * QUAD)
    for n in range(seqs * grps):
        pieces = [all_facts[n % grps, (n // grps) * QUAD + q, :, :width] for q in range(QUAD)]
        gains[:, n * QUAD * width : (n + 1) * QUAD * width] = jnp.concatenate(pieces, axis=1)
    token_gather.forward(0)
    token_gather.forward(1)
    up_swap = Exchange(place, up, up_rank, swap_send.at[1], swap_recv.at[1], own_sem.at[5])
    qkv_z.second()
    token_gather.forward(2)
    token_gather.arrive(3)
    token_gather.copies[3].wait_recv()
    token_gather.copies[4].wait_recv()
    token_gather.finish()

    @pl.loop(0, count)
    def _(seq):
        values = both_blocks(blocks, seq)
        scale = lax.rsqrt(jnp.mean(values * values, axis=-1, keepdims=True) + NORM_EPSILON)
        norm[seq] = (values * scale * gains[0:1, :]).astype(bf16)

    stores = [keep(norm, first_h, 0)]
    grad_gather = PlaneGather(place, grad_blocks, all_send.at[1], all_recv.at[1])
    grad_gather.start()
    qkv_z.third()
    up_swap.finish()
    qkv_z.finish()
    up_z.start()
    fetch(qkv_landed, qkv, 2).wait()

    lane = lax.broadcasted_iota(jnp.int32, (full_rows, head_width), 1)
    first_half = (lane % HEAD_DIM) < HEAD_DIM // 2

    if aligned:
        out_z.finish()
        fetch(out_landed, out_w, 3).wait()
    else:
        fetch(out_own, out_w, 3).wait()

    plane_sum = PlaneSum(place, part, near, far, (near_send, near_recv, far_send, far_recv))
    mixed = heads.at[3]
    for k in range(4):
        seq = plane_sum.sequence(k)
        for n in range(3):
            lanes = slice(n * head_width, (n + 1) * head_width)
            values = times_slices(norm[seq], qkv, lanes)
            if n < 2:
                values = values * cosine[...] + swap_halves(values, first_half) * sine[...]
            heads[n, seq] = values.astype(bf16)
        heads[3, seq] = attention(facts[seq, 2:3, 0:1], heads[0, seq], heads[1, seq], heads[2, seq])
        shares_from(seq, mixed, out_w, part)
        if k % 2 == 0:
            plane_sum.near(k)
        else:
            plane_sum.far(k)
        if k == 0:
            grad_gather.forward(0)
            grad_gather.forward(1)
    grad_gather.forward(2)
    grad_gather.arrive(3)
    grad_gather.copies[3].wait_recv()
    grad_gather.copies[4].wait_recv()
    grad_gather.finish()
    stores += [keep(heads.at[n], ref, 1 + n) for n, ref in enumerate((q_h, k_h, v_h, o_h))]
    up_z.second()

    @pl.loop(0, count)
    def _(seq):
        grad_seq[seq] = both_blocks(grad_blocks, seq).astype(bf16)

    fetch(tokens_h, grad_blocks.at[mine], 4).wait()
    plane_sum.finish()
    squares = jnp.zeros((rows, 1), f32)
    for n in range(D // LANES):
        lanes = slice(n * LANES, (n + 1) * LANES)
        values = grad_blocks[mine, :, lanes].astype(f32) + plane_sum.chunk(lanes)
        residual[:, lanes] = values
        squares += jnp.sum(values * values, axis=-1, keepdims=True)
    scale = lax.rsqrt(squares / D + NORM_EPSILON)
    for n in range(D // LANES):
        lanes = slice(n * LANES, (n + 1) * LANES)
        blocks[mine, :, lanes] = (residual[:, lanes] * scale * gains[1:2, lanes]).astype(bf16)
    norm_gather = PlaneGather(place, blocks, all_send.at[2], all_recv.at[2])
    norm_gather.start()
    up_z.third()
    stores[0].wait()
    half = hidden.shape[2]
    for k in range(4):
        norm_gather.arrive(k, forwarded=k == 1)
        seq = norm_gather.sequence(k)
        norm[seq] = both_blocks(blocks, seq).astype(bf16)
        if k == 0:
            norm_gather.forward(1)
            up_z.finish()
            down_z.start()
            fetch(up_landed, up, 5).wait()
        elif k == 2:
            down_z.second()
        gate = times_slices(norm[seq], up, slice(0, half))
        above = times_slices(norm[seq], up, slice(half, 2 * half))
        both[seq, :, :half] = gate
        both[seq, :, half:] = above
        hidden[seq] = (gate * jax.nn.sigmoid(gate) * above).astype(bf16)
    norm_gather.finish()
    stores[0] = keep(norm, second_h, 5)
    stores.append(keep(hidden, hidden_h, 7))
    tall = min(256, half)
    slab = part.shape[1] // 128 * 128

    def down_shares(side):
        lanes = slice(side * D // 2, (side + 1) * D // 2)

        @pl.loop(0, half // tall)
        def _(b):
            product = over_tokens(hidden, lanes_of(b, tall), grad_seq, lanes).astype(bf16)
            for p in range(tall // slab):
                part[b * (tall // slab) + p, :slab, lanes] = product[p * slab : (p + 1) * slab]

    down_shares(0)
    if grps == 4:
        chain = Chain(place, part, near, grads_landed, chain_send, chain_recv, own_sem.at[6])
        chain.start()
    else:
        spread = [pltpu.make_async_copy(rows_of(part, place.g), grads_landed.at[place.g], own_sem.at[6])]
        for dz in range(1, grps):
            spread.append(
                remote(
                    rows_of(part, (place.g + dz) % grps),
                    grads_landed.at[place.g],
                    chain_send.at[dz],
                    chain_recv.at[dz],
                    place.plane(dz),
                )
            )
        for copy in spread:
            copy.start()
    down_z.third()
    down_shares(1)
    stores.append(keep(part.at[: half // slab, :slab, D // 2 :], down_share_h, 6))
    down_z.finish()
    fetch(down_landed, down, 6).wait()

    def feed_forward_grads(seq):
        grads = dot(grad_seq[seq], down[...], 1, 1)
        gate, above = both[seq, :, :half], both[seq, :, half:]
        sigmoid = jax.nn.sigmoid(gate)
        dgu[seq, :, :half] = (grads * above * sigmoid * (1.0 + gate * (1.0 - sigmoid))).astype(bf16)
        dgu[seq, :, half:] = (grads * (gate * sigmoid)).astype(bf16)

    pl.loop(0, count // 2)(feed_forward_grads)
    if grps == 4:
        chain.step(1)
    pl.loop(count // 2, count)(feed_forward_grads)
    stores.append(keep(dgu, dgu_h, 8))
    if grps == 4:
        chain.step(2)
        chain.last()
        chain.finish()
    else:
        for copy in spread:
            copy.wait()
    for copy in stores:
        copy.wait()


def forward(grps, aligned, tables, own_facts, tokens, own_grad, qkv_own, up_own, out_own, down_own):
    rows = tokens.shape[0]
    shard = qkv_own.shape[0]
    seqs = D // (shard * grps * QUAD)
    ranks = seqs * QUAD
    triple, both = qkv_own.shape[1] // ranks, up_own.shape[1] // ranks
    count, full_rows, head_width = QUAD, rows * seqs, triple // 3
    half = both // 2
    hbm = pl.BlockSpec(memory_space=pl.ANY)
    vmem = pl.BlockSpec(memory_space=pltpu.VMEM)
    shape = jax.ShapeDtypeStruct
    dma = pltpu.SemaphoreType.DMA
    by_heads = shape((count, full_rows, head_width), bf16)
    return pl.pallas_call(
        lambda *refs: forward_kernel(grps, aligned, *refs),
        in_specs=[vmem] * 3 + [hbm] * 6,
        out_specs=[vmem] * 3 + [hbm] * 14,
        out_shape=[
            shape((rows, D), f32),
            shape((8, D), f32),
            shape((ranks, 8, 128), f32),
            shape((count, full_rows, D), bf16),
            by_heads,
            by_heads,
            by_heads,
            by_heads,
            shape((count, full_rows, D), bf16),
            shape((3 if grps == 4 else grps, half // grps, D // 2), bf16),
            shape((half // 128, 128, D // 2), bf16),
            shape((count, full_rows, half), bf16),
            shape((count, full_rows, both), bf16),
            shape((seqs, grps, QUAD, shard, triple), bf16),
            shape((seqs, grps, QUAD, shard, both), bf16),
            shape((head_width, D), bf16),
            shape((half, D), bf16),
        ],
        scratch_shapes=[
            pltpu.VMEM((ranks, rows, D), bf16),
            pltpu.VMEM((ranks, rows, D), bf16),
            pltpu.VMEM((count, full_rows, D), bf16),
            pltpu.VMEM((count, full_rows, D), bf16),
            pltpu.VMEM((seqs, QUAD, shard, triple), bf16),
            pltpu.VMEM((seqs, QUAD, shard, both), bf16),
            pltpu.VMEM((seqs, grps, QUAD, shard, triple), bf16),
            pltpu.VMEM((seqs, grps, QUAD, shard, both), bf16),
            pltpu.VMEM((head_width, D), bf16),
            pltpu.VMEM((half, D), bf16),
            pltpu.VMEM((4, count, full_rows, head_width), bf16),
            pltpu.VMEM((ranks, rows, D), bf16),
            pltpu.VMEM((4, rows, D), bf16),
            pltpu.VMEM((3, rows, D), bf16),
            pltpu.VMEM((count, full_rows, both), f32),
            pltpu.VMEM((count, full_rows, half), bf16),
            pltpu.VMEM((count, full_rows, both), bf16),
            pltpu.VMEM((grps, ranks, 8, 128), f32),
            dma((20,)),
            dma((7,)),
            dma((9,)),
            dma((2, 7)),
            dma((2, 7)),
            dma((4,)),
            dma((4,)),
            dma((3,)),
            dma((3,)),
            dma((3, 7)),
            dma((3, 7)),
            dma((4, 2 * grps)),
            dma((4, grps)),
            dma((7 + grps,)),
            dma((7 + grps,)),
            dma((max(5, grps),)),
            dma((max(5, grps),)),
            dma((7,)),
        ],
        compiler_params=pltpu.CompilerParams(
            collective_id=1, has_side_effects=True, vmem_limit_bytes=VMEM_LIMIT
        ),
        cost_estimate=pl.CostEstimate(
            flops=20 * 10**9, bytes_accessed=60 * 2**20, transcendentals=4 * 10**6
        ),
        name="forward",
    )(*tables, own_facts, tokens, own_grad, qkv_own, up_own, out_own, down_own)


DEPTH = 5


def adam_kernel(grps, rows_first, rows_second, down_low, down_high, out_planes, up_ranks, qkv_ranks, gains_sum, gains, gains_m, gains_v, *refs):
    states, outs = refs[:12], refs[12:28]
    gains_outs = refs[28:31]
    state, planes, ranks, fresh, copied, in_sem, out_sem, row_sem = refs[33:]
    passed = [
        pltpu.make_async_copy(src, dst, row_sem.at[n])
        for n, (src, dst) in enumerate(((rows_first, refs[31]), (rows_second, refs[32])))
    ]
    plane = lax.axis_index("grp")
    rows = state.shape[2]
    units = CHUNK // QUAD
    pieces = []
    for n, (name, rate) in enumerate(
        (("down", FF ** (-0.5)), ("out", (D // 128) ** (-0.5)), ("up", D ** (-0.5)), ("qkv", D ** (-0.5)))
    ):
        arrays = states[3 * n : 3 * n + 3]
        for top in range(0, arrays[0].shape[0], rows):
            for left in range(0, arrays[0].shape[1], CHUNK):
                pieces.append((name, rate, n, top, left))

    def grad_source(name, top, left, slot):
        if name in ("down", "out"):
            source = out_planes
            if name == "down":
                source, left = (down_low, left) if left < D // 2 else (down_high, left - D // 2)
            return (
                source.at[:, top : top + rows, left : left + CHUNK],
                planes.at[slot, : source.shape[0]],
            )
        source, parts = (up_ranks, 2) if name == "up" else (qkv_ranks, 3)
        width = source.shape[2] // parts
        per_seq = width // units
        n = left // CHUNK
        seqs = source.shape[0] // QUAD
        seq = n // per_seq % seqs
        first = n // (per_seq * seqs) * width + n % per_seq * units
        return source.at[seq * QUAD : (seq + 1) * QUAD, :, first : first + units], ranks.at[slot]

    def reads(k):
        name, _, n, top, left = pieces[k]
        slot = k % DEPTH
        window = (slice(top, top + rows), slice(left, left + CHUNK))
        copies = [
            pltpu.make_async_copy(states[3 * n + i].at[window], state.at[slot, i], in_sem.at[slot, i])
            for i in range(3)
        ]
        source, space = grad_source(name, top, left, slot)
        return copies + [pltpu.make_async_copy(source, space, in_sem.at[slot, 3])]

    def writes(k):
        _, _, n, top, left = pieces[k]
        slot = k % DEPTH
        window = (slice(top, top + rows), slice(left, left + CHUNK))
        copies = [
            pltpu.make_async_copy(fresh.at[slot, i], outs[4 * n + i].at[window], out_sem.at[slot, i])
            for i in range(3)
        ]
        return copies + [
            pltpu.make_async_copy(copied.at[slot], outs[4 * n + 3].at[window], out_sem.at[slot, 3])
        ]

    def gradient(name, left, slot):
        if name in ("down", "out"):
            chained = name == "down" and left < D // 2
            source = (down_low if chained else down_high) if name == "down" else out_planes
            total = jnp.zeros((rows, CHUNK), f32)
            for j in range(source.shape[0]):
                held = planes[slot, j].astype(f32)
                if grps == 4 and chained and j < 2:
                    held = jnp.where(plane > 0 if j == 0 else plane < 3, held, 0.0)
                elif grps == 4 and not chained and j in (0, 3):
                    held = jnp.where(plane != 3 - j, held, 0.0)
                total += held
            return total
        lanes = down_low.shape[1] if name == "up" else HEAD_DIM
        values = [ranks[slot, q].astype(f32) for q in range(QUAD)]
        return jnp.concatenate(
            [
                values[q][:, n * lanes : (n + 1) * lanes]
                for n in range(units // lanes)
                for q in range(QUAD)
            ],
            axis=1,
        )

    for k in range(DEPTH - 1):
        for copy in reads(k):
            copy.start()
    for copy in passed:
        copy.start()
    results = adam_update(gains[...], gains_m[...], gains_v[...], gains_sum[...], 0.3)
    for out, result in zip(gains_outs, results):
        out[...] = result
    for k, (name, rate, _, _, left) in enumerate(pieces):
        slot = k % DEPTH
        if k + DEPTH - 1 < len(pieces):
            for copy in reads(k + DEPTH - 1):
                copy.start()
        for copy in reads(k):
            copy.wait()
        if k >= DEPTH:
            for copy in writes(k - DEPTH):
                copy.wait()
        results = adam_update(state[slot, 0], state[slot, 1], state[slot, 2], gradient(name, left, slot), rate)
        for i in range(3):
            fresh[slot, i] = results[i]
        copied[slot] = results[0].astype(bf16)
        for copy in writes(k):
            copy.start()
    for k in range(len(pieces) - DEPTH, len(pieces)):
        for copy in writes(k):
            copy.wait()
    for copy in passed:
        copy.wait()


def adam(grps, rows_first, rows_second, down_low, down_high, out_planes, up_ranks, qkv_ranks, gains_sum, gains, states):
    rows = up_ranks.shape[1]
    hbm = pl.BlockSpec(memory_space=pl.ANY)
    vmem = pl.BlockSpec(memory_space=pltpu.VMEM)
    shapes = []
    for array in states[::3]:
        shapes += [jax.ShapeDtypeStruct(array.shape, f32)] * 3
        shapes.append(jax.ShapeDtypeStruct(array.shape, bf16))
    shapes += [jax.ShapeDtypeStruct(gains[0].shape, f32)] * 3
    shapes += [jax.ShapeDtypeStruct(rows_first.shape, f32), jax.ShapeDtypeStruct(rows_second.shape, bf16)]
    size = sum(array.size for array in states) // 3
    outs = pl.pallas_call(
        lambda *refs: adam_kernel(grps, *refs),
        in_specs=[hbm] * 7 + [vmem] * 4 + [hbm] * 12,
        out_specs=[hbm] * 16 + [vmem] * 3 + [hbm] * 2,
        out_shape=shapes,
        scratch_shapes=[
            pltpu.VMEM((DEPTH, 3, rows, CHUNK), f32),
            pltpu.VMEM((DEPTH, grps, rows, CHUNK), bf16),
            pltpu.VMEM((DEPTH, QUAD, rows, CHUNK // QUAD), bf16),
            pltpu.VMEM((DEPTH, 3, rows, CHUNK), f32),
            pltpu.VMEM((DEPTH, rows, CHUNK), bf16),
            pltpu.SemaphoreType.DMA((DEPTH, 4)),
            pltpu.SemaphoreType.DMA((DEPTH, 4)),
            pltpu.SemaphoreType.DMA((2,)),
        ],
        compiler_params=pltpu.CompilerParams(vmem_limit_bytes=VMEM_LIMIT),
        cost_estimate=pl.CostEstimate(flops=size * 16, bytes_accessed=size * 28, transcendentals=size),
        name="adam",
    )(rows_first, rows_second, down_low, down_high, out_planes, up_ranks, qkv_ranks, gains_sum, *gains, *states)
    return outs[:4], outs[4:8], outs[8:12], outs[12:16], outs[16:19], outs[19:]


def on_device(
    tokens,
    cotangent,
    lengths,
    qkv_weight,
    qkv_moment,
    qkv_square,
    out_weight,
    out_moment,
    out_square,
    up_weight,
    up_moment,
    up_square,
    down_weight,
    down_moment,
    down_square,
    norm_gains,
    gains_moment,
    gains_square,
):
    seqs = lax.axis_size("seq")
    grps = lax.axis_size("grp")
    ranks = seqs * QUAD
    own_rows = tokens.shape[1]
    full_rows = own_rows * seqs
    all_rows = full_rows * QUAD
    heads_local = HEADS // ranks
    head_width = heads_local * HEAD_DIM
    units = down_weight.shape[0]
    aligned = out_weight.shape[0] == HEAD_DIM
    tables = rotate_table(full_rows, heads_local)

    positions = lax.axis_index("seq") * own_rows + jnp.arange(own_rows, dtype=jnp.int32)
    own_grad = jnp.where((positions < lengths[0])[:, None], cotangent[0], 0)
    own_gains = norm_gains.shape[1]
    own_facts = jnp.zeros((8, 128), f32)
    own_facts = own_facts.at[:2, :own_gains].set(norm_gains.astype(bf16).astype(f32))
    own_facts = own_facts.at[2].set(lengths[0].astype(f32))

    out_own = out_weight
    if not aligned:
        out_all = lax.all_gather(out_weight.astype(bf16), EVERY, axis=0, tiled=True)
        out_all = out_all.reshape(seqs, heads_local, QUAD, HEAD_DIM, D)
        seat = lax.axis_index("row") * 2 + lax.axis_index("core")
        out_own = lax.dynamic_index_in_dim(
            lax.dynamic_index_in_dim(out_all, lax.axis_index("seq"), 0, False), seat, 1, False
        ).reshape(head_width, D)
    (
        residual,
        gains,
        facts,
        first_norm,
        queries,
        key_vectors,
        value_vectors,
        attended,
        second_norm,
        down_low,
        down_share,
        hidden,
        grad_both,
        qkv_local,
        up_local,
        out_local,
        down_local,
    ) = forward(
        grps,
        aligned,
        tables,
        own_facts,
        tokens[0],
        own_grad,
        qkv_weight,
        up_weight,
        out_own,
        down_weight,
    )
    if not aligned:
        out_local = out_own
    (
        input_grad,
        block_output,
        gains_total,
        down_high,
        out_planes,
        up_ranks,
        qkv_ranks,
        *_,
    ) = backward(
        grps,
        aligned,
        facts,
        gains,
        tables,
        residual,
        tokens[0],
        own_grad,
        grad_both,
        up_local.reshape(D, -1),
        down_share.reshape(grps, units, D // 2),
        second_norm,
        first_norm,
        out_local,
        qkv_local.reshape(D, -1),
        (queries, key_vectors, value_vectors, attended),
        hidden,
        down_local,
    )
    if aligned:
        out_sum = out_planes
    else:
        placed_term = jnp.zeros((seqs, QUAD, heads_local, HEAD_DIM, D), bf16)
        placed_term = lax.dynamic_update_slice(
            placed_term,
            out_planes.reshape(1, 1, heads_local, HEAD_DIM, D),
            (lax.axis_index("seq"), seat, 0, 0, 0),
        )
        out_sum = lax.psum_scatter(
            placed_term.transpose(0, 2, 1, 3, 4).reshape(D, D),
            EVERY,
            scatter_dimension=0,
            tiled=True,
        )[None]
    device = ((lax.axis_index("seq") * grps + lax.axis_index("grp")) * 2 + lax.axis_index("row")) * 2
    gains_sum = lax.dynamic_slice(
        gains_total, (0, (device + lax.axis_index("core")) * own_gains), (2, own_gains)
    )
    down_new, out_new, up_new, qkv_new, gains_new, (input_grad, block_output) = adam(
        grps,
        input_grad,
        block_output,
        down_low,
        down_high,
        out_sum,
        up_ranks,
        qkv_ranks,
        gains_sum,
        (norm_gains, gains_moment, gains_square),
        (
            down_weight,
            down_moment,
            down_square,
            out_weight,
            out_moment,
            out_square,
            up_weight,
            up_moment,
            up_square,
            qkv_weight,
            qkv_moment,
            qkv_square,
        ),
    )
    return (
        block_output[None],
        input_grad[None],
        *qkv_new,
        *out_new,
        *up_new,
        *down_new,
        *gains_new,
    )


def solution(mesh):
    seqs, rest = mesh.shape["seq"], mesh.shape["fsdp"]
    planes = Mesh(
        mesh.devices.reshape(seqs, rest // QUAD, 2, 2), ("seq", "grp", "row", "core")
    )
    rows = P(("grp", "row", "core"), "seq", None)
    shards = P(EVERY, None)
    gains = P(None, EVERY)
    return jax.shard_map(
        on_device,
        mesh=planes,
        in_specs=(rows, rows, P(("grp", "row", "core"))) + (shards,) * 12 + (gains,) * 3,
        out_specs=(rows, rows) + (shards,) * 16 + (gains,) * 3,
        check_vma=False,
    )
```

```python
import math

import jax
import jax.numpy as jnp
from jax import lax
from jax.experimental import pallas as pl
from jax.experimental.pallas import tpu as pltpu
from jax.sharding import Mesh, PartitionSpec as P

D = 2048
HEADS = 32
HEAD_DIM = 64
FF = 4096
WINDOW = 128
STEP = 5


NORM_EPSILON = 1e-05
MOMENT_DECAY = 0.5
WEIGHT_DECAY = 0.1
ADAM_EPSILON = 1e-08

SEATS = ("row", "core", "seq")
RANKS = ("seq", "row", "core")
EVERY = ("seq", "grp", "row", "core")
QUAD = 4
VMEM_LIMIT = 63 * 2**20

bf16 = jnp.bfloat16
f32 = jnp.float32


def rotate_table(length, copies):
    halves = HEAD_DIM // 2
    freqs = jnp.exp(-math.log(10000.0) * 2.0 * jnp.arange(halves).astype(f32) / HEAD_DIM)
    angles = jnp.arange(length, dtype=jnp.int32).astype(f32)[:, None] * freqs[None, :]
    cosine, sine = jnp.cos(angles), jnp.sin(angles)
    return (
        jnp.tile(jnp.concatenate([cosine, cosine], axis=1), (1, copies)),
        jnp.tile(jnp.concatenate([-sine, sine], axis=1), (1, copies)),
    )


def adam_update(weight, moment, square, gradient, step_rate):
    moment_new = MOMENT_DECAY * moment + (1.0 - MOMENT_DECAY) * gradient
    square_new = MOMENT_DECAY * square + (1.0 - MOMENT_DECAY) * gradient * gradient
    correction = 1.0 - MOMENT_DECAY**STEP
    unbias = 1.0 / correction
    update = (moment_new * unbias) / (jnp.sqrt(square_new * unbias) + ADAM_EPSILON)
    return (weight - step_rate * (update + WEIGHT_DECAY * weight), moment_new, square_new)


def dot(a, b, lhs=1, rhs=0):
    return lax.dot_general(a, b, (((lhs,), (rhs,)), ((), ())), preferred_element_type=f32)


def swap_halves(values, first):
    width = values.shape[1]
    half = HEAD_DIM // 2
    return jnp.where(
        first, pltpu.roll(values, width - half, 1), pltpu.roll(values, half, 1)
    )


def allowed_mask(rows, length):
    row = lax.broadcasted_iota(jnp.int32, (rows, rows), 0)
    col = lax.broadcasted_iota(jnp.int32, (rows, rows), 1)
    return (col <= row) & (row - col < WINDOW) & (col.astype(f32) < length)


def head_lanes(rows, width, head):
    lane = lax.broadcasted_iota(jnp.int32, (rows, width), 1)
    return (lane // HEAD_DIM) == head


def softmax_rows(queries, key_vectors, allowed):
    scores = jnp.where(allowed, dot(queries, key_vectors, 1, 1) * (HEAD_DIM**-0.5), -1e30)
    shifted = jnp.exp(scores - jnp.max(scores, axis=-1, keepdims=True))
    return shifted / jnp.sum(shifted, axis=-1, keepdims=True)


def attention(length, queries, key_vectors, value_vectors):
    rows, width = queries.shape
    allowed = allowed_mask(rows, length)
    total = jnp.zeros((rows, width), f32)
    for head in range(width // HEAD_DIM):
        mine = head_lanes(rows, width, head)
        weights = softmax_rows(jnp.where(mine, queries, 0), key_vectors, allowed)
        total += dot(weights.astype(bf16), jnp.where(mine, value_vectors, 0))
    return total.astype(bf16)


def attention_grads(length, queries, key_vectors, value_vectors, grads):
    rows, width = queries.shape
    allowed = allowed_mask(rows, length)
    grad_q = jnp.zeros((rows, width), f32)
    grad_k = jnp.zeros((rows, width), f32)
    grad_v = jnp.zeros((rows, width), f32)
    for head in range(width // HEAD_DIM):
        mine = head_lanes(rows, width, head)
        q_head = jnp.where(mine, queries, 0)
        g_head = jnp.where(mine, grads, 0)
        weights = softmax_rows(q_head, key_vectors, allowed)
        grad_p = dot(g_head, value_vectors, 1, 1)
        delta = jnp.sum(weights * grad_p, axis=-1, keepdims=True)
        grad_s = jnp.where(allowed, weights * (grad_p - delta), 0.0).astype(bf16)
        grad_q += dot(grad_s, jnp.where(mine, key_vectors, 0))
        grad_k += dot(grad_s, q_head, 0, 0)
        grad_v += dot(weights.astype(bf16), g_head, 0, 0)
    return grad_q, grad_k, grad_v


MESH = pl.DeviceIdType.MESH
RELATIONS = tuple((a, b, d) for a in range(2) for b in range(2) for d in range(2))[1:]


class Place:
    def __init__(self, grps):
        self.grps = grps
        self.s = lax.axis_index("seq")
        self.g = lax.axis_index("grp")
        self.r = lax.axis_index("row")
        self.c = lax.axis_index("core")

    def peer(self, relation):
        ds, dr, dc = relation
        return ((self.s + ds) % 2, self.g, (self.r + dr) % 2, (self.c + dc) % 2)

    def plane(self, dz):
        return (self.s, (self.g + dz) % self.grps, self.r, self.c)

    def rank(self, relation=(0, 0, 0)):
        s, _, r, c = self.peer(relation)
        return (s * 2 + r) * 2 + c

    def seat(self, relation=(0, 0, 0)):
        s, _, r, c = self.peer(relation)
        return (r * 2 + c) * 2 + s

    def corner(self, relation=(0, 0, 0)):
        s, _, r, _ = self.peer(relation)
        return r * 2 + s

    def greet(self):
        barrier = pltpu.get_barrier_semaphore()
        for relation in RELATIONS:
            pl.semaphore_signal(barrier, inc=1, device_id=self.peer(relation), device_id_type=MESH)
        for dz in range(1, self.grps):
            pl.semaphore_signal(barrier, inc=1, device_id=self.plane(dz), device_id_type=MESH)
        pl.semaphore_wait(barrier, len(RELATIONS) + self.grps - 1)


SIBLING = (0, 0, 1)
ACROSS = ((1, 0, 0), (0, 1, 0), (1, 1, 0))


def remote(src, dst, send_sem, recv_sem, device):
    return pltpu.make_async_remote_copy(
        src_ref=src,
        dst_ref=dst,
        send_sem=send_sem,
        recv_sem=recv_sem,
        device_id=device,
        device_id_type=MESH,
    )


class PlaneSum:
    def __init__(self, place, part, near, far, sems):
        self.place, self.part, self.nears, self.fars = place, part, near, far
        self.near_send, self.near_recv, self.far_send, self.far_recv = sems
        self.first, self.second = [None] * 4, []

    def sequence(self, k):
        place = self.place
        row = (place.r + 1) % 2 if k < 2 else place.r
        return row * 2 + ((place.c + 1) % 2 if k % 2 == 0 else place.c)

    def near(self, k):
        for s in range(2):
            copy = remote(
                self.part.at[2 * self.sequence(k) + s],
                self.nears.at[k + s],
                self.near_send.at[k + s],
                self.near_recv.at[k + s],
                self.place.peer(SIBLING),
            )
            copy.start()
            self.first[k + s] = copy

    def far(self, k):
        place = self.place
        for s in range(2):
            self.first[k - 1 + s].wait()
            self.nears[k - 1 + s] = (
                self.part[2 * self.sequence(k) + s].astype(f32)
                + self.nears[k - 1 + s].astype(f32)
            ).astype(bf16)
        for d in (1, 2) if k == 1 else (0,):
            relation = ACROSS[d]
            copy = remote(
                self.nears.at[k - 1 + (place.s + relation[0]) % 2],
                self.fars.at[d],
                self.far_send.at[d],
                self.far_recv.at[d],
                place.peer(relation),
            )
            copy.start()
            self.second.append(copy)

    def finish(self):
        for copy in self.second:
            copy.wait()

    def chunk(self, lanes):
        total = self.nears[2 + self.place.s, :, lanes].astype(f32)
        for d in range(3):
            total += self.fars[d, :, lanes].astype(f32)
        return total


class PlaneGather:
    def __init__(self, place, blocks, send, recv):
        self.place, self.blocks, self.sends, self.recvs = place, blocks, send, recv
        self.copies = [None] * 7

    def send(self, block, sem, relation):
        copy = remote(
            self.blocks.at[block],
            self.blocks.at[block],
            self.sends.at[sem],
            self.recvs.at[sem],
            self.place.peer(relation),
        )
        copy.start()
        self.copies[sem] = copy

    def start(self):
        mine = self.place.seat()
        for d in range(2):
            self.send(mine, d, ACROSS[d])
        self.send(mine, 3, SIBLING)

    def forward(self, d):
        self.copies[d].wait_recv()
        self.send(self.place.seat(ACROSS[d]), 4 + d, SIBLING)
        if d == 0:
            self.send(self.place.seat(), 2, ACROSS[2])

    def sequence(self, k):
        place = self.place
        row = place.r if k < 2 else (place.r + 1) % 2
        return row * 2 + (place.c if k % 2 == 0 else (place.c + 1) % 2)

    def arrive(self, k, forwarded=False):
        if k == 0:
            self.forward(0)
        elif k == 1:
            if not forwarded:
                self.forward(1)
            self.copies[3].wait_recv()
            self.copies[4].wait_recv()
        elif k == 2:
            self.forward(2)
        else:
            self.copies[5].wait_recv()
            self.copies[6].wait_recv()

    def finish(self):
        for copy in self.copies:
            copy.wait_send()


class ToOwners:
    def __init__(self, place, shares, landed, met, stage, send, recv, own):
        self.place, self.shares, self.landed, self.met, self.stage = place, shares, landed, met, stage
        self.send, self.recv, self.own_sem = send, recv, own
        self.line = place.grps == 4
        self.own = pltpu.make_async_copy(shares.at[place.g], landed.at[place.g], own)

    def copy(self, block, landing, sem, recv, target):
        place = self.place
        return remote(
            self.shares.at[block],
            landing,
            self.send.at[sem],
            self.recv.at[recv],
            (place.s, target, place.r, place.c),
        )

    def direct(self, g):
        targets = ((2, 1), (2, 0), (1, 3), (1, 2))[g]
        return [self.copy(t, self.landed.at[g], t, g, t) for t in targets]

    def meeting(self, g):
        far, inner = (3, 1) if g == 0 else (0, 2)
        return self.copy(far, self.met, far, inner, inner)

    def joined(self, g):
        far = 3 if g == 1 else 0
        return self.copy(far, self.landed.at[g], far, g, far)

    def start(self, waits=False):
        place, self.waits = self.place, waits
        self.own.start()
        if self.line:
            for g in range(4):

                @pl.when(place.g == g)
                def _():
                    if g in (0, 3):
                        self.meeting(g).start()
                    if g in (1, 2) or not waits:
                        for copy in self.direct(g):
                            copy.start()

        else:
            self.copies = [
                self.copy((place.g + dz) % place.grps, self.landed.at[place.g], dz, dz, (place.g + dz) % place.grps)
                for dz in range(1, place.grps)
            ]
            for copy in self.copies:
                copy.start()
        return self

    def proceed(self):
        if self.line:
            for g in (0, 3):

                @pl.when(self.place.g == g)
                def _():
                    self.meeting(g).wait_send()
                    for copy in self.direct(g):
                        copy.start()

    def join(self):
        if not self.line:
            return
        for g in (1, 2):

            @pl.when(self.place.g == g)
            def _():
                outer, far = (0, 3) if g == 1 else (3, 0)
                self.copy(far, self.met, far, g, outer).wait_recv()
                copy = pltpu.make_async_copy(self.met, self.stage, self.own_sem)
                self.own.wait()
                copy.start()
                copy.wait()
                if len(self.stage.shape) == 2:
                    self.shares[far] = (
                        self.shares[far].astype(f32) + self.stage[...].astype(f32)
                    ).astype(bf16)
                else:
                    for n in range(self.stage.shape[0]):
                        self.shares[far, n] = (
                            self.shares[far, n].astype(f32) + self.stage[n].astype(f32)
                        ).astype(bf16)
                self.joined(g).start()

        for g in (0, 3):

            @pl.when(self.place.g == g)
            def _():
                self.own.wait()

    def sent(self):
        if not self.line:
            for copy in self.copies:
                copy.wait_send()
            return
        for g in range(4):

            @pl.when(self.place.g == g)
            def _():
                for copy in self.direct(g):
                    copy.wait_send()
                if g in (1, 2):
                    self.joined(g).wait_send()
                elif not self.waits:
                    self.meeting(g).wait_send()

    def received(self):
        if not self.line:
            self.own.wait()
            for copy in self.copies:
                copy.wait_recv()
            return
        for g in range(4):

            @pl.when(self.place.g == g)
            def _():
                for j in ((1, 2), (0, 2, 3), (0, 1, 3), (1, 2))[g]:
                    self.copy(g, self.landed.at[j], j, j, j).wait_recv()

    def finish(self):
        self.sent()
        self.received()

    def holds(self, j):
        g = self.place.g
        return (g % 3 != 0) | (j + g != 3) if self.line else True


class Exchange:
    def __init__(self, place, blocks, held, send, recv, own):
        mine = place.rank()
        kept = held.at[mine // QUAD, mine % QUAD] if len(held.shape) == 4 else held.at[mine]

        def block(t):
            return blocks.at[0, t // QUAD, t % QUAD] if len(blocks.shape) == 5 else blocks.at[t]

        self.copies = []
        for n, relation in enumerate(RELATIONS):
            copy = remote(
                block(place.rank(relation)),
                kept,
                send.at[n],
                recv.at[n],
                place.peer(relation),
            )
            copy.start()
            self.copies.append(copy)
        copy = pltpu.make_async_copy(block(mine), kept, own)
        copy.start()
        self.copies.append(copy)

    def finish(self):
        for copy in self.copies:
            copy.wait()


LANES = 512


def lanes_of(n, width=LANES):
    return pl.ds(pl.multiple_of(n * width, width), width)


def shares_of(seq, values, weight, part):
    rows = part.shape[1]

    @pl.loop(0, part.shape[2] // LANES)
    def _(n):
        product = dot(values[seq], weight[lanes_of(n)], 1, 1)
        part[2 * seq, :, lanes_of(n)] = product[:rows].astype(bf16)
        part[2 * seq + 1, :, lanes_of(n)] = product[rows:].astype(bf16)


def over_tokens(first, lanes, second, other):
    total = dot(first[0, :, lanes], second[0, :, other], 0, 0)
    for seq in range(1, first.shape[0]):
        total += dot(first[seq, :, lanes], second[seq, :, other], 0, 0)
    return total


def row_shares(first, second, shares):
    grps, seqs, rows, _ = shares.shape
    width = 256
    pieces = width // rows

    @pl.loop(0, first.shape[2] // width)
    def _(b):
        product = over_tokens(first, lanes_of(b, width), second, slice(None)).astype(bf16)
        for p in range(pieces):
            index = b * pieces + p
            shares[index % grps, index // grps] = product[p * rows : (p + 1) * rows]


def summed_rows(landed, holds, blocks):
    seqs, rows = landed.shape[1], blocks.shape[1]
    for seq in range(seqs):
        for quad in range(QUAD):
            block = slice(quad * rows, (quad + 1) * rows)
            total = jnp.zeros((rows, landed.shape[3]), f32)
            for j in range(landed.shape[0]):
                total += jnp.where(holds(j), landed[j, seq, block].astype(f32), 0.0)
            blocks[seq * QUAD + quad] = total.astype(bf16)


def back_kernel(
    grps,
    aligned,
    facts,
    gains,
    cosine,
    sine,
    residual,
    own_tokens,
    own_grad,
    dgu_h,
    up_h,
    second_h,
    first_h,
    out_h,
    qkv_h,
    q_h,
    k_h,
    v_h,
    o_h,
    hidden_h,
    down_h,
    input_grad,
    block_output,
    gains_sum,
    out_landed,
    up_held,
    qkv_held,
    up_landed,
    qkv_landed,
    up_met,
    out_met,
    qkv_met,
    wide,
    up,
    acts,
    out_w,
    qkv,
    part,
    near,
    far,
    blocks,
    turned,
    up_share,
    out_share,
    qkv_share,
    up_sum,
    qkv_sum,
    stage_low,
    stage_wide,
    gain_part,
    gain_plane,
    gain_far,
    load,
    near_send,
    near_recv,
    far_send,
    far_recv,
    all_send,
    all_recv,
    z_send,
    z_recv,
    swap_send,
    swap_recv,
    gain_send,
    gain_recv,
    own_sem,
    near_free,
    far_free,
):
    place = Place(grps)
    rows = residual.shape[0]
    gain_part[...] = jnp.zeros_like(gain_part)
    count, full_rows, head_width = q_h.shape

    def fetch(src, dst, n):
        copy = pltpu.make_async_copy(src, dst, load.at[n])
        copy.start()
        return copy

    loads = [fetch(dgu_h, wide, 0), fetch(second_h, acts, 3), fetch(up_h, up, 1)]
    weights = [fetch(out_h, out_w, 5), fetch(qkv_h, qkv, 6)]
    place.greet()
    for copy in loads[:2]:
        copy.wait()

    sums = (near_send, near_recv, far_send, far_recv)
    def to_owners(n, shares, landed, met, stage, waits=False):
        return ToOwners(
            place, shares, landed, met, stage, z_send.at[n], z_recv.at[n], own_sem.at[n]
        ).start(waits)

    def summed_over_plane(values, weight):
        total = PlaneSum(place, part, near, far, sums)
        for k in range(4):
            shares_of(total.sequence(k), values, weight, part)
            if k % 2 == 0:
                total.near(k)
            else:
                total.far(k)
        return total

    row_shares(acts, wide, up_share)
    up_out = to_owners(1, up_share, up_landed, up_met, stage_wide, True)
    loads[2].wait()
    second_sum = summed_over_plane(wide, up)
    fetch_first = fetch(first_h, acts, 3)
    heads = [
        fetch(ref, wide.at[:, :, n * head_width : (n + 1) * head_width], 7 + n)
        for n, ref in enumerate((q_h, k_h, v_h, o_h))
    ]

    half = hidden_h.shape[2]
    hidden = turned.at[:, :, :half]
    last = [fetch(hidden_h, hidden, 11)]
    for n in range(2):
        columns = slice(n * D // 2, (n + 1) * D // 2)
        last.append(fetch(down_h.at[:, columns], up.at[n * half : (n + 1) * half, : D // 2], 12 + n))
    up_out.proceed()
    up_out.join()
    second_sum.finish()
    mine = place.seat()
    inner = jnp.zeros((rows, 1), f32)
    squares = jnp.zeros((rows, 1), f32)
    for n in range(D // LANES):
        lanes = slice(n * LANES, (n + 1) * LANES)
        grad = second_sum.chunk(lanes)
        values = residual[:, lanes]
        inner += jnp.sum(grad * gains[1:2, lanes] * values, axis=-1, keepdims=True)
        squares += jnp.sum(values * values, axis=-1, keepdims=True)
    scale = lax.rsqrt(squares / D + NORM_EPSILON)
    inner = inner / D
    for n in range(D // LANES):
        lanes = slice(n * LANES, (n + 1) * LANES)
        grad, values = second_sum.chunk(lanes), residual[:, lanes]
        gain_part[1:2, lanes] = jnp.sum(grad * values * scale, axis=0, keepdims=True)
        total = own_grad[:, lanes].astype(f32) + scale * (
            grad * gains[1:2, lanes] - values * scale * scale * inner
        )
        input_grad[:, lanes] = total
        blocks[mine, :, lanes] = total.astype(bf16)

    gather = PlaneGather(place, blocks, all_send, all_recv)
    gather.start()
    for copy in weights + heads:
        copy.wait()

    lane = lax.broadcasted_iota(jnp.int32, (full_rows, head_width), 1)
    first_half = (lane % HEAD_DIM) < HEAD_DIM // 2

    for copy in last:
        copy.wait()

    @pl.loop(0, count)
    def _(seq):
        for n in range(D // LANES):
            top, left = n * LANES // (D // 2) * half, n * LANES % (D // 2)
            product = dot(hidden[seq], up[top : top + half, left : left + LANES])
            part[2 * seq, :, n * LANES : (n + 1) * LANES] = product[:rows].astype(bf16)
            part[2 * seq + 1, :, n * LANES : (n + 1) * LANES] = product[rows:].astype(bf16)

    out_rows = out_share.shape[1]

    def out_shares():
        @pl.loop(0, D // LANES)
        def _(n):
            lanes = lanes_of(n)
            total = jnp.zeros((head_width, LANES), f32)
            for seq in range(count):
                values = wide[seq, :, 3 * head_width : 4 * head_width].astype(f32)
                total += dot(values[:rows].astype(bf16), blocks[2 * seq, :, lanes], 0, 0)
                total += dot(values[rows:].astype(bf16), blocks[2 * seq + 1, :, lanes], 0, 0)
            total = total.astype(bf16)
            for j in range(out_share.shape[0]):
                out_share[j, :, lanes] = total[j * out_rows : (j + 1) * out_rows]

    last_sum = PlaneSum(place, part, near, far, sums)
    for k in range(4):
        gather.arrive(k)
        seq = gather.sequence(k)
        if k == 3:
            out_shares()
            if aligned:
                out_out = to_owners(3, out_share, out_landed, out_met, stage_low)
            else:
                out_out = pltpu.make_async_copy(out_share, out_landed, own_sem.at[3])
                out_out.start()
        grads = jnp.concatenate(
            [dot(blocks[2 * seq], out_w[...], 1, 1), dot(blocks[2 * seq + 1], out_w[...], 1, 1)],
            axis=0,
        ).astype(bf16)
        queries = wide[seq, :, 0:head_width]
        key_vectors = wide[seq, :, head_width : 2 * head_width]
        value_vectors = wide[seq, :, 2 * head_width : 3 * head_width]
        grad_q, grad_k, grad_v = attention_grads(
            facts[seq, 2:3, 0:1], queries, key_vectors, value_vectors, grads
        )
        for n, grad in enumerate((grad_q, grad_k)):
            values = (grad * HEAD_DIM**-0.5).astype(bf16).astype(f32)
            back = values * cosine[...] - swap_halves(values, first_half) * sine[...]
            turned[seq, :, n * head_width : (n + 1) * head_width] = back.astype(bf16)
        turned[seq, :, 2 * head_width : 3 * head_width] = grad_v.astype(bf16)
        if k == 1:
            last_sum.near(0)
            last_sum.near(2)
        elif k == 2:
            last_sum.far(1)
            last_sum.far(3)

    gather.finish()
    fetch_first.wait()
    row_shares(acts, turned, qkv_share)
    triple = turned.shape[2]
    qkv_out = to_owners(2, qkv_share, qkv_landed, qkv_met, stage_wide.at[:, :, :triple], True)

    last_sum.finish()
    for n in range(D // LANES):
        lanes = slice(n * LANES, (n + 1) * LANES)
        block_output[:, lanes] = (residual[:, lanes] + last_sum.chunk(lanes)).astype(bf16)
    pl.semaphore_signal(near_free, inc=1, device_id=place.peer(SIBLING), device_id_type=MESH)
    for relation in ACROSS:
        pl.semaphore_signal(far_free, inc=1, device_id=place.peer(relation), device_id_type=MESH)
    pl.semaphore_wait(near_free, 1)
    pl.semaphore_wait(far_free, 3)
    first_sum = summed_over_plane(turned, qkv)
    if aligned:
        out_out.join()
    qkv_out.proceed()
    qkv_out.join()
    first_sum.finish()
    inner = jnp.zeros((rows, 1), f32)
    squares = jnp.zeros((rows, 1), f32)
    for n in range(D // LANES):
        lanes = slice(n * LANES, (n + 1) * LANES)
        grad = first_sum.chunk(lanes)
        values = own_tokens[:, lanes].astype(f32)
        inner += jnp.sum(grad * gains[0:1, lanes] * values, axis=-1, keepdims=True)
        squares += jnp.sum(values * values, axis=-1, keepdims=True)
    scale = lax.rsqrt(squares / D + NORM_EPSILON)
    inner = inner / D
    for n in range(D // LANES):
        lanes = slice(n * LANES, (n + 1) * LANES)
        grad, values = first_sum.chunk(lanes), own_tokens[:, lanes].astype(f32)
        gain_part[0:1, lanes] = jnp.sum(grad * values * scale, axis=0, keepdims=True)
        input_grad[:, lanes] += scale * (
            grad * gains[0:1, lanes] - values * scale * scale * inner
        )

    gain_copies = []
    for n, relation in enumerate(RELATIONS):
        copy = remote(
            gain_part, gain_plane.at[n], gain_send.at[n], gain_recv.at[n], place.peer(relation)
        )
        copy.start()
        gain_copies.append(copy)

    up_out.finish()
    landed = pltpu.make_async_copy(up_landed, up_share, load.at[1])
    landed.start()
    for copy in gain_copies:
        copy.wait()
    total = gain_part[...]
    for n in range(len(RELATIONS)):
        total += gain_plane[n]
    gain_far[0] = total
    gain_copies = []
    for dz in range(1, grps):
        copy = remote(
            gain_far.at[0],
            gain_far.at[dz],
            gain_send.at[7 + dz],
            gain_recv.at[7 + dz],
            place.plane(dz),
        )
        copy.start()
        gain_copies.append(copy)
    landed.wait()
    summed_rows(up_share, up_out.holds, up_sum)
    up_swap = Exchange(place, up_sum, up_held, swap_send.at[0], swap_recv.at[0], own_sem.at[4])
    for copy in gain_copies:
        copy.wait()
    total = gain_far[0]
    for dz in range(1, grps):
        total += gain_far[dz]
    gains_sum[...] = total

    qkv_out.finish()
    landed = pltpu.make_async_copy(qkv_landed, qkv_share, load.at[6])
    landed.start()
    landed.wait()
    summed_rows(qkv_share, qkv_out.holds, qkv_sum)
    qkv_swap = Exchange(place, qkv_sum, qkv_held, swap_send.at[1], swap_recv.at[1], own_sem.at[5])
    if aligned:
        out_out.finish()
    else:
        out_out.wait()
    up_swap.finish()
    qkv_swap.finish()


def backward(
    grps,
    aligned,
    facts,
    gains,
    tables,
    residual,
    own_tokens,
    own_grad,
    grad_both,
    up_local,
    second_norm,
    first_norm,
    out_local,
    qkv_local,
    heads,
    hidden,
    down_local,
):
    rows = residual.shape[0]
    count, full_rows, head_width = heads[0].shape
    seqs = full_rows // rows
    ranks = seqs * QUAD
    both = grad_both.shape[2]
    quad_rows = D // (seqs * grps)
    shard = quad_rows // QUAD
    out_rows = head_width // grps if aligned else HEAD_DIM
    triple = 3 * head_width
    out_count = head_width // out_rows
    hbm = pl.BlockSpec(memory_space=pl.ANY)
    vmem = pl.BlockSpec(memory_space=pltpu.VMEM)
    shape = jax.ShapeDtypeStruct
    dma = pltpu.SemaphoreType.DMA
    return pl.pallas_call(
        lambda *refs: back_kernel(grps, aligned, *refs),
        in_specs=[vmem] * 7 + [hbm] * 12,
        out_specs=[vmem] * 3 + [hbm] * 8,
        out_shape=[
            shape((rows, D), f32),
            shape((rows, D), bf16),
            shape((8, D), f32),
            shape((out_count, out_rows, D), bf16),
            shape((ranks, shard, both), bf16),
            shape((ranks, shard, triple), bf16),
            shape((grps, seqs, quad_rows, both), bf16),
            shape((grps, seqs, quad_rows, triple), bf16),
            shape((seqs, quad_rows, both), bf16),
            shape((out_rows, D), bf16),
            shape((seqs, quad_rows, triple), bf16),
        ],
        scratch_shapes=[
            pltpu.VMEM((count, full_rows, both), bf16),
            pltpu.VMEM((D, both), bf16),
            pltpu.VMEM((count, full_rows, D), bf16),
            pltpu.VMEM((head_width, D), bf16),
            pltpu.VMEM((D, triple), bf16),
            pltpu.VMEM((ranks, rows, D), bf16),
            pltpu.VMEM((4, rows, D), bf16),
            pltpu.VMEM((3, rows, D), bf16),
            pltpu.VMEM((ranks, rows, D), bf16),
            pltpu.VMEM((count, full_rows, triple), bf16),
            pltpu.VMEM((grps, seqs, quad_rows, both), bf16),
            pltpu.VMEM((out_count, out_rows, D), bf16),
            pltpu.VMEM((grps, seqs, quad_rows, triple), bf16),
            pltpu.VMEM((ranks, shard, both), bf16),
            pltpu.VMEM((ranks, shard, triple), bf16),
            pltpu.VMEM((out_rows, D), bf16),
            pltpu.VMEM((seqs, quad_rows, both), bf16),
            pltpu.VMEM((8, D), f32),
            pltpu.VMEM((7, 8, D), f32),
            pltpu.VMEM((grps, 8, D), f32),
            dma((14,)),
            dma((4,)),
            dma((4,)),
            dma((3,)),
            dma((3,)),
            dma((7,)),
            dma((7,)),
            dma((4, grps)),
            dma((4, grps)),
            dma((2, 7)),
            dma((2, 7)),
            dma((7 + grps,)),
            dma((7 + grps,)),
            dma((6,)),
            pltpu.SemaphoreType.REGULAR,
            pltpu.SemaphoreType.REGULAR,
        ],
        compiler_params=pltpu.CompilerParams(
            collective_id=0, has_side_effects=True, vmem_limit_bytes=VMEM_LIMIT
        ),
        cost_estimate=pl.CostEstimate(
            flops=30 * 10**9, bytes_accessed=60 * 2**20, transcendentals=2 * 10**6
        ),
        name="backward",
    )(
        facts,
        gains,
        *tables,
        residual,
        own_tokens,
        own_grad,
        grad_both,
        up_local,
        second_norm,
        first_norm,
        out_local,
        qkv_local,
        *heads,
        hidden,
        down_local,
    )


CHUNK = 1024


class FromOwners:
    def __init__(self, place, source, landed, landing, send, recv, own):
        self.place, self.source, self.send, self.recv = place, source, send, recv
        self.slot = lambda j: landing(landed, j)
        self.own = pltpu.make_async_copy(source, self.slot(place.g), own)
        self.line = place.grps == 4

    def copy(self, source, slot, sem, recv, target):
        place = self.place
        return remote(
            source, self.slot(slot), self.send.at[sem], self.recv.at[recv], (place.s, target, place.r, place.c)
        )

    def passed(self, g, j, target):
        source = self.source if j == g else self.slot(j)
        return self.copy(source, j, j + (4 if target > g else 0), j, target)

    def arrived(self, j):
        self.copy(self.source, j, j, j, j).wait_recv()

    def on_line(self, steps):
        for g in range(4):
            if steps[g]:

                @pl.when(self.place.g == g)
                def _():
                    for awaited, j, target in steps[g]:
                        if awaited is not None:
                            self.arrived(awaited)
                        if target is not None:
                            self.passed(g, j, target).start()

    FIRST = (
        ((None, 0, 1),),
        ((None, 1, 0), (None, 1, 2)),
        ((None, 2, 3), (None, 2, 1)),
        ((None, 3, 2),),
    )
    SECOND = (
        ((1, 1, None),),
        ((2, 2, 0), (0, 0, 2)),
        ((1, 1, 3), (3, 3, 1)),
        ((2, 2, None),),
    )
    THIRD = ((), ((3, 3, 0),), ((0, 0, 3),), ())

    def start(self):
        place = self.place
        self.own.start()
        if self.line:
            self.on_line(self.FIRST)
        else:
            self.copies = [
                self.copy(self.source, place.g, dz, dz, (place.g + dz) % place.grps)
                for dz in range(1, place.grps)
            ]
            for copy in self.copies:
                copy.start()

    def second(self):
        if self.line:
            self.on_line(self.SECOND)

    def third(self):
        if self.line:
            self.on_line(self.THIRD)

    def finish(self):
        self.own.wait()
        if self.line:
            for g in range(4):

                @pl.when(self.place.g == g)
                def _():
                    for j in {0: (2, 3), 3: (1, 0)}.get(g, ()):
                        self.arrived(j)
                    for steps in (self.FIRST, self.SECOND, self.THIRD):
                        for _, j, target in steps[g]:
                            if target is not None:
                                self.passed(g, j, target).wait_send()

        else:
            for copy in self.copies:
                copy.wait()


class Chain:
    def __init__(self, place, part, through, landed, lanes, send, recv, own):
        self.place, self.part, self.through, self.landed = place, part, through, landed
        self.send, self.recv = send, recv
        self.area = (slice(0, landed.shape[1]), lanes)
        self.own = pltpu.make_async_copy(self.block(part, place.g), self.block(landed, 2), own)

    def block(self, ref, j):
        return ref.at[(j, *self.area)]

    def copy(self, g, j):
        place, target = self.place, g + 1 if j > g else g - 1
        if target == j:
            landing = self.block(self.landed, 0 if j > g else 1)
        else:
            landing = self.block(self.through, j)
        recv = j if target != j else (j if j > g else 4)
        return remote(
            self.block(self.part, j), landing, self.send.at[j], self.recv.at[recv], (place.s, target, place.r, place.c)
        )

    def each(self, planes, action):
        for g in planes:

            @pl.when(self.place.g == g)
            def _():
                action(g)

    def blocks(self, g):
        return (3, 2, 1) if g == 0 else (0, 1, 2)

    def start(self):
        self.own.start()
        self.each((0, 3), lambda g: self.copy(g, self.blocks(g)[0]).start())

    def add(self, g, source, j):
        self.copy(source, j).wait_recv()
        area = (j, *self.area)
        self.part[area] = (self.part[area].astype(f32) + self.through[area].astype(f32)).astype(bf16)
        self.copy(g, j).start()

    def step(self, n):
        def ends(g):
            self.copy(g, self.blocks(g)[n - 1]).wait_send()
            self.copy(g, self.blocks(g)[n]).start()

        def inner(g):
            end = 0 if g == 1 else 3
            self.add(g, end, self.blocks(end)[n - 1])

        self.each((0, 3), ends)
        self.each((1, 2), inner)

    def last(self):
        self.each((1, 2), lambda g: self.add(g, 3 - g, 0 if g == 1 else 3))

    def finish(self):
        self.own.wait()

        def done(g):
            if g > 0:
                self.copy(g - 1, g).wait_recv()
            if g < 3:
                self.copy(g + 1, g).wait_recv()
            if g in (0, 3):
                self.copy(g, self.blocks(g)[2]).wait_send()
            else:
                for j in range(4):
                    if j != g:
                        self.copy(g, j).wait_send()

        self.each(range(4), done)


def shares_from(seq, values, weight, part):
    rows = part.shape[1]

    @pl.loop(0, part.shape[2] // LANES)
    def _(n):
        product = dot(values[seq], weight[:, lanes_of(n)])
        part[2 * seq, :, lanes_of(n)] = product[:rows].astype(bf16)
        part[2 * seq + 1, :, lanes_of(n)] = product[rows:].astype(bf16)


def times_slices(values, weight, lanes):
    seqs, grps, quad, shard, _ = weight.shape
    depth = quad * shard
    total = None
    for n in range(seqs * grps):
        piece = weight[n // grps, n % grps, :, :, lanes]
        term = dot(values[:, n * depth : (n + 1) * depth], piece.reshape(depth, piece.shape[2]))
        total = term if total is None else total + term
    return total


def both_blocks(blocks, seq):
    return jnp.concatenate([blocks[2 * seq].astype(f32), blocks[2 * seq + 1].astype(f32)], axis=0)


def forward_kernel(
    grps,
    aligned,
    cosine,
    sine,
    own_facts,
    tokens_h,
    own_grad_h,
    qkv_own,
    up_own,
    out_own,
    down_own,
    residual,
    gains,
    facts,
    first_h,
    q_h,
    k_h,
    v_h,
    o_h,
    second_h,
    grads_landed,
    hidden_h,
    dgu_h,
    qkv_landed,
    up_landed,
    out_landed,
    down_landed,
    blocks,
    grad_blocks,
    norm,
    grad_seq,
    qkv_rank,
    up_rank,
    qkv,
    up,
    out_w,
    down,
    heads,
    part,
    near,
    far,
    both,
    hidden,
    dgu,
    all_facts,
    early,
    load,
    store,
    swap_send,
    swap_recv,
    near_send,
    near_recv,
    far_send,
    far_recv,
    all_send,
    all_recv,
    z_send,
    z_recv,
    fact_send,
    fact_recv,
    chain_send,
    chain_recv,
    own_sem,
):
    place = Place(grps)
    count, full_rows, _ = norm.shape
    rows = residual.shape[0]
    head_width = heads.shape[3]
    mine, rank = place.seat(), place.rank()

    def fetch(src, dst, n):
        copy = pltpu.make_async_copy(src, dst, load.at[n])
        copy.start()
        return copy

    def keep(src, dst, n):
        copy = pltpu.make_async_copy(src, dst, store.at[n])
        copy.start()
        return copy

    shard = qkv_own.shape[0]
    units = down.shape[0] // grps
    seqs = qkv_landed.shape[0]
    slots = iter(range(20))

    def fetch_chunks(src):
        pieces = []
        for top in range(0, src.shape[0], shard):
            for left in range(0, src.shape[1], CHUNK):
                slot = next(slots)
                space = both.at[slot // 5, (slot % 5) * shard : (slot % 5 + 1) * shard]
                copy = pltpu.make_async_copy(
                    src.at[top : top + shard, left : left + CHUNK], space, early.at[slot]
                )
                copy.start()
                pieces.append((copy, space))
        return pieces

    def dealt(pieces, weight, lanes, parts):
        count = CHUNK // (QUAD * lanes)
        width = count * lanes
        each = len(pieces) // (parts * seqs)
        for n, (copy, space) in enumerate(pieces):
            copy.wait()
            values = space[...]
            seq = n // each % seqs
            first = (n // (each * seqs) * each + n % each) * width
            for q in range(QUAD):
                taken = [
                    values[:, (k * QUAD + q) * lanes : (k * QUAD + q + 1) * lanes] for k in range(count)
                ]
                weight[0, seq, q, :, first : first + width] = jnp.concatenate(taken, axis=1).astype(bf16)

    facts[rank] = own_facts[...]
    if aligned:
        out_pieces = fetch_chunks(out_own)
    qkv_pieces = fetch_chunks(qkv_own)
    up_pieces = fetch_chunks(up_own)
    down_pieces = fetch_chunks(down_own)
    own_blocks = [fetch(tokens_h, blocks.at[mine], 0), fetch(own_grad_h, grad_blocks.at[mine], 1)]

    def plane_rows(ref, j):
        return ref.at[:, j]

    def own_rows(ref, j):
        size = ref.shape[0] // grps
        return ref.at[pl.ds(pl.multiple_of(j * size, size), size)]

    def rows_of(ref, j):
        top = j * units
        return ref.at[top // 128, pl.ds(pl.multiple_of(top % 128, units), units)]

    def from_owners(n, source, landed, landing):
        return FromOwners(place, source, landed, landing, z_send.at[n], z_recv.at[n], own_sem.at[n])

    def stacked(pieces, weight):
        across = weight.shape[1] // CHUNK
        for n, (copy, space) in enumerate(pieces):
            copy.wait()
            top, left = n // across * shard, n % across * CHUNK
            weight[top : top + shard, left : left + CHUNK] = space[...].astype(bf16)

    down_z = from_owners(3, down.at[:units], down_landed, own_rows)
    if aligned:
        stacked(out_pieces, out_w)
        out_z = from_owners(2, out_w.at[:shard], out_landed, own_rows)
    place.greet()
    if aligned:
        out_z.start()
    dealt(qkv_pieces, qkv, HEAD_DIM, 3)
    qkv_swap = Exchange(place, qkv, qkv_rank, swap_send.at[0], swap_recv.at[0], own_sem.at[4])
    fact_copies = []
    for n, relation in enumerate(RELATIONS):
        copy = remote(own_facts, facts.at[rank], fact_send.at[n], fact_recv.at[n], place.peer(relation))
        copy.start()
        fact_copies.append(copy)
    if aligned:
        out_z.second()
    dealt(up_pieces, up, units, 2)
    stacked(down_pieces, down)
    for copy in own_blocks:
        copy.wait()
    if aligned:
        out_z.third()
    qkv_swap.finish()
    qkv_z = from_owners(0, qkv_rank, qkv_landed, plane_rows)
    up_z = from_owners(1, up_rank, up_landed, plane_rows)
    qkv_z.start()
    token_gather = PlaneGather(place, blocks, all_send.at[0], all_recv.at[0])
    token_gather.start()
    for copy in fact_copies:
        copy.wait()
    all_facts[place.g] = facts[...]
    fact_copies = []
    for dz in range(1, grps):
        copy = remote(
            facts,
            all_facts.at[place.g],
            fact_send.at[7 + dz],
            fact_recv.at[7 + dz],
            place.plane(dz),
        )
        copy.start()
        fact_copies.append(copy)
    for copy in fact_copies:
        copy.wait()
    width = D // (seqs * grps * QUAD)
    for n in range(seqs * grps):
        pieces = [all_facts[n % grps, (n // grps) * QUAD + q, :, :width] for q in range(QUAD)]
        gains[:, n * QUAD * width : (n + 1) * QUAD * width] = jnp.concatenate(pieces, axis=1)
    token_gather.forward(0)
    token_gather.forward(1)
    up_swap = Exchange(place, up, up_rank, swap_send.at[1], swap_recv.at[1], own_sem.at[5])
    qkv_z.second()
    token_gather.forward(2)
    token_gather.arrive(3)
    token_gather.copies[3].wait_recv()
    token_gather.copies[4].wait_recv()
    token_gather.finish()

    @pl.loop(0, count)
    def _(seq):
        values = both_blocks(blocks, seq)
        scale = lax.rsqrt(jnp.mean(values * values, axis=-1, keepdims=True) + NORM_EPSILON)
        norm[seq] = (values * scale * gains[0:1, :]).astype(bf16)

    stores = [keep(norm, first_h, 0)]
    grad_gather = PlaneGather(place, grad_blocks, all_send.at[1], all_recv.at[1])
    grad_gather.start()
    qkv_z.third()
    up_swap.finish()
    qkv_z.finish()
    up_z.start()
    fetch(qkv_landed, qkv, 2).wait()

    lane = lax.broadcasted_iota(jnp.int32, (full_rows, head_width), 1)
    first_half = (lane % HEAD_DIM) < HEAD_DIM // 2

    if aligned:
        out_z.finish()
        fetch(out_landed, out_w, 3).wait()
    else:
        fetch(out_own, out_w, 3).wait()

    plane_sum = PlaneSum(place, part, near, far, (near_send, near_recv, far_send, far_recv))
    mixed = heads.at[3]
    for k in range(4):
        seq = plane_sum.sequence(k)
        for n in range(3):
            lanes = slice(n * head_width, (n + 1) * head_width)
            values = times_slices(norm[seq], qkv, lanes)
            if n < 2:
                values = values * cosine[...] + swap_halves(values, first_half) * sine[...]
            heads[n, seq] = values.astype(bf16)
        heads[3, seq] = attention(facts[seq, 2:3, 0:1], heads[0, seq], heads[1, seq], heads[2, seq])
        shares_from(seq, mixed, out_w, part)
        if k % 2 == 0:
            plane_sum.near(k)
        else:
            plane_sum.far(k)
        if k == 0:
            grad_gather.forward(0)
            grad_gather.forward(1)
    grad_gather.forward(2)
    grad_gather.arrive(3)
    grad_gather.copies[3].wait_recv()
    grad_gather.copies[4].wait_recv()
    grad_gather.finish()
    stores += [keep(heads.at[n], ref, 1 + n) for n, ref in enumerate((q_h, k_h, v_h, o_h))]
    up_z.second()

    @pl.loop(0, count)
    def _(seq):
        grad_seq[seq] = both_blocks(grad_blocks, seq).astype(bf16)

    fetch(tokens_h, grad_blocks.at[mine], 4).wait()
    plane_sum.finish()
    squares = jnp.zeros((rows, 1), f32)
    for n in range(D // LANES):
        lanes = slice(n * LANES, (n + 1) * LANES)
        values = grad_blocks[mine, :, lanes].astype(f32) + plane_sum.chunk(lanes)
        residual[:, lanes] = values
        squares += jnp.sum(values * values, axis=-1, keepdims=True)
    scale = lax.rsqrt(squares / D + NORM_EPSILON)
    for n in range(D // LANES):
        lanes = slice(n * LANES, (n + 1) * LANES)
        blocks[mine, :, lanes] = (residual[:, lanes] * scale * gains[1:2, lanes]).astype(bf16)
    norm_gather = PlaneGather(place, blocks, all_send.at[2], all_recv.at[2])
    norm_gather.start()
    up_z.third()
    stores[0].wait()
    half = hidden.shape[2]
    for k in range(4):
        norm_gather.arrive(k, forwarded=k == 1)
        seq = norm_gather.sequence(k)
        norm[seq] = both_blocks(blocks, seq).astype(bf16)
        if k == 0:
            norm_gather.forward(1)
            up_z.finish()
            down_z.start()
            fetch(up_landed, up, 5).wait()
        elif k == 2:
            down_z.second()
        gate = times_slices(norm[seq], up, slice(0, half))
        above = times_slices(norm[seq], up, slice(half, 2 * half))
        both[seq, :, :half] = gate
        both[seq, :, half:] = above
        hidden[seq] = (gate * jax.nn.sigmoid(gate) * above).astype(bf16)
    norm_gather.finish()
    stores[0] = keep(norm, second_h, 5)
    stores.append(keep(hidden, hidden_h, 7))
    tall = min(256, half)
    slab = part.shape[1] // 128 * 128

    def down_shares(side):
        lanes = slice(side * D // 2, (side + 1) * D // 2)

        @pl.loop(0, half // tall)
        def _(b):
            product = over_tokens(hidden, lanes_of(b, tall), grad_seq, lanes).astype(bf16)
            for p in range(tall // slab):
                part[b * (tall // slab) + p, :slab, lanes] = product[p * slab : (p + 1) * slab]

    down_shares(0)
    if grps == 4:
        chains = [
            Chain(
                place,
                part,
                near,
                grads_landed,
                slice(side * D // 2, (side + 1) * D // 2),
                chain_send.at[side],
                chain_recv.at[side],
                own_sem.at[6 + side],
            )
            for side in range(2)
        ]
        chains[0].start()
    down_z.third()
    down_shares(1)
    if grps == 4:
        chains[1].start()
        chains[0].step(1)
        chains[1].step(1)
        chains[0].step(2)
    else:
        spread = [pltpu.make_async_copy(rows_of(part, place.g), grads_landed.at[place.g], own_sem.at[6])]
        for dz in range(1, grps):
            spread.append(
                remote(
                    rows_of(part, (place.g + dz) % grps),
                    grads_landed.at[place.g],
                    chain_send.at[0, dz],
                    chain_recv.at[0, dz],
                    place.plane(dz),
                )
            )
        for copy in spread:
            copy.start()
    down_z.finish()
    down_copy = fetch(down_landed, down, 6)
    if grps == 4:
        chains[0].last()
        chains[1].step(2)
        chains[1].last()
    down_copy.wait()

    def feed_forward_grads(seq):
        grads = dot(grad_seq[seq], down[...], 1, 1)
        gate, above = both[seq, :, :half], both[seq, :, half:]
        sigmoid = jax.nn.sigmoid(gate)
        dgu[seq, :, :half] = (grads * above * sigmoid * (1.0 + gate * (1.0 - sigmoid))).astype(bf16)
        dgu[seq, :, half:] = (grads * (gate * sigmoid)).astype(bf16)

    pl.loop(0, count)(feed_forward_grads)
    stores.append(keep(dgu, dgu_h, 8))
    if grps == 4:
        for chain in chains:
            chain.finish()
    else:
        for copy in spread:
            copy.wait()
    for copy in stores:
        copy.wait()


def forward(grps, aligned, tables, own_facts, tokens, own_grad, qkv_own, up_own, out_own, down_own):
    rows = tokens.shape[0]
    shard = qkv_own.shape[0]
    seqs = D // (shard * grps * QUAD)
    ranks = seqs * QUAD
    triple, both = qkv_own.shape[1] // ranks, up_own.shape[1] // ranks
    count, full_rows, head_width = QUAD, rows * seqs, triple // 3
    half = both // 2
    hbm = pl.BlockSpec(memory_space=pl.ANY)
    vmem = pl.BlockSpec(memory_space=pltpu.VMEM)
    shape = jax.ShapeDtypeStruct
    dma = pltpu.SemaphoreType.DMA
    by_heads = shape((count, full_rows, head_width), bf16)
    return pl.pallas_call(
        lambda *refs: forward_kernel(grps, aligned, *refs),
        in_specs=[vmem] * 3 + [hbm] * 6,
        out_specs=[vmem] * 3 + [hbm] * 13,
        out_shape=[
            shape((rows, D), f32),
            shape((8, D), f32),
            shape((ranks, 8, 128), f32),
            shape((count, full_rows, D), bf16),
            by_heads,
            by_heads,
            by_heads,
            by_heads,
            shape((count, full_rows, D), bf16),
            shape((3 if grps == 4 else grps, half // grps, D), bf16),
            shape((count, full_rows, half), bf16),
            shape((count, full_rows, both), bf16),
            shape((seqs, grps, QUAD, shard, triple), bf16),
            shape((seqs, grps, QUAD, shard, both), bf16),
            shape((head_width, D), bf16),
            shape((half, D), bf16),
        ],
        scratch_shapes=[
            pltpu.VMEM((ranks, rows, D), bf16),
            pltpu.VMEM((ranks, rows, D), bf16),
            pltpu.VMEM((count, full_rows, D), bf16),
            pltpu.VMEM((count, full_rows, D), bf16),
            pltpu.VMEM((seqs, QUAD, shard, triple), bf16),
            pltpu.VMEM((seqs, QUAD, shard, both), bf16),
            pltpu.VMEM((seqs, grps, QUAD, shard, triple), bf16),
            pltpu.VMEM((seqs, grps, QUAD, shard, both), bf16),
            pltpu.VMEM((head_width, D), bf16),
            pltpu.VMEM((half, D), bf16),
            pltpu.VMEM((4, count, full_rows, head_width), bf16),
            pltpu.VMEM((ranks, rows, D), bf16),
            pltpu.VMEM((4, rows, D), bf16),
            pltpu.VMEM((3, rows, D), bf16),
            pltpu.VMEM((count, full_rows, both), f32),
            pltpu.VMEM((count, full_rows, half), bf16),
            pltpu.VMEM((count, full_rows, both), bf16),
            pltpu.VMEM((grps, ranks, 8, 128), f32),
            dma((20,)),
            dma((7,)),
            dma((9,)),
            dma((2, 7)),
            dma((2, 7)),
            dma((4,)),
            dma((4,)),
            dma((3,)),
            dma((3,)),
            dma((3, 7)),
            dma((3, 7)),
            dma((4, 2 * grps)),
            dma((4, grps)),
            dma((7 + grps,)),
            dma((7 + grps,)),
            dma((2, max(5, grps))),
            dma((2, max(5, grps))),
            dma((8,)),
        ],
        compiler_params=pltpu.CompilerParams(
            collective_id=1, has_side_effects=True, vmem_limit_bytes=VMEM_LIMIT
        ),
        cost_estimate=pl.CostEstimate(
            flops=20 * 10**9, bytes_accessed=60 * 2**20, transcendentals=4 * 10**6
        ),
        name="forward",
    )(*tables, own_facts, tokens, own_grad, qkv_own, up_own, out_own, down_own)


DEPTH = 4


def adam_kernel(grps, down_planes, out_planes, up_ranks, qkv_ranks, gains_sum, gains, gains_m, gains_v, *refs):
    states, outs = refs[:12], refs[12:28]
    gains_outs = refs[28:31]
    state, planes, ranks, fresh, copied, in_sem, out_sem = refs[31:]
    plane = lax.axis_index("grp")
    rows = state.shape[2]
    units = CHUNK // QUAD
    pieces = []
    for n, (name, rate) in enumerate(
        (("down", FF ** (-0.5)), ("out", (D // 128) ** (-0.5)), ("up", D ** (-0.5)), ("qkv", D ** (-0.5)))
    ):
        arrays = states[3 * n : 3 * n + 3]
        for top in range(0, arrays[0].shape[0], rows):
            for left in range(0, arrays[0].shape[1], CHUNK):
                pieces.append((name, rate, n, top, left))

    def grad_source(name, top, left, slot):
        if name in ("down", "out"):
            source = down_planes if name == "down" else out_planes
            return (
                source.at[:, top : top + rows, left : left + CHUNK],
                planes.at[slot, : source.shape[0]],
            )
        source, parts = (up_ranks, 2) if name == "up" else (qkv_ranks, 3)
        width = source.shape[2] // parts
        per_seq = width // units
        n = left // CHUNK
        seqs = source.shape[0] // QUAD
        seq = n // per_seq % seqs
        first = n // (per_seq * seqs) * width + n % per_seq * units
        return source.at[seq * QUAD : (seq + 1) * QUAD, :, first : first + units], ranks.at[slot]

    def reads(k):
        name, _, n, top, left = pieces[k]
        slot = k % DEPTH
        window = (slice(top, top + rows), slice(left, left + CHUNK))
        copies = [
            pltpu.make_async_copy(states[3 * n + i].at[window], state.at[slot, i], in_sem.at[slot, i])
            for i in range(3)
        ]
        source, space = grad_source(name, top, left, slot)
        return copies + [pltpu.make_async_copy(source, space, in_sem.at[slot, 3])]

    def writes(k):
        _, _, n, top, left = pieces[k]
        slot = k % DEPTH
        window = (slice(top, top + rows), slice(left, left + CHUNK))
        copies = [
            pltpu.make_async_copy(fresh.at[slot, i], outs[4 * n + i].at[window], out_sem.at[slot, i])
            for i in range(3)
        ]
        return copies + [
            pltpu.make_async_copy(copied.at[slot], outs[4 * n + 3].at[window], out_sem.at[slot, 3])
        ]

    def gradient(name, slot):
        if name in ("down", "out"):
            chained = name == "down"
            source = down_planes if chained else out_planes
            total = jnp.zeros((rows, CHUNK), f32)
            for j in range(source.shape[0]):
                held = planes[slot, j].astype(f32)
                if grps == 4 and chained and j < 2:
                    held = jnp.where(plane > 0 if j == 0 else plane < 3, held, 0.0)
                elif grps == 4 and not chained and j in (0, 3):
                    held = jnp.where(plane != 3 - j, held, 0.0)
                total += held
            return total
        lanes = down_planes.shape[1] if name == "up" else HEAD_DIM
        values = [ranks[slot, q].astype(f32) for q in range(QUAD)]
        return jnp.concatenate(
            [
                values[q][:, n * lanes : (n + 1) * lanes]
                for n in range(units // lanes)
                for q in range(QUAD)
            ],
            axis=1,
        )

    for k in range(DEPTH - 1):
        for copy in reads(k):
            copy.start()
    results = adam_update(gains[...], gains_m[...], gains_v[...], gains_sum[...], 0.3)
    for out, result in zip(gains_outs, results):
        out[...] = result
    for k, (name, rate, _, _, _) in enumerate(pieces):
        slot = k % DEPTH
        if k + DEPTH - 1 < len(pieces):
            for copy in reads(k + DEPTH - 1):
                copy.start()
        for copy in reads(k):
            copy.wait()
        if k >= DEPTH:
            for copy in writes(k - DEPTH):
                copy.wait()
        results = adam_update(state[slot, 0], state[slot, 1], state[slot, 2], gradient(name, slot), rate)
        for i in range(3):
            fresh[slot, i] = results[i]
        copied[slot] = results[0].astype(bf16)
        for copy in writes(k):
            copy.start()
    for k in range(len(pieces) - DEPTH, len(pieces)):
        for copy in writes(k):
            copy.wait()


def adam(grps, down_planes, out_planes, up_ranks, qkv_ranks, gains_sum, gains, states):
    rows = up_ranks.shape[1]
    hbm = pl.BlockSpec(memory_space=pl.ANY)
    vmem = pl.BlockSpec(memory_space=pltpu.VMEM)
    shapes = []
    for array in states[::3]:
        shapes += [jax.ShapeDtypeStruct(array.shape, f32)] * 3
        shapes.append(jax.ShapeDtypeStruct(array.shape, bf16))
    shapes += [jax.ShapeDtypeStruct(gains[0].shape, f32)] * 3
    size = sum(array.size for array in states) // 3
    outs = pl.pallas_call(
        lambda *refs: adam_kernel(grps, *refs),
        in_specs=[hbm] * 4 + [vmem] * 4 + [hbm] * 12,
        out_specs=[hbm] * 16 + [vmem] * 3,
        out_shape=shapes,
        scratch_shapes=[
            pltpu.VMEM((DEPTH, 3, rows, CHUNK), f32),
            pltpu.VMEM((DEPTH, grps, rows, CHUNK), bf16),
            pltpu.VMEM((DEPTH, QUAD, rows, CHUNK // QUAD), bf16),
            pltpu.VMEM((DEPTH, 3, rows, CHUNK), f32),
            pltpu.VMEM((DEPTH, rows, CHUNK), bf16),
            pltpu.SemaphoreType.DMA((DEPTH, 4)),
            pltpu.SemaphoreType.DMA((DEPTH, 4)),
        ],
        compiler_params=pltpu.CompilerParams(vmem_limit_bytes=VMEM_LIMIT),
        cost_estimate=pl.CostEstimate(flops=size * 16, bytes_accessed=size * 28, transcendentals=size),
        name="adam",
    )(down_planes, out_planes, up_ranks, qkv_ranks, gains_sum, *gains, *states)
    return outs[:4], outs[4:8], outs[8:12], outs[12:16], outs[16:]


def on_device(
    tokens,
    cotangent,
    lengths,
    qkv_weight,
    qkv_moment,
    qkv_square,
    out_weight,
    out_moment,
    out_square,
    up_weight,
    up_moment,
    up_square,
    down_weight,
    down_moment,
    down_square,
    norm_gains,
    gains_moment,
    gains_square,
):
    seqs = lax.axis_size("seq")
    grps = lax.axis_size("grp")
    ranks = seqs * QUAD
    own_rows = tokens.shape[1]
    full_rows = own_rows * seqs
    all_rows = full_rows * QUAD
    heads_local = HEADS // ranks
    head_width = heads_local * HEAD_DIM
    units = down_weight.shape[0]
    aligned = out_weight.shape[0] == HEAD_DIM
    tables = rotate_table(full_rows, heads_local)

    positions = lax.axis_index("seq") * own_rows + jnp.arange(own_rows, dtype=jnp.int32)
    own_grad = jnp.where((positions < lengths[0])[:, None], cotangent[0], 0)
    own_gains = norm_gains.shape[1]
    own_facts = jnp.zeros((8, 128), f32)
    own_facts = own_facts.at[:2, :own_gains].set(norm_gains.astype(bf16).astype(f32))
    own_facts = own_facts.at[2].set(lengths[0].astype(f32))

    out_own = out_weight
    if not aligned:
        out_all = lax.all_gather(out_weight.astype(bf16), EVERY, axis=0, tiled=True)
        out_all = out_all.reshape(seqs, heads_local, QUAD, HEAD_DIM, D)
        seat = lax.axis_index("row") * 2 + lax.axis_index("core")
        out_own = lax.dynamic_index_in_dim(
            lax.dynamic_index_in_dim(out_all, lax.axis_index("seq"), 0, False), seat, 1, False
        ).reshape(head_width, D)
    (
        residual,
        gains,
        facts,
        first_norm,
        queries,
        key_vectors,
        value_vectors,
        attended,
        second_norm,
        down_planes,
        hidden,
        grad_both,
        qkv_local,
        up_local,
        out_local,
        down_local,
    ) = forward(
        grps,
        aligned,
        tables,
        own_facts,
        tokens[0],
        own_grad,
        qkv_weight,
        up_weight,
        out_own,
        down_weight,
    )
    if not aligned:
        out_local = out_own
    (
        input_grad,
        block_output,
        gains_total,
        out_planes,
        up_ranks,
        qkv_ranks,
        *_,
    ) = backward(
        grps,
        aligned,
        facts,
        gains,
        tables,
        residual,
        tokens[0],
        own_grad,
        grad_both,
        up_local.reshape(D, -1),
        second_norm,
        first_norm,
        out_local,
        qkv_local.reshape(D, -1),
        (queries, key_vectors, value_vectors, attended),
        hidden,
        down_local,
    )
    if aligned:
        out_sum = out_planes
    else:
        placed_term = jnp.zeros((seqs, QUAD, heads_local, HEAD_DIM, D), bf16)
        placed_term = lax.dynamic_update_slice(
            placed_term,
            out_planes.reshape(1, 1, heads_local, HEAD_DIM, D),
            (lax.axis_index("seq"), seat, 0, 0, 0),
        )
        out_sum = lax.psum_scatter(
            placed_term.transpose(0, 2, 1, 3, 4).reshape(D, D),
            EVERY,
            scatter_dimension=0,
            tiled=True,
        )[None]
    device = ((lax.axis_index("seq") * grps + lax.axis_index("grp")) * 2 + lax.axis_index("row")) * 2
    gains_sum = lax.dynamic_slice(
        gains_total, (0, (device + lax.axis_index("core")) * own_gains), (2, own_gains)
    )
    down_new, out_new, up_new, qkv_new, gains_new = adam(
        grps,
        down_planes,
        out_sum,
        up_ranks,
        qkv_ranks,
        gains_sum,
        (norm_gains, gains_moment, gains_square),
        (
            down_weight,
            down_moment,
            down_square,
            out_weight,
            out_moment,
            out_square,
            up_weight,
            up_moment,
            up_square,
            qkv_weight,
            qkv_moment,
            qkv_square,
        ),
    )
    return (
        block_output[None],
        input_grad[None],
        *qkv_new,
        *out_new,
        *up_new,
        *down_new,
        *gains_new,
    )


def solution(mesh):
    seqs, rest = mesh.shape["seq"], mesh.shape["fsdp"]
    planes = Mesh(
        mesh.devices.reshape(seqs, rest // QUAD, 2, 2), ("seq", "grp", "row", "core")
    )
    rows = P(("grp", "row", "core"), "seq", None)
    shards = P(EVERY, None)
    gains = P(None, EVERY)
    return jax.shard_map(
        on_device,
        mesh=planes,
        in_specs=(rows, rows, P(("grp", "row", "core"))) + (shards,) * 12 + (gains,) * 3,
        out_specs=(rows, rows) + (shards,) * 16 + (gains,) * 3,
        check_vma=False,
    )
```

```python
import math

import jax
import jax.numpy as jnp
from jax import lax
from jax.experimental import pallas as pl
from jax.experimental.pallas import tpu as pltpu
from jax.sharding import Mesh, PartitionSpec as P

D = 2048
HEADS = 32
HEAD_DIM = 64
FF = 4096
WINDOW = 128
STEP = 5


NORM_EPSILON = 1e-05
MOMENT_DECAY = 0.5
WEIGHT_DECAY = 0.1
ADAM_EPSILON = 1e-08

SEATS = ("row", "core", "seq")
RANKS = ("seq", "row", "core")
EVERY = ("seq", "grp", "row", "core")
QUAD = 4
VMEM_LIMIT = 63 * 2**20

bf16 = jnp.bfloat16
f32 = jnp.float32


def rotate_table(length, copies):
    halves = HEAD_DIM // 2
    freqs = jnp.exp(-math.log(10000.0) * 2.0 * jnp.arange(halves).astype(f32) / HEAD_DIM)
    angles = jnp.arange(length, dtype=jnp.int32).astype(f32)[:, None] * freqs[None, :]
    cosine, sine = jnp.cos(angles), jnp.sin(angles)
    return (
        jnp.tile(jnp.concatenate([cosine, cosine], axis=1), (1, copies)),
        jnp.tile(jnp.concatenate([-sine, sine], axis=1), (1, copies)),
    )


def adam_update(weight, moment, square, gradient, step_rate):
    moment_new = MOMENT_DECAY * moment + (1.0 - MOMENT_DECAY) * gradient
    square_new = MOMENT_DECAY * square + (1.0 - MOMENT_DECAY) * gradient * gradient
    correction = 1.0 - MOMENT_DECAY**STEP
    unbias = 1.0 / correction
    update = (moment_new * unbias) / (jnp.sqrt(square_new * unbias) + ADAM_EPSILON)
    return (weight - step_rate * (update + WEIGHT_DECAY * weight), moment_new, square_new)


def dot(a, b, lhs=1, rhs=0):
    return lax.dot_general(a, b, (((lhs,), (rhs,)), ((), ())), preferred_element_type=f32)


def swap_halves(values, first):
    width = values.shape[1]
    half = HEAD_DIM // 2
    return jnp.where(
        first, pltpu.roll(values, width - half, 1), pltpu.roll(values, half, 1)
    )


def allowed_mask(rows, length):
    row = lax.broadcasted_iota(jnp.int32, (rows, rows), 0)
    col = lax.broadcasted_iota(jnp.int32, (rows, rows), 1)
    return (col <= row) & (row - col < WINDOW) & (col.astype(f32) < length)


def head_lanes(rows, width, head):
    lane = lax.broadcasted_iota(jnp.int32, (rows, width), 1)
    return (lane // HEAD_DIM) == head


def softmax_rows(queries, key_vectors, allowed):
    scores = jnp.where(allowed, dot(queries, key_vectors, 1, 1) * (HEAD_DIM**-0.5), -1e30)
    shifted = jnp.exp(scores - jnp.max(scores, axis=-1, keepdims=True))
    return shifted / jnp.sum(shifted, axis=-1, keepdims=True)


def attention(length, queries, key_vectors, value_vectors):
    rows, width = queries.shape
    allowed = allowed_mask(rows, length)
    total = jnp.zeros((rows, width), f32)
    for head in range(width // HEAD_DIM):
        mine = head_lanes(rows, width, head)
        weights = softmax_rows(jnp.where(mine, queries, 0), key_vectors, allowed)
        total += dot(weights.astype(bf16), jnp.where(mine, value_vectors, 0))
    return total.astype(bf16)


def attention_grads(length, queries, key_vectors, value_vectors, grads):
    rows, width = queries.shape
    allowed = allowed_mask(rows, length)
    grad_q = jnp.zeros((rows, width), f32)
    grad_k = jnp.zeros((rows, width), f32)
    grad_v = jnp.zeros((rows, width), f32)
    for head in range(width // HEAD_DIM):
        mine = head_lanes(rows, width, head)
        q_head = jnp.where(mine, queries, 0)
        g_head = jnp.where(mine, grads, 0)
        weights = softmax_rows(q_head, key_vectors, allowed)
        grad_p = dot(g_head, value_vectors, 1, 1)
        delta = jnp.sum(weights * grad_p, axis=-1, keepdims=True)
        grad_s = jnp.where(allowed, weights * (grad_p - delta), 0.0).astype(bf16)
        grad_q += dot(grad_s, jnp.where(mine, key_vectors, 0))
        grad_k += dot(grad_s, q_head, 0, 0)
        grad_v += dot(weights.astype(bf16), g_head, 0, 0)
    return grad_q, grad_k, grad_v


MESH = pl.DeviceIdType.MESH
RELATIONS = tuple((a, b, d) for a in range(2) for b in range(2) for d in range(2))[1:]


class Place:
    def __init__(self, grps):
        self.grps = grps
        self.s = lax.axis_index("seq")
        self.g = lax.axis_index("grp")
        self.r = lax.axis_index("row")
        self.c = lax.axis_index("core")

    def peer(self, relation):
        ds, dr, dc = relation
        return ((self.s + ds) % 2, self.g, (self.r + dr) % 2, (self.c + dc) % 2)

    def plane(self, dz):
        return (self.s, (self.g + dz) % self.grps, self.r, self.c)

    def rank(self, relation=(0, 0, 0)):
        s, _, r, c = self.peer(relation)
        return (s * 2 + r) * 2 + c

    def seat(self, relation=(0, 0, 0)):
        s, _, r, c = self.peer(relation)
        return (r * 2 + c) * 2 + s

    def corner(self, relation=(0, 0, 0)):
        s, _, r, _ = self.peer(relation)
        return r * 2 + s

    def greet(self):
        barrier = pltpu.get_barrier_semaphore()
        for relation in RELATIONS:
            pl.semaphore_signal(barrier, inc=1, device_id=self.peer(relation), device_id_type=MESH)
        for dz in range(1, self.grps):
            pl.semaphore_signal(barrier, inc=1, device_id=self.plane(dz), device_id_type=MESH)
        pl.semaphore_wait(barrier, len(RELATIONS) + self.grps - 1)


SIBLING = (0, 0, 1)
ACROSS = ((1, 0, 0), (0, 1, 0), (1, 1, 0))


def remote(src, dst, send_sem, recv_sem, device):
    return pltpu.make_async_remote_copy(
        src_ref=src,
        dst_ref=dst,
        send_sem=send_sem,
        recv_sem=recv_sem,
        device_id=device,
        device_id_type=MESH,
    )


class PlaneSum:
    def __init__(self, place, part, near, far, sems):
        self.place, self.part, self.nears, self.fars = place, part, near, far
        self.near_send, self.near_recv, self.far_send, self.far_recv = sems
        self.first, self.second = [None] * 4, []

    def sequence(self, k):
        place = self.place
        row = (place.r + 1) % 2 if k < 2 else place.r
        return row * 2 + ((place.c + 1) % 2 if k % 2 == 0 else place.c)

    def near(self, k):
        for s in range(2):
            copy = remote(
                self.part.at[2 * self.sequence(k) + s],
                self.nears.at[k + s],
                self.near_send.at[k + s],
                self.near_recv.at[k + s],
                self.place.peer(SIBLING),
            )
            copy.start()
            self.first[k + s] = copy

    def far(self, k):
        place = self.place
        for s in range(2):
            self.first[k - 1 + s].wait()
            self.nears[k - 1 + s] = (
                self.part[2 * self.sequence(k) + s].astype(f32)
                + self.nears[k - 1 + s].astype(f32)
            ).astype(bf16)
        for d in (1, 2) if k == 1 else (0,):
            relation = ACROSS[d]
            copy = remote(
                self.nears.at[k - 1 + (place.s + relation[0]) % 2],
                self.fars.at[d],
                self.far_send.at[d],
                self.far_recv.at[d],
                place.peer(relation),
            )
            copy.start()
            self.second.append(copy)

    def finish(self):
        for copy in self.second:
            copy.wait()

    def chunk(self, lanes):
        total = self.nears[2 + self.place.s, :, lanes].astype(f32)
        for d in range(3):
            total += self.fars[d, :, lanes].astype(f32)
        return total


class PlaneGather:
    def __init__(self, place, blocks, send, recv):
        self.place, self.blocks, self.sends, self.recvs = place, blocks, send, recv
        self.copies = [None] * 7

    def send(self, block, sem, relation):
        copy = remote(
            self.blocks.at[block],
            self.blocks.at[block],
            self.sends.at[sem],
            self.recvs.at[sem],
            self.place.peer(relation),
        )
        copy.start()
        self.copies[sem] = copy

    def start(self):
        mine = self.place.seat()
        for d in range(2):
            self.send(mine, d, ACROSS[d])
        self.send(mine, 3, SIBLING)

    def forward(self, d):
        self.copies[d].wait_recv()
        self.send(self.place.seat(ACROSS[d]), 4 + d, SIBLING)
        if d == 0:
            self.send(self.place.seat(), 2, ACROSS[2])

    def sequence(self, k):
        place = self.place
        row = place.r if k < 2 else (place.r + 1) % 2
        return row * 2 + (place.c if k % 2 == 0 else (place.c + 1) % 2)

    def arrive(self, k, forwarded=False):
        if k == 0:
            self.forward(0)
        elif k == 1:
            if not forwarded:
                self.forward(1)
            self.copies[3].wait_recv()
            self.copies[4].wait_recv()
        elif k == 2:
            self.forward(2)
        else:
            self.copies[5].wait_recv()
            self.copies[6].wait_recv()

    def finish(self):
        for copy in self.copies:
            copy.wait_send()


class ToOwners:
    def __init__(self, place, shares, landed, met, stage, send, recv, own):
        self.place, self.shares, self.landed, self.met, self.stage = place, shares, landed, met, stage
        self.send, self.recv, self.own_sem = send, recv, own
        self.line = place.grps == 4
        self.own = pltpu.make_async_copy(shares.at[place.g], landed.at[place.g], own)

    def copy(self, block, landing, sem, recv, target):
        place = self.place
        return remote(
            self.shares.at[block],
            landing,
            self.send.at[sem],
            self.recv.at[recv],
            (place.s, target, place.r, place.c),
        )

    def direct(self, g):
        targets = ((2, 1), (2, 0), (1, 3), (1, 2))[g]
        return [self.copy(t, self.landed.at[g], t, g, t) for t in targets]

    def meeting(self, g):
        far, inner = (3, 1) if g == 0 else (0, 2)
        return self.copy(far, self.met, far, inner, inner)

    def joined(self, g):
        far = 3 if g == 1 else 0
        return self.copy(far, self.landed.at[g], far, g, far)

    def start(self, waits=False):
        place, self.waits = self.place, waits
        self.own.start()
        if self.line:
            for g in range(4):

                @pl.when(place.g == g)
                def _():
                    if g in (0, 3):
                        self.meeting(g).start()
                    if g in (1, 2) or not waits:
                        for copy in self.direct(g):
                            copy.start()

        else:
            self.copies = [
                self.copy((place.g + dz) % place.grps, self.landed.at[place.g], dz, dz, (place.g + dz) % place.grps)
                for dz in range(1, place.grps)
            ]
            for copy in self.copies:
                copy.start()
        return self

    def proceed(self):
        if self.line:
            for g in (0, 3):

                @pl.when(self.place.g == g)
                def _():
                    self.meeting(g).wait_send()
                    for copy in self.direct(g):
                        copy.start()

    def join(self):
        if not self.line:
            return
        for g in (1, 2):

            @pl.when(self.place.g == g)
            def _():
                outer, far = (0, 3) if g == 1 else (3, 0)
                self.copy(far, self.met, far, g, outer).wait_recv()
                copy = pltpu.make_async_copy(self.met, self.stage, self.own_sem)
                self.own.wait()
                copy.start()
                copy.wait()
                if len(self.stage.shape) == 2:
                    self.shares[far] = (
                        self.shares[far].astype(f32) + self.stage[...].astype(f32)
                    ).astype(bf16)
                else:
                    for n in range(self.stage.shape[0]):
                        self.shares[far, n] = (
                            self.shares[far, n].astype(f32) + self.stage[n].astype(f32)
                        ).astype(bf16)
                self.joined(g).start()

        for g in (0, 3):

            @pl.when(self.place.g == g)
            def _():
                self.own.wait()

    def sent(self):
        if not self.line:
            for copy in self.copies:
                copy.wait_send()
            return
        for g in range(4):

            @pl.when(self.place.g == g)
            def _():
                for copy in self.direct(g):
                    copy.wait_send()
                if g in (1, 2):
                    self.joined(g).wait_send()
                elif not self.waits:
                    self.meeting(g).wait_send()

    def received(self):
        if not self.line:
            self.own.wait()
            for copy in self.copies:
                copy.wait_recv()
            return
        for g in range(4):

            @pl.when(self.place.g == g)
            def _():
                for j in ((1, 2), (0, 2, 3), (0, 1, 3), (1, 2))[g]:
                    self.copy(g, self.landed.at[j], j, j, j).wait_recv()

    def finish(self):
        self.sent()
        self.received()

    def holds(self, j):
        g = self.place.g
        return (g % 3 != 0) | (j + g != 3) if self.line else True


class Exchange:
    def __init__(self, place, blocks, held, send, recv, own):
        mine = place.rank()
        kept = held.at[mine // QUAD, mine % QUAD] if len(held.shape) == 4 else held.at[mine]

        def block(t):
            return blocks.at[0, t // QUAD, t % QUAD] if len(blocks.shape) == 5 else blocks.at[t]

        self.copies = []
        for n, relation in enumerate(RELATIONS):
            copy = remote(
                block(place.rank(relation)),
                kept,
                send.at[n],
                recv.at[n],
                place.peer(relation),
            )
            copy.start()
            self.copies.append(copy)
        copy = pltpu.make_async_copy(block(mine), kept, own)
        copy.start()
        self.copies.append(copy)

    def finish(self):
        for copy in self.copies:
            copy.wait()


LANES = 512


def lanes_of(n, width=LANES):
    return pl.ds(pl.multiple_of(n * width, width), width)


def shares_of(seq, values, weight, part):
    rows = part.shape[1]

    @pl.loop(0, part.shape[2] // LANES)
    def _(n):
        product = dot(values[seq], weight[lanes_of(n)], 1, 1)
        part[2 * seq, :, lanes_of(n)] = product[:rows].astype(bf16)
        part[2 * seq + 1, :, lanes_of(n)] = product[rows:].astype(bf16)


def over_tokens(first, lanes, second, other):
    left, right = first[:, :, lanes], second[:, :, other]
    tokens = left.shape[0] * left.shape[1]
    return dot(left.reshape(tokens, left.shape[2]), right.reshape(tokens, right.shape[2]), 0, 0)


def row_shares(first, second, shares):
    grps, seqs, rows, _ = shares.shape
    width = 256
    pieces = width // rows

    @pl.loop(0, first.shape[2] // width)
    def _(b):
        product = over_tokens(first, lanes_of(b, width), second, slice(None)).astype(bf16)
        for p in range(pieces):
            index = b * pieces + p
            shares[index % grps, index // grps] = product[p * rows : (p + 1) * rows]


def summed_rows(landed, holds, blocks):
    seqs, rows = landed.shape[1], blocks.shape[1]
    for seq in range(seqs):
        for quad in range(QUAD):
            block = slice(quad * rows, (quad + 1) * rows)
            total = jnp.zeros((rows, landed.shape[3]), f32)
            for j in range(landed.shape[0]):
                total += jnp.where(holds(j), landed[j, seq, block].astype(f32), 0.0)
            blocks[seq * QUAD + quad] = total.astype(bf16)


def back_kernel(
    grps,
    aligned,
    facts,
    gains,
    cosine,
    sine,
    residual,
    own_tokens,
    own_grad,
    dgu_h,
    up_h,
    second_h,
    first_h,
    out_h,
    qkv_h,
    q_h,
    k_h,
    v_h,
    o_h,
    hidden_h,
    down_h,
    input_grad,
    block_output,
    gains_sum,
    out_landed,
    up_held,
    qkv_held,
    up_landed,
    qkv_landed,
    up_met,
    out_met,
    qkv_met,
    wide,
    up,
    acts,
    out_w,
    qkv,
    part,
    near,
    far,
    blocks,
    turned,
    up_share,
    out_share,
    qkv_share,
    up_sum,
    qkv_sum,
    stage_low,
    stage_wide,
    gain_part,
    gain_plane,
    gain_far,
    load,
    near_send,
    near_recv,
    far_send,
    far_recv,
    all_send,
    all_recv,
    z_send,
    z_recv,
    swap_send,
    swap_recv,
    gain_send,
    gain_recv,
    own_sem,
    near_free,
    far_free,
):
    place = Place(grps)
    rows = residual.shape[0]
    gain_part[...] = jnp.zeros_like(gain_part)
    count, full_rows, head_width = q_h.shape

    def fetch(src, dst, n):
        copy = pltpu.make_async_copy(src, dst, load.at[n])
        copy.start()
        return copy

    loads = [fetch(dgu_h, wide, 0), fetch(up_h, up, 1), fetch(second_h, acts, 3)]
    weights = [fetch(out_h, out_w, 5), fetch(qkv_h, qkv, 6)]
    place.greet()
    for copy in loads[:2]:
        copy.wait()

    sums = (near_send, near_recv, far_send, far_recv)
    def to_owners(n, shares, landed, met, stage, waits=False):
        return ToOwners(
            place, shares, landed, met, stage, z_send.at[n], z_recv.at[n], own_sem.at[n]
        ).start(waits)

    def summed_over_plane(values, weight):
        total = PlaneSum(place, part, near, far, sums)
        for k in range(4):
            shares_of(total.sequence(k), values, weight, part)
            if k % 2 == 0:
                total.near(k)
            else:
                total.far(k)
        return total

    second_sum = summed_over_plane(wide, up)
    loads[2].wait()
    row_shares(acts, wide, up_share)
    up_out = to_owners(1, up_share, up_landed, up_met, stage_wide, True)
    fetch_first = fetch(first_h, acts, 3)
    heads = [
        fetch(ref, wide.at[:, :, n * head_width : (n + 1) * head_width], 7 + n)
        for n, ref in enumerate((q_h, k_h, v_h, o_h))
    ]

    half = hidden_h.shape[2]
    hidden = turned.at[:, :, :half]
    last = [fetch(hidden_h, hidden, 11)]
    for n in range(2):
        columns = slice(n * D // 2, (n + 1) * D // 2)
        last.append(fetch(down_h.at[:, columns], up.at[n * half : (n + 1) * half, : D // 2], 12 + n))
    second_sum.finish()
    mine = place.seat()
    inner = jnp.zeros((rows, 1), f32)
    squares = jnp.zeros((rows, 1), f32)
    for n in range(D // LANES):
        lanes = slice(n * LANES, (n + 1) * LANES)
        grad = second_sum.chunk(lanes)
        values = residual[:, lanes]
        inner += jnp.sum(grad * gains[1:2, lanes] * values, axis=-1, keepdims=True)
        squares += jnp.sum(values * values, axis=-1, keepdims=True)
    scale = lax.rsqrt(squares / D + NORM_EPSILON)
    inner = inner / D
    for n in range(D // LANES):
        lanes = slice(n * LANES, (n + 1) * LANES)
        grad, values = second_sum.chunk(lanes), residual[:, lanes]
        gain_part[1:2, lanes] = jnp.sum(grad * values * scale, axis=0, keepdims=True)
        total = own_grad[:, lanes].astype(f32) + scale * (
            grad * gains[1:2, lanes] - values * scale * scale * inner
        )
        input_grad[:, lanes] = total
        blocks[mine, :, lanes] = total.astype(bf16)

    gather = PlaneGather(place, blocks, all_send, all_recv)
    gather.start()
    up_out.proceed()
    up_out.join()
    for copy in weights + heads:
        copy.wait()

    lane = lax.broadcasted_iota(jnp.int32, (full_rows, head_width), 1)
    first_half = (lane % HEAD_DIM) < HEAD_DIM // 2

    for copy in last:
        copy.wait()

    @pl.loop(0, count)
    def _(seq):
        for n in range(D // LANES):
            top, left = n * LANES // (D // 2) * half, n * LANES % (D // 2)
            product = dot(hidden[seq], up[top : top + half, left : left + LANES])
            part[2 * seq, :, n * LANES : (n + 1) * LANES] = product[:rows].astype(bf16)
            part[2 * seq + 1, :, n * LANES : (n + 1) * LANES] = product[rows:].astype(bf16)

    out_rows = out_share.shape[1]

    def out_shares():
        @pl.loop(0, D // LANES)
        def _(n):
            lanes = lanes_of(n)
            total = jnp.zeros((head_width, LANES), f32)
            for seq in range(count):
                values = wide[seq, :, 3 * head_width : 4 * head_width].astype(f32)
                total += dot(values[:rows].astype(bf16), blocks[2 * seq, :, lanes], 0, 0)
                total += dot(values[rows:].astype(bf16), blocks[2 * seq + 1, :, lanes], 0, 0)
            total = total.astype(bf16)
            for j in range(out_share.shape[0]):
                out_share[j, :, lanes] = total[j * out_rows : (j + 1) * out_rows]

    last_sum = PlaneSum(place, part, near, far, sums)
    for k in range(4):
        gather.arrive(k)
        seq = gather.sequence(k)
        if k == 3:
            out_shares()
            if aligned:
                out_out = to_owners(3, out_share, out_landed, out_met, stage_low)
            else:
                out_out = pltpu.make_async_copy(out_share, out_landed, own_sem.at[3])
                out_out.start()
        grads = jnp.concatenate(
            [dot(blocks[2 * seq], out_w[...], 1, 1), dot(blocks[2 * seq + 1], out_w[...], 1, 1)],
            axis=0,
        ).astype(bf16)
        queries = wide[seq, :, 0:head_width]
        key_vectors = wide[seq, :, head_width : 2 * head_width]
        value_vectors = wide[seq, :, 2 * head_width : 3 * head_width]
        grad_q, grad_k, grad_v = attention_grads(
            facts[seq, 2:3, 0:1], queries, key_vectors, value_vectors, grads
        )
        for n, grad in enumerate((grad_q, grad_k)):
            values = (grad * HEAD_DIM**-0.5).astype(bf16).astype(f32)
            back = values * cosine[...] - swap_halves(values, first_half) * sine[...]
            turned[seq, :, n * head_width : (n + 1) * head_width] = back.astype(bf16)
        turned[seq, :, 2 * head_width : 3 * head_width] = grad_v.astype(bf16)
        if k == 1:
            last_sum.near(0)
            last_sum.near(2)
        elif k == 2:
            last_sum.far(1)
            last_sum.far(3)

    gather.finish()
    fetch_first.wait()
    row_shares(acts, turned, qkv_share)
    triple = turned.shape[2]
    qkv_out = to_owners(2, qkv_share, qkv_landed, qkv_met, stage_wide.at[:, :, :triple], True)

    last_sum.finish()
    for n in range(D // LANES):
        lanes = slice(n * LANES, (n + 1) * LANES)
        block_output[:, lanes] = (residual[:, lanes] + last_sum.chunk(lanes)).astype(bf16)
    pl.semaphore_signal(near_free, inc=1, device_id=place.peer(SIBLING), device_id_type=MESH)
    for relation in ACROSS:
        pl.semaphore_signal(far_free, inc=1, device_id=place.peer(relation), device_id_type=MESH)
    pl.semaphore_wait(near_free, 1)
    pl.semaphore_wait(far_free, 3)
    first_sum = summed_over_plane(turned, qkv)
    if aligned:
        out_out.join()
    qkv_out.proceed()
    qkv_out.join()
    first_sum.finish()
    inner = jnp.zeros((rows, 1), f32)
    squares = jnp.zeros((rows, 1), f32)
    for n in range(D // LANES):
        lanes = slice(n * LANES, (n + 1) * LANES)
        grad = first_sum.chunk(lanes)
        values = own_tokens[:, lanes].astype(f32)
        inner += jnp.sum(grad * gains[0:1, lanes] * values, axis=-1, keepdims=True)
        squares += jnp.sum(values * values, axis=-1, keepdims=True)
    scale = lax.rsqrt(squares / D + NORM_EPSILON)
    inner = inner / D
    for n in range(D // LANES):
        lanes = slice(n * LANES, (n + 1) * LANES)
        grad, values = first_sum.chunk(lanes), own_tokens[:, lanes].astype(f32)
        gain_part[0:1, lanes] = jnp.sum(grad * values * scale, axis=0, keepdims=True)
        input_grad[:, lanes] += scale * (
            grad * gains[0:1, lanes] - values * scale * scale * inner
        )

    gain_copies = []
    for n, relation in enumerate(RELATIONS):
        copy = remote(
            gain_part, gain_plane.at[n], gain_send.at[n], gain_recv.at[n], place.peer(relation)
        )
        copy.start()
        gain_copies.append(copy)

    up_out.finish()
    landed = pltpu.make_async_copy(up_landed, up_share, load.at[1])
    landed.start()
    for copy in gain_copies:
        copy.wait()
    total = gain_part[...]
    for n in range(len(RELATIONS)):
        total += gain_plane[n]
    gain_far[0] = total
    gain_copies = []
    for dz in range(1, grps):
        copy = remote(
            gain_far.at[0],
            gain_far.at[dz],
            gain_send.at[7 + dz],
            gain_recv.at[7 + dz],
            place.plane(dz),
        )
        copy.start()
        gain_copies.append(copy)
    landed.wait()
    summed_rows(up_share, up_out.holds, up_sum)
    up_swap = Exchange(place, up_sum, up_held, swap_send.at[0], swap_recv.at[0], own_sem.at[4])
    for copy in gain_copies:
        copy.wait()
    total = gain_far[0]
    for dz in range(1, grps):
        total += gain_far[dz]
    gains_sum[...] = total

    qkv_out.finish()
    landed = pltpu.make_async_copy(qkv_landed, qkv_share, load.at[6])
    landed.start()
    landed.wait()
    summed_rows(qkv_share, qkv_out.holds, qkv_sum)
    qkv_swap = Exchange(place, qkv_sum, qkv_held, swap_send.at[1], swap_recv.at[1], own_sem.at[5])
    if aligned:
        out_out.finish()
    else:
        out_out.wait()
    up_swap.finish()
    qkv_swap.finish()


def backward(
    grps,
    aligned,
    facts,
    gains,
    tables,
    residual,
    own_tokens,
    own_grad,
    grad_both,
    up_local,
    second_norm,
    first_norm,
    out_local,
    qkv_local,
    heads,
    hidden,
    down_local,
):
    rows = residual.shape[0]
    count, full_rows, head_width = heads[0].shape
    seqs = full_rows // rows
    ranks = seqs * QUAD
    both = grad_both.shape[2]
    quad_rows = D // (seqs * grps)
    shard = quad_rows // QUAD
    out_rows = head_width // grps if aligned else HEAD_DIM
    triple = 3 * head_width
    out_count = head_width // out_rows
    hbm = pl.BlockSpec(memory_space=pl.ANY)
    vmem = pl.BlockSpec(memory_space=pltpu.VMEM)
    shape = jax.ShapeDtypeStruct
    dma = pltpu.SemaphoreType.DMA
    return pl.pallas_call(
        lambda *refs: back_kernel(grps, aligned, *refs),
        in_specs=[vmem] * 7 + [hbm] * 12,
        out_specs=[vmem] * 3 + [hbm] * 8,
        out_shape=[
            shape((rows, D), f32),
            shape((rows, D), bf16),
            shape((8, D), f32),
            shape((out_count, out_rows, D), bf16),
            shape((ranks, shard, both), bf16),
            shape((ranks, shard, triple), bf16),
            shape((grps, seqs, quad_rows, both), bf16),
            shape((grps, seqs, quad_rows, triple), bf16),
            shape((seqs, quad_rows, both), bf16),
            shape((out_rows, D), bf16),
            shape((seqs, quad_rows, triple), bf16),
        ],
        scratch_shapes=[
            pltpu.VMEM((count, full_rows, both), bf16),
            pltpu.VMEM((D, both), bf16),
            pltpu.VMEM((count, full_rows, D), bf16),
            pltpu.VMEM((head_width, D), bf16),
            pltpu.VMEM((D, triple), bf16),
            pltpu.VMEM((ranks, rows, D), bf16),
            pltpu.VMEM((4, rows, D), bf16),
            pltpu.VMEM((3, rows, D), bf16),
            pltpu.VMEM((ranks, rows, D), bf16),
            pltpu.VMEM((count, full_rows, triple), bf16),
            pltpu.VMEM((grps, seqs, quad_rows, both), bf16),
            pltpu.VMEM((out_count, out_rows, D), bf16),
            pltpu.VMEM((grps, seqs, quad_rows, triple), bf16),
            pltpu.VMEM((ranks, shard, both), bf16),
            pltpu.VMEM((ranks, shard, triple), bf16),
            pltpu.VMEM((out_rows, D), bf16),
            pltpu.VMEM((seqs, quad_rows, both), bf16),
            pltpu.VMEM((8, D), f32),
            pltpu.VMEM((7, 8, D), f32),
            pltpu.VMEM((grps, 8, D), f32),
            dma((14,)),
            dma((4,)),
            dma((4,)),
            dma((3,)),
            dma((3,)),
            dma((7,)),
            dma((7,)),
            dma((4, grps)),
            dma((4, grps)),
            dma((2, 7)),
            dma((2, 7)),
            dma((7 + grps,)),
            dma((7 + grps,)),
            dma((6,)),
            pltpu.SemaphoreType.REGULAR,
            pltpu.SemaphoreType.REGULAR,
        ],
        compiler_params=pltpu.CompilerParams(
            collective_id=0, has_side_effects=True, vmem_limit_bytes=VMEM_LIMIT
        ),
        cost_estimate=pl.CostEstimate(
            flops=30 * 10**9, bytes_accessed=60 * 2**20, transcendentals=2 * 10**6
        ),
        name="backward",
    )(
        facts,
        gains,
        *tables,
        residual,
        own_tokens,
        own_grad,
        grad_both,
        up_local,
        second_norm,
        first_norm,
        out_local,
        qkv_local,
        *heads,
        hidden,
        down_local,
    )


CHUNK = 1024


class FromOwners:
    def __init__(self, place, source, landed, landing, send, recv, own):
        self.place, self.source, self.send, self.recv = place, source, send, recv
        self.slot = lambda j: landing(landed, j)
        self.own = pltpu.make_async_copy(source, self.slot(place.g), own)
        self.line = place.grps == 4

    def copy(self, source, slot, sem, recv, target):
        place = self.place
        return remote(
            source, self.slot(slot), self.send.at[sem], self.recv.at[recv], (place.s, target, place.r, place.c)
        )

    def passed(self, g, j, target):
        source = self.source if j == g else self.slot(j)
        return self.copy(source, j, j + (4 if target > g else 0), j, target)

    def arrived(self, j):
        self.copy(self.source, j, j, j, j).wait_recv()

    def on_line(self, steps):
        for g in range(4):
            if steps[g]:

                @pl.when(self.place.g == g)
                def _():
                    for awaited, j, target in steps[g]:
                        if awaited is not None:
                            self.arrived(awaited)
                        if target is not None:
                            self.passed(g, j, target).start()

    FIRST = (
        ((None, 0, 1),),
        ((None, 1, 0), (None, 1, 2)),
        ((None, 2, 3), (None, 2, 1)),
        ((None, 3, 2),),
    )
    SECOND = (
        ((1, 1, None),),
        ((2, 2, 0), (0, 0, 2)),
        ((1, 1, 3), (3, 3, 1)),
        ((2, 2, None),),
    )
    THIRD = ((), ((3, 3, 0),), ((0, 0, 3),), ())

    def start(self):
        place = self.place
        self.own.start()
        if self.line:
            self.on_line(self.FIRST)
        else:
            self.copies = [
                self.copy(self.source, place.g, dz, dz, (place.g + dz) % place.grps)
                for dz in range(1, place.grps)
            ]
            for copy in self.copies:
                copy.start()

    def second(self):
        if self.line:
            self.on_line(self.SECOND)

    def third(self):
        if self.line:
            self.on_line(self.THIRD)

    def finish(self):
        self.own.wait()
        if self.line:
            for g in range(4):

                @pl.when(self.place.g == g)
                def _():
                    for j in {0: (2, 3), 3: (1, 0)}.get(g, ()):
                        self.arrived(j)
                    for steps in (self.FIRST, self.SECOND, self.THIRD):
                        for _, j, target in steps[g]:
                            if target is not None:
                                self.passed(g, j, target).wait_send()

        else:
            for copy in self.copies:
                copy.wait()


class Chain:
    def __init__(self, place, part, through, landed, lanes, send, recv, own):
        self.place, self.part, self.through, self.landed = place, part, through, landed
        self.send, self.recv = send, recv
        self.area = (slice(0, landed.shape[1]), lanes)
        self.own = pltpu.make_async_copy(self.block(part, place.g), self.block(landed, 2), own)

    def block(self, ref, j):
        return ref.at[(j, *self.area)]

    def copy(self, g, j):
        place, target = self.place, g + 1 if j > g else g - 1
        if target == j:
            landing = self.block(self.landed, 0 if j > g else 1)
        else:
            landing = self.block(self.through, j)
        recv = j if target != j else (j if j > g else 4)
        return remote(
            self.block(self.part, j), landing, self.send.at[j], self.recv.at[recv], (place.s, target, place.r, place.c)
        )

    def each(self, planes, action):
        for g in planes:

            @pl.when(self.place.g == g)
            def _():
                action(g)

    def blocks(self, g):
        return (3, 2, 1) if g == 0 else (0, 1, 2)

    def start(self):
        self.own.start()
        self.each((0, 3), lambda g: self.copy(g, self.blocks(g)[0]).start())

    def add(self, g, source, j):
        self.copy(source, j).wait_recv()
        area = (j, *self.area)
        self.part[area] = (self.part[area].astype(f32) + self.through[area].astype(f32)).astype(bf16)
        self.copy(g, j).start()

    def step(self, n):
        def ends(g):
            self.copy(g, self.blocks(g)[n - 1]).wait_send()
            self.copy(g, self.blocks(g)[n]).start()

        def inner(g):
            end = 0 if g == 1 else 3
            self.add(g, end, self.blocks(end)[n - 1])

        self.each((0, 3), ends)
        self.each((1, 2), inner)

    def last(self):
        self.each((1, 2), lambda g: self.add(g, 3 - g, 0 if g == 1 else 3))

    def finish(self):
        self.own.wait()

        def done(g):
            if g > 0:
                self.copy(g - 1, g).wait_recv()
            if g < 3:
                self.copy(g + 1, g).wait_recv()
            if g in (0, 3):
                self.copy(g, self.blocks(g)[2]).wait_send()
            else:
                for j in range(4):
                    if j != g:
                        self.copy(g, j).wait_send()

        self.each(range(4), done)


def shares_from(seq, values, weight, part):
    rows = part.shape[1]

    @pl.loop(0, part.shape[2] // LANES)
    def _(n):
        product = dot(values[seq], weight[:, lanes_of(n)])
        part[2 * seq, :, lanes_of(n)] = product[:rows].astype(bf16)
        part[2 * seq + 1, :, lanes_of(n)] = product[rows:].astype(bf16)


def times_slices(values, weight, lanes):
    piece = weight[:, :, :, :, lanes]
    return dot(values, piece.reshape(values.shape[1], piece.shape[4]))


def both_blocks(blocks, seq):
    return jnp.concatenate([blocks[2 * seq].astype(f32), blocks[2 * seq + 1].astype(f32)], axis=0)


def forward_kernel(
    grps,
    aligned,
    cosine,
    sine,
    own_facts,
    tokens_h,
    own_grad_h,
    qkv_own,
    up_own,
    out_own,
    down_own,
    residual,
    gains,
    facts,
    first_h,
    q_h,
    k_h,
    v_h,
    o_h,
    second_h,
    grads_landed,
    hidden_h,
    dgu_h,
    qkv_landed,
    up_landed,
    out_landed,
    down_landed,
    blocks,
    grad_blocks,
    norm,
    grad_seq,
    qkv_rank,
    up_rank,
    qkv,
    up,
    out_w,
    down,
    heads,
    part,
    near,
    far,
    both,
    hidden,
    dgu,
    all_facts,
    early,
    load,
    store,
    swap_send,
    swap_recv,
    near_send,
    near_recv,
    far_send,
    far_recv,
    all_send,
    all_recv,
    z_send,
    z_recv,
    fact_send,
    fact_recv,
    chain_send,
    chain_recv,
    own_sem,
):
    place = Place(grps)
    count, full_rows, _ = norm.shape
    rows = residual.shape[0]
    head_width = heads.shape[3]
    mine, rank = place.seat(), place.rank()

    def fetch(src, dst, n):
        copy = pltpu.make_async_copy(src, dst, load.at[n])
        copy.start()
        return copy

    def keep(src, dst, n):
        copy = pltpu.make_async_copy(src, dst, store.at[n])
        copy.start()
        return copy

    shard = qkv_own.shape[0]
    units = down.shape[0] // grps
    seqs = qkv_landed.shape[0]
    slots = iter(range(20))

    def fetch_chunks(src):
        pieces = []
        for top in range(0, src.shape[0], shard):
            for left in range(0, src.shape[1], CHUNK):
                slot = next(slots)
                space = both.at[slot // 5, (slot % 5) * shard : (slot % 5 + 1) * shard]
                copy = pltpu.make_async_copy(
                    src.at[top : top + shard, left : left + CHUNK], space, early.at[slot]
                )
                copy.start()
                pieces.append((copy, space))
        return pieces

    def dealt(pieces, weight, lanes, parts):
        count = CHUNK // (QUAD * lanes)
        width = count * lanes
        each = len(pieces) // (parts * seqs)
        for n, (copy, space) in enumerate(pieces):
            copy.wait()
            values = space[...]
            seq = n // each % seqs
            first = (n // (each * seqs) * each + n % each) * width
            for q in range(QUAD):
                taken = [
                    values[:, (k * QUAD + q) * lanes : (k * QUAD + q + 1) * lanes] for k in range(count)
                ]
                weight[0, seq, q, :, first : first + width] = jnp.concatenate(taken, axis=1).astype(bf16)

    facts[rank] = own_facts[...]
    if aligned:
        out_pieces = fetch_chunks(out_own)
    qkv_pieces = fetch_chunks(qkv_own)
    up_pieces = fetch_chunks(up_own)
    down_pieces = fetch_chunks(down_own)
    own_blocks = [fetch(tokens_h, blocks.at[mine], 0), fetch(own_grad_h, grad_blocks.at[mine], 1)]

    def plane_rows(ref, j):
        return ref.at[:, j]

    def own_rows(ref, j):
        size = ref.shape[0] // grps
        return ref.at[pl.ds(pl.multiple_of(j * size, size), size)]

    def rows_of(ref, j):
        top = j * units
        return ref.at[top // 128, pl.ds(pl.multiple_of(top % 128, units), units)]

    def from_owners(n, source, landed, landing):
        return FromOwners(place, source, landed, landing, z_send.at[n], z_recv.at[n], own_sem.at[n])

    def stacked(pieces, weight):
        across = weight.shape[1] // CHUNK
        for n, (copy, space) in enumerate(pieces):
            copy.wait()
            top, left = n // across * shard, n % across * CHUNK
            weight[top : top + shard, left : left + CHUNK] = space[...].astype(bf16)

    down_z = from_owners(3, down.at[:units], down_landed, own_rows)
    if aligned:
        stacked(out_pieces, out_w)
        out_z = from_owners(2, out_w.at[:shard], out_landed, own_rows)
    place.greet()
    if aligned:
        out_z.start()
    dealt(qkv_pieces, qkv, HEAD_DIM, 3)
    qkv_swap = Exchange(place, qkv, qkv_rank, swap_send.at[0], swap_recv.at[0], own_sem.at[4])
    fact_copies = []
    for n, relation in enumerate(RELATIONS):
        copy = remote(own_facts, facts.at[rank], fact_send.at[n], fact_recv.at[n], place.peer(relation))
        copy.start()
        fact_copies.append(copy)
    if aligned:
        out_z.second()
    dealt(up_pieces, up, units, 2)
    stacked(down_pieces, down)
    for copy in own_blocks:
        copy.wait()
    if aligned:
        out_z.third()
    qkv_swap.finish()
    qkv_z = from_owners(0, qkv_rank, qkv_landed, plane_rows)
    up_z = from_owners(1, up_rank, up_landed, plane_rows)
    qkv_z.start()
    token_gather = PlaneGather(place, blocks, all_send.at[0], all_recv.at[0])
    token_gather.start()
    for copy in fact_copies:
        copy.wait()
    all_facts[place.g] = facts[...]
    fact_copies = []
    for dz in range(1, grps):
        copy = remote(
            facts,
            all_facts.at[place.g],
            fact_send.at[7 + dz],
            fact_recv.at[7 + dz],
            place.plane(dz),
        )
        copy.start()
        fact_copies.append(copy)
    for copy in fact_copies:
        copy.wait()
    width = D // (seqs * grps * QUAD)
    for n in range(seqs * grps):
        pieces = [all_facts[n % grps, (n // grps) * QUAD + q, :, :width] for q in range(QUAD)]
        gains[:, n * QUAD * width : (n + 1) * QUAD * width] = jnp.concatenate(pieces, axis=1)
    token_gather.forward(0)
    token_gather.forward(1)
    up_swap = Exchange(place, up, up_rank, swap_send.at[1], swap_recv.at[1], own_sem.at[5])
    qkv_z.second()
    token_gather.forward(2)
    token_gather.arrive(3)
    token_gather.copies[3].wait_recv()
    token_gather.copies[4].wait_recv()
    token_gather.finish()

    @pl.loop(0, count)
    def _(seq):
        values = both_blocks(blocks, seq)
        scale = lax.rsqrt(jnp.mean(values * values, axis=-1, keepdims=True) + NORM_EPSILON)
        norm[seq] = (values * scale * gains[0:1, :]).astype(bf16)

    stores = [keep(norm, first_h, 0)]
    grad_gather = PlaneGather(place, grad_blocks, all_send.at[1], all_recv.at[1])
    grad_gather.start()
    qkv_z.third()
    up_swap.finish()
    qkv_z.finish()
    up_z.start()
    fetch(qkv_landed, qkv, 2).wait()

    lane = lax.broadcasted_iota(jnp.int32, (full_rows, head_width), 1)
    first_half = (lane % HEAD_DIM) < HEAD_DIM // 2

    if aligned:
        out_z.finish()
        fetch(out_landed, out_w, 3).wait()
    else:
        fetch(out_own, out_w, 3).wait()

    plane_sum = PlaneSum(place, part, near, far, (near_send, near_recv, far_send, far_recv))
    mixed = heads.at[3]
    for k in range(4):
        seq = plane_sum.sequence(k)
        for n in range(3):
            lanes = slice(n * head_width, (n + 1) * head_width)
            values = times_slices(norm[seq], qkv, lanes)
            if n < 2:
                values = values * cosine[...] + swap_halves(values, first_half) * sine[...]
            heads[n, seq] = values.astype(bf16)
        heads[3, seq] = attention(facts[seq, 2:3, 0:1], heads[0, seq], heads[1, seq], heads[2, seq])
        shares_from(seq, mixed, out_w, part)
        if k % 2 == 0:
            plane_sum.near(k)
        else:
            plane_sum.far(k)
        if k == 0:
            grad_gather.forward(0)
            grad_gather.forward(1)
    grad_gather.forward(2)
    grad_gather.arrive(3)
    grad_gather.copies[3].wait_recv()
    grad_gather.copies[4].wait_recv()
    grad_gather.finish()
    stores += [keep(heads.at[n], ref, 1 + n) for n, ref in enumerate((q_h, k_h, v_h, o_h))]
    up_z.second()

    @pl.loop(0, count)
    def _(seq):
        grad_seq[seq] = both_blocks(grad_blocks, seq).astype(bf16)

    fetch(tokens_h, grad_blocks.at[mine], 4).wait()
    plane_sum.finish()
    squares = jnp.zeros((rows, 1), f32)
    for n in range(D // LANES):
        lanes = slice(n * LANES, (n + 1) * LANES)
        values = grad_blocks[mine, :, lanes].astype(f32) + plane_sum.chunk(lanes)
        residual[:, lanes] = values
        squares += jnp.sum(values * values, axis=-1, keepdims=True)
    scale = lax.rsqrt(squares / D + NORM_EPSILON)
    for n in range(D // LANES):
        lanes = slice(n * LANES, (n + 1) * LANES)
        blocks[mine, :, lanes] = (residual[:, lanes] * scale * gains[1:2, lanes]).astype(bf16)
    norm_gather = PlaneGather(place, blocks, all_send.at[2], all_recv.at[2])
    norm_gather.start()
    up_z.third()
    stores[0].wait()
    half = hidden.shape[2]
    for k in range(4):
        norm_gather.arrive(k, forwarded=k == 1)
        seq = norm_gather.sequence(k)
        norm[seq] = both_blocks(blocks, seq).astype(bf16)
        if k == 0:
            norm_gather.forward(1)
            up_z.finish()
            down_z.start()
            fetch(up_landed, up, 5).wait()
        elif k == 2:
            down_z.second()
        gate = times_slices(norm[seq], up, slice(0, half))
        above = times_slices(norm[seq], up, slice(half, 2 * half))
        both[seq, :, :half] = gate
        both[seq, :, half:] = above
        hidden[seq] = (gate * jax.nn.sigmoid(gate) * above).astype(bf16)
    norm_gather.finish()
    stores[0] = keep(norm, second_h, 5)
    stores.append(keep(hidden, hidden_h, 7))
    tall = min(256, half)
    slab = part.shape[1] // 128 * 128

    def down_shares(side):
        lanes = slice(side * D // 2, (side + 1) * D // 2)

        @pl.loop(0, half // tall)
        def _(b):
            product = over_tokens(hidden, lanes_of(b, tall), grad_seq, lanes).astype(bf16)
            for p in range(tall // slab):
                part[b * (tall // slab) + p, :slab, lanes] = product[p * slab : (p + 1) * slab]

    down_shares(0)
    if grps == 4:
        chains = [
            Chain(
                place,
                part,
                near,
                grads_landed,
                slice(side * D // 2, (side + 1) * D // 2),
                chain_send.at[side],
                chain_recv.at[side],
                own_sem.at[6 + side],
            )
            for side in range(2)
        ]
        chains[0].start()
    down_z.third()
    down_shares(1)
    if grps == 4:
        chains[1].start()
        chains[0].step(1)
        chains[1].step(1)
        chains[0].step(2)
    else:
        spread = [pltpu.make_async_copy(rows_of(part, place.g), grads_landed.at[place.g], own_sem.at[6])]
        for dz in range(1, grps):
            spread.append(
                remote(
                    rows_of(part, (place.g + dz) % grps),
                    grads_landed.at[place.g],
                    chain_send.at[0, dz],
                    chain_recv.at[0, dz],
                    place.plane(dz),
                )
            )
        for copy in spread:
            copy.start()
    down_z.finish()
    down_copy = fetch(down_landed, down, 6)
    if grps == 4:
        chains[0].last()
        chains[1].step(2)
        chains[1].last()
    down_copy.wait()

    def feed_forward_grads(seq):
        grads = dot(grad_seq[seq], down[...], 1, 1)
        gate, above = both[seq, :, :half], both[seq, :, half:]
        sigmoid = jax.nn.sigmoid(gate)
        dgu[seq, :, :half] = (grads * above * sigmoid * (1.0 + gate * (1.0 - sigmoid))).astype(bf16)
        dgu[seq, :, half:] = (grads * (gate * sigmoid)).astype(bf16)

    pl.loop(0, count)(feed_forward_grads)
    stores.append(keep(dgu, dgu_h, 8))
    if grps == 4:
        for chain in chains:
            chain.finish()
    else:
        for copy in spread:
            copy.wait()
    for copy in stores:
        copy.wait()


def forward(grps, aligned, tables, own_facts, tokens, own_grad, qkv_own, up_own, out_own, down_own):
    rows = tokens.shape[0]
    shard = qkv_own.shape[0]
    seqs = D // (shard * grps * QUAD)
    ranks = seqs * QUAD
    triple, both = qkv_own.shape[1] // ranks, up_own.shape[1] // ranks
    count, full_rows, head_width = QUAD, rows * seqs, triple // 3
    half = both // 2
    hbm = pl.BlockSpec(memory_space=pl.ANY)
    vmem = pl.BlockSpec(memory_space=pltpu.VMEM)
    shape = jax.ShapeDtypeStruct
    dma = pltpu.SemaphoreType.DMA
    by_heads = shape((count, full_rows, head_width), bf16)
    return pl.pallas_call(
        lambda *refs: forward_kernel(grps, aligned, *refs),
        in_specs=[vmem] * 3 + [hbm] * 6,
        out_specs=[vmem] * 3 + [hbm] * 13,
        out_shape=[
            shape((rows, D), f32),
            shape((8, D), f32),
            shape((ranks, 8, 128), f32),
            shape((count, full_rows, D), bf16),
            by_heads,
            by_heads,
            by_heads,
            by_heads,
            shape((count, full_rows, D), bf16),
            shape((3 if grps == 4 else grps, half // grps, D), bf16),
            shape((count, full_rows, half), bf16),
            shape((count, full_rows, both), bf16),
            shape((seqs, grps, QUAD, shard, triple), bf16),
            shape((seqs, grps, QUAD, shard, both), bf16),
            shape((head_width, D), bf16),
            shape((half, D), bf16),
        ],
        scratch_shapes=[
            pltpu.VMEM((ranks, rows, D), bf16),
            pltpu.VMEM((ranks, rows, D), bf16),
            pltpu.VMEM((count, full_rows, D), bf16),
            pltpu.VMEM((count, full_rows, D), bf16),
            pltpu.VMEM((seqs, QUAD, shard, triple), bf16),
            pltpu.VMEM((seqs, QUAD, shard, both), bf16),
            pltpu.VMEM((seqs, grps, QUAD, shard, triple), bf16),
            pltpu.VMEM((seqs, grps, QUAD, shard, both), bf16),
            pltpu.VMEM((head_width, D), bf16),
            pltpu.VMEM((half, D), bf16),
            pltpu.VMEM((4, count, full_rows, head_width), bf16),
            pltpu.VMEM((ranks, rows, D), bf16),
            pltpu.VMEM((4, rows, D), bf16),
            pltpu.VMEM((3, rows, D), bf16),
            pltpu.VMEM((count, full_rows, both), f32),
            pltpu.VMEM((count, full_rows, half), bf16),
            pltpu.VMEM((count, full_rows, both), bf16),
            pltpu.VMEM((grps, ranks, 8, 128), f32),
            dma((20,)),
            dma((7,)),
            dma((9,)),
            dma((2, 7)),
            dma((2, 7)),
            dma((4,)),
            dma((4,)),
            dma((3,)),
            dma((3,)),
            dma((3, 7)),
            dma((3, 7)),
            dma((4, 2 * grps)),
            dma((4, grps)),
            dma((7 + grps,)),
            dma((7 + grps,)),
            dma((2, max(5, grps))),
            dma((2, max(5, grps))),
            dma((8,)),
        ],
        compiler_params=pltpu.CompilerParams(
            collective_id=1, has_side_effects=True, vmem_limit_bytes=VMEM_LIMIT
        ),
        cost_estimate=pl.CostEstimate(
            flops=20 * 10**9, bytes_accessed=60 * 2**20, transcendentals=4 * 10**6
        ),
        name="forward",
    )(*tables, own_facts, tokens, own_grad, qkv_own, up_own, out_own, down_own)


DEPTH = 4


def adam_kernel(grps, down_planes, out_planes, up_ranks, qkv_ranks, gains_sum, gains, gains_m, gains_v, *refs):
    states, outs = refs[:12], refs[12:28]
    gains_outs = refs[28:31]
    state, planes, ranks, fresh, copied, in_sem, out_sem = refs[31:]
    plane = lax.axis_index("grp")
    rows = state.shape[2]
    units = CHUNK // QUAD
    pieces = []
    for n, (name, rate) in enumerate(
        (("down", FF ** (-0.5)), ("out", (D // 128) ** (-0.5)), ("up", D ** (-0.5)), ("qkv", D ** (-0.5)))
    ):
        arrays = states[3 * n : 3 * n + 3]
        for top in range(0, arrays[0].shape[0], rows):
            for left in range(0, arrays[0].shape[1], CHUNK):
                pieces.append((name, rate, n, top, left))

    def grad_source(name, top, left, slot):
        if name in ("down", "out"):
            source = down_planes if name == "down" else out_planes
            return (
                source.at[:, top : top + rows, left : left + CHUNK],
                planes.at[slot, : source.shape[0]],
            )
        source, parts = (up_ranks, 2) if name == "up" else (qkv_ranks, 3)
        width = source.shape[2] // parts
        per_seq = width // units
        n = left // CHUNK
        seqs = source.shape[0] // QUAD
        seq = n // per_seq % seqs
        first = n // (per_seq * seqs) * width + n % per_seq * units
        return source.at[seq * QUAD : (seq + 1) * QUAD, :, first : first + units], ranks.at[slot]

    def reads(k):
        name, _, n, top, left = pieces[k]
        slot = k % DEPTH
        window = (slice(top, top + rows), slice(left, left + CHUNK))
        copies = [
            pltpu.make_async_copy(states[3 * n + i].at[window], state.at[slot, i], in_sem.at[slot, i])
            for i in range(3)
        ]
        source, space = grad_source(name, top, left, slot)
        return copies + [pltpu.make_async_copy(source, space, in_sem.at[slot, 3])]

    def writes(k):
        _, _, n, top, left = pieces[k]
        slot = k % DEPTH
        window = (slice(top, top + rows), slice(left, left + CHUNK))
        copies = [
            pltpu.make_async_copy(fresh.at[slot, i], outs[4 * n + i].at[window], out_sem.at[slot, i])
            for i in range(3)
        ]
        return copies + [
            pltpu.make_async_copy(copied.at[slot], outs[4 * n + 3].at[window], out_sem.at[slot, 3])
        ]

    def gradient(name, slot):
        if name in ("down", "out"):
            chained = name == "down"
            source = down_planes if chained else out_planes
            total = jnp.zeros((rows, CHUNK), f32)
            for j in range(source.shape[0]):
                held = planes[slot, j].astype(f32)
                if grps == 4 and chained and j < 2:
                    held = jnp.where(plane > 0 if j == 0 else plane < 3, held, 0.0)
                elif grps == 4 and not chained and j in (0, 3):
                    held = jnp.where(plane != 3 - j, held, 0.0)
                total += held
            return total
        lanes = down_planes.shape[1] if name == "up" else HEAD_DIM
        values = [ranks[slot, q].astype(f32) for q in range(QUAD)]
        return jnp.concatenate(
            [
                values[q][:, n * lanes : (n + 1) * lanes]
                for n in range(units // lanes)
                for q in range(QUAD)
            ],
            axis=1,
        )

    for k in range(DEPTH - 1):
        for copy in reads(k):
            copy.start()
    results = adam_update(gains[...], gains_m[...], gains_v[...], gains_sum[...], 0.3)
    for out, result in zip(gains_outs, results):
        out[...] = result
    for k, (name, rate, _, _, _) in enumerate(pieces):
        slot = k % DEPTH
        if k + DEPTH - 1 < len(pieces):
            for copy in reads(k + DEPTH - 1):
                copy.start()
        for copy in reads(k):
            copy.wait()
        if k >= DEPTH:
            for copy in writes(k - DEPTH):
                copy.wait()
        results = adam_update(state[slot, 0], state[slot, 1], state[slot, 2], gradient(name, slot), rate)
        for i in range(3):
            fresh[slot, i] = results[i]
        copied[slot] = results[0].astype(bf16)
        for copy in writes(k):
            copy.start()
    for k in range(len(pieces) - DEPTH, len(pieces)):
        for copy in writes(k):
            copy.wait()


def adam(grps, down_planes, out_planes, up_ranks, qkv_ranks, gains_sum, gains, states):
    rows = up_ranks.shape[1]
    hbm = pl.BlockSpec(memory_space=pl.ANY)
    vmem = pl.BlockSpec(memory_space=pltpu.VMEM)
    shapes = []
    for array in states[::3]:
        shapes += [jax.ShapeDtypeStruct(array.shape, f32)] * 3
        shapes.append(jax.ShapeDtypeStruct(array.shape, bf16))
    shapes += [jax.ShapeDtypeStruct(gains[0].shape, f32)] * 3
    size = sum(array.size for array in states) // 3
    outs = pl.pallas_call(
        lambda *refs: adam_kernel(grps, *refs),
        in_specs=[hbm] * 4 + [vmem] * 4 + [hbm] * 12,
        out_specs=[hbm] * 16 + [vmem] * 3,
        out_shape=shapes,
        scratch_shapes=[
            pltpu.VMEM((DEPTH, 3, rows, CHUNK), f32),
            pltpu.VMEM((DEPTH, grps, rows, CHUNK), bf16),
            pltpu.VMEM((DEPTH, QUAD, rows, CHUNK // QUAD), bf16),
            pltpu.VMEM((DEPTH, 3, rows, CHUNK), f32),
            pltpu.VMEM((DEPTH, rows, CHUNK), bf16),
            pltpu.SemaphoreType.DMA((DEPTH, 4)),
            pltpu.SemaphoreType.DMA((DEPTH, 4)),
        ],
        compiler_params=pltpu.CompilerParams(vmem_limit_bytes=VMEM_LIMIT),
        cost_estimate=pl.CostEstimate(flops=size * 16, bytes_accessed=size * 28, transcendentals=size),
        name="adam",
    )(down_planes, out_planes, up_ranks, qkv_ranks, gains_sum, *gains, *states)
    return outs[:4], outs[4:8], outs[8:12], outs[12:16], outs[16:]


def on_device(
    tokens,
    cotangent,
    lengths,
    qkv_weight,
    qkv_moment,
    qkv_square,
    out_weight,
    out_moment,
    out_square,
    up_weight,
    up_moment,
    up_square,
    down_weight,
    down_moment,
    down_square,
    norm_gains,
    gains_moment,
    gains_square,
):
    seqs = lax.axis_size("seq")
    grps = lax.axis_size("grp")
    ranks = seqs * QUAD
    own_rows = tokens.shape[1]
    full_rows = own_rows * seqs
    all_rows = full_rows * QUAD
    heads_local = HEADS // ranks
    head_width = heads_local * HEAD_DIM
    units = down_weight.shape[0]
    aligned = out_weight.shape[0] == HEAD_DIM
    tables = rotate_table(full_rows, heads_local)

    positions = lax.axis_index("seq") * own_rows + jnp.arange(own_rows, dtype=jnp.int32)
    own_grad = jnp.where((positions < lengths[0])[:, None], cotangent[0], 0)
    own_gains = norm_gains.shape[1]
    own_facts = jnp.zeros((8, 128), f32)
    own_facts = own_facts.at[:2, :own_gains].set(norm_gains.astype(bf16).astype(f32))
    own_facts = own_facts.at[2].set(lengths[0].astype(f32))

    out_own = out_weight
    if not aligned:
        out_all = lax.all_gather(out_weight.astype(bf16), EVERY, axis=0, tiled=True)
        out_all = out_all.reshape(seqs, heads_local, QUAD, HEAD_DIM, D)
        seat = lax.axis_index("row") * 2 + lax.axis_index("core")
        out_own = lax.dynamic_index_in_dim(
            lax.dynamic_index_in_dim(out_all, lax.axis_index("seq"), 0, False), seat, 1, False
        ).reshape(head_width, D)
    (
        residual,
        gains,
        facts,
        first_norm,
        queries,
        key_vectors,
        value_vectors,
        attended,
        second_norm,
        down_planes,
        hidden,
        grad_both,
        qkv_local,
        up_local,
        out_local,
        down_local,
    ) = forward(
        grps,
        aligned,
        tables,
        own_facts,
        tokens[0],
        own_grad,
        qkv_weight,
        up_weight,
        out_own,
        down_weight,
    )
    if not aligned:
        out_local = out_own
    (
        input_grad,
        block_output,
        gains_total,
        out_planes,
        up_ranks,
        qkv_ranks,
        *_,
    ) = backward(
        grps,
        aligned,
        facts,
        gains,
        tables,
        residual,
        tokens[0],
        own_grad,
        grad_both,
        up_local.reshape(D, -1),
        second_norm,
        first_norm,
        out_local,
        qkv_local.reshape(D, -1),
        (queries, key_vectors, value_vectors, attended),
        hidden,
        down_local,
    )
    if aligned:
        out_sum = out_planes
    else:
        placed_term = jnp.zeros((seqs, QUAD, heads_local, HEAD_DIM, D), bf16)
        placed_term = lax.dynamic_update_slice(
            placed_term,
            out_planes.reshape(1, 1, heads_local, HEAD_DIM, D),
            (lax.axis_index("seq"), seat, 0, 0, 0),
        )
        out_sum = lax.psum_scatter(
            placed_term.transpose(0, 2, 1, 3, 4).reshape(D, D),
            EVERY,
            scatter_dimension=0,
            tiled=True,
        )[None]
    device = ((lax.axis_index("seq") * grps + lax.axis_index("grp")) * 2 + lax.axis_index("row")) * 2
    gains_sum = lax.dynamic_slice(
        gains_total, (0, (device + lax.axis_index("core")) * own_gains), (2, own_gains)
    )
    down_new, out_new, up_new, qkv_new, gains_new = adam(
        grps,
        down_planes,
        out_sum,
        up_ranks,
        qkv_ranks,
        gains_sum,
        (norm_gains, gains_moment, gains_square),
        (
            down_weight,
            down_moment,
            down_square,
            out_weight,
            out_moment,
            out_square,
            up_weight,
            up_moment,
            up_square,
            qkv_weight,
            qkv_moment,
            qkv_square,
        ),
    )
    return (
        block_output[None],
        input_grad[None],
        *qkv_new,
        *out_new,
        *up_new,
        *down_new,
        *gains_new,
    )


def solution(mesh):
    seqs, rest = mesh.shape["seq"], mesh.shape["fsdp"]
    planes = Mesh(
        mesh.devices.reshape(seqs, rest // QUAD, 2, 2), ("seq", "grp", "row", "core")
    )
    rows = P(("grp", "row", "core"), "seq", None)
    shards = P(EVERY, None)
    gains = P(None, EVERY)
    return jax.shard_map(
        on_device,
        mesh=planes,
        in_specs=(rows, rows, P(("grp", "row", "core"))) + (shards,) * 12 + (gains,) * 3,
        out_specs=(rows, rows) + (shards,) * 16 + (gains,) * 3,
        check_vma=False,
    )
```

```python
import math

import jax
import jax.numpy as jnp
from jax import lax
from jax.experimental import pallas as pl
from jax.experimental.pallas import tpu as pltpu
from jax.sharding import Mesh, PartitionSpec as P

D = 2048
HEADS = 32
HEAD_DIM = 64
FF = 4096
WINDOW = 128
STEP = 5


NORM_EPSILON = 1e-05
MOMENT_DECAY = 0.5
WEIGHT_DECAY = 0.1
ADAM_EPSILON = 1e-08

SEATS = ("row", "core", "seq")
RANKS = ("seq", "row", "core")
EVERY = ("seq", "grp", "row", "core")
QUAD = 4
VMEM_LIMIT = 63 * 2**20

bf16 = jnp.bfloat16
f32 = jnp.float32


def rotate_table(length, copies):
    halves = HEAD_DIM // 2
    freqs = jnp.exp(-math.log(10000.0) * 2.0 * jnp.arange(halves).astype(f32) / HEAD_DIM)
    angles = jnp.arange(length, dtype=jnp.int32).astype(f32)[:, None] * freqs[None, :]
    cosine, sine = jnp.cos(angles), jnp.sin(angles)
    return (
        jnp.tile(jnp.concatenate([cosine, cosine], axis=1), (1, copies)),
        jnp.tile(jnp.concatenate([-sine, sine], axis=1), (1, copies)),
    )


def adam_update(weight, moment, square, gradient, step_rate):
    moment_new = MOMENT_DECAY * moment + (1.0 - MOMENT_DECAY) * gradient
    square_new = MOMENT_DECAY * square + (1.0 - MOMENT_DECAY) * gradient * gradient
    correction = 1.0 - MOMENT_DECAY**STEP
    unbias = 1.0 / correction
    update = (moment_new * unbias) / (jnp.sqrt(square_new * unbias) + ADAM_EPSILON)
    return (weight - step_rate * (update + WEIGHT_DECAY * weight), moment_new, square_new)


def dot(a, b, lhs=1, rhs=0):
    return lax.dot_general(a, b, (((lhs,), (rhs,)), ((), ())), preferred_element_type=f32)


def swap_halves(values, first):
    width = values.shape[1]
    half = HEAD_DIM // 2
    return jnp.where(
        first, pltpu.roll(values, width - half, 1), pltpu.roll(values, half, 1)
    )


def allowed_mask(rows, length):
    row = lax.broadcasted_iota(jnp.int32, (rows, rows), 0)
    col = lax.broadcasted_iota(jnp.int32, (rows, rows), 1)
    return (col <= row) & (row - col < WINDOW) & (col.astype(f32) < length)


def head_lanes(rows, width, head):
    lane = lax.broadcasted_iota(jnp.int32, (rows, width), 1)
    return (lane // HEAD_DIM) == head


def softmax_rows(queries, key_vectors, allowed):
    scores = jnp.where(allowed, dot(queries, key_vectors, 1, 1) * (HEAD_DIM**-0.5), -1e30)
    shifted = jnp.exp(scores - jnp.max(scores, axis=-1, keepdims=True))
    return shifted / jnp.sum(shifted, axis=-1, keepdims=True)


def attention(length, queries, key_vectors, value_vectors):
    rows, width = queries.shape
    allowed = allowed_mask(rows, length)
    total = jnp.zeros((rows, width), f32)
    for head in range(width // HEAD_DIM):
        mine = head_lanes(rows, width, head)
        weights = softmax_rows(jnp.where(mine, queries, 0), key_vectors, allowed)
        total += dot(weights.astype(bf16), jnp.where(mine, value_vectors, 0))
    return total.astype(bf16)


def attention_grads(length, queries, key_vectors, value_vectors, grads):
    rows, width = queries.shape
    allowed = allowed_mask(rows, length)
    grad_q = jnp.zeros((rows, width), f32)
    grad_k = jnp.zeros((rows, width), f32)
    grad_v = jnp.zeros((rows, width), f32)
    for head in range(width // HEAD_DIM):
        mine = head_lanes(rows, width, head)
        q_head = jnp.where(mine, queries, 0)
        g_head = jnp.where(mine, grads, 0)
        weights = softmax_rows(q_head, key_vectors, allowed)
        grad_p = dot(g_head, value_vectors, 1, 1)
        delta = jnp.sum(weights * grad_p, axis=-1, keepdims=True)
        grad_s = jnp.where(allowed, weights * (grad_p - delta), 0.0).astype(bf16)
        grad_q += dot(grad_s, jnp.where(mine, key_vectors, 0))
        grad_k += dot(grad_s, q_head, 0, 0)
        grad_v += dot(weights.astype(bf16), g_head, 0, 0)
    return grad_q, grad_k, grad_v


MESH = pl.DeviceIdType.MESH
RELATIONS = tuple((a, b, d) for a in range(2) for b in range(2) for d in range(2))[1:]


class Place:
    def __init__(self, grps):
        self.grps = grps
        self.s = lax.axis_index("seq")
        self.g = lax.axis_index("grp")
        self.r = lax.axis_index("row")
        self.c = lax.axis_index("core")

    def peer(self, relation):
        ds, dr, dc = relation
        return ((self.s + ds) % 2, self.g, (self.r + dr) % 2, (self.c + dc) % 2)

    def plane(self, dz):
        return (self.s, (self.g + dz) % self.grps, self.r, self.c)

    def rank(self, relation=(0, 0, 0)):
        s, _, r, c = self.peer(relation)
        return (s * 2 + r) * 2 + c

    def seat(self, relation=(0, 0, 0)):
        s, _, r, c = self.peer(relation)
        return (r * 2 + c) * 2 + s

    def corner(self, relation=(0, 0, 0)):
        s, _, r, _ = self.peer(relation)
        return r * 2 + s

    def greet(self):
        barrier = pltpu.get_barrier_semaphore()
        for relation in RELATIONS:
            pl.semaphore_signal(barrier, inc=1, device_id=self.peer(relation), device_id_type=MESH)
        for dz in range(1, self.grps):
            pl.semaphore_signal(barrier, inc=1, device_id=self.plane(dz), device_id_type=MESH)
        pl.semaphore_wait(barrier, len(RELATIONS) + self.grps - 1)


SIBLING = (0, 0, 1)
ACROSS = ((1, 0, 0), (0, 1, 0), (1, 1, 0))


def remote(src, dst, send_sem, recv_sem, device):
    return pltpu.make_async_remote_copy(
        src_ref=src,
        dst_ref=dst,
        send_sem=send_sem,
        recv_sem=recv_sem,
        device_id=device,
        device_id_type=MESH,
    )


class PlaneSum:
    def __init__(self, place, part, near, far, sems):
        self.place, self.part, self.nears, self.fars = place, part, near, far
        self.near_send, self.near_recv, self.far_send, self.far_recv = sems
        self.first, self.second = [None] * 4, []

    def sequence(self, k):
        place = self.place
        row = (place.r + 1) % 2 if k < 2 else place.r
        return row * 2 + ((place.c + 1) % 2 if k % 2 == 0 else place.c)

    def near(self, k):
        for s in range(2):
            copy = remote(
                self.part.at[2 * self.sequence(k) + s],
                self.nears.at[k + s],
                self.near_send.at[k + s],
                self.near_recv.at[k + s],
                self.place.peer(SIBLING),
            )
            copy.start()
            self.first[k + s] = copy

    def far(self, k):
        place = self.place
        for s in range(2):
            self.first[k - 1 + s].wait()
            self.nears[k - 1 + s] = (
                self.part[2 * self.sequence(k) + s].astype(f32)
                + self.nears[k - 1 + s].astype(f32)
            ).astype(bf16)
        for d in (1, 2) if k == 1 else (0,):
            relation = ACROSS[d]
            copy = remote(
                self.nears.at[k - 1 + (place.s + relation[0]) % 2],
                self.fars.at[d],
                self.far_send.at[d],
                self.far_recv.at[d],
                place.peer(relation),
            )
            copy.start()
            self.second.append(copy)

    def finish(self):
        for copy in self.second:
            copy.wait()

    def chunk(self, lanes):
        total = self.nears[2 + self.place.s, :, lanes].astype(f32)
        for d in range(3):
            total += self.fars[d, :, lanes].astype(f32)
        return total


class PlaneGather:
    def __init__(self, place, blocks, send, recv):
        self.place, self.blocks, self.sends, self.recvs = place, blocks, send, recv
        self.copies = [None] * 7

    def send(self, block, sem, relation):
        copy = remote(
            self.blocks.at[block],
            self.blocks.at[block],
            self.sends.at[sem],
            self.recvs.at[sem],
            self.place.peer(relation),
        )
        copy.start()
        self.copies[sem] = copy

    def start(self):
        mine = self.place.seat()
        for d in range(2):
            self.send(mine, d, ACROSS[d])
        self.send(mine, 3, SIBLING)

    def forward(self, d):
        self.copies[d].wait_recv()
        self.send(self.place.seat(ACROSS[d]), 4 + d, SIBLING)
        if d == 0:
            self.send(self.place.seat(), 2, ACROSS[2])

    def sequence(self, k):
        place = self.place
        row = place.r if k < 2 else (place.r + 1) % 2
        return row * 2 + (place.c if k % 2 == 0 else (place.c + 1) % 2)

    def arrive(self, k, forwarded=False):
        if k == 0:
            self.forward(0)
        elif k == 1:
            if not forwarded:
                self.forward(1)
            self.copies[3].wait_recv()
            self.copies[4].wait_recv()
        elif k == 2:
            self.forward(2)
        else:
            self.copies[5].wait_recv()
            self.copies[6].wait_recv()

    def finish(self):
        for copy in self.copies:
            copy.wait_send()


class ToOwners:
    def __init__(self, place, shares, landed, met, stage, send, recv, own):
        self.place, self.shares, self.landed, self.met, self.stage = place, shares, landed, met, stage
        self.send, self.recv, self.own_sem = send, recv, own
        self.line = place.grps == 4
        self.own = pltpu.make_async_copy(shares.at[place.g], landed.at[place.g], own)

    def copy(self, block, landing, sem, recv, target):
        place = self.place
        return remote(
            self.shares.at[block],
            landing,
            self.send.at[sem],
            self.recv.at[recv],
            (place.s, target, place.r, place.c),
        )

    def direct(self, g):
        targets = ((2, 1), (2, 0), (1, 3), (1, 2))[g]
        return [self.copy(t, self.landed.at[g], t, g, t) for t in targets]

    def meeting(self, g):
        far, inner = (3, 1) if g == 0 else (0, 2)
        return self.copy(far, self.met, far, inner, inner)

    def joined(self, g):
        far = 3 if g == 1 else 0
        return self.copy(far, self.landed.at[g], far, g, far)

    def start(self, waits=False):
        place, self.waits = self.place, waits
        self.own.start()
        if self.line:
            for g in range(4):

                @pl.when(place.g == g)
                def _():
                    if g in (0, 3):
                        self.meeting(g).start()
                    if g in (1, 2) or not waits:
                        for copy in self.direct(g):
                            copy.start()

        else:
            self.copies = [
                self.copy((place.g + dz) % place.grps, self.landed.at[place.g], dz, dz, (place.g + dz) % place.grps)
                for dz in range(1, place.grps)
            ]
            for copy in self.copies:
                copy.start()
        return self

    def proceed(self):
        if self.line:
            for g in (0, 3):

                @pl.when(self.place.g == g)
                def _():
                    self.meeting(g).wait_send()
                    for copy in self.direct(g):
                        copy.start()

    def join(self):
        if not self.line:
            return
        for g in (1, 2):

            @pl.when(self.place.g == g)
            def _():
                outer, far = (0, 3) if g == 1 else (3, 0)
                self.copy(far, self.met, far, g, outer).wait_recv()
                copy = pltpu.make_async_copy(self.met, self.stage, self.own_sem)
                self.own.wait()
                copy.start()
                copy.wait()
                if len(self.stage.shape) == 2:
                    self.shares[far] = (
                        self.shares[far].astype(f32) + self.stage[...].astype(f32)
                    ).astype(bf16)
                else:
                    for n in range(self.stage.shape[0]):
                        self.shares[far, n] = (
                            self.shares[far, n].astype(f32) + self.stage[n].astype(f32)
                        ).astype(bf16)
                self.joined(g).start()

        for g in (0, 3):

            @pl.when(self.place.g == g)
            def _():
                self.own.wait()

    def sent(self):
        if not self.line:
            for copy in self.copies:
                copy.wait_send()
            return
        for g in range(4):

            @pl.when(self.place.g == g)
            def _():
                for copy in self.direct(g):
                    copy.wait_send()
                if g in (1, 2):
                    self.joined(g).wait_send()
                elif not self.waits:
                    self.meeting(g).wait_send()

    def received(self):
        if not self.line:
            self.own.wait()
            for copy in self.copies:
                copy.wait_recv()
            return
        for g in range(4):

            @pl.when(self.place.g == g)
            def _():
                for j in ((1, 2), (0, 2, 3), (0, 1, 3), (1, 2))[g]:
                    self.copy(g, self.landed.at[j], j, j, j).wait_recv()

    def finish(self):
        self.sent()
        self.received()

    def holds(self, j):
        g = self.place.g
        return (g % 3 != 0) | (j + g != 3) if self.line else True


class Exchange:
    def __init__(self, place, blocks, held, send, recv, own):
        mine = place.rank()
        kept = held.at[mine // QUAD, mine % QUAD] if len(held.shape) == 4 else held.at[mine]

        def block(t):
            return blocks.at[0, t // QUAD, t % QUAD] if len(blocks.shape) == 5 else blocks.at[t]

        self.copies = []
        for n, relation in enumerate(RELATIONS):
            copy = remote(
                block(place.rank(relation)),
                kept,
                send.at[n],
                recv.at[n],
                place.peer(relation),
            )
            copy.start()
            self.copies.append(copy)
        copy = pltpu.make_async_copy(block(mine), kept, own)
        copy.start()
        self.copies.append(copy)

    def finish(self):
        for copy in self.copies:
            copy.wait()


LANES = 512


def lanes_of(n, width=LANES):
    return pl.ds(pl.multiple_of(n * width, width), width)


def shares_of(seq, values, weight, part):
    rows = part.shape[1]

    @pl.loop(0, part.shape[2] // LANES)
    def _(n):
        product = dot(values[seq], weight[lanes_of(n)], 1, 1)
        part[2 * seq, :, lanes_of(n)] = product[:rows].astype(bf16)
        part[2 * seq + 1, :, lanes_of(n)] = product[rows:].astype(bf16)


def over_tokens(first, lanes, second, other):
    left, right = first[:, :, lanes], second[:, :, other]
    tokens = left.shape[0] * left.shape[1]
    return dot(left.reshape(tokens, left.shape[2]), right.reshape(tokens, right.shape[2]), 0, 0)


def row_shares(first, second, shares):
    grps, seqs, rows, _ = shares.shape
    width = 256
    pieces = width // rows

    @pl.loop(0, first.shape[2] // width)
    def _(b):
        product = over_tokens(first, lanes_of(b, width), second, slice(None)).astype(bf16)
        for p in range(pieces):
            index = b * pieces + p
            shares[index % grps, index // grps] = product[p * rows : (p + 1) * rows]


def summed_rows(landed, holds, blocks):
    seqs, rows = landed.shape[1], blocks.shape[1]
    for seq in range(seqs):
        for quad in range(QUAD):
            block = slice(quad * rows, (quad + 1) * rows)
            total = jnp.zeros((rows, landed.shape[3]), f32)
            for j in range(landed.shape[0]):
                total += jnp.where(holds(j), landed[j, seq, block].astype(f32), 0.0)
            blocks[seq * QUAD + quad] = total.astype(bf16)


def back_kernel(
    grps,
    aligned,
    facts,
    gains,
    cosine,
    sine,
    residual_h,
    own_tokens_h,
    own_grad_h,
    dgu_h,
    up_h,
    second_h,
    first_h,
    out_h,
    qkv_h,
    q_h,
    k_h,
    v_h,
    o_h,
    hidden_h,
    down_h,
    input_grad,
    block_output,
    gains_sum,
    out_landed,
    up_held,
    qkv_held,
    up_landed,
    qkv_landed,
    up_met,
    out_met,
    qkv_met,
    wide,
    up,
    acts,
    out_w,
    qkv,
    part,
    near,
    far,
    blocks,
    turned,
    up_share,
    out_share,
    qkv_share,
    up_sum,
    qkv_sum,
    stage_low,
    stage_wide,
    gain_part,
    gain_plane,
    gain_far,
    residual,
    own_tokens,
    own_grad,
    load,
    near_send,
    near_recv,
    far_send,
    far_recv,
    all_send,
    all_recv,
    z_send,
    z_recv,
    swap_send,
    swap_recv,
    gain_send,
    gain_recv,
    own_sem,
    near_free,
    far_free,
):
    place = Place(grps)
    rows = residual.shape[0]
    gain_part[...] = jnp.zeros_like(gain_part)
    count, full_rows, head_width = q_h.shape

    def fetch(src, dst, n):
        copy = pltpu.make_async_copy(src, dst, load.at[n])
        copy.start()
        return copy

    loads = [fetch(dgu_h, wide, 0), fetch(up_h, up, 1), fetch(second_h, acts, 3)]
    weights = [fetch(out_h, out_w, 5), fetch(qkv_h, qkv, 6)]
    small = [
        fetch(src, dst, 14 + n)
        for n, (src, dst) in enumerate(
            ((residual_h, residual), (own_grad_h, own_grad), (own_tokens_h, own_tokens))
        )
    ]
    place.greet()
    for copy in loads[:2]:
        copy.wait()

    sums = (near_send, near_recv, far_send, far_recv)
    def to_owners(n, shares, landed, met, stage, waits=False):
        return ToOwners(
            place, shares, landed, met, stage, z_send.at[n], z_recv.at[n], own_sem.at[n]
        ).start(waits)

    def summed_over_plane(values, weight):
        total = PlaneSum(place, part, near, far, sums)
        for k in range(4):
            shares_of(total.sequence(k), values, weight, part)
            if k % 2 == 0:
                total.near(k)
            else:
                total.far(k)
        return total

    second_sum = summed_over_plane(wide, up)
    loads[2].wait()
    row_shares(acts, wide, up_share)
    up_out = to_owners(1, up_share, up_landed, up_met, stage_wide, True)
    fetch_first = fetch(first_h, acts, 3)
    heads = [
        fetch(ref, wide.at[:, :, n * head_width : (n + 1) * head_width], 7 + n)
        for n, ref in enumerate((q_h, k_h, v_h, o_h))
    ]

    half = hidden_h.shape[2]
    hidden = turned.at[:, :, :half]
    last = [fetch(hidden_h, hidden, 11)]
    for n in range(2):
        columns = slice(n * D // 2, (n + 1) * D // 2)
        last.append(fetch(down_h.at[:, columns], up.at[n * half : (n + 1) * half, : D // 2], 12 + n))
    for copy in small:
        copy.wait()
    second_sum.finish()
    mine = place.seat()
    inner = jnp.zeros((rows, 1), f32)
    squares = jnp.zeros((rows, 1), f32)
    for n in range(D // LANES):
        lanes = slice(n * LANES, (n + 1) * LANES)
        grad = second_sum.chunk(lanes)
        values = residual[:, lanes]
        inner += jnp.sum(grad * gains[1:2, lanes] * values, axis=-1, keepdims=True)
        squares += jnp.sum(values * values, axis=-1, keepdims=True)
    scale = lax.rsqrt(squares / D + NORM_EPSILON)
    inner = inner / D
    for n in range(D // LANES):
        lanes = slice(n * LANES, (n + 1) * LANES)
        grad, values = second_sum.chunk(lanes), residual[:, lanes]
        gain_part[1:2, lanes] = jnp.sum(grad * values * scale, axis=0, keepdims=True)
        total = own_grad[:, lanes].astype(f32) + scale * (
            grad * gains[1:2, lanes] - values * scale * scale * inner
        )
        input_grad[:, lanes] = total
        blocks[mine, :, lanes] = total.astype(bf16)

    gather = PlaneGather(place, blocks, all_send, all_recv)
    gather.start()
    up_out.proceed()
    up_out.join()
    for copy in weights + heads:
        copy.wait()

    lane = lax.broadcasted_iota(jnp.int32, (full_rows, head_width), 1)
    first_half = (lane % HEAD_DIM) < HEAD_DIM // 2

    for copy in last:
        copy.wait()

    @pl.loop(0, count)
    def _(seq):
        for n in range(D // LANES):
            top, left = n * LANES // (D // 2) * half, n * LANES % (D // 2)
            product = dot(hidden[seq], up[top : top + half, left : left + LANES])
            part[2 * seq, :, n * LANES : (n + 1) * LANES] = product[:rows].astype(bf16)
            part[2 * seq + 1, :, n * LANES : (n + 1) * LANES] = product[rows:].astype(bf16)

    out_rows = out_share.shape[1]

    def out_shares():
        @pl.loop(0, D // LANES)
        def _(n):
            lanes = lanes_of(n)
            total = jnp.zeros((head_width, LANES), f32)
            for seq in range(count):
                values = wide[seq, :, 3 * head_width : 4 * head_width].astype(f32)
                total += dot(values[:rows].astype(bf16), blocks[2 * seq, :, lanes], 0, 0)
                total += dot(values[rows:].astype(bf16), blocks[2 * seq + 1, :, lanes], 0, 0)
            total = total.astype(bf16)
            for j in range(out_share.shape[0]):
                out_share[j, :, lanes] = total[j * out_rows : (j + 1) * out_rows]

    last_sum = PlaneSum(place, part, near, far, sums)
    for k in range(4):
        gather.arrive(k)
        seq = gather.sequence(k)
        if k == 3:
            out_shares()
            if aligned:
                out_out = to_owners(3, out_share, out_landed, out_met, stage_low)
            else:
                out_out = pltpu.make_async_copy(out_share, out_landed, own_sem.at[3])
                out_out.start()
        grads = jnp.concatenate(
            [dot(blocks[2 * seq], out_w[...], 1, 1), dot(blocks[2 * seq + 1], out_w[...], 1, 1)],
            axis=0,
        ).astype(bf16)
        queries = wide[seq, :, 0:head_width]
        key_vectors = wide[seq, :, head_width : 2 * head_width]
        value_vectors = wide[seq, :, 2 * head_width : 3 * head_width]
        grad_q, grad_k, grad_v = attention_grads(
            facts[seq, 2:3, 0:1], queries, key_vectors, value_vectors, grads
        )
        for n, grad in enumerate((grad_q, grad_k)):
            values = (grad * HEAD_DIM**-0.5).astype(bf16).astype(f32)
            back = values * cosine[...] - swap_halves(values, first_half) * sine[...]
            turned[seq, :, n * head_width : (n + 1) * head_width] = back.astype(bf16)
        turned[seq, :, 2 * head_width : 3 * head_width] = grad_v.astype(bf16)
        if k == 1:
            last_sum.near(0)
            last_sum.near(2)
        elif k == 2:
            last_sum.far(1)
            last_sum.far(3)

    gather.finish()
    fetch_first.wait()
    row_shares(acts, turned, qkv_share)
    triple = turned.shape[2]
    qkv_out = to_owners(2, qkv_share, qkv_landed, qkv_met, stage_wide.at[:, :, :triple], True)

    last_sum.finish()
    for n in range(D // LANES):
        lanes = slice(n * LANES, (n + 1) * LANES)
        block_output[:, lanes] = (residual[:, lanes] + last_sum.chunk(lanes)).astype(bf16)
    pl.semaphore_signal(near_free, inc=1, device_id=place.peer(SIBLING), device_id_type=MESH)
    for relation in ACROSS:
        pl.semaphore_signal(far_free, inc=1, device_id=place.peer(relation), device_id_type=MESH)
    pl.semaphore_wait(near_free, 1)
    pl.semaphore_wait(far_free, 3)
    first_sum = summed_over_plane(turned, qkv)
    if aligned:
        out_out.join()
    qkv_out.proceed()
    qkv_out.join()
    first_sum.finish()
    inner = jnp.zeros((rows, 1), f32)
    squares = jnp.zeros((rows, 1), f32)
    for n in range(D // LANES):
        lanes = slice(n * LANES, (n + 1) * LANES)
        grad = first_sum.chunk(lanes)
        values = own_tokens[:, lanes].astype(f32)
        inner += jnp.sum(grad * gains[0:1, lanes] * values, axis=-1, keepdims=True)
        squares += jnp.sum(values * values, axis=-1, keepdims=True)
    scale = lax.rsqrt(squares / D + NORM_EPSILON)
    inner = inner / D
    for n in range(D // LANES):
        lanes = slice(n * LANES, (n + 1) * LANES)
        grad, values = first_sum.chunk(lanes), own_tokens[:, lanes].astype(f32)
        gain_part[0:1, lanes] = jnp.sum(grad * values * scale, axis=0, keepdims=True)
        input_grad[:, lanes] += scale * (
            grad * gains[0:1, lanes] - values * scale * scale * inner
        )

    gain_copies = []
    for n, relation in enumerate(RELATIONS):
        copy = remote(
            gain_part, gain_plane.at[n], gain_send.at[n], gain_recv.at[n], place.peer(relation)
        )
        copy.start()
        gain_copies.append(copy)

    up_out.finish()
    landed = pltpu.make_async_copy(up_landed, up_share, load.at[1])
    landed.start()
    for copy in gain_copies:
        copy.wait()
    total = gain_part[...]
    for n in range(len(RELATIONS)):
        total += gain_plane[n]
    gain_far[0] = total
    gain_copies = []
    for dz in range(1, grps):
        copy = remote(
            gain_far.at[0],
            gain_far.at[dz],
            gain_send.at[7 + dz],
            gain_recv.at[7 + dz],
            place.plane(dz),
        )
        copy.start()
        gain_copies.append(copy)
    landed.wait()
    summed_rows(up_share, up_out.holds, up_sum)
    up_swap = Exchange(place, up_sum, up_held, swap_send.at[0], swap_recv.at[0], own_sem.at[4])
    for copy in gain_copies:
        copy.wait()
    total = gain_far[0]
    for dz in range(1, grps):
        total += gain_far[dz]
    gains_sum[...] = total

    qkv_out.finish()
    landed = pltpu.make_async_copy(qkv_landed, qkv_share, load.at[6])
    landed.start()
    landed.wait()
    summed_rows(qkv_share, qkv_out.holds, qkv_sum)
    qkv_swap = Exchange(place, qkv_sum, qkv_held, swap_send.at[1], swap_recv.at[1], own_sem.at[5])
    if aligned:
        out_out.finish()
    else:
        out_out.wait()
    up_swap.finish()
    qkv_swap.finish()


def backward(
    grps,
    aligned,
    facts,
    gains,
    tables,
    residual,
    own_tokens,
    own_grad,
    grad_both,
    up_local,
    second_norm,
    first_norm,
    out_local,
    qkv_local,
    heads,
    hidden,
    down_local,
):
    rows = residual.shape[0]
    count, full_rows, head_width = heads[0].shape
    seqs = full_rows // rows
    ranks = seqs * QUAD
    both = grad_both.shape[2]
    quad_rows = D // (seqs * grps)
    shard = quad_rows // QUAD
    out_rows = head_width // grps if aligned else HEAD_DIM
    triple = 3 * head_width
    out_count = head_width // out_rows
    hbm = pl.BlockSpec(memory_space=pl.ANY)
    vmem = pl.BlockSpec(memory_space=pltpu.VMEM)
    shape = jax.ShapeDtypeStruct
    dma = pltpu.SemaphoreType.DMA
    return pl.pallas_call(
        lambda *refs: back_kernel(grps, aligned, *refs),
        in_specs=[vmem] * 4 + [hbm] * 15,
        out_specs=[vmem] * 3 + [hbm] * 8,
        out_shape=[
            shape((rows, D), f32),
            shape((rows, D), bf16),
            shape((8, D), f32),
            shape((out_count, out_rows, D), bf16),
            shape((ranks, shard, both), bf16),
            shape((ranks, shard, triple), bf16),
            shape((grps, seqs, quad_rows, both), bf16),
            shape((grps, seqs, quad_rows, triple), bf16),
            shape((seqs, quad_rows, both), bf16),
            shape((out_rows, D), bf16),
            shape((seqs, quad_rows, triple), bf16),
        ],
        scratch_shapes=[
            pltpu.VMEM((count, full_rows, both), bf16),
            pltpu.VMEM((D, both), bf16),
            pltpu.VMEM((count, full_rows, D), bf16),
            pltpu.VMEM((head_width, D), bf16),
            pltpu.VMEM((D, triple), bf16),
            pltpu.VMEM((ranks, rows, D), bf16),
            pltpu.VMEM((4, rows, D), bf16),
            pltpu.VMEM((3, rows, D), bf16),
            pltpu.VMEM((ranks, rows, D), bf16),
            pltpu.VMEM((count, full_rows, triple), bf16),
            pltpu.VMEM((grps, seqs, quad_rows, both), bf16),
            pltpu.VMEM((out_count, out_rows, D), bf16),
            pltpu.VMEM((grps, seqs, quad_rows, triple), bf16),
            pltpu.VMEM((ranks, shard, both), bf16),
            pltpu.VMEM((ranks, shard, triple), bf16),
            pltpu.VMEM((out_rows, D), bf16),
            pltpu.VMEM((seqs, quad_rows, both), bf16),
            pltpu.VMEM((8, D), f32),
            pltpu.VMEM((7, 8, D), f32),
            pltpu.VMEM((grps, 8, D), f32),
            pltpu.VMEM((rows, D), f32),
            pltpu.VMEM((rows, D), bf16),
            pltpu.VMEM((rows, D), bf16),
            dma((17,)),
            dma((4,)),
            dma((4,)),
            dma((3,)),
            dma((3,)),
            dma((7,)),
            dma((7,)),
            dma((4, grps)),
            dma((4, grps)),
            dma((2, 7)),
            dma((2, 7)),
            dma((7 + grps,)),
            dma((7 + grps,)),
            dma((6,)),
            pltpu.SemaphoreType.REGULAR,
            pltpu.SemaphoreType.REGULAR,
        ],
        compiler_params=pltpu.CompilerParams(
            collective_id=0, has_side_effects=True, vmem_limit_bytes=VMEM_LIMIT
        ),
        cost_estimate=pl.CostEstimate(
            flops=30 * 10**9, bytes_accessed=60 * 2**20, transcendentals=2 * 10**6
        ),
        name="backward",
    )(
        facts,
        gains,
        *tables,
        residual,
        own_tokens,
        own_grad,
        grad_both,
        up_local,
        second_norm,
        first_norm,
        out_local,
        qkv_local,
        *heads,
        hidden,
        down_local,
    )


CHUNK = 1024


class FromOwners:
    def __init__(self, place, source, landed, landing, send, recv, own):
        self.place, self.source, self.send, self.recv = place, source, send, recv
        self.slot = lambda j: landing(landed, j)
        self.own = pltpu.make_async_copy(source, self.slot(place.g), own)
        self.line = place.grps == 4

    def copy(self, source, slot, sem, recv, target):
        place = self.place
        return remote(
            source, self.slot(slot), self.send.at[sem], self.recv.at[recv], (place.s, target, place.r, place.c)
        )

    def passed(self, g, j, target):
        source = self.source if j == g else self.slot(j)
        return self.copy(source, j, j + (4 if target > g else 0), j, target)

    def arrived(self, j):
        self.copy(self.source, j, j, j, j).wait_recv()

    def on_line(self, steps):
        for g in range(4):
            if steps[g]:

                @pl.when(self.place.g == g)
                def _():
                    for awaited, j, target in steps[g]:
                        if awaited is not None:
                            self.arrived(awaited)
                        if target is not None:
                            self.passed(g, j, target).start()

    INWARD = (((None, 0, 1),), ((None, 1, 2),), ((None, 2, 1),), ((None, 3, 2),))
    OUTWARD = ((), ((None, 1, 0),), ((None, 2, 3),), ())
    SECOND = (
        ((1, 1, None),),
        ((2, 2, 0), (0, 0, 2)),
        ((1, 1, 3), (3, 3, 1)),
        ((2, 2, None),),
    )
    THIRD = ((), ((3, 3, 0),), ((0, 0, 3),), ())

    def inward(self):
        self.own.start()
        if self.line:
            self.on_line(self.INWARD)

    def outward(self):
        place = self.place
        if self.line:
            self.on_line(self.OUTWARD)
        else:
            self.copies = [
                self.copy(self.source, place.g, dz, dz, (place.g + dz) % place.grps)
                for dz in range(1, place.grps)
            ]
            for copy in self.copies:
                copy.start()

    def start(self):
        self.inward()
        self.outward()

    def second(self):
        if self.line:
            self.on_line(self.SECOND)

    def third(self):
        if self.line:
            self.on_line(self.THIRD)

    def finish(self):
        self.own.wait()
        if self.line:
            for g in range(4):

                @pl.when(self.place.g == g)
                def _():
                    for j in {0: (2, 3), 3: (1, 0)}.get(g, ()):
                        self.arrived(j)
                    for steps in (self.INWARD, self.OUTWARD, self.SECOND, self.THIRD):
                        for _, j, target in steps[g]:
                            if target is not None:
                                self.passed(g, j, target).wait_send()

        else:
            for copy in self.copies:
                copy.wait()


class Chain:
    def __init__(self, place, part, through, landed, lanes, send, recv, own):
        self.place, self.part, self.through, self.landed = place, part, through, landed
        self.send, self.recv = send, recv
        self.area = (slice(0, landed.shape[1]), lanes)
        self.own = pltpu.make_async_copy(self.block(part, place.g), self.block(landed, 2), own)

    def block(self, ref, j):
        return ref.at[(j, *self.area)]

    def copy(self, g, j):
        place, target = self.place, g + 1 if j > g else g - 1
        if target == j:
            landing = self.block(self.landed, 0 if j > g else 1)
        else:
            landing = self.block(self.through, j)
        recv = j if target != j else (j if j > g else 4)
        return remote(
            self.block(self.part, j), landing, self.send.at[j], self.recv.at[recv], (place.s, target, place.r, place.c)
        )

    def each(self, planes, action):
        for g in planes:

            @pl.when(self.place.g == g)
            def _():
                action(g)

    def blocks(self, g):
        return (3, 2, 1) if g == 0 else (0, 1, 2)

    def start(self):
        self.own.start()
        self.each((0, 3), lambda g: self.copy(g, self.blocks(g)[0]).start())

    def add(self, g, source, j):
        self.copy(source, j).wait_recv()
        area = (j, *self.area)
        self.part[area] = (self.part[area].astype(f32) + self.through[area].astype(f32)).astype(bf16)
        self.copy(g, j).start()

    def step(self, n):
        def ends(g):
            self.copy(g, self.blocks(g)[n - 1]).wait_send()
            self.copy(g, self.blocks(g)[n]).start()

        def inner(g):
            end = 0 if g == 1 else 3
            self.add(g, end, self.blocks(end)[n - 1])

        self.each((0, 3), ends)
        self.each((1, 2), inner)

    def last(self):
        self.each((1, 2), lambda g: self.add(g, 3 - g, 0 if g == 1 else 3))

    def finish(self):
        self.own.wait()

        def done(g):
            if g > 0:
                self.copy(g - 1, g).wait_recv()
            if g < 3:
                self.copy(g + 1, g).wait_recv()
            if g in (0, 3):
                self.copy(g, self.blocks(g)[2]).wait_send()
            else:
                for j in range(4):
                    if j != g:
                        self.copy(g, j).wait_send()

        self.each(range(4), done)


def shares_from(seq, values, weight, part):
    rows = part.shape[1]

    @pl.loop(0, part.shape[2] // LANES)
    def _(n):
        product = dot(values[seq], weight[:, lanes_of(n)])
        part[2 * seq, :, lanes_of(n)] = product[:rows].astype(bf16)
        part[2 * seq + 1, :, lanes_of(n)] = product[rows:].astype(bf16)


def times_slices(values, weight, lanes):
    piece = weight[:, :, :, :, lanes]
    return dot(values, piece.reshape(values.shape[1], piece.shape[4]))


def both_blocks(blocks, seq):
    return jnp.concatenate([blocks[2 * seq].astype(f32), blocks[2 * seq + 1].astype(f32)], axis=0)


def forward_kernel(
    grps,
    aligned,
    cosine,
    sine,
    own_facts,
    tokens_h,
    own_grad_h,
    qkv_own,
    up_own,
    out_own,
    down_own,
    residual,
    gains,
    facts,
    first_h,
    q_h,
    k_h,
    v_h,
    o_h,
    second_h,
    grads_landed,
    hidden_h,
    dgu_h,
    qkv_landed,
    up_landed,
    out_landed,
    down_landed,
    blocks,
    grad_blocks,
    norm,
    grad_seq,
    qkv_rank,
    up_rank,
    qkv,
    up,
    out_w,
    down,
    heads,
    part,
    near,
    far,
    both,
    hidden,
    dgu,
    all_facts,
    early,
    load,
    store,
    swap_send,
    swap_recv,
    near_send,
    near_recv,
    far_send,
    far_recv,
    all_send,
    all_recv,
    z_send,
    z_recv,
    fact_send,
    fact_recv,
    chain_send,
    chain_recv,
    own_sem,
):
    place = Place(grps)
    count, full_rows, _ = norm.shape
    rows = residual.shape[0]
    head_width = heads.shape[3]
    mine, rank = place.seat(), place.rank()

    def fetch(src, dst, n):
        copy = pltpu.make_async_copy(src, dst, load.at[n])
        copy.start()
        return copy

    def keep(src, dst, n):
        copy = pltpu.make_async_copy(src, dst, store.at[n])
        copy.start()
        return copy

    shard = qkv_own.shape[0]
    units = down.shape[0] // grps
    seqs = qkv_landed.shape[0]
    slots = iter(range(20))

    def fetch_chunks(src):
        pieces = []
        for top in range(0, src.shape[0], shard):
            for left in range(0, src.shape[1], CHUNK):
                slot = next(slots)
                space = both.at[slot // 5, (slot % 5) * shard : (slot % 5 + 1) * shard]
                copy = pltpu.make_async_copy(
                    src.at[top : top + shard, left : left + CHUNK], space, early.at[slot]
                )
                copy.start()
                pieces.append((copy, space))
        return pieces

    def dealt(pieces, weight, lanes, parts):
        count = CHUNK // (QUAD * lanes)
        width = count * lanes
        each = len(pieces) // (parts * seqs)
        for n, (copy, space) in enumerate(pieces):
            copy.wait()
            values = space[...]
            seq = n // each % seqs
            first = (n // (each * seqs) * each + n % each) * width
            for q in range(QUAD):
                taken = [
                    values[:, (k * QUAD + q) * lanes : (k * QUAD + q + 1) * lanes] for k in range(count)
                ]
                weight[0, seq, q, :, first : first + width] = jnp.concatenate(taken, axis=1).astype(bf16)

    facts[rank] = own_facts[...]
    if aligned:
        out_pieces = fetch_chunks(out_own)
    qkv_pieces = fetch_chunks(qkv_own)
    up_pieces = fetch_chunks(up_own)
    down_pieces = fetch_chunks(down_own)
    own_blocks = [fetch(tokens_h, blocks.at[mine], 0), fetch(own_grad_h, grad_blocks.at[mine], 1)]

    def plane_rows(ref, j):
        return ref.at[:, j]

    def own_rows(ref, j):
        size = ref.shape[0] // grps
        return ref.at[pl.ds(pl.multiple_of(j * size, size), size)]

    def rows_of(ref, j):
        top = j * units
        return ref.at[top // 128, pl.ds(pl.multiple_of(top % 128, units), units)]

    def from_owners(n, source, landed, landing):
        return FromOwners(place, source, landed, landing, z_send.at[n], z_recv.at[n], own_sem.at[n])

    def stacked(pieces, weight):
        across = weight.shape[1] // CHUNK
        for n, (copy, space) in enumerate(pieces):
            copy.wait()
            top, left = n // across * shard, n % across * CHUNK
            weight[top : top + shard, left : left + CHUNK] = space[...].astype(bf16)

    down_z = from_owners(3, down.at[:units], down_landed, own_rows)
    if aligned:
        stacked(out_pieces, out_w)
        out_z = from_owners(2, out_w.at[:shard], out_landed, own_rows)
    place.greet()
    if aligned:
        out_z.start()
    dealt(qkv_pieces, qkv, HEAD_DIM, 3)
    qkv_swap = Exchange(place, qkv, qkv_rank, swap_send.at[0], swap_recv.at[0], own_sem.at[4])
    fact_copies = []
    for n, relation in enumerate(RELATIONS):
        copy = remote(own_facts, facts.at[rank], fact_send.at[n], fact_recv.at[n], place.peer(relation))
        copy.start()
        fact_copies.append(copy)
    if aligned:
        out_z.second()
    dealt(up_pieces, up, units, 2)
    stacked(down_pieces, down)
    for copy in own_blocks:
        copy.wait()
    if aligned:
        out_z.third()
    qkv_swap.finish()
    qkv_z = from_owners(0, qkv_rank, qkv_landed, plane_rows)
    up_z = from_owners(1, up_rank, up_landed, plane_rows)
    qkv_z.start()
    token_gather = PlaneGather(place, blocks, all_send.at[0], all_recv.at[0])
    token_gather.start()
    for copy in fact_copies:
        copy.wait()
    all_facts[place.g] = facts[...]
    fact_copies = []
    for dz in range(1, grps):
        copy = remote(
            facts,
            all_facts.at[place.g],
            fact_send.at[7 + dz],
            fact_recv.at[7 + dz],
            place.plane(dz),
        )
        copy.start()
        fact_copies.append(copy)
    for copy in fact_copies:
        copy.wait()
    width = D // (seqs * grps * QUAD)
    for n in range(seqs * grps):
        pieces = [all_facts[n % grps, (n // grps) * QUAD + q, :, :width] for q in range(QUAD)]
        gains[:, n * QUAD * width : (n + 1) * QUAD * width] = jnp.concatenate(pieces, axis=1)
    token_gather.forward(0)
    token_gather.forward(1)
    up_swap = Exchange(place, up, up_rank, swap_send.at[1], swap_recv.at[1], own_sem.at[5])
    qkv_z.second()
    token_gather.forward(2)
    token_gather.arrive(3)
    token_gather.copies[3].wait_recv()
    token_gather.copies[4].wait_recv()
    token_gather.finish()

    @pl.loop(0, count)
    def _(seq):
        values = both_blocks(blocks, seq)
        scale = lax.rsqrt(jnp.mean(values * values, axis=-1, keepdims=True) + NORM_EPSILON)
        norm[seq] = (values * scale * gains[0:1, :]).astype(bf16)

    stores = [keep(norm, first_h, 0)]
    grad_gather = PlaneGather(place, grad_blocks, all_send.at[1], all_recv.at[1])
    grad_gather.start()
    qkv_z.third()
    up_swap.finish()
    up_z.inward()
    qkv_z.finish()
    up_z.outward()
    fetch(qkv_landed, qkv, 2).wait()

    lane = lax.broadcasted_iota(jnp.int32, (full_rows, head_width), 1)
    first_half = (lane % HEAD_DIM) < HEAD_DIM // 2

    if aligned:
        out_z.finish()
        fetch(out_landed, out_w, 3).wait()
    else:
        fetch(out_own, out_w, 3).wait()

    plane_sum = PlaneSum(place, part, near, far, (near_send, near_recv, far_send, far_recv))
    mixed = heads.at[3]
    for k in range(4):
        seq = plane_sum.sequence(k)
        for n in range(3):
            lanes = slice(n * head_width, (n + 1) * head_width)
            values = times_slices(norm[seq], qkv, lanes)
            if n < 2:
                values = values * cosine[...] + swap_halves(values, first_half) * sine[...]
            heads[n, seq] = values.astype(bf16)
        heads[3, seq] = attention(facts[seq, 2:3, 0:1], heads[0, seq], heads[1, seq], heads[2, seq])
        shares_from(seq, mixed, out_w, part)
        if k % 2 == 0:
            plane_sum.near(k)
        else:
            plane_sum.far(k)
        if k == 0:
            grad_gather.forward(0)
            grad_gather.forward(1)
        elif k == 1:
            up_z.second()
    grad_gather.forward(2)
    grad_gather.arrive(3)
    grad_gather.copies[3].wait_recv()
    grad_gather.copies[4].wait_recv()
    grad_gather.finish()
    stores += [keep(heads.at[n], ref, 1 + n) for n, ref in enumerate((q_h, k_h, v_h, o_h))]

    @pl.loop(0, count)
    def _(seq):
        grad_seq[seq] = both_blocks(grad_blocks, seq).astype(bf16)

    fetch(tokens_h, grad_blocks.at[mine], 4).wait()
    plane_sum.finish()
    squares = jnp.zeros((rows, 1), f32)
    for n in range(D // LANES):
        lanes = slice(n * LANES, (n + 1) * LANES)
        values = grad_blocks[mine, :, lanes].astype(f32) + plane_sum.chunk(lanes)
        residual[:, lanes] = values
        squares += jnp.sum(values * values, axis=-1, keepdims=True)
    scale = lax.rsqrt(squares / D + NORM_EPSILON)
    for n in range(D // LANES):
        lanes = slice(n * LANES, (n + 1) * LANES)
        blocks[mine, :, lanes] = (residual[:, lanes] * scale * gains[1:2, lanes]).astype(bf16)
    norm_gather = PlaneGather(place, blocks, all_send.at[2], all_recv.at[2])
    norm_gather.start()
    up_z.third()
    down_z.inward()
    stores[0].wait()
    half = hidden.shape[2]
    for k in range(4):
        norm_gather.arrive(k, forwarded=k == 1)
        seq = norm_gather.sequence(k)
        norm[seq] = both_blocks(blocks, seq).astype(bf16)
        if k == 0:
            norm_gather.forward(1)
            up_z.finish()
            down_z.outward()
            fetch(up_landed, up, 5).wait()
        elif k == 1:
            down_z.second()
        gate = times_slices(norm[seq], up, slice(0, half))
        above = times_slices(norm[seq], up, slice(half, 2 * half))
        both[seq, :, :half] = gate
        both[seq, :, half:] = above
        hidden[seq] = (gate * jax.nn.sigmoid(gate) * above).astype(bf16)
    norm_gather.finish()
    stores[0] = keep(norm, second_h, 5)
    stores.append(keep(hidden, hidden_h, 7))
    tall = min(256, half)
    slab = part.shape[1] // 128 * 128

    def down_shares(side):
        lanes = slice(side * D // 2, (side + 1) * D // 2)

        @pl.loop(0, half // tall)
        def _(b):
            product = over_tokens(hidden, lanes_of(b, tall), grad_seq, lanes).astype(bf16)
            for p in range(tall // slab):
                part[b * (tall // slab) + p, :slab, lanes] = product[p * slab : (p + 1) * slab]

    down_shares(0)
    if grps == 4:
        chains = [
            Chain(
                place,
                part,
                near,
                grads_landed,
                slice(side * D // 2, (side + 1) * D // 2),
                chain_send.at[side],
                chain_recv.at[side],
                own_sem.at[6 + side],
            )
            for side in range(2)
        ]
        chains[0].start()
    down_z.third()
    down_shares(1)
    if grps == 4:
        chains[1].start()
        chains[0].step(1)
        chains[1].step(1)
        chains[0].step(2)
    else:
        spread = [pltpu.make_async_copy(rows_of(part, place.g), grads_landed.at[place.g], own_sem.at[6])]
        for dz in range(1, grps):
            spread.append(
                remote(
                    rows_of(part, (place.g + dz) % grps),
                    grads_landed.at[place.g],
                    chain_send.at[0, dz],
                    chain_recv.at[0, dz],
                    place.plane(dz),
                )
            )
        for copy in spread:
            copy.start()
    down_z.finish()
    down_copy = fetch(down_landed, down, 6)
    if grps == 4:
        chains[0].last()
        chains[1].step(2)
        chains[1].last()
    down_copy.wait()

    def feed_forward_grads(seq):
        grads = dot(grad_seq[seq], down[...], 1, 1)
        gate, above = both[seq, :, :half], both[seq, :, half:]
        sigmoid = jax.nn.sigmoid(gate)
        dgu[seq, :, :half] = (grads * above * sigmoid * (1.0 + gate * (1.0 - sigmoid))).astype(bf16)
        dgu[seq, :, half:] = (grads * (gate * sigmoid)).astype(bf16)

    pl.loop(0, count)(feed_forward_grads)
    stores.append(keep(dgu, dgu_h, 8))
    if grps == 4:
        for chain in chains:
            chain.finish()
    else:
        for copy in spread:
            copy.wait()
    for copy in stores:
        copy.wait()


def forward(grps, aligned, tables, own_facts, tokens, own_grad, qkv_own, up_own, out_own, down_own):
    rows = tokens.shape[0]
    shard = qkv_own.shape[0]
    seqs = D // (shard * grps * QUAD)
    ranks = seqs * QUAD
    triple, both = qkv_own.shape[1] // ranks, up_own.shape[1] // ranks
    count, full_rows, head_width = QUAD, rows * seqs, triple // 3
    half = both // 2
    hbm = pl.BlockSpec(memory_space=pl.ANY)
    vmem = pl.BlockSpec(memory_space=pltpu.VMEM)
    shape = jax.ShapeDtypeStruct
    dma = pltpu.SemaphoreType.DMA
    by_heads = shape((count, full_rows, head_width), bf16)
    return pl.pallas_call(
        lambda *refs: forward_kernel(grps, aligned, *refs),
        in_specs=[vmem] * 3 + [hbm] * 6,
        out_specs=[vmem] * 3 + [hbm] * 13,
        out_shape=[
            shape((rows, D), f32),
            shape((8, D), f32),
            shape((ranks, 8, 128), f32),
            shape((count, full_rows, D), bf16),
            by_heads,
            by_heads,
            by_heads,
            by_heads,
            shape((count, full_rows, D), bf16),
            shape((3 if grps == 4 else grps, half // grps, D), bf16),
            shape((count, full_rows, half), bf16),
            shape((count, full_rows, both), bf16),
            shape((seqs, grps, QUAD, shard, triple), bf16),
            shape((seqs, grps, QUAD, shard, both), bf16),
            shape((head_width, D), bf16),
            shape((half, D), bf16),
        ],
        scratch_shapes=[
            pltpu.VMEM((ranks, rows, D), bf16),
            pltpu.VMEM((ranks, rows, D), bf16),
            pltpu.VMEM((count, full_rows, D), bf16),
            pltpu.VMEM((count, full_rows, D), bf16),
            pltpu.VMEM((seqs, QUAD, shard, triple), bf16),
            pltpu.VMEM((seqs, QUAD, shard, both), bf16),
            pltpu.VMEM((seqs, grps, QUAD, shard, triple), bf16),
            pltpu.VMEM((seqs, grps, QUAD, shard, both), bf16),
            pltpu.VMEM((head_width, D), bf16),
            pltpu.VMEM((half, D), bf16),
            pltpu.VMEM((4, count, full_rows, head_width), bf16),
            pltpu.VMEM((ranks, rows, D), bf16),
            pltpu.VMEM((4, rows, D), bf16),
            pltpu.VMEM((3, rows, D), bf16),
            pltpu.VMEM((count, full_rows, both), f32),
            pltpu.VMEM((count, full_rows, half), bf16),
            pltpu.VMEM((count, full_rows, both), bf16),
            pltpu.VMEM((grps, ranks, 8, 128), f32),
            dma((20,)),
            dma((7,)),
            dma((9,)),
            dma((2, 7)),
            dma((2, 7)),
            dma((4,)),
            dma((4,)),
            dma((3,)),
            dma((3,)),
            dma((3, 7)),
            dma((3, 7)),
            dma((4, 2 * grps)),
            dma((4, grps)),
            dma((7 + grps,)),
            dma((7 + grps,)),
            dma((2, max(5, grps))),
            dma((2, max(5, grps))),
            dma((8,)),
        ],
        compiler_params=pltpu.CompilerParams(
            collective_id=1, has_side_effects=True, vmem_limit_bytes=VMEM_LIMIT
        ),
        cost_estimate=pl.CostEstimate(
            flops=20 * 10**9, bytes_accessed=60 * 2**20, transcendentals=4 * 10**6
        ),
        name="forward",
    )(*tables, own_facts, tokens, own_grad, qkv_own, up_own, out_own, down_own)


DEPTH = 4


def adam_kernel(grps, down_planes, out_planes, up_ranks, qkv_ranks, gains_sum, gains, gains_m, gains_v, *refs):
    states, outs = refs[:12], refs[12:28]
    gains_outs = refs[28:31]
    state, planes, ranks, fresh, copied, in_sem, out_sem = refs[31:]
    plane = lax.axis_index("grp")
    rows = state.shape[2]
    units = CHUNK // QUAD
    pieces = []
    for n, (name, rate) in enumerate(
        (("down", FF ** (-0.5)), ("out", (D // 128) ** (-0.5)), ("up", D ** (-0.5)), ("qkv", D ** (-0.5)))
    ):
        arrays = states[3 * n : 3 * n + 3]
        for top in range(0, arrays[0].shape[0], rows):
            for left in range(0, arrays[0].shape[1], CHUNK):
                pieces.append((name, rate, n, top, left))

    def grad_source(name, top, left, slot):
        if name in ("down", "out"):
            source = down_planes if name == "down" else out_planes
            return (
                source.at[:, top : top + rows, left : left + CHUNK],
                planes.at[slot, : source.shape[0]],
            )
        source, parts = (up_ranks, 2) if name == "up" else (qkv_ranks, 3)
        width = source.shape[2] // parts
        per_seq = width // units
        n = left // CHUNK
        seqs = source.shape[0] // QUAD
        seq = n // per_seq % seqs
        first = n // (per_seq * seqs) * width + n % per_seq * units
        return source.at[seq * QUAD : (seq + 1) * QUAD, :, first : first + units], ranks.at[slot]

    def reads(k):
        name, _, n, top, left = pieces[k]
        slot = k % DEPTH
        window = (slice(top, top + rows), slice(left, left + CHUNK))
        copies = [
            pltpu.make_async_copy(states[3 * n + i].at[window], state.at[slot, i], in_sem.at[slot, i])
            for i in range(3)
        ]
        source, space = grad_source(name, top, left, slot)
        return copies + [pltpu.make_async_copy(source, space, in_sem.at[slot, 3])]

    def writes(k):
        _, _, n, top, left = pieces[k]
        slot = k % DEPTH
        window = (slice(top, top + rows), slice(left, left + CHUNK))
        copies = [
            pltpu.make_async_copy(fresh.at[slot, i], outs[4 * n + i].at[window], out_sem.at[slot, i])
            for i in range(3)
        ]
        return copies + [
            pltpu.make_async_copy(copied.at[slot], outs[4 * n + 3].at[window], out_sem.at[slot, 3])
        ]

    def gradient(name, slot):
        if name in ("down", "out"):
            chained = name == "down"
            source = down_planes if chained else out_planes
            total = jnp.zeros((rows, CHUNK), f32)
            for j in range(source.shape[0]):
                held = planes[slot, j].astype(f32)
                if grps == 4 and chained and j < 2:
                    held = jnp.where(plane > 0 if j == 0 else plane < 3, held, 0.0)
                elif grps == 4 and not chained and j in (0, 3):
                    held = jnp.where(plane != 3 - j, held, 0.0)
                total += held
            return total
        lanes = down_planes.shape[1] if name == "up" else HEAD_DIM
        values = [ranks[slot, q].astype(f32) for q in range(QUAD)]
        return jnp.concatenate(
            [
                values[q][:, n * lanes : (n + 1) * lanes]
                for n in range(units // lanes)
                for q in range(QUAD)
            ],
            axis=1,
        )

    for k in range(DEPTH - 1):
        for copy in reads(k):
            copy.start()
    results = adam_update(gains[...], gains_m[...], gains_v[...], gains_sum[...], 0.3)
    for out, result in zip(gains_outs, results):
        out[...] = result
    for k, (name, rate, _, _, _) in enumerate(pieces):
        slot = k % DEPTH
        if k + DEPTH - 1 < len(pieces):
            for copy in reads(k + DEPTH - 1):
                copy.start()
        for copy in reads(k):
            copy.wait()
        if k >= DEPTH:
            for copy in writes(k - DEPTH):
                copy.wait()
        results = adam_update(state[slot, 0], state[slot, 1], state[slot, 2], gradient(name, slot), rate)
        for i in range(3):
            fresh[slot, i] = results[i]
        copied[slot] = results[0].astype(bf16)
        for copy in writes(k):
            copy.start()
    for k in range(len(pieces) - DEPTH, len(pieces)):
        for copy in writes(k):
            copy.wait()


def adam(grps, down_planes, out_planes, up_ranks, qkv_ranks, gains_sum, gains, states):
    rows = up_ranks.shape[1]
    hbm = pl.BlockSpec(memory_space=pl.ANY)
    vmem = pl.BlockSpec(memory_space=pltpu.VMEM)
    shapes = []
    for array in states[::3]:
        shapes += [jax.ShapeDtypeStruct(array.shape, f32)] * 3
        shapes.append(jax.ShapeDtypeStruct(array.shape, bf16))
    shapes += [jax.ShapeDtypeStruct(gains[0].shape, f32)] * 3
    size = sum(array.size for array in states) // 3
    outs = pl.pallas_call(
        lambda *refs: adam_kernel(grps, *refs),
        in_specs=[hbm] * 4 + [vmem] * 4 + [hbm] * 12,
        out_specs=[hbm] * 16 + [vmem] * 3,
        out_shape=shapes,
        scratch_shapes=[
            pltpu.VMEM((DEPTH, 3, rows, CHUNK), f32),
            pltpu.VMEM((DEPTH, grps, rows, CHUNK), bf16),
            pltpu.VMEM((DEPTH, QUAD, rows, CHUNK // QUAD), bf16),
            pltpu.VMEM((DEPTH, 3, rows, CHUNK), f32),
            pltpu.VMEM((DEPTH, rows, CHUNK), bf16),
            pltpu.SemaphoreType.DMA((DEPTH, 4)),
            pltpu.SemaphoreType.DMA((DEPTH, 4)),
        ],
        compiler_params=pltpu.CompilerParams(vmem_limit_bytes=VMEM_LIMIT),
        cost_estimate=pl.CostEstimate(flops=size * 16, bytes_accessed=size * 28, transcendentals=size),
        name="adam",
    )(down_planes, out_planes, up_ranks, qkv_ranks, gains_sum, *gains, *states)
    return outs[:4], outs[4:8], outs[8:12], outs[12:16], outs[16:]


def on_device(
    tokens,
    cotangent,
    lengths,
    qkv_weight,
    qkv_moment,
    qkv_square,
    out_weight,
    out_moment,
    out_square,
    up_weight,
    up_moment,
    up_square,
    down_weight,
    down_moment,
    down_square,
    norm_gains,
    gains_moment,
    gains_square,
):
    seqs = lax.axis_size("seq")
    grps = lax.axis_size("grp")
    ranks = seqs * QUAD
    own_rows = tokens.shape[1]
    full_rows = own_rows * seqs
    all_rows = full_rows * QUAD
    heads_local = HEADS // ranks
    head_width = heads_local * HEAD_DIM
    units = down_weight.shape[0]
    aligned = out_weight.shape[0] == HEAD_DIM
    tables = rotate_table(full_rows, heads_local)

    positions = lax.axis_index("seq") * own_rows + jnp.arange(own_rows, dtype=jnp.int32)
    own_grad = jnp.where((positions < lengths[0])[:, None], cotangent[0], 0)
    own_gains = norm_gains.shape[1]
    own_facts = jnp.zeros((8, 128), f32)
    own_facts = own_facts.at[:2, :own_gains].set(norm_gains.astype(bf16).astype(f32))
    own_facts = own_facts.at[2].set(lengths[0].astype(f32))

    out_own = out_weight
    if not aligned:
        out_all = lax.all_gather(out_weight.astype(bf16), EVERY, axis=0, tiled=True)
        out_all = out_all.reshape(seqs, heads_local, QUAD, HEAD_DIM, D)
        seat = lax.axis_index("row") * 2 + lax.axis_index("core")
        out_own = lax.dynamic_index_in_dim(
            lax.dynamic_index_in_dim(out_all, lax.axis_index("seq"), 0, False), seat, 1, False
        ).reshape(head_width, D)
    (
        residual,
        gains,
        facts,
        first_norm,
        queries,
        key_vectors,
        value_vectors,
        attended,
        second_norm,
        down_planes,
        hidden,
        grad_both,
        qkv_local,
        up_local,
        out_local,
        down_local,
    ) = forward(
        grps,
        aligned,
        tables,
        own_facts,
        tokens[0],
        own_grad,
        qkv_weight,
        up_weight,
        out_own,
        down_weight,
    )
    if not aligned:
        out_local = out_own
    (
        input_grad,
        block_output,
        gains_total,
        out_planes,
        up_ranks,
        qkv_ranks,
        *_,
    ) = backward(
        grps,
        aligned,
        facts,
        gains,
        tables,
        residual,
        tokens[0],
        own_grad,
        grad_both,
        up_local.reshape(D, -1),
        second_norm,
        first_norm,
        out_local,
        qkv_local.reshape(D, -1),
        (queries, key_vectors, value_vectors, attended),
        hidden,
        down_local,
    )
    if aligned:
        out_sum = out_planes
    else:
        placed_term = jnp.zeros((seqs, QUAD, heads_local, HEAD_DIM, D), bf16)
        placed_term = lax.dynamic_update_slice(
            placed_term,
            out_planes.reshape(1, 1, heads_local, HEAD_DIM, D),
            (lax.axis_index("seq"), seat, 0, 0, 0),
        )
        out_sum = lax.psum_scatter(
            placed_term.transpose(0, 2, 1, 3, 4).reshape(D, D),
            EVERY,
            scatter_dimension=0,
            tiled=True,
        )[None]
    device = ((lax.axis_index("seq") * grps + lax.axis_index("grp")) * 2 + lax.axis_index("row")) * 2
    gains_sum = lax.dynamic_slice(
        gains_total, (0, (device + lax.axis_index("core")) * own_gains), (2, own_gains)
    )
    down_new, out_new, up_new, qkv_new, gains_new = adam(
        grps,
        down_planes,
        out_sum,
        up_ranks,
        qkv_ranks,
        gains_sum,
        (norm_gains, gains_moment, gains_square),
        (
            down_weight,
            down_moment,
            down_square,
            out_weight,
            out_moment,
            out_square,
            up_weight,
            up_moment,
            up_square,
            qkv_weight,
            qkv_moment,
            qkv_square,
        ),
    )
    return (
        block_output[None],
        input_grad[None],
        *qkv_new,
        *out_new,
        *up_new,
        *down_new,
        *gains_new,
    )


def solution(mesh):
    seqs, rest = mesh.shape["seq"], mesh.shape["fsdp"]
    planes = Mesh(
        mesh.devices.reshape(seqs, rest // QUAD, 2, 2), ("seq", "grp", "row", "core")
    )
    rows = P(("grp", "row", "core"), "seq", None)
    shards = P(EVERY, None)
    gains = P(None, EVERY)
    return jax.shard_map(
        on_device,
        mesh=planes,
        in_specs=(rows, rows, P(("grp", "row", "core"))) + (shards,) * 12 + (gains,) * 3,
        out_specs=(rows, rows) + (shards,) * 16 + (gains,) * 3,
        check_vma=False,
    )
```

```python
import math

import jax
import jax.numpy as jnp
from jax import lax
from jax.experimental import pallas as pl
from jax.experimental.pallas import tpu as pltpu
from jax.sharding import Mesh, PartitionSpec as P

D = 2048
HEADS = 32
HEAD_DIM = 64
FF = 4096
WINDOW = 128
STEP = 5


NORM_EPSILON = 1e-05
MOMENT_DECAY = 0.5
WEIGHT_DECAY = 0.1
ADAM_EPSILON = 1e-08

SEATS = ("row", "core", "seq")
RANKS = ("seq", "row", "core")
EVERY = ("seq", "grp", "row", "core")
QUAD = 4
VMEM_LIMIT = 63 * 2**20

bf16 = jnp.bfloat16
f32 = jnp.float32


def rotate_table(length, copies):
    halves = HEAD_DIM // 2
    freqs = jnp.exp(-math.log(10000.0) * 2.0 * jnp.arange(halves).astype(f32) / HEAD_DIM)
    angles = jnp.arange(length, dtype=jnp.int32).astype(f32)[:, None] * freqs[None, :]
    cosine, sine = jnp.cos(angles), jnp.sin(angles)
    return (
        jnp.tile(jnp.concatenate([cosine, cosine], axis=1), (1, copies)),
        jnp.tile(jnp.concatenate([-sine, sine], axis=1), (1, copies)),
    )


def adam_update(weight, moment, square, gradient, step_rate):
    moment_new = MOMENT_DECAY * moment + (1.0 - MOMENT_DECAY) * gradient
    square_new = MOMENT_DECAY * square + (1.0 - MOMENT_DECAY) * gradient * gradient
    correction = 1.0 - MOMENT_DECAY**STEP
    unbias = 1.0 / correction
    update = (moment_new * unbias) / (jnp.sqrt(square_new * unbias) + ADAM_EPSILON)
    return (weight - step_rate * (update + WEIGHT_DECAY * weight), moment_new, square_new)


def dot(a, b, lhs=1, rhs=0):
    return lax.dot_general(a, b, (((lhs,), (rhs,)), ((), ())), preferred_element_type=f32)


def swap_halves(values, first):
    width = values.shape[1]
    half = HEAD_DIM // 2
    return jnp.where(
        first, pltpu.roll(values, width - half, 1), pltpu.roll(values, half, 1)
    )


def allowed_mask(rows, length):
    row = lax.broadcasted_iota(jnp.int32, (rows, rows), 0)
    col = lax.broadcasted_iota(jnp.int32, (rows, rows), 1)
    return (col <= row) & (row - col < WINDOW) & (col.astype(f32) < length)


def head_lanes(rows, width, head):
    lane = lax.broadcasted_iota(jnp.int32, (rows, width), 1)
    return (lane // HEAD_DIM) == head


def softmax_rows(queries, key_vectors, allowed):
    scores = jnp.where(allowed, dot(queries, key_vectors, 1, 1) * (HEAD_DIM**-0.5), -1e30)
    shifted = jnp.exp(scores - jnp.max(scores, axis=-1, keepdims=True))
    return shifted / jnp.sum(shifted, axis=-1, keepdims=True)


def attention(length, queries, key_vectors, value_vectors):
    rows, width = queries.shape
    allowed = allowed_mask(rows, length)
    total = jnp.zeros((rows, width), f32)
    for head in range(width // HEAD_DIM):
        mine = head_lanes(rows, width, head)
        weights = softmax_rows(jnp.where(mine, queries, 0), key_vectors, allowed)
        total += dot(weights.astype(bf16), jnp.where(mine, value_vectors, 0))
    return total.astype(bf16)


def attention_grads(length, queries, key_vectors, value_vectors, grads):
    rows, width = queries.shape
    allowed = allowed_mask(rows, length)
    grad_q = jnp.zeros((rows, width), f32)
    grad_k = jnp.zeros((rows, width), f32)
    grad_v = jnp.zeros((rows, width), f32)
    for head in range(width // HEAD_DIM):
        mine = head_lanes(rows, width, head)
        q_head = jnp.where(mine, queries, 0)
        g_head = jnp.where(mine, grads, 0)
        weights = softmax_rows(q_head, key_vectors, allowed)
        grad_p = dot(g_head, value_vectors, 1, 1)
        delta = jnp.sum(weights * grad_p, axis=-1, keepdims=True)
        grad_s = jnp.where(allowed, weights * (grad_p - delta), 0.0).astype(bf16)
        grad_q += dot(grad_s, jnp.where(mine, key_vectors, 0))
        grad_k += dot(grad_s, q_head, 0, 0)
        grad_v += dot(weights.astype(bf16), g_head, 0, 0)
    return grad_q, grad_k, grad_v


MESH = pl.DeviceIdType.MESH
RELATIONS = tuple((a, b, d) for a in range(2) for b in range(2) for d in range(2))[1:]


class Place:
    def __init__(self, grps):
        self.grps = grps
        self.s = lax.axis_index("seq")
        self.g = lax.axis_index("grp")
        self.r = lax.axis_index("row")
        self.c = lax.axis_index("core")

    def peer(self, relation):
        ds, dr, dc = relation
        return ((self.s + ds) % 2, self.g, (self.r + dr) % 2, (self.c + dc) % 2)

    def plane(self, dz):
        return (self.s, (self.g + dz) % self.grps, self.r, self.c)

    def rank(self, relation=(0, 0, 0)):
        s, _, r, c = self.peer(relation)
        return (s * 2 + r) * 2 + c

    def seat(self, relation=(0, 0, 0)):
        s, _, r, c = self.peer(relation)
        return (r * 2 + c) * 2 + s

    def corner(self, relation=(0, 0, 0)):
        s, _, r, _ = self.peer(relation)
        return r * 2 + s

    def greet(self):
        barrier = pltpu.get_barrier_semaphore()
        for relation in RELATIONS:
            pl.semaphore_signal(barrier, inc=1, device_id=self.peer(relation), device_id_type=MESH)
        for dz in range(1, self.grps):
            pl.semaphore_signal(barrier, inc=1, device_id=self.plane(dz), device_id_type=MESH)
        pl.semaphore_wait(barrier, len(RELATIONS) + self.grps - 1)


SIBLING = (0, 0, 1)
ACROSS = ((1, 0, 0), (0, 1, 0), (1, 1, 0))


def remote(src, dst, send_sem, recv_sem, device):
    return pltpu.make_async_remote_copy(
        src_ref=src,
        dst_ref=dst,
        send_sem=send_sem,
        recv_sem=recv_sem,
        device_id=device,
        device_id_type=MESH,
    )


class PlaneSum:
    def __init__(self, place, part, near, far, sems):
        self.place, self.part, self.nears, self.fars = place, part, near, far
        self.near_send, self.near_recv, self.far_send, self.far_recv = sems
        self.first, self.second = [None] * 4, []

    def sequence(self, k):
        place = self.place
        row = (place.r + 1) % 2 if k < 2 else place.r
        return row * 2 + ((place.c + 1) % 2 if k % 2 == 0 else place.c)

    def near(self, k):
        for s in range(2):
            copy = remote(
                self.part.at[2 * self.sequence(k) + s],
                self.nears.at[k + s],
                self.near_send.at[k + s],
                self.near_recv.at[k + s],
                self.place.peer(SIBLING),
            )
            copy.start()
            self.first[k + s] = copy

    def far(self, k):
        place = self.place
        for s in range(2):
            self.first[k - 1 + s].wait()
            self.nears[k - 1 + s] = (
                self.part[2 * self.sequence(k) + s].astype(f32)
                + self.nears[k - 1 + s].astype(f32)
            ).astype(bf16)
        for d in (1, 2) if k == 1 else (0,):
            relation = ACROSS[d]
            copy = remote(
                self.nears.at[k - 1 + (place.s + relation[0]) % 2],
                self.fars.at[d],
                self.far_send.at[d],
                self.far_recv.at[d],
                place.peer(relation),
            )
            copy.start()
            self.second.append(copy)

    def finish(self):
        for copy in self.second:
            copy.wait()

    def chunk(self, lanes):
        total = self.nears[2 + self.place.s, :, lanes].astype(f32)
        for d in range(3):
            total += self.fars[d, :, lanes].astype(f32)
        return total


class PlaneGather:
    def __init__(self, place, blocks, send, recv):
        self.place, self.blocks, self.sends, self.recvs = place, blocks, send, recv
        self.copies = [None] * 7

    def send(self, block, sem, relation):
        copy = remote(
            self.blocks.at[block],
            self.blocks.at[block],
            self.sends.at[sem],
            self.recvs.at[sem],
            self.place.peer(relation),
        )
        copy.start()
        self.copies[sem] = copy

    def start(self):
        mine = self.place.seat()
        for d in range(2):
            self.send(mine, d, ACROSS[d])
        self.send(mine, 3, SIBLING)

    def forward(self, d):
        self.copies[d].wait_recv()
        self.send(self.place.seat(ACROSS[d]), 4 + d, SIBLING)
        if d == 0:
            self.send(self.place.seat(), 2, ACROSS[2])

    def sequence(self, k):
        place = self.place
        row = place.r if k < 2 else (place.r + 1) % 2
        return row * 2 + (place.c if k % 2 == 0 else (place.c + 1) % 2)

    def arrive(self, k, forwarded=False):
        if k == 0:
            self.forward(0)
        elif k == 1:
            if not forwarded:
                self.forward(1)
            self.copies[3].wait_recv()
            self.copies[4].wait_recv()
        elif k == 2:
            self.forward(2)
        else:
            self.copies[5].wait_recv()
            self.copies[6].wait_recv()

    def finish(self):
        for copy in self.copies:
            copy.wait_send()


class ToOwners:
    def __init__(self, place, shares, landed, met, stage, send, recv, own):
        self.place, self.shares, self.landed, self.met, self.stage = place, shares, landed, met, stage
        self.send, self.recv, self.own_sem = send, recv, own
        self.line = place.grps == 4
        self.own = pltpu.make_async_copy(shares.at[place.g], landed.at[place.g], own)

    def copy(self, block, landing, sem, recv, target):
        place = self.place
        return remote(
            self.shares.at[block],
            landing,
            self.send.at[sem],
            self.recv.at[recv],
            (place.s, target, place.r, place.c),
        )

    def direct(self, g):
        targets = ((2, 1), (2, 0), (1, 3), (1, 2))[g]
        return [self.copy(t, self.landed.at[g], t, g, t) for t in targets]

    def meeting(self, g):
        far, inner = (3, 1) if g == 0 else (0, 2)
        return self.copy(far, self.met, far, inner, inner)

    def joined(self, g):
        far = 3 if g == 1 else 0
        return self.copy(far, self.landed.at[g], far, g, far)

    def start(self, waits=False):
        place, self.waits = self.place, waits
        self.own.start()
        if self.line:
            for g in range(4):

                @pl.when(place.g == g)
                def _():
                    if g in (0, 3):
                        self.meeting(g).start()
                    if g in (1, 2) or not waits:
                        for copy in self.direct(g):
                            copy.start()

        else:
            self.copies = [
                self.copy((place.g + dz) % place.grps, self.landed.at[place.g], dz, dz, (place.g + dz) % place.grps)
                for dz in range(1, place.grps)
            ]
            for copy in self.copies:
                copy.start()
        return self

    def proceed(self):
        if self.line:
            for g in (0, 3):

                @pl.when(self.place.g == g)
                def _():
                    self.meeting(g).wait_send()
                    for copy in self.direct(g):
                        copy.start()

    def join(self):
        if not self.line:
            return
        for g in (1, 2):

            @pl.when(self.place.g == g)
            def _():
                outer, far = (0, 3) if g == 1 else (3, 0)
                self.copy(far, self.met, far, g, outer).wait_recv()
                copy = pltpu.make_async_copy(self.met, self.stage, self.own_sem)
                self.own.wait()
                copy.start()
                copy.wait()
                if len(self.stage.shape) == 2:
                    self.shares[far] = (
                        self.shares[far].astype(f32) + self.stage[...].astype(f32)
                    ).astype(bf16)
                else:
                    for n in range(self.stage.shape[0]):
                        self.shares[far, n] = (
                            self.shares[far, n].astype(f32) + self.stage[n].astype(f32)
                        ).astype(bf16)
                self.joined(g).start()

        for g in (0, 3):

            @pl.when(self.place.g == g)
            def _():
                self.own.wait()

    def sent(self):
        if not self.line:
            for copy in self.copies:
                copy.wait_send()
            return
        for g in range(4):

            @pl.when(self.place.g == g)
            def _():
                for copy in self.direct(g):
                    copy.wait_send()
                if g in (1, 2):
                    self.joined(g).wait_send()
                elif not self.waits:
                    self.meeting(g).wait_send()

    def received(self):
        if not self.line:
            self.own.wait()
            for copy in self.copies:
                copy.wait_recv()
            return
        for g in range(4):

            @pl.when(self.place.g == g)
            def _():
                for j in ((1, 2), (0, 2, 3), (0, 1, 3), (1, 2))[g]:
                    self.copy(g, self.landed.at[j], j, j, j).wait_recv()

    def finish(self):
        self.sent()
        self.received()

    def holds(self, j):
        g = self.place.g
        return (g % 3 != 0) | (j + g != 3) if self.line else True


class Exchange:
    def __init__(self, place, blocks, held, send, recv, own):
        mine = place.rank()
        kept = held.at[mine // QUAD, mine % QUAD] if len(held.shape) == 4 else held.at[mine]

        def block(t):
            return blocks.at[0, t // QUAD, t % QUAD] if len(blocks.shape) == 5 else blocks.at[t]

        self.copies = []
        for n, relation in enumerate(RELATIONS):
            copy = remote(
                block(place.rank(relation)),
                kept,
                send.at[n],
                recv.at[n],
                place.peer(relation),
            )
            copy.start()
            self.copies.append(copy)
        copy = pltpu.make_async_copy(block(mine), kept, own)
        copy.start()
        self.copies.append(copy)

    def finish(self):
        for copy in self.copies:
            copy.wait()


LANES = 512


def lanes_of(n, width=LANES):
    return pl.ds(pl.multiple_of(n * width, width), width)


def shares_of(seq, values, weight, part):
    rows = part.shape[1]

    @pl.loop(0, part.shape[2] // LANES)
    def _(n):
        product = dot(values[seq], weight[lanes_of(n)], 1, 1)
        part[2 * seq, :, lanes_of(n)] = product[:rows].astype(bf16)
        part[2 * seq + 1, :, lanes_of(n)] = product[rows:].astype(bf16)


def over_tokens(first, lanes, second, other):
    left, right = first[:, :, lanes], second[:, :, other]
    tokens = left.shape[0] * left.shape[1]
    return dot(left.reshape(tokens, left.shape[2]), right.reshape(tokens, right.shape[2]), 0, 0)


def row_shares(first, second, shares):
    grps, seqs, rows, _ = shares.shape
    width = 256
    pieces = width // rows

    @pl.loop(0, first.shape[2] // width)
    def _(b):
        product = over_tokens(first, lanes_of(b, width), second, slice(None)).astype(bf16)
        for p in range(pieces):
            index = b * pieces + p
            shares[index % grps, index // grps] = product[p * rows : (p + 1) * rows]


def summed_rows(landed, holds, blocks):
    seqs, rows = landed.shape[1], blocks.shape[1]
    for seq in range(seqs):
        for quad in range(QUAD):
            block = slice(quad * rows, (quad + 1) * rows)
            total = jnp.zeros((rows, landed.shape[3]), f32)
            for j in range(landed.shape[0]):
                total += jnp.where(holds(j), landed[j, seq, block].astype(f32), 0.0)
            blocks[seq * QUAD + quad] = total.astype(bf16)


def back_kernel(
    grps,
    aligned,
    facts,
    gains,
    cosine,
    sine,
    residual_h,
    own_tokens_h,
    own_grad_h,
    dgu_h,
    up_h,
    down_share_h,
    second_h,
    first_h,
    out_h,
    qkv_h,
    q_h,
    k_h,
    v_h,
    o_h,
    hidden_h,
    down_h,
    input_grad,
    block_output,
    gains_sum,
    down_landed,
    out_landed,
    up_held,
    qkv_held,
    up_landed,
    qkv_landed,
    down_met,
    up_met,
    out_met,
    qkv_met,
    wide,
    up,
    acts,
    out_w,
    qkv,
    part,
    near,
    far,
    blocks,
    turned,
    down_share,
    up_share,
    out_share,
    qkv_share,
    up_sum,
    qkv_sum,
    stage_down,
    stage_low,
    stage_wide,
    gain_part,
    gain_plane,
    gain_far,
    residual,
    own_tokens,
    own_grad,
    load,
    near_send,
    near_recv,
    far_send,
    far_recv,
    all_send,
    all_recv,
    z_send,
    z_recv,
    swap_send,
    swap_recv,
    gain_send,
    gain_recv,
    own_sem,
    near_free,
    far_free,
):
    place = Place(grps)
    rows = residual.shape[0]
    gain_part[...] = jnp.zeros_like(gain_part)
    count, full_rows, head_width = q_h.shape

    def fetch(src, dst, n):
        copy = pltpu.make_async_copy(src, dst, load.at[n])
        copy.start()
        return copy

    loads = [fetch(dgu_h, wide, 0), fetch(up_h, up, 1), fetch(second_h, acts, 3)]
    down_load = fetch(down_share_h, down_share, 2)
    weights = [fetch(out_h, out_w, 5), fetch(qkv_h, qkv, 6)]
    small = [
        fetch(src, dst, 14 + n)
        for n, (src, dst) in enumerate(
            ((residual_h, residual), (own_grad_h, own_grad), (own_tokens_h, own_tokens))
        )
    ]
    place.greet()
    down_load.wait()
    for copy in loads[:2]:
        copy.wait()

    sums = (near_send, near_recv, far_send, far_recv)
    def to_owners(n, shares, landed, met, stage, waits=False):
        return ToOwners(
            place, shares, landed, met, stage, z_send.at[n], z_recv.at[n], own_sem.at[n]
        ).start(waits)

    def summed_over_plane(values, weight):
        total = PlaneSum(place, part, near, far, sums)
        for k in range(4):
            shares_of(total.sequence(k), values, weight, part)
            if k % 2 == 0:
                total.near(k)
            else:
                total.far(k)
        return total

    down_out = to_owners(0, down_share, down_landed, down_met, stage_down)
    second_sum = summed_over_plane(wide, up)
    loads[2].wait()
    row_shares(acts, wide, up_share)
    up_out = to_owners(1, up_share, up_landed, up_met, stage_wide, True)
    down_out.join()
    fetch_first = fetch(first_h, acts, 3)
    heads = [
        fetch(ref, wide.at[:, :, n * head_width : (n + 1) * head_width], 7 + n)
        for n, ref in enumerate((q_h, k_h, v_h, o_h))
    ]

    half = hidden_h.shape[2]
    hidden = turned.at[:, :, :half]
    last = [fetch(hidden_h, hidden, 11)]
    for n in range(2):
        columns = slice(n * D // 2, (n + 1) * D // 2)
        last.append(fetch(down_h.at[:, columns], up.at[n * half : (n + 1) * half, : D // 2], 12 + n))
    for copy in small:
        copy.wait()
    second_sum.finish()
    mine = place.seat()
    inner = jnp.zeros((rows, 1), f32)
    squares = jnp.zeros((rows, 1), f32)
    for n in range(D // LANES):
        lanes = slice(n * LANES, (n + 1) * LANES)
        grad = second_sum.chunk(lanes)
        values = residual[:, lanes]
        inner += jnp.sum(grad * gains[1:2, lanes] * values, axis=-1, keepdims=True)
        squares += jnp.sum(values * values, axis=-1, keepdims=True)
    scale = lax.rsqrt(squares / D + NORM_EPSILON)
    inner = inner / D
    for n in range(D // LANES):
        lanes = slice(n * LANES, (n + 1) * LANES)
        grad, values = second_sum.chunk(lanes), residual[:, lanes]
        gain_part[1:2, lanes] = jnp.sum(grad * values * scale, axis=0, keepdims=True)
        total = own_grad[:, lanes].astype(f32) + scale * (
            grad * gains[1:2, lanes] - values * scale * scale * inner
        )
        input_grad[:, lanes] = total
        blocks[mine, :, lanes] = total.astype(bf16)

    gather = PlaneGather(place, blocks, all_send, all_recv)
    gather.start()
    for copy in weights + heads:
        copy.wait()

    lane = lax.broadcasted_iota(jnp.int32, (full_rows, head_width), 1)
    first_half = (lane % HEAD_DIM) < HEAD_DIM // 2

    for copy in last:
        copy.wait()

    @pl.loop(0, count)
    def _(seq):
        for n in range(D // LANES):
            top, left = n * LANES // (D // 2) * half, n * LANES % (D // 2)
            product = dot(hidden[seq], up[top : top + half, left : left + LANES])
            part[2 * seq, :, n * LANES : (n + 1) * LANES] = product[:rows].astype(bf16)
            part[2 * seq + 1, :, n * LANES : (n + 1) * LANES] = product[rows:].astype(bf16)

    out_rows = out_share.shape[1]

    def out_shares():
        @pl.loop(0, D // LANES)
        def _(n):
            lanes = lanes_of(n)
            total = jnp.zeros((head_width, LANES), f32)
            for seq in range(count):
                values = wide[seq, :, 3 * head_width : 4 * head_width].astype(f32)
                total += dot(values[:rows].astype(bf16), blocks[2 * seq, :, lanes], 0, 0)
                total += dot(values[rows:].astype(bf16), blocks[2 * seq + 1, :, lanes], 0, 0)
            total = total.astype(bf16)
            for j in range(out_share.shape[0]):
                out_share[j, :, lanes] = total[j * out_rows : (j + 1) * out_rows]

    up_out.proceed()
    up_out.join()
    last_sum = PlaneSum(place, part, near, far, sums)
    for k in range(4):
        gather.arrive(k)
        seq = gather.sequence(k)
        if k == 3:
            out_shares()
            if aligned:
                out_out = to_owners(3, out_share, out_landed, out_met, stage_low)
            else:
                out_out = pltpu.make_async_copy(out_share, out_landed, own_sem.at[3])
                out_out.start()
        grads = jnp.concatenate(
            [dot(blocks[2 * seq], out_w[...], 1, 1), dot(blocks[2 * seq + 1], out_w[...], 1, 1)],
            axis=0,
        ).astype(bf16)
        queries = wide[seq, :, 0:head_width]
        key_vectors = wide[seq, :, head_width : 2 * head_width]
        value_vectors = wide[seq, :, 2 * head_width : 3 * head_width]
        grad_q, grad_k, grad_v = attention_grads(
            facts[seq, 2:3, 0:1], queries, key_vectors, value_vectors, grads
        )
        for n, grad in enumerate((grad_q, grad_k)):
            values = (grad * HEAD_DIM**-0.5).astype(bf16).astype(f32)
            back = values * cosine[...] - swap_halves(values, first_half) * sine[...]
            turned[seq, :, n * head_width : (n + 1) * head_width] = back.astype(bf16)
        turned[seq, :, 2 * head_width : 3 * head_width] = grad_v.astype(bf16)
        if k == 1:
            last_sum.near(0)
            last_sum.near(2)
        elif k == 2:
            last_sum.far(1)
            last_sum.far(3)

    gather.finish()
    fetch_first.wait()
    row_shares(acts, turned, qkv_share)
    triple = turned.shape[2]
    qkv_out = to_owners(2, qkv_share, qkv_landed, qkv_met, stage_wide.at[:, :, :triple], True)

    last_sum.finish()
    for n in range(D // LANES):
        lanes = slice(n * LANES, (n + 1) * LANES)
        block_output[:, lanes] = (residual[:, lanes] + last_sum.chunk(lanes)).astype(bf16)
    pl.semaphore_signal(near_free, inc=1, device_id=place.peer(SIBLING), device_id_type=MESH)
    for relation in ACROSS:
        pl.semaphore_signal(far_free, inc=1, device_id=place.peer(relation), device_id_type=MESH)
    pl.semaphore_wait(near_free, 1)
    pl.semaphore_wait(far_free, 3)
    first_sum = summed_over_plane(turned, qkv)
    if aligned:
        out_out.join()
    qkv_out.proceed()
    qkv_out.join()
    first_sum.finish()
    inner = jnp.zeros((rows, 1), f32)
    squares = jnp.zeros((rows, 1), f32)
    for n in range(D // LANES):
        lanes = slice(n * LANES, (n + 1) * LANES)
        grad = first_sum.chunk(lanes)
        values = own_tokens[:, lanes].astype(f32)
        inner += jnp.sum(grad * gains[0:1, lanes] * values, axis=-1, keepdims=True)
        squares += jnp.sum(values * values, axis=-1, keepdims=True)
    scale = lax.rsqrt(squares / D + NORM_EPSILON)
    inner = inner / D
    for n in range(D // LANES):
        lanes = slice(n * LANES, (n + 1) * LANES)
        grad, values = first_sum.chunk(lanes), own_tokens[:, lanes].astype(f32)
        gain_part[0:1, lanes] = jnp.sum(grad * values * scale, axis=0, keepdims=True)
        input_grad[:, lanes] += scale * (
            grad * gains[0:1, lanes] - values * scale * scale * inner
        )

    gain_copies = []
    for n, relation in enumerate(RELATIONS):
        copy = remote(
            gain_part, gain_plane.at[n], gain_send.at[n], gain_recv.at[n], place.peer(relation)
        )
        copy.start()
        gain_copies.append(copy)

    up_out.finish()
    landed = pltpu.make_async_copy(up_landed, up_share, load.at[1])
    landed.start()
    for copy in gain_copies:
        copy.wait()
    total = gain_part[...]
    for n in range(len(RELATIONS)):
        total += gain_plane[n]
    gain_far[0] = total
    gain_copies = []
    for dz in range(1, grps):
        copy = remote(
            gain_far.at[0],
            gain_far.at[dz],
            gain_send.at[7 + dz],
            gain_recv.at[7 + dz],
            place.plane(dz),
        )
        copy.start()
        gain_copies.append(copy)
    landed.wait()
    summed_rows(up_share, up_out.holds, up_sum)
    up_swap = Exchange(place, up_sum, up_held, swap_send.at[0], swap_recv.at[0], own_sem.at[4])
    for copy in gain_copies:
        copy.wait()
    total = gain_far[0]
    for dz in range(1, grps):
        total += gain_far[dz]
    gains_sum[...] = total

    qkv_out.finish()
    landed = pltpu.make_async_copy(qkv_landed, qkv_share, load.at[6])
    landed.start()
    landed.wait()
    summed_rows(qkv_share, qkv_out.holds, qkv_sum)
    qkv_swap = Exchange(place, qkv_sum, qkv_held, swap_send.at[1], swap_recv.at[1], own_sem.at[5])
    if aligned:
        out_out.finish()
    else:
        out_out.wait()
    down_out.finish()
    up_swap.finish()
    qkv_swap.finish()


def backward(
    grps,
    aligned,
    facts,
    gains,
    tables,
    residual,
    own_tokens,
    own_grad,
    grad_both,
    up_local,
    down_share,
    second_norm,
    first_norm,
    out_local,
    qkv_local,
    heads,
    hidden,
    down_local,
):
    rows = residual.shape[0]
    count, full_rows, head_width = heads[0].shape
    seqs = full_rows // rows
    ranks = seqs * QUAD
    both = grad_both.shape[2]
    down_shape = down_share.shape[1:]
    quad_rows = D // (seqs * grps)
    shard = quad_rows // QUAD
    out_rows = head_width // grps if aligned else HEAD_DIM
    triple = 3 * head_width
    out_count = head_width // out_rows
    hbm = pl.BlockSpec(memory_space=pl.ANY)
    vmem = pl.BlockSpec(memory_space=pltpu.VMEM)
    shape = jax.ShapeDtypeStruct
    dma = pltpu.SemaphoreType.DMA
    return pl.pallas_call(
        lambda *refs: back_kernel(grps, aligned, *refs),
        in_specs=[vmem] * 4 + [hbm] * 16,
        out_specs=[vmem] * 3 + [hbm] * 10,
        out_shape=[
            shape((rows, D), f32),
            shape((rows, D), bf16),
            shape((8, D), f32),
            shape((grps, *down_shape), bf16),
            shape((out_count, out_rows, D), bf16),
            shape((ranks, shard, both), bf16),
            shape((ranks, shard, triple), bf16),
            shape((grps, seqs, quad_rows, both), bf16),
            shape((grps, seqs, quad_rows, triple), bf16),
            shape(down_shape, bf16),
            shape((seqs, quad_rows, both), bf16),
            shape((out_rows, D), bf16),
            shape((seqs, quad_rows, triple), bf16),
        ],
        scratch_shapes=[
            pltpu.VMEM((count, full_rows, both), bf16),
            pltpu.VMEM((D, both), bf16),
            pltpu.VMEM((count, full_rows, D), bf16),
            pltpu.VMEM((head_width, D), bf16),
            pltpu.VMEM((D, triple), bf16),
            pltpu.VMEM((ranks, rows, D), bf16),
            pltpu.VMEM((4, rows, D), bf16),
            pltpu.VMEM((3, rows, D), bf16),
            pltpu.VMEM((ranks, rows, D), bf16),
            pltpu.VMEM((count, full_rows, triple), bf16),
            pltpu.VMEM((grps, *down_shape), bf16),
            pltpu.VMEM((grps, seqs, quad_rows, both), bf16),
            pltpu.VMEM((out_count, out_rows, D), bf16),
            pltpu.VMEM((grps, seqs, quad_rows, triple), bf16),
            pltpu.VMEM((ranks, shard, both), bf16),
            pltpu.VMEM((ranks, shard, triple), bf16),
            pltpu.VMEM(down_shape, bf16),
            pltpu.VMEM((out_rows, D), bf16),
            pltpu.VMEM((seqs, quad_rows, both), bf16),
            pltpu.VMEM((8, D), f32),
            pltpu.VMEM((7, 8, D), f32),
            pltpu.VMEM((grps, 8, D), f32),
            pltpu.VMEM((rows, D), f32),
            pltpu.VMEM((rows, D), bf16),
            pltpu.VMEM((rows, D), bf16),
            dma((17,)),
            dma((4,)),
            dma((4,)),
            dma((3,)),
            dma((3,)),
            dma((7,)),
            dma((7,)),
            dma((4, grps)),
            dma((4, grps)),
            dma((2, 7)),
            dma((2, 7)),
            dma((7 + grps,)),
            dma((7 + grps,)),
            dma((6,)),
            pltpu.SemaphoreType.REGULAR,
            pltpu.SemaphoreType.REGULAR,
        ],
        compiler_params=pltpu.CompilerParams(
            collective_id=0, has_side_effects=True, vmem_limit_bytes=VMEM_LIMIT
        ),
        cost_estimate=pl.CostEstimate(
            flops=30 * 10**9, bytes_accessed=60 * 2**20, transcendentals=2 * 10**6
        ),
        name="backward",
    )(
        facts,
        gains,
        *tables,
        residual,
        own_tokens,
        own_grad,
        grad_both,
        up_local,
        down_share,
        second_norm,
        first_norm,
        out_local,
        qkv_local,
        *heads,
        hidden,
        down_local,
    )


CHUNK = 1024


class FromOwners:
    def __init__(self, place, source, landed, landing, send, recv, own):
        self.place, self.source, self.send, self.recv = place, source, send, recv
        self.slot = lambda j: landing(landed, j)
        self.own = pltpu.make_async_copy(source, self.slot(place.g), own)
        self.line = place.grps == 4

    def copy(self, source, slot, sem, recv, target):
        place = self.place
        return remote(
            source, self.slot(slot), self.send.at[sem], self.recv.at[recv], (place.s, target, place.r, place.c)
        )

    def passed(self, g, j, target):
        source = self.source if j == g else self.slot(j)
        return self.copy(source, j, j + (4 if target > g else 0), j, target)

    def arrived(self, j):
        self.copy(self.source, j, j, j, j).wait_recv()

    def on_line(self, steps):
        for g in range(4):
            if steps[g]:

                @pl.when(self.place.g == g)
                def _():
                    for awaited, j, target in steps[g]:
                        if awaited is not None:
                            self.arrived(awaited)
                        self.passed(g, j, target).start()

    FIRST = (
        ((None, 0, 1),),
        ((None, 1, 0), (None, 1, 2)),
        ((None, 2, 3), (None, 2, 1)),
        ((None, 3, 2),),
    )
    SECOND = ((), ((2, 2, 0), (0, 0, 2)), ((1, 1, 3), (3, 3, 1)), ())
    THIRD = ((), ((3, 3, 0),), ((0, 0, 3),), ())

    def start(self):
        place = self.place
        self.own.start()
        if self.line:
            self.on_line(self.FIRST)
        else:
            self.copies = [
                self.copy(self.source, place.g, dz, dz, (place.g + dz) % place.grps)
                for dz in range(1, place.grps)
            ]
            for copy in self.copies:
                copy.start()

    def second(self):
        if self.line:
            self.on_line(self.SECOND)

    def third(self):
        if self.line:
            self.on_line(self.THIRD)

    def finish(self):
        self.own.wait()
        if self.line:
            for g in range(4):

                @pl.when(self.place.g == g)
                def _():
                    for j in range(4):
                        if g in (0, 3) and j != g:
                            self.arrived(j)
                    for steps in (self.FIRST, self.SECOND, self.THIRD):
                        for _, j, target in steps[g]:
                            self.passed(g, j, target).wait_send()

        else:
            for copy in self.copies:
                copy.wait()


def shares_from(seq, values, weight, part):
    rows = part.shape[1]

    @pl.loop(0, part.shape[2] // LANES)
    def _(n):
        product = dot(values[seq], weight[:, lanes_of(n)])
        part[2 * seq, :, lanes_of(n)] = product[:rows].astype(bf16)
        part[2 * seq + 1, :, lanes_of(n)] = product[rows:].astype(bf16)


def times_slices(values, weight, lanes):
    piece = weight[:, :, :, :, lanes]
    return dot(values, piece.reshape(values.shape[1], piece.shape[4]))


def both_blocks(blocks, seq):
    return jnp.concatenate([blocks[2 * seq].astype(f32), blocks[2 * seq + 1].astype(f32)], axis=0)


def forward_kernel(
    grps,
    aligned,
    cosine,
    sine,
    own_facts,
    tokens_h,
    own_grad_h,
    qkv_own,
    up_own,
    out_own,
    down_own,
    residual,
    gains,
    facts,
    first_h,
    q_h,
    k_h,
    v_h,
    o_h,
    second_h,
    down_share_h,
    hidden_h,
    dgu_h,
    qkv_landed,
    up_landed,
    out_landed,
    down_landed,
    blocks,
    grad_blocks,
    norm,
    grad_seq,
    qkv_rank,
    up_rank,
    qkv,
    up,
    out_w,
    down,
    heads,
    part,
    near,
    far,
    both,
    hidden,
    dgu,
    all_facts,
    early,
    load,
    store,
    swap_send,
    swap_recv,
    near_send,
    near_recv,
    far_send,
    far_recv,
    all_send,
    all_recv,
    z_send,
    z_recv,
    fact_send,
    fact_recv,
    own_sem,
):
    place = Place(grps)
    count, full_rows, _ = norm.shape
    rows = residual.shape[0]
    head_width = heads.shape[3]
    mine, rank = place.seat(), place.rank()

    def fetch(src, dst, n):
        copy = pltpu.make_async_copy(src, dst, load.at[n])
        copy.start()
        return copy

    def keep(src, dst, n):
        copy = pltpu.make_async_copy(src, dst, store.at[n])
        copy.start()
        return copy

    shard = qkv_own.shape[0]
    units = down.shape[0] // grps
    seqs = qkv_landed.shape[0]
    slots = iter(range(20))

    def fetch_chunks(src):
        pieces = []
        for top in range(0, src.shape[0], shard):
            for left in range(0, src.shape[1], CHUNK):
                slot = next(slots)
                space = both.at[slot // 5, (slot % 5) * shard : (slot % 5 + 1) * shard]
                copy = pltpu.make_async_copy(
                    src.at[top : top + shard, left : left + CHUNK], space, early.at[slot]
                )
                copy.start()
                pieces.append((copy, space))
        return pieces

    def dealt(pieces, weight, lanes, parts):
        count = CHUNK // (QUAD * lanes)
        width = count * lanes
        each = len(pieces) // (parts * seqs)
        for n, (copy, space) in enumerate(pieces):
            copy.wait()
            values = space[...]
            seq = n // each % seqs
            first = (n // (each * seqs) * each + n % each) * width
            for q in range(QUAD):
                taken = [
                    values[:, (k * QUAD + q) * lanes : (k * QUAD + q + 1) * lanes] for k in range(count)
                ]
                weight[0, seq, q, :, first : first + width] = jnp.concatenate(taken, axis=1).astype(bf16)

    facts[rank] = own_facts[...]
    if aligned:
        out_pieces = fetch_chunks(out_own)
    qkv_pieces = fetch_chunks(qkv_own)
    up_pieces = fetch_chunks(up_own)
    down_pieces = fetch_chunks(down_own)
    own_blocks = [fetch(tokens_h, blocks.at[mine], 0), fetch(own_grad_h, grad_blocks.at[mine], 1)]

    def plane_rows(ref, j):
        return ref.at[:, j]

    def own_rows(ref, j):
        size = ref.shape[0] // grps
        return ref.at[pl.ds(pl.multiple_of(j * size, size), size)]

    def from_owners(n, source, landed, landing):
        return FromOwners(place, source, landed, landing, z_send.at[n], z_recv.at[n], own_sem.at[n])

    def stacked(pieces, weight):
        across = weight.shape[1] // CHUNK
        for n, (copy, space) in enumerate(pieces):
            copy.wait()
            top, left = n // across * shard, n % across * CHUNK
            weight[top : top + shard, left : left + CHUNK] = space[...].astype(bf16)

    down_z = from_owners(3, down.at[:units], down_landed, own_rows)
    if aligned:
        stacked(out_pieces, out_w)
        out_z = from_owners(2, out_w.at[:shard], out_landed, own_rows)
    place.greet()
    if aligned:
        out_z.start()
    dealt(qkv_pieces, qkv, HEAD_DIM, 3)
    qkv_swap = Exchange(place, qkv, qkv_rank, swap_send.at[0], swap_recv.at[0], own_sem.at[4])
    fact_copies = []
    for n, relation in enumerate(RELATIONS):
        copy = remote(own_facts, facts.at[rank], fact_send.at[n], fact_recv.at[n], place.peer(relation))
        copy.start()
        fact_copies.append(copy)
    if aligned:
        out_z.second()
    dealt(up_pieces, up, units, 2)
    stacked(down_pieces, down)
    for copy in own_blocks:
        copy.wait()
    if aligned:
        out_z.third()
    qkv_swap.finish()
    qkv_z = from_owners(0, qkv_rank, qkv_landed, plane_rows)
    up_z = from_owners(1, up_rank, up_landed, plane_rows)
    qkv_z.start()
    token_gather = PlaneGather(place, blocks, all_send.at[0], all_recv.at[0])
    token_gather.start()
    for copy in fact_copies:
        copy.wait()
    all_facts[place.g] = facts[...]
    fact_copies = []
    for dz in range(1, grps):
        copy = remote(
            facts,
            all_facts.at[place.g],
            fact_send.at[7 + dz],
            fact_recv.at[7 + dz],
            place.plane(dz),
        )
        copy.start()
        fact_copies.append(copy)
    for copy in fact_copies:
        copy.wait()
    width = D // (seqs * grps * QUAD)
    for n in range(seqs * grps):
        pieces = [all_facts[n % grps, (n // grps) * QUAD + q, :, :width] for q in range(QUAD)]
        gains[:, n * QUAD * width : (n + 1) * QUAD * width] = jnp.concatenate(pieces, axis=1)
    token_gather.forward(0)
    token_gather.forward(1)
    up_swap = Exchange(place, up, up_rank, swap_send.at[1], swap_recv.at[1], own_sem.at[5])
    qkv_z.second()
    token_gather.forward(2)
    token_gather.arrive(3)
    token_gather.copies[3].wait_recv()
    token_gather.copies[4].wait_recv()
    token_gather.finish()

    @pl.loop(0, count)
    def _(seq):
        values = both_blocks(blocks, seq)
        scale = lax.rsqrt(jnp.mean(values * values, axis=-1, keepdims=True) + NORM_EPSILON)
        norm[seq] = (values * scale * gains[0:1, :]).astype(bf16)

    stores = [keep(norm, first_h, 0)]
    grad_gather = PlaneGather(place, grad_blocks, all_send.at[1], all_recv.at[1])
    grad_gather.start()
    qkv_z.third()
    up_swap.finish()
    qkv_z.finish()
    up_z.start()
    fetch(qkv_landed, qkv, 2).wait()

    lane = lax.broadcasted_iota(jnp.int32, (full_rows, head_width), 1)
    first_half = (lane % HEAD_DIM) < HEAD_DIM // 2

    if aligned:
        out_z.finish()
        fetch(out_landed, out_w, 3).wait()
    else:
        fetch(out_own, out_w, 3).wait()

    plane_sum = PlaneSum(place, part, near, far, (near_send, near_recv, far_send, far_recv))
    mixed = heads.at[3]
    for k in range(4):
        seq = plane_sum.sequence(k)
        for n in range(3):
            lanes = slice(n * head_width, (n + 1) * head_width)
            values = times_slices(norm[seq], qkv, lanes)
            if n < 2:
                values = values * cosine[...] + swap_halves(values, first_half) * sine[...]
            heads[n, seq] = values.astype(bf16)
        heads[3, seq] = attention(facts[seq, 2:3, 0:1], heads[0, seq], heads[1, seq], heads[2, seq])
        shares_from(seq, mixed, out_w, part)
        if k % 2 == 0:
            plane_sum.near(k)
        else:
            plane_sum.far(k)
        if k == 0:
            grad_gather.forward(0)
            grad_gather.forward(1)
    grad_gather.forward(2)
    grad_gather.arrive(3)
    grad_gather.copies[3].wait_recv()
    grad_gather.copies[4].wait_recv()
    grad_gather.finish()
    stores += [keep(heads.at[n], ref, 1 + n) for n, ref in enumerate((q_h, k_h, v_h, o_h))]
    up_z.second()

    @pl.loop(0, count)
    def _(seq):
        grad_seq[seq] = both_blocks(grad_blocks, seq).astype(bf16)

    fetch(tokens_h, grad_blocks.at[mine], 4).wait()
    plane_sum.finish()
    squares = jnp.zeros((rows, 1), f32)
    for n in range(D // LANES):
        lanes = slice(n * LANES, (n + 1) * LANES)
        values = grad_blocks[mine, :, lanes].astype(f32) + plane_sum.chunk(lanes)
        residual[:, lanes] = values
        squares += jnp.sum(values * values, axis=-1, keepdims=True)
    scale = lax.rsqrt(squares / D + NORM_EPSILON)
    for n in range(D // LANES):
        lanes = slice(n * LANES, (n + 1) * LANES)
        blocks[mine, :, lanes] = (residual[:, lanes] * scale * gains[1:2, lanes]).astype(bf16)
    norm_gather = PlaneGather(place, blocks, all_send.at[2], all_recv.at[2])
    norm_gather.start()
    up_z.third()
    stores[0].wait()
    half = hidden.shape[2]
    for k in range(4):
        norm_gather.arrive(k, forwarded=k == 1)
        seq = norm_gather.sequence(k)
        norm[seq] = both_blocks(blocks, seq).astype(bf16)
        if k == 0:
            norm_gather.forward(1)
            up_z.finish()
            down_z.start()
            fetch(up_landed, up, 5).wait()
        elif k == 2:
            down_z.second()
        gate = times_slices(norm[seq], up, slice(0, half))
        above = times_slices(norm[seq], up, slice(half, 2 * half))
        both[seq, :, :half] = gate
        both[seq, :, half:] = above
        hidden[seq] = (gate * jax.nn.sigmoid(gate) * above).astype(bf16)
    norm_gather.finish()
    stores[0] = keep(norm, second_h, 5)
    down_z.third()
    stores.append(keep(hidden, hidden_h, 7))
    tall = min(256, half)
    slab = part.shape[1] // 128 * 128

    @pl.loop(0, half // tall)
    def _(b):
        for side in range(2):
            lanes = slice(side * D // 2, (side + 1) * D // 2)
            product = over_tokens(hidden, lanes_of(b, tall), grad_seq, lanes).astype(bf16)
            for p in range(tall // slab):
                part[b * (tall // slab) + p, :slab, lanes] = product[p * slab : (p + 1) * slab]

    stores.append(keep(part.at[: half // slab, :slab], down_share_h, 6))
    down_z.finish()
    fetch(down_landed, down, 6).wait()

    @pl.loop(0, count)
    def _(seq):
        grads = dot(grad_seq[seq], down[...], 1, 1)
        gate, above = both[seq, :, :half], both[seq, :, half:]
        sigmoid = jax.nn.sigmoid(gate)
        dgu[seq, :, :half] = (grads * above * sigmoid * (1.0 + gate * (1.0 - sigmoid))).astype(bf16)
        dgu[seq, :, half:] = (grads * (gate * sigmoid)).astype(bf16)

    stores.append(keep(dgu, dgu_h, 8))
    for copy in stores:
        copy.wait()


def forward(grps, aligned, tables, own_facts, tokens, own_grad, qkv_own, up_own, out_own, down_own):
    rows = tokens.shape[0]
    shard = qkv_own.shape[0]
    seqs = D // (shard * grps * QUAD)
    ranks = seqs * QUAD
    triple, both = qkv_own.shape[1] // ranks, up_own.shape[1] // ranks
    count, full_rows, head_width = QUAD, rows * seqs, triple // 3
    half = both // 2
    hbm = pl.BlockSpec(memory_space=pl.ANY)
    vmem = pl.BlockSpec(memory_space=pltpu.VMEM)
    shape = jax.ShapeDtypeStruct
    dma = pltpu.SemaphoreType.DMA
    by_heads = shape((count, full_rows, head_width), bf16)
    return pl.pallas_call(
        lambda *refs: forward_kernel(grps, aligned, *refs),
        in_specs=[vmem] * 3 + [hbm] * 6,
        out_specs=[vmem] * 3 + [hbm] * 13,
        out_shape=[
            shape((rows, D), f32),
            shape((8, D), f32),
            shape((ranks, 8, 128), f32),
            shape((count, full_rows, D), bf16),
            by_heads,
            by_heads,
            by_heads,
            by_heads,
            shape((count, full_rows, D), bf16),
            shape((half // 128, 128, D), bf16),
            shape((count, full_rows, half), bf16),
            shape((count, full_rows, both), bf16),
            shape((seqs, grps, QUAD, shard, triple), bf16),
            shape((seqs, grps, QUAD, shard, both), bf16),
            shape((head_width, D), bf16),
            shape((half, D), bf16),
        ],
        scratch_shapes=[
            pltpu.VMEM((ranks, rows, D), bf16),
            pltpu.VMEM((ranks, rows, D), bf16),
            pltpu.VMEM((count, full_rows, D), bf16),
            pltpu.VMEM((count, full_rows, D), bf16),
            pltpu.VMEM((seqs, QUAD, shard, triple), bf16),
            pltpu.VMEM((seqs, QUAD, shard, both), bf16),
            pltpu.VMEM((seqs, grps, QUAD, shard, triple), bf16),
            pltpu.VMEM((seqs, grps, QUAD, shard, both), bf16),
            pltpu.VMEM((head_width, D), bf16),
            pltpu.VMEM((half, D), bf16),
            pltpu.VMEM((4, count, full_rows, head_width), bf16),
            pltpu.VMEM((ranks, rows, D), bf16),
            pltpu.VMEM((4, rows, D), bf16),
            pltpu.VMEM((3, rows, D), bf16),
            pltpu.VMEM((count, full_rows, both), f32),
            pltpu.VMEM((count, full_rows, half), bf16),
            pltpu.VMEM((count, full_rows, both), bf16),
            pltpu.VMEM((grps, ranks, 8, 128), f32),
            dma((20,)),
            dma((7,)),
            dma((9,)),
            dma((2, 7)),
            dma((2, 7)),
            dma((4,)),
            dma((4,)),
            dma((3,)),
            dma((3,)),
            dma((3, 7)),
            dma((3, 7)),
            dma((4, 2 * grps)),
            dma((4, grps)),
            dma((7 + grps,)),
            dma((7 + grps,)),
            dma((6,)),
        ],
        compiler_params=pltpu.CompilerParams(
            collective_id=1, has_side_effects=True, vmem_limit_bytes=VMEM_LIMIT
        ),
        cost_estimate=pl.CostEstimate(
            flops=20 * 10**9, bytes_accessed=60 * 2**20, transcendentals=4 * 10**6
        ),
        name="forward",
    )(*tables, own_facts, tokens, own_grad, qkv_own, up_own, out_own, down_own)


DEPTH = 4


def adam_kernel(grps, down_planes, out_planes, up_ranks, qkv_ranks, gains_sum, gains, gains_m, gains_v, *refs):
    states, outs = refs[:12], refs[12:28]
    gains_outs = refs[28:31]
    state, planes, ranks, fresh, copied, in_sem, out_sem = refs[31:]
    plane = lax.axis_index("grp")
    rows = state.shape[2]
    units = CHUNK // QUAD
    pieces = []
    for n, (name, rate) in enumerate(
        (("down", FF ** (-0.5)), ("out", (D // 128) ** (-0.5)), ("up", D ** (-0.5)), ("qkv", D ** (-0.5)))
    ):
        arrays = states[3 * n : 3 * n + 3]
        for top in range(0, arrays[0].shape[0], rows):
            for left in range(0, arrays[0].shape[1], CHUNK):
                pieces.append((name, rate, n, top, left))

    def grad_source(name, top, left, slot):
        if name in ("down", "out"):
            source = down_planes if name == "down" else out_planes
            return (
                source.at[:, top : top + rows, left : left + CHUNK],
                planes.at[slot, : source.shape[0]],
            )
        source, parts = (up_ranks, 2) if name == "up" else (qkv_ranks, 3)
        width = source.shape[2] // parts
        per_seq = width // units
        n = left // CHUNK
        seqs = source.shape[0] // QUAD
        seq = n // per_seq % seqs
        first = n // (per_seq * seqs) * width + n % per_seq * units
        return source.at[seq * QUAD : (seq + 1) * QUAD, :, first : first + units], ranks.at[slot]

    def reads(k):
        name, _, n, top, left = pieces[k]
        slot = k % DEPTH
        window = (slice(top, top + rows), slice(left, left + CHUNK))
        copies = [
            pltpu.make_async_copy(states[3 * n + i].at[window], state.at[slot, i], in_sem.at[slot, i])
            for i in range(3)
        ]
        source, space = grad_source(name, top, left, slot)
        return copies + [pltpu.make_async_copy(source, space, in_sem.at[slot, 3])]

    def writes(k):
        _, _, n, top, left = pieces[k]
        slot = k % DEPTH
        window = (slice(top, top + rows), slice(left, left + CHUNK))
        copies = [
            pltpu.make_async_copy(fresh.at[slot, i], outs[4 * n + i].at[window], out_sem.at[slot, i])
            for i in range(3)
        ]
        return copies + [
            pltpu.make_async_copy(copied.at[slot], outs[4 * n + 3].at[window], out_sem.at[slot, 3])
        ]

    def gradient(name, slot):
        if name in ("down", "out"):
            source = down_planes if name == "down" else out_planes
            total = jnp.zeros((rows, CHUNK), f32)
            for j in range(source.shape[0]):
                held = planes[slot, j].astype(f32)
                if grps == 4 and j in (0, 3):
                    held = jnp.where(plane != 3 - j, held, 0.0)
                total += held
            return total
        lanes = down_planes.shape[1] if name == "up" else HEAD_DIM
        values = [ranks[slot, q].astype(f32) for q in range(QUAD)]
        return jnp.concatenate(
            [
                values[q][:, n * lanes : (n + 1) * lanes]
                for n in range(units // lanes)
                for q in range(QUAD)
            ],
            axis=1,
        )

    for k in range(DEPTH - 1):
        for copy in reads(k):
            copy.start()
    results = adam_update(gains[...], gains_m[...], gains_v[...], gains_sum[...], 0.3)
    for out, result in zip(gains_outs, results):
        out[...] = result
    for k, (name, rate, _, _, _) in enumerate(pieces):
        slot = k % DEPTH
        if k + DEPTH - 1 < len(pieces):
            for copy in reads(k + DEPTH - 1):
                copy.start()
        for copy in reads(k):
            copy.wait()
        if k >= DEPTH:
            for copy in writes(k - DEPTH):
                copy.wait()
        results = adam_update(state[slot, 0], state[slot, 1], state[slot, 2], gradient(name, slot), rate)
        for i in range(3):
            fresh[slot, i] = results[i]
        copied[slot] = results[0].astype(bf16)
        for copy in writes(k):
            copy.start()
    for k in range(len(pieces) - DEPTH, len(pieces)):
        for copy in writes(k):
            copy.wait()


def adam(grps, down_planes, out_planes, up_ranks, qkv_ranks, gains_sum, gains, states):
    rows = up_ranks.shape[1]
    hbm = pl.BlockSpec(memory_space=pl.ANY)
    vmem = pl.BlockSpec(memory_space=pltpu.VMEM)
    shapes = []
    for array in states[::3]:
        shapes += [jax.ShapeDtypeStruct(array.shape, f32)] * 3
        shapes.append(jax.ShapeDtypeStruct(array.shape, bf16))
    shapes += [jax.ShapeDtypeStruct(gains[0].shape, f32)] * 3
    size = sum(array.size for array in states) // 3
    outs = pl.pallas_call(
        lambda *refs: adam_kernel(grps, *refs),
        in_specs=[hbm] * 4 + [vmem] * 4 + [hbm] * 12,
        out_specs=[hbm] * 16 + [vmem] * 3,
        out_shape=shapes,
        scratch_shapes=[
            pltpu.VMEM((DEPTH, 3, rows, CHUNK), f32),
            pltpu.VMEM((DEPTH, grps, rows, CHUNK), bf16),
            pltpu.VMEM((DEPTH, QUAD, rows, CHUNK // QUAD), bf16),
            pltpu.VMEM((DEPTH, 3, rows, CHUNK), f32),
            pltpu.VMEM((DEPTH, rows, CHUNK), bf16),
            pltpu.SemaphoreType.DMA((DEPTH, 4)),
            pltpu.SemaphoreType.DMA((DEPTH, 4)),
        ],
        compiler_params=pltpu.CompilerParams(vmem_limit_bytes=VMEM_LIMIT),
        cost_estimate=pl.CostEstimate(flops=size * 16, bytes_accessed=size * 28, transcendentals=size),
        name="adam",
    )(down_planes, out_planes, up_ranks, qkv_ranks, gains_sum, *gains, *states)
    return outs[:4], outs[4:8], outs[8:12], outs[12:16], outs[16:]


def on_device(
    tokens,
    cotangent,
    lengths,
    qkv_weight,
    qkv_moment,
    qkv_square,
    out_weight,
    out_moment,
    out_square,
    up_weight,
    up_moment,
    up_square,
    down_weight,
    down_moment,
    down_square,
    norm_gains,
    gains_moment,
    gains_square,
):
    seqs = lax.axis_size("seq")
    grps = lax.axis_size("grp")
    ranks = seqs * QUAD
    own_rows = tokens.shape[1]
    full_rows = own_rows * seqs
    all_rows = full_rows * QUAD
    heads_local = HEADS // ranks
    head_width = heads_local * HEAD_DIM
    units = down_weight.shape[0]
    aligned = out_weight.shape[0] == HEAD_DIM
    tables = rotate_table(full_rows, heads_local)

    positions = lax.axis_index("seq") * own_rows + jnp.arange(own_rows, dtype=jnp.int32)
    own_grad = jnp.where((positions < lengths[0])[:, None], cotangent[0], 0)
    own_gains = norm_gains.shape[1]
    own_facts = jnp.zeros((8, 128), f32)
    own_facts = own_facts.at[:2, :own_gains].set(norm_gains.astype(bf16).astype(f32))
    own_facts = own_facts.at[2].set(lengths[0].astype(f32))

    out_own = out_weight
    if not aligned:
        out_all = lax.all_gather(out_weight.astype(bf16), EVERY, axis=0, tiled=True)
        out_all = out_all.reshape(seqs, heads_local, QUAD, HEAD_DIM, D)
        seat = lax.axis_index("row") * 2 + lax.axis_index("core")
        out_own = lax.dynamic_index_in_dim(
            lax.dynamic_index_in_dim(out_all, lax.axis_index("seq"), 0, False), seat, 1, False
        ).reshape(head_width, D)
    (
        residual,
        gains,
        facts,
        first_norm,
        queries,
        key_vectors,
        value_vectors,
        attended,
        second_norm,
        down_share,
        hidden,
        grad_both,
        qkv_local,
        up_local,
        out_local,
        down_local,
    ) = forward(
        grps,
        aligned,
        tables,
        own_facts,
        tokens[0],
        own_grad,
        qkv_weight,
        up_weight,
        out_own,
        down_weight,
    )
    if not aligned:
        out_local = out_own
    (
        input_grad,
        block_output,
        gains_total,
        down_planes,
        out_planes,
        up_ranks,
        qkv_ranks,
        *_,
    ) = backward(
        grps,
        aligned,
        facts,
        gains,
        tables,
        residual,
        tokens[0],
        own_grad,
        grad_both,
        up_local.reshape(D, -1),
        down_share.reshape(grps, units, D),
        second_norm,
        first_norm,
        out_local,
        qkv_local.reshape(D, -1),
        (queries, key_vectors, value_vectors, attended),
        hidden,
        down_local,
    )
    if aligned:
        out_sum = out_planes
    else:
        placed_term = jnp.zeros((seqs, QUAD, heads_local, HEAD_DIM, D), bf16)
        placed_term = lax.dynamic_update_slice(
            placed_term,
            out_planes.reshape(1, 1, heads_local, HEAD_DIM, D),
            (lax.axis_index("seq"), seat, 0, 0, 0),
        )
        out_sum = lax.psum_scatter(
            placed_term.transpose(0, 2, 1, 3, 4).reshape(D, D),
            EVERY,
            scatter_dimension=0,
            tiled=True,
        )[None]
    device = ((lax.axis_index("seq") * grps + lax.axis_index("grp")) * 2 + lax.axis_index("row")) * 2
    gains_sum = lax.dynamic_slice(
        gains_total, (0, (device + lax.axis_index("core")) * own_gains), (2, own_gains)
    )
    down_new, out_new, up_new, qkv_new, gains_new = adam(
        grps,
        down_planes,
        out_sum,
        up_ranks,
        qkv_ranks,
        gains_sum,
        (norm_gains, gains_moment, gains_square),
        (
            down_weight,
            down_moment,
            down_square,
            out_weight,
            out_moment,
            out_square,
            up_weight,
            up_moment,
            up_square,
            qkv_weight,
            qkv_moment,
            qkv_square,
        ),
    )
    return (
        block_output[None],
        input_grad[None],
        *qkv_new,
        *out_new,
        *up_new,
        *down_new,
        *gains_new,
    )


def solution(mesh):
    seqs, rest = mesh.shape["seq"], mesh.shape["fsdp"]
    planes = Mesh(
        mesh.devices.reshape(seqs, rest // QUAD, 2, 2), ("seq", "grp", "row", "core")
    )
    rows = P(("grp", "row", "core"), "seq", None)
    shards = P(EVERY, None)
    gains = P(None, EVERY)
    return jax.shard_map(
        on_device,
        mesh=planes,
        in_specs=(rows, rows, P(("grp", "row", "core"))) + (shards,) * 12 + (gains,) * 3,
        out_specs=(rows, rows) + (shards,) * 16 + (gains,) * 3,
        check_vma=False,
    )
```

```python
import math

import jax
import jax.numpy as jnp
from jax import lax
from jax.experimental import pallas as pl
from jax.experimental.pallas import tpu as pltpu
from jax.sharding import Mesh, PartitionSpec as P

D = 2048
HEADS = 32
HEAD_DIM = 64
FF = 4096
WINDOW = 128
STEP = 5


NORM_EPSILON = 1e-05
MOMENT_DECAY = 0.5
WEIGHT_DECAY = 0.1
ADAM_EPSILON = 1e-08

SEATS = ("row", "core", "seq")
RANKS = ("seq", "row", "core")
EVERY = ("seq", "grp", "row", "core")
QUAD = 4
VMEM_LIMIT = 63 * 2**20

bf16 = jnp.bfloat16
f32 = jnp.float32


def rotate_table(length, copies):
    halves = HEAD_DIM // 2
    freqs = jnp.exp(-math.log(10000.0) * 2.0 * jnp.arange(halves).astype(f32) / HEAD_DIM)
    angles = jnp.arange(length, dtype=jnp.int32).astype(f32)[:, None] * freqs[None, :]
    cosine, sine = jnp.cos(angles), jnp.sin(angles)
    return (
        jnp.tile(jnp.concatenate([cosine, cosine], axis=1), (1, copies)),
        jnp.tile(jnp.concatenate([-sine, sine], axis=1), (1, copies)),
    )


def adam_update(weight, moment, square, gradient, step_rate):
    moment_new = MOMENT_DECAY * moment + (1.0 - MOMENT_DECAY) * gradient
    square_new = MOMENT_DECAY * square + (1.0 - MOMENT_DECAY) * gradient * gradient
    correction = 1.0 - MOMENT_DECAY**STEP
    unbias = 1.0 / correction
    update = (moment_new * unbias) / (jnp.sqrt(square_new * unbias) + ADAM_EPSILON)
    return (weight - step_rate * (update + WEIGHT_DECAY * weight), moment_new, square_new)


def dot(a, b, lhs=1, rhs=0):
    return lax.dot_general(a, b, (((lhs,), (rhs,)), ((), ())), preferred_element_type=f32)


def swap_halves(values, first):
    width = values.shape[1]
    half = HEAD_DIM // 2
    return jnp.where(
        first, pltpu.roll(values, width - half, 1), pltpu.roll(values, half, 1)
    )


def allowed_mask(rows, length):
    row = lax.broadcasted_iota(jnp.int32, (rows, rows), 0)
    col = lax.broadcasted_iota(jnp.int32, (rows, rows), 1)
    return (col <= row) & (row - col < WINDOW) & (col.astype(f32) < length)


def head_lanes(rows, width, head):
    lane = lax.broadcasted_iota(jnp.int32, (rows, width), 1)
    return (lane // HEAD_DIM) == head


def softmax_rows(queries, key_vectors, allowed):
    scores = jnp.where(allowed, dot(queries, key_vectors, 1, 1) * (HEAD_DIM**-0.5), -1e30)
    shifted = jnp.exp(scores - jnp.max(scores, axis=-1, keepdims=True))
    return shifted / jnp.sum(shifted, axis=-1, keepdims=True)


def attention(length, queries, key_vectors, value_vectors):
    rows, width = queries.shape
    allowed = allowed_mask(rows, length)
    total = jnp.zeros((rows, width), f32)
    for head in range(width // HEAD_DIM):
        mine = head_lanes(rows, width, head)
        weights = softmax_rows(jnp.where(mine, queries, 0), key_vectors, allowed)
        total += dot(weights.astype(bf16), jnp.where(mine, value_vectors, 0))
    return total.astype(bf16)


def attention_grads(length, queries, key_vectors, value_vectors, grads):
    rows, width = queries.shape
    allowed = allowed_mask(rows, length)
    grad_q = jnp.zeros((rows, width), f32)
    grad_k = jnp.zeros((rows, width), f32)
    grad_v = jnp.zeros((rows, width), f32)
    for head in range(width // HEAD_DIM):
        mine = head_lanes(rows, width, head)
        q_head = jnp.where(mine, queries, 0)
        g_head = jnp.where(mine, grads, 0)
        weights = softmax_rows(q_head, key_vectors, allowed)
        grad_p = dot(g_head, value_vectors, 1, 1)
        delta = jnp.sum(weights * grad_p, axis=-1, keepdims=True)
        grad_s = jnp.where(allowed, weights * (grad_p - delta), 0.0).astype(bf16)
        grad_q += dot(grad_s, jnp.where(mine, key_vectors, 0))
        grad_k += dot(grad_s, q_head, 0, 0)
        grad_v += dot(weights.astype(bf16), g_head, 0, 0)
    return grad_q, grad_k, grad_v


MESH = pl.DeviceIdType.MESH
RELATIONS = tuple((a, b, d) for a in range(2) for b in range(2) for d in range(2))[1:]


class Place:
    def __init__(self, grps):
        self.grps = grps
        self.s = lax.axis_index("seq")
        self.g = lax.axis_index("grp")
        self.r = lax.axis_index("row")
        self.c = lax.axis_index("core")

    def peer(self, relation):
        ds, dr, dc = relation
        return ((self.s + ds) % 2, self.g, (self.r + dr) % 2, (self.c + dc) % 2)

    def plane(self, dz):
        return (self.s, (self.g + dz) % self.grps, self.r, self.c)

    def rank(self, relation=(0, 0, 0)):
        s, _, r, c = self.peer(relation)
        return (s * 2 + r) * 2 + c

    def seat(self, relation=(0, 0, 0)):
        s, _, r, c = self.peer(relation)
        return (r * 2 + c) * 2 + s

    def corner(self, relation=(0, 0, 0)):
        s, _, r, _ = self.peer(relation)
        return r * 2 + s

    def greet(self):
        barrier = pltpu.get_barrier_semaphore()
        for relation in RELATIONS:
            pl.semaphore_signal(barrier, inc=1, device_id=self.peer(relation), device_id_type=MESH)
        for dz in range(1, self.grps):
            pl.semaphore_signal(barrier, inc=1, device_id=self.plane(dz), device_id_type=MESH)
        pl.semaphore_wait(barrier, len(RELATIONS) + self.grps - 1)


SIBLING = (0, 0, 1)
ACROSS = ((1, 0, 0), (0, 1, 0), (1, 1, 0))


def remote(src, dst, send_sem, recv_sem, device):
    return pltpu.make_async_remote_copy(
        src_ref=src,
        dst_ref=dst,
        send_sem=send_sem,
        recv_sem=recv_sem,
        device_id=device,
        device_id_type=MESH,
    )


class PlaneSum:
    def __init__(self, place, part, near, far, sems):
        self.place, self.part, self.nears, self.fars = place, part, near, far
        self.near_send, self.near_recv, self.far_send, self.far_recv = sems
        self.first, self.second = [None] * 4, []

    def sequence(self, k):
        place = self.place
        row = (place.r + 1) % 2 if k < 2 else place.r
        return row * 2 + ((place.c + 1) % 2 if k % 2 == 0 else place.c)

    def near(self, k):
        for s in range(2):
            copy = remote(
                self.part.at[2 * self.sequence(k) + s],
                self.nears.at[k + s],
                self.near_send.at[k + s],
                self.near_recv.at[k + s],
                self.place.peer(SIBLING),
            )
            copy.start()
            self.first[k + s] = copy

    def far(self, k):
        place = self.place
        for s in range(2):
            self.first[k - 1 + s].wait()
            self.nears[k - 1 + s] = (
                self.part[2 * self.sequence(k) + s].astype(f32)
                + self.nears[k - 1 + s].astype(f32)
            ).astype(bf16)
        for d in (1, 2) if k == 1 else (0,):
            relation = ACROSS[d]
            copy = remote(
                self.nears.at[k - 1 + (place.s + relation[0]) % 2],
                self.fars.at[d],
                self.far_send.at[d],
                self.far_recv.at[d],
                place.peer(relation),
            )
            copy.start()
            self.second.append(copy)

    def finish(self):
        for copy in self.second:
            copy.wait()

    def chunk(self, lanes):
        total = self.nears[2 + self.place.s, :, lanes].astype(f32)
        for d in range(3):
            total += self.fars[d, :, lanes].astype(f32)
        return total


class PlaneGather:
    def __init__(self, place, blocks, send, recv):
        self.place, self.blocks, self.sends, self.recvs = place, blocks, send, recv
        self.copies = [None] * 7

    def send(self, block, sem, relation):
        copy = remote(
            self.blocks.at[block],
            self.blocks.at[block],
            self.sends.at[sem],
            self.recvs.at[sem],
            self.place.peer(relation),
        )
        copy.start()
        self.copies[sem] = copy

    def start(self):
        mine = self.place.seat()
        for d in range(2):
            self.send(mine, d, ACROSS[d])
        self.send(mine, 3, SIBLING)

    def forward(self, d):
        self.copies[d].wait_recv()
        self.send(self.place.seat(ACROSS[d]), 4 + d, SIBLING)
        if d == 0:
            self.send(self.place.seat(), 2, ACROSS[2])

    def sequence(self, k):
        place = self.place
        row = place.r if k < 2 else (place.r + 1) % 2
        return row * 2 + (place.c if k % 2 == 0 else (place.c + 1) % 2)

    def arrive(self, k, forwarded=False):
        if k == 0:
            self.forward(0)
        elif k == 1:
            if not forwarded:
                self.forward(1)
            self.copies[3].wait_recv()
            self.copies[4].wait_recv()
        elif k == 2:
            self.forward(2)
        else:
            self.copies[5].wait_recv()
            self.copies[6].wait_recv()

    def finish(self):
        for copy in self.copies:
            copy.wait_send()


class ToOwners:
    def __init__(self, place, shares, landed, met, stage, send, recv, own):
        self.place, self.shares, self.landed, self.met, self.stage = place, shares, landed, met, stage
        self.send, self.recv, self.own_sem = send, recv, own
        self.line = place.grps == 4
        self.own = pltpu.make_async_copy(shares.at[place.g], landed.at[place.g], own)

    def copy(self, block, landing, sem, recv, target):
        place = self.place
        return remote(
            self.shares.at[block],
            landing,
            self.send.at[sem],
            self.recv.at[recv],
            (place.s, target, place.r, place.c),
        )

    def direct(self, g):
        targets = ((2, 1), (2, 0), (1, 3), (1, 2))[g]
        return [self.copy(t, self.landed.at[g], t, g, t) for t in targets]

    def meeting(self, g):
        far, inner = (3, 1) if g == 0 else (0, 2)
        return self.copy(far, self.met, far, inner, inner)

    def joined(self, g):
        far = 3 if g == 1 else 0
        return self.copy(far, self.landed.at[g], far, g, far)

    def start(self, waits=False):
        place, self.waits = self.place, waits
        self.own.start()
        if self.line:
            for g in range(4):

                @pl.when(place.g == g)
                def _():
                    if g in (0, 3):
                        self.meeting(g).start()
                    if g in (1, 2) or not waits:
                        for copy in self.direct(g):
                            copy.start()

        else:
            self.copies = [
                self.copy((place.g + dz) % place.grps, self.landed.at[place.g], dz, dz, (place.g + dz) % place.grps)
                for dz in range(1, place.grps)
            ]
            for copy in self.copies:
                copy.start()
        return self

    def proceed(self):
        if self.line:
            for g in (0, 3):

                @pl.when(self.place.g == g)
                def _():
                    self.meeting(g).wait_send()
                    for copy in self.direct(g):
                        copy.start()

    def join(self):
        if not self.line:
            return
        for g in (1, 2):

            @pl.when(self.place.g == g)
            def _():
                outer, far = (0, 3) if g == 1 else (3, 0)
                self.copy(far, self.met, far, g, outer).wait_recv()
                copy = pltpu.make_async_copy(self.met, self.stage, self.own_sem)
                self.own.wait()
                copy.start()
                copy.wait()
                if len(self.stage.shape) == 2:
                    self.shares[far] = (
                        self.shares[far].astype(f32) + self.stage[...].astype(f32)
                    ).astype(bf16)
                else:
                    for n in range(self.stage.shape[0]):
                        self.shares[far, n] = (
                            self.shares[far, n].astype(f32) + self.stage[n].astype(f32)
                        ).astype(bf16)
                self.joined(g).start()

        for g in (0, 3):

            @pl.when(self.place.g == g)
            def _():
                self.own.wait()

    def sent(self):
        if not self.line:
            for copy in self.copies:
                copy.wait_send()
            return
        for g in range(4):

            @pl.when(self.place.g == g)
            def _():
                for copy in self.direct(g):
                    copy.wait_send()
                if g in (1, 2):
                    self.joined(g).wait_send()
                elif not self.waits:
                    self.meeting(g).wait_send()

    def received(self):
        if not self.line:
            self.own.wait()
            for copy in self.copies:
                copy.wait_recv()
            return
        for g in range(4):

            @pl.when(self.place.g == g)
            def _():
                for j in ((1, 2), (0, 2, 3), (0, 1, 3), (1, 2))[g]:
                    self.copy(g, self.landed.at[j], j, j, j).wait_recv()

    def finish(self):
        self.sent()
        self.received()

    def holds(self, j):
        g = self.place.g
        return (g % 3 != 0) | (j + g != 3) if self.line else True


class Exchange:
    def __init__(self, place, blocks, held, send, recv, own):
        mine = place.rank()
        kept = held.at[mine // QUAD, mine % QUAD] if len(held.shape) == 4 else held.at[mine]

        def block(t):
            return blocks.at[0, t // QUAD, t % QUAD] if len(blocks.shape) == 5 else blocks.at[t]

        self.copies = []
        for n, relation in enumerate(RELATIONS):
            copy = remote(
                block(place.rank(relation)),
                kept,
                send.at[n],
                recv.at[n],
                place.peer(relation),
            )
            copy.start()
            self.copies.append(copy)
        copy = pltpu.make_async_copy(block(mine), kept, own)
        copy.start()
        self.copies.append(copy)

    def finish(self):
        for copy in self.copies:
            copy.wait()


LANES = 512


def lanes_of(n, width=LANES):
    return pl.ds(pl.multiple_of(n * width, width), width)


def shares_of(seq, values, weight, part):
    rows = part.shape[1]

    @pl.loop(0, part.shape[2] // LANES)
    def _(n):
        product = dot(values[seq], weight[lanes_of(n)], 1, 1)
        part[2 * seq, :, lanes_of(n)] = product[:rows].astype(bf16)
        part[2 * seq + 1, :, lanes_of(n)] = product[rows:].astype(bf16)


def over_tokens(first, lanes, second, other):
    left, right = first[:, :, lanes], second[:, :, other]
    tokens = left.shape[0] * left.shape[1]
    return dot(left.reshape(tokens, left.shape[2]), right.reshape(tokens, right.shape[2]), 0, 0)


def row_shares(first, second, shares):
    grps, seqs, rows, _ = shares.shape
    width = 256
    pieces = width // rows

    @pl.loop(0, first.shape[2] // width)
    def _(b):
        product = over_tokens(first, lanes_of(b, width), second, slice(None)).astype(bf16)
        for p in range(pieces):
            index = b * pieces + p
            shares[index % grps, index // grps] = product[p * rows : (p + 1) * rows]


def summed_rows(landed, holds, blocks):
    seqs, rows = landed.shape[1], blocks.shape[1]
    for seq in range(seqs):
        for quad in range(QUAD):
            block = slice(quad * rows, (quad + 1) * rows)
            total = jnp.zeros((rows, landed.shape[3]), f32)
            for j in range(landed.shape[0]):
                total += jnp.where(holds(j), landed[j, seq, block].astype(f32), 0.0)
            blocks[seq * QUAD + quad] = total.astype(bf16)


def back_kernel(
    grps,
    aligned,
    facts,
    gains,
    cosine,
    sine,
    residual_h,
    own_tokens_h,
    own_grad_h,
    dgu_h,
    up_h,
    second_h,
    first_h,
    out_h,
    qkv_h,
    q_h,
    k_h,
    v_h,
    o_h,
    hidden_h,
    down_h,
    input_grad,
    block_output,
    gains_sum,
    out_landed,
    up_held,
    qkv_held,
    up_landed,
    qkv_landed,
    up_met,
    out_met,
    qkv_met,
    wide,
    up,
    acts,
    out_w,
    qkv,
    part,
    near,
    far,
    blocks,
    turned,
    up_share,
    out_share,
    qkv_share,
    up_sum,
    qkv_sum,
    stage_low,
    stage_wide,
    gain_part,
    gain_plane,
    gain_far,
    residual,
    own_tokens,
    own_grad,
    load,
    near_send,
    near_recv,
    far_send,
    far_recv,
    all_send,
    all_recv,
    z_send,
    z_recv,
    swap_send,
    swap_recv,
    gain_send,
    gain_recv,
    own_sem,
    near_free,
    far_free,
):
    place = Place(grps)
    rows = residual.shape[0]
    gain_part[...] = jnp.zeros_like(gain_part)
    count, full_rows, head_width = q_h.shape

    def fetch(src, dst, n):
        copy = pltpu.make_async_copy(src, dst, load.at[n])
        copy.start()
        return copy

    loads = [fetch(dgu_h, wide, 0), fetch(up_h, up, 1), fetch(second_h, acts, 3)]
    weights = [fetch(out_h, out_w, 5), fetch(qkv_h, qkv, 6)]
    small = [
        fetch(src, dst, 14 + n)
        for n, (src, dst) in enumerate(
            ((residual_h, residual), (own_grad_h, own_grad), (own_tokens_h, own_tokens))
        )
    ]
    place.greet()
    for copy in loads[:2]:
        copy.wait()

    sums = (near_send, near_recv, far_send, far_recv)
    def to_owners(n, shares, landed, met, stage, waits=False):
        return ToOwners(
            place, shares, landed, met, stage, z_send.at[n], z_recv.at[n], own_sem.at[n]
        ).start(waits)

    def summed_over_plane(values, weight):
        total = PlaneSum(place, part, near, far, sums)
        for k in range(4):
            shares_of(total.sequence(k), values, weight, part)
            if k % 2 == 0:
                total.near(k)
            else:
                total.far(k)
        return total

    second_sum = summed_over_plane(wide, up)
    loads[2].wait()
    row_shares(acts, wide, up_share)
    up_out = to_owners(1, up_share, up_landed, up_met, stage_wide, True)
    fetch_first = fetch(first_h, acts, 3)
    heads = [
        fetch(ref, wide.at[:, :, n * head_width : (n + 1) * head_width], 7 + n)
        for n, ref in enumerate((q_h, k_h, v_h, o_h))
    ]

    half = hidden_h.shape[2]
    hidden = turned.at[:, :, :half]
    last = [fetch(hidden_h, hidden, 11)]
    for n in range(2):
        columns = slice(n * D // 2, (n + 1) * D // 2)
        last.append(fetch(down_h.at[:, columns], up.at[n * half : (n + 1) * half, : D // 2], 12 + n))
    for copy in small:
        copy.wait()
    second_sum.finish()
    mine = place.seat()
    inner = jnp.zeros((rows, 1), f32)
    squares = jnp.zeros((rows, 1), f32)
    for n in range(D // LANES):
        lanes = slice(n * LANES, (n + 1) * LANES)
        grad = second_sum.chunk(lanes)
        values = residual[:, lanes]
        inner += jnp.sum(grad * gains[1:2, lanes] * values, axis=-1, keepdims=True)
        squares += jnp.sum(values * values, axis=-1, keepdims=True)
    scale = lax.rsqrt(squares / D + NORM_EPSILON)
    inner = inner / D
    for n in range(D // LANES):
        lanes = slice(n * LANES, (n + 1) * LANES)
        grad, values = second_sum.chunk(lanes), residual[:, lanes]
        gain_part[1:2, lanes] = jnp.sum(grad * values * scale, axis=0, keepdims=True)
        total = own_grad[:, lanes].astype(f32) + scale * (
            grad * gains[1:2, lanes] - values * scale * scale * inner
        )
        input_grad[:, lanes] = total
        blocks[mine, :, lanes] = total.astype(bf16)

    gather = PlaneGather(place, blocks, all_send, all_recv)
    gather.start()
    up_out.proceed()
    up_out.join()
    for copy in weights + heads:
        copy.wait()

    lane = lax.broadcasted_iota(jnp.int32, (full_rows, head_width), 1)
    first_half = (lane % HEAD_DIM) < HEAD_DIM // 2

    for copy in last:
        copy.wait()

    @pl.loop(0, count)
    def _(seq):
        for n in range(D // LANES):
            top, left = n * LANES // (D // 2) * half, n * LANES % (D // 2)
            product = dot(hidden[seq], up[top : top + half, left : left + LANES])
            part[2 * seq, :, n * LANES : (n + 1) * LANES] = product[:rows].astype(bf16)
            part[2 * seq + 1, :, n * LANES : (n + 1) * LANES] = product[rows:].astype(bf16)

    out_rows = out_share.shape[1]

    def out_shares():
        @pl.loop(0, D // LANES)
        def _(n):
            lanes = lanes_of(n)
            total = jnp.zeros((head_width, LANES), f32)
            for seq in range(count):
                values = wide[seq, :, 3 * head_width : 4 * head_width].astype(f32)
                total += dot(values[:rows].astype(bf16), blocks[2 * seq, :, lanes], 0, 0)
                total += dot(values[rows:].astype(bf16), blocks[2 * seq + 1, :, lanes], 0, 0)
            total = total.astype(bf16)
            for j in range(out_share.shape[0]):
                out_share[j, :, lanes] = total[j * out_rows : (j + 1) * out_rows]

    last_sum = PlaneSum(place, part, near, far, sums)
    for k in range(4):
        gather.arrive(k)
        seq = gather.sequence(k)
        if k == 3:
            out_shares()
            if aligned:
                out_out = to_owners(3, out_share, out_landed, out_met, stage_low)
            else:
                out_out = pltpu.make_async_copy(out_share, out_landed, own_sem.at[3])
                out_out.start()
        grads = jnp.concatenate(
            [dot(blocks[2 * seq], out_w[...], 1, 1), dot(blocks[2 * seq + 1], out_w[...], 1, 1)],
            axis=0,
        ).astype(bf16)
        queries = wide[seq, :, 0:head_width]
        key_vectors = wide[seq, :, head_width : 2 * head_width]
        value_vectors = wide[seq, :, 2 * head_width : 3 * head_width]
        grad_q, grad_k, grad_v = attention_grads(
            facts[seq, 2:3, 0:1], queries, key_vectors, value_vectors, grads
        )
        for n, grad in enumerate((grad_q, grad_k)):
            values = (grad * HEAD_DIM**-0.5).astype(bf16).astype(f32)
            back = values * cosine[...] - swap_halves(values, first_half) * sine[...]
            turned[seq, :, n * head_width : (n + 1) * head_width] = back.astype(bf16)
        turned[seq, :, 2 * head_width : 3 * head_width] = grad_v.astype(bf16)
        if k == 1:
            last_sum.near(0)
            last_sum.near(2)
        elif k == 2:
            last_sum.far(1)
            last_sum.far(3)

    gather.finish()
    fetch_first.wait()
    row_shares(acts, turned, qkv_share)
    triple = turned.shape[2]
    qkv_out = to_owners(2, qkv_share, qkv_landed, qkv_met, stage_wide.at[:, :, :triple], True)

    last_sum.finish()
    for n in range(D // LANES):
        lanes = slice(n * LANES, (n + 1) * LANES)
        block_output[:, lanes] = (residual[:, lanes] + last_sum.chunk(lanes)).astype(bf16)
    pl.semaphore_signal(near_free, inc=1, device_id=place.peer(SIBLING), device_id_type=MESH)
    for relation in ACROSS:
        pl.semaphore_signal(far_free, inc=1, device_id=place.peer(relation), device_id_type=MESH)
    pl.semaphore_wait(near_free, 1)
    pl.semaphore_wait(far_free, 3)
    first_sum = summed_over_plane(turned, qkv)
    if aligned:
        out_out.join()
    qkv_out.proceed()
    qkv_out.join()
    first_sum.finish()
    inner = jnp.zeros((rows, 1), f32)
    squares = jnp.zeros((rows, 1), f32)
    for n in range(D // LANES):
        lanes = slice(n * LANES, (n + 1) * LANES)
        grad = first_sum.chunk(lanes)
        values = own_tokens[:, lanes].astype(f32)
        inner += jnp.sum(grad * gains[0:1, lanes] * values, axis=-1, keepdims=True)
        squares += jnp.sum(values * values, axis=-1, keepdims=True)
    scale = lax.rsqrt(squares / D + NORM_EPSILON)
    inner = inner / D
    for n in range(D // LANES):
        lanes = slice(n * LANES, (n + 1) * LANES)
        grad, values = first_sum.chunk(lanes), own_tokens[:, lanes].astype(f32)
        gain_part[0:1, lanes] = jnp.sum(grad * values * scale, axis=0, keepdims=True)
        input_grad[:, lanes] += scale * (
            grad * gains[0:1, lanes] - values * scale * scale * inner
        )

    gain_copies = []
    for n, relation in enumerate(RELATIONS):
        copy = remote(
            gain_part, gain_plane.at[n], gain_send.at[n], gain_recv.at[n], place.peer(relation)
        )
        copy.start()
        gain_copies.append(copy)

    up_out.finish()
    landed = pltpu.make_async_copy(up_landed, up_share, load.at[1])
    landed.start()
    for copy in gain_copies:
        copy.wait()
    total = gain_part[...]
    for n in range(len(RELATIONS)):
        total += gain_plane[n]
    gain_far[0] = total
    gain_copies = []
    for dz in range(1, grps):
        copy = remote(
            gain_far.at[0],
            gain_far.at[dz],
            gain_send.at[7 + dz],
            gain_recv.at[7 + dz],
            place.plane(dz),
        )
        copy.start()
        gain_copies.append(copy)
    landed.wait()
    summed_rows(up_share, up_out.holds, up_sum)
    up_swap = Exchange(place, up_sum, up_held, swap_send.at[0], swap_recv.at[0], own_sem.at[4])
    for copy in gain_copies:
        copy.wait()
    total = gain_far[0]
    for dz in range(1, grps):
        total += gain_far[dz]
    gains_sum[...] = total

    qkv_out.finish()
    landed = pltpu.make_async_copy(qkv_landed, qkv_share, load.at[6])
    landed.start()
    landed.wait()
    summed_rows(qkv_share, qkv_out.holds, qkv_sum)
    qkv_swap = Exchange(place, qkv_sum, qkv_held, swap_send.at[1], swap_recv.at[1], own_sem.at[5])
    if aligned:
        out_out.finish()
    else:
        out_out.wait()
    up_swap.finish()
    qkv_swap.finish()


def backward(
    grps,
    aligned,
    facts,
    gains,
    tables,
    residual,
    own_tokens,
    own_grad,
    grad_both,
    up_local,
    second_norm,
    first_norm,
    out_local,
    qkv_local,
    heads,
    hidden,
    down_local,
):
    rows = residual.shape[0]
    count, full_rows, head_width = heads[0].shape
    seqs = full_rows // rows
    ranks = seqs * QUAD
    both = grad_both.shape[2]
    quad_rows = D // (seqs * grps)
    shard = quad_rows // QUAD
    out_rows = head_width // grps if aligned else HEAD_DIM
    triple = 3 * head_width
    out_count = head_width // out_rows
    hbm = pl.BlockSpec(memory_space=pl.ANY)
    vmem = pl.BlockSpec(memory_space=pltpu.VMEM)
    shape = jax.ShapeDtypeStruct
    dma = pltpu.SemaphoreType.DMA
    return pl.pallas_call(
        lambda *refs: back_kernel(grps, aligned, *refs),
        in_specs=[vmem] * 4 + [hbm] * 15,
        out_specs=[vmem] * 3 + [hbm] * 8,
        out_shape=[
            shape((rows, D), f32),
            shape((rows, D), bf16),
            shape((8, D), f32),
            shape((out_count, out_rows, D), bf16),
            shape((ranks, shard, both), bf16),
            shape((ranks, shard, triple), bf16),
            shape((grps, seqs, quad_rows, both), bf16),
            shape((grps, seqs, quad_rows, triple), bf16),
            shape((seqs, quad_rows, both), bf16),
            shape((out_rows, D), bf16),
            shape((seqs, quad_rows, triple), bf16),
        ],
        scratch_shapes=[
            pltpu.VMEM((count, full_rows, both), bf16),
            pltpu.VMEM((D, both), bf16),
            pltpu.VMEM((count, full_rows, D), bf16),
            pltpu.VMEM((head_width, D), bf16),
            pltpu.VMEM((D, triple), bf16),
            pltpu.VMEM((ranks, rows, D), bf16),
            pltpu.VMEM((4, rows, D), bf16),
            pltpu.VMEM((3, rows, D), bf16),
            pltpu.VMEM((ranks, rows, D), bf16),
            pltpu.VMEM((count, full_rows, triple), bf16),
            pltpu.VMEM((grps, seqs, quad_rows, both), bf16),
            pltpu.VMEM((out_count, out_rows, D), bf16),
            pltpu.VMEM((grps, seqs, quad_rows, triple), bf16),
            pltpu.VMEM((ranks, shard, both), bf16),
            pltpu.VMEM((ranks, shard, triple), bf16),
            pltpu.VMEM((out_rows, D), bf16),
            pltpu.VMEM((seqs, quad_rows, both), bf16),
            pltpu.VMEM((8, D), f32),
            pltpu.VMEM((7, 8, D), f32),
            pltpu.VMEM((grps, 8, D), f32),
            pltpu.VMEM((rows, D), f32),
            pltpu.VMEM((rows, D), bf16),
            pltpu.VMEM((rows, D), bf16),
            dma((17,)),
            dma((4,)),
            dma((4,)),
            dma((3,)),
            dma((3,)),
            dma((7,)),
            dma((7,)),
            dma((4, grps)),
            dma((4, grps)),
            dma((2, 7)),
            dma((2, 7)),
            dma((7 + grps,)),
            dma((7 + grps,)),
            dma((6,)),
            pltpu.SemaphoreType.REGULAR,
            pltpu.SemaphoreType.REGULAR,
        ],
        compiler_params=pltpu.CompilerParams(
            collective_id=0, has_side_effects=True, vmem_limit_bytes=VMEM_LIMIT
        ),
        cost_estimate=pl.CostEstimate(
            flops=30 * 10**9, bytes_accessed=60 * 2**20, transcendentals=2 * 10**6
        ),
        name="backward",
    )(
        facts,
        gains,
        *tables,
        residual,
        own_tokens,
        own_grad,
        grad_both,
        up_local,
        second_norm,
        first_norm,
        out_local,
        qkv_local,
        *heads,
        hidden,
        down_local,
    )


CHUNK = 1024


class FromOwners:
    def __init__(self, place, source, landed, landing, send, recv, own):
        self.place, self.source, self.send, self.recv = place, source, send, recv
        self.slot = lambda j: landing(landed, j)
        self.own = pltpu.make_async_copy(source, self.slot(place.g), own)
        self.line = place.grps == 4

    def copy(self, source, slot, sem, recv, target):
        place = self.place
        return remote(
            source, self.slot(slot), self.send.at[sem], self.recv.at[recv], (place.s, target, place.r, place.c)
        )

    def passed(self, g, j, target):
        source = self.source if j == g else self.slot(j)
        return self.copy(source, j, j + (4 if target > g else 0), j, target)

    def arrived(self, j):
        self.copy(self.source, j, j, j, j).wait_recv()

    def on_line(self, steps):
        for g in range(4):
            if steps[g]:

                @pl.when(self.place.g == g)
                def _():
                    for awaited, j, target in steps[g]:
                        if awaited is not None:
                            self.arrived(awaited)
                        if target is not None:
                            self.passed(g, j, target).start()

    FIRST = (
        ((None, 0, 1),),
        ((None, 1, 0), (None, 1, 2)),
        ((None, 2, 3), (None, 2, 1)),
        ((None, 3, 2),),
    )
    SECOND = (
        ((1, 1, None),),
        ((2, 2, 0), (0, 0, 2)),
        ((1, 1, 3), (3, 3, 1)),
        ((2, 2, None),),
    )
    THIRD = ((), ((3, 3, 0),), ((0, 0, 3),), ())

    def start(self):
        place = self.place
        self.own.start()
        if self.line:
            self.on_line(self.FIRST)
        else:
            self.copies = [
                self.copy(self.source, place.g, dz, dz, (place.g + dz) % place.grps)
                for dz in range(1, place.grps)
            ]
            for copy in self.copies:
                copy.start()

    def second(self):
        if self.line:
            self.on_line(self.SECOND)

    def third(self):
        if self.line:
            self.on_line(self.THIRD)

    def finish(self):
        self.own.wait()
        if self.line:
            for g in range(4):

                @pl.when(self.place.g == g)
                def _():
                    for j in {0: (2, 3), 3: (1, 0)}.get(g, ()):
                        self.arrived(j)
                    for steps in (self.FIRST, self.SECOND, self.THIRD):
                        for _, j, target in steps[g]:
                            if target is not None:
                                self.passed(g, j, target).wait_send()

        else:
            for copy in self.copies:
                copy.wait()


class Chain:
    def __init__(self, place, part, through, landed, lanes, send, recv, own):
        self.place, self.part, self.through, self.landed = place, part, through, landed
        self.send, self.recv = send, recv
        self.area = (slice(0, landed.shape[1]), lanes)
        self.own = pltpu.make_async_copy(self.block(part, place.g), self.block(landed, 2), own)

    def block(self, ref, j):
        return ref.at[(j, *self.area)]

    def copy(self, g, j):
        place, target = self.place, g + 1 if j > g else g - 1
        if target == j:
            landing = self.block(self.landed, 0 if j > g else 1)
        else:
            landing = self.block(self.through, j)
        recv = j if target != j else (j if j > g else 4)
        return remote(
            self.block(self.part, j), landing, self.send.at[j], self.recv.at[recv], (place.s, target, place.r, place.c)
        )

    def each(self, planes, action):
        for g in planes:

            @pl.when(self.place.g == g)
            def _():
                action(g)

    def blocks(self, g):
        return (3, 2, 1) if g == 0 else (0, 1, 2)

    def start(self):
        self.own.start()
        self.each((0, 3), lambda g: self.copy(g, self.blocks(g)[0]).start())

    def add(self, g, source, j):
        self.copy(source, j).wait_recv()
        area = (j, *self.area)
        self.part[area] = (self.part[area].astype(f32) + self.through[area].astype(f32)).astype(bf16)
        self.copy(g, j).start()

    def step(self, n):
        def ends(g):
            self.copy(g, self.blocks(g)[n - 1]).wait_send()
            self.copy(g, self.blocks(g)[n]).start()

        def inner(g):
            end = 0 if g == 1 else 3
            self.add(g, end, self.blocks(end)[n - 1])

        self.each((0, 3), ends)
        self.each((1, 2), inner)

    def last(self):
        self.each((1, 2), lambda g: self.add(g, 3 - g, 0 if g == 1 else 3))

    def finish(self):
        self.own.wait()

        def done(g):
            if g > 0:
                self.copy(g - 1, g).wait_recv()
            if g < 3:
                self.copy(g + 1, g).wait_recv()
            if g in (0, 3):
                self.copy(g, self.blocks(g)[2]).wait_send()
            else:
                for j in range(4):
                    if j != g:
                        self.copy(g, j).wait_send()

        self.each(range(4), done)


def shares_from(seq, values, weight, part):
    rows = part.shape[1]

    @pl.loop(0, part.shape[2] // LANES)
    def _(n):
        product = dot(values[seq], weight[:, lanes_of(n)])
        part[2 * seq, :, lanes_of(n)] = product[:rows].astype(bf16)
        part[2 * seq + 1, :, lanes_of(n)] = product[rows:].astype(bf16)


def times_slices(values, weight, lanes):
    piece = weight[:, :, :, :, lanes]
    return dot(values, piece.reshape(values.shape[1], piece.shape[4]))


def both_blocks(blocks, seq):
    return jnp.concatenate([blocks[2 * seq].astype(f32), blocks[2 * seq + 1].astype(f32)], axis=0)


def forward_kernel(
    grps,
    aligned,
    cosine,
    sine,
    own_facts,
    tokens_h,
    own_grad_h,
    qkv_own,
    up_own,
    out_own,
    down_own,
    residual,
    gains,
    facts,
    first_h,
    q_h,
    k_h,
    v_h,
    o_h,
    second_h,
    grads_landed,
    hidden_h,
    dgu_h,
    qkv_landed,
    up_landed,
    out_landed,
    down_landed,
    blocks,
    grad_blocks,
    norm,
    grad_seq,
    qkv_rank,
    up_rank,
    qkv,
    up,
    out_w,
    down,
    heads,
    part,
    near,
    far,
    both,
    hidden,
    dgu,
    all_facts,
    early,
    load,
    store,
    swap_send,
    swap_recv,
    near_send,
    near_recv,
    far_send,
    far_recv,
    all_send,
    all_recv,
    z_send,
    z_recv,
    fact_send,
    fact_recv,
    chain_send,
    chain_recv,
    own_sem,
):
    place = Place(grps)
    count, full_rows, _ = norm.shape
    rows = residual.shape[0]
    head_width = heads.shape[3]
    mine, rank = place.seat(), place.rank()

    def fetch(src, dst, n):
        copy = pltpu.make_async_copy(src, dst, load.at[n])
        copy.start()
        return copy

    def keep(src, dst, n):
        copy = pltpu.make_async_copy(src, dst, store.at[n])
        copy.start()
        return copy

    shard = qkv_own.shape[0]
    units = down.shape[0] // grps
    seqs = qkv_landed.shape[0]
    slots = iter(range(20))

    def fetch_chunks(src):
        pieces = []
        for top in range(0, src.shape[0], shard):
            for left in range(0, src.shape[1], CHUNK):
                slot = next(slots)
                space = both.at[slot // 5, (slot % 5) * shard : (slot % 5 + 1) * shard]
                copy = pltpu.make_async_copy(
                    src.at[top : top + shard, left : left + CHUNK], space, early.at[slot]
                )
                copy.start()
                pieces.append((copy, space))
        return pieces

    def dealt(pieces, weight, lanes, parts):
        count = CHUNK // (QUAD * lanes)
        width = count * lanes
        each = len(pieces) // (parts * seqs)
        for n, (copy, space) in enumerate(pieces):
            copy.wait()
            values = space[...]
            seq = n // each % seqs
            first = (n // (each * seqs) * each + n % each) * width
            for q in range(QUAD):
                taken = [
                    values[:, (k * QUAD + q) * lanes : (k * QUAD + q + 1) * lanes] for k in range(count)
                ]
                weight[0, seq, q, :, first : first + width] = jnp.concatenate(taken, axis=1).astype(bf16)

    facts[rank] = own_facts[...]
    if aligned:
        out_pieces = fetch_chunks(out_own)
    qkv_pieces = fetch_chunks(qkv_own)
    up_pieces = fetch_chunks(up_own)
    down_pieces = fetch_chunks(down_own)
    own_blocks = [fetch(tokens_h, blocks.at[mine], 0), fetch(own_grad_h, grad_blocks.at[mine], 1)]

    def plane_rows(ref, j):
        return ref.at[:, j]

    def own_rows(ref, j):
        size = ref.shape[0] // grps
        return ref.at[pl.ds(pl.multiple_of(j * size, size), size)]

    def rows_of(ref, j):
        top = j * units
        return ref.at[top // 128, pl.ds(pl.multiple_of(top % 128, units), units)]

    def from_owners(n, source, landed, landing):
        return FromOwners(place, source, landed, landing, z_send.at[n], z_recv.at[n], own_sem.at[n])

    def stacked(pieces, weight):
        across = weight.shape[1] // CHUNK
        for n, (copy, space) in enumerate(pieces):
            copy.wait()
            top, left = n // across * shard, n % across * CHUNK
            weight[top : top + shard, left : left + CHUNK] = space[...].astype(bf16)

    down_z = from_owners(3, down.at[:units], down_landed, own_rows)
    if aligned:
        stacked(out_pieces, out_w)
        out_z = from_owners(2, out_w.at[:shard], out_landed, own_rows)
    place.greet()
    if aligned:
        out_z.start()
    dealt(qkv_pieces, qkv, HEAD_DIM, 3)
    qkv_swap = Exchange(place, qkv, qkv_rank, swap_send.at[0], swap_recv.at[0], own_sem.at[4])
    fact_copies = []
    for n, relation in enumerate(RELATIONS):
        copy = remote(own_facts, facts.at[rank], fact_send.at[n], fact_recv.at[n], place.peer(relation))
        copy.start()
        fact_copies.append(copy)
    if aligned:
        out_z.second()
    dealt(up_pieces, up, units, 2)
    stacked(down_pieces, down)
    for copy in own_blocks:
        copy.wait()
    if aligned:
        out_z.third()
    qkv_swap.finish()
    qkv_z = from_owners(0, qkv_rank, qkv_landed, plane_rows)
    up_z = from_owners(1, up_rank, up_landed, plane_rows)
    qkv_z.start()
    token_gather = PlaneGather(place, blocks, all_send.at[0], all_recv.at[0])
    token_gather.start()
    for copy in fact_copies:
        copy.wait()
    all_facts[place.g] = facts[...]
    fact_copies = []
    for dz in range(1, grps):
        copy = remote(
            facts,
            all_facts.at[place.g],
            fact_send.at[7 + dz],
            fact_recv.at[7 + dz],
            place.plane(dz),
        )
        copy.start()
        fact_copies.append(copy)
    for copy in fact_copies:
        copy.wait()
    width = D // (seqs * grps * QUAD)
    for n in range(seqs * grps):
        pieces = [all_facts[n % grps, (n // grps) * QUAD + q, :, :width] for q in range(QUAD)]
        gains[:, n * QUAD * width : (n + 1) * QUAD * width] = jnp.concatenate(pieces, axis=1)
    token_gather.forward(0)
    token_gather.forward(1)
    up_swap = Exchange(place, up, up_rank, swap_send.at[1], swap_recv.at[1], own_sem.at[5])
    qkv_z.second()
    token_gather.forward(2)
    token_gather.arrive(3)
    token_gather.copies[3].wait_recv()
    token_gather.copies[4].wait_recv()
    token_gather.finish()

    @pl.loop(0, count)
    def _(seq):
        values = both_blocks(blocks, seq)
        scale = lax.rsqrt(jnp.mean(values * values, axis=-1, keepdims=True) + NORM_EPSILON)
        norm[seq] = (values * scale * gains[0:1, :]).astype(bf16)

    stores = [keep(norm, first_h, 0)]
    grad_gather = PlaneGather(place, grad_blocks, all_send.at[1], all_recv.at[1])
    grad_gather.start()
    qkv_z.third()
    up_swap.finish()
    qkv_z.finish()
    up_z.start()
    fetch(qkv_landed, qkv, 2).wait()

    lane = lax.broadcasted_iota(jnp.int32, (full_rows, head_width), 1)
    first_half = (lane % HEAD_DIM) < HEAD_DIM // 2

    if aligned:
        out_z.finish()
        fetch(out_landed, out_w, 3).wait()
    else:
        fetch(out_own, out_w, 3).wait()

    plane_sum = PlaneSum(place, part, near, far, (near_send, near_recv, far_send, far_recv))
    mixed = heads.at[3]
    for k in range(4):
        seq = plane_sum.sequence(k)
        for n in range(3):
            lanes = slice(n * head_width, (n + 1) * head_width)
            values = times_slices(norm[seq], qkv, lanes)
            if n < 2:
                values = values * cosine[...] + swap_halves(values, first_half) * sine[...]
            heads[n, seq] = values.astype(bf16)
        heads[3, seq] = attention(facts[seq, 2:3, 0:1], heads[0, seq], heads[1, seq], heads[2, seq])
        shares_from(seq, mixed, out_w, part)
        if k % 2 == 0:
            plane_sum.near(k)
        else:
            plane_sum.far(k)
        if k == 0:
            grad_gather.forward(0)
            grad_gather.forward(1)
    grad_gather.forward(2)
    grad_gather.arrive(3)
    grad_gather.copies[3].wait_recv()
    grad_gather.copies[4].wait_recv()
    grad_gather.finish()
    stores += [keep(heads.at[n], ref, 1 + n) for n, ref in enumerate((q_h, k_h, v_h, o_h))]
    up_z.second()

    @pl.loop(0, count)
    def _(seq):
        grad_seq[seq] = both_blocks(grad_blocks, seq).astype(bf16)

    fetch(tokens_h, grad_blocks.at[mine], 4).wait()
    plane_sum.finish()
    squares = jnp.zeros((rows, 1), f32)
    for n in range(D // LANES):
        lanes = slice(n * LANES, (n + 1) * LANES)
        values = grad_blocks[mine, :, lanes].astype(f32) + plane_sum.chunk(lanes)
        residual[:, lanes] = values
        squares += jnp.sum(values * values, axis=-1, keepdims=True)
    scale = lax.rsqrt(squares / D + NORM_EPSILON)
    for n in range(D // LANES):
        lanes = slice(n * LANES, (n + 1) * LANES)
        blocks[mine, :, lanes] = (residual[:, lanes] * scale * gains[1:2, lanes]).astype(bf16)
    norm_gather = PlaneGather(place, blocks, all_send.at[2], all_recv.at[2])
    norm_gather.start()
    up_z.third()
    stores[0].wait()
    half = hidden.shape[2]
    for k in range(4):
        norm_gather.arrive(k, forwarded=k == 1)
        seq = norm_gather.sequence(k)
        norm[seq] = both_blocks(blocks, seq).astype(bf16)
        if k == 0:
            norm_gather.forward(1)
            up_z.finish()
            down_z.start()
            fetch(up_landed, up, 5).wait()
        elif k == 2:
            down_z.second()
        gate = times_slices(norm[seq], up, slice(0, half))
        above = times_slices(norm[seq], up, slice(half, 2 * half))
        both[seq, :, :half] = gate
        both[seq, :, half:] = above
        hidden[seq] = (gate * jax.nn.sigmoid(gate) * above).astype(bf16)
    norm_gather.finish()
    stores[0] = keep(norm, second_h, 5)
    stores.append(keep(hidden, hidden_h, 7))
    tall = min(256, half)
    slab = part.shape[1] // 128 * 128

    def down_shares(side):
        lanes = slice(side * D // 2, (side + 1) * D // 2)

        @pl.loop(0, half // tall)
        def _(b):
            product = over_tokens(hidden, lanes_of(b, tall), grad_seq, lanes).astype(bf16)
            for p in range(tall // slab):
                part[b * (tall // slab) + p, :slab, lanes] = product[p * slab : (p + 1) * slab]

    down_shares(0)
    if grps == 4:
        chains = [
            Chain(
                place,
                part,
                near,
                grads_landed,
                slice(side * D // 2, (side + 1) * D // 2),
                chain_send.at[side],
                chain_recv.at[side],
                own_sem.at[6 + side],
            )
            for side in range(2)
        ]
        chains[0].start()
    down_z.third()
    down_shares(1)
    if grps == 4:
        chains[1].start()
        chains[0].step(1)
        chains[1].step(1)
        chains[0].step(2)
    else:
        spread = [pltpu.make_async_copy(rows_of(part, place.g), grads_landed.at[place.g], own_sem.at[6])]
        for dz in range(1, grps):
            spread.append(
                remote(
                    rows_of(part, (place.g + dz) % grps),
                    grads_landed.at[place.g],
                    chain_send.at[0, dz],
                    chain_recv.at[0, dz],
                    place.plane(dz),
                )
            )
        for copy in spread:
            copy.start()
    down_z.finish()
    down_copy = fetch(down_landed, down, 6)
    if grps == 4:
        chains[0].last()
        chains[1].step(2)
        chains[1].last()
    down_copy.wait()

    def feed_forward_grads(seq):
        grads = dot(grad_seq[seq], down[...], 1, 1)
        gate, above = both[seq, :, :half], both[seq, :, half:]
        sigmoid = jax.nn.sigmoid(gate)
        dgu[seq, :, :half] = (grads * above * sigmoid * (1.0 + gate * (1.0 - sigmoid))).astype(bf16)
        dgu[seq, :, half:] = (grads * (gate * sigmoid)).astype(bf16)

    pl.loop(0, count)(feed_forward_grads)
    stores.append(keep(dgu, dgu_h, 8))
    if grps == 4:
        for chain in chains:
            chain.finish()
    else:
        for copy in spread:
            copy.wait()
    for copy in stores:
        copy.wait()


def forward(grps, aligned, tables, own_facts, tokens, own_grad, qkv_own, up_own, out_own, down_own):
    rows = tokens.shape[0]
    shard = qkv_own.shape[0]
    seqs = D // (shard * grps * QUAD)
    ranks = seqs * QUAD
    triple, both = qkv_own.shape[1] // ranks, up_own.shape[1] // ranks
    count, full_rows, head_width = QUAD, rows * seqs, triple // 3
    half = both // 2
    hbm = pl.BlockSpec(memory_space=pl.ANY)
    vmem = pl.BlockSpec(memory_space=pltpu.VMEM)
    shape = jax.ShapeDtypeStruct
    dma = pltpu.SemaphoreType.DMA
    by_heads = shape((count, full_rows, head_width), bf16)
    return pl.pallas_call(
        lambda *refs: forward_kernel(grps, aligned, *refs),
        in_specs=[vmem] * 3 + [hbm] * 6,
        out_specs=[vmem] * 3 + [hbm] * 13,
        out_shape=[
            shape((rows, D), f32),
            shape((8, D), f32),
            shape((ranks, 8, 128), f32),
            shape((count, full_rows, D), bf16),
            by_heads,
            by_heads,
            by_heads,
            by_heads,
            shape((count, full_rows, D), bf16),
            shape((3 if grps == 4 else grps, half // grps, D), bf16),
            shape((count, full_rows, half), bf16),
            shape((count, full_rows, both), bf16),
            shape((seqs, grps, QUAD, shard, triple), bf16),
            shape((seqs, grps, QUAD, shard, both), bf16),
            shape((head_width, D), bf16),
            shape((half, D), bf16),
        ],
        scratch_shapes=[
            pltpu.VMEM((ranks, rows, D), bf16),
            pltpu.VMEM((ranks, rows, D), bf16),
            pltpu.VMEM((count, full_rows, D), bf16),
            pltpu.VMEM((count, full_rows, D), bf16),
            pltpu.VMEM((seqs, QUAD, shard, triple), bf16),
            pltpu.VMEM((seqs, QUAD, shard, both), bf16),
            pltpu.VMEM((seqs, grps, QUAD, shard, triple), bf16),
            pltpu.VMEM((seqs, grps, QUAD, shard, both), bf16),
            pltpu.VMEM((head_width, D), bf16),
            pltpu.VMEM((half, D), bf16),
            pltpu.VMEM((4, count, full_rows, head_width), bf16),
            pltpu.VMEM((ranks, rows, D), bf16),
            pltpu.VMEM((4, rows, D), bf16),
            pltpu.VMEM((3, rows, D), bf16),
            pltpu.VMEM((count, full_rows, both), f32),
            pltpu.VMEM((count, full_rows, half), bf16),
            pltpu.VMEM((count, full_rows, both), bf16),
            pltpu.VMEM((grps, ranks, 8, 128), f32),
            dma((20,)),
            dma((7,)),
            dma((9,)),
            dma((2, 7)),
            dma((2, 7)),
            dma((4,)),
            dma((4,)),
            dma((3,)),
            dma((3,)),
            dma((3, 7)),
            dma((3, 7)),
            dma((4, 2 * grps)),
            dma((4, grps)),
            dma((7 + grps,)),
            dma((7 + grps,)),
            dma((2, max(5, grps))),
            dma((2, max(5, grps))),
            dma((8,)),
        ],
        compiler_params=pltpu.CompilerParams(
            collective_id=1, has_side_effects=True, vmem_limit_bytes=VMEM_LIMIT
        ),
        cost_estimate=pl.CostEstimate(
            flops=20 * 10**9, bytes_accessed=60 * 2**20, transcendentals=4 * 10**6
        ),
        name="forward",
    )(*tables, own_facts, tokens, own_grad, qkv_own, up_own, out_own, down_own)


DEPTH = 4


def adam_kernel(grps, down_planes, out_planes, up_ranks, qkv_ranks, gains_sum, gains, gains_m, gains_v, *refs):
    states, outs = refs[:12], refs[12:28]
    gains_outs = refs[28:31]
    state, planes, ranks, fresh, copied, in_sem, out_sem = refs[31:]
    plane = lax.axis_index("grp")
    rows = state.shape[2]
    units = CHUNK // QUAD
    pieces = []
    for n, (name, rate) in enumerate(
        (("down", FF ** (-0.5)), ("out", (D // 128) ** (-0.5)), ("up", D ** (-0.5)), ("qkv", D ** (-0.5)))
    ):
        arrays = states[3 * n : 3 * n + 3]
        for top in range(0, arrays[0].shape[0], rows):
            for left in range(0, arrays[0].shape[1], CHUNK):
                pieces.append((name, rate, n, top, left))

    def grad_source(name, top, left, slot):
        if name in ("down", "out"):
            source = down_planes if name == "down" else out_planes
            return (
                source.at[:, top : top + rows, left : left + CHUNK],
                planes.at[slot, : source.shape[0]],
            )
        source, parts = (up_ranks, 2) if name == "up" else (qkv_ranks, 3)
        width = source.shape[2] // parts
        per_seq = width // units
        n = left // CHUNK
        seqs = source.shape[0] // QUAD
        seq = n // per_seq % seqs
        first = n // (per_seq * seqs) * width + n % per_seq * units
        return source.at[seq * QUAD : (seq + 1) * QUAD, :, first : first + units], ranks.at[slot]

    def reads(k):
        name, _, n, top, left = pieces[k]
        slot = k % DEPTH
        window = (slice(top, top + rows), slice(left, left + CHUNK))
        copies = [
            pltpu.make_async_copy(states[3 * n + i].at[window], state.at[slot, i], in_sem.at[slot, i])
            for i in range(3)
        ]
        source, space = grad_source(name, top, left, slot)
        return copies + [pltpu.make_async_copy(source, space, in_sem.at[slot, 3])]

    def writes(k):
        _, _, n, top, left = pieces[k]
        slot = k % DEPTH
        window = (slice(top, top + rows), slice(left, left + CHUNK))
        copies = [
            pltpu.make_async_copy(fresh.at[slot, i], outs[4 * n + i].at[window], out_sem.at[slot, i])
            for i in range(3)
        ]
        return copies + [
            pltpu.make_async_copy(copied.at[slot], outs[4 * n + 3].at[window], out_sem.at[slot, 3])
        ]

    def gradient(name, slot):
        if name in ("down", "out"):
            chained = name == "down"
            source = down_planes if chained else out_planes
            total = jnp.zeros((rows, CHUNK), f32)
            for j in range(source.shape[0]):
                held = planes[slot, j].astype(f32)
                if grps == 4 and chained and j < 2:
                    held = jnp.where(plane > 0 if j == 0 else plane < 3, held, 0.0)
                elif grps == 4 and not chained and j in (0, 3):
                    held = jnp.where(plane != 3 - j, held, 0.0)
                total += held
            return total
        lanes = down_planes.shape[1] if name == "up" else HEAD_DIM
        values = [ranks[slot, q].astype(f32) for q in range(QUAD)]
        return jnp.concatenate(
            [
                values[q][:, n * lanes : (n + 1) * lanes]
                for n in range(units // lanes)
                for q in range(QUAD)
            ],
            axis=1,
        )

    for k in range(DEPTH - 1):
        for copy in reads(k):
            copy.start()
    results = adam_update(gains[...], gains_m[...], gains_v[...], gains_sum[...], 0.3)
    for out, result in zip(gains_outs, results):
        out[...] = result
    for k, (name, rate, _, _, _) in enumerate(pieces):
        slot = k % DEPTH
        if k + DEPTH - 1 < len(pieces):
            for copy in reads(k + DEPTH - 1):
                copy.start()
        for copy in reads(k):
            copy.wait()
        if k >= DEPTH:
            for copy in writes(k - DEPTH):
                copy.wait()
        results = adam_update(state[slot, 0], state[slot, 1], state[slot, 2], gradient(name, slot), rate)
        for i in range(3):
            fresh[slot, i] = results[i]
        copied[slot] = results[0].astype(bf16)
        for copy in writes(k):
            copy.start()
    for k in range(len(pieces) - DEPTH, len(pieces)):
        for copy in writes(k):
            copy.wait()


def adam(grps, down_planes, out_planes, up_ranks, qkv_ranks, gains_sum, gains, states):
    rows = up_ranks.shape[1]
    hbm = pl.BlockSpec(memory_space=pl.ANY)
    vmem = pl.BlockSpec(memory_space=pltpu.VMEM)
    shapes = []
    for array in states[::3]:
        shapes += [jax.ShapeDtypeStruct(array.shape, f32)] * 3
        shapes.append(jax.ShapeDtypeStruct(array.shape, bf16))
    shapes += [jax.ShapeDtypeStruct(gains[0].shape, f32)] * 3
    size = sum(array.size for array in states) // 3
    outs = pl.pallas_call(
        lambda *refs: adam_kernel(grps, *refs),
        in_specs=[hbm] * 4 + [vmem] * 4 + [hbm] * 12,
        out_specs=[hbm] * 16 + [vmem] * 3,
        out_shape=shapes,
        scratch_shapes=[
            pltpu.VMEM((DEPTH, 3, rows, CHUNK), f32),
            pltpu.VMEM((DEPTH, grps, rows, CHUNK), bf16),
            pltpu.VMEM((DEPTH, QUAD, rows, CHUNK // QUAD), bf16),
            pltpu.VMEM((DEPTH, 3, rows, CHUNK), f32),
            pltpu.VMEM((DEPTH, rows, CHUNK), bf16),
            pltpu.SemaphoreType.DMA((DEPTH, 4)),
            pltpu.SemaphoreType.DMA((DEPTH, 4)),
        ],
        compiler_params=pltpu.CompilerParams(vmem_limit_bytes=VMEM_LIMIT),
        cost_estimate=pl.CostEstimate(flops=size * 16, bytes_accessed=size * 28, transcendentals=size),
        name="adam",
    )(down_planes, out_planes, up_ranks, qkv_ranks, gains_sum, *gains, *states)
    return outs[:4], outs[4:8], outs[8:12], outs[12:16], outs[16:]


def on_device(
    tokens,
    cotangent,
    lengths,
    qkv_weight,
    qkv_moment,
    qkv_square,
    out_weight,
    out_moment,
    out_square,
    up_weight,
    up_moment,
    up_square,
    down_weight,
    down_moment,
    down_square,
    norm_gains,
    gains_moment,
    gains_square,
):
    seqs = lax.axis_size("seq")
    grps = lax.axis_size("grp")
    ranks = seqs * QUAD
    own_rows = tokens.shape[1]
    full_rows = own_rows * seqs
    all_rows = full_rows * QUAD
    heads_local = HEADS // ranks
    head_width = heads_local * HEAD_DIM
    units = down_weight.shape[0]
    aligned = out_weight.shape[0] == HEAD_DIM
    tables = rotate_table(full_rows, heads_local)

    positions = lax.axis_index("seq") * own_rows + jnp.arange(own_rows, dtype=jnp.int32)
    own_grad = jnp.where((positions < lengths[0])[:, None], cotangent[0], 0)
    own_gains = norm_gains.shape[1]
    own_facts = jnp.zeros((8, 128), f32)
    own_facts = own_facts.at[:2, :own_gains].set(norm_gains.astype(bf16).astype(f32))
    own_facts = own_facts.at[2].set(lengths[0].astype(f32))

    out_own = out_weight
    if not aligned:
        out_all = lax.all_gather(out_weight.astype(bf16), EVERY, axis=0, tiled=True)
        out_all = out_all.reshape(seqs, heads_local, QUAD, HEAD_DIM, D)
        seat = lax.axis_index("row") * 2 + lax.axis_index("core")
        out_own = lax.dynamic_index_in_dim(
            lax.dynamic_index_in_dim(out_all, lax.axis_index("seq"), 0, False), seat, 1, False
        ).reshape(head_width, D)
    (
        residual,
        gains,
        facts,
        first_norm,
        queries,
        key_vectors,
        value_vectors,
        attended,
        second_norm,
        down_planes,
        hidden,
        grad_both,
        qkv_local,
        up_local,
        out_local,
        down_local,
    ) = forward(
        grps,
        aligned,
        tables,
        own_facts,
        tokens[0],
        own_grad,
        qkv_weight,
        up_weight,
        out_own,
        down_weight,
    )
    if not aligned:
        out_local = out_own
    (
        input_grad,
        block_output,
        gains_total,
        out_planes,
        up_ranks,
        qkv_ranks,
        *_,
    ) = backward(
        grps,
        aligned,
        facts,
        gains,
        tables,
        residual,
        tokens[0],
        own_grad,
        grad_both,
        up_local.reshape(D, -1),
        second_norm,
        first_norm,
        out_local,
        qkv_local.reshape(D, -1),
        (queries, key_vectors, value_vectors, attended),
        hidden,
        down_local,
    )
    if aligned:
        out_sum = out_planes
    else:
        placed_term = jnp.zeros((seqs, QUAD, heads_local, HEAD_DIM, D), bf16)
        placed_term = lax.dynamic_update_slice(
            placed_term,
            out_planes.reshape(1, 1, heads_local, HEAD_DIM, D),
            (lax.axis_index("seq"), seat, 0, 0, 0),
        )
        out_sum = lax.psum_scatter(
            placed_term.transpose(0, 2, 1, 3, 4).reshape(D, D),
            EVERY,
            scatter_dimension=0,
            tiled=True,
        )[None]
    device = ((lax.axis_index("seq") * grps + lax.axis_index("grp")) * 2 + lax.axis_index("row")) * 2
    gains_sum = lax.dynamic_slice(
        gains_total, (0, (device + lax.axis_index("core")) * own_gains), (2, own_gains)
    )
    down_new, out_new, up_new, qkv_new, gains_new = adam(
        grps,
        down_planes,
        out_sum,
        up_ranks,
        qkv_ranks,
        gains_sum,
        (norm_gains, gains_moment, gains_square),
        (
            down_weight,
            down_moment,
            down_square,
            out_weight,
            out_moment,
            out_square,
            up_weight,
            up_moment,
            up_square,
            qkv_weight,
            qkv_moment,
            qkv_square,
        ),
    )
    return (
        block_output[None],
        input_grad[None],
        *qkv_new,
        *out_new,
        *up_new,
        *down_new,
        *gains_new,
    )


def solution(mesh):
    seqs, rest = mesh.shape["seq"], mesh.shape["fsdp"]
    planes = Mesh(
        mesh.devices.reshape(seqs, rest // QUAD, 2, 2), ("seq", "grp", "row", "core")
    )
    rows = P(("grp", "row", "core"), "seq", None)
    shards = P(EVERY, None)
    gains = P(None, EVERY)
    return jax.shard_map(
        on_device,
        mesh=planes,
        in_specs=(rows, rows, P(("grp", "row", "core"))) + (shards,) * 12 + (gains,) * 3,
        out_specs=(rows, rows) + (shards,) * 16 + (gains,) * 3,
        check_vma=False,
    )
```
